32 devices in a mesh: dp: 2 (over core), mem: 16 (over z, y, x).
Axes of the slice: x: 2, y: 2, z: 4, core: 2. Of those that a mesh axis runs over, the one named last changes fastest.
Arguments:
- tokens: bfloat16 [4096, 1024], P(('dp', 'mem')), may hold values from -6 to 6
- attn_gain: float32 [1024], replicated, may hold values from 0.5 to 1.5
- qkv_weight: bfloat16 [1024, 3072], replicated, may hold values from -0.1875 to 0.1875
- out_weight: bfloat16 [1024, 1024], replicated, may hold values from -0.75 to 0.75
- bias_table: float32 [8, 32], replicated, may hold values from -4 to 4
- gate_logit: float32 [8], replicated, may hold values from -1.5 to 1.5
- ffn_gain: float32 [1024], replicated, may hold values from 0.5 to 1.5
- up_weight: bfloat16 [1024, 4096], replicated, may hold values from -0.1875 to 0.1875
- down_weight: bfloat16 [1024, 4096], replicated, may hold values from -0.09375 to 0.09375
- memory_keys: bfloat16 [65536, 1024], P('mem'), may hold values from -6 to 6
- memory_values: bfloat16 [65536, 1024], P('mem'), may hold values from -6 to 6
- book_lengths: int32 [2, 3], P('dp'), may hold values from 1 to 2046, as said below
- slot_shard: int32 [4096, 8, 32, 1], P(('dp', 'mem')), may hold values from 0 to 15; in each aligned block of 32768 rows (0 to 32767, 32768 to 65535, ..., all dimensions but the last counted through in order) at most 3072 rows name the same one
- slot_index: int32 [4096, 8, 32], P(('dp', 'mem')), may hold values from 0 to 4095
- slot_live: int32 [4096, 8, 32], P(('dp', 'mem')), may hold values from 0 to 1, as said below
- cotangent: bfloat16 [4096, 1024], P(('dp', 'mem')), may hold values from -6 to 6
Outputs:
- block_out: bfloat16 [4096, 1024], P(('dp', 'mem'))
- tokens_grad: float32 [4096, 1024], P(('dp', 'mem'))
- qkv_grad: float32 [1024, 3072], P('mem')
- out_grad: float32 [1024, 1024], P('mem')
- up_grad: float32 [1024, 4096], P('mem')
- down_grad: float32 [1024, 4096], P('mem')
- attn_gain_grad: float32 [1024], replicated
- ffn_gain_grad: float32 [1024], replicated
- bias_grad: float32 [8, 32], replicated
- gate_grad: float32 [8], replicated
The draws below stay inside these ranges and needn't reach their ends.
Inputs may be any that keep to these rules, and one draw needn't show every extreme that they name: `book_lengths`: the 3 books of a group fill its 2048 tokens; the middle one begins in the first 128 tokens and ends in the last 128; in some group the first and last books are one token long. `slot_shard`: among the 32768 entries of one device's tokens no device of mem is named more than 3072 times, and some device is named exactly 3072 times. `slot_live`: some token heads have no live entry.
All inputs are finite; a program needn't handle non-finite values.
Results may differ from the reference program's by a relative error of at most 0.014.
Values may be sent and summed in bfloat16 or wider, within the bound.
A program may use at most 256 MiB of HBM per device.

```python
import math
import jax
import jax.numpy as jnp
import numpy as np
from jax import lax

D = 1024
H = 8
HD = 128
FF = 4096
W = 512
K = 32
NB = 32
TOK_DEV = 128
SLOT_DEV = 4096
GROUP = 2048
TOKENS = 4096
SLOTS = 65536
CAP = 3072
N_DP = 2
N_MEM = 16


def draw_book_lengths(key, part):
    key = jax.random.fold_in(key, 5)
    first_key, last_key, pick_key = jax.random.split(key, 3)
    head_len = jax.random.randint(first_key, (N_DP, 1), 1, TOK_DEV)
    tail_len = jax.random.randint(last_key, (N_DP, 1), 1, TOK_DEV)
    picked = jax.random.randint(pick_key, (), 0, N_DP)
    chosen = (jnp.arange(N_DP, dtype=jnp.int32) == picked)[:, None]
    head_len = jnp.where(chosen, 1, head_len)
    tail_len = jnp.where(chosen, 1, tail_len)
    return jnp.concatenate([head_len, GROUP - head_len - tail_len, tail_len], axis=1).astype(jnp.int32)


def draw_slot_live(key, part):
    key = jax.random.fold_in(key, 7)
    dead_key, keep_key = jax.random.split(key)
    dead_rows = jax.random.randint(dead_key, (TOKENS, H, 1), 0, 8) == 0
    kept_slots = jax.random.randint(keep_key, (TOKENS, H, K), 0, 4) != 0
    return jnp.logical_and(kept_slots, jnp.logical_not(dead_rows)).astype(jnp.int32)


def with_ends(values, stream_key, least, largest):
    longest = values.shape.index(max(values.shape))
    spots = []
    for shift in (0, 1):
        where = [jax.random.randint(jax.random.fold_in(stream_key, axis), (), 0, length) for axis, length in enumerate(values.shape)]
        where[longest] = (where[longest] + shift) % values.shape[longest]
        spots.append(tuple(where))
    return values.at[spots[0]].set(least).at[spots[1]].set(largest)


def block_levels(rng, shape, shards, low, top_value):
    factor_of = 1.0
    for dim, parts in shards:
        steps = jax.random.uniform(jax.random.fold_in(jax.random.fold_in(rng, 6), dim), (parts,), jnp.float32, low / len(shards), top_value / len(shards))
        factor_of = factor_of * jnp.repeat(jnp.exp(steps), shape[dim] // parts).reshape((-1,) + (1,) * (len(shape) - 1 - dim))
    return factor_of


def deal_out(key, own, number, rows, number_of, top, bound, slope):
    order = jax.random.permutation(key, number_of)
    heavy_load, ordinary = load_shares(number_of, rows * top, bound, slope, True), load_shares(number_of, rows * top, bound, slope, False)
    places = jnp.arange(number_of)

    def named(sizes, turn):
        used = int((sizes > 0).sum())
        fixed = max(1, used // 4)
        shifted = fixed + (places - fixed + turn * (used - fixed)) % max(1, number_of - fixed)
        return jnp.zeros((number_of,), jnp.int32).at[order[jnp.where(places < fixed, places, shifted)]].set(jnp.asarray(sizes, jnp.int32))

    sizes = jnp.where(number % 4 == 0, named(heavy_load, number // 4), named(ordinary, number - number // 4 - 1))
    mixed = jax.random.permutation(jax.random.fold_in(own, 3), number_of)
    source_of, receiver = mixed[0:number_of // 2 * 2:2], mixed[1:number_of // 2 * 2:2]
    margin = jnp.minimum(sizes[source_of] - 1, bound - sizes[receiver]) // 2
    margin = jnp.where((source_of == order[0]) | (receiver == order[0]) | (sizes[receiver] == 0), 0, jnp.maximum(margin, 0))
    shifted = jax.random.randint(jax.random.fold_in(own, 4), (number_of // 2,), 0, 1 << 20) % (margin + 1)
    sizes = sizes.at[source_of].add(-shifted).at[receiver].add(shifted)
    items = jnp.searchsorted(jnp.cumsum(sizes), jnp.arange(rows * top), side="right").astype(jnp.int32)
    listing = items.reshape(top, rows).T
    listing = listing[jax.random.permutation(jax.random.fold_in(own, 1), rows)]
    turn = jax.random.randint(jax.random.fold_in(own, 2), (rows, 1), 0, top)
    return jnp.take_along_axis(listing, (jnp.arange(top)[None, :] + turn) % top, axis=1)


def load_shares(amount, total, bound, lean, full):
    loads = [(1 << 20) // math.isqrt(grade ** lean) + 1 for grade in range(1, amount + 1)]
    largest = bound if full else min(bound, max(-(-total // amount), total * loads[0] // sum(loads)))
    least = 1 if total - largest >= amount - 1 else 0
    holding, spare = [largest] + [least] * (amount - 1), total - largest - least * (amount - 1)
    while spare > 0:
        movable = [i for i in range(1, amount) if holding[i] < largest] or [i for i in range(1, amount) if holding[i] < bound]
        pool, remaining = sum([loads[i] for i in movable]), spare
        for i in movable:
            more = min(bound - holding[i], max(1, remaining * loads[i] // pool), spare)
            holding[i] = holding[i] + more
            spare = spare - more
    return np.array(holding)


def scatter_about(stream_key, dims, width, most, shards=(), kind=jnp.bfloat16):
    gain = block_levels(stream_key, dims, shards, -0.22, 0.18) if shards else 1.0
    array = jax.random.normal(stream_key, dims, jnp.float32) * width * gain
    return jnp.minimum(jnp.maximum(array, -most), most).astype(kind)


def setup_inputs(seed: int = 0) -> dict:
    key_list = jax.random.split(jax.random.key(seed), 17)
    tokens = scatter_about(key_list[0], (TOKENS, D), 1.0, 6.0, ((0, 32),))
    attn_gain = jnp.clip(1.0 + 0.1 * jax.random.normal(key_list[1], (D,), jnp.float32), 0.5, 1.5)
    qkv_weight = scatter_about(key_list[2], (D, 3 * D), D ** -0.5, 0.1875)
    out_weight = scatter_about(key_list[3], (D, D), (D // 16) ** -0.5, 0.75)
    bias_table = scatter_about(key_list[4], (H, NB), 1.0, 4.0, (), jnp.float32)
    gate_logit = jnp.clip(jax.random.uniform(key_list[5], (H,), jnp.float32, -1.5, 1.5), -1.5, 1.5)
    ffn_gain = jnp.clip(1.0 + 0.1 * jax.random.normal(key_list[6], (D,), jnp.float32), 0.5, 1.5)
    up_weight = scatter_about(key_list[7], (D, FF), D ** -0.5, 0.1875)
    down_weight = scatter_about(key_list[8], (D, FF), FF ** -0.5, 0.09375)
    memory_keys = scatter_about(key_list[9], (SLOTS, D), 1.0, 6.0, ((0, 16),))
    memory_values = scatter_about(key_list[10], (SLOTS, D), 1.0, 6.0, ((0, 16),))
    book_lengths = draw_book_lengths(jax.random.fold_in(key_list[16], 71), 0)
    slot_shard_keys = jax.random.split(jax.random.fold_in(key_list[12], 1), TOKENS * H * K // (TOK_DEV * H * K))
    slot_shard_turns = jax.random.permutation(jax.random.fold_in(key_list[12], 3), TOKENS * H * K // (TOK_DEV * H * K))
    slot_shard = jax.vmap(lambda own, number: deal_out(jax.random.fold_in(key_list[12], 2), own, number, TOK_DEV * H * K, N_MEM, 1, CAP, 1))(slot_shard_keys, slot_shard_turns).reshape((TOKENS, H, K, 1))
    slot_index = with_ends(jax.random.randint(key_list[13], (TOKENS, H, K), 0, SLOT_DEV), jax.random.fold_in(key_list[13], 1), 0, SLOT_DEV - 1).astype(jnp.int32)
    slot_live = draw_slot_live(jax.random.fold_in(key_list[16], 71), 0)
    cotangent = scatter_about(key_list[15], (TOKENS, D), 1.0, 6.0, ((0, 32),))
    return {"tokens": tokens, "attn_gain": attn_gain, "qkv_weight": qkv_weight, "out_weight": out_weight, "bias_table": bias_table, "gate_logit": gate_logit, "ffn_gain": ffn_gain, "up_weight": up_weight, "down_weight": down_weight, "memory_keys": memory_keys, "memory_values": memory_values, "book_lengths": book_lengths, "slot_shard": slot_shard, "slot_index": slot_index, "slot_live": slot_live, "cotangent": cotangent}


@jax.custom_vjp
def low(v):
    return lax.optimization_barrier(v.astype(jnp.bfloat16)).astype(jnp.float32)

@jax.custom_vjp
def low_back(v):
    return v

def low_keep(v):
    return (low(v), None)

def low_pass(kept, grad):
    return (grad,)

def back_keep(v):
    return (v, None)

def back_low(kept, grad):
    return (low(grad),)
low.defvjp(low_keep, low_pass)
low_back.defvjp(back_keep, back_low)
eps_norm = 1e-06
bucket_edges = tuple((math.ceil(16 * 8 ** (edge_step / 16)) for edge_step in range(1, 16)))
highest = lax.Precision.HIGHEST
masked_score = -1e+30
dead_score = -10000.0

def bucket_of(offset):
    past_edges = sum(((offset >= edge_pos).astype(jnp.int32) for edge_pos in bucket_edges))
    return jnp.where(offset < 16, offset, 16 + past_edges).astype(jnp.int32)

def normed(values, gain_vec):
    return values * lax.rsqrt(lax.optimization_barrier(jnp.mean(values * values, axis=-1, keepdims=True)) + eps_norm) * gain_vec

def book_of(positions, lengths):
    book_ends = jnp.cumsum(lengths, dtype=jnp.int32)
    return lax.optimization_barrier(jnp.sum((positions[..., None] >= book_ends).astype(jnp.int32), axis=-1)).astype(jnp.int32)

def local_attention(queries, keys_all, values_all, table, books):
    block_rows = math.gcd(GROUP, 512)
    pad_keys = jnp.pad(keys_all, ((0, 0), (W, 0), (0, 0), (0, 0)))
    pad_values = jnp.pad(values_all, ((0, 0), (W, 0), (0, 0), (0, 0)))
    pad_books = jnp.pad(books, ((0, 0), (W, 0)), constant_values=-1)
    offset = jnp.arange(block_rows, dtype=jnp.int32)[:, None] + W - jnp.arange(W + block_rows, dtype=jnp.int32)[None, :]
    inside = (offset >= 0) & (offset < W)
    score_bias = jnp.take(table, bucket_of(jnp.maximum(offset, 0)), axis=1)

    def one_block(row_start):
        block_q = lax.dynamic_slice_in_dim(queries, row_start, block_rows, 1)
        block_k = lax.dynamic_slice_in_dim(pad_keys, row_start, W + block_rows, 1)
        block_v = lax.dynamic_slice_in_dim(pad_values, row_start, W + block_rows, 1)
        book_q = lax.dynamic_slice_in_dim(books, row_start, block_rows, 1)
        book_k = lax.dynamic_slice_in_dim(pad_books, row_start, W + block_rows, 1)
        allowed = inside[None] & (book_q[:, :, None] == book_k[:, None, :])
        raw_scores = jnp.einsum('gqhd,gkhd->ghqk', block_q, block_k, precision=highest) / math.sqrt(HD) + score_bias[None]
        scores = low_back(jnp.where(allowed[:, None], raw_scores, masked_score))
        row_max = lax.optimization_barrier(jnp.max(scores, axis=-1, keepdims=True))
        exp_scores = jnp.exp(scores - row_max)
        local_probs = exp_scores / lax.optimization_barrier(jnp.sum(exp_scores, axis=-1, keepdims=True))
        return jnp.einsum('ghqk,gkhd->gqhd', low(local_probs), block_v, precision=highest)
    row_starts = jnp.arange(GROUP // block_rows, dtype=jnp.int32) * block_rows
    outputs = lax.map(jax.checkpoint(one_block), row_starts)
    return jnp.transpose(outputs, (1, 0, 2, 3, 4)).reshape(queries.shape)

def memory_attention(queries, key_rows, value_rows, slot_shard, slot_index, slot_live):
    block_rows = math.gcd(TOKENS, 512)
    head_ids = jnp.arange(H, dtype=jnp.int32)[None, :, None]

    def one_block(row_start):
        block_q = lax.dynamic_slice_in_dim(queries, row_start, block_rows, 0)
        shard_ids = lax.dynamic_slice_in_dim(slot_shard, row_start, block_rows, 0)[..., 0]
        index_ids = lax.dynamic_slice_in_dim(slot_index, row_start, block_rows, 0)
        live_mask = lax.dynamic_slice_in_dim(slot_live, row_start, block_rows, 0) > 0
        slot_ids = (shard_ids * SLOT_DEV + index_ids).astype(jnp.int32)
        fetched_keys = key_rows[slot_ids, head_ids]
        fetched_values = value_rows[slot_ids, head_ids]
        raw_scores = jnp.einsum('thd,thkd->thk', block_q, fetched_keys, precision=highest) / math.sqrt(HD)
        scores = low_back(raw_scores)
        row_max = lax.optimization_barrier(jnp.max(jnp.where(live_mask, scores, dead_score), axis=-1, keepdims=True))
        exp_scores = jnp.exp(jnp.where(live_mask, scores - row_max, dead_score))
        sums_mem = lax.optimization_barrier(jnp.sum(exp_scores, axis=-1, keepdims=True))
        mem_probs = exp_scores / jnp.where(sums_mem > 0, sums_mem, 1.0)
        return jnp.einsum('thk,thkd->thd', low(mem_probs), fetched_values, precision=highest)
    row_starts = jnp.arange(TOKENS // block_rows, dtype=jnp.int32) * block_rows
    outputs = lax.map(jax.checkpoint(one_block), row_starts)
    return outputs.reshape(queries.shape)

def reference(tokens, attn_gain, qkv_weight, out_weight, bias_table, gate_logit, ffn_gain, up_weight, down_weight, memory_keys, memory_values, book_lengths, slot_shard, slot_index, slot_live, cotangent):
    positions = jnp.arange(GROUP, dtype=jnp.int32)
    books = jnp.stack([book_of(positions, book_lengths[group_id]) for group_id in range(N_DP)])
    key_rows = memory_keys.astype(jnp.float32).reshape(SLOTS, H, HD)
    value_rows = memory_values.astype(jnp.float32).reshape(SLOTS, H, HD)

    def forward(tokens_f, gain_in, qkv_f, out_f, table, gate_in, gain_mid, up_f, down_f):
        normed_in = low(normed(tokens_f, gain_in))
        projected = jnp.dot(normed_in, qkv_f, precision=highest)
        queries = low_back(low(projected[:, :D])).reshape(TOKENS, H, HD)
        keys_all = low_back(low(projected[:, D:2 * D])).reshape(N_DP, GROUP, H, HD)
        values_all = low_back(low(projected[:, 2 * D:])).reshape(N_DP, GROUP, H, HD)
        local_out = local_attention(queries.reshape(N_DP, GROUP, H, HD), keys_all, values_all, table, books).reshape(TOKENS, H, HD)
        memory_out = memory_attention(queries, key_rows, value_rows, slot_shard, slot_index, slot_live)
        gate_share = jax.nn.sigmoid(gate_in)[:, None]
        mixed_heads = gate_share * low_back(memory_out) + (1.0 - gate_share) * low_back(local_out)
        mixed_heads = low(mixed_heads.reshape(TOKENS, D))
        residual = tokens_f + low_back(jnp.dot(mixed_heads, out_f, precision=highest))
        normed_mid = low(normed(residual, gain_mid))
        up_proj = low_back(jnp.dot(normed_mid, up_f, precision=highest))
        activated = low(jax.nn.gelu(up_proj, approximate=False))
        return residual + low_back(jnp.dot(activated, down_f.T, precision=highest))
    primals = (tokens.astype(jnp.float32), attn_gain, qkv_weight.astype(jnp.float32), out_weight.astype(jnp.float32), bias_table, gate_logit, ffn_gain, up_weight.astype(jnp.float32), down_weight.astype(jnp.float32))
    result, pullback = jax.vjp(forward, *primals)
    grads = pullback(cotangent.astype(jnp.float32))
    return (result.astype(jnp.bfloat16), grads[0], grads[2], grads[3], grads[7], grads[8], grads[1], grads[6], grads[4], grads[5])
```

```python
import math

import jax
import jax.numpy as jnp
from jax import lax
from jax.sharding import PartitionSpec as P

W = 512


eps_norm = 1e-06
bucket_edges = tuple((math.ceil(16 * 8 ** (edge_step / 16)) for edge_step in range(1, 16)))
masked_score = -1e30
dead_score = -10000.0
contract_rows = (((0,), (0,)), ((), ()))
contract_cols = (((1,), (1,)), ((), ()))


def passed_along(value, axis, by):
    size = lax.axis_size(axis)
    pairs = [(i, i + by) for i in range(size) if 0 <= i + by < size]
    return lax.ppermute(value, axis, pairs)


def swapped(value):
    return lax.ppermute(value, "dp", [(0, 1), (1, 0)])


def bucket_of(offset):
    past_edges = sum(((offset >= edge_pos).astype(jnp.int32) for edge_pos in bucket_edges))
    return jnp.where(offset < 16, offset, 16 + past_edges)


def normed(values, gain_vec):
    return (
        values * lax.rsqrt(jnp.mean(values * values, axis=-1, keepdims=True) + eps_norm) * gain_vec
    )


def gelu_exact(values):
    return jax.nn.gelu(values, approximate=False)


def book_of(positions, lengths):
    book_ends = jnp.cumsum(lengths, dtype=jnp.int32)
    return jnp.sum((positions[..., None] >= book_ends).astype(jnp.int32), axis=-1)


def place_requests(slot_shard, slot_index, groups, capacity, heads):
    targets = slot_shard.reshape(-1)
    head_ids = jnp.broadcast_to(jnp.arange(heads, dtype=jnp.int32)[None, :, None], slot_index.shape)
    wanted = (slot_index * heads + head_ids).reshape(-1)
    total = targets.shape[0]
    block = math.gcd(total, 128)
    blocks = total // block
    owner_hot = (
        targets.reshape(blocks, block)[:, :, None]
        == jnp.arange(groups, dtype=jnp.int32)[None, None, :]
    )
    hot_low = owner_hot.astype(jnp.bfloat16)
    earlier = (
        jnp.arange(block, dtype=jnp.int32)[:, None] > jnp.arange(block, dtype=jnp.int32)[None, :]
    ).astype(jnp.bfloat16)
    inside_count = jnp.einsum("ij,bjg->big", earlier, hot_low, preferred_element_type=jnp.float32)
    block_totals = jnp.sum(owner_hot.astype(jnp.float32), axis=1)
    before_blocks = jnp.cumsum(block_totals, axis=0) - block_totals
    counts = inside_count + before_blocks[:, None, :]
    within = jnp.sum(jnp.where(owner_hot, counts, 0.0), axis=-1).reshape(-1).astype(jnp.int32)
    places = targets * capacity + within
    requests = jnp.zeros((groups * capacity,), jnp.int32).at[places].set(wanted)
    return (requests.reshape(groups, capacity), places)


def lookup(incoming, memory_keys, memory_values, heads):
    key_table = memory_keys.reshape(-1, memory_keys.shape[1] // heads)
    value_table = memory_values.reshape(-1, memory_values.shape[1] // heads)
    flat_ids = incoming.reshape(-1)
    found_rows = jnp.stack(
        [jnp.take(key_table, flat_ids, axis=0), jnp.take(value_table, flat_ids, axis=0)], axis=1
    )
    return found_rows.reshape(incoming.shape[0], incoming.shape[1], 2, key_table.shape[1])


def unpack(replies, places, entry_shape):
    flat_rows = replies.reshape(-1, 2, replies.shape[3])
    picked = jnp.take(flat_rows, places, axis=0)
    return picked.reshape(entry_shape + (2, replies.shape[3]))


def fetch_rows(requests, places, memory_keys, memory_values, heads, entry_shape):
    replies = lax.all_to_all(
        lookup(
            lax.all_to_all(requests, "mem", split_axis=0, concat_axis=0, tiled=True),
            memory_keys,
            memory_values,
            heads,
        ),
        "mem",
        split_axis=0,
        concat_axis=0,
        tiled=True,
    )
    return unpack(replies, places, entry_shape)


def memory_probs(queries, fetched_keys, live_mask, score_scale):
    raw_scores = (
        jnp.einsum("qhd,qhkd->qhk", queries, fetched_keys, preferred_element_type=jnp.float32)
        * score_scale
    )
    row_max = jnp.max(jnp.where(live_mask, raw_scores, dead_score), axis=-1, keepdims=True)
    exp_scores = jnp.exp(jnp.where(live_mask, raw_scores - row_max, dead_score))
    sums_mem = jnp.sum(exp_scores, axis=-1, keepdims=True)
    return exp_scores / jnp.where(sums_mem > 0, sums_mem, 1.0)


def on_device(
    tokens,
    attn_gain,
    qkv_weight,
    out_weight,
    bias_table,
    gate_logit,
    ffn_gain,
    up_weight,
    down_weight,
    memory_keys,
    memory_values,
    book_lengths,
    slot_shard,
    slot_index,
    slot_live,
    cotangent,
):
    rows, width = tokens.shape
    heads, buckets = bias_table.shape
    head_dim = width // heads
    top_count = slot_index.shape[2]
    hidden = up_weight.shape[1]
    groups = lax.axis_size("mem")
    capacity = max(2, 3 * rows * heads * top_count // (2 * groups))
    score_scale = 1.0 / math.sqrt(head_dim)
    sent_rows = min(W, rows)
    repeats = W // sent_rows
    first_pos = lax.axis_index("mem") * rows
    query_pos = first_pos + jnp.arange(rows, dtype=jnp.int32)
    key_pos = first_pos - W + jnp.arange(W + rows, dtype=jnp.int32)
    lengths = book_lengths[0]
    query_book = book_of(query_pos, lengths)
    key_book = jnp.where(key_pos >= 0, book_of(key_pos, lengths), -1)
    offset = (
        jnp.arange(rows, dtype=jnp.int32)[:, None]
        + W
        - jnp.arange(W + rows, dtype=jnp.int32)[None, :]
    )
    allowed = (offset >= 0) & (offset < W) & (query_book[:, None] == key_book[None, :])
    bucket = bucket_of(jnp.maximum(offset, 0))
    one_hot_f = (bucket[:, :, None] == jnp.arange(buckets, dtype=jnp.int32)).astype(jnp.float32)
    score_bias = jnp.einsum("qkb,hb->hqk", one_hot_f, bias_table, precision=lax.Precision.HIGHEST)
    tokens_f = tokens.astype(jnp.float32)
    normed_f, norm_in_back = jax.vjp(normed, tokens_f, attn_gain)
    normed_in = normed_f.astype(jnp.bfloat16)
    projected = jnp.dot(normed_in, qkv_weight, preferred_element_type=jnp.float32).astype(
        jnp.bfloat16
    )
    queries = projected[:, :width].reshape(rows, heads, head_dim)
    keys_own = projected[:, width : 2 * width].reshape(rows, heads, head_dim)
    values_own = projected[:, 2 * width :].reshape(rows, heads, head_dim)
    tail_rows = jnp.stack([keys_own, values_own])
    received = []
    for distance in range(repeats, 0, -1):
        received.append(passed_along(tail_rows, "mem", distance))
    halo_rows = jnp.concatenate(received, axis=1)
    keys_all = jnp.concatenate([halo_rows[0], keys_own], axis=0)
    values_all = jnp.concatenate([halo_rows[1], values_own], axis=0)

    def local_scores():
        raw_scores = (
            jnp.einsum("qhd,khd->hqk", queries, keys_all, preferred_element_type=jnp.float32)
            * score_scale
            + score_bias
        )
        return jnp.where(allowed[None], raw_scores, masked_score)

    scores = local_scores()
    row_max = jnp.max(scores, axis=-1, keepdims=True)
    exp_scores = jnp.exp(scores - row_max)
    sums_local = jnp.sum(exp_scores, axis=-1, keepdims=True)
    local_probs = exp_scores / sums_local
    log_total = row_max + jnp.log(sums_local)
    local_out = jnp.einsum(
        "hqk,khd->qhd",
        local_probs.astype(jnp.bfloat16),
        values_all,
        preferred_element_type=jnp.float32,
    )
    requests, places = place_requests(slot_shard, slot_index, groups, capacity, heads)
    entry_shape = (rows, heads, top_count)
    fetched = fetch_rows(requests, places, memory_keys, memory_values, heads, entry_shape)
    live_mask = slot_live > 0
    mem_probs = memory_probs(queries, fetched[..., 0, :], live_mask, score_scale)
    memory_out = jnp.einsum(
        "qhk,qhkd->qhd",
        mem_probs.astype(jnp.bfloat16),
        fetched[..., 1, :],
        preferred_element_type=jnp.float32,
    )
    gate_share = jax.nn.sigmoid(gate_logit)[:, None]
    mixed_heads = (
        (gate_share * memory_out + (1.0 - gate_share) * local_out)
        .reshape(rows, width)
        .astype(jnp.bfloat16)
    )
    residual = tokens_f + jnp.dot(mixed_heads, out_weight, preferred_element_type=jnp.float32)
    normed_mid_f, norm_mid_back = jax.vjp(normed, residual, ffn_gain)
    normed_mid = normed_mid_f.astype(jnp.bfloat16)
    up_proj = jnp.dot(normed_mid, up_weight, preferred_element_type=jnp.float32)
    activated_f, gelu_back = jax.vjp(gelu_exact, up_proj)
    activated = activated_f.astype(jnp.bfloat16)
    ffn_branch = lax.dot_general(
        activated, down_weight, contract_cols, preferred_element_type=jnp.float32
    )
    block_out = (residual + ffn_branch).astype(jnp.bfloat16)
    d_act = jnp.dot(cotangent, down_weight, preferred_element_type=jnp.float32)
    d_up = gelu_back(d_act)[0].astype(jnp.bfloat16)
    d_mid = lax.dot_general(d_up, up_weight, contract_cols, preferred_element_type=jnp.float32)
    d_resid_part, ffn_gain_part = norm_mid_back(d_mid)
    d_residual = cotangent.astype(jnp.float32) + d_resid_part
    d_branch = d_residual.astype(jnp.bfloat16)
    d_mixed = lax.dot_general(
        d_branch, out_weight, contract_cols, preferred_element_type=jnp.float32
    ).reshape(rows, heads, head_dim)
    gate_part = (
        jnp.sum(d_mixed * (memory_out - local_out), axis=(0, 2))
        * (gate_share * (1.0 - gate_share))[:, 0]
    )
    d_memory = (gate_share * d_mixed).astype(jnp.bfloat16)
    d_local_out = ((1.0 - gate_share) * d_mixed).astype(jnp.bfloat16)
    probs_again = jnp.exp(local_scores() - log_total)
    d_lw = jnp.einsum("qhd,khd->hqk", d_local_out, values_all, preferred_element_type=jnp.float32)
    d_local = (probs_again * (d_lw - jnp.sum(probs_again * d_lw, axis=-1, keepdims=True))).astype(
        jnp.bfloat16
    )
    d_values_all = jnp.einsum(
        "hqk,qhd->khd",
        probs_again.astype(jnp.bfloat16),
        d_local_out,
        preferred_element_type=jnp.float32,
    )
    d_keys_all = (
        jnp.einsum("hqk,qhd->khd", d_local, queries, preferred_element_type=jnp.float32)
        * score_scale
    )
    d_queries = (
        jnp.einsum("hqk,khd->qhd", d_local, keys_all, preferred_element_type=jnp.float32)
        * score_scale
    )
    bias_part = jnp.einsum(
        "hqk,qkb->hb", d_local, one_hot_f.astype(jnp.bfloat16), preferred_element_type=jnp.float32
    )
    d_mw = jnp.einsum(
        "qhd,qhkd->qhk", d_memory, fetched[..., 1, :], preferred_element_type=jnp.float32
    )
    d_mem = (mem_probs * (d_mw - jnp.sum(mem_probs * d_mw, axis=-1, keepdims=True))).astype(
        jnp.bfloat16
    )
    d_queries = (
        d_queries
        + jnp.einsum("qhk,qhkd->qhd", d_mem, fetched[..., 0, :], preferred_element_type=jnp.float32)
        * score_scale
    )
    halo_grads = jnp.stack([d_keys_all[:W], d_values_all[:W]])
    d_tails = jnp.zeros((2, sent_rows, heads, head_dim), jnp.float32)
    for distance in range(repeats, 0, -1):
        first_row = (repeats - distance) * sent_rows
        d_tails = d_tails + passed_along(
            halo_grads[:, first_row : first_row + sent_rows].astype(jnp.bfloat16), "mem", -distance
        ).astype(jnp.float32)
    d_keys = d_keys_all[W:] + d_tails[0]
    d_values = d_values_all[W:] + d_tails[1]
    d_projected = jnp.concatenate(
        [
            d_queries.reshape(rows, width),
            d_keys.reshape(rows, width),
            d_values.reshape(rows, width),
        ],
        axis=1,
    ).astype(jnp.bfloat16)
    d_in = lax.dot_general(
        d_projected, qkv_weight, contract_cols, preferred_element_type=jnp.float32
    )
    d_tokens_part, attn_gain_part = norm_in_back(d_in)
    tokens_grad = d_residual + d_tokens_part
    core = lax.axis_index("dp")
    lefts, rights = [], []
    for left, right in (
        (normed_in, d_projected),
        (mixed_heads, d_branch),
        (normed_mid, d_up),
        (cotangent, activated),
    ):
        half = right.shape[1] // 2
        kept = lax.dynamic_slice_in_dim(right, core * half, half, 1)
        sent = lax.dynamic_slice_in_dim(right, (1 - core) * half, half, 1)
        lefts.append(left)
        rights.append((kept, sent))
    other_left = swapped(jnp.concatenate(lefts, axis=1))
    other_right = swapped(jnp.concatenate([sent for _, sent in rights], axis=1))
    partials, at = [], 0
    for i, (left, (kept, _)) in enumerate(zip(lefts, rights)):
        half = kept.shape[1]
        left_both = jnp.concatenate([left, other_left[:, i * width : (i + 1) * width]], axis=0)
        right_both = jnp.concatenate([kept, other_right[:, at : at + half]], axis=0)
        at += half
        partials.append(
            lax.dot_general(
                left_both, right_both, contract_rows, preferred_element_type=jnp.float32
            ).astype(jnp.bfloat16)
        )
    summed = lax.psum_scatter(
        jnp.concatenate(partials, axis=1), "mem", scatter_dimension=0, tiled=True
    )
    halves = lax.all_gather(summed, "dp", axis=0).astype(jnp.float32)
    grads, at = [], 0
    for kept, _ in rights:
        half = kept.shape[1]
        grads.append(jnp.concatenate([halves[0, :, at : at + half], halves[1, :, at : at + half]], 1))
        at += half
    small_sums = lax.psum((attn_gain_part, ffn_gain_part, bias_part, gate_part), ("dp", "mem"))
    return (
        block_out,
        tokens_grad,
        *grads,
        small_sums[0],
        small_sums[1],
        small_sums[2],
        small_sums[3],
    )


def solution(mesh):
    in_specs = (
        P(("dp", "mem"), None),
        P(),
        P(),
        P(),
        P(),
        P(),
        P(),
        P(),
        P(),
        P("mem", None),
        P("mem", None),
        P("dp", None),
        P(("dp", "mem"), None, None, None),
        P(("dp", "mem"), None, None),
        P(("dp", "mem"), None, None),
        P(("dp", "mem"), None),
    )
    out_specs = (
        P(("dp", "mem"), None),
        P(("dp", "mem"), None),
        P("mem", None),
        P("mem", None),
        P("mem", None),
        P("mem", None),
        P(),
        P(),
        P(),
        P(),
    )
    return jax.shard_map(
        on_device, mesh=mesh, in_specs=in_specs, out_specs=out_specs, check_vma=False
    )
```

```python
import math

import jax
import jax.numpy as jnp
from jax import lax
from jax.experimental import pallas as pl
from jax.experimental.pallas import tpu as pltpu
from jax.sharding import PartitionSpec as P

W = 512
VMEM_LIMIT = 56 * 1024 * 1024


eps_norm = 1e-06
bucket_edges = tuple((math.ceil(16 * 8 ** (edge_step / 16)) for edge_step in range(1, 16)))
masked_score = -1e30
dead_score = -10000.0
contract_rows = (((0,), (0,)), ((), ()))
contract_cols = (((1,), (1,)), ((), ()))


def passed_along(value, axis, by):
    size = lax.axis_size(axis)
    pairs = [(i, i + by) for i in range(size) if 0 <= i + by < size]
    return lax.ppermute(value, axis, pairs)


def swapped(value):
    return lax.ppermute(value, "dp", [(0, 1), (1, 0)])


def bucket_of(offset):
    past_edges = sum(((offset >= edge_pos).astype(jnp.int32) for edge_pos in bucket_edges))
    return jnp.where(offset < 16, offset, 16 + past_edges)


def normed(values, gain_vec):
    return (
        values * lax.rsqrt(jnp.mean(values * values, axis=-1, keepdims=True) + eps_norm) * gain_vec
    )


def gelu_exact(values):
    return jax.nn.gelu(values, approximate=False)


def book_of(positions, lengths):
    book_ends = jnp.cumsum(lengths, dtype=jnp.int32)
    return jnp.sum((positions[..., None] >= book_ends).astype(jnp.int32), axis=-1)


def place_requests(slot_shard, slot_index, slot_live, owners, capacity, slots):
    rows, heads, top_count = slot_index.shape
    entries = rows * heads * top_count
    row_of = (
        jnp.arange(heads, dtype=jnp.int32)[None, :] * rows
        + jnp.arange(rows, dtype=jnp.int32)[:, None]
    )
    place = row_of[:, :, None] * top_count + jnp.arange(top_count, dtype=jnp.int32)
    owner = jnp.where(slot_live > 0, slot_shard[..., 0], owners)
    keys, picked = lax.sort(
        ((owner * entries + place).reshape(-1), slot_index.reshape(-1)), num_keys=1
    )
    ends = jnp.sum(
        (keys[None, :] < (jnp.arange(owners, dtype=jnp.int32) + 1)[:, None] * entries).astype(jnp.int32),
        axis=1,
    )
    starts = jnp.concatenate([jnp.zeros((1,), jnp.int32), ends[:-1]])
    codes = jnp.concatenate(
        [(keys % entries) // top_count * slots + picked, jnp.zeros((capacity,), jnp.int32)]
    )
    lists = jnp.stack(
        [lax.dynamic_slice_in_dim(codes, starts[i], capacity) for i in range(owners)]
    )
    used = jnp.arange(capacity, dtype=jnp.int32)[None, :] < (ends - starts)[:, None]
    return jnp.where(used, lists, heads * rows * slots)


def split3(stat):
    high = lax.reduce_precision(stat, 8, 7)
    middle = lax.reduce_precision(stat - high, 8, 7)
    return jnp.concatenate([high, middle, stat - high - middle], axis=1).astype(jnp.bfloat16)


def gather_rows(index, counts, memory_keys, memory_values, heads, sources, capacity):
    slots, width = memory_keys.shape
    head_dim = width // heads
    step = 16

    def kernel(index_ref, counts_ref, keys, values, out_keys, out_values, key_table, value_table, key_rows, value_rows):
        i = pl.program_id(0)

        @pl.when(i == 0)
        def _():
            key_rows[...] = jnp.zeros_like(key_rows)
            value_rows[...] = jnp.zeros_like(value_rows)

        @pl.when(i < heads)
        def _():
            place = pl.ds(pl.multiple_of(i * slots, slots), slots)
            key_table[place, :] = keys[...].astype(jnp.float32)
            value_table[place, :] = values[...].astype(jnp.float32)

        @pl.when(i >= heads)
        def _():
            source = i - heads

            @pl.loop(0, (counts_ref[source] + step - 1) // step)
            def _(group):
                first = pl.multiple_of(group * step, step)
                for u in range(step):
                    row = index_ref[source * capacity + first + u]
                    key_rows[pl.ds(first + u, 1), :] = key_table[pl.ds(row, 1), :]
                    value_rows[pl.ds(first + u, 1), :] = value_table[pl.ds(row, 1), :]

            out_keys[...] = key_rows[...].astype(jnp.bfloat16)
            out_values[...] = value_rows[...].astype(jnp.bfloat16)

    table_spec = pl.BlockSpec((slots, head_dim), lambda i, *_: (0, jnp.minimum(i, heads - 1)))
    out_spec = pl.BlockSpec((capacity, head_dim), lambda i, *_: (jnp.maximum(i - heads, 0), 0))
    out_shape = jax.ShapeDtypeStruct((sources * capacity, head_dim), jnp.bfloat16)
    return pl.pallas_call(
        kernel,
        grid_spec=pltpu.PrefetchScalarGridSpec(
            num_scalar_prefetch=2,
            grid=(heads + sources,),
            in_specs=[table_spec, table_spec],
            out_specs=[out_spec, out_spec],
            scratch_shapes=[
                pltpu.VMEM((heads * slots, head_dim), jnp.float32),
                pltpu.VMEM((heads * slots, head_dim), jnp.float32),
                pltpu.VMEM((capacity, head_dim), jnp.float32),
                pltpu.VMEM((capacity, head_dim), jnp.float32),
            ],
        ),
        out_shape=[out_shape, out_shape],
        compiler_params=pltpu.CompilerParams(vmem_limit_bytes=VMEM_LIMIT),
        name="gather_rows",
    )(index, counts, memory_keys, memory_values)


def triple(stat):
    part = lax.broadcasted_iota(jnp.int32, stat.shape, 1) // 16
    high = stat.astype(jnp.bfloat16).astype(jnp.float32)
    rest = stat - high
    middle = rest.astype(jnp.bfloat16).astype(jnp.float32)
    low = rest - middle
    chosen = jnp.where(part == 0, high, jnp.where(part == 1, middle, jnp.where(part == 2, low, 0.0)))
    return chosen.astype(jnp.bfloat16)


def window_of(bounds, source, head, heads, span, capacity):
    first = bounds[source * (heads + 1) + head]
    last = bounds[source * (heads + 1) + head + 1]
    start = jnp.minimum((first // 128) * 128, capacity - span)
    extra = jnp.maximum(last - start - span + span - 1, 0) // span
    return start, extra


def memory_forward(bounds, queries, key_rows, value_rows, row_ids, heads, sources, rows, score_scale):
    capacity, head_dim = key_rows.shape[0] // sources, key_rows.shape[1]
    width = heads * head_dim
    span = min(512, capacity)

    def kernel(bounds_ref, q_ref, k_ref, v_ref, id_ref, out_ref, sums, tops, totals):
        source = pl.program_id(0)
        token = lax.broadcasted_iota(jnp.int32, (rows, span), 0)
        lane = lax.broadcasted_iota(jnp.int32, (rows, 128), 1) % 16

        def scores_of(head, start, least):
            here = pl.ds(pl.multiple_of(start, 128), span)
            ids = id_ref[0, :, here]
            mine = ids == token + head * rows
            if least is not None:
                place = lax.broadcasted_iota(jnp.int32, (1, span), 1) + start
                mine = mine & (place >= least)
            q = q_ref[:, head * head_dim : (head + 1) * head_dim]
            raw = lax.dot_general(q, k_ref[here, :], contract_cols, preferred_element_type=jnp.float32)
            return jnp.where(mine, raw * score_scale, masked_score), mine, v_ref[here, :]

        windows = [window_of(bounds_ref, source, head, heads, span, capacity) for head in range(heads)]
        top_tile = jnp.zeros((rows, 128), jnp.float32)
        total_tile = jnp.zeros((rows, 128), jnp.float32)
        for head in range(heads):
            scores, mine, v = scores_of(head, windows[head][0], None)
            top = jnp.max(scores, axis=1, keepdims=True)
            weights = jnp.where(mine, jnp.exp(scores - top), 0.0)
            sums[:, head * head_dim : (head + 1) * head_dim] = jnp.dot(
                weights.astype(jnp.bfloat16), v, preferred_element_type=jnp.float32
            )
            top_tile = jnp.where(lane == head, top, top_tile)
            total_tile = jnp.where(
                lane == heads + head, jnp.sum(weights, axis=1, keepdims=True), total_tile
            )
        tops[...] = top_tile
        totals[...] = total_tile
        more = sum(extra for _, extra in windows)

        @pl.when(more > 0)
        def _():
            for head in range(heads):
                start, extra = windows[head]
                columns = slice(head * head_dim, (head + 1) * head_dim)

                @pl.loop(0, extra)
                def _(turn):
                    least = start + (turn + 1) * span
                    scores, mine, v = scores_of(head, jnp.minimum(least, capacity - span), least)
                    old_top = jnp.max(
                        jnp.where(lane == head, tops[...], masked_score), axis=1, keepdims=True
                    )
                    top = jnp.maximum(old_top, jnp.max(scores, axis=1, keepdims=True))
                    weights = jnp.where(mine, jnp.exp(scores - top), 0.0)
                    faded = jnp.exp(old_top - top)
                    sums[:, columns] = sums[:, columns] * faded + jnp.dot(
                        weights.astype(jnp.bfloat16), v, preferred_element_type=jnp.float32
                    )
                    tops[...] = jnp.where(lane == head, top, tops[...])
                    totals[...] = jnp.where(
                        lane == heads + head,
                        totals[...] * faded + jnp.sum(weights, axis=1, keepdims=True),
                        totals[...],
                    )

        out_ref[:, :width] = sums[...].astype(jnp.bfloat16)
        out_ref[:, width:] = triple(jnp.where(lane < heads, tops[...], totals[...]))

    return pl.pallas_call(
        kernel,
        grid_spec=pltpu.PrefetchScalarGridSpec(
            num_scalar_prefetch=1,
            grid=(sources,),
            in_specs=[
                pl.BlockSpec((rows, width), lambda i, *_: (i, 0)),
                pl.BlockSpec((capacity, head_dim), lambda i, *_: (i, 0)),
                pl.BlockSpec((capacity, head_dim), lambda i, *_: (i, 0)),
                pl.BlockSpec((1, 1, capacity), lambda i, *_: (i, 0, 0)),
            ],
            out_specs=pl.BlockSpec((rows, width + 128), lambda i, *_: (i, 0)),
            scratch_shapes=[
                pltpu.VMEM((rows, width), jnp.float32),
                pltpu.VMEM((rows, 128), jnp.float32),
                pltpu.VMEM((rows, 128), jnp.float32),
            ],
        ),
        out_shape=jax.ShapeDtypeStruct((sources * rows, width + 128), jnp.bfloat16),
        compiler_params=pltpu.CompilerParams(vmem_limit_bytes=VMEM_LIMIT),
        name="memory_forward",
    )(bounds, queries, key_rows, value_rows, row_ids)


def combine_partials(partial, heads, sources, rows):
    width = partial.shape[1] - 128
    head_dim = width // heads

    def kernel(part_ref, out_ref, log_ref, sums, tops, totals):
        i = pl.program_id(0)

        @pl.when(i == 0)
        def _():
            sums[...] = jnp.zeros_like(sums)
            tops[...] = jnp.full_like(tops, masked_score)
            totals[...] = jnp.zeros_like(totals)

        stat = part_ref[:, width:].astype(jnp.float32)
        stat = stat + pltpu.roll(stat, 128 - 16, 1) + pltpu.roll(stat, 128 - 32, 1)
        new_total = pltpu.roll(stat, 128 - heads, 1)
        top = jnp.maximum(tops[...], stat)
        old_fade, new_fade = jnp.exp(tops[...] - top), jnp.exp(stat - top)
        tops[...] = top
        totals[...] = totals[...] * old_fade + new_total * new_fade
        for head in range(heads):
            columns = slice(head * head_dim, (head + 1) * head_dim)
            sums[:, columns] = (
                sums[:, columns] * old_fade[:, head : head + 1]
                + part_ref[:, columns].astype(jnp.float32) * new_fade[:, head : head + 1]
            )

        @pl.when(i == sources - 1)
        def _():
            live = totals[...] > 0
            total = jnp.where(live, totals[...], 1.0)
            log_ref[...] = jnp.where(live, tops[...] + jnp.log(total), 0.0)
            for head in range(heads):
                columns = slice(head * head_dim, (head + 1) * head_dim)
                out_ref[:, columns] = sums[:, columns] / total[:, head : head + 1]

    return pl.pallas_call(
        kernel,
        grid=(sources,),
        in_specs=[pl.BlockSpec((rows, width + 128), lambda i: (i, 0))],
        out_specs=[
            pl.BlockSpec((rows, width), lambda i: (0, 0)),
            pl.BlockSpec((rows, 128), lambda i: (0, 0)),
        ],
        scratch_shapes=[
            pltpu.VMEM((rows, width), jnp.float32),
            pltpu.VMEM((rows, 128), jnp.float32),
            pltpu.VMEM((rows, 128), jnp.float32),
        ],
        out_shape=[
            jax.ShapeDtypeStruct((rows, width), jnp.float32),
            jax.ShapeDtypeStruct((rows, 128), jnp.float32),
        ],
        compiler_params=pltpu.CompilerParams(vmem_limit_bytes=VMEM_LIMIT),
        name="combine_partials",
    )(partial)


def memory_backward(bounds, queries, grads, key_rows, value_rows, row_ids, heads, sources, rows, score_scale):
    capacity, head_dim = key_rows.shape[0] // sources, key_rows.shape[1]
    width = heads * head_dim
    span = min(512, capacity)

    def kernel(bounds_ref, q_ref, g_ref, k_ref, v_ref, id_ref, out_ref, sums):
        source = pl.program_id(0)
        token = lax.broadcasted_iota(jnp.int32, (rows, span), 0)
        stat = g_ref[:, width : width + 128].astype(jnp.float32)

        def term(column):
            return (
                stat[:, column : column + 1]
                + stat[:, column + 16 : column + 17]
                + stat[:, column + 32 : column + 33]
            )

        def part_of(head, start, least):
            here = pl.ds(pl.multiple_of(start, 128), span)
            columns = slice(head * head_dim, (head + 1) * head_dim)
            mine = id_ref[0, :, here] == token + head * rows
            if least is not None:
                place = lax.broadcasted_iota(jnp.int32, (1, span), 1) + start
                mine = mine & (place >= least)
            k, v = k_ref[here, :], v_ref[here, :]
            raw = lax.dot_general(
                q_ref[:, columns], k, contract_cols, preferred_element_type=jnp.float32
            )
            products = lax.dot_general(
                g_ref[:, columns], v, contract_cols, preferred_element_type=jnp.float32
            )
            probs = jnp.exp(jnp.where(mine, raw * score_scale - term(head), dead_score))
            slopes = (probs * (products - term(heads + head))).astype(jnp.bfloat16)
            return jnp.dot(slopes, k, preferred_element_type=jnp.float32)

        windows = [window_of(bounds_ref, source, head, heads, span, capacity) for head in range(heads)]
        for head in range(heads):
            sums[:, head * head_dim : (head + 1) * head_dim] = part_of(head, windows[head][0], None)
        more = sum(extra for _, extra in windows)

        @pl.when(more > 0)
        def _():
            for head in range(heads):
                start, extra = windows[head]
                columns = slice(head * head_dim, (head + 1) * head_dim)

                @pl.loop(0, extra)
                def _(turn):
                    least = start + (turn + 1) * span
                    sums[:, columns] += part_of(head, jnp.minimum(least, capacity - span), least)

        out_ref[...] = sums[...].astype(jnp.bfloat16)

    return pl.pallas_call(
        kernel,
        grid_spec=pltpu.PrefetchScalarGridSpec(
            num_scalar_prefetch=1,
            grid=(sources,),
            in_specs=[
                pl.BlockSpec((rows, width), lambda i, *_: (i, 0)),
                pl.BlockSpec((rows, width + 128), lambda i, *_: (i, 0)),
                pl.BlockSpec((capacity, head_dim), lambda i, *_: (i, 0)),
                pl.BlockSpec((capacity, head_dim), lambda i, *_: (i, 0)),
                pl.BlockSpec((1, 1, capacity), lambda i, *_: (i, 0, 0)),
            ],
            out_specs=pl.BlockSpec((rows, width), lambda i, *_: (i, 0)),
            scratch_shapes=[pltpu.VMEM((rows, width), jnp.float32)],
        ),
        out_shape=jax.ShapeDtypeStruct((sources * rows, width), jnp.bfloat16),
        compiler_params=pltpu.CompilerParams(vmem_limit_bytes=VMEM_LIMIT),
        name="memory_backward",
    )(bounds, queries, grads, key_rows, value_rows, row_ids)


def on_device(
    tokens,
    attn_gain,
    qkv_weight,
    out_weight,
    bias_table,
    gate_logit,
    ffn_gain,
    up_weight,
    down_weight,
    memory_keys,
    memory_values,
    book_lengths,
    slot_shard,
    slot_index,
    slot_live,
    cotangent,
):
    rows, width = tokens.shape
    heads, buckets = bias_table.shape
    head_dim = width // heads
    top_count = slot_index.shape[2]
    hidden = up_weight.shape[1]
    groups = lax.axis_size("mem")
    capacity = max(2, 3 * rows * heads * top_count // (2 * groups))
    score_scale = 1.0 / math.sqrt(head_dim)
    sent_rows = min(W, rows)
    repeats = W // sent_rows
    first_pos = lax.axis_index("mem") * rows
    query_pos = first_pos + jnp.arange(rows, dtype=jnp.int32)
    key_pos = first_pos - W + jnp.arange(W + rows, dtype=jnp.int32)
    lengths = book_lengths[0]
    query_book = book_of(query_pos, lengths)
    key_book = jnp.where(key_pos >= 0, book_of(key_pos, lengths), -1)
    offset = (
        jnp.arange(rows, dtype=jnp.int32)[:, None]
        + W
        - jnp.arange(W + rows, dtype=jnp.int32)[None, :]
    )
    allowed = (offset >= 0) & (offset < W) & (query_book[:, None] == key_book[None, :])
    bucket = bucket_of(jnp.maximum(offset, 0))
    one_hot_f = (bucket[:, :, None] == jnp.arange(buckets, dtype=jnp.int32)).astype(jnp.float32)
    score_bias = jnp.einsum("qkb,hb->hqk", one_hot_f, bias_table, precision=lax.Precision.HIGHEST)
    tokens_f = tokens.astype(jnp.float32)
    normed_f, norm_in_back = jax.vjp(normed, tokens_f, attn_gain)
    normed_in = normed_f.astype(jnp.bfloat16)
    projected = jnp.dot(normed_in, qkv_weight, preferred_element_type=jnp.float32).astype(
        jnp.bfloat16
    )
    queries = projected[:, :width].reshape(rows, heads, head_dim)
    keys_own = projected[:, width : 2 * width].reshape(rows, heads, head_dim)
    values_own = projected[:, 2 * width :].reshape(rows, heads, head_dim)
    tail_rows = jnp.stack([keys_own, values_own])
    received = []
    for distance in range(repeats, 0, -1):
        received.append(passed_along(tail_rows, "mem", distance))
    halo_rows = jnp.concatenate(received, axis=1)
    keys_all = jnp.concatenate([halo_rows[0], keys_own], axis=0)
    values_all = jnp.concatenate([halo_rows[1], values_own], axis=0)

    def local_scores():
        raw_scores = (
            jnp.einsum("qhd,khd->hqk", queries, keys_all, preferred_element_type=jnp.float32)
            * score_scale
            + score_bias
        )
        return jnp.where(allowed[None], raw_scores, masked_score)

    scores = local_scores()
    row_max = jnp.max(scores, axis=-1, keepdims=True)
    exp_scores = jnp.exp(scores - row_max)
    sums_local = jnp.sum(exp_scores, axis=-1, keepdims=True)
    local_probs = exp_scores / sums_local
    log_total = row_max + jnp.log(sums_local)
    local_out = jnp.einsum(
        "hqk,khd->qhd",
        local_probs.astype(jnp.bfloat16),
        values_all,
        preferred_element_type=jnp.float32,
    )
    slots = memory_keys.shape[0]
    requests = place_requests(slot_shard, slot_index, slot_live, groups, capacity, slots)
    incoming = lax.all_to_all(requests, "mem", split_axis=0, concat_axis=0, tiled=True)
    row_ids = incoming // slots
    limits = jnp.arange(heads + 1, dtype=jnp.int32) * (rows * slots)
    bounds = jnp.sum((incoming[:, None, :] < limits[None, :, None]).astype(jnp.int32), axis=2)
    index = jnp.where(row_ids < heads * rows, row_ids // rows * slots + incoming % slots, 0)
    key_rows, value_rows = gather_rows(
        index.reshape(-1), bounds[:, heads], memory_keys, memory_values, heads, groups, capacity
    )
    all_queries = lax.all_gather(projected[:, :width], "mem", axis=0, tiled=True)
    entry_rows = row_ids[:, None, :]
    partial = memory_forward(
        bounds.reshape(-1),
        all_queries,
        key_rows,
        value_rows,
        entry_rows,
        heads,
        groups,
        rows,
        score_scale,
    )
    partial = lax.all_to_all(
        partial.reshape(groups, rows, width + 128), "mem", split_axis=0, concat_axis=0, tiled=True
    )
    memory_out, mem_log = combine_partials(
        partial.reshape(groups * rows, width + 128), heads, groups, rows
    )
    memory_out = memory_out.reshape(rows, heads, head_dim)
    gate_share = jax.nn.sigmoid(gate_logit)[:, None]
    mixed_heads = (
        (gate_share * memory_out + (1.0 - gate_share) * local_out)
        .reshape(rows, width)
        .astype(jnp.bfloat16)
    )
    residual = tokens_f + jnp.dot(mixed_heads, out_weight, preferred_element_type=jnp.float32)
    normed_mid_f, norm_mid_back = jax.vjp(normed, residual, ffn_gain)
    normed_mid = normed_mid_f.astype(jnp.bfloat16)
    up_proj = jnp.dot(normed_mid, up_weight, preferred_element_type=jnp.float32)
    activated_f, gelu_back = jax.vjp(gelu_exact, up_proj)
    activated = activated_f.astype(jnp.bfloat16)
    ffn_branch = lax.dot_general(
        activated, down_weight, contract_cols, preferred_element_type=jnp.float32
    )
    block_out = (residual + ffn_branch).astype(jnp.bfloat16)
    d_act = jnp.dot(cotangent, down_weight, preferred_element_type=jnp.float32)
    d_up = gelu_back(d_act)[0].astype(jnp.bfloat16)
    d_mid = lax.dot_general(d_up, up_weight, contract_cols, preferred_element_type=jnp.float32)
    d_resid_part, ffn_gain_part = norm_mid_back(d_mid)
    d_residual = cotangent.astype(jnp.float32) + d_resid_part
    d_branch = d_residual.astype(jnp.bfloat16)
    d_mixed = lax.dot_general(
        d_branch, out_weight, contract_cols, preferred_element_type=jnp.float32
    ).reshape(rows, heads, head_dim)
    gate_part = (
        jnp.sum(d_mixed * (memory_out - local_out), axis=(0, 2))
        * (gate_share * (1.0 - gate_share))[:, 0]
    )
    d_memory = (gate_share * d_mixed).astype(jnp.bfloat16)
    d_local_out = ((1.0 - gate_share) * d_mixed).astype(jnp.bfloat16)
    probs_again = jnp.exp(local_scores() - log_total)
    d_lw = jnp.einsum("qhd,khd->hqk", d_local_out, values_all, preferred_element_type=jnp.float32)
    d_local = (probs_again * (d_lw - jnp.sum(probs_again * d_lw, axis=-1, keepdims=True))).astype(
        jnp.bfloat16
    )
    d_values_all = jnp.einsum(
        "hqk,qhd->khd",
        probs_again.astype(jnp.bfloat16),
        d_local_out,
        preferred_element_type=jnp.float32,
    )
    d_keys_all = (
        jnp.einsum("hqk,qhd->khd", d_local, queries, preferred_element_type=jnp.float32)
        * score_scale
    )
    d_queries = (
        jnp.einsum("hqk,khd->qhd", d_local, keys_all, preferred_element_type=jnp.float32)
        * score_scale
    )
    bias_part = jnp.einsum(
        "hqk,qkb->hb", d_local, one_hot_f.astype(jnp.bfloat16), preferred_element_type=jnp.float32
    )
    mem_delta = jnp.sum(d_memory.astype(jnp.float32) * memory_out, axis=-1)
    sent_grads = jnp.concatenate(
        [
            d_memory.reshape(rows, width),
            split3(jnp.concatenate([mem_log[:, :heads], mem_delta], axis=1)),
            jnp.zeros((rows, 80), jnp.bfloat16),
        ],
        axis=1,
    )
    all_grads = lax.all_gather(sent_grads, "mem", axis=0, tiled=True)
    d_partial = memory_backward(
        bounds.reshape(-1),
        all_queries,
        all_grads,
        key_rows,
        value_rows,
        entry_rows,
        heads,
        groups,
        rows,
        score_scale,
    )
    d_partial = lax.all_to_all(
        d_partial.reshape(groups, rows, width), "mem", split_axis=0, concat_axis=0, tiled=True
    )
    d_queries = (
        d_queries
        + jnp.sum(d_partial.astype(jnp.float32), axis=0).reshape(rows, heads, head_dim) * score_scale
    )
    halo_grads = jnp.stack([d_keys_all[:W], d_values_all[:W]])
    d_tails = jnp.zeros((2, sent_rows, heads, head_dim), jnp.float32)
    for distance in range(repeats, 0, -1):
        first_row = (repeats - distance) * sent_rows
        d_tails = d_tails + passed_along(
            halo_grads[:, first_row : first_row + sent_rows].astype(jnp.bfloat16), "mem", -distance
        ).astype(jnp.float32)
    d_keys = d_keys_all[W:] + d_tails[0]
    d_values = d_values_all[W:] + d_tails[1]
    d_projected = jnp.concatenate(
        [
            d_queries.reshape(rows, width),
            d_keys.reshape(rows, width),
            d_values.reshape(rows, width),
        ],
        axis=1,
    ).astype(jnp.bfloat16)
    d_in = lax.dot_general(
        d_projected, qkv_weight, contract_cols, preferred_element_type=jnp.float32
    )
    d_tokens_part, attn_gain_part = norm_in_back(d_in)
    tokens_grad = d_residual + d_tokens_part
    core = lax.axis_index("dp")
    lefts, rights = [], []
    for left, right in (
        (normed_in, d_projected),
        (mixed_heads, d_branch),
        (normed_mid, d_up),
        (cotangent, activated),
    ):
        half = right.shape[1] // 2
        kept = lax.dynamic_slice_in_dim(right, core * half, half, 1)
        sent = lax.dynamic_slice_in_dim(right, (1 - core) * half, half, 1)
        lefts.append(left)
        rights.append((kept, sent))
    other_left = swapped(jnp.concatenate(lefts, axis=1))
    other_right = swapped(jnp.concatenate([sent for _, sent in rights], axis=1))
    partials, at = [], 0
    for i, (left, (kept, _)) in enumerate(zip(lefts, rights)):
        half = kept.shape[1]
        left_both = jnp.concatenate([left, other_left[:, i * width : (i + 1) * width]], axis=0)
        right_both = jnp.concatenate([kept, other_right[:, at : at + half]], axis=0)
        at += half
        partials.append(
            lax.dot_general(
                left_both, right_both, contract_rows, preferred_element_type=jnp.float32
            ).astype(jnp.bfloat16)
        )
    summed = lax.psum_scatter(
        jnp.concatenate(partials, axis=1), "mem", scatter_dimension=0, tiled=True
    )
    halves = lax.all_gather(summed, "dp", axis=0).astype(jnp.float32)
    grads, at = [], 0
    for kept, _ in rights:
        half = kept.shape[1]
        grads.append(jnp.concatenate([halves[0, :, at : at + half], halves[1, :, at : at + half]], 1))
        at += half
    small_sums = lax.psum((attn_gain_part, ffn_gain_part, bias_part, gate_part), ("dp", "mem"))
    return (
        block_out,
        tokens_grad,
        *grads,
        small_sums[0],
        small_sums[1],
        small_sums[2],
        small_sums[3],
    )


def solution(mesh):
    in_specs = (
        P(("dp", "mem"), None),
        P(),
        P(),
        P(),
        P(),
        P(),
        P(),
        P(),
        P(),
        P("mem", None),
        P("mem", None),
        P("dp", None),
        P(("dp", "mem"), None, None, None),
        P(("dp", "mem"), None, None),
        P(("dp", "mem"), None, None),
        P(("dp", "mem"), None),
    )
    out_specs = (
        P(("dp", "mem"), None),
        P(("dp", "mem"), None),
        P("mem", None),
        P("mem", None),
        P("mem", None),
        P("mem", None),
        P(),
        P(),
        P(),
        P(),
    )
    return jax.shard_map(
        on_device, mesh=mesh, in_specs=in_specs, out_specs=out_specs, check_vma=False
    )
```

```python
import math

import jax
import jax.numpy as jnp
from jax import lax
from jax.experimental import pallas as pl
from jax.experimental.pallas import tpu as pltpu
from jax.sharding import PartitionSpec as P

W = 512
VMEM_LIMIT = 56 * 1024 * 1024


eps_norm = 1e-06
bucket_edges = tuple((math.ceil(16 * 8 ** (edge_step / 16)) for edge_step in range(1, 16)))
masked_score = -1e30
dead_score = -10000.0
contract_rows = (((0,), (0,)), ((), ()))
contract_cols = (((1,), (1,)), ((), ()))


def passed_along(value, axis, by):
    size = lax.axis_size(axis)
    pairs = [(i, i + by) for i in range(size) if 0 <= i + by < size]
    return lax.ppermute(value, axis, pairs)


def swapped(value):
    return lax.ppermute(value, "dp", [(0, 1), (1, 0)])


def bucket_of(offset):
    past_edges = sum(((offset >= edge_pos).astype(jnp.int32) for edge_pos in bucket_edges))
    return jnp.where(offset < 16, offset, 16 + past_edges)


def normed(values, gain_vec):
    return (
        values * lax.rsqrt(jnp.mean(values * values, axis=-1, keepdims=True) + eps_norm) * gain_vec
    )


def gelu_exact(values):
    return jax.nn.gelu(values, approximate=False)


def book_of(positions, lengths):
    book_ends = jnp.cumsum(lengths, dtype=jnp.int32)
    return jnp.sum((positions[..., None] >= book_ends).astype(jnp.int32), axis=-1)


def place_requests(slot_shard, slot_index, slot_live, owners, capacity, slots):
    rows, heads, top_count = slot_index.shape
    entries = rows * heads * top_count
    row_of = (
        jnp.arange(heads, dtype=jnp.int32)[None, :] * rows
        + jnp.arange(rows, dtype=jnp.int32)[:, None]
    )
    place = row_of[:, :, None] * top_count + jnp.arange(top_count, dtype=jnp.int32)
    owner = jnp.where(slot_live > 0, slot_shard[..., 0], owners)
    keys, picked = lax.sort(
        ((owner * entries + place).reshape(-1), slot_index.reshape(-1)), num_keys=1
    )
    ends = jnp.sum(
        (keys[None, :] < (jnp.arange(owners, dtype=jnp.int32) + 1)[:, None] * entries).astype(jnp.int32),
        axis=1,
    )
    starts = jnp.concatenate([jnp.zeros((1,), jnp.int32), ends[:-1]])
    codes = jnp.concatenate(
        [(keys % entries) // top_count * slots + picked, jnp.zeros((capacity,), jnp.int32)]
    )
    lists = jnp.stack(
        [lax.dynamic_slice_in_dim(codes, starts[i], capacity) for i in range(owners)]
    )
    used = jnp.arange(capacity, dtype=jnp.int32)[None, :] < (ends - starts)[:, None]
    return jnp.where(used, lists, heads * rows * slots)


def split3(stat):
    high = lax.reduce_precision(stat, 8, 7)
    middle = lax.reduce_precision(stat - high, 8, 7)
    return jnp.concatenate([high, middle, stat - high - middle], axis=1).astype(jnp.bfloat16)


def gather_rows(index, counts, memory_keys, memory_values, heads, sources, capacity):
    slots, width = memory_keys.shape
    head_dim = width // heads
    step = 16

    def kernel(index_ref, counts_ref, keys, values, out_keys, out_values, key_table, value_table, key_rows, value_rows):
        i = pl.program_id(0)

        @pl.when(i == 0)
        def _():
            key_rows[...] = jnp.zeros_like(key_rows)
            value_rows[...] = jnp.zeros_like(value_rows)

        @pl.when(i < heads)
        def _():
            place = pl.ds(pl.multiple_of(i * slots, slots), slots)
            key_table[place, :] = keys[...].astype(jnp.float32)
            value_table[place, :] = values[...].astype(jnp.float32)

        @pl.when(i >= heads)
        def _():
            source = i - heads

            @pl.loop(0, (counts_ref[source] + step - 1) // step)
            def _(group):
                first = pl.multiple_of(group * step, step)
                for u in range(step):
                    row = index_ref[source * capacity + first + u]
                    key_rows[pl.ds(first + u, 1), :] = key_table[pl.ds(row, 1), :]
                    value_rows[pl.ds(first + u, 1), :] = value_table[pl.ds(row, 1), :]

            out_keys[...] = key_rows[...].astype(jnp.bfloat16)
            out_values[...] = value_rows[...].astype(jnp.bfloat16)

    table_spec = pl.BlockSpec((slots, head_dim), lambda i, *_: (0, jnp.minimum(i, heads - 1)))
    out_spec = pl.BlockSpec((capacity, head_dim), lambda i, *_: (jnp.maximum(i - heads, 0), 0))
    out_shape = jax.ShapeDtypeStruct((sources * capacity, head_dim), jnp.bfloat16)
    return pl.pallas_call(
        kernel,
        grid_spec=pltpu.PrefetchScalarGridSpec(
            num_scalar_prefetch=2,
            grid=(heads + sources,),
            in_specs=[table_spec, table_spec],
            out_specs=[out_spec, out_spec],
            scratch_shapes=[
                pltpu.VMEM((heads * slots, head_dim), jnp.float32),
                pltpu.VMEM((heads * slots, head_dim), jnp.float32),
                pltpu.VMEM((capacity, head_dim), jnp.float32),
                pltpu.VMEM((capacity, head_dim), jnp.float32),
            ],
        ),
        out_shape=[out_shape, out_shape],
        compiler_params=pltpu.CompilerParams(vmem_limit_bytes=VMEM_LIMIT),
        cost_estimate=lasting(42),
        name="gather_rows",
    )(index, counts, memory_keys, memory_values)


def lasting(microseconds):
    return pl.CostEstimate(flops=0, bytes_accessed=3_000_000 * microseconds, transcendentals=0)


def triple(stat):
    part = lax.broadcasted_iota(jnp.int32, stat.shape, 1) // 16
    high = stat.astype(jnp.bfloat16).astype(jnp.float32)
    rest = stat - high
    middle = rest.astype(jnp.bfloat16).astype(jnp.float32)
    low = rest - middle
    chosen = jnp.where(part == 0, high, jnp.where(part == 1, middle, jnp.where(part == 2, low, 0.0)))
    return chosen.astype(jnp.bfloat16)


def window_of(bounds, source, head, heads, span, capacity):
    first = bounds[source * (heads + 1) + head]
    last = bounds[source * (heads + 1) + head + 1]
    start = jnp.minimum((first // 128) * 128, capacity - span)
    extra = jnp.maximum(last - start - span + span - 1, 0) // span
    return start, extra


def memory_forward(bounds, queries, key_rows, value_rows, row_ids, heads, sources, rows, score_scale):
    capacity, head_dim = key_rows.shape[0] // sources, key_rows.shape[1]
    width = heads * head_dim
    span = min(512, capacity)

    def kernel(bounds_ref, q_ref, k_ref, v_ref, id_ref, out_ref, sums, tops, totals):
        source = pl.program_id(0)
        token = lax.broadcasted_iota(jnp.int32, (rows, span), 0)
        lane = lax.broadcasted_iota(jnp.int32, (rows, 128), 1) % 16

        def scores_of(head, start, least):
            here = pl.ds(pl.multiple_of(start, 128), span)
            ids = id_ref[0, :, here]
            mine = ids == token + head * rows
            if least is not None:
                place = lax.broadcasted_iota(jnp.int32, (1, span), 1) + start
                mine = mine & (place >= least)
            q = q_ref[:, head * head_dim : (head + 1) * head_dim]
            raw = lax.dot_general(q, k_ref[here, :], contract_cols, preferred_element_type=jnp.float32)
            return jnp.where(mine, raw * score_scale, masked_score), mine, v_ref[here, :]

        windows = [window_of(bounds_ref, source, head, heads, span, capacity) for head in range(heads)]
        top_tile = jnp.zeros((rows, 128), jnp.float32)
        total_tile = jnp.zeros((rows, 128), jnp.float32)
        for head in range(heads):
            scores, mine, v = scores_of(head, windows[head][0], None)
            top = jnp.max(scores, axis=1, keepdims=True)
            weights = jnp.where(mine, jnp.exp(scores - top), 0.0)
            sums[:, head * head_dim : (head + 1) * head_dim] = jnp.dot(
                weights.astype(jnp.bfloat16), v, preferred_element_type=jnp.float32
            )
            top_tile = jnp.where(lane == head, top, top_tile)
            total_tile = jnp.where(
                lane == heads + head, jnp.sum(weights, axis=1, keepdims=True), total_tile
            )
        tops[...] = top_tile
        totals[...] = total_tile
        more = sum(extra for _, extra in windows)

        @pl.when(more > 0)
        def _():
            for head in range(heads):
                start, extra = windows[head]
                columns = slice(head * head_dim, (head + 1) * head_dim)

                @pl.loop(0, extra)
                def _(turn):
                    least = start + (turn + 1) * span
                    scores, mine, v = scores_of(head, jnp.minimum(least, capacity - span), least)
                    old_top = jnp.max(
                        jnp.where(lane == head, tops[...], masked_score), axis=1, keepdims=True
                    )
                    top = jnp.maximum(old_top, jnp.max(scores, axis=1, keepdims=True))
                    weights = jnp.where(mine, jnp.exp(scores - top), 0.0)
                    faded = jnp.exp(old_top - top)
                    sums[:, columns] = sums[:, columns] * faded + jnp.dot(
                        weights.astype(jnp.bfloat16), v, preferred_element_type=jnp.float32
                    )
                    tops[...] = jnp.where(lane == head, top, tops[...])
                    totals[...] = jnp.where(
                        lane == heads + head,
                        totals[...] * faded + jnp.sum(weights, axis=1, keepdims=True),
                        totals[...],
                    )

        out_ref[:, :width] = sums[...].astype(jnp.bfloat16)
        out_ref[:, width:] = triple(jnp.where(lane < heads, tops[...], totals[...]))

    return pl.pallas_call(
        kernel,
        grid_spec=pltpu.PrefetchScalarGridSpec(
            num_scalar_prefetch=1,
            grid=(sources,),
            in_specs=[
                pl.BlockSpec((rows, width), lambda i, *_: (i, 0)),
                pl.BlockSpec((capacity, head_dim), lambda i, *_: (i, 0)),
                pl.BlockSpec((capacity, head_dim), lambda i, *_: (i, 0)),
                pl.BlockSpec((1, 1, capacity), lambda i, *_: (i, 0, 0)),
            ],
            out_specs=pl.BlockSpec((rows, width + 128), lambda i, *_: (i, 0)),
            scratch_shapes=[
                pltpu.VMEM((rows, width), jnp.float32),
                pltpu.VMEM((rows, 128), jnp.float32),
                pltpu.VMEM((rows, 128), jnp.float32),
            ],
        ),
        out_shape=jax.ShapeDtypeStruct((sources * rows, width + 128), jnp.bfloat16),
        compiler_params=pltpu.CompilerParams(vmem_limit_bytes=VMEM_LIMIT),
        cost_estimate=lasting(41),
        name="memory_forward",
    )(bounds, queries, key_rows, value_rows, row_ids)


def combine_partials(partial, heads, sources, rows):
    width = partial.shape[1] - 128
    head_dim = width // heads

    def kernel(part_ref, out_ref, log_ref, sums, tops, totals):
        i = pl.program_id(0)

        @pl.when(i == 0)
        def _():
            sums[...] = jnp.zeros_like(sums)
            tops[...] = jnp.full_like(tops, masked_score)
            totals[...] = jnp.zeros_like(totals)

        stat = part_ref[:, width:].astype(jnp.float32)
        stat = stat + pltpu.roll(stat, 128 - 16, 1) + pltpu.roll(stat, 128 - 32, 1)
        new_total = pltpu.roll(stat, 128 - heads, 1)
        top = jnp.maximum(tops[...], stat)
        old_fade, new_fade = jnp.exp(tops[...] - top), jnp.exp(stat - top)
        tops[...] = top
        totals[...] = totals[...] * old_fade + new_total * new_fade
        for head in range(heads):
            columns = slice(head * head_dim, (head + 1) * head_dim)
            sums[:, columns] = (
                sums[:, columns] * old_fade[:, head : head + 1]
                + part_ref[:, columns].astype(jnp.float32) * new_fade[:, head : head + 1]
            )

        @pl.when(i == sources - 1)
        def _():
            live = totals[...] > 0
            total = jnp.where(live, totals[...], 1.0)
            log_ref[...] = jnp.where(live, tops[...] + jnp.log(total), 0.0)
            for head in range(heads):
                columns = slice(head * head_dim, (head + 1) * head_dim)
                out_ref[:, columns] = sums[:, columns] / total[:, head : head + 1]

    return pl.pallas_call(
        kernel,
        grid=(sources,),
        in_specs=[pl.BlockSpec((rows, width + 128), lambda i: (i, 0))],
        out_specs=[
            pl.BlockSpec((rows, width), lambda i: (0, 0)),
            pl.BlockSpec((rows, 128), lambda i: (0, 0)),
        ],
        scratch_shapes=[
            pltpu.VMEM((rows, width), jnp.float32),
            pltpu.VMEM((rows, 128), jnp.float32),
            pltpu.VMEM((rows, 128), jnp.float32),
        ],
        out_shape=[
            jax.ShapeDtypeStruct((rows, width), jnp.float32),
            jax.ShapeDtypeStruct((rows, 128), jnp.float32),
        ],
        compiler_params=pltpu.CompilerParams(vmem_limit_bytes=VMEM_LIMIT),
        cost_estimate=lasting(13),
        name="combine_partials",
    )(partial)


def memory_backward(bounds, queries, grads, key_rows, value_rows, row_ids, heads, sources, rows, score_scale):
    capacity, head_dim = key_rows.shape[0] // sources, key_rows.shape[1]
    width = heads * head_dim
    span = min(512, capacity)

    def kernel(bounds_ref, q_ref, g_ref, k_ref, v_ref, id_ref, out_ref, sums):
        source = pl.program_id(0)
        token = lax.broadcasted_iota(jnp.int32, (rows, span), 0)
        stat = g_ref[:, width : width + 128].astype(jnp.float32)

        def term(column):
            return (
                stat[:, column : column + 1]
                + stat[:, column + 16 : column + 17]
                + stat[:, column + 32 : column + 33]
            )

        def part_of(head, start, least):
            here = pl.ds(pl.multiple_of(start, 128), span)
            columns = slice(head * head_dim, (head + 1) * head_dim)
            mine = id_ref[0, :, here] == token + head * rows
            if least is not None:
                place = lax.broadcasted_iota(jnp.int32, (1, span), 1) + start
                mine = mine & (place >= least)
            k, v = k_ref[here, :], v_ref[here, :]
            raw = lax.dot_general(
                q_ref[:, columns], k, contract_cols, preferred_element_type=jnp.float32
            )
            products = lax.dot_general(
                g_ref[:, columns], v, contract_cols, preferred_element_type=jnp.float32
            )
            probs = jnp.exp(jnp.where(mine, raw * score_scale - term(head), dead_score))
            slopes = (probs * (products - term(heads + head))).astype(jnp.bfloat16)
            return jnp.dot(slopes, k, preferred_element_type=jnp.float32)

        windows = [window_of(bounds_ref, source, head, heads, span, capacity) for head in range(heads)]
        for head in range(heads):
            sums[:, head * head_dim : (head + 1) * head_dim] = part_of(head, windows[head][0], None)
        more = sum(extra for _, extra in windows)

        @pl.when(more > 0)
        def _():
            for head in range(heads):
                start, extra = windows[head]
                columns = slice(head * head_dim, (head + 1) * head_dim)

                @pl.loop(0, extra)
                def _(turn):
                    least = start + (turn + 1) * span
                    sums[:, columns] += part_of(head, jnp.minimum(least, capacity - span), least)

        out_ref[...] = sums[...].astype(jnp.bfloat16)

    return pl.pallas_call(
        kernel,
        grid_spec=pltpu.PrefetchScalarGridSpec(
            num_scalar_prefetch=1,
            grid=(sources,),
            in_specs=[
                pl.BlockSpec((rows, width), lambda i, *_: (i, 0)),
                pl.BlockSpec((rows, width + 128), lambda i, *_: (i, 0)),
                pl.BlockSpec((capacity, head_dim), lambda i, *_: (i, 0)),
                pl.BlockSpec((capacity, head_dim), lambda i, *_: (i, 0)),
                pl.BlockSpec((1, 1, capacity), lambda i, *_: (i, 0, 0)),
            ],
            out_specs=pl.BlockSpec((rows, width), lambda i, *_: (i, 0)),
            scratch_shapes=[pltpu.VMEM((rows, width), jnp.float32)],
        ),
        out_shape=jax.ShapeDtypeStruct((sources * rows, width), jnp.bfloat16),
        compiler_params=pltpu.CompilerParams(vmem_limit_bytes=VMEM_LIMIT),
        cost_estimate=lasting(35),
        name="memory_backward",
    )(bounds, queries, grads, key_rows, value_rows, row_ids)


def remote(source, target, send_sem, recv_sem, device):
    return pltpu.make_async_remote_copy(
        src_ref=source,
        dst_ref=target,
        send_sem=send_sem,
        recv_sem=recv_sem,
        device_id={"mem": device},
        device_id_type=pl.DeviceIdType.MESH,
    )


def grid_place(depth):
    me = lax.axis_index("mem")
    layer, column = me // 4, me % 4
    beside_x = column + 1 - 2 * (column % 2)
    beside_y = column + 2 - 4 * (column // 2)
    across = 3 - column

    def index_of(step, place):
        return (layer + step + depth) % depth * 4 + place

    return me, column, beside_x, beside_y, across, index_of


def greet(devices):
    barrier = pltpu.get_barrier_semaphore()
    for device in devices:
        pl.semaphore_signal(
            barrier, inc=1, device_id={"mem": device}, device_id_type=pl.DeviceIdType.MESH
        )
    pl.semaphore_wait(barrier, len(devices))


def gather_group(block, sources, collective_id):
    rows, width = block.shape
    depth, half = sources // 4, rows // 2

    def kernel(x_ref, out_ref, own_sem, send, recv_z, recv_x, recv_y, recv_a, recv_b):
        me, column, beside_x, beside_y, across, index_of = grid_place(depth)
        to_x, to_y = index_of(0, beside_x), index_of(0, beside_y)
        greet([to_x, to_y] + [index_of(-k, column) for k in range(1, depth)])

        def rows_of(index, part=None):
            if part is None:
                return out_ref.at[pl.ds(pl.multiple_of(index * rows, rows), rows), :]
            return out_ref.at[pl.ds(pl.multiple_of(index * rows + part * half, half), half), :]

        own = pltpu.make_async_copy(x_ref, rows_of(me), own_sem)
        own.start()
        sent = []

        def push(source, target, kind, k, recv, device):
            copy = remote(source, target, send.at[kind, k], recv.at[k], device)
            copy.start()
            sent.append(copy)

        def arrived(target, recv, k):
            remote(target, target, send.at[0, 0], recv.at[k], to_x).wait_recv()

        push(x_ref, rows_of(me), 1, 0, recv_x, to_x)
        push(x_ref, rows_of(me), 2, 0, recv_y, to_y)
        for k in range(1, depth):
            push(x_ref, rows_of(me), 0, k, recv_z, index_of(-k, column))

        def pass_on(k):
            from_x, from_y = index_of(k, beside_x), index_of(k, beside_y)
            arrived(rows_of(from_x), recv_x, k)
            push(rows_of(from_x, 0), rows_of(from_x, 0), 3, k, recv_a, to_y)
            arrived(rows_of(from_y), recv_y, k)
            push(rows_of(from_y, 1), rows_of(from_y, 1), 4, k, recv_b, to_x)

        for k in range(1, depth):
            above = index_of(k, column)
            arrived(rows_of(above), recv_z, k)
            push(rows_of(above), rows_of(above), 1, k, recv_x, to_x)
            push(rows_of(above), rows_of(above), 2, k, recv_y, to_y)
            pass_on(k - 1)
        pass_on(depth - 1)
        for k in range(depth):
            far = index_of(k, across)
            arrived(rows_of(far, 0), recv_a, k)
            arrived(rows_of(far, 1), recv_b, k)
        for copy in sent:
            copy.wait_send()
        own.wait()

    return pl.pallas_call(
        kernel,
        in_specs=[pl.BlockSpec(memory_space=pl.ANY)],
        out_specs=pl.BlockSpec(memory_space=pl.ANY),
        out_shape=jax.ShapeDtypeStruct((sources * rows, width), block.dtype),
        scratch_shapes=[pltpu.SemaphoreType.DMA, pltpu.SemaphoreType.DMA((5, depth))]
        + [pltpu.SemaphoreType.DMA((depth,))] * 5,
        compiler_params=pltpu.CompilerParams(
            collective_id=collective_id, has_side_effects=True, vmem_limit_bytes=VMEM_LIMIT
        ),
        cost_estimate=lasting(50),
        name="gather_group",
    )(block)


def reduce_group(parts, sources, collective_id, merge, pack, finish, out_shape):
    rows, width = parts.shape[0] // sources, parts.shape[1]
    depth, half = sources // 4, rows // 2
    outs = len(out_shape)

    def kernel(parts_ref, *refs):
        out_refs = refs[:outs]
        half_a, half_b, from_x, from_y, from_z, out_x, out_y, out_z = refs[outs : outs + 8]
        send, recv_a, recv_b, recv_x, recv_y, recv_z = refs[outs + 8 :]
        me, column, beside_x, beside_y, across, index_of = grid_place(depth)
        to_x, to_y = index_of(0, beside_x), index_of(0, beside_y)
        greet([to_x, to_y] + [index_of(-k, column) for k in range(1, depth)])
        order = [*range(1, depth), 0]
        sent = []

        def piece(index, part):
            return parts_ref.at[pl.ds(pl.multiple_of(index * rows + part * half, half), half), :]

        def part_rows(part):
            return pl.ds(part * half, half)

        def push(source, target, kind, k, recv_sem, device):
            copy = remote(source, target, send.at[kind, k], recv_sem, device)
            copy.start()
            sent.append(copy)

        def arrived(target, recv_sem):
            remote(target, target, send.at[0, 0], recv_sem, to_x).wait_recv()

        for k in order:
            far = index_of(k, across)
            push(piece(far, 0), half_a.at[k], 0, k, recv_a.at[k], to_x)
            push(piece(far, 1), half_b.at[k], 1, k, recv_b.at[k], to_y)
        for k in order:
            push(piece(index_of(k, beside_x), 0), from_x.at[k, part_rows(0)], 2, k, recv_x.at[0, k], to_x)
            push(piece(index_of(k, beside_y), 1), from_y.at[k, part_rows(1)], 3, k, recv_y.at[1, k], to_y)
        for k in order:
            arrived(half_a.at[k], recv_a.at[k])
            pack(out_y.at[k], merge([piece(index_of(k, beside_y), 0), half_a.at[k]]))
            push(out_y.at[k], from_y.at[k, part_rows(0)], 4, k, recv_y.at[0, k], to_y)
            arrived(half_b.at[k], recv_b.at[k])
            pack(out_x.at[k], merge([piece(index_of(k, beside_x), 1), half_b.at[k]]))
            push(out_x.at[k], from_x.at[k, part_rows(1)], 5, k, recv_x.at[1, k], to_x)
        for k in order:
            for part in (0, 1):
                arrived(from_x.at[k, part_rows(part)], recv_x.at[part, k])
                arrived(from_y.at[k, part_rows(part)], recv_y.at[part, k])
            if k:
                for part in (0, 1):
                    here = part_rows(part)
                    blocks = [piece(index_of(k, column), part), from_x.at[k, here], from_y.at[k, here]]
                    pack(out_z.at[k, here], merge(blocks))
                push(out_z.at[k], from_z.at[k], 6, k, recv_z.at[k], index_of(k, column))
        for k in range(1, depth):
            arrived(from_z.at[k], recv_z.at[k])
        for part in (0, 1):
            here = part_rows(part)
            blocks = [piece(me, part), from_x.at[0, here], from_y.at[0, here]]
            blocks += [from_z.at[k, here] for k in range(1, depth)]
            finish([out.at[here] for out in out_refs], merge(blocks))
        for copy in sent:
            copy.wait_send()

    def slots(size):
        return pltpu.VMEM((depth, size, width), parts.dtype)

    return pl.pallas_call(
        kernel,
        in_specs=[pl.BlockSpec(memory_space=pltpu.VMEM)],
        out_specs=[pl.BlockSpec(memory_space=pltpu.VMEM)] * outs,
        out_shape=out_shape,
        scratch_shapes=[slots(half), slots(half), slots(rows), slots(rows), slots(rows)]
        + [slots(half), slots(half), slots(rows)]
        + [pltpu.SemaphoreType.DMA((7, depth))]
        + [pltpu.SemaphoreType.DMA((depth,))] * 2
        + [pltpu.SemaphoreType.DMA((2, depth))] * 2
        + [pltpu.SemaphoreType.DMA((depth,))],
        compiler_params=pltpu.CompilerParams(
            collective_id=collective_id, has_side_effects=True, vmem_limit_bytes=VMEM_LIMIT
        ),
        cost_estimate=lasting(55),
        name="reduce_group",
    )(parts)


def sum_blocks(parts, sources, collective_id):
    rows, width = parts.shape[0] // sources, parts.shape[1]

    def merge(blocks):
        total = blocks[0][...].astype(jnp.float32)
        for block in blocks[1:]:
            total = total + block[...].astype(jnp.float32)
        return total

    def pack(target, total):
        target[...] = total.astype(parts.dtype)

    def finish(targets, total):
        targets[0][...] = total

    out_shape = [jax.ShapeDtypeStruct((rows, width), jnp.float32)]
    return reduce_group(parts, sources, collective_id, merge, pack, finish, out_shape)[0]


def merge_partials(parts, sources, collective_id, heads):
    rows, width = parts.shape[0] // sources, parts.shape[1] - 128
    head_dim = width // heads

    def merge(blocks):
        stats = []
        for block in blocks:
            stat = block[:, width:].astype(jnp.float32)
            stats.append(stat + pltpu.roll(stat, 128 - 16, 1) + pltpu.roll(stat, 128 - 32, 1))
        top = stats[0]
        for stat in stats[1:]:
            top = jnp.maximum(top, stat)
        fades = [jnp.exp(stat - top) for stat in stats]
        total = sum(fade * pltpu.roll(stat, 128 - heads, 1) for fade, stat in zip(fades, stats))
        sums = []
        for head in range(heads):
            columns = slice(head * head_dim, (head + 1) * head_dim)
            sums.append(
                sum(
                    block[:, columns].astype(jnp.float32) * fade[:, head : head + 1]
                    for block, fade in zip(blocks, fades)
                )
            )
        return sums, top, total

    def pack(target, merged):
        sums, top, total = merged
        for head in range(heads):
            target[:, head * head_dim : (head + 1) * head_dim] = sums[head].astype(parts.dtype)
        lane = lax.broadcasted_iota(jnp.int32, top.shape, 1)
        stat = jnp.where(lane < heads, top, jnp.where(lane < 16, pltpu.roll(total, heads, 1), 0.0))
        target[:, width:] = triple(stat + pltpu.roll(stat, 16, 1) + pltpu.roll(stat, 32, 1))

    def finish(targets, merged):
        sums, top, total = merged
        live = total > 0
        total = jnp.where(live, total, 1.0)
        targets[1][...] = jnp.where(live, top + jnp.log(total), 0.0)
        for head in range(heads):
            targets[0][:, head * head_dim : (head + 1) * head_dim] = sums[head] / total[:, head : head + 1]

    out_shape = [
        jax.ShapeDtypeStruct((rows, width), jnp.float32),
        jax.ShapeDtypeStruct((rows, 128), jnp.float32),
    ]
    return reduce_group(parts, sources, collective_id, merge, pack, finish, out_shape)


def weight_halves(pairs):
    core = lax.axis_index("dp")
    lefts, kept, sent = [], [], []
    for left, right in pairs:
        half = right.shape[1] // 2
        lefts.append(left)
        kept.append(lax.dynamic_slice_in_dim(right, core * half, half, 1))
        sent.append(lax.dynamic_slice_in_dim(right, (1 - core) * half, half, 1))
    other = swapped(jnp.concatenate(lefts + sent, axis=1))
    partials, left_at, at = [], 0, sum(left.shape[1] for left in lefts)
    for left, right in zip(lefts, kept):
        other_left = other[:, left_at : left_at + left.shape[1]]
        other_right = other[:, at : at + right.shape[1]]
        left_at, at = left_at + left.shape[1], at + right.shape[1]
        partials.append(
            lax.dot_general(
                jnp.concatenate([left, other_left], axis=0),
                jnp.concatenate([right, other_right], axis=0),
                contract_rows,
                preferred_element_type=jnp.float32,
            ).astype(jnp.bfloat16)
        )
    return jnp.concatenate(partials, axis=1)


def scattered(halves):
    return lax.psum_scatter(halves, "mem", scatter_dimension=0, tiled=True)


def whole_grads(sums, widths):
    both = lax.all_gather(sums, "dp", axis=0).astype(jnp.float32)
    grads, at = [], 0
    for size in widths:
        half = size // 2
        grads.append(jnp.concatenate([both[0, :, at : at + half], both[1, :, at : at + half]], 1))
        at += half
    return grads


def on_device(
    tokens,
    attn_gain,
    qkv_weight,
    out_weight,
    bias_table,
    gate_logit,
    ffn_gain,
    up_weight,
    down_weight,
    memory_keys,
    memory_values,
    book_lengths,
    slot_shard,
    slot_index,
    slot_live,
    cotangent,
):
    rows, width = tokens.shape
    heads, buckets = bias_table.shape
    head_dim = width // heads
    top_count = slot_index.shape[2]
    hidden = up_weight.shape[1]
    groups = lax.axis_size("mem")
    capacity = max(2, 3 * rows * heads * top_count // (2 * groups))
    score_scale = 1.0 / math.sqrt(head_dim)
    sent_rows = min(W, rows)
    repeats = W // sent_rows
    first_pos = lax.axis_index("mem") * rows
    query_pos = first_pos + jnp.arange(rows, dtype=jnp.int32)
    key_pos = first_pos - W + jnp.arange(W + rows, dtype=jnp.int32)
    lengths = book_lengths[0]
    query_book = book_of(query_pos, lengths)
    key_book = jnp.where(key_pos >= 0, book_of(key_pos, lengths), -1)
    offset = (
        jnp.arange(rows, dtype=jnp.int32)[:, None]
        + W
        - jnp.arange(W + rows, dtype=jnp.int32)[None, :]
    )
    allowed = (offset >= 0) & (offset < W) & (query_book[:, None] == key_book[None, :])
    bucket = bucket_of(jnp.maximum(offset, 0))
    one_hot_f = (bucket[:, :, None] == jnp.arange(buckets, dtype=jnp.int32)).astype(jnp.float32)
    score_bias = jnp.einsum("qkb,hb->hqk", one_hot_f, bias_table, precision=lax.Precision.HIGHEST)
    tokens_f = tokens.astype(jnp.float32)
    normed_f, norm_in_back = jax.vjp(normed, tokens_f, attn_gain)
    normed_in = normed_f.astype(jnp.bfloat16)
    projected = jnp.dot(normed_in, qkv_weight, preferred_element_type=jnp.float32).astype(
        jnp.bfloat16
    )
    queries = projected[:, :width].reshape(rows, heads, head_dim)
    keys_own = projected[:, width : 2 * width].reshape(rows, heads, head_dim)
    values_own = projected[:, 2 * width :].reshape(rows, heads, head_dim)
    tail_rows = jnp.stack([keys_own, values_own])
    received = []
    for distance in range(repeats, 0, -1):
        received.append(passed_along(tail_rows, "mem", distance))
    halo_rows = jnp.concatenate(received, axis=1)
    keys_all = jnp.concatenate([halo_rows[0], keys_own], axis=0)
    values_all = jnp.concatenate([halo_rows[1], values_own], axis=0)

    def local_scores():
        raw_scores = (
            jnp.einsum("qhd,khd->hqk", queries, keys_all, preferred_element_type=jnp.float32)
            * score_scale
            + score_bias
        )
        return jnp.where(allowed[None], raw_scores, masked_score)

    scores = local_scores()
    row_max = jnp.max(scores, axis=-1, keepdims=True)
    exp_scores = jnp.exp(scores - row_max)
    sums_local = jnp.sum(exp_scores, axis=-1, keepdims=True)
    local_probs = exp_scores / sums_local
    log_total = row_max + jnp.log(sums_local)
    local_out = jnp.einsum(
        "hqk,khd->qhd",
        local_probs.astype(jnp.bfloat16),
        values_all,
        preferred_element_type=jnp.float32,
    )
    slots = memory_keys.shape[0]
    requests = place_requests(slot_shard, slot_index, slot_live, groups, capacity, slots)
    incoming = lax.all_to_all(requests, "mem", split_axis=0, concat_axis=0, tiled=True)
    row_ids = incoming // slots
    limits = jnp.arange(heads + 1, dtype=jnp.int32) * (rows * slots)
    bounds = jnp.sum((incoming[:, None, :] < limits[None, :, None]).astype(jnp.int32), axis=2)
    index = jnp.where(row_ids < heads * rows, row_ids // rows * slots + incoming % slots, 0)
    key_rows, value_rows = gather_rows(
        index.reshape(-1), bounds[:, heads], memory_keys, memory_values, heads, groups, capacity
    )
    all_queries = lax.all_gather(projected[:, :width], "mem", axis=0, tiled=True)
    entry_rows = row_ids[:, None, :]
    partial = memory_forward(
        bounds.reshape(-1),
        all_queries,
        key_rows,
        value_rows,
        entry_rows,
        heads,
        groups,
        rows,
        score_scale,
    )
    if groups == 16:
        memory_out, mem_log = merge_partials(partial, groups, 1, heads)
    else:
        partial = lax.all_to_all(
            partial.reshape(groups, rows, width + 128),
            "mem",
            split_axis=0,
            concat_axis=0,
            tiled=True,
        ).reshape(groups * rows, width + 128)
        memory_out, mem_log = combine_partials(partial, heads, groups, rows)
    memory_out = memory_out.reshape(rows, heads, head_dim)
    gate_share = jax.nn.sigmoid(gate_logit)[:, None]
    mixed_heads = (
        (gate_share * memory_out + (1.0 - gate_share) * local_out)
        .reshape(rows, width)
        .astype(jnp.bfloat16)
    )
    residual = tokens_f + jnp.dot(mixed_heads, out_weight, preferred_element_type=jnp.float32)
    normed_mid_f, norm_mid_back = jax.vjp(normed, residual, ffn_gain)
    normed_mid = normed_mid_f.astype(jnp.bfloat16)
    up_proj = jnp.dot(normed_mid, up_weight, preferred_element_type=jnp.float32)
    activated_f, gelu_back = jax.vjp(gelu_exact, up_proj)
    activated = activated_f.astype(jnp.bfloat16)
    ffn_branch = lax.dot_general(
        activated, down_weight, contract_cols, preferred_element_type=jnp.float32
    )
    block_out = (residual + ffn_branch).astype(jnp.bfloat16)
    d_act = jnp.dot(cotangent, down_weight, preferred_element_type=jnp.float32)
    d_up = gelu_back(d_act)[0].astype(jnp.bfloat16)
    d_mid = lax.dot_general(d_up, up_weight, contract_cols, preferred_element_type=jnp.float32)
    d_resid_part, ffn_gain_part = norm_mid_back(d_mid)
    d_residual = cotangent.astype(jnp.float32) + d_resid_part
    d_branch = d_residual.astype(jnp.bfloat16)
    d_mixed = lax.dot_general(
        d_branch, out_weight, contract_cols, preferred_element_type=jnp.float32
    ).reshape(rows, heads, head_dim)
    gate_part = (
        jnp.sum(d_mixed * (memory_out - local_out), axis=(0, 2))
        * (gate_share * (1.0 - gate_share))[:, 0]
    )
    early_halves = weight_halves([(mixed_heads, d_branch), (normed_mid, d_up), (cotangent, activated)])
    d_memory = (gate_share * d_mixed).astype(jnp.bfloat16)
    d_local_out = ((1.0 - gate_share) * d_mixed).astype(jnp.bfloat16)
    probs_again = jnp.exp(local_scores() - log_total)
    d_lw = jnp.einsum("qhd,khd->hqk", d_local_out, values_all, preferred_element_type=jnp.float32)
    d_local = (probs_again * (d_lw - jnp.sum(probs_again * d_lw, axis=-1, keepdims=True))).astype(
        jnp.bfloat16
    )
    d_values_all = jnp.einsum(
        "hqk,qhd->khd",
        probs_again.astype(jnp.bfloat16),
        d_local_out,
        preferred_element_type=jnp.float32,
    )
    d_keys_all = (
        jnp.einsum("hqk,qhd->khd", d_local, queries, preferred_element_type=jnp.float32)
        * score_scale
    )
    d_queries = (
        jnp.einsum("hqk,khd->qhd", d_local, keys_all, preferred_element_type=jnp.float32)
        * score_scale
    )
    bias_part = jnp.einsum(
        "hqk,qkb->hb", d_local, one_hot_f.astype(jnp.bfloat16), preferred_element_type=jnp.float32
    )
    mem_delta = jnp.sum(d_memory.astype(jnp.float32) * memory_out, axis=-1)
    sent_grads = jnp.concatenate(
        [
            d_memory.reshape(rows, width),
            split3(jnp.concatenate([mem_log[:, :heads], mem_delta], axis=1)),
            jnp.zeros((rows, 80), jnp.bfloat16),
        ],
        axis=1,
    )
    sent_grads, early_halves = lax.optimization_barrier((sent_grads, early_halves))
    early_sums = scattered(early_halves)
    if groups == 16:
        all_grads = gather_group(sent_grads, groups, 2)
    else:
        all_grads = lax.all_gather(sent_grads, "mem", axis=0, tiled=True)
    d_partial = memory_backward(
        bounds.reshape(-1),
        all_queries,
        all_grads,
        key_rows,
        value_rows,
        entry_rows,
        heads,
        groups,
        rows,
        score_scale,
    )
    if groups == 16:
        d_partial = sum_blocks(d_partial, groups, 3)
    else:
        d_partial = jnp.sum(
            lax.all_to_all(
                d_partial.reshape(groups, rows, width), "mem", split_axis=0, concat_axis=0, tiled=True
            ).astype(jnp.float32),
            axis=0,
        )
    d_queries = d_queries + d_partial.reshape(rows, heads, head_dim) * score_scale
    halo_grads = jnp.stack([d_keys_all[:W], d_values_all[:W]])
    d_tails = jnp.zeros((2, sent_rows, heads, head_dim), jnp.float32)
    for distance in range(repeats, 0, -1):
        first_row = (repeats - distance) * sent_rows
        d_tails = d_tails + passed_along(
            halo_grads[:, first_row : first_row + sent_rows].astype(jnp.bfloat16), "mem", -distance
        ).astype(jnp.float32)
    d_keys = d_keys_all[W:] + d_tails[0]
    d_values = d_values_all[W:] + d_tails[1]
    d_projected = jnp.concatenate(
        [
            d_queries.reshape(rows, width),
            d_keys.reshape(rows, width),
            d_values.reshape(rows, width),
        ],
        axis=1,
    ).astype(jnp.bfloat16)
    d_in = lax.dot_general(
        d_projected, qkv_weight, contract_cols, preferred_element_type=jnp.float32
    )
    d_tokens_part, attn_gain_part = norm_in_back(d_in)
    tokens_grad = d_residual + d_tokens_part
    late_halves = weight_halves([(normed_in, d_projected)])
    late_halves, early_sums = lax.optimization_barrier((late_halves, early_sums))
    late_sums = scattered(late_halves)
    out_grad, up_grad, down_grad = whole_grads(early_sums, [width, hidden, hidden])
    qkv_grad = whole_grads(late_sums, [3 * width])[0]
    small_sums = lax.psum((attn_gain_part, ffn_gain_part, bias_part, gate_part), ("dp", "mem"))
    return (
        block_out,
        tokens_grad,
        qkv_grad,
        out_grad,
        up_grad,
        down_grad,
        small_sums[0],
        small_sums[1],
        small_sums[2],
        small_sums[3],
    )


def solution(mesh):
    in_specs = (
        P(("dp", "mem"), None),
        P(),
        P(),
        P(),
        P(),
        P(),
        P(),
        P(),
        P(),
        P("mem", None),
        P("mem", None),
        P("dp", None),
        P(("dp", "mem"), None, None, None),
        P(("dp", "mem"), None, None),
        P(("dp", "mem"), None, None),
        P(("dp", "mem"), None),
    )
    out_specs = (
        P(("dp", "mem"), None),
        P(("dp", "mem"), None),
        P("mem", None),
        P("mem", None),
        P("mem", None),
        P("mem", None),
        P(),
        P(),
        P(),
        P(),
    )
    return jax.shard_map(
        on_device, mesh=mesh, in_specs=in_specs, out_specs=out_specs, check_vma=False
    )
```

```python
import math

import jax
import jax.numpy as jnp
from jax import lax
from jax.experimental import pallas as pl
from jax.experimental.pallas import tpu as pltpu
from jax.sharding import PartitionSpec as P

W = 512
VMEM_LIMIT = 56 * 1024 * 1024


eps_norm = 1e-06
bucket_edges = tuple((math.ceil(16 * 8 ** (edge_step / 16)) for edge_step in range(1, 16)))
masked_score = -1e30
dead_score = -10000.0
contract_rows = (((0,), (0,)), ((), ()))
contract_cols = (((1,), (1,)), ((), ()))


def passed_along(value, axis, by):
    size = lax.axis_size(axis)
    pairs = [(i, i + by) for i in range(size) if 0 <= i + by < size]
    return lax.ppermute(value, axis, pairs)


def swapped(value):
    return lax.ppermute(value, "dp", [(0, 1), (1, 0)])


def bucket_of(offset):
    past_edges = sum(((offset >= edge_pos).astype(jnp.int32) for edge_pos in bucket_edges))
    return jnp.where(offset < 16, offset, 16 + past_edges)


def normed(values, gain_vec):
    return (
        values * lax.rsqrt(jnp.mean(values * values, axis=-1, keepdims=True) + eps_norm) * gain_vec
    )


def gelu_exact(values):
    return jax.nn.gelu(values, approximate=False)


def book_of(positions, lengths):
    book_ends = jnp.cumsum(lengths, dtype=jnp.int32)
    return jnp.sum((positions[..., None] >= book_ends).astype(jnp.int32), axis=-1)


def place_requests(slot_shard, slot_index, slot_live, owners, capacity, slots):
    rows, heads, top_count = slot_index.shape
    entries = rows * heads * top_count
    row_of = (
        jnp.arange(heads, dtype=jnp.int32)[None, :] * rows
        + jnp.arange(rows, dtype=jnp.int32)[:, None]
    )
    place = row_of[:, :, None] * top_count + jnp.arange(top_count, dtype=jnp.int32)
    owner = jnp.where(slot_live > 0, slot_shard[..., 0], owners)
    keys, picked = lax.sort(
        ((owner * entries + place).reshape(-1), slot_index.reshape(-1)), num_keys=1
    )
    ends = jnp.sum(
        (keys[None, :] < (jnp.arange(owners, dtype=jnp.int32) + 1)[:, None] * entries).astype(jnp.int32),
        axis=1,
    )
    starts = jnp.concatenate([jnp.zeros((1,), jnp.int32), ends[:-1]])
    codes = jnp.concatenate(
        [(keys % entries) // top_count * slots + picked, jnp.zeros((capacity,), jnp.int32)]
    )
    lists = jnp.stack(
        [lax.dynamic_slice_in_dim(codes, starts[i], capacity) for i in range(owners)]
    )
    used = jnp.arange(capacity, dtype=jnp.int32)[None, :] < (ends - starts)[:, None]
    return jnp.where(used, lists, heads * rows * slots)


def gather_rows(index, counts, memory_keys, memory_values, heads, sources, capacity):
    slots, width = memory_keys.shape
    head_dim = width // heads
    step = 16

    def kernel(index_ref, counts_ref, keys, values, out_keys, out_values, key_table, value_table, key_rows, value_rows):
        i = pl.program_id(0)

        @pl.when(i == 0)
        def _():
            key_rows[...] = jnp.zeros_like(key_rows)
            value_rows[...] = jnp.zeros_like(value_rows)

        @pl.when(i < heads)
        def _():
            place = pl.ds(pl.multiple_of(i * slots, slots), slots)
            key_table[place, :] = keys[...].astype(jnp.float32)
            value_table[place, :] = values[...].astype(jnp.float32)

        @pl.when(i >= heads)
        def _():
            source = i - heads

            @pl.loop(0, (counts_ref[source] + step - 1) // step)
            def _(group):
                first = pl.multiple_of(group * step, step)
                for u in range(step):
                    row = index_ref[source * capacity + first + u]
                    key_rows[pl.ds(first + u, 1), :] = key_table[pl.ds(row, 1), :]
                    value_rows[pl.ds(first + u, 1), :] = value_table[pl.ds(row, 1), :]

            out_keys[...] = key_rows[...].astype(jnp.bfloat16)
            out_values[...] = value_rows[...].astype(jnp.bfloat16)

    table_spec = pl.BlockSpec((slots, head_dim), lambda i, *_: (0, jnp.minimum(i, heads - 1)))
    out_spec = pl.BlockSpec((capacity, head_dim), lambda i, *_: (jnp.maximum(i - heads, 0), 0))
    out_shape = jax.ShapeDtypeStruct((sources * capacity, head_dim), jnp.bfloat16)
    return pl.pallas_call(
        kernel,
        grid_spec=pltpu.PrefetchScalarGridSpec(
            num_scalar_prefetch=2,
            grid=(heads + sources,),
            in_specs=[table_spec, table_spec],
            out_specs=[out_spec, out_spec],
            scratch_shapes=[
                pltpu.VMEM((heads * slots, head_dim), jnp.float32),
                pltpu.VMEM((heads * slots, head_dim), jnp.float32),
                pltpu.VMEM((capacity, head_dim), jnp.float32),
                pltpu.VMEM((capacity, head_dim), jnp.float32),
            ],
        ),
        out_shape=[out_shape, out_shape],
        compiler_params=pltpu.CompilerParams(vmem_limit_bytes=VMEM_LIMIT),
        cost_estimate=lasting(42),
        name="gather_rows",
    )(index, counts, memory_keys, memory_values)


def lasting(microseconds):
    return pl.CostEstimate(flops=0, bytes_accessed=3_000_000 * microseconds, transcendentals=0)


def triple(stat):
    part = lax.broadcasted_iota(jnp.int32, stat.shape, 1) // 16
    high = stat.astype(jnp.bfloat16).astype(jnp.float32)
    rest = stat - high
    middle = rest.astype(jnp.bfloat16).astype(jnp.float32)
    low = rest - middle
    chosen = jnp.where(part == 0, high, jnp.where(part == 1, middle, jnp.where(part == 2, low, 0.0)))
    return chosen.astype(jnp.bfloat16)


def window_of(bounds, source, head, heads, span, capacity):
    first = bounds[source * (heads + 1) + head]
    last = bounds[source * (heads + 1) + head + 1]
    start = jnp.minimum((first // 128) * 128, capacity - span)
    extra = jnp.maximum(last - start - span + span - 1, 0) // span
    return start, extra


def memory_forward(bounds, queries, key_rows, value_rows, row_ids, heads, sources, rows, score_scale):
    capacity, head_dim = key_rows.shape[0] // sources, key_rows.shape[1]
    width = heads * head_dim
    span = min(512, capacity)

    def kernel(bounds_ref, q_ref, k_ref, v_ref, id_ref, out_ref, sums, tops, totals):
        source = pl.program_id(0)
        token = lax.broadcasted_iota(jnp.int32, (rows, span), 0)
        lane = lax.broadcasted_iota(jnp.int32, (rows, 128), 1) % 16

        def scores_of(head, start, least):
            here = pl.ds(pl.multiple_of(start, 128), span)
            ids = id_ref[0, :, here]
            mine = ids == token + head * rows
            if least is not None:
                place = lax.broadcasted_iota(jnp.int32, (1, span), 1) + start
                mine = mine & (place >= least)
            q = q_ref[:, head * head_dim : (head + 1) * head_dim]
            raw = lax.dot_general(q, k_ref[here, :], contract_cols, preferred_element_type=jnp.float32)
            return jnp.where(mine, raw * score_scale, masked_score), mine, v_ref[here, :]

        windows = [window_of(bounds_ref, source, head, heads, span, capacity) for head in range(heads)]
        top_tile = jnp.zeros((rows, 128), jnp.float32)
        total_tile = jnp.zeros((rows, 128), jnp.float32)
        for head in range(heads):
            scores, mine, v = scores_of(head, windows[head][0], None)
            top = jnp.max(scores, axis=1, keepdims=True)
            weights = jnp.where(mine, jnp.exp(scores - top), 0.0)
            sums[:, head * head_dim : (head + 1) * head_dim] = jnp.dot(
                weights.astype(jnp.bfloat16), v, preferred_element_type=jnp.float32
            )
            top_tile = jnp.where(lane == head, top, top_tile)
            total_tile = jnp.where(
                lane == heads + head, jnp.sum(weights, axis=1, keepdims=True), total_tile
            )
        tops[...] = top_tile
        totals[...] = total_tile
        more = sum(extra for _, extra in windows)

        @pl.when(more > 0)
        def _():
            for head in range(heads):
                start, extra = windows[head]
                columns = slice(head * head_dim, (head + 1) * head_dim)

                @pl.loop(0, extra)
                def _(turn):
                    least = start + (turn + 1) * span
                    scores, mine, v = scores_of(head, jnp.minimum(least, capacity - span), least)
                    old_top = jnp.max(
                        jnp.where(lane == head, tops[...], masked_score), axis=1, keepdims=True
                    )
                    top = jnp.maximum(old_top, jnp.max(scores, axis=1, keepdims=True))
                    weights = jnp.where(mine, jnp.exp(scores - top), 0.0)
                    faded = jnp.exp(old_top - top)
                    sums[:, columns] = sums[:, columns] * faded + jnp.dot(
                        weights.astype(jnp.bfloat16), v, preferred_element_type=jnp.float32
                    )
                    tops[...] = jnp.where(lane == head, top, tops[...])
                    totals[...] = jnp.where(
                        lane == heads + head,
                        totals[...] * faded + jnp.sum(weights, axis=1, keepdims=True),
                        totals[...],
                    )

        out_ref[:, :width] = sums[...].astype(jnp.bfloat16)
        out_ref[:, width:] = triple(jnp.where(lane < heads, tops[...], totals[...]))

    return pl.pallas_call(
        kernel,
        grid_spec=pltpu.PrefetchScalarGridSpec(
            num_scalar_prefetch=1,
            grid=(sources,),
            in_specs=[
                pl.BlockSpec((rows, width), lambda i, *_: (i, 0)),
                pl.BlockSpec((capacity, head_dim), lambda i, *_: (i, 0)),
                pl.BlockSpec((capacity, head_dim), lambda i, *_: (i, 0)),
                pl.BlockSpec((1, 1, capacity), lambda i, *_: (i, 0, 0)),
            ],
            out_specs=pl.BlockSpec((rows, width + 128), lambda i, *_: (i, 0)),
            scratch_shapes=[
                pltpu.VMEM((rows, width), jnp.float32),
                pltpu.VMEM((rows, 128), jnp.float32),
                pltpu.VMEM((rows, 128), jnp.float32),
            ],
        ),
        out_shape=jax.ShapeDtypeStruct((sources * rows, width + 128), jnp.bfloat16),
        compiler_params=pltpu.CompilerParams(vmem_limit_bytes=VMEM_LIMIT),
        cost_estimate=lasting(41),
        name="memory_forward",
    )(bounds, queries, key_rows, value_rows, row_ids)


def combine_partials(partial, heads, sources, rows):
    width = partial.shape[1] - 128
    head_dim = width // heads

    def kernel(part_ref, out_ref, log_ref, sums, tops, totals):
        i = pl.program_id(0)

        @pl.when(i == 0)
        def _():
            sums[...] = jnp.zeros_like(sums)
            tops[...] = jnp.full_like(tops, masked_score)
            totals[...] = jnp.zeros_like(totals)

        stat = part_ref[:, width:].astype(jnp.float32)
        stat = stat + pltpu.roll(stat, 128 - 16, 1) + pltpu.roll(stat, 128 - 32, 1)
        new_total = pltpu.roll(stat, 128 - heads, 1)
        top = jnp.maximum(tops[...], stat)
        old_fade, new_fade = jnp.exp(tops[...] - top), jnp.exp(stat - top)
        tops[...] = top
        totals[...] = totals[...] * old_fade + new_total * new_fade
        for head in range(heads):
            columns = slice(head * head_dim, (head + 1) * head_dim)
            sums[:, columns] = (
                sums[:, columns] * old_fade[:, head : head + 1]
                + part_ref[:, columns].astype(jnp.float32) * new_fade[:, head : head + 1]
            )

        @pl.when(i == sources - 1)
        def _():
            live = totals[...] > 0
            total = jnp.where(live, totals[...], 1.0)
            log_ref[...] = jnp.where(live, tops[...] + jnp.log(total), 0.0)
            for head in range(heads):
                columns = slice(head * head_dim, (head + 1) * head_dim)
                out_ref[:, columns] = sums[:, columns] / total[:, head : head + 1]

    return pl.pallas_call(
        kernel,
        grid=(sources,),
        in_specs=[pl.BlockSpec((rows, width + 128), lambda i: (i, 0))],
        out_specs=[
            pl.BlockSpec((rows, width), lambda i: (0, 0)),
            pl.BlockSpec((rows, 128), lambda i: (0, 0)),
        ],
        scratch_shapes=[
            pltpu.VMEM((rows, width), jnp.float32),
            pltpu.VMEM((rows, 128), jnp.float32),
            pltpu.VMEM((rows, 128), jnp.float32),
        ],
        out_shape=[
            jax.ShapeDtypeStruct((rows, width), jnp.float32),
            jax.ShapeDtypeStruct((rows, 128), jnp.float32),
        ],
        compiler_params=pltpu.CompilerParams(vmem_limit_bytes=VMEM_LIMIT),
        cost_estimate=lasting(13),
        name="combine_partials",
    )(partial)


def memory_backward(bounds, queries, grads, key_rows, value_rows, row_ids, heads, sources, rows, score_scale):
    capacity, head_dim = key_rows.shape[0] // sources, key_rows.shape[1]
    width = heads * head_dim
    span = min(512, capacity)

    def kernel(bounds_ref, q_ref, g_ref, k_ref, v_ref, id_ref, out_ref, sums):
        source = pl.program_id(0)
        token = lax.broadcasted_iota(jnp.int32, (rows, span), 0)
        stat = joined_tile(g_ref[:, width : width + 128])

        def term(column):
            return stat[:, column : column + 1]

        def part_of(head, start, least):
            here = pl.ds(pl.multiple_of(start, 128), span)
            columns = slice(head * head_dim, (head + 1) * head_dim)
            mine = id_ref[0, :, here] == token + head * rows
            if least is not None:
                place = lax.broadcasted_iota(jnp.int32, (1, span), 1) + start
                mine = mine & (place >= least)
            k, v = k_ref[here, :], v_ref[here, :]
            raw = lax.dot_general(
                q_ref[:, columns], k, contract_cols, preferred_element_type=jnp.float32
            )
            products = lax.dot_general(
                g_ref[:, columns], v, contract_cols, preferred_element_type=jnp.float32
            )
            probs = jnp.exp(jnp.where(mine, raw * score_scale - term(head), dead_score))
            slopes = (probs * (products - term(heads + head))).astype(jnp.bfloat16)
            return jnp.dot(slopes, k, preferred_element_type=jnp.float32)

        windows = [window_of(bounds_ref, source, head, heads, span, capacity) for head in range(heads)]
        for head in range(heads):
            sums[:, head * head_dim : (head + 1) * head_dim] = part_of(head, windows[head][0], None)
        more = sum(extra for _, extra in windows)

        @pl.when(more > 0)
        def _():
            for head in range(heads):
                start, extra = windows[head]
                columns = slice(head * head_dim, (head + 1) * head_dim)

                @pl.loop(0, extra)
                def _(turn):
                    least = start + (turn + 1) * span
                    sums[:, columns] += part_of(head, jnp.minimum(least, capacity - span), least)

        out_ref[...] = sums[...].astype(jnp.bfloat16)

    return pl.pallas_call(
        kernel,
        grid_spec=pltpu.PrefetchScalarGridSpec(
            num_scalar_prefetch=1,
            grid=(sources,),
            in_specs=[
                pl.BlockSpec((rows, width), lambda i, *_: (i, 0)),
                pl.BlockSpec((rows, width + 128), lambda i, *_: (i, 0)),
                pl.BlockSpec((capacity, head_dim), lambda i, *_: (i, 0)),
                pl.BlockSpec((capacity, head_dim), lambda i, *_: (i, 0)),
                pl.BlockSpec((1, 1, capacity), lambda i, *_: (i, 0, 0)),
            ],
            out_specs=pl.BlockSpec((rows, width), lambda i, *_: (i, 0)),
            scratch_shapes=[pltpu.VMEM((rows, width), jnp.float32)],
        ),
        out_shape=jax.ShapeDtypeStruct((sources * rows, width), jnp.bfloat16),
        compiler_params=pltpu.CompilerParams(vmem_limit_bytes=VMEM_LIMIT),
        cost_estimate=lasting(35),
        name="memory_backward",
    )(bounds, queries, grads, key_rows, value_rows, row_ids)


def remote(source, target, send_sem, recv_sem, device):
    return pltpu.make_async_remote_copy(
        src_ref=source,
        dst_ref=target,
        send_sem=send_sem,
        recv_sem=recv_sem,
        device_id={"mem": device},
        device_id_type=pl.DeviceIdType.MESH,
    )


def grid_place(depth):
    me = lax.axis_index("mem")
    layer, column = me // 4, me % 4
    beside_x = column + 1 - 2 * (column % 2)
    beside_y = column + 2 - 4 * (column // 2)
    across = 3 - column

    def index_of(step, place):
        return (layer + step + depth) % depth * 4 + place

    return me, column, beside_x, beside_y, across, index_of


def greet(devices):
    barrier = pltpu.get_barrier_semaphore()
    for device in devices:
        pl.semaphore_signal(
            barrier, inc=1, device_id={"mem": device}, device_id_type=pl.DeviceIdType.MESH
        )
    pl.semaphore_wait(barrier, len(devices))


def gather_group(block, sources, collective_id):
    rows, width = block.shape
    depth, half = sources // 4, rows // 2

    def kernel(x_ref, out_ref, own_sem, send, recv_z, recv_x, recv_y, recv_a, recv_b):
        me, column, beside_x, beside_y, across, index_of = grid_place(depth)
        to_x, to_y = index_of(0, beside_x), index_of(0, beside_y)
        greet([to_x, to_y] + [index_of(-k, column) for k in range(1, depth)])

        def rows_of(index, part=None):
            if part is None:
                return out_ref.at[pl.ds(pl.multiple_of(index * rows, rows), rows), :]
            return out_ref.at[pl.ds(pl.multiple_of(index * rows + part * half, half), half), :]

        own = pltpu.make_async_copy(x_ref, rows_of(me), own_sem)
        own.start()
        sent = []

        def push(source, target, kind, k, recv, device):
            copy = remote(source, target, send.at[kind, k], recv.at[k], device)
            copy.start()
            sent.append(copy)

        def arrived(target, recv, k):
            remote(target, target, send.at[0, 0], recv.at[k], to_x).wait_recv()

        push(x_ref, rows_of(me), 1, 0, recv_x, to_x)
        push(x_ref, rows_of(me), 2, 0, recv_y, to_y)
        for k in range(1, depth):
            push(x_ref, rows_of(me), 0, k, recv_z, index_of(-k, column))

        def pass_on(k):
            from_x, from_y = index_of(k, beside_x), index_of(k, beside_y)
            arrived(rows_of(from_x), recv_x, k)
            push(rows_of(from_x, 0), rows_of(from_x, 0), 3, k, recv_a, to_y)
            arrived(rows_of(from_y), recv_y, k)
            push(rows_of(from_y, 1), rows_of(from_y, 1), 4, k, recv_b, to_x)

        for k in range(1, depth):
            above = index_of(k, column)
            arrived(rows_of(above), recv_z, k)
            push(rows_of(above), rows_of(above), 1, k, recv_x, to_x)
            push(rows_of(above), rows_of(above), 2, k, recv_y, to_y)
            pass_on(k - 1)
        pass_on(depth - 1)
        for k in range(depth):
            far = index_of(k, across)
            arrived(rows_of(far, 0), recv_a, k)
            arrived(rows_of(far, 1), recv_b, k)
        for copy in sent:
            copy.wait_send()
        own.wait()

    return pl.pallas_call(
        kernel,
        in_specs=[pl.BlockSpec(memory_space=pl.ANY)],
        out_specs=pl.BlockSpec(memory_space=pl.ANY),
        out_shape=jax.ShapeDtypeStruct((sources * rows, width), block.dtype),
        scratch_shapes=[pltpu.SemaphoreType.DMA, pltpu.SemaphoreType.DMA((5, depth))]
        + [pltpu.SemaphoreType.DMA((depth,))] * 5,
        compiler_params=pltpu.CompilerParams(
            collective_id=collective_id, has_side_effects=True, vmem_limit_bytes=VMEM_LIMIT
        ),
        cost_estimate=lasting(50),
        name="gather_group",
    )(block)


def reduce_group(parts, sources, collective_id, merge, pack, finish, out_shape):
    rows, width = parts.shape[0] // sources, parts.shape[1]
    depth, half = sources // 4, rows // 2
    outs = len(out_shape)

    def kernel(parts_ref, *refs):
        out_refs = refs[:outs]
        half_a, half_b, from_x, from_y, from_z, out_x, out_y, out_z = refs[outs : outs + 8]
        send, recv_a, recv_b, recv_x, recv_y, recv_z = refs[outs + 8 :]
        me, column, beside_x, beside_y, across, index_of = grid_place(depth)
        to_x, to_y = index_of(0, beside_x), index_of(0, beside_y)
        greet([to_x, to_y] + [index_of(-k, column) for k in range(1, depth)])
        order = [*range(1, depth), 0]
        sent = []

        def piece(index, part):
            return parts_ref.at[pl.ds(pl.multiple_of(index * rows + part * half, half), half), :]

        def part_rows(part):
            return pl.ds(part * half, half)

        def push(source, target, kind, k, recv_sem, device):
            copy = remote(source, target, send.at[kind, k], recv_sem, device)
            copy.start()
            sent.append(copy)

        def arrived(target, recv_sem):
            remote(target, target, send.at[0, 0], recv_sem, to_x).wait_recv()

        for k in order:
            far = index_of(k, across)
            push(piece(far, 0), half_a.at[k], 0, k, recv_a.at[k], to_x)
            push(piece(far, 1), half_b.at[k], 1, k, recv_b.at[k], to_y)
        for k in order:
            push(piece(index_of(k, beside_x), 0), from_x.at[k, part_rows(0)], 2, k, recv_x.at[0, k], to_x)
            push(piece(index_of(k, beside_y), 1), from_y.at[k, part_rows(1)], 3, k, recv_y.at[1, k], to_y)
        for k in order:
            arrived(half_a.at[k], recv_a.at[k])
            pack(out_y.at[k], merge([piece(index_of(k, beside_y), 0), half_a.at[k]]))
            push(out_y.at[k], from_y.at[k, part_rows(0)], 4, k, recv_y.at[0, k], to_y)
            arrived(half_b.at[k], recv_b.at[k])
            pack(out_x.at[k], merge([piece(index_of(k, beside_x), 1), half_b.at[k]]))
            push(out_x.at[k], from_x.at[k, part_rows(1)], 5, k, recv_x.at[1, k], to_x)
        for k in order:
            for part in (0, 1):
                arrived(from_x.at[k, part_rows(part)], recv_x.at[part, k])
                arrived(from_y.at[k, part_rows(part)], recv_y.at[part, k])
            if k:
                for part in (0, 1):
                    here = part_rows(part)
                    blocks = [piece(index_of(k, column), part), from_x.at[k, here], from_y.at[k, here]]
                    pack(out_z.at[k, here], merge(blocks))
                push(out_z.at[k], from_z.at[k], 6, k, recv_z.at[k], index_of(k, column))
        for k in range(1, depth):
            arrived(from_z.at[k], recv_z.at[k])
        for part in (0, 1):
            here = part_rows(part)
            blocks = [piece(me, part), from_x.at[0, here], from_y.at[0, here]]
            blocks += [from_z.at[k, here] for k in range(1, depth)]
            finish([out.at[here] for out in out_refs], merge(blocks))
        for copy in sent:
            copy.wait_send()

    def slots(size):
        return pltpu.VMEM((depth, size, width), parts.dtype)

    return pl.pallas_call(
        kernel,
        in_specs=[pl.BlockSpec(memory_space=pltpu.VMEM)],
        out_specs=[pl.BlockSpec(memory_space=pltpu.VMEM)] * outs,
        out_shape=out_shape,
        scratch_shapes=[slots(half), slots(half), slots(rows), slots(rows), slots(rows)]
        + [slots(half), slots(half), slots(rows)]
        + [pltpu.SemaphoreType.DMA((7, depth))]
        + [pltpu.SemaphoreType.DMA((depth,))] * 2
        + [pltpu.SemaphoreType.DMA((2, depth))] * 2
        + [pltpu.SemaphoreType.DMA((depth,))],
        compiler_params=pltpu.CompilerParams(
            collective_id=collective_id, has_side_effects=True, vmem_limit_bytes=VMEM_LIMIT
        ),
        cost_estimate=lasting(55),
        name="reduce_group",
    )(parts)


def sum_blocks(parts, sources, collective_id):
    rows, width = parts.shape[0] // sources, parts.shape[1]

    def merge(blocks):
        total = blocks[0][...].astype(jnp.float32)
        for block in blocks[1:]:
            total = total + block[...].astype(jnp.float32)
        return total

    def pack(target, total):
        target[...] = total.astype(parts.dtype)

    def finish(targets, total):
        targets[0][...] = total

    out_shape = [jax.ShapeDtypeStruct((rows, width), jnp.float32)]
    return reduce_group(parts, sources, collective_id, merge, pack, finish, out_shape)[0]


def merge_partials(parts, sources, collective_id, heads):
    rows, width = parts.shape[0] // sources, parts.shape[1] - 128
    head_dim = width // heads

    def merge(blocks):
        stats = []
        for block in blocks:
            stat = block[:, width:].astype(jnp.float32)
            stats.append(stat + pltpu.roll(stat, 128 - 16, 1) + pltpu.roll(stat, 128 - 32, 1))
        top = stats[0]
        for stat in stats[1:]:
            top = jnp.maximum(top, stat)
        fades = [jnp.exp(stat - top) for stat in stats]
        total = sum(fade * pltpu.roll(stat, 128 - heads, 1) for fade, stat in zip(fades, stats))
        sums = []
        for head in range(heads):
            columns = slice(head * head_dim, (head + 1) * head_dim)
            sums.append(
                sum(
                    block[:, columns].astype(jnp.float32) * fade[:, head : head + 1]
                    for block, fade in zip(blocks, fades)
                )
            )
        return sums, top, total

    def pack(target, merged):
        sums, top, total = merged
        for head in range(heads):
            target[:, head * head_dim : (head + 1) * head_dim] = sums[head].astype(parts.dtype)
        lane = lax.broadcasted_iota(jnp.int32, top.shape, 1)
        stat = jnp.where(lane < heads, top, jnp.where(lane < 16, pltpu.roll(total, heads, 1), 0.0))
        target[:, width:] = triple(stat + pltpu.roll(stat, 16, 1) + pltpu.roll(stat, 32, 1))

    def finish(targets, merged):
        sums, top, total = merged
        live = total > 0
        total = jnp.where(live, total, 1.0)
        targets[1][...] = jnp.where(live, top + jnp.log(total), 0.0)
        for head in range(heads):
            targets[0][:, head * head_dim : (head + 1) * head_dim] = sums[head] / total[:, head : head + 1]

    out_shape = [
        jax.ShapeDtypeStruct((rows, width), jnp.float32),
        jax.ShapeDtypeStruct((rows, 128), jnp.float32),
    ]
    return reduce_group(parts, sources, collective_id, merge, pack, finish, out_shape)


def weight_halves(pairs):
    core = lax.axis_index("dp")
    lefts, kept, sent = [], [], []
    for left, right in pairs:
        half = right.shape[1] // 2
        lefts.append(left)
        kept.append(lax.dynamic_slice_in_dim(right, core * half, half, 1))
        sent.append(lax.dynamic_slice_in_dim(right, (1 - core) * half, half, 1))
    other = swapped(jnp.concatenate(lefts + sent, axis=1))
    partials, left_at, at = [], 0, sum(left.shape[1] for left in lefts)
    for left, right in zip(lefts, kept):
        other_left = other[:, left_at : left_at + left.shape[1]]
        other_right = other[:, at : at + right.shape[1]]
        left_at, at = left_at + left.shape[1], at + right.shape[1]
        partials.append(
            lax.dot_general(
                jnp.concatenate([left, other_left], axis=0),
                jnp.concatenate([right, other_right], axis=0),
                contract_rows,
                preferred_element_type=jnp.float32,
            ).astype(jnp.bfloat16)
        )
    return jnp.concatenate(partials, axis=1)


def scattered(halves):
    return lax.psum_scatter(halves, "mem", scatter_dimension=0, tiled=True)


def whole_grads(both, widths):
    both = both.astype(jnp.float32)
    grads, at = [], 0
    for size in widths:
        half = size // 2
        grads.append(jnp.concatenate([both[0, :, at : at + half], both[1, :, at : at + half]], 1))
        at += half
    return grads


def lane_tile(columns, rows):
    lane = lax.broadcasted_iota(jnp.int32, (rows, 128), 1)
    tile = jnp.zeros((rows, 128), jnp.float32)
    for i, column in enumerate(columns):
        tile = jnp.where(lane == i, column, tile)
    return tile


def split_tile(tile):
    lane = lax.broadcasted_iota(jnp.int32, tile.shape, 1)
    kept = jnp.where(lane < 32, tile, 0.0)
    kept = kept + pltpu.roll(kept, 32, 1) + pltpu.roll(kept, 64, 1)
    high = kept.astype(jnp.bfloat16).astype(jnp.float32)
    middle = (kept - high).astype(jnp.bfloat16).astype(jnp.float32)
    low = kept - high - middle
    part = lane // 32
    return jnp.where(part == 0, high, jnp.where(part == 1, middle, low)).astype(jnp.bfloat16)


def joined_tile(tile):
    tile = tile.astype(jnp.float32)
    return tile + pltpu.roll(tile, 128 - 32, 1) + pltpu.roll(tile, 128 - 64, 1)


def slanted(base, rows):
    return pltpu.roll(jnp.broadcast_to(base, (rows, base.shape[1])), 0, 1, stride=1, stride_axis=0)


def local_forward(base, book_column, book_row, own, halos, heads, score_scale):
    rows, width = own.shape[0], own.shape[1] // 3
    head_dim = width // heads
    count = len(halos) + 1

    def kernel(base_ref, column_ref, row_ref, own_ref, *refs):
        halo_refs, (out_ref, log_ref) = refs[: count - 1], refs[count - 1 :]
        same = column_ref[:, :1] == row_ref[:1, :]
        logs = []
        for head in range(heads):
            columns = slice(head * head_dim, (head + 1) * head_dim)
            above = slice(width + head * head_dim, width + (head + 1) * head_dim)
            twice = slice(2 * width + head * head_dim, 2 * width + (head + 1) * head_dim)
            keys = [ref[:, columns] for ref in halo_refs] + [own_ref[:, above]]
            values = [ref[:, above] for ref in halo_refs] + [own_ref[:, twice]]
            q = own_ref[:, columns]
            raw = [
                lax.dot_general(q, k, contract_cols, preferred_element_type=jnp.float32) for k in keys
            ]
            bias = slanted(base_ref[head : head + 1, :], rows)[:, : count * rows]
            scores = jnp.concatenate(raw, axis=1) * score_scale + bias
            scores = jnp.where(same, scores, masked_score)
            top = jnp.max(scores, axis=1, keepdims=True)
            weights = jnp.exp(scores - top)
            total = jnp.sum(weights, axis=1, keepdims=True)
            weights = (weights / total).astype(jnp.bfloat16)
            out_ref[:, columns] = sum(
                jnp.dot(
                    weights[:, i * rows : (i + 1) * rows], v, preferred_element_type=jnp.float32
                )
                for i, v in enumerate(values)
            )
            logs.append(top + jnp.log(total))
        log_ref[...] = lane_tile(logs, rows)

    return pl.pallas_call(
        kernel,
        out_shape=[
            jax.ShapeDtypeStruct((rows, width), jnp.float32),
            jax.ShapeDtypeStruct((rows, 128), jnp.float32),
        ],
        compiler_params=pltpu.CompilerParams(vmem_limit_bytes=VMEM_LIMIT),
        cost_estimate=lasting(10),
        name="local_forward",
    )(base, book_column, book_row, own, *halos)


def local_queries(
    base, book_column, book_row, own, halos, d_mixed, memory_out, local_out, mem_log, local_log, share, heads, score_scale
):
    rows, width = d_mixed.shape
    head_dim = width // heads
    count = len(halos) + 1
    span = base.shape[1]

    def kernel(
        base_ref, column_ref, row_ref, own_ref, mix_ref, mem_ref, loc_ref, mem_log_ref, log_ref, share_ref, *refs
    ):
        halo_refs, (dq_ref, diagonal_ref, gate_ref, sent_ref) = refs[: count - 1], refs[count - 1 :]
        same = column_ref[:, :1] == row_ref[:1, :]
        turned = (
            lax.broadcasted_iota(jnp.int32, (rows, rows), 0)
            + lax.broadcasted_iota(jnp.int32, (rows, rows), 1)
            == rows - 1
        ).astype(jnp.bfloat16)
        mem_deltas, deltas = [], []
        for head in range(heads):
            columns = slice(head * head_dim, (head + 1) * head_dim)
            above = slice(width + head * head_dim, width + (head + 1) * head_dim)
            twice = slice(2 * width + head * head_dim, 2 * width + (head + 1) * head_dim)
            keys = [ref[:, columns] for ref in halo_refs] + [own_ref[:, above]]
            values = [ref[:, above] for ref in halo_refs] + [own_ref[:, twice]]
            q = own_ref[:, columns]
            share_here = share_ref[head]
            d_mix, mem_here, loc_here = mix_ref[:, columns], mem_ref[:, columns], loc_ref[:, columns]
            d_mem = (share_here * d_mix).astype(jnp.bfloat16)
            d_out = ((1.0 - share_here) * d_mix).astype(jnp.bfloat16)
            sent_ref[:, columns] = d_mem
            mem_deltas.append(
                jnp.sum(d_mem.astype(jnp.float32) * mem_here, axis=1, keepdims=True)
            )
            delta = jnp.sum(d_out.astype(jnp.float32) * loc_here, axis=1, keepdims=True)
            deltas.append(delta)
            gate_ref[head : head + 1, :] = jnp.sum(
                d_mix * (mem_here - loc_here), axis=0, keepdims=True
            )
            raw = [
                lax.dot_general(q, k, contract_cols, preferred_element_type=jnp.float32) for k in keys
            ]
            bias = slanted(base_ref[head : head + 1, :], rows)[:, : count * rows]
            scores = jnp.concatenate(raw, axis=1) * score_scale + bias
            probs = jnp.exp(jnp.where(same, scores - log_ref[:, head : head + 1], masked_score))
            products = [
                lax.dot_general(d_out, v, contract_cols, preferred_element_type=jnp.float32)
                for v in values
            ]
            slopes = (probs * (jnp.concatenate(products, axis=1) - delta)).astype(jnp.bfloat16)
            slope_blocks = [slopes[:, i * rows : (i + 1) * rows] for i in range(count)]
            dq_ref[:, columns] = score_scale * sum(
                jnp.dot(s, k, preferred_element_type=jnp.float32) for s, k in zip(slope_blocks, keys)
            )
            mirrored = [
                jnp.dot(s, turned, preferred_element_type=jnp.float32) for s in slope_blocks[::-1]
            ]
            mirrored.append(jnp.zeros((rows, span - count * rows), jnp.float32))
            leaned = pltpu.roll(jnp.concatenate(mirrored, axis=1), 0, 1, stride=1, stride_axis=0)
            diagonal_ref[head : head + 1, :] = jnp.sum(leaned, axis=0, keepdims=True)
        mem_logs = [mem_log_ref[:, head : head + 1] for head in range(heads)]
        logs = [log_ref[:, head : head + 1] for head in range(heads)]
        sent_ref[:, width:] = split_tile(lane_tile(mem_logs + mem_deltas + logs + deltas, rows))

    vmem = pl.BlockSpec(memory_space=pltpu.VMEM)
    return pl.pallas_call(
        kernel,
        in_specs=[vmem] * 9 + [pl.BlockSpec(memory_space=pltpu.SMEM)] + [vmem] * len(halos),
        out_shape=[
            jax.ShapeDtypeStruct((rows, width), jnp.float32),
            jax.ShapeDtypeStruct((heads, span), jnp.float32),
            jax.ShapeDtypeStruct((heads, head_dim), jnp.float32),
            jax.ShapeDtypeStruct((rows, width + 128), jnp.bfloat16),
        ],
        compiler_params=pltpu.CompilerParams(vmem_limit_bytes=VMEM_LIMIT),
        cost_estimate=lasting(15),
        name="local_queries",
    )(base, book_column, book_row, own, d_mixed, memory_out, local_out, mem_log, local_log, share, *halos)


def local_keys(base, book_column, book_row, own, queries, sent, ratio, me, count, heads, score_scale):
    rows, width = own.shape[0], own.shape[1] // 3
    head_dim = width // heads
    groups = queries.shape[0] // rows

    def kernel(me_ref, base_ref, column_ref, row_ref, own_ref, ratio_ref, *refs):
        q_refs, g_refs, out_ref = refs[:count], refs[count : 2 * count], refs[2 * count]
        same = column_ref[:, :1] == row_ref[:1, :]
        stats = jnp.concatenate([joined_tile(ref[:, width:]).T for ref in g_refs], axis=1)
        for head in range(heads):
            columns = slice(head * head_dim, (head + 1) * head_dim)
            above = slice(width + head * head_dim, width + (head + 1) * head_dim)
            twice = slice(2 * width + head * head_dim, 2 * width + (head + 1) * head_dim)
            k, v = own_ref[:, above], own_ref[:, twice]
            qs = [ref[:, columns] for ref in q_refs]
            gs = [
                (ref[:, columns].astype(jnp.float32) * ratio_ref[head]).astype(jnp.bfloat16)
                for ref in g_refs
            ]
            raw = [
                lax.dot_general(k, q, contract_cols, preferred_element_type=jnp.float32) for q in qs
            ]
            bias = slanted(base_ref[head : head + 1, :], rows)[:, : count * rows]
            scores = jnp.concatenate(raw, axis=1) * score_scale + bias
            log = stats[2 * heads + head : 2 * heads + head + 1, :]
            delta = stats[3 * heads + head : 3 * heads + head + 1, :]
            probs = jnp.exp(jnp.where(same, scores - log, masked_score))
            products = [
                lax.dot_general(v, g, contract_cols, preferred_element_type=jnp.float32) for g in gs
            ]
            slopes = (probs * (jnp.concatenate(products, axis=1) - delta)).astype(jnp.bfloat16)
            weights = probs.astype(jnp.bfloat16)
            blocks = [slice(i * rows, (i + 1) * rows) for i in range(count)]
            d_key = sum(
                jnp.dot(slopes[:, b], q, preferred_element_type=jnp.float32) for b, q in zip(blocks, qs)
            )
            d_value = sum(
                jnp.dot(weights[:, b], g, preferred_element_type=jnp.float32)
                for b, g in zip(blocks, gs)
            )
            out_ref[:, columns] = (d_key * score_scale).astype(jnp.bfloat16)
            out_ref[:, above] = d_value.astype(jnp.bfloat16)

    def whole(array):
        return pl.BlockSpec(array.shape, lambda i, *_: (0, 0))

    def later(distance, size):
        return pl.BlockSpec((rows, size), lambda i, m: (jnp.minimum(m[0] + distance, groups - 1), 0))

    return pl.pallas_call(
        kernel,
        grid_spec=pltpu.PrefetchScalarGridSpec(
            num_scalar_prefetch=1,
            grid=(1,),
            in_specs=[whole(base), whole(book_column), whole(book_row), whole(own)]
            + [pl.BlockSpec(memory_space=pltpu.SMEM)]
            + [later(i, width) for i in range(count)]
            + [later(i, width + 128) for i in range(count)],
            out_specs=pl.BlockSpec((rows, 2 * width), lambda i, *_: (0, 0)),
        ),
        out_shape=jax.ShapeDtypeStruct((rows, 2 * width), jnp.bfloat16),
        compiler_params=pltpu.CompilerParams(vmem_limit_bytes=VMEM_LIMIT),
        cost_estimate=lasting(15),
        name="local_keys",
    )(me, base, book_column, book_row, own, ratio, *([queries] * count), *([sent] * count))


def finish_grads(parts, early, small, sources, collective_id):
    rows, width = parts.shape[0] // sources, parts.shape[1]
    depth, half = sources // 4, rows // 2
    early_width = early.shape[1]
    mesh_type = pl.DeviceIdType.MESH

    def kernel(parts_ref, early_ref, small_ref, late_out, early_out, small_out, *refs):
        half_a, half_b, from_x, from_y, from_z, out_x, out_y, out_z, smalls, core_small = refs[:10]
        send, recv_a, recv_b, recv_x, recv_y, recv_z, small_send, small_recv, core_send, core_recv = refs[10:]
        me, column, beside_x, beside_y, across, index_of = grid_place(depth)
        core = lax.axis_index("dp")
        to_x, to_y = index_of(0, beside_x), index_of(0, beside_y)
        barrier = pltpu.get_barrier_semaphore()
        peers = [lax.rem(me + k, sources) for k in range(1, sources)]
        for peer in peers:
            pl.semaphore_signal(barrier, inc=1, device_id={"mem": peer}, device_id_type=mesh_type)
        pl.semaphore_signal(barrier, inc=1, device_id={"dp": 1 - core}, device_id_type=mesh_type)
        pl.semaphore_wait(barrier, sources)
        order = [*range(1, depth), 0]
        sent = []

        def piece(index, part):
            return parts_ref.at[pl.ds(pl.multiple_of(index * rows + part * half, half), half), :]

        def part_rows(part):
            return pl.ds(part * half, half)

        def push(source, target, kind, k, recv_sem, device):
            copy = remote(source, target, send.at[kind, k], recv_sem, device)
            copy.start()
            sent.append(copy)

        def arrived(target, recv_sem):
            remote(target, target, send.at[0, 0], recv_sem, to_x).wait_recv()

        def added(blocks):
            total = blocks[0][...].astype(jnp.float32)
            for block in blocks[1:]:
                total = total + block[...].astype(jnp.float32)
            return total

        def across_cores(source, target, i):
            copy = pltpu.make_async_remote_copy(
                src_ref=source,
                dst_ref=target,
                send_sem=core_send.at[i],
                recv_sem=core_recv.at[i],
                device_id={"dp": 1 - core},
                device_id_type=mesh_type,
            )
            copy.start()
            return copy

        for k in order:
            far = index_of(k, across)
            push(piece(far, 0), half_a.at[k], 0, k, recv_a.at[k], to_x)
            push(piece(far, 1), half_b.at[k], 1, k, recv_b.at[k], to_y)
        smalls[me] = small_ref[...]
        for i, peer in enumerate(peers):
            copy = remote(small_ref, smalls.at[me], small_send.at[i], small_recv.at[me], peer)
            copy.start()
            sent.append(copy)
        early_copy = across_cores(early_ref, early_out.at[core], 0)
        early_out[core] = early_ref[...]
        for k in order:
            push(piece(index_of(k, beside_x), 0), from_x.at[k, part_rows(0)], 2, k, recv_x.at[0, k], to_x)
            push(piece(index_of(k, beside_y), 1), from_y.at[k, part_rows(1)], 3, k, recv_y.at[1, k], to_y)
        for k in order:
            arrived(half_a.at[k], recv_a.at[k])
            out_y[k] = added([piece(index_of(k, beside_y), 0), half_a.at[k]]).astype(parts.dtype)
            push(out_y.at[k], from_y.at[k, part_rows(0)], 4, k, recv_y.at[0, k], to_y)
            arrived(half_b.at[k], recv_b.at[k])
            out_x[k] = added([piece(index_of(k, beside_x), 1), half_b.at[k]]).astype(parts.dtype)
            push(out_x.at[k], from_x.at[k, part_rows(1)], 5, k, recv_x.at[1, k], to_x)
        for peer in peers:
            arrived(smalls.at[peer], small_recv.at[peer])
        group_small = smalls[0]
        for i in range(1, sources):
            group_small = group_small + smalls[i]
        core_small[0] = group_small
        small_copy = across_cores(core_small.at[0], core_small.at[1], 1)
        for k in order:
            for part in (0, 1):
                arrived(from_x.at[k, part_rows(part)], recv_x.at[part, k])
                arrived(from_y.at[k, part_rows(part)], recv_y.at[part, k])
            if k:
                for part in (0, 1):
                    here = part_rows(part)
                    blocks = [piece(index_of(k, column), part), from_x.at[k, here], from_y.at[k, here]]
                    out_z[k, here] = added(blocks).astype(parts.dtype)
                push(out_z.at[k], from_z.at[k], 6, k, recv_z.at[k], index_of(k, column))
        for k in range(1, depth):
            arrived(from_z.at[k], recv_z.at[k])
        for part in (0, 1):
            here = part_rows(part)
            blocks = [piece(me, part), from_x.at[0, here], from_y.at[0, here]]
            blocks += [from_z.at[k, here] for k in range(1, depth)]
            late_out[core, here] = added(blocks).astype(parts.dtype)
        late_copy = across_cores(late_out.at[core], late_out.at[core], 2)
        for copy in (early_copy, small_copy, late_copy):
            copy.wait()
        small_out[...] = core_small[0] + core_small[1]
        for copy in sent:
            copy.wait_send()

    def slots(size):
        return pltpu.VMEM((depth, size, width), parts.dtype)

    vmem = pl.BlockSpec(memory_space=pltpu.VMEM)
    return pl.pallas_call(
        kernel,
        in_specs=[vmem] * 3,
        out_specs=[vmem] * 3,
        out_shape=[
            jax.ShapeDtypeStruct((2, rows, width), parts.dtype),
            jax.ShapeDtypeStruct((2, rows, early_width), early.dtype),
            jax.ShapeDtypeStruct(small.shape, small.dtype),
        ],
        scratch_shapes=[slots(half), slots(half), slots(rows), slots(rows), slots(rows)]
        + [slots(half), slots(half), slots(rows)]
        + [pltpu.VMEM((sources, *small.shape), small.dtype), pltpu.VMEM((2, *small.shape), small.dtype)]
        + [pltpu.SemaphoreType.DMA((7, depth))]
        + [pltpu.SemaphoreType.DMA((depth,))] * 2
        + [pltpu.SemaphoreType.DMA((2, depth))] * 2
        + [pltpu.SemaphoreType.DMA((depth,))]
        + [pltpu.SemaphoreType.DMA((sources,))] * 2
        + [pltpu.SemaphoreType.DMA((3,))] * 2,
        compiler_params=pltpu.CompilerParams(
            collective_id=collective_id, has_side_effects=True, vmem_limit_bytes=VMEM_LIMIT
        ),
        cost_estimate=lasting(55),
        name="finish_grads",
    )(parts, early, small)


def on_device(
    tokens,
    attn_gain,
    qkv_weight,
    out_weight,
    bias_table,
    gate_logit,
    ffn_gain,
    up_weight,
    down_weight,
    memory_keys,
    memory_values,
    book_lengths,
    slot_shard,
    slot_index,
    slot_live,
    cotangent,
):
    rows, width = tokens.shape
    heads, buckets = bias_table.shape
    head_dim = width // heads
    top_count = slot_index.shape[2]
    hidden = up_weight.shape[1]
    groups = lax.axis_size("mem")
    capacity = max(2, 3 * rows * heads * top_count // (2 * groups))
    score_scale = 1.0 / math.sqrt(head_dim)
    repeats = W // rows
    span = W + 2 * rows
    me = lax.axis_index("mem")
    first_pos = me * rows
    lengths = book_lengths[0]
    window = jnp.arange(W + rows, dtype=jnp.int32)
    key_pos = first_pos - W + window
    key_book = jnp.where(key_pos >= 0, book_of(key_pos, lengths), -1)
    later_book = book_of(first_pos + window, lengths)
    own_book = jnp.broadcast_to(later_book[:rows, None], (rows, 128))
    key_book = jnp.broadcast_to(key_book[None, :], (8, W + rows))
    later_book = jnp.broadcast_to(later_book[None, :], (8, W + rows))
    bucket = bucket_of(jnp.arange(W, dtype=jnp.int32))
    one_hot = (bucket[:, None] == jnp.arange(buckets, dtype=jnp.int32)).astype(jnp.float32)
    offset_bias = jnp.einsum("rb,hb->hr", one_hot, bias_table, precision=lax.Precision.HIGHEST)
    after_bias = jnp.pad(offset_bias, ((0, 0), (0, span - W)), constant_values=masked_score)
    before_bias = jnp.pad(
        offset_bias[:, ::-1], ((0, 0), (1, span - W - 1)), constant_values=masked_score
    )
    tokens_f = tokens.astype(jnp.float32)
    normed_f, norm_in_back = jax.vjp(normed, tokens_f, attn_gain)
    normed_in = normed_f.astype(jnp.bfloat16)
    projected = jnp.dot(normed_in, qkv_weight, preferred_element_type=jnp.float32).astype(
        jnp.bfloat16
    )
    halos = [
        passed_along(projected[:, width:], "mem", distance) for distance in range(repeats, 0, -1)
    ]
    local_out, local_log = local_forward(
        before_bias, own_book, key_book, projected, halos, heads, score_scale
    )
    slots = memory_keys.shape[0]
    requests = place_requests(slot_shard, slot_index, slot_live, groups, capacity, slots)
    incoming = lax.all_to_all(requests, "mem", split_axis=0, concat_axis=0, tiled=True)
    row_ids = incoming // slots
    limits = jnp.arange(heads + 1, dtype=jnp.int32) * (rows * slots)
    bounds = jnp.sum((incoming[:, None, :] < limits[None, :, None]).astype(jnp.int32), axis=2)
    index = jnp.where(row_ids < heads * rows, row_ids // rows * slots + incoming % slots, 0)
    key_rows, value_rows = gather_rows(
        index.reshape(-1), bounds[:, heads], memory_keys, memory_values, heads, groups, capacity
    )
    all_queries = lax.all_gather(projected[:, :width], "mem", axis=0, tiled=True)
    entry_rows = row_ids[:, None, :]
    partial = memory_forward(
        bounds.reshape(-1),
        all_queries,
        key_rows,
        value_rows,
        entry_rows,
        heads,
        groups,
        rows,
        score_scale,
    )
    if groups == 16:
        memory_out, mem_log = merge_partials(partial, groups, 1, heads)
    else:
        partial = lax.all_to_all(
            partial.reshape(groups, rows, width + 128),
            "mem",
            split_axis=0,
            concat_axis=0,
            tiled=True,
        ).reshape(groups * rows, width + 128)
        memory_out, mem_log = combine_partials(partial, heads, groups, rows)
    gate_share = jax.nn.sigmoid(gate_logit)
    share_wide = jnp.repeat(gate_share, head_dim)[None, :]
    mixed_heads = (share_wide * memory_out + (1.0 - share_wide) * local_out).astype(jnp.bfloat16)
    residual = tokens_f + jnp.dot(mixed_heads, out_weight, preferred_element_type=jnp.float32)
    normed_mid_f, norm_mid_back = jax.vjp(normed, residual, ffn_gain)
    normed_mid = normed_mid_f.astype(jnp.bfloat16)
    up_proj = jnp.dot(normed_mid, up_weight, preferred_element_type=jnp.float32)
    activated_f, gelu_back = jax.vjp(gelu_exact, up_proj)
    activated = activated_f.astype(jnp.bfloat16)
    ffn_branch = lax.dot_general(
        activated, down_weight, contract_cols, preferred_element_type=jnp.float32
    )
    block_out = (residual + ffn_branch).astype(jnp.bfloat16)
    d_act = jnp.dot(cotangent, down_weight, preferred_element_type=jnp.float32)
    d_up = gelu_back(d_act)[0].astype(jnp.bfloat16)
    d_mid = lax.dot_general(d_up, up_weight, contract_cols, preferred_element_type=jnp.float32)
    d_resid_part, ffn_gain_part = norm_mid_back(d_mid)
    d_residual = cotangent.astype(jnp.float32) + d_resid_part
    d_branch = d_residual.astype(jnp.bfloat16)
    d_mixed = lax.dot_general(
        d_branch, out_weight, contract_cols, preferred_element_type=jnp.float32
    )
    early_halves = weight_halves([(mixed_heads, d_branch), (normed_mid, d_up), (cotangent, activated)])
    d_queries, diagonals, gate_products, sent_grads = local_queries(
        before_bias,
        own_book,
        key_book,
        projected,
        halos,
        d_mixed,
        memory_out,
        local_out,
        mem_log,
        local_log,
        gate_share,
        heads,
        score_scale,
    )
    gate_part = jnp.sum(gate_products, axis=1) * gate_share * (1.0 - gate_share)
    bias_part = jnp.dot(diagonals[:, rows - 1 : rows - 1 + W], one_hot, precision=lax.Precision.HIGHEST)
    sent_grads, early_halves = lax.optimization_barrier((sent_grads, early_halves))
    early_sums = scattered(early_halves)
    if groups == 16:
        all_grads = gather_group(sent_grads, groups, 2)
    else:
        all_grads = lax.all_gather(sent_grads, "mem", axis=0, tiled=True)
    d_partial = memory_backward(
        bounds.reshape(-1),
        all_queries,
        all_grads,
        key_rows,
        value_rows,
        entry_rows,
        heads,
        groups,
        rows,
        score_scale,
    )
    d_keys_values = local_keys(
        after_bias,
        own_book,
        later_book,
        projected,
        all_queries,
        all_grads,
        (1.0 - gate_share) / gate_share,
        me[None],
        repeats + 1,
        heads,
        score_scale,
    )
    if groups == 16:
        d_partial = sum_blocks(d_partial, groups, 3)
    else:
        d_partial, d_keys_values = lax.optimization_barrier((d_partial, d_keys_values))
        d_partial = jnp.sum(
            lax.all_to_all(
                d_partial.reshape(groups, rows, width), "mem", split_axis=0, concat_axis=0, tiled=True
            ).astype(jnp.float32),
            axis=0,
        )
    d_queries = (d_queries + d_partial * score_scale).astype(jnp.bfloat16)
    d_projected = jnp.concatenate([d_queries, d_keys_values], axis=1)
    d_in = lax.dot_general(
        d_projected, qkv_weight, contract_cols, preferred_element_type=jnp.float32
    )
    d_tokens_part, attn_gain_part = norm_in_back(d_in)
    tokens_grad = d_residual + d_tokens_part
    late_halves = weight_halves([(normed_in, d_projected)])
    late_halves, early_sums = lax.optimization_barrier((late_halves, early_sums))
    small = jnp.concatenate(
        [attn_gain_part, ffn_gain_part, bias_part.reshape(-1), gate_part], axis=0
    )
    small = jnp.pad(small, (0, -small.shape[0] % 1024)).reshape(-1, 128)
    if groups == 16:
        late_both, early_both, small = finish_grads(late_halves, early_sums, small, groups, 4)
    else:
        late_both = lax.all_gather(scattered(late_halves), "dp", axis=0)
        early_both = lax.all_gather(early_sums, "dp", axis=0)
        small = lax.psum(small, ("dp", "mem"))
    small = small.reshape(-1)
    out_grad, up_grad, down_grad = whole_grads(early_both, [width, hidden, hidden])
    qkv_grad = whole_grads(late_both, [3 * width])[0]
    at_bias = 2 * width + heads * buckets
    return (
        block_out,
        tokens_grad,
        qkv_grad,
        out_grad,
        up_grad,
        down_grad,
        small[:width],
        small[width : 2 * width],
        small[2 * width : at_bias].reshape(heads, buckets),
        small[at_bias : at_bias + heads],
    )


def solution(mesh):
    in_specs = (
        P(("dp", "mem"), None),
        P(),
        P(),
        P(),
        P(),
        P(),
        P(),
        P(),
        P(),
        P("mem", None),
        P("mem", None),
        P("dp", None),
        P(("dp", "mem"), None, None, None),
        P(("dp", "mem"), None, None),
        P(("dp", "mem"), None, None),
        P(("dp", "mem"), None),
    )
    out_specs = (
        P(("dp", "mem"), None),
        P(("dp", "mem"), None),
        P("mem", None),
        P("mem", None),
        P("mem", None),
        P("mem", None),
        P(),
        P(),
        P(),
        P(),
    )
    return jax.shard_map(
        on_device, mesh=mesh, in_specs=in_specs, out_specs=out_specs, check_vma=False
    )
```

```python
import math

import jax
import jax.numpy as jnp
from jax import lax
from jax.experimental import pallas as pl
from jax.experimental.pallas import tpu as pltpu
from jax.sharding import PartitionSpec as P

W = 512
VMEM_LIMIT = 56 * 1024 * 1024


eps_norm = 1e-06
bucket_edges = tuple((math.ceil(16 * 8 ** (edge_step / 16)) for edge_step in range(1, 16)))
masked_score = -1e30
dead_score = -10000.0
contract_rows = (((0,), (0,)), ((), ()))
contract_cols = (((1,), (1,)), ((), ()))


def passed_along(value, axis, by):
    size = lax.axis_size(axis)
    pairs = [(i, i + by) for i in range(size) if 0 <= i + by < size]
    return lax.ppermute(value, axis, pairs)


def swapped(value):
    return lax.ppermute(value, "dp", [(0, 1), (1, 0)])


def bucket_of(offset):
    past_edges = sum(((offset >= edge_pos).astype(jnp.int32) for edge_pos in bucket_edges))
    return jnp.where(offset < 16, offset, 16 + past_edges)


def normed(values, gain_vec):
    return (
        values * lax.rsqrt(jnp.mean(values * values, axis=-1, keepdims=True) + eps_norm) * gain_vec
    )


def gelu_exact(values):
    return jax.nn.gelu(values, approximate=False)


def book_of(positions, lengths):
    book_ends = jnp.cumsum(lengths, dtype=jnp.int32)
    return jnp.sum((positions[..., None] >= book_ends).astype(jnp.int32), axis=-1)


def place_requests(slot_shard, slot_index, slot_live, owners, capacity, slots):
    rows, heads, top_count = slot_index.shape
    entries = rows * heads * top_count
    row_of = (
        jnp.arange(heads, dtype=jnp.int32)[None, :] * rows
        + jnp.arange(rows, dtype=jnp.int32)[:, None]
    )
    place = row_of[:, :, None] * top_count + jnp.arange(top_count, dtype=jnp.int32)
    owner = jnp.where(slot_live > 0, slot_shard[..., 0], owners)
    keys, picked = lax.sort(
        ((owner * entries + place).reshape(-1), slot_index.reshape(-1)), num_keys=1
    )
    ends = jnp.sum(
        (keys[None, :] < (jnp.arange(owners, dtype=jnp.int32) + 1)[:, None] * entries).astype(jnp.int32),
        axis=1,
    )
    starts = jnp.concatenate([jnp.zeros((1,), jnp.int32), ends[:-1]])
    codes = keys % entries // top_count * slots + picked
    tall = -(-entries // 128)
    codes = jnp.pad(codes, (0, tall * 128 - entries)).reshape(tall, 128)
    long = capacity // 128
    empty = heads * rows * slots

    def kernel(starts_ref, ends_ref, codes_ref, lists_ref, padded):
        padded[:tall, :] = codes_ref[...]
        padded[tall:, :] = jnp.zeros((long + 8, 128), jnp.int32)
        lane = lax.broadcasted_iota(jnp.int32, (long, 128), 1)
        place = lax.broadcasted_iota(jnp.int32, (long, 128), 0) * 128 + lane

        @pl.loop(0, owners)
        def _(i):
            start, end = starts_ref[i], ends_ref[i]
            shift = start % 128
            lines = padded[pl.ds(start // 128, long + 1), :]
            turned = pltpu.roll(lines, (128 - shift) % 128, 1)
            joined = jnp.where(lane < 128 - shift, turned[:long], turned[1:])
            lists_ref[i] = jnp.where(place < end - start, joined, empty)

    return pl.pallas_call(
        kernel,
        in_specs=[pl.BlockSpec(memory_space=pltpu.SMEM)] * 2 + [pl.BlockSpec(memory_space=pltpu.VMEM)],
        out_shape=jax.ShapeDtypeStruct((owners, long, 128), jnp.int32),
        scratch_shapes=[pltpu.VMEM((tall + long + 8, 128), jnp.int32)],
        cost_estimate=lasting(3),
        name="make_lists",
    )(starts, ends, codes)


def gather_rows(index, counts, memory_keys, memory_values, heads, sources, capacity):
    slots, width = memory_keys.shape
    head_dim = width // heads
    step = 16

    def kernel(index_ref, counts_ref, keys, values, out_keys, out_values, key_table, value_table, key_rows, value_rows):
        i = pl.program_id(0)

        @pl.when(i == 0)
        def _():
            key_rows[...] = jnp.zeros_like(key_rows)
            value_rows[...] = jnp.zeros_like(value_rows)

        @pl.when(i < heads)
        def _():
            place = pl.ds(pl.multiple_of(i * slots, slots), slots)
            key_table[place, :] = keys[...].astype(jnp.float32)
            value_table[place, :] = values[...].astype(jnp.float32)

        @pl.when(i >= heads)
        def _():
            source = i - heads

            @pl.loop(0, (counts_ref[source] + step - 1) // step)
            def _(group):
                first = pl.multiple_of(group * step, step)
                for u in range(step):
                    row = index_ref[source * capacity + first + u]
                    key_rows[pl.ds(first + u, 1), :] = key_table[pl.ds(row, 1), :]
                    value_rows[pl.ds(first + u, 1), :] = value_table[pl.ds(row, 1), :]

            out_keys[...] = key_rows[...].astype(jnp.bfloat16)
            out_values[...] = value_rows[...].astype(jnp.bfloat16)

    table_spec = pl.BlockSpec((slots, head_dim), lambda i, *_: (0, jnp.minimum(i, heads - 1)))
    out_spec = pl.BlockSpec((capacity, head_dim), lambda i, *_: (jnp.maximum(i - heads, 0), 0))
    out_shape = jax.ShapeDtypeStruct((sources * capacity, head_dim), jnp.bfloat16)
    return pl.pallas_call(
        kernel,
        grid_spec=pltpu.PrefetchScalarGridSpec(
            num_scalar_prefetch=2,
            grid=(heads + sources,),
            in_specs=[table_spec, table_spec],
            out_specs=[out_spec, out_spec],
            scratch_shapes=[
                pltpu.VMEM((heads * slots, head_dim), jnp.float32),
                pltpu.VMEM((heads * slots, head_dim), jnp.float32),
                pltpu.VMEM((capacity, head_dim), jnp.float32),
                pltpu.VMEM((capacity, head_dim), jnp.float32),
            ],
        ),
        out_shape=[out_shape, out_shape],
        compiler_params=pltpu.CompilerParams(vmem_limit_bytes=VMEM_LIMIT),
        cost_estimate=lasting(42),
        name="gather_rows",
    )(index, counts, memory_keys, memory_values)


def lasting(microseconds):
    return pl.CostEstimate(flops=0, bytes_accessed=3_000_000 * microseconds, transcendentals=0)


def triple(stat):
    part = lax.broadcasted_iota(jnp.int32, stat.shape, 1) // 16
    high = stat.astype(jnp.bfloat16).astype(jnp.float32)
    rest = stat - high
    middle = rest.astype(jnp.bfloat16).astype(jnp.float32)
    low = rest - middle
    chosen = jnp.where(part == 0, high, jnp.where(part == 1, middle, jnp.where(part == 2, low, 0.0)))
    return chosen.astype(jnp.bfloat16)


def window_of(bounds, source, head, heads, span, capacity):
    first = bounds[source * (heads + 1) + head]
    last = bounds[source * (heads + 1) + head + 1]
    start = jnp.minimum((first // 128) * 128, capacity - span)
    extra = jnp.maximum(last - start - span + span - 1, 0) // span
    return start, extra


def owned(id_ref, start, head, rows, span, least):
    lines = id_ref[0, pl.ds(start // 128, span // 128), :]
    token = lax.broadcasted_iota(jnp.int32, (rows, 128), 0) + head * rows
    masks = []
    for i in range(span // 128):
        mask = lines[i : i + 1, :] == token
        if least is not None:
            place = lax.broadcasted_iota(jnp.int32, (1, 128), 1) + start + i * 128
            mask = mask & (place >= least)
        masks.append(mask)
    return jnp.concatenate(masks, axis=1)


def memory_forward(bounds, queries, key_rows, value_rows, row_ids, heads, sources, rows, score_scale):
    capacity, head_dim = key_rows.shape[0] // sources, key_rows.shape[1]
    width = heads * head_dim
    span = min(512, capacity)

    def kernel(bounds_ref, q_ref, k_ref, v_ref, id_ref, out_ref, sums, tops, totals):
        source = pl.program_id(0)
        lane = lax.broadcasted_iota(jnp.int32, (rows, 128), 1) % 16

        def scores_of(head, start, least):
            here = pl.ds(pl.multiple_of(start, 128), span)
            mine = owned(id_ref, start, head, rows, span, least)
            q = q_ref[:, head * head_dim : (head + 1) * head_dim]
            raw = lax.dot_general(q, k_ref[here, :], contract_cols, preferred_element_type=jnp.float32)
            return jnp.where(mine, raw * score_scale, masked_score), mine, v_ref[here, :]

        windows = [window_of(bounds_ref, source, head, heads, span, capacity) for head in range(heads)]
        top_tile = jnp.zeros((rows, 128), jnp.float32)
        total_tile = jnp.zeros((rows, 128), jnp.float32)
        for head in range(heads):
            scores, mine, v = scores_of(head, windows[head][0], None)
            top = jnp.max(scores, axis=1, keepdims=True)
            weights = jnp.where(mine, jnp.exp(scores - top), 0.0)
            sums[:, head * head_dim : (head + 1) * head_dim] = jnp.dot(
                weights.astype(jnp.bfloat16), v, preferred_element_type=jnp.float32
            )
            top_tile = jnp.where(lane == head, top, top_tile)
            total_tile = jnp.where(
                lane == heads + head, jnp.sum(weights, axis=1, keepdims=True), total_tile
            )
        tops[...] = top_tile
        totals[...] = total_tile
        more = sum(extra for _, extra in windows)

        @pl.when(more > 0)
        def _():
            for head in range(heads):
                start, extra = windows[head]
                columns = slice(head * head_dim, (head + 1) * head_dim)

                @pl.loop(0, extra)
                def _(turn):
                    least = start + (turn + 1) * span
                    scores, mine, v = scores_of(head, jnp.minimum(least, capacity - span), least)
                    old_top = jnp.max(
                        jnp.where(lane == head, tops[...], masked_score), axis=1, keepdims=True
                    )
                    top = jnp.maximum(old_top, jnp.max(scores, axis=1, keepdims=True))
                    weights = jnp.where(mine, jnp.exp(scores - top), 0.0)
                    faded = jnp.exp(old_top - top)
                    sums[:, columns] = sums[:, columns] * faded + jnp.dot(
                        weights.astype(jnp.bfloat16), v, preferred_element_type=jnp.float32
                    )
                    tops[...] = jnp.where(lane == head, top, tops[...])
                    totals[...] = jnp.where(
                        lane == heads + head,
                        totals[...] * faded + jnp.sum(weights, axis=1, keepdims=True),
                        totals[...],
                    )

        out_ref[:, :width] = sums[...].astype(jnp.bfloat16)
        out_ref[:, width:] = triple(jnp.where(lane < heads, tops[...], totals[...]))

    return pl.pallas_call(
        kernel,
        grid_spec=pltpu.PrefetchScalarGridSpec(
            num_scalar_prefetch=1,
            grid=(sources,),
            in_specs=[
                pl.BlockSpec((rows, width), lambda i, *_: (i, 0)),
                pl.BlockSpec((capacity, head_dim), lambda i, *_: (i, 0)),
                pl.BlockSpec((capacity, head_dim), lambda i, *_: (i, 0)),
                pl.BlockSpec((1, capacity // 128, 128), lambda i, *_: (i, 0, 0)),
            ],
            out_specs=pl.BlockSpec((rows, width + 128), lambda i, *_: (i, 0)),
            scratch_shapes=[
                pltpu.VMEM((rows, width), jnp.float32),
                pltpu.VMEM((rows, 128), jnp.float32),
                pltpu.VMEM((rows, 128), jnp.float32),
            ],
        ),
        out_shape=jax.ShapeDtypeStruct((sources * rows, width + 128), jnp.bfloat16),
        compiler_params=pltpu.CompilerParams(vmem_limit_bytes=VMEM_LIMIT),
        cost_estimate=lasting(41),
        name="memory_forward",
    )(bounds, queries, key_rows, value_rows, row_ids)


def combine_partials(partial, heads, sources, rows):
    width = partial.shape[1] - 128
    head_dim = width // heads

    def kernel(part_ref, out_ref, log_ref, sums, tops, totals):
        i = pl.program_id(0)

        @pl.when(i == 0)
        def _():
            sums[...] = jnp.zeros_like(sums)
            tops[...] = jnp.full_like(tops, masked_score)
            totals[...] = jnp.zeros_like(totals)

        stat = part_ref[:, width:].astype(jnp.float32)
        stat = stat + pltpu.roll(stat, 128 - 16, 1) + pltpu.roll(stat, 128 - 32, 1)
        new_total = pltpu.roll(stat, 128 - heads, 1)
        top = jnp.maximum(tops[...], stat)
        old_fade, new_fade = jnp.exp(tops[...] - top), jnp.exp(stat - top)
        tops[...] = top
        totals[...] = totals[...] * old_fade + new_total * new_fade
        for head in range(heads):
            columns = slice(head * head_dim, (head + 1) * head_dim)
            sums[:, columns] = (
                sums[:, columns] * old_fade[:, head : head + 1]
                + part_ref[:, columns].astype(jnp.float32) * new_fade[:, head : head + 1]
            )

        @pl.when(i == sources - 1)
        def _():
            live = totals[...] > 0
            total = jnp.where(live, totals[...], 1.0)
            log_ref[...] = jnp.where(live, tops[...] + jnp.log(total), 0.0)
            for head in range(heads):
                columns = slice(head * head_dim, (head + 1) * head_dim)
                out_ref[:, columns] = sums[:, columns] / total[:, head : head + 1]

    return pl.pallas_call(
        kernel,
        grid=(sources,),
        in_specs=[pl.BlockSpec((rows, width + 128), lambda i: (i, 0))],
        out_specs=[
            pl.BlockSpec((rows, width), lambda i: (0, 0)),
            pl.BlockSpec((rows, 128), lambda i: (0, 0)),
        ],
        scratch_shapes=[
            pltpu.VMEM((rows, width), jnp.float32),
            pltpu.VMEM((rows, 128), jnp.float32),
            pltpu.VMEM((rows, 128), jnp.float32),
        ],
        out_shape=[
            jax.ShapeDtypeStruct((rows, width), jnp.float32),
            jax.ShapeDtypeStruct((rows, 128), jnp.float32),
        ],
        compiler_params=pltpu.CompilerParams(vmem_limit_bytes=VMEM_LIMIT),
        cost_estimate=lasting(13),
        name="combine_partials",
    )(partial)


def memory_backward(bounds, queries, grads, key_rows, value_rows, row_ids, heads, sources, rows, score_scale):
    capacity, head_dim = key_rows.shape[0] // sources, key_rows.shape[1]
    width = heads * head_dim
    span = min(512, capacity)

    def kernel(bounds_ref, q_ref, g_ref, k_ref, v_ref, id_ref, out_ref, sums):
        source = pl.program_id(0)
        stat = joined_tile(g_ref[:, width : width + 128])

        def term(column):
            return stat[:, column : column + 1]

        def part_of(head, start, least):
            here = pl.ds(pl.multiple_of(start, 128), span)
            columns = slice(head * head_dim, (head + 1) * head_dim)
            mine = owned(id_ref, start, head, rows, span, least)
            k, v = k_ref[here, :], v_ref[here, :]
            raw = lax.dot_general(
                q_ref[:, columns], k, contract_cols, preferred_element_type=jnp.float32
            )
            products = lax.dot_general(
                g_ref[:, columns], v, contract_cols, preferred_element_type=jnp.float32
            )
            probs = jnp.exp(jnp.where(mine, raw * score_scale - term(head), dead_score))
            slopes = (probs * (products - term(heads + head))).astype(jnp.bfloat16)
            return jnp.dot(slopes, k, preferred_element_type=jnp.float32)

        windows = [window_of(bounds_ref, source, head, heads, span, capacity) for head in range(heads)]
        for head in range(heads):
            sums[:, head * head_dim : (head + 1) * head_dim] = part_of(head, windows[head][0], None)
        more = sum(extra for _, extra in windows)

        @pl.when(more > 0)
        def _():
            for head in range(heads):
                start, extra = windows[head]
                columns = slice(head * head_dim, (head + 1) * head_dim)

                @pl.loop(0, extra)
                def _(turn):
                    least = start + (turn + 1) * span
                    sums[:, columns] += part_of(head, jnp.minimum(least, capacity - span), least)

        out_ref[...] = sums[...].astype(jnp.bfloat16)

    return pl.pallas_call(
        kernel,
        grid_spec=pltpu.PrefetchScalarGridSpec(
            num_scalar_prefetch=1,
            grid=(sources,),
            in_specs=[
                pl.BlockSpec((rows, width), lambda i, *_: (i, 0)),
                pl.BlockSpec((rows, width + 128), lambda i, *_: (i, 0)),
                pl.BlockSpec((capacity, head_dim), lambda i, *_: (i, 0)),
                pl.BlockSpec((capacity, head_dim), lambda i, *_: (i, 0)),
                pl.BlockSpec((1, capacity // 128, 128), lambda i, *_: (i, 0, 0)),
            ],
            out_specs=pl.BlockSpec((rows, width), lambda i, *_: (i, 0)),
            scratch_shapes=[pltpu.VMEM((rows, width), jnp.float32)],
        ),
        out_shape=jax.ShapeDtypeStruct((sources * rows, width), jnp.bfloat16),
        compiler_params=pltpu.CompilerParams(vmem_limit_bytes=VMEM_LIMIT),
        cost_estimate=lasting(35),
        name="memory_backward",
    )(bounds, queries, grads, key_rows, value_rows, row_ids)


def remote(source, target, send_sem, recv_sem, device):
    return pltpu.make_async_remote_copy(
        src_ref=source,
        dst_ref=target,
        send_sem=send_sem,
        recv_sem=recv_sem,
        device_id={"mem": device},
        device_id_type=pl.DeviceIdType.MESH,
    )


def grid_place(depth):
    me = lax.axis_index("mem")
    layer, column = me // 4, me % 4
    beside_x = column + 1 - 2 * (column % 2)
    beside_y = column + 2 - 4 * (column // 2)
    across = 3 - column

    def index_of(step, place):
        return (layer + step + depth) % depth * 4 + place

    return me, column, beside_x, beside_y, across, index_of


def greet(devices):
    barrier = pltpu.get_barrier_semaphore()
    for device in devices:
        pl.semaphore_signal(
            barrier, inc=1, device_id={"mem": device}, device_id_type=pl.DeviceIdType.MESH
        )
    pl.semaphore_wait(barrier, len(devices))


def gather_group(block, sources, collective_id):
    rows, width = block.shape
    depth, half = sources // 4, rows // 2
    slots = 2 * depth - 1

    def kernel(x_ref, out_ref, own_sem, send, recv):
        me = lax.axis_index("mem")
        layer, column = me // 4, me % 4
        to_x = me + 1 - 2 * (column % 2)
        to_y = me + 2 - 4 * (column // 2)
        across = layer * 4 + 3 - column
        has_above, has_below = layer + 1 < depth, layer > 0
        barrier = pltpu.get_barrier_semaphore()

        def signal(device):
            pl.semaphore_signal(
                barrier, inc=1, device_id={"mem": device}, device_id_type=pl.DeviceIdType.MESH
            )

        signal(to_x)
        signal(to_y)
        pl.when(has_above)(lambda: signal(me + 4))
        pl.when(has_below)(lambda: signal(me - 4))
        pl.semaphore_wait(barrier, 2 + has_above.astype(jnp.int32) + has_below.astype(jnp.int32))

        def part_of(index, part):
            start = pl.multiple_of(index * rows + part * half, half)
            return out_ref.at[pl.ds(start, half), :]

        own = pltpu.make_async_copy(x_ref, out_ref.at[pl.ds(pl.multiple_of(me * rows, rows), rows), :], own_sem)
        own.start()
        sent = []

        def push(condition, source, target, kind, slot, to_slot, part, device):
            copy = remote(source, target, send.at[kind, slot, part], recv.at[kind, to_slot, part], device)
            if condition is None:
                copy.start()
            else:
                pl.when(condition)(copy.start)
            sent.append((condition, copy))

        def arrived(index, kind, slot, part):
            target = part_of(index, part)
            remote(target, target, send.at[kind, slot, part], recv.at[kind, slot, part], to_x).wait_recv()

        def up_slot(distance):
            return distance

        def down_slot(distance):
            return depth - 1 + distance

        for part in (0, 1):
            mine = x_ref.at[pl.ds(part * half, half), :]
            push(has_above, mine, part_of(me, part), 0, 0, down_slot(1), part, me + 4)
            push(has_below, mine, part_of(me, part), 1, 0, up_slot(1), part, me - 4)
            mine_y = x_ref.at[pl.ds((1 - part) * half, half), :]
            push(None, mine, part_of(me, part), 2, 0, 0, part, to_x)
            push(None, mine_y, part_of(me, 1 - part), 3, 0, 0, 1 - part, to_y)

        def pass_on(condition, step, slot):
            def go():
                arrived(to_x + step, 2, slot, 0)
                copy_a.start()
                arrived(to_y + step, 3, slot, 1)
                copy_b.start()

            source_a, source_b = part_of(to_x + step, 0), part_of(to_y + step, 1)
            copy_a = remote(source_a, source_a, send.at[4, slot, 0], recv.at[4, slot, 0], to_y)
            copy_b = remote(source_b, source_b, send.at[5, slot, 1], recv.at[5, slot, 1], to_x)
            sent.append((condition, copy_a))
            sent.append((condition, copy_b))
            if condition is None:
                go()
            else:
                pl.when(condition)(go)

        for distance in range(1, depth):
            from_above, from_below = layer + distance < depth, layer - distance >= 0

            def take(kind, back_kind, step, slot, next_slot, onward, onward_device):
                for part in (0, 1):
                    arrived(me + step, kind, slot, part)
                    here = part_of(me + step, part)
                    if next_slot is not None:
                        pl.when(onward)(
                            remote(
                                here, here, send.at[kind, slot, part], recv.at[kind, next_slot, part], onward_device
                            ).start
                        )
                    remote(here, here, send.at[2, slot, part], recv.at[2, slot, part], to_x).start()
                    remote(here, here, send.at[3, slot, part], recv.at[3, slot, part], to_y).start()

            last = distance == depth - 1
            pl.when(from_above)(
                lambda: take(
                    1, 0, 4 * distance, up_slot(distance), None if last else up_slot(distance + 1), has_below, me - 4
                )
            )
            pl.when(from_below)(
                lambda: take(
                    0, 1, -4 * distance, down_slot(distance), None if last else down_slot(distance + 1), has_above, me + 4
                )
            )
            for condition, step, slot, kind, onward in (
                (from_above, 4 * distance, up_slot(distance), 1, has_below),
                (from_below, -4 * distance, down_slot(distance), 0, has_above),
            ):
                for part in (0, 1):
                    here = part_of(me + step, part)
                    if not last:
                        sent.append((condition & onward, remote(here, here, send.at[kind, slot, part], own_sem, me)))
                    sent.append((condition, remote(here, here, send.at[2, slot, part], own_sem, to_x)))
                    sent.append((condition, remote(here, here, send.at[3, slot, part], own_sem, to_y)))
            if distance == 1:
                pass_on(None, 0, 0)
            else:
                pass_on(layer + distance - 1 < depth, 4 * (distance - 1), up_slot(distance - 1))
                pass_on(layer - distance + 1 >= 0, -4 * (distance - 1), down_slot(distance - 1))
        pass_on(layer + depth - 1 < depth, 4 * (depth - 1), up_slot(depth - 1))
        pass_on(layer - depth + 1 >= 0, -4 * (depth - 1), down_slot(depth - 1))

        def close(step, slot):
            arrived(to_x + step, 2, slot, 1)
            arrived(to_y + step, 3, slot, 0)
            arrived(across + step, 4, slot, 0)
            arrived(across + step, 5, slot, 1)

        close(0, 0)
        for distance in range(1, depth):
            pl.when(layer + distance < depth)(lambda: close(4 * distance, up_slot(distance)))
            pl.when(layer - distance >= 0)(lambda: close(-4 * distance, down_slot(distance)))
        for condition, copy in sent:
            if condition is None:
                copy.wait_send()
            else:
                pl.when(condition)(copy.wait_send)
        own.wait()

    return pl.pallas_call(
        kernel,
        in_specs=[pl.BlockSpec(memory_space=pl.ANY)],
        out_specs=pl.BlockSpec(memory_space=pl.ANY),
        out_shape=jax.ShapeDtypeStruct((sources * rows, width), block.dtype),
        scratch_shapes=[
            pltpu.SemaphoreType.DMA,
            pltpu.SemaphoreType.DMA((6, slots, 2)),
            pltpu.SemaphoreType.DMA((6, slots, 2)),
        ],
        compiler_params=pltpu.CompilerParams(
            collective_id=collective_id, has_side_effects=True, vmem_limit_bytes=VMEM_LIMIT
        ),
        cost_estimate=lasting(50),
        name="gather_group",
    )(block)


def reduce_steps(parts_ref, sources, refs, sems, merge, pack):
    half_a, half_b, from_x, from_y, from_z, out_x, out_y, out_z = refs
    send, recv_a, recv_b, recv_x, recv_y, recv_z = sems
    rows = parts_ref.shape[0] // sources
    depth, half = sources // 4, rows // 2
    me, column, beside_x, beside_y, across, index_of = grid_place(depth)
    to_x, to_y = index_of(0, beside_x), index_of(0, beside_y)
    order = [*range(1, depth), 0]
    queues, sent = {"x": [], "y": [], "z": []}, []

    def piece(index, part):
        return parts_ref.at[pl.ds(pl.multiple_of(index * rows + part * half, half), half), :]

    def part_rows(part):
        return pl.ds(part * half, half)

    def push(link, source, target, kind, k, recv_sem, device):
        queue = queues[link]
        if link != "z" and len(queue) >= 2:
            queue.pop(0).wait_send()
        copy = remote(source, target, send.at[kind, k], recv_sem, device)
        copy.start()
        queue.append(copy)

    def arrived(target, recv_sem):
        remote(target, target, send.at[0, 0], recv_sem, to_x).wait_recv()

    def plane_rest(k):
        push("x", piece(index_of(k, beside_x), 0), from_x.at[k, part_rows(0)], 2, k, recv_x.at[0, k], to_x)
        push("y", piece(index_of(k, beside_y), 1), from_y.at[k, part_rows(1)], 3, k, recv_y.at[1, k], to_y)

    def plane_merged(k):
        arrived(half_a.at[k], recv_a.at[k])
        pack(out_y.at[k], merge([piece(index_of(k, beside_y), 0), half_a.at[k]]))
        push("y", out_y.at[k], from_y.at[k, part_rows(0)], 4, k, recv_y.at[0, k], to_y)
        arrived(half_b.at[k], recv_b.at[k])
        pack(out_x.at[k], merge([piece(index_of(k, beside_x), 1), half_b.at[k]]))
        push("x", out_x.at[k], from_x.at[k, part_rows(1)], 5, k, recv_x.at[1, k], to_x)

    def column_step(k):
        for part in (0, 1):
            here = part_rows(part)
            arrived(from_x.at[k, here], recv_x.at[part, k])
            arrived(from_y.at[k, here], recv_y.at[part, k])
            if k:
                blocks = [piece(index_of(k, column), part), from_x.at[k, here], from_y.at[k, here]]
                pack(out_z.at[k, here], merge(blocks))
        if k:
            push("z", out_z.at[k], from_z.at[k], 6, k, recv_z.at[k], index_of(k, column))

    for k in order:
        far = index_of(k, across)
        push("x", piece(far, 0), half_a.at[k], 0, k, recv_a.at[k], to_x)
        push("y", piece(far, 1), half_b.at[k], 1, k, recv_b.at[k], to_y)
    for i, k in enumerate(order):
        plane_rest(k)
        plane_merged(k)
        if i:
            column_step(order[i - 1])
    column_step(order[-1])
    for k in range(1, depth):
        arrived(from_z.at[k], recv_z.at[k])
    final = []
    for part in (0, 1):
        here = part_rows(part)
        blocks = [piece(me, part), from_x.at[0, here], from_y.at[0, here]]
        final.append((here, blocks + [from_z.at[k, here] for k in range(1, depth)]))
    return final, [copy for queue in queues.values() for copy in queue]


def reduce_scratch(rows, width, dtype, sources):
    depth, half = sources // 4, rows // 2

    def slots(size):
        return pltpu.VMEM((depth, size, width), dtype)

    refs = [slots(half), slots(half), slots(rows), slots(rows), slots(rows)]
    refs += [slots(half), slots(half), slots(rows)]
    sems = [pltpu.SemaphoreType.DMA((7, depth))]
    sems += [pltpu.SemaphoreType.DMA((depth,))] * 2
    sems += [pltpu.SemaphoreType.DMA((2, depth))] * 2
    sems += [pltpu.SemaphoreType.DMA((depth,))]
    return refs, sems


def reduce_group(parts, sources, collective_id, merge, pack, finish, out_shape):
    rows, width = parts.shape[0] // sources, parts.shape[1]
    depth = sources // 4
    outs = len(out_shape)
    ref_shapes, sem_shapes = reduce_scratch(rows, width, parts.dtype, sources)

    def kernel(parts_ref, *refs):
        out_refs, refs = refs[:outs], refs[outs:]
        me, column, beside_x, beside_y, across, index_of = grid_place(depth)
        greet(
            [index_of(0, beside_x), index_of(0, beside_y)]
            + [index_of(-k, column) for k in range(1, depth)]
        )
        final, still_open = reduce_steps(
            parts_ref, sources, refs[: len(ref_shapes)], refs[len(ref_shapes) :], merge, pack
        )
        for here, blocks in final:
            finish([out.at[here] for out in out_refs], merge(blocks))
        for copy in still_open:
            copy.wait_send()

    return pl.pallas_call(
        kernel,
        in_specs=[pl.BlockSpec(memory_space=pltpu.VMEM)],
        out_specs=[pl.BlockSpec(memory_space=pltpu.VMEM)] * outs,
        out_shape=out_shape,
        scratch_shapes=ref_shapes + sem_shapes,
        compiler_params=pltpu.CompilerParams(
            collective_id=collective_id, has_side_effects=True, vmem_limit_bytes=VMEM_LIMIT
        ),
        cost_estimate=lasting(55),
        name="reduce_group",
    )(parts)


def sum_blocks(parts, sources, collective_id):
    rows, width = parts.shape[0] // sources, parts.shape[1]

    def merge(blocks):
        total = blocks[0][...].astype(jnp.float32)
        for block in blocks[1:]:
            total = total + block[...].astype(jnp.float32)
        return total

    def pack(target, total):
        target[...] = total.astype(parts.dtype)

    def finish(targets, total):
        targets[0][...] = total

    out_shape = [jax.ShapeDtypeStruct((rows, width), jnp.float32)]
    return reduce_group(parts, sources, collective_id, merge, pack, finish, out_shape)[0]


def merge_partials(parts, sources, collective_id, heads):
    rows, width = parts.shape[0] // sources, parts.shape[1] - 128
    head_dim = width // heads

    def merge(blocks):
        stats = []
        for block in blocks:
            stat = block[:, width:].astype(jnp.float32)
            stats.append(stat + pltpu.roll(stat, 128 - 16, 1) + pltpu.roll(stat, 128 - 32, 1))
        top = stats[0]
        for stat in stats[1:]:
            top = jnp.maximum(top, stat)
        fades = [jnp.exp(stat - top) for stat in stats]
        total = sum(fade * pltpu.roll(stat, 128 - heads, 1) for fade, stat in zip(fades, stats))
        sums = []
        for head in range(heads):
            columns = slice(head * head_dim, (head + 1) * head_dim)
            sums.append(
                sum(
                    block[:, columns].astype(jnp.float32) * fade[:, head : head + 1]
                    for block, fade in zip(blocks, fades)
                )
            )
        return sums, top, total

    def pack(target, merged):
        sums, top, total = merged
        for head in range(heads):
            target[:, head * head_dim : (head + 1) * head_dim] = sums[head].astype(parts.dtype)
        lane = lax.broadcasted_iota(jnp.int32, top.shape, 1)
        stat = jnp.where(lane < heads, top, jnp.where(lane < 16, pltpu.roll(total, heads, 1), 0.0))
        target[:, width:] = triple(stat + pltpu.roll(stat, 16, 1) + pltpu.roll(stat, 32, 1))

    def finish(targets, merged):
        sums, top, total = merged
        live = total > 0
        total = jnp.where(live, total, 1.0)
        targets[1][...] = jnp.where(live, top + jnp.log(total), 0.0)
        for head in range(heads):
            targets[0][:, head * head_dim : (head + 1) * head_dim] = sums[head] / total[:, head : head + 1]

    out_shape = [
        jax.ShapeDtypeStruct((rows, width), jnp.float32),
        jax.ShapeDtypeStruct((rows, 128), jnp.float32),
    ]
    return reduce_group(parts, sources, collective_id, merge, pack, finish, out_shape)


def weight_halves(pairs):
    core = lax.axis_index("dp")
    lefts, kept, sent = [], [], []
    for left, right in pairs:
        half = right.shape[1] // 2
        lefts.append(left)
        kept.append(lax.dynamic_slice_in_dim(right, core * half, half, 1))
        sent.append(lax.dynamic_slice_in_dim(right, (1 - core) * half, half, 1))
    other = swapped(jnp.concatenate(lefts + sent, axis=1))
    partials, left_at, at = [], 0, sum(left.shape[1] for left in lefts)
    for left, right in zip(lefts, kept):
        other_left = other[:, left_at : left_at + left.shape[1]]
        other_right = other[:, at : at + right.shape[1]]
        left_at, at = left_at + left.shape[1], at + right.shape[1]
        partials.append(
            lax.dot_general(
                jnp.concatenate([left, other_left], axis=0),
                jnp.concatenate([right, other_right], axis=0),
                contract_rows,
                preferred_element_type=jnp.float32,
            ).astype(jnp.bfloat16)
        )
    return jnp.concatenate(partials, axis=1)


def scattered(halves):
    return lax.psum_scatter(halves, "mem", scatter_dimension=0, tiled=True)


def whole_grads(both, widths):
    both = both.astype(jnp.float32)
    grads, at = [], 0
    for size in widths:
        half = size // 2
        grads.append(jnp.concatenate([both[0, :, at : at + half], both[1, :, at : at + half]], 1))
        at += half
    return grads


def lane_tile(columns, rows):
    lane = lax.broadcasted_iota(jnp.int32, (rows, 128), 1)
    tile = jnp.zeros((rows, 128), jnp.float32)
    for i, column in enumerate(columns):
        tile = jnp.where(lane == i, column, tile)
    return tile


def split_tile(tile):
    lane = lax.broadcasted_iota(jnp.int32, tile.shape, 1)
    kept = jnp.where(lane < 32, tile, 0.0)
    kept = kept + pltpu.roll(kept, 32, 1) + pltpu.roll(kept, 64, 1)
    high = kept.astype(jnp.bfloat16).astype(jnp.float32)
    middle = (kept - high).astype(jnp.bfloat16).astype(jnp.float32)
    low = kept - high - middle
    part = lane // 32
    return jnp.where(part == 0, high, jnp.where(part == 1, middle, low)).astype(jnp.bfloat16)


def joined_tile(tile):
    tile = tile.astype(jnp.float32)
    return tile + pltpu.roll(tile, 128 - 32, 1) + pltpu.roll(tile, 128 - 64, 1)


def slanted(base, rows):
    return pltpu.roll(jnp.broadcast_to(base, (rows, base.shape[1])), 0, 1, stride=1, stride_axis=0)


def local_forward(base, book_column, book_row, own, halos, heads, score_scale):
    rows, width = own.shape[0], own.shape[1] // 3
    head_dim = width // heads
    count = len(halos) + 1

    def kernel(base_ref, column_ref, row_ref, own_ref, *refs):
        halo_refs, (out_ref, log_ref) = refs[: count - 1], refs[count - 1 :]
        same = column_ref[:, :1] == row_ref[:1, :]
        logs = []
        for head in range(heads):
            columns = slice(head * head_dim, (head + 1) * head_dim)
            above = slice(width + head * head_dim, width + (head + 1) * head_dim)
            twice = slice(2 * width + head * head_dim, 2 * width + (head + 1) * head_dim)
            keys = [ref[:, columns] for ref in halo_refs] + [own_ref[:, above]]
            values = [ref[:, above] for ref in halo_refs] + [own_ref[:, twice]]
            q = own_ref[:, columns]
            raw = [
                lax.dot_general(q, k, contract_cols, preferred_element_type=jnp.float32) for k in keys
            ]
            bias = slanted(base_ref[head : head + 1, :], rows)[:, : count * rows]
            scores = jnp.concatenate(raw, axis=1) * score_scale + bias
            scores = jnp.where(same, scores, masked_score)
            top = jnp.max(scores, axis=1, keepdims=True)
            weights = jnp.exp(scores - top)
            total = jnp.sum(weights, axis=1, keepdims=True)
            weights = (weights / total).astype(jnp.bfloat16)
            out_ref[:, columns] = sum(
                jnp.dot(
                    weights[:, i * rows : (i + 1) * rows], v, preferred_element_type=jnp.float32
                )
                for i, v in enumerate(values)
            )
            logs.append(top + jnp.log(total))
        log_ref[...] = lane_tile(logs, rows)

    return pl.pallas_call(
        kernel,
        out_shape=[
            jax.ShapeDtypeStruct((rows, width), jnp.float32),
            jax.ShapeDtypeStruct((rows, 128), jnp.float32),
        ],
        compiler_params=pltpu.CompilerParams(vmem_limit_bytes=VMEM_LIMIT),
        cost_estimate=lasting(10),
        name="local_forward",
    )(base, book_column, book_row, own, *halos)


def local_queries(
    base, book_column, book_row, own, halos, d_mixed, memory_out, local_out, mem_log, local_log, share, heads, score_scale
):
    rows, width = d_mixed.shape
    head_dim = width // heads
    count = len(halos) + 1
    span = base.shape[1]

    def kernel(
        base_ref, column_ref, row_ref, own_ref, mix_ref, mem_ref, loc_ref, mem_log_ref, log_ref, share_ref, *refs
    ):
        halo_refs, (dq_ref, diagonal_ref, gate_ref, sent_ref) = refs[: count - 1], refs[count - 1 :]
        same = column_ref[:, :1] == row_ref[:1, :]
        turned = (
            lax.broadcasted_iota(jnp.int32, (rows, rows), 0)
            + lax.broadcasted_iota(jnp.int32, (rows, rows), 1)
            == rows - 1
        ).astype(jnp.bfloat16)
        mem_deltas, deltas = [], []
        for head in range(heads):
            columns = slice(head * head_dim, (head + 1) * head_dim)
            above = slice(width + head * head_dim, width + (head + 1) * head_dim)
            twice = slice(2 * width + head * head_dim, 2 * width + (head + 1) * head_dim)
            keys = [ref[:, columns] for ref in halo_refs] + [own_ref[:, above]]
            values = [ref[:, above] for ref in halo_refs] + [own_ref[:, twice]]
            q = own_ref[:, columns]
            share_here = share_ref[head]
            d_mix, mem_here, loc_here = mix_ref[:, columns], mem_ref[:, columns], loc_ref[:, columns]
            d_mem = (share_here * d_mix).astype(jnp.bfloat16)
            d_out = ((1.0 - share_here) * d_mix).astype(jnp.bfloat16)
            sent_ref[:, columns] = d_mem
            mem_deltas.append(
                jnp.sum(d_mem.astype(jnp.float32) * mem_here, axis=1, keepdims=True)
            )
            delta = jnp.sum(d_out.astype(jnp.float32) * loc_here, axis=1, keepdims=True)
            deltas.append(delta)
            gate_ref[head : head + 1, :] = jnp.sum(
                d_mix * (mem_here - loc_here), axis=0, keepdims=True
            )
            raw = [
                lax.dot_general(q, k, contract_cols, preferred_element_type=jnp.float32) for k in keys
            ]
            bias = slanted(base_ref[head : head + 1, :], rows)[:, : count * rows]
            scores = jnp.concatenate(raw, axis=1) * score_scale + bias
            probs = jnp.exp(jnp.where(same, scores - log_ref[:, head : head + 1], masked_score))
            products = [
                lax.dot_general(d_out, v, contract_cols, preferred_element_type=jnp.float32)
                for v in values
            ]
            slopes = (probs * (jnp.concatenate(products, axis=1) - delta)).astype(jnp.bfloat16)
            slope_blocks = [slopes[:, i * rows : (i + 1) * rows] for i in range(count)]
            dq_ref[:, columns] = score_scale * sum(
                jnp.dot(s, k, preferred_element_type=jnp.float32) for s, k in zip(slope_blocks, keys)
            )
            mirrored = [
                jnp.dot(s, turned, preferred_element_type=jnp.float32) for s in slope_blocks[::-1]
            ]
            mirrored.append(jnp.zeros((rows, span - count * rows), jnp.float32))
            leaned = pltpu.roll(jnp.concatenate(mirrored, axis=1), 0, 1, stride=1, stride_axis=0)
            diagonal_ref[head : head + 1, :] = jnp.sum(leaned, axis=0, keepdims=True)
        mem_logs = [mem_log_ref[:, head : head + 1] for head in range(heads)]
        logs = [log_ref[:, head : head + 1] for head in range(heads)]
        sent_ref[:, width:] = split_tile(lane_tile(mem_logs + mem_deltas + logs + deltas, rows))

    vmem = pl.BlockSpec(memory_space=pltpu.VMEM)
    return pl.pallas_call(
        kernel,
        in_specs=[vmem] * 9 + [pl.BlockSpec(memory_space=pltpu.SMEM)] + [vmem] * len(halos),
        out_shape=[
            jax.ShapeDtypeStruct((rows, width), jnp.float32),
            jax.ShapeDtypeStruct((heads, span), jnp.float32),
            jax.ShapeDtypeStruct((heads, head_dim), jnp.float32),
            jax.ShapeDtypeStruct((rows, width + 128), jnp.bfloat16),
        ],
        compiler_params=pltpu.CompilerParams(vmem_limit_bytes=VMEM_LIMIT),
        cost_estimate=lasting(15),
        name="local_queries",
    )(base, book_column, book_row, own, d_mixed, memory_out, local_out, mem_log, local_log, share, *halos)


def local_keys(base, book_column, book_row, own, queries, sent, ratio, me, count, heads, score_scale):
    rows, width = own.shape[0], own.shape[1] // 3
    head_dim = width // heads
    groups = queries.shape[0] // rows

    def kernel(me_ref, base_ref, column_ref, row_ref, own_ref, ratio_ref, *refs):
        q_refs, g_refs, out_ref = refs[:count], refs[count : 2 * count], refs[2 * count]
        same = column_ref[:, :1] == row_ref[:1, :]
        stats = jnp.concatenate([joined_tile(ref[:, width:]).T for ref in g_refs], axis=1)
        for head in range(heads):
            columns = slice(head * head_dim, (head + 1) * head_dim)
            above = slice(width + head * head_dim, width + (head + 1) * head_dim)
            twice = slice(2 * width + head * head_dim, 2 * width + (head + 1) * head_dim)
            k, v = own_ref[:, above], own_ref[:, twice]
            qs = [ref[:, columns] for ref in q_refs]
            gs = [
                (ref[:, columns].astype(jnp.float32) * ratio_ref[head]).astype(jnp.bfloat16)
                for ref in g_refs
            ]
            raw = [
                lax.dot_general(k, q, contract_cols, preferred_element_type=jnp.float32) for q in qs
            ]
            bias = slanted(base_ref[head : head + 1, :], rows)[:, : count * rows]
            scores = jnp.concatenate(raw, axis=1) * score_scale + bias
            log = stats[2 * heads + head : 2 * heads + head + 1, :]
            delta = stats[3 * heads + head : 3 * heads + head + 1, :]
            probs = jnp.exp(jnp.where(same, scores - log, masked_score))
            products = [
                lax.dot_general(v, g, contract_cols, preferred_element_type=jnp.float32) for g in gs
            ]
            slopes = (probs * (jnp.concatenate(products, axis=1) - delta)).astype(jnp.bfloat16)
            weights = probs.astype(jnp.bfloat16)
            blocks = [slice(i * rows, (i + 1) * rows) for i in range(count)]
            d_key = sum(
                jnp.dot(slopes[:, b], q, preferred_element_type=jnp.float32) for b, q in zip(blocks, qs)
            )
            d_value = sum(
                jnp.dot(weights[:, b], g, preferred_element_type=jnp.float32)
                for b, g in zip(blocks, gs)
            )
            out_ref[:, columns] = (d_key * score_scale).astype(jnp.bfloat16)
            out_ref[:, above] = d_value.astype(jnp.bfloat16)

    def whole(array):
        return pl.BlockSpec(array.shape, lambda i, *_: (0, 0))

    def later(distance, size):
        return pl.BlockSpec((rows, size), lambda i, m: (jnp.minimum(m[0] + distance, groups - 1), 0))

    return pl.pallas_call(
        kernel,
        grid_spec=pltpu.PrefetchScalarGridSpec(
            num_scalar_prefetch=1,
            grid=(1,),
            in_specs=[whole(base), whole(book_column), whole(book_row), whole(own)]
            + [pl.BlockSpec(memory_space=pltpu.SMEM)]
            + [later(i, width) for i in range(count)]
            + [later(i, width + 128) for i in range(count)],
            out_specs=pl.BlockSpec((rows, 2 * width), lambda i, *_: (0, 0)),
        ),
        out_shape=jax.ShapeDtypeStruct((rows, 2 * width), jnp.bfloat16),
        compiler_params=pltpu.CompilerParams(vmem_limit_bytes=VMEM_LIMIT),
        cost_estimate=lasting(15),
        name="local_keys",
    )(me, base, book_column, book_row, own, ratio, *([queries] * count), *([sent] * count))


def finish_grads(parts, early, small, sources, collective_id):
    rows, width = parts.shape[0] // sources, parts.shape[1]
    mesh_type = pl.DeviceIdType.MESH
    ref_shapes, sem_shapes = reduce_scratch(rows, width, parts.dtype, sources)

    def kernel(parts_ref, early_ref, small_ref, late_out, early_out, small_out, *refs):
        steps_refs, refs = refs[: len(ref_shapes)], refs[len(ref_shapes) :]
        steps_sems, refs = refs[: len(sem_shapes)], refs[len(sem_shapes) :]
        smalls, core_small, small_send, small_recv, core_send, core_recv = refs
        me, core = lax.axis_index("mem"), lax.axis_index("dp")
        barrier = pltpu.get_barrier_semaphore()
        peers = [lax.rem(me + k, sources) for k in range(1, sources)]
        for peer in peers:
            pl.semaphore_signal(barrier, inc=1, device_id={"mem": peer}, device_id_type=mesh_type)
        pl.semaphore_signal(barrier, inc=1, device_id={"dp": 1 - core}, device_id_type=mesh_type)
        pl.semaphore_wait(barrier, sources)

        def merge(blocks):
            total = blocks[0][...].astype(jnp.float32)
            for block in blocks[1:]:
                total = total + block[...].astype(jnp.float32)
            return total

        def pack(target, total):
            target[...] = total.astype(parts.dtype)

        def across_cores(source, target, i):
            copy = pltpu.make_async_remote_copy(
                src_ref=source,
                dst_ref=target,
                send_sem=core_send.at[i],
                recv_sem=core_recv.at[i],
                device_id={"dp": 1 - core},
                device_id_type=mesh_type,
            )
            copy.start()
            return copy

        smalls[me] = small_ref[...]
        small_copies = [
            remote(small_ref, smalls.at[me], small_send.at[i], small_recv.at[me], peer)
            for i, peer in enumerate(peers)
        ]
        for copy in small_copies:
            copy.start()
        early_copy = across_cores(early_ref, early_out.at[core], 0)
        early_out[core] = early_ref[...]
        final, still_open = reduce_steps(parts_ref, sources, steps_refs, steps_sems, merge, pack)
        for here, blocks in final:
            late_out[core, here] = merge(blocks).astype(parts.dtype)
        late_copy = across_cores(late_out.at[core], late_out.at[core], 2)
        for peer in peers:
            remote(
                smalls.at[peer], smalls.at[peer], small_send.at[0], small_recv.at[peer], peer
            ).wait_recv()
        group_small = smalls[0]
        for i in range(1, sources):
            group_small = group_small + smalls[i]
        core_small[0] = group_small
        small_copy = across_cores(core_small.at[0], core_small.at[1], 1)
        for copy in (early_copy, late_copy, small_copy):
            copy.wait()
        small_out[...] = core_small[0] + core_small[1]
        for copy in still_open + small_copies:
            copy.wait_send()

    vmem = pl.BlockSpec(memory_space=pltpu.VMEM)
    return pl.pallas_call(
        kernel,
        in_specs=[vmem] * 3,
        out_specs=[vmem] * 3,
        out_shape=[
            jax.ShapeDtypeStruct((2, rows, width), parts.dtype),
            jax.ShapeDtypeStruct((2, *early.shape), early.dtype),
            jax.ShapeDtypeStruct(small.shape, small.dtype),
        ],
        scratch_shapes=ref_shapes
        + sem_shapes
        + [pltpu.VMEM((sources, *small.shape), small.dtype), pltpu.VMEM((2, *small.shape), small.dtype)]
        + [pltpu.SemaphoreType.DMA((sources,))] * 2
        + [pltpu.SemaphoreType.DMA((3,))] * 2,
        compiler_params=pltpu.CompilerParams(
            collective_id=collective_id, has_side_effects=True, vmem_limit_bytes=VMEM_LIMIT
        ),
        cost_estimate=lasting(45),
        name="finish_grads",
    )(parts, early, small)


def on_device(
    tokens,
    attn_gain,
    qkv_weight,
    out_weight,
    bias_table,
    gate_logit,
    ffn_gain,
    up_weight,
    down_weight,
    memory_keys,
    memory_values,
    book_lengths,
    slot_shard,
    slot_index,
    slot_live,
    cotangent,
):
    rows, width = tokens.shape
    heads, buckets = bias_table.shape
    head_dim = width // heads
    top_count = slot_index.shape[2]
    hidden = up_weight.shape[1]
    groups = lax.axis_size("mem")
    capacity = -(-3 * rows * heads * top_count // (2 * groups) // 128) * 128
    score_scale = 1.0 / math.sqrt(head_dim)
    repeats = W // rows
    span = W + 2 * rows
    me = lax.axis_index("mem")
    first_pos = me * rows
    lengths = book_lengths[0]
    window = jnp.arange(W + rows, dtype=jnp.int32)
    key_pos = first_pos - W + window
    key_book = jnp.where(key_pos >= 0, book_of(key_pos, lengths), -1)
    later_book = book_of(first_pos + window, lengths)
    own_book = jnp.broadcast_to(later_book[:rows, None], (rows, 128))
    key_book = jnp.broadcast_to(key_book[None, :], (8, W + rows))
    later_book = jnp.broadcast_to(later_book[None, :], (8, W + rows))
    bucket = bucket_of(jnp.arange(W, dtype=jnp.int32))
    one_hot = (bucket[:, None] == jnp.arange(buckets, dtype=jnp.int32)).astype(jnp.float32)
    offset_bias = jnp.einsum("rb,hb->hr", one_hot, bias_table, precision=lax.Precision.HIGHEST)
    after_bias = jnp.pad(offset_bias, ((0, 0), (0, span - W)), constant_values=masked_score)
    before_bias = jnp.pad(
        offset_bias[:, ::-1], ((0, 0), (1, span - W - 1)), constant_values=masked_score
    )
    tokens_f = tokens.astype(jnp.float32)
    normed_f, norm_in_back = jax.vjp(normed, tokens_f, attn_gain)
    normed_in = normed_f.astype(jnp.bfloat16)
    projected = jnp.dot(normed_in, qkv_weight, preferred_element_type=jnp.float32).astype(
        jnp.bfloat16
    )
    halos = [
        passed_along(projected[:, width:], "mem", distance) for distance in range(repeats, 0, -1)
    ]
    local_out, local_log = local_forward(
        before_bias, own_book, key_book, projected, halos, heads, score_scale
    )
    slots = memory_keys.shape[0]
    requests = place_requests(slot_shard, slot_index, slot_live, groups, capacity, slots)
    incoming = lax.all_to_all(requests, "mem", split_axis=0, concat_axis=0, tiled=True)
    row_ids = incoming // slots
    limits = jnp.arange(heads + 1, dtype=jnp.int32) * (rows * slots)
    bounds = jnp.sum((incoming[:, None] < limits[None, :, None, None]).astype(jnp.int32), axis=(2, 3))
    index = jnp.where(row_ids < heads * rows, row_ids // rows * slots + incoming % slots, 0)
    key_rows, value_rows = gather_rows(
        index.reshape(-1), bounds[:, heads], memory_keys, memory_values, heads, groups, capacity
    )
    all_queries = lax.all_gather(projected[:, :width], "mem", axis=0, tiled=True)
    partial = memory_forward(
        bounds.reshape(-1),
        all_queries,
        key_rows,
        value_rows,
        row_ids,
        heads,
        groups,
        rows,
        score_scale,
    )
    if groups == 16:
        memory_out, mem_log = merge_partials(partial, groups, 1, heads)
    else:
        partial = lax.all_to_all(
            partial.reshape(groups, rows, width + 128),
            "mem",
            split_axis=0,
            concat_axis=0,
            tiled=True,
        ).reshape(groups * rows, width + 128)
        memory_out, mem_log = combine_partials(partial, heads, groups, rows)
    gate_share = jax.nn.sigmoid(gate_logit)
    share_wide = jnp.repeat(gate_share, head_dim)[None, :]
    mixed_heads = (share_wide * memory_out + (1.0 - share_wide) * local_out).astype(jnp.bfloat16)
    residual = tokens_f + jnp.dot(mixed_heads, out_weight, preferred_element_type=jnp.float32)
    normed_mid_f, norm_mid_back = jax.vjp(normed, residual, ffn_gain)
    normed_mid = normed_mid_f.astype(jnp.bfloat16)
    up_proj = jnp.dot(normed_mid, up_weight, preferred_element_type=jnp.float32)
    activated_f, gelu_back = jax.vjp(gelu_exact, up_proj)
    activated = activated_f.astype(jnp.bfloat16)
    ffn_branch = lax.dot_general(
        activated, down_weight, contract_cols, preferred_element_type=jnp.float32
    )
    block_out = (residual + ffn_branch).astype(jnp.bfloat16)
    d_act = jnp.dot(cotangent, down_weight, preferred_element_type=jnp.float32)
    d_up = gelu_back(d_act)[0].astype(jnp.bfloat16)
    d_mid = lax.dot_general(d_up, up_weight, contract_cols, preferred_element_type=jnp.float32)
    d_resid_part, ffn_gain_part = norm_mid_back(d_mid)
    d_residual = cotangent.astype(jnp.float32) + d_resid_part
    d_branch = d_residual.astype(jnp.bfloat16)
    d_mixed = lax.dot_general(
        d_branch, out_weight, contract_cols, preferred_element_type=jnp.float32
    )
    early_halves = weight_halves([(mixed_heads, d_branch), (normed_mid, d_up), (cotangent, activated)])
    d_queries, diagonals, gate_products, sent_grads = local_queries(
        before_bias,
        own_book,
        key_book,
        projected,
        halos,
        d_mixed,
        memory_out,
        local_out,
        mem_log,
        local_log,
        gate_share,
        heads,
        score_scale,
    )
    gate_part = jnp.sum(gate_products, axis=1) * gate_share * (1.0 - gate_share)
    bias_part = jnp.dot(diagonals[:, rows - 1 : rows - 1 + W], one_hot, precision=lax.Precision.HIGHEST)
    sent_grads, early_halves = lax.optimization_barrier((sent_grads, early_halves))
    early_sums = scattered(early_halves)
    if groups == 16:
        all_grads = gather_group(sent_grads, groups, 2)
    else:
        all_grads = lax.all_gather(sent_grads, "mem", axis=0, tiled=True)
    d_partial = memory_backward(
        bounds.reshape(-1),
        all_queries,
        all_grads,
        key_rows,
        value_rows,
        row_ids,
        heads,
        groups,
        rows,
        score_scale,
    )
    d_keys_values = local_keys(
        after_bias,
        own_book,
        later_book,
        projected,
        all_queries,
        all_grads,
        (1.0 - gate_share) / gate_share,
        me[None],
        repeats + 1,
        heads,
        score_scale,
    )
    if groups == 16:
        d_partial = sum_blocks(d_partial, groups, 3)
    else:
        d_partial, d_keys_values = lax.optimization_barrier((d_partial, d_keys_values))
        d_partial = jnp.sum(
            lax.all_to_all(
                d_partial.reshape(groups, rows, width), "mem", split_axis=0, concat_axis=0, tiled=True
            ).astype(jnp.float32),
            axis=0,
        )
    d_queries = (d_queries + d_partial * score_scale).astype(jnp.bfloat16)
    d_projected = jnp.concatenate([d_queries, d_keys_values], axis=1)
    d_in = lax.dot_general(
        d_projected, qkv_weight, contract_cols, preferred_element_type=jnp.float32
    )
    d_tokens_part, attn_gain_part = norm_in_back(d_in)
    tokens_grad = d_residual + d_tokens_part
    late_halves = weight_halves([(normed_in, d_projected)])
    late_halves, early_sums = lax.optimization_barrier((late_halves, early_sums))
    small = jnp.concatenate(
        [attn_gain_part, ffn_gain_part, bias_part.reshape(-1), gate_part], axis=0
    )
    small = jnp.pad(small, (0, -small.shape[0] % 1024)).reshape(-1, 128)
    if groups == 16:
        late_both, early_both, small = finish_grads(late_halves, early_sums, small, groups, 4)
    else:
        late_both = lax.all_gather(scattered(late_halves), "dp", axis=0)
        early_both = lax.all_gather(early_sums, "dp", axis=0)
        small = lax.psum(small, ("dp", "mem"))
    small = small.reshape(-1)
    out_grad, up_grad, down_grad = whole_grads(early_both, [width, hidden, hidden])
    qkv_grad = whole_grads(late_both, [3 * width])[0]
    at_bias = 2 * width + heads * buckets
    return (
        block_out,
        tokens_grad,
        qkv_grad,
        out_grad,
        up_grad,
        down_grad,
        small[:width],
        small[width : 2 * width],
        small[2 * width : at_bias].reshape(heads, buckets),
        small[at_bias : at_bias + heads],
    )


def solution(mesh):
    in_specs = (
        P(("dp", "mem"), None),
        P(),
        P(),
        P(),
        P(),
        P(),
        P(),
        P(),
        P(),
        P("mem", None),
        P("mem", None),
        P("dp", None),
        P(("dp", "mem"), None, None, None),
        P(("dp", "mem"), None, None),
        P(("dp", "mem"), None, None),
        P(("dp", "mem"), None),
    )
    out_specs = (
        P(("dp", "mem"), None),
        P(("dp", "mem"), None),
        P("mem", None),
        P("mem", None),
        P("mem", None),
        P("mem", None),
        P(),
        P(),
        P(),
        P(),
    )
    return jax.shard_map(
        on_device, mesh=mesh, in_specs=in_specs, out_specs=out_specs, check_vma=False
    )
```

```python
import math

import jax
import jax.numpy as jnp
from jax import lax
from jax.experimental import pallas as pl
from jax.experimental.pallas import tpu as pltpu
from jax.sharding import PartitionSpec as P

W = 512
VMEM_LIMIT = 56 * 1024 * 1024


eps_norm = 1e-06
bucket_edges = tuple((math.ceil(16 * 8 ** (edge_step / 16)) for edge_step in range(1, 16)))
masked_score = -1e30
dead_score = -10000.0
contract_rows = (((0,), (0,)), ((), ()))
contract_cols = (((1,), (1,)), ((), ()))


def passed_along(value, axis, by):
    size = lax.axis_size(axis)
    pairs = [(i, i + by) for i in range(size) if 0 <= i + by < size]
    return lax.ppermute(value, axis, pairs)


def swapped(value):
    return lax.ppermute(value, "dp", [(0, 1), (1, 0)])


def bucket_of(offset):
    past_edges = sum(((offset >= edge_pos).astype(jnp.int32) for edge_pos in bucket_edges))
    return jnp.where(offset < 16, offset, 16 + past_edges)


def normed(values, gain_vec):
    return (
        values * lax.rsqrt(jnp.mean(values * values, axis=-1, keepdims=True) + eps_norm) * gain_vec
    )


def gelu_exact(values):
    return jax.nn.gelu(values, approximate=False)


def book_of(positions, lengths):
    book_ends = jnp.cumsum(lengths, dtype=jnp.int32)
    return jnp.sum((positions[..., None] >= book_ends).astype(jnp.int32), axis=-1)


def place_requests(slot_shard, slot_index, slot_live, owners, capacity, slots):
    rows, heads, top_count = slot_index.shape
    entries = rows * heads * top_count
    row_of = (
        jnp.arange(heads, dtype=jnp.int32)[None, :] * rows
        + jnp.arange(rows, dtype=jnp.int32)[:, None]
    )
    place = row_of[:, :, None] * top_count + jnp.arange(top_count, dtype=jnp.int32)
    owner = jnp.where(slot_live > 0, slot_shard[..., 0], owners)
    keys, picked = lax.sort(
        ((owner * entries + place).reshape(-1), slot_index.reshape(-1)), num_keys=1
    )
    ends = jnp.sum(
        (keys[None, :] < (jnp.arange(owners, dtype=jnp.int32) + 1)[:, None] * entries).astype(jnp.int32),
        axis=1,
    )
    starts = jnp.concatenate([jnp.zeros((1,), jnp.int32), ends[:-1]])
    codes = keys % entries // top_count * slots + picked
    tall = -(-entries // 128)
    codes = jnp.pad(codes, (0, tall * 128 - entries)).reshape(tall, 128)
    long = capacity // 128
    empty = heads * rows * slots

    def kernel(starts_ref, ends_ref, codes_ref, lists_ref, padded):
        padded[:tall, :] = codes_ref[...]
        padded[tall:, :] = jnp.zeros((long + 8, 128), jnp.int32)
        lane = lax.broadcasted_iota(jnp.int32, (long, 128), 1)
        place = lax.broadcasted_iota(jnp.int32, (long, 128), 0) * 128 + lane

        @pl.loop(0, owners)
        def _(i):
            start, end = starts_ref[i], ends_ref[i]
            shift = start % 128
            lines = padded[pl.ds(start // 128, long + 1), :]
            turned = pltpu.roll(lines, (128 - shift) % 128, 1)
            joined = jnp.where(lane < 128 - shift, turned[:long], turned[1:])
            lists_ref[i] = jnp.where(place < end - start, joined, empty)

    return pl.pallas_call(
        kernel,
        in_specs=[pl.BlockSpec(memory_space=pltpu.SMEM)] * 2 + [pl.BlockSpec(memory_space=pltpu.VMEM)],
        out_shape=jax.ShapeDtypeStruct((owners, long, 128), jnp.int32),
        scratch_shapes=[pltpu.VMEM((tall + long + 8, 128), jnp.int32)],
        cost_estimate=lasting(3),
        name="make_lists",
    )(starts, ends, codes)


def gather_rows(index, counts, memory_keys, memory_values, heads, sources, capacity):
    slots, width = memory_keys.shape
    head_dim = width // heads
    step, part = 128, 16

    def kernel(index_ref, counts_ref, keys, values, out_keys, out_values, key_table, value_table, key_rows, value_rows):
        i = pl.program_id(0)

        @pl.when(i < heads)
        def _():
            place = pl.ds(pl.multiple_of(i * slots, slots), slots)
            key_table[place, :] = keys[...].astype(jnp.float32)
            value_table[place, :] = values[...].astype(jnp.float32)

        @pl.when(i >= heads)
        def _():
            source = i - heads

            used = (counts_ref[source] + step - 1) // step

            def store(group):
                for at in range(0, step, part):
                    here = pl.ds(pl.multiple_of(group * step, step) + at, part)
                    out_keys[here, :] = key_rows[at : at + part, :].astype(jnp.bfloat16)
                    out_values[here, :] = value_rows[at : at + part, :].astype(jnp.bfloat16)

            @pl.loop(0, used)
            def _(group):
                store(jnp.maximum(group - 1, 0))
                first = source * capacity + group * step
                for u in range(step):
                    row = index_ref[first + u]
                    key_rows[u : u + 1, :] = key_table[pl.ds(row, 1), :]
                    value_rows[u : u + 1, :] = value_table[pl.ds(row, 1), :]

            pl.when(used > 0)(lambda: store(used - 1))

            @pl.loop(used, capacity // step)
            def _(group):
                here = pl.ds(pl.multiple_of(group * step, step), step)
                out_keys[here, :] = jnp.zeros((step, head_dim), jnp.bfloat16)
                out_values[here, :] = jnp.zeros((step, head_dim), jnp.bfloat16)

    table_spec = pl.BlockSpec((slots, head_dim), lambda i, *_: (0, jnp.minimum(i, heads - 1)))
    out_spec = pl.BlockSpec((capacity, head_dim), lambda i, *_: (jnp.maximum(i - heads, 0), 0))
    out_shape = jax.ShapeDtypeStruct((sources * capacity, head_dim), jnp.bfloat16)
    return pl.pallas_call(
        kernel,
        grid_spec=pltpu.PrefetchScalarGridSpec(
            num_scalar_prefetch=2,
            grid=(heads + sources,),
            in_specs=[table_spec, table_spec],
            out_specs=[out_spec, out_spec],
            scratch_shapes=[
                pltpu.VMEM((heads * slots, head_dim), jnp.float32),
                pltpu.VMEM((heads * slots, head_dim), jnp.float32),
                pltpu.VMEM((step, head_dim), jnp.float32),
                pltpu.VMEM((step, head_dim), jnp.float32),
            ],
        ),
        out_shape=[out_shape, out_shape],
        compiler_params=pltpu.CompilerParams(vmem_limit_bytes=VMEM_LIMIT),
        cost_estimate=lasting(42),
        name="gather_rows",
    )(index, counts, memory_keys, memory_values)


def lasting(microseconds):
    return pl.CostEstimate(flops=0, bytes_accessed=3_000_000 * microseconds, transcendentals=0)


def triple(stat):
    part = lax.broadcasted_iota(jnp.int32, stat.shape, 1) // 16
    high = stat.astype(jnp.bfloat16).astype(jnp.float32)
    rest = stat - high
    middle = rest.astype(jnp.bfloat16).astype(jnp.float32)
    low = rest - middle
    chosen = jnp.where(part == 0, high, jnp.where(part == 1, middle, jnp.where(part == 2, low, 0.0)))
    return chosen.astype(jnp.bfloat16)


def window_of(bounds, source, head, heads, span, capacity):
    first = bounds[source * (heads + 1) + head]
    last = bounds[source * (heads + 1) + head + 1]
    start = jnp.minimum(first // 16 * 16, capacity - span)
    extra = jnp.maximum(last - start - 1, 0) // span
    return start, extra


def columns_of(head, head_dim):
    if isinstance(head, int):
        return slice(head * head_dim, (head + 1) * head_dim)
    return pl.ds(pl.multiple_of(head * head_dim, head_dim), head_dim)


def window_ids(id_ref, start, span):
    lines = id_ref[0, pl.ds(start // 128, span // 128 + 1), :]
    shift = start % 128
    turned = pltpu.roll(lines, (128 - shift) % 128, 1)
    lane = lax.broadcasted_iota(jnp.int32, (span // 128, 128), 1)
    return jnp.where(lane < 128 - shift, turned[:-1], turned[1:])


def owned(lines, first_row, count, start, least):
    row = lax.broadcasted_iota(jnp.int32, (count, 128), 0) + first_row
    masks = []
    for i in range(lines.shape[0]):
        mask = lines[i : i + 1, :] == row
        if least is not None:
            place = lax.broadcasted_iota(jnp.int32, (1, 128), 1) + start + i * 128
            mask = mask & (place >= least)
        masks.append(mask)
    return jnp.concatenate(masks, axis=1)


def memory_forward(bounds, queries, key_rows, value_rows, row_ids, heads, sources, rows, score_scale):
    capacity, head_dim = key_rows.shape[0] // sources, key_rows.shape[1]
    width = heads * head_dim
    span = min(384, capacity)
    chunk = math.gcd(rows, 32)

    def kernel(bounds_ref, q_ref, k_ref, v_ref, id_ref, out_ref, sums, tops, totals, raw, weights):
        source = pl.program_id(0)
        lane = lax.broadcasted_iota(jnp.int32, (chunk, 128), 1) % 16

        def window(heads_here, starts, least):
            here = [pl.ds(pl.multiple_of(start, 16), span) for start in starts]
            columns = [columns_of(head, head_dim) for head in heads_here]
            for slot in range(len(starts)):
                raw[slot] = lax.dot_general(
                    q_ref[:, columns[slot]],
                    k_ref[here[slot], :],
                    contract_cols,
                    preferred_element_type=jnp.float32,
                )
            for slot, (head, start) in enumerate(zip(heads_here, starts)):
                lines = window_ids(id_ref, start, span)
                for at in range(0, rows, chunk):
                    some = slice(at, at + chunk)
                    mine = owned(lines, head * rows + at, chunk, start, least)
                    scores = jnp.where(mine, raw[slot, some, :], masked_score)
                    top = jnp.maximum(jnp.max(scores, axis=1, keepdims=True), 0.1 * masked_score)
                    if least is not None:
                        old_top = jnp.max(
                            jnp.where(lane == head, tops[some, :], masked_score), axis=1, keepdims=True
                        )
                        top = jnp.maximum(top, old_top)
                    exps = jnp.exp((scores - top) * score_scale)
                    weights[slot, some, :] = exps.astype(jnp.bfloat16)
                    total = jnp.sum(exps, axis=1, keepdims=True)
                    if least is not None:
                        faded = jnp.exp((old_top - top) * score_scale)
                        sums[some, columns[slot]] = sums[some, columns[slot]] * faded
                        total = total + totals[some, :] * faded
                    tops[some, :] = jnp.where(lane == head, top, tops[some, :])
                    totals[some, :] = jnp.where(lane == heads + head, total, totals[some, :])
            for slot in range(len(starts)):
                found = jnp.dot(
                    weights[slot], v_ref[here[slot], :], preferred_element_type=jnp.float32
                )
                sums[:, columns[slot]] = found if least is None else sums[:, columns[slot]] + found

        tops[...] = jnp.zeros_like(tops)
        totals[...] = jnp.zeros_like(totals)

        window(
            list(range(heads)),
            [window_of(bounds_ref, source, head, heads, span, capacity)[0] for head in range(heads)],
            None,
        )

        @pl.loop(0, heads)
        def _(head):
            start, extra = window_of(bounds_ref, source, head, heads, span, capacity)

            @pl.loop(0, extra)
            def _(turn):
                least = start + (turn + 1) * span
                window([head], [jnp.minimum(least, capacity - span)], least)

        out_ref[:, :width] = sums[...].astype(jnp.bfloat16)
        wide = lax.broadcasted_iota(jnp.int32, (rows, 128), 1) % 16
        out_ref[:, width:] = triple(jnp.where(wide < heads, tops[...] * score_scale, totals[...]))

    return pl.pallas_call(
        kernel,
        grid_spec=pltpu.PrefetchScalarGridSpec(
            num_scalar_prefetch=1,
            grid=(sources,),
            in_specs=[
                pl.BlockSpec((rows, width), lambda i, *_: (i, 0)),
                pl.BlockSpec((capacity, head_dim), lambda i, *_: (i, 0)),
                pl.BlockSpec((capacity, head_dim), lambda i, *_: (i, 0)),
                pl.BlockSpec((1, *row_ids.shape[1:]), lambda i, *_: (i, 0, 0)),
            ],
            out_specs=pl.BlockSpec((rows, width + 128), lambda i, *_: (i, 0)),
            scratch_shapes=[
                pltpu.VMEM((rows, width), jnp.float32),
                pltpu.VMEM((rows, 128), jnp.float32),
                pltpu.VMEM((rows, 128), jnp.float32),
                pltpu.VMEM((heads, rows, span), jnp.float32),
                pltpu.VMEM((heads, rows, span), jnp.bfloat16),
            ],
        ),
        out_shape=jax.ShapeDtypeStruct((sources * rows, width + 128), jnp.bfloat16),
        compiler_params=pltpu.CompilerParams(vmem_limit_bytes=VMEM_LIMIT),
        cost_estimate=lasting(25),
        name="memory_forward",
    )(bounds, queries, key_rows, value_rows, row_ids)


def combine_partials(partial, heads, sources, rows):
    width = partial.shape[1] - 128
    head_dim = width // heads

    def kernel(part_ref, out_ref, log_ref, sums, tops, totals):
        i = pl.program_id(0)

        @pl.when(i == 0)
        def _():
            sums[...] = jnp.zeros_like(sums)
            tops[...] = jnp.full_like(tops, masked_score)
            totals[...] = jnp.zeros_like(totals)

        stat = part_ref[:, width:].astype(jnp.float32)
        stat = stat + pltpu.roll(stat, 128 - 16, 1) + pltpu.roll(stat, 128 - 32, 1)
        new_total = pltpu.roll(stat, 128 - heads, 1)
        top = jnp.maximum(tops[...], stat)
        old_fade, new_fade = jnp.exp(tops[...] - top), jnp.exp(stat - top)
        tops[...] = top
        totals[...] = totals[...] * old_fade + new_total * new_fade
        for head in range(heads):
            columns = slice(head * head_dim, (head + 1) * head_dim)
            sums[:, columns] = (
                sums[:, columns] * old_fade[:, head : head + 1]
                + part_ref[:, columns].astype(jnp.float32) * new_fade[:, head : head + 1]
            )

        @pl.when(i == sources - 1)
        def _():
            live = totals[...] > 0
            total = jnp.where(live, totals[...], 1.0)
            log_ref[...] = jnp.where(live, tops[...] + jnp.log(total), 0.0)
            for head in range(heads):
                columns = slice(head * head_dim, (head + 1) * head_dim)
                out_ref[:, columns] = sums[:, columns] / total[:, head : head + 1]

    return pl.pallas_call(
        kernel,
        grid=(sources,),
        in_specs=[pl.BlockSpec((rows, width + 128), lambda i: (i, 0))],
        out_specs=[
            pl.BlockSpec((rows, width), lambda i: (0, 0)),
            pl.BlockSpec((rows, 128), lambda i: (0, 0)),
        ],
        scratch_shapes=[
            pltpu.VMEM((rows, width), jnp.float32),
            pltpu.VMEM((rows, 128), jnp.float32),
            pltpu.VMEM((rows, 128), jnp.float32),
        ],
        out_shape=[
            jax.ShapeDtypeStruct((rows, width), jnp.float32),
            jax.ShapeDtypeStruct((rows, 128), jnp.float32),
        ],
        compiler_params=pltpu.CompilerParams(vmem_limit_bytes=VMEM_LIMIT),
        cost_estimate=lasting(13),
        name="combine_partials",
    )(partial)


def memory_backward(bounds, queries, grads, key_rows, value_rows, row_ids, heads, sources, rows, score_scale):
    capacity, head_dim = key_rows.shape[0] // sources, key_rows.shape[1]
    width = heads * head_dim
    span = min(384, capacity)
    chunk = math.gcd(rows, 32)

    def kernel(bounds_ref, q_ref, g_ref, k_ref, v_ref, id_ref, out_ref, sums, stats, raw, products, slopes):
        source = pl.program_id(0)
        stats[...] = joined_tile(g_ref[:, width : width + 128])

        def window(heads_here, starts, least):
            here = [pl.ds(pl.multiple_of(start, 16), span) for start in starts]
            columns = [columns_of(head, head_dim) for head in heads_here]
            for slot in range(len(starts)):
                raw[slot] = lax.dot_general(
                    q_ref[:, columns[slot]],
                    k_ref[here[slot], :],
                    contract_cols,
                    preferred_element_type=jnp.float32,
                )
                products[slot] = lax.dot_general(
                    g_ref[:, columns[slot]],
                    v_ref[here[slot], :],
                    contract_cols,
                    preferred_element_type=jnp.float32,
                )
            for slot, (head, start) in enumerate(zip(heads_here, starts)):
                lines = window_ids(id_ref, start, span)
                turned = stats[...]
                if least is not None:
                    turned = pltpu.roll(turned, 128 - head, 1)
                elif head:
                    turned = turned[:, head:]
                for at in range(0, rows, chunk):
                    some = slice(at, at + chunk)
                    mine = owned(lines, head * rows + at, chunk, start, least)
                    log, delta = turned[some, :1], turned[some, heads : heads + 1]
                    probs = jnp.exp(jnp.where(mine, raw[slot, some, :] * score_scale - log, dead_score))
                    slopes[slot, some, :] = (probs * (products[slot, some, :] - delta)).astype(
                        jnp.bfloat16
                    )
            for slot in range(len(starts)):
                found = jnp.dot(
                    slopes[slot], k_ref[here[slot], :], preferred_element_type=jnp.float32
                )
                sums[:, columns[slot]] = found if least is None else sums[:, columns[slot]] + found

        window(
            list(range(heads)),
            [window_of(bounds_ref, source, head, heads, span, capacity)[0] for head in range(heads)],
            None,
        )

        @pl.loop(0, heads)
        def _(head):
            start, extra = window_of(bounds_ref, source, head, heads, span, capacity)

            @pl.loop(0, extra)
            def _(turn):
                least = start + (turn + 1) * span
                window([head], [jnp.minimum(least, capacity - span)], least)

        out_ref[...] = sums[...].astype(jnp.bfloat16)

    return pl.pallas_call(
        kernel,
        grid_spec=pltpu.PrefetchScalarGridSpec(
            num_scalar_prefetch=1,
            grid=(sources,),
            in_specs=[
                pl.BlockSpec((rows, width), lambda i, *_: (i, 0)),
                pl.BlockSpec((rows, width + 128), lambda i, *_: (i, 0)),
                pl.BlockSpec((capacity, head_dim), lambda i, *_: (i, 0)),
                pl.BlockSpec((capacity, head_dim), lambda i, *_: (i, 0)),
                pl.BlockSpec((1, *row_ids.shape[1:]), lambda i, *_: (i, 0, 0)),
            ],
            out_specs=pl.BlockSpec((rows, width), lambda i, *_: (i, 0)),
            scratch_shapes=[
                pltpu.VMEM((rows, width), jnp.float32),
                pltpu.VMEM((rows, 128), jnp.float32),
                pltpu.VMEM((heads, rows, span), jnp.float32),
                pltpu.VMEM((heads, rows, span), jnp.float32),
                pltpu.VMEM((heads, rows, span), jnp.bfloat16),
            ],
        ),
        out_shape=jax.ShapeDtypeStruct((sources * rows, width), jnp.bfloat16),
        compiler_params=pltpu.CompilerParams(vmem_limit_bytes=VMEM_LIMIT),
        cost_estimate=lasting(25),
        name="memory_backward",
    )(bounds, queries, grads, key_rows, value_rows, row_ids)


def remote(source, target, send_sem, recv_sem, device):
    return pltpu.make_async_remote_copy(
        src_ref=source,
        dst_ref=target,
        send_sem=send_sem,
        recv_sem=recv_sem,
        device_id={"mem": device},
        device_id_type=pl.DeviceIdType.MESH,
    )


def grid_place(depth):
    me = lax.axis_index("mem")
    layer, column = me // 4, me % 4
    beside_x = column + 1 - 2 * (column % 2)
    beside_y = column + 2 - 4 * (column // 2)
    across = 3 - column

    def index_of(step, place):
        return (layer + step + depth) % depth * 4 + place

    return me, column, beside_x, beside_y, across, index_of


def greet(devices):
    barrier = pltpu.get_barrier_semaphore()
    for device in devices:
        pl.semaphore_signal(
            barrier, inc=1, device_id={"mem": device}, device_id_type=pl.DeviceIdType.MESH
        )
    pl.semaphore_wait(barrier, len(devices))


def gather_group(block, sources, collective_id):
    rows, width = block.shape
    depth, half = sources // 4, rows // 2
    slots = 2 * depth - 1

    def kernel(x_ref, out_ref, own_sem, send, recv):
        me = lax.axis_index("mem")
        layer, column = me // 4, me % 4
        to_x = me + 1 - 2 * (column % 2)
        to_y = me + 2 - 4 * (column // 2)
        across = layer * 4 + 3 - column
        has_above, has_below = layer + 1 < depth, layer > 0
        barrier = pltpu.get_barrier_semaphore()

        def signal(device):
            pl.semaphore_signal(
                barrier, inc=1, device_id={"mem": device}, device_id_type=pl.DeviceIdType.MESH
            )

        signal(to_x)
        signal(to_y)
        pl.when(has_above)(lambda: signal(me + 4))
        pl.when(has_below)(lambda: signal(me - 4))
        pl.semaphore_wait(barrier, 2 + has_above.astype(jnp.int32) + has_below.astype(jnp.int32))

        def part_of(index, part):
            start = pl.multiple_of(index * rows + part * half, half)
            return out_ref.at[pl.ds(start, half), :]

        own = pltpu.make_async_copy(x_ref, out_ref.at[pl.ds(pl.multiple_of(me * rows, rows), rows), :], own_sem)
        own.start()
        sent = []

        def push(condition, source, target, kind, slot, to_slot, part, device):
            copy = remote(source, target, send.at[kind, slot, part], recv.at[kind, to_slot, part], device)
            if condition is None:
                copy.start()
            else:
                pl.when(condition)(copy.start)
            sent.append((condition, copy))

        def arrived(index, kind, slot, part):
            target = part_of(index, part)
            remote(target, target, send.at[kind, slot, part], recv.at[kind, slot, part], to_x).wait_recv()

        def up_slot(distance):
            return distance

        def down_slot(distance):
            return depth - 1 + distance

        for part in (0, 1):
            mine = x_ref.at[pl.ds(part * half, half), :]
            push(has_above, mine, part_of(me, part), 0, 0, down_slot(1), part, me + 4)
            push(has_below, mine, part_of(me, part), 1, 0, up_slot(1), part, me - 4)
            mine_y = x_ref.at[pl.ds((1 - part) * half, half), :]
            push(None, mine, part_of(me, part), 2, 0, 0, part, to_x)
            push(None, mine_y, part_of(me, 1 - part), 3, 0, 0, 1 - part, to_y)

        def pass_on(condition, step, slot):
            def go():
                arrived(to_x + step, 2, slot, 0)
                copy_a.start()
                arrived(to_y + step, 3, slot, 1)
                copy_b.start()

            source_a, source_b = part_of(to_x + step, 0), part_of(to_y + step, 1)
            copy_a = remote(source_a, source_a, send.at[4, slot, 0], recv.at[4, slot, 0], to_y)
            copy_b = remote(source_b, source_b, send.at[5, slot, 1], recv.at[5, slot, 1], to_x)
            sent.append((condition, copy_a))
            sent.append((condition, copy_b))
            if condition is None:
                go()
            else:
                pl.when(condition)(go)

        for distance in range(1, depth):
            from_above, from_below = layer + distance < depth, layer - distance >= 0

            def take(kind, back_kind, step, slot, next_slot, onward, onward_device):
                for part in (0, 1):
                    arrived(me + step, kind, slot, part)
                    here = part_of(me + step, part)
                    if next_slot is not None:
                        pl.when(onward)(
                            remote(
                                here, here, send.at[kind, slot, part], recv.at[kind, next_slot, part], onward_device
                            ).start
                        )
                    remote(here, here, send.at[2, slot, part], recv.at[2, slot, part], to_x).start()
                    remote(here, here, send.at[3, slot, part], recv.at[3, slot, part], to_y).start()

            last = distance == depth - 1
            pl.when(from_above)(
                lambda: take(
                    1, 0, 4 * distance, up_slot(distance), None if last else up_slot(distance + 1), has_below, me - 4
                )
            )
            pl.when(from_below)(
                lambda: take(
                    0, 1, -4 * distance, down_slot(distance), None if last else down_slot(distance + 1), has_above, me + 4
                )
            )
            for condition, step, slot, kind, onward in (
                (from_above, 4 * distance, up_slot(distance), 1, has_below),
                (from_below, -4 * distance, down_slot(distance), 0, has_above),
            ):
                for part in (0, 1):
                    here = part_of(me + step, part)
                    if not last:
                        sent.append((condition & onward, remote(here, here, send.at[kind, slot, part], own_sem, me)))
                    sent.append((condition, remote(here, here, send.at[2, slot, part], own_sem, to_x)))
                    sent.append((condition, remote(here, here, send.at[3, slot, part], own_sem, to_y)))
            if distance == 1:
                pass_on(None, 0, 0)
            else:
                pass_on(layer + distance - 1 < depth, 4 * (distance - 1), up_slot(distance - 1))
                pass_on(layer - distance + 1 >= 0, -4 * (distance - 1), down_slot(distance - 1))
        pass_on(layer + depth - 1 < depth, 4 * (depth - 1), up_slot(depth - 1))
        pass_on(layer - depth + 1 >= 0, -4 * (depth - 1), down_slot(depth - 1))

        def close(step, slot):
            arrived(to_x + step, 2, slot, 1)
            arrived(to_y + step, 3, slot, 0)
            arrived(across + step, 4, slot, 0)
            arrived(across + step, 5, slot, 1)

        close(0, 0)
        for distance in range(1, depth):
            pl.when(layer + distance < depth)(lambda: close(4 * distance, up_slot(distance)))
            pl.when(layer - distance >= 0)(lambda: close(-4 * distance, down_slot(distance)))
        for condition, copy in sent:
            if condition is None:
                copy.wait_send()
            else:
                pl.when(condition)(copy.wait_send)
        own.wait()

    return pl.pallas_call(
        kernel,
        in_specs=[pl.BlockSpec(memory_space=pl.ANY)],
        out_specs=pl.BlockSpec(memory_space=pl.ANY),
        out_shape=jax.ShapeDtypeStruct((sources * rows, width), block.dtype),
        scratch_shapes=[
            pltpu.SemaphoreType.DMA,
            pltpu.SemaphoreType.DMA((6, slots, 2)),
            pltpu.SemaphoreType.DMA((6, slots, 2)),
        ],
        compiler_params=pltpu.CompilerParams(
            collective_id=collective_id, has_side_effects=True, vmem_limit_bytes=VMEM_LIMIT
        ),
        cost_estimate=lasting(50),
        name="gather_group",
    )(block)


def reduce_steps(parts_ref, sources, refs, sems, merge, pack):
    half_a, half_b, from_x, from_y, from_z, out_x, out_y, out_z = refs
    send, recv_a, recv_b, recv_x, recv_y, recv_z = sems
    rows = parts_ref.shape[0] // sources
    depth, half = sources // 4, rows // 2
    me, column, beside_x, beside_y, across, index_of = grid_place(depth)
    to_x, to_y = index_of(0, beside_x), index_of(0, beside_y)
    order = [*range(1, depth), 0]
    queues, sent = {"x": [], "y": [], "z": []}, []

    def piece(index, part):
        return parts_ref.at[pl.ds(pl.multiple_of(index * rows + part * half, half), half), :]

    def part_rows(part):
        return pl.ds(part * half, half)

    def push(link, source, target, kind, k, recv_sem, device):
        queue = queues[link]
        if link != "z" and len(queue) >= 2:
            queue.pop(0).wait_send()
        copy = remote(source, target, send.at[kind, k], recv_sem, device)
        copy.start()
        queue.append(copy)

    def arrived(target, recv_sem):
        remote(target, target, send.at[0, 0], recv_sem, to_x).wait_recv()

    def plane_rest(k):
        push("x", piece(index_of(k, beside_x), 0), from_x.at[k, part_rows(0)], 2, k, recv_x.at[0, k], to_x)
        push("y", piece(index_of(k, beside_y), 1), from_y.at[k, part_rows(1)], 3, k, recv_y.at[1, k], to_y)

    def plane_merged(k):
        arrived(half_a.at[k], recv_a.at[k])
        pack(out_y.at[k], merge([piece(index_of(k, beside_y), 0), half_a.at[k]]))
        push("y", out_y.at[k], from_y.at[k, part_rows(0)], 4, k, recv_y.at[0, k], to_y)
        arrived(half_b.at[k], recv_b.at[k])
        pack(out_x.at[k], merge([piece(index_of(k, beside_x), 1), half_b.at[k]]))
        push("x", out_x.at[k], from_x.at[k, part_rows(1)], 5, k, recv_x.at[1, k], to_x)

    def column_step(k):
        for part in (0, 1):
            here = part_rows(part)
            arrived(from_x.at[k, here], recv_x.at[part, k])
            arrived(from_y.at[k, here], recv_y.at[part, k])
            if k:
                blocks = [piece(index_of(k, column), part), from_x.at[k, here], from_y.at[k, here]]
                pack(out_z.at[k, here], merge(blocks))
        if k:
            push("z", out_z.at[k], from_z.at[k], 6, k, recv_z.at[k], index_of(k, column))

    for k in order:
        far = index_of(k, across)
        push("x", piece(far, 0), half_a.at[k], 0, k, recv_a.at[k], to_x)
        push("y", piece(far, 1), half_b.at[k], 1, k, recv_b.at[k], to_y)
    for i, k in enumerate(order):
        plane_rest(k)
        plane_merged(k)
        if i:
            column_step(order[i - 1])
    column_step(order[-1])
    for k in range(1, depth):
        arrived(from_z.at[k], recv_z.at[k])
    final = []
    for part in (0, 1):
        here = part_rows(part)
        blocks = [piece(me, part), from_x.at[0, here], from_y.at[0, here]]
        final.append((here, blocks + [from_z.at[k, here] for k in range(1, depth)]))
    return final, [copy for queue in queues.values() for copy in queue]


def reduce_scratch(rows, width, dtype, sources):
    depth, half = sources // 4, rows // 2

    def slots(size):
        return pltpu.VMEM((depth, size, width), dtype)

    refs = [slots(half), slots(half), slots(rows), slots(rows), slots(rows)]
    refs += [slots(half), slots(half), slots(rows)]
    sems = [pltpu.SemaphoreType.DMA((7, depth))]
    sems += [pltpu.SemaphoreType.DMA((depth,))] * 2
    sems += [pltpu.SemaphoreType.DMA((2, depth))] * 2
    sems += [pltpu.SemaphoreType.DMA((depth,))]
    return refs, sems


def reduce_group(parts, sources, collective_id, merge, pack, finish, out_shape):
    rows, width = parts.shape[0] // sources, parts.shape[1]
    depth = sources // 4
    outs = len(out_shape)
    ref_shapes, sem_shapes = reduce_scratch(rows, width, parts.dtype, sources)

    def kernel(parts_ref, *refs):
        out_refs, refs = refs[:outs], refs[outs:]
        me, column, beside_x, beside_y, across, index_of = grid_place(depth)
        greet(
            [index_of(0, beside_x), index_of(0, beside_y)]
            + [index_of(-k, column) for k in range(1, depth)]
        )
        final, still_open = reduce_steps(
            parts_ref, sources, refs[: len(ref_shapes)], refs[len(ref_shapes) :], merge, pack
        )
        for here, blocks in final:
            finish([out.at[here] for out in out_refs], merge(blocks))
        for copy in still_open:
            copy.wait_send()

    return pl.pallas_call(
        kernel,
        in_specs=[pl.BlockSpec(memory_space=pltpu.VMEM)],
        out_specs=[pl.BlockSpec(memory_space=pltpu.VMEM)] * outs,
        out_shape=out_shape,
        scratch_shapes=ref_shapes + sem_shapes,
        compiler_params=pltpu.CompilerParams(
            collective_id=collective_id, has_side_effects=True, vmem_limit_bytes=VMEM_LIMIT
        ),
        cost_estimate=lasting(55),
        name="reduce_group",
    )(parts)


def sum_blocks(parts, sources, collective_id):
    rows, width = parts.shape[0] // sources, parts.shape[1]

    def merge(blocks):
        total = blocks[0][...].astype(jnp.float32)
        for block in blocks[1:]:
            total = total + block[...].astype(jnp.float32)
        return total

    def pack(target, total):
        target[...] = total.astype(parts.dtype)

    def finish(targets, total):
        targets[0][...] = total

    out_shape = [jax.ShapeDtypeStruct((rows, width), jnp.float32)]
    return reduce_group(parts, sources, collective_id, merge, pack, finish, out_shape)[0]


def merge_partials(parts, sources, collective_id, heads):
    rows, width = parts.shape[0] // sources, parts.shape[1] - 128
    head_dim = width // heads

    def merge(blocks):
        stats = []
        for block in blocks:
            stat = block[:, width:].astype(jnp.float32)
            stats.append(stat + pltpu.roll(stat, 128 - 16, 1) + pltpu.roll(stat, 128 - 32, 1))
        top = stats[0]
        for stat in stats[1:]:
            top = jnp.maximum(top, stat)
        fades = [jnp.exp(stat - top) for stat in stats]
        total = sum(fade * pltpu.roll(stat, 128 - heads, 1) for fade, stat in zip(fades, stats))
        sums = []
        for head in range(heads):
            columns = slice(head * head_dim, (head + 1) * head_dim)
            sums.append(
                sum(
                    block[:, columns].astype(jnp.float32) * fade[:, head : head + 1]
                    for block, fade in zip(blocks, fades)
                )
            )
        return sums, top, total

    def pack(target, merged):
        sums, top, total = merged
        for head in range(heads):
            target[:, head * head_dim : (head + 1) * head_dim] = sums[head].astype(parts.dtype)
        lane = lax.broadcasted_iota(jnp.int32, top.shape, 1)
        stat = jnp.where(lane < heads, top, jnp.where(lane < 16, pltpu.roll(total, heads, 1), 0.0))
        target[:, width:] = triple(stat + pltpu.roll(stat, 16, 1) + pltpu.roll(stat, 32, 1))

    def finish(targets, merged):
        sums, top, total = merged
        live = total > 0
        total = jnp.where(live, total, 1.0)
        targets[1][...] = jnp.where(live, top + jnp.log(total), 0.0)
        for head in range(heads):
            targets[0][:, head * head_dim : (head + 1) * head_dim] = sums[head] / total[:, head : head + 1]

    out_shape = [
        jax.ShapeDtypeStruct((rows, width), jnp.float32),
        jax.ShapeDtypeStruct((rows, 128), jnp.float32),
    ]
    return reduce_group(parts, sources, collective_id, merge, pack, finish, out_shape)


def weight_halves(pairs):
    core = lax.axis_index("dp")
    lefts, kept, sent = [], [], []
    for left, right in pairs:
        half = right.shape[1] // 2
        lefts.append(left)
        kept.append(lax.dynamic_slice_in_dim(right, core * half, half, 1))
        sent.append(lax.dynamic_slice_in_dim(right, (1 - core) * half, half, 1))
    other = swapped(jnp.concatenate(lefts + sent, axis=1))
    partials, left_at, at = [], 0, sum(left.shape[1] for left in lefts)
    for left, right in zip(lefts, kept):
        other_left = other[:, left_at : left_at + left.shape[1]]
        other_right = other[:, at : at + right.shape[1]]
        left_at, at = left_at + left.shape[1], at + right.shape[1]
        partials.append(
            lax.dot_general(
                jnp.concatenate([left, other_left], axis=0),
                jnp.concatenate([right, other_right], axis=0),
                contract_rows,
                preferred_element_type=jnp.float32,
            ).astype(jnp.bfloat16)
        )
    return jnp.concatenate(partials, axis=1)


def scattered(halves):
    return lax.psum_scatter(halves, "mem", scatter_dimension=0, tiled=True)


def whole_grads(both, widths):
    both = both.astype(jnp.float32)
    grads, at = [], 0
    for size in widths:
        half = size // 2
        grads.append(jnp.concatenate([both[0, :, at : at + half], both[1, :, at : at + half]], 1))
        at += half
    return grads


def lane_tile(columns, rows):
    lane = lax.broadcasted_iota(jnp.int32, (rows, 128), 1)
    tile = jnp.zeros((rows, 128), jnp.float32)
    for i, column in enumerate(columns):
        tile = jnp.where(lane == i, column, tile)
    return tile


def split_tile(tile):
    lane = lax.broadcasted_iota(jnp.int32, tile.shape, 1)
    kept = jnp.where(lane < 32, tile, 0.0)
    kept = kept + pltpu.roll(kept, 32, 1) + pltpu.roll(kept, 64, 1)
    high = kept.astype(jnp.bfloat16).astype(jnp.float32)
    middle = (kept - high).astype(jnp.bfloat16).astype(jnp.float32)
    low = kept - high - middle
    part = lane // 32
    return jnp.where(part == 0, high, jnp.where(part == 1, middle, low)).astype(jnp.bfloat16)


def joined_tile(tile):
    tile = tile.astype(jnp.float32)
    return tile + pltpu.roll(tile, 128 - 32, 1) + pltpu.roll(tile, 128 - 64, 1)


def slanted(base, rows):
    return pltpu.roll(jnp.broadcast_to(base, (rows, base.shape[1])), 0, 1, stride=1, stride_axis=0)


def local_forward(base, book_column, book_row, own, halos, heads, score_scale):
    rows, width = own.shape[0], own.shape[1] // 3
    head_dim = width // heads
    count = len(halos) + 1

    def kernel(base_ref, column_ref, row_ref, own_ref, *refs):
        halo_refs, (out_ref, log_ref) = refs[: count - 1], refs[count - 1 :]
        same = column_ref[:, :1] == row_ref[:1, :]
        logs = []
        for head in range(heads):
            columns = slice(head * head_dim, (head + 1) * head_dim)
            above = slice(width + head * head_dim, width + (head + 1) * head_dim)
            twice = slice(2 * width + head * head_dim, 2 * width + (head + 1) * head_dim)
            keys = [ref[:, columns] for ref in halo_refs] + [own_ref[:, above]]
            values = [ref[:, above] for ref in halo_refs] + [own_ref[:, twice]]
            q = own_ref[:, columns]
            raw = [
                lax.dot_general(q, k, contract_cols, preferred_element_type=jnp.float32) for k in keys
            ]
            bias = slanted(base_ref[head : head + 1, :], rows)[:, : count * rows]
            scores = jnp.concatenate(raw, axis=1) * score_scale + bias
            scores = jnp.where(same, scores, masked_score)
            top = jnp.max(scores, axis=1, keepdims=True)
            weights = jnp.exp(scores - top)
            total = jnp.sum(weights, axis=1, keepdims=True)
            weights = (weights / total).astype(jnp.bfloat16)
            out_ref[:, columns] = sum(
                jnp.dot(
                    weights[:, i * rows : (i + 1) * rows], v, preferred_element_type=jnp.float32
                )
                for i, v in enumerate(values)
            )
            logs.append(top + jnp.log(total))
        log_ref[...] = lane_tile(logs, rows)

    return pl.pallas_call(
        kernel,
        out_shape=[
            jax.ShapeDtypeStruct((rows, width), jnp.float32),
            jax.ShapeDtypeStruct((rows, 128), jnp.float32),
        ],
        compiler_params=pltpu.CompilerParams(vmem_limit_bytes=VMEM_LIMIT),
        cost_estimate=lasting(10),
        name="local_forward",
    )(base, book_column, book_row, own, *halos)


def local_queries(
    base, book_column, book_row, own, halos, d_mixed, memory_out, local_out, mem_log, local_log, share, heads, score_scale
):
    rows, width = d_mixed.shape
    head_dim = width // heads
    count = len(halos) + 1
    span = base.shape[1]

    def kernel(
        base_ref, column_ref, row_ref, own_ref, mix_ref, mem_ref, loc_ref, mem_log_ref, log_ref, share_ref, *refs
    ):
        halo_refs, (dq_ref, diagonal_ref, gate_ref, sent_ref) = refs[: count - 1], refs[count - 1 :]
        same = column_ref[:, :1] == row_ref[:1, :]
        turned = (
            lax.broadcasted_iota(jnp.int32, (rows, rows), 0)
            + lax.broadcasted_iota(jnp.int32, (rows, rows), 1)
            == rows - 1
        ).astype(jnp.bfloat16)
        mem_deltas, deltas = [], []
        for head in range(heads):
            columns = slice(head * head_dim, (head + 1) * head_dim)
            above = slice(width + head * head_dim, width + (head + 1) * head_dim)
            twice = slice(2 * width + head * head_dim, 2 * width + (head + 1) * head_dim)
            keys = [ref[:, columns] for ref in halo_refs] + [own_ref[:, above]]
            values = [ref[:, above] for ref in halo_refs] + [own_ref[:, twice]]
            q = own_ref[:, columns]
            share_here = share_ref[head]
            d_mix, mem_here, loc_here = mix_ref[:, columns], mem_ref[:, columns], loc_ref[:, columns]
            d_mem = (share_here * d_mix).astype(jnp.bfloat16)
            d_out = ((1.0 - share_here) * d_mix).astype(jnp.bfloat16)
            sent_ref[:, columns] = d_mem
            mem_deltas.append(
                jnp.sum(d_mem.astype(jnp.float32) * mem_here, axis=1, keepdims=True)
            )
            delta = jnp.sum(d_out.astype(jnp.float32) * loc_here, axis=1, keepdims=True)
            deltas.append(delta)
            gate_ref[head : head + 1, :] = jnp.sum(
                d_mix * (mem_here - loc_here), axis=0, keepdims=True
            )
            raw = [
                lax.dot_general(q, k, contract_cols, preferred_element_type=jnp.float32) for k in keys
            ]
            bias = slanted(base_ref[head : head + 1, :], rows)[:, : count * rows]
            scores = jnp.concatenate(raw, axis=1) * score_scale + bias
            probs = jnp.exp(jnp.where(same, scores - log_ref[:, head : head + 1], masked_score))
            products = [
                lax.dot_general(d_out, v, contract_cols, preferred_element_type=jnp.float32)
                for v in values
            ]
            slopes = (probs * (jnp.concatenate(products, axis=1) - delta)).astype(jnp.bfloat16)
            slope_blocks = [slopes[:, i * rows : (i + 1) * rows] for i in range(count)]
            dq_ref[:, columns] = score_scale * sum(
                jnp.dot(s, k, preferred_element_type=jnp.float32) for s, k in zip(slope_blocks, keys)
            )
            mirrored = [
                jnp.dot(s, turned, preferred_element_type=jnp.float32) for s in slope_blocks[::-1]
            ]
            mirrored.append(jnp.zeros((rows, span - count * rows), jnp.float32))
            leaned = pltpu.roll(jnp.concatenate(mirrored, axis=1), 0, 1, stride=1, stride_axis=0)
            diagonal_ref[head : head + 1, :] = jnp.sum(leaned, axis=0, keepdims=True)
        mem_logs = [mem_log_ref[:, head : head + 1] for head in range(heads)]
        logs = [log_ref[:, head : head + 1] for head in range(heads)]
        sent_ref[:, width:] = split_tile(lane_tile(mem_logs + mem_deltas + logs + deltas, rows))

    vmem = pl.BlockSpec(memory_space=pltpu.VMEM)
    return pl.pallas_call(
        kernel,
        in_specs=[vmem] * 9 + [pl.BlockSpec(memory_space=pltpu.SMEM)] + [vmem] * len(halos),
        out_shape=[
            jax.ShapeDtypeStruct((rows, width), jnp.float32),
            jax.ShapeDtypeStruct((heads, span), jnp.float32),
            jax.ShapeDtypeStruct((heads, head_dim), jnp.float32),
            jax.ShapeDtypeStruct((rows, width + 128), jnp.bfloat16),
        ],
        compiler_params=pltpu.CompilerParams(vmem_limit_bytes=VMEM_LIMIT),
        cost_estimate=lasting(15),
        name="local_queries",
    )(base, book_column, book_row, own, d_mixed, memory_out, local_out, mem_log, local_log, share, *halos)


def local_keys(base, book_column, book_row, own, queries, sent, ratio, me, count, heads, score_scale):
    rows, width = own.shape[0], own.shape[1] // 3
    head_dim = width // heads
    groups = queries.shape[0] // rows

    def kernel(me_ref, base_ref, column_ref, row_ref, own_ref, ratio_ref, *refs):
        q_refs, g_refs, out_ref = refs[:count], refs[count : 2 * count], refs[2 * count]
        same = column_ref[:, :1] == row_ref[:1, :]
        stats = jnp.concatenate([joined_tile(ref[:, width:]).T for ref in g_refs], axis=1)
        for head in range(heads):
            columns = slice(head * head_dim, (head + 1) * head_dim)
            above = slice(width + head * head_dim, width + (head + 1) * head_dim)
            twice = slice(2 * width + head * head_dim, 2 * width + (head + 1) * head_dim)
            k, v = own_ref[:, above], own_ref[:, twice]
            qs = [ref[:, columns] for ref in q_refs]
            gs = [
                (ref[:, columns].astype(jnp.float32) * ratio_ref[head]).astype(jnp.bfloat16)
                for ref in g_refs
            ]
            raw = [
                lax.dot_general(k, q, contract_cols, preferred_element_type=jnp.float32) for q in qs
            ]
            bias = slanted(base_ref[head : head + 1, :], rows)[:, : count * rows]
            scores = jnp.concatenate(raw, axis=1) * score_scale + bias
            log = stats[2 * heads + head : 2 * heads + head + 1, :]
            delta = stats[3 * heads + head : 3 * heads + head + 1, :]
            probs = jnp.exp(jnp.where(same, scores - log, masked_score))
            products = [
                lax.dot_general(v, g, contract_cols, preferred_element_type=jnp.float32) for g in gs
            ]
            slopes = (probs * (jnp.concatenate(products, axis=1) - delta)).astype(jnp.bfloat16)
            weights = probs.astype(jnp.bfloat16)
            blocks = [slice(i * rows, (i + 1) * rows) for i in range(count)]
            d_key = sum(
                jnp.dot(slopes[:, b], q, preferred_element_type=jnp.float32) for b, q in zip(blocks, qs)
            )
            d_value = sum(
                jnp.dot(weights[:, b], g, preferred_element_type=jnp.float32)
                for b, g in zip(blocks, gs)
            )
            out_ref[:, columns] = (d_key * score_scale).astype(jnp.bfloat16)
            out_ref[:, above] = d_value.astype(jnp.bfloat16)

    def whole(array):
        return pl.BlockSpec(array.shape, lambda i, *_: (0, 0))

    def later(distance, size):
        return pl.BlockSpec((rows, size), lambda i, m: (jnp.minimum(m[0] + distance, groups - 1), 0))

    return pl.pallas_call(
        kernel,
        grid_spec=pltpu.PrefetchScalarGridSpec(
            num_scalar_prefetch=1,
            grid=(1,),
            in_specs=[whole(base), whole(book_column), whole(book_row), whole(own)]
            + [pl.BlockSpec(memory_space=pltpu.SMEM)]
            + [later(i, width) for i in range(count)]
            + [later(i, width + 128) for i in range(count)],
            out_specs=pl.BlockSpec((rows, 2 * width), lambda i, *_: (0, 0)),
        ),
        out_shape=jax.ShapeDtypeStruct((rows, 2 * width), jnp.bfloat16),
        compiler_params=pltpu.CompilerParams(vmem_limit_bytes=VMEM_LIMIT),
        cost_estimate=lasting(15),
        name="local_keys",
    )(me, base, book_column, book_row, own, ratio, *([queries] * count), *([sent] * count))


def finish_grads(parts, early, small, sources, collective_id):
    rows, width = parts.shape[0] // sources, parts.shape[1]
    mesh_type = pl.DeviceIdType.MESH
    ref_shapes, sem_shapes = reduce_scratch(rows, width, parts.dtype, sources)

    def kernel(parts_ref, early_ref, small_ref, late_out, early_out, small_out, *refs):
        steps_refs, refs = refs[: len(ref_shapes)], refs[len(ref_shapes) :]
        steps_sems, refs = refs[: len(sem_shapes)], refs[len(sem_shapes) :]
        smalls, core_small, small_send, small_recv, core_send, core_recv = refs
        me, core = lax.axis_index("mem"), lax.axis_index("dp")
        barrier = pltpu.get_barrier_semaphore()
        peers = [lax.rem(me + k, sources) for k in range(1, sources)]
        for peer in peers:
            pl.semaphore_signal(barrier, inc=1, device_id={"mem": peer}, device_id_type=mesh_type)
        pl.semaphore_signal(barrier, inc=1, device_id={"dp": 1 - core}, device_id_type=mesh_type)
        pl.semaphore_wait(barrier, sources)

        def merge(blocks):
            total = blocks[0][...].astype(jnp.float32)
            for block in blocks[1:]:
                total = total + block[...].astype(jnp.float32)
            return total

        def pack(target, total):
            target[...] = total.astype(parts.dtype)

        def across_cores(source, target, i):
            copy = pltpu.make_async_remote_copy(
                src_ref=source,
                dst_ref=target,
                send_sem=core_send.at[i],
                recv_sem=core_recv.at[i],
                device_id={"dp": 1 - core},
                device_id_type=mesh_type,
            )
            copy.start()
            return copy

        smalls[me] = small_ref[...]
        small_copies = [
            remote(small_ref, smalls.at[me], small_send.at[i], small_recv.at[me], peer)
            for i, peer in enumerate(peers)
        ]
        for copy in small_copies:
            copy.start()
        early_copy = across_cores(early_ref, early_out.at[core], 0)
        early_out[core] = early_ref[...]
        final, still_open = reduce_steps(parts_ref, sources, steps_refs, steps_sems, merge, pack)
        for here, blocks in final:
            late_out[core, here] = merge(blocks).astype(parts.dtype)
        late_copy = across_cores(late_out.at[core], late_out.at[core], 2)
        for peer in peers:
            remote(
                smalls.at[peer], smalls.at[peer], small_send.at[0], small_recv.at[peer], peer
            ).wait_recv()
        group_small = smalls[0]
        for i in range(1, sources):
            group_small = group_small + smalls[i]
        core_small[0] = group_small
        small_copy = across_cores(core_small.at[0], core_small.at[1], 1)
        for copy in (early_copy, late_copy, small_copy):
            copy.wait()
        small_out[...] = core_small[0] + core_small[1]
        for copy in still_open + small_copies:
            copy.wait_send()

    vmem = pl.BlockSpec(memory_space=pltpu.VMEM)
    return pl.pallas_call(
        kernel,
        in_specs=[vmem] * 3,
        out_specs=[vmem] * 3,
        out_shape=[
            jax.ShapeDtypeStruct((2, rows, width), parts.dtype),
            jax.ShapeDtypeStruct((2, *early.shape), early.dtype),
            jax.ShapeDtypeStruct(small.shape, small.dtype),
        ],
        scratch_shapes=ref_shapes
        + sem_shapes
        + [pltpu.VMEM((sources, *small.shape), small.dtype), pltpu.VMEM((2, *small.shape), small.dtype)]
        + [pltpu.SemaphoreType.DMA((sources,))] * 2
        + [pltpu.SemaphoreType.DMA((3,))] * 2,
        compiler_params=pltpu.CompilerParams(
            collective_id=collective_id, has_side_effects=True, vmem_limit_bytes=VMEM_LIMIT
        ),
        cost_estimate=lasting(45),
        name="finish_grads",
    )(parts, early, small)


def on_device(
    tokens,
    attn_gain,
    qkv_weight,
    out_weight,
    bias_table,
    gate_logit,
    ffn_gain,
    up_weight,
    down_weight,
    memory_keys,
    memory_values,
    book_lengths,
    slot_shard,
    slot_index,
    slot_live,
    cotangent,
):
    rows, width = tokens.shape
    heads, buckets = bias_table.shape
    head_dim = width // heads
    top_count = slot_index.shape[2]
    hidden = up_weight.shape[1]
    groups = lax.axis_size("mem")
    capacity = -(-3 * rows * heads * top_count // (2 * groups) // 128) * 128
    score_scale = 1.0 / math.sqrt(head_dim)
    repeats = W // rows
    span = W + 2 * rows
    me = lax.axis_index("mem")
    first_pos = me * rows
    lengths = book_lengths[0]
    window = jnp.arange(W + rows, dtype=jnp.int32)
    key_pos = first_pos - W + window
    key_book = jnp.where(key_pos >= 0, book_of(key_pos, lengths), -1)
    later_book = book_of(first_pos + window, lengths)
    own_book = jnp.broadcast_to(later_book[:rows, None], (rows, 128))
    key_book = jnp.broadcast_to(key_book[None, :], (8, W + rows))
    later_book = jnp.broadcast_to(later_book[None, :], (8, W + rows))
    bucket = bucket_of(jnp.arange(W, dtype=jnp.int32))
    one_hot = (bucket[:, None] == jnp.arange(buckets, dtype=jnp.int32)).astype(jnp.float32)
    offset_bias = jnp.einsum("rb,hb->hr", one_hot, bias_table, precision=lax.Precision.HIGHEST)
    after_bias = jnp.pad(offset_bias, ((0, 0), (0, span - W)), constant_values=masked_score)
    before_bias = jnp.pad(
        offset_bias[:, ::-1], ((0, 0), (1, span - W - 1)), constant_values=masked_score
    )
    tokens_f = tokens.astype(jnp.float32)
    normed_f, norm_in_back = jax.vjp(normed, tokens_f, attn_gain)
    normed_in = normed_f.astype(jnp.bfloat16)
    projected = jnp.dot(normed_in, qkv_weight, preferred_element_type=jnp.float32).astype(
        jnp.bfloat16
    )
    slots = memory_keys.shape[0]
    requests = place_requests(slot_shard, slot_index, slot_live, groups, capacity, slots)
    incoming = lax.all_to_all(requests, "mem", split_axis=0, concat_axis=0, tiled=True)
    keys_values, _ = lax.optimization_barrier((projected[:, width:], requests))
    halos = [passed_along(keys_values, "mem", distance) for distance in range(repeats, 0, -1)]
    row_ids = incoming // slots
    limits = jnp.arange(heads + 1, dtype=jnp.int32) * (rows * slots)
    bounds = jnp.sum((incoming[:, None] < limits[None, :, None, None]).astype(jnp.int32), axis=(2, 3))
    index = jnp.where(row_ids < heads * rows, row_ids // rows * slots + incoming % slots, 0)
    padded_ids = jnp.pad(row_ids, ((0, 0), (0, 1), (0, 0)), constant_values=heads * rows)
    key_rows, value_rows = gather_rows(
        index.reshape(-1), bounds[:, heads], memory_keys, memory_values, heads, groups, capacity
    )
    all_queries = lax.all_gather(projected[:, :width], "mem", axis=0, tiled=True)
    local_out, local_log = local_forward(
        before_bias, own_book, key_book, projected, halos, heads, score_scale
    )
    partial = memory_forward(
        bounds.reshape(-1),
        all_queries,
        key_rows,
        value_rows,
        padded_ids,
        heads,
        groups,
        rows,
        score_scale,
    )
    if groups == 16:
        memory_out, mem_log = merge_partials(partial, groups, 1, heads)
    else:
        partial = lax.all_to_all(
            partial.reshape(groups, rows, width + 128),
            "mem",
            split_axis=0,
            concat_axis=0,
            tiled=True,
        ).reshape(groups * rows, width + 128)
        memory_out, mem_log = combine_partials(partial, heads, groups, rows)
    gate_share = jax.nn.sigmoid(gate_logit)
    share_wide = jnp.repeat(gate_share, head_dim)[None, :]
    mixed_heads = (share_wide * memory_out + (1.0 - share_wide) * local_out).astype(jnp.bfloat16)
    residual = tokens_f + jnp.dot(mixed_heads, out_weight, preferred_element_type=jnp.float32)
    normed_mid_f, norm_mid_back = jax.vjp(normed, residual, ffn_gain)
    normed_mid = normed_mid_f.astype(jnp.bfloat16)
    up_proj = jnp.dot(normed_mid, up_weight, preferred_element_type=jnp.float32)
    activated_f, gelu_back = jax.vjp(gelu_exact, up_proj)
    activated = activated_f.astype(jnp.bfloat16)
    ffn_branch = lax.dot_general(
        activated, down_weight, contract_cols, preferred_element_type=jnp.float32
    )
    block_out = (residual + ffn_branch).astype(jnp.bfloat16)
    d_act = jnp.dot(cotangent, down_weight, preferred_element_type=jnp.float32)
    d_up = gelu_back(d_act)[0].astype(jnp.bfloat16)
    d_mid = lax.dot_general(d_up, up_weight, contract_cols, preferred_element_type=jnp.float32)
    d_resid_part, ffn_gain_part = norm_mid_back(d_mid)
    d_residual = cotangent.astype(jnp.float32) + d_resid_part
    d_branch = d_residual.astype(jnp.bfloat16)
    d_mixed = lax.dot_general(
        d_branch, out_weight, contract_cols, preferred_element_type=jnp.float32
    )
    early_halves = weight_halves([(mixed_heads, d_branch), (normed_mid, d_up), (cotangent, activated)])
    d_queries, diagonals, gate_products, sent_grads = local_queries(
        before_bias,
        own_book,
        key_book,
        projected,
        halos,
        d_mixed,
        memory_out,
        local_out,
        mem_log,
        local_log,
        gate_share,
        heads,
        score_scale,
    )
    gate_part = jnp.sum(gate_products, axis=1) * gate_share * (1.0 - gate_share)
    bias_part = jnp.dot(diagonals[:, rows - 1 : rows - 1 + W], one_hot, precision=lax.Precision.HIGHEST)
    sent_grads, early_halves = lax.optimization_barrier((sent_grads, early_halves))
    early_sums = scattered(early_halves)
    if groups == 16:
        all_grads = gather_group(sent_grads, groups, 2)
    else:
        all_grads = lax.all_gather(sent_grads, "mem", axis=0, tiled=True)
    d_partial = memory_backward(
        bounds.reshape(-1),
        all_queries,
        all_grads,
        key_rows,
        value_rows,
        padded_ids,
        heads,
        groups,
        rows,
        score_scale,
    )
    d_keys_values = local_keys(
        after_bias,
        own_book,
        later_book,
        projected,
        all_queries,
        all_grads,
        (1.0 - gate_share) / gate_share,
        me[None],
        repeats + 1,
        heads,
        score_scale,
    )
    if groups == 16:
        d_partial = sum_blocks(d_partial, groups, 3)
    else:
        d_partial, d_keys_values = lax.optimization_barrier((d_partial, d_keys_values))
        d_partial = jnp.sum(
            lax.all_to_all(
                d_partial.reshape(groups, rows, width), "mem", split_axis=0, concat_axis=0, tiled=True
            ).astype(jnp.float32),
            axis=0,
        )
    d_queries = (d_queries + d_partial * score_scale).astype(jnp.bfloat16)
    d_projected = jnp.concatenate([d_queries, d_keys_values], axis=1)
    d_in = lax.dot_general(
        d_projected, qkv_weight, contract_cols, preferred_element_type=jnp.float32
    )
    d_tokens_part, attn_gain_part = norm_in_back(d_in)
    tokens_grad = d_residual + d_tokens_part
    late_halves = weight_halves([(normed_in, d_projected)])
    late_halves, early_sums = lax.optimization_barrier((late_halves, early_sums))
    small = jnp.concatenate(
        [attn_gain_part, ffn_gain_part, bias_part.reshape(-1), gate_part], axis=0
    )
    small = jnp.pad(small, (0, -small.shape[0] % 1024)).reshape(-1, 128)
    if groups == 16:
        late_both, early_both, small = finish_grads(late_halves, early_sums, small, groups, 4)
    else:
        late_both = lax.all_gather(scattered(late_halves), "dp", axis=0)
        early_both = lax.all_gather(early_sums, "dp", axis=0)
        small = lax.psum(small, ("dp", "mem"))
    small = small.reshape(-1)
    out_grad, up_grad, down_grad = whole_grads(early_both, [width, hidden, hidden])
    qkv_grad = whole_grads(late_both, [3 * width])[0]
    at_bias = 2 * width + heads * buckets
    return (
        block_out,
        tokens_grad,
        qkv_grad,
        out_grad,
        up_grad,
        down_grad,
        small[:width],
        small[width : 2 * width],
        small[2 * width : at_bias].reshape(heads, buckets),
        small[at_bias : at_bias + heads],
    )


def solution(mesh):
    in_specs = (
        P(("dp", "mem"), None),
        P(),
        P(),
        P(),
        P(),
        P(),
        P(),
        P(),
        P(),
        P("mem", None),
        P("mem", None),
        P("dp", None),
        P(("dp", "mem"), None, None, None),
        P(("dp", "mem"), None, None),
        P(("dp", "mem"), None, None),
        P(("dp", "mem"), None),
    )
    out_specs = (
        P(("dp", "mem"), None),
        P(("dp", "mem"), None),
        P("mem", None),
        P("mem", None),
        P("mem", None),
        P("mem", None),
        P(),
        P(),
        P(),
        P(),
    )
    return jax.shard_map(
        on_device, mesh=mesh, in_specs=in_specs, out_specs=out_specs, check_vma=False
    )
```

```python
import math

import jax
import jax.numpy as jnp
from jax import lax
from jax.experimental import pallas as pl
from jax.experimental.pallas import tpu as pltpu
from jax.sharding import PartitionSpec as P

W = 512
VMEM_LIMIT = 56 * 1024 * 1024


eps_norm = 1e-06
bucket_edges = tuple((math.ceil(16 * 8 ** (edge_step / 16)) for edge_step in range(1, 16)))
masked_score = -1e30
dead_score = -10000.0
contract_rows = (((0,), (0,)), ((), ()))
contract_cols = (((1,), (1,)), ((), ()))


def passed_along(value, axis, by):
    size = lax.axis_size(axis)
    pairs = [(i, i + by) for i in range(size) if 0 <= i + by < size]
    return lax.ppermute(value, axis, pairs)


def bucket_of(offset):
    past_edges = sum(((offset >= edge_pos).astype(jnp.int32) for edge_pos in bucket_edges))
    return jnp.where(offset < 16, offset, 16 + past_edges)


def normed(values, gain_vec):
    return (
        values * lax.rsqrt(jnp.mean(values * values, axis=-1, keepdims=True) + eps_norm) * gain_vec
    )


def book_of(positions, lengths):
    book_ends = jnp.cumsum(lengths, dtype=jnp.int32)
    return jnp.sum((positions[..., None] >= book_ends).astype(jnp.int32), axis=-1)


def place_requests(slot_shard, slot_index, slot_live, owners, capacity, slots):
    rows, heads, top_count = slot_index.shape
    entries = rows * heads * top_count
    row_of = (
        jnp.arange(heads, dtype=jnp.int32)[None, :] * rows
        + jnp.arange(rows, dtype=jnp.int32)[:, None]
    )
    place = row_of[:, :, None] * top_count + jnp.arange(top_count, dtype=jnp.int32)
    owner = jnp.where(slot_live > 0, slot_shard[..., 0], owners)
    keys, picked = lax.sort(
        ((owner * entries + place).reshape(-1), slot_index.reshape(-1)), num_keys=1
    )
    ends = jnp.sum(
        (keys[None, :] < (jnp.arange(owners, dtype=jnp.int32) + 1)[:, None] * entries).astype(jnp.int32),
        axis=1,
    )
    starts = jnp.concatenate([jnp.zeros((1,), jnp.int32), ends[:-1]])
    codes = keys % entries // top_count * slots + picked
    tall = -(-entries // 128)
    codes = jnp.pad(codes, (0, tall * 128 - entries)).reshape(tall, 128)
    long = capacity // 128
    empty = heads * rows * slots

    def kernel(starts_ref, ends_ref, codes_ref, lists_ref, padded):
        padded[:tall, :] = codes_ref[...]
        padded[tall:, :] = jnp.zeros((long + 8, 128), jnp.int32)
        lane = lax.broadcasted_iota(jnp.int32, (long, 128), 1)
        place = lax.broadcasted_iota(jnp.int32, (long, 128), 0) * 128 + lane

        @pl.loop(0, owners)
        def _(i):
            start, end = starts_ref[i], ends_ref[i]
            shift = start % 128
            lines = padded[pl.ds(start // 128, long + 1), :]
            turned = pltpu.roll(lines, (128 - shift) % 128, 1)
            joined = jnp.where(lane < 128 - shift, turned[:long], turned[1:])
            lists_ref[i] = jnp.where(place < end - start, joined, empty)

    return pl.pallas_call(
        kernel,
        in_specs=[pl.BlockSpec(memory_space=pltpu.SMEM)] * 2 + [pl.BlockSpec(memory_space=pltpu.VMEM)],
        out_shape=jax.ShapeDtypeStruct((owners, long, 128), jnp.int32),
        scratch_shapes=[pltpu.VMEM((tall + long + 8, 128), jnp.int32)],
        cost_estimate=lasting(3),
        name="make_lists",
    )(starts, ends, codes)


def gather_rows(index, counts, memory_keys, memory_values, heads, sources, capacity):
    slots, width = memory_keys.shape
    head_dim = width // heads
    step, part = 128, 16

    def kernel(index_ref, counts_ref, keys, values, out_keys, out_values, key_table, value_table, key_rows, value_rows):
        i = pl.program_id(0)

        @pl.when(i < heads)
        def _():
            place = pl.ds(pl.multiple_of(i * slots, slots), slots)
            key_table[place, :] = keys[...].astype(jnp.float32)
            value_table[place, :] = values[...].astype(jnp.float32)

        @pl.when(i >= heads)
        def _():
            source = i - heads

            used = (counts_ref[source] + step - 1) // step

            def store(group):
                for at in range(0, step, part):
                    here = pl.ds(pl.multiple_of(group * step, step) + at, part)
                    out_keys[here, :] = key_rows[at : at + part, :].astype(jnp.bfloat16)
                    out_values[here, :] = value_rows[at : at + part, :].astype(jnp.bfloat16)

            @pl.loop(0, used)
            def _(group):
                store(jnp.maximum(group - 1, 0))
                first = source * capacity + group * step
                for u in range(step):
                    row = index_ref[first + u]
                    key_rows[u : u + 1, :] = key_table[pl.ds(row, 1), :]
                    value_rows[u : u + 1, :] = value_table[pl.ds(row, 1), :]

            pl.when(used > 0)(lambda: store(used - 1))

            @pl.loop(used, capacity // step)
            def _(group):
                here = pl.ds(pl.multiple_of(group * step, step), step)
                out_keys[here, :] = jnp.zeros((step, head_dim), jnp.bfloat16)
                out_values[here, :] = jnp.zeros((step, head_dim), jnp.bfloat16)

    table_spec = pl.BlockSpec((slots, head_dim), lambda i, *_: (0, jnp.minimum(i, heads - 1)))
    out_spec = pl.BlockSpec((capacity, head_dim), lambda i, *_: (jnp.maximum(i - heads, 0), 0))
    out_shape = jax.ShapeDtypeStruct((sources * capacity, head_dim), jnp.bfloat16)
    return pl.pallas_call(
        kernel,
        grid_spec=pltpu.PrefetchScalarGridSpec(
            num_scalar_prefetch=2,
            grid=(heads + sources,),
            in_specs=[table_spec, table_spec],
            out_specs=[out_spec, out_spec],
            scratch_shapes=[
                pltpu.VMEM((heads * slots, head_dim), jnp.float32),
                pltpu.VMEM((heads * slots, head_dim), jnp.float32),
                pltpu.VMEM((step, head_dim), jnp.float32),
                pltpu.VMEM((step, head_dim), jnp.float32),
            ],
        ),
        out_shape=[out_shape, out_shape],
        compiler_params=pltpu.CompilerParams(vmem_limit_bytes=VMEM_LIMIT),
        cost_estimate=lasting(42),
        name="gather_rows",
    )(index, counts, memory_keys, memory_values)


def lasting(microseconds):
    return pl.CostEstimate(flops=0, bytes_accessed=3_000_000 * microseconds, transcendentals=0)


def triple(stat):
    part = lax.broadcasted_iota(jnp.int32, stat.shape, 1) // 16
    high = stat.astype(jnp.bfloat16).astype(jnp.float32)
    rest = stat - high
    middle = rest.astype(jnp.bfloat16).astype(jnp.float32)
    low = rest - middle
    chosen = jnp.where(part == 0, high, jnp.where(part == 1, middle, jnp.where(part == 2, low, 0.0)))
    return chosen.astype(jnp.bfloat16)


def window_of(bounds, source, head, heads, span, capacity):
    first = bounds[source * (heads + 1) + head]
    last = bounds[source * (heads + 1) + head + 1]
    start = jnp.minimum(first // 16 * 16, capacity - span)
    extra = jnp.maximum(last - start - 1, 0) // span
    return start, extra


def columns_of(head, head_dim):
    if isinstance(head, int):
        return slice(head * head_dim, (head + 1) * head_dim)
    return pl.ds(pl.multiple_of(head * head_dim, head_dim), head_dim)


def window_ids(id_ref, start, span):
    lines = id_ref[0, pl.ds(start // 128, span // 128 + 1), :]
    shift = start % 128
    turned = pltpu.roll(lines, (128 - shift) % 128, 1)
    lane = lax.broadcasted_iota(jnp.int32, (span // 128, 128), 1)
    return jnp.where(lane < 128 - shift, turned[:-1], turned[1:])


def owned(lines, first_row, count, start, least):
    row = lax.broadcasted_iota(jnp.int32, (count, 128), 0) + first_row
    masks = []
    for i in range(lines.shape[0]):
        mask = lines[i : i + 1, :] == row
        if least is not None:
            place = lax.broadcasted_iota(jnp.int32, (1, 128), 1) + start + i * 128
            mask = mask & (place >= least)
        masks.append(mask)
    return jnp.concatenate(masks, axis=1)


def memory_forward(bounds, queries, key_rows, value_rows, row_ids, heads, sources, rows, score_scale):
    capacity, head_dim = key_rows.shape[0] // sources, key_rows.shape[1]
    width = heads * head_dim
    span = min(384, capacity)
    chunk = math.gcd(rows, 32)

    def kernel(bounds_ref, q_ref, k_ref, v_ref, id_ref, out_ref, sums, tops, totals, raw, weights):
        source = pl.program_id(0)
        lane = lax.broadcasted_iota(jnp.int32, (chunk, 128), 1) % 16

        def window(heads_here, starts, least):
            here = [pl.ds(pl.multiple_of(start, 16), span) for start in starts]
            columns = [columns_of(head, head_dim) for head in heads_here]
            for slot in range(len(starts)):
                raw[slot] = lax.dot_general(
                    q_ref[:, columns[slot]],
                    k_ref[here[slot], :],
                    contract_cols,
                    preferred_element_type=jnp.float32,
                )
            for slot, (head, start) in enumerate(zip(heads_here, starts)):
                lines = window_ids(id_ref, start, span)
                for at in range(0, rows, chunk):
                    some = slice(at, at + chunk)
                    mine = owned(lines, head * rows + at, chunk, start, least)
                    scores = jnp.where(mine, raw[slot, some, :], masked_score)
                    top = jnp.maximum(jnp.max(scores, axis=1, keepdims=True), 0.1 * masked_score)
                    if least is not None:
                        old_top = jnp.max(
                            jnp.where(lane == head, tops[some, :], masked_score), axis=1, keepdims=True
                        )
                        top = jnp.maximum(top, old_top)
                    exps = jnp.exp((scores - top) * score_scale)
                    weights[slot, some, :] = exps.astype(jnp.bfloat16)
                    total = jnp.sum(exps, axis=1, keepdims=True)
                    if least is not None:
                        faded = jnp.exp((old_top - top) * score_scale)
                        sums[some, columns[slot]] = sums[some, columns[slot]] * faded
                        total = total + totals[some, :] * faded
                    tops[some, :] = jnp.where(lane == head, top, tops[some, :])
                    totals[some, :] = jnp.where(lane == heads + head, total, totals[some, :])
            for slot in range(len(starts)):
                found = jnp.dot(
                    weights[slot], v_ref[here[slot], :], preferred_element_type=jnp.float32
                )
                sums[:, columns[slot]] = found if least is None else sums[:, columns[slot]] + found

        tops[...] = jnp.zeros_like(tops)
        totals[...] = jnp.zeros_like(totals)

        window(
            list(range(heads)),
            [window_of(bounds_ref, source, head, heads, span, capacity)[0] for head in range(heads)],
            None,
        )

        @pl.loop(0, heads)
        def _(head):
            start, extra = window_of(bounds_ref, source, head, heads, span, capacity)

            @pl.loop(0, extra)
            def _(turn):
                least = start + (turn + 1) * span
                window([head], [jnp.minimum(least, capacity - span)], least)

        out_ref[:, :width] = sums[...].astype(jnp.bfloat16)
        wide = lax.broadcasted_iota(jnp.int32, (rows, 128), 1) % 16
        out_ref[:, width:] = triple(jnp.where(wide < heads, tops[...] * score_scale, totals[...]))

    return pl.pallas_call(
        kernel,
        grid_spec=pltpu.PrefetchScalarGridSpec(
            num_scalar_prefetch=1,
            grid=(sources,),
            in_specs=[
                pl.BlockSpec((rows, width), lambda i, *_: (i, 0)),
                pl.BlockSpec((capacity, head_dim), lambda i, *_: (i, 0)),
                pl.BlockSpec((capacity, head_dim), lambda i, *_: (i, 0)),
                pl.BlockSpec((1, *row_ids.shape[1:]), lambda i, *_: (i, 0, 0)),
            ],
            out_specs=pl.BlockSpec((rows, width + 128), lambda i, *_: (i, 0)),
            scratch_shapes=[
                pltpu.VMEM((rows, width), jnp.float32),
                pltpu.VMEM((rows, 128), jnp.float32),
                pltpu.VMEM((rows, 128), jnp.float32),
                pltpu.VMEM((heads, rows, span), jnp.float32),
                pltpu.VMEM((heads, rows, span), jnp.bfloat16),
            ],
        ),
        out_shape=jax.ShapeDtypeStruct((sources * rows, width + 128), jnp.bfloat16),
        compiler_params=pltpu.CompilerParams(vmem_limit_bytes=VMEM_LIMIT),
        cost_estimate=lasting(25),
        name="memory_forward",
    )(bounds, queries, key_rows, value_rows, row_ids)


def combine_partials(partial, heads, sources, rows):
    width = partial.shape[1] - 128
    head_dim = width // heads

    def kernel(part_ref, out_ref, log_ref, sums, tops, totals):
        i = pl.program_id(0)

        @pl.when(i == 0)
        def _():
            sums[...] = jnp.zeros_like(sums)
            tops[...] = jnp.full_like(tops, masked_score)
            totals[...] = jnp.zeros_like(totals)

        stat = part_ref[:, width:].astype(jnp.float32)
        stat = stat + pltpu.roll(stat, 128 - 16, 1) + pltpu.roll(stat, 128 - 32, 1)
        new_total = pltpu.roll(stat, 128 - heads, 1)
        top = jnp.maximum(tops[...], stat)
        old_fade, new_fade = jnp.exp(tops[...] - top), jnp.exp(stat - top)
        tops[...] = top
        totals[...] = totals[...] * old_fade + new_total * new_fade
        for head in range(heads):
            columns = slice(head * head_dim, (head + 1) * head_dim)
            sums[:, columns] = (
                sums[:, columns] * old_fade[:, head : head + 1]
                + part_ref[:, columns].astype(jnp.float32) * new_fade[:, head : head + 1]
            )

        @pl.when(i == sources - 1)
        def _():
            live = totals[...] > 0
            total = jnp.where(live, totals[...], 1.0)
            log_ref[...] = jnp.where(live, tops[...] + jnp.log(total), 0.0)
            for head in range(heads):
                columns = slice(head * head_dim, (head + 1) * head_dim)
                out_ref[:, columns] = sums[:, columns] / total[:, head : head + 1]

    return pl.pallas_call(
        kernel,
        grid=(sources,),
        in_specs=[pl.BlockSpec((rows, width + 128), lambda i: (i, 0))],
        out_specs=[
            pl.BlockSpec((rows, width), lambda i: (0, 0)),
            pl.BlockSpec((rows, 128), lambda i: (0, 0)),
        ],
        scratch_shapes=[
            pltpu.VMEM((rows, width), jnp.float32),
            pltpu.VMEM((rows, 128), jnp.float32),
            pltpu.VMEM((rows, 128), jnp.float32),
        ],
        out_shape=[
            jax.ShapeDtypeStruct((rows, width), jnp.float32),
            jax.ShapeDtypeStruct((rows, 128), jnp.float32),
        ],
        compiler_params=pltpu.CompilerParams(vmem_limit_bytes=VMEM_LIMIT),
        cost_estimate=lasting(13),
        name="combine_partials",
    )(partial)


def memory_backward(bounds, queries, grads, key_rows, value_rows, row_ids, heads, sources, rows, score_scale):
    capacity, head_dim = key_rows.shape[0] // sources, key_rows.shape[1]
    width = heads * head_dim
    span = min(384, capacity)
    chunk = math.gcd(rows, 32)

    def kernel(bounds_ref, q_ref, g_ref, k_ref, v_ref, id_ref, out_ref, sums, stats, raw, products, slopes):
        source = pl.program_id(0)
        stats[...] = joined_tile(g_ref[:, width : width + 128])

        def window(heads_here, starts, least):
            here = [pl.ds(pl.multiple_of(start, 16), span) for start in starts]
            columns = [columns_of(head, head_dim) for head in heads_here]
            for slot in range(len(starts)):
                raw[slot] = lax.dot_general(
                    q_ref[:, columns[slot]],
                    k_ref[here[slot], :],
                    contract_cols,
                    preferred_element_type=jnp.float32,
                )
                products[slot] = lax.dot_general(
                    g_ref[:, columns[slot]],
                    v_ref[here[slot], :],
                    contract_cols,
                    preferred_element_type=jnp.float32,
                )
            for slot, (head, start) in enumerate(zip(heads_here, starts)):
                lines = window_ids(id_ref, start, span)
                turned = stats[...]
                if least is not None:
                    turned = pltpu.roll(turned, 128 - head, 1)
                elif head:
                    turned = turned[:, head:]
                for at in range(0, rows, chunk):
                    some = slice(at, at + chunk)
                    mine = owned(lines, head * rows + at, chunk, start, least)
                    log, delta = turned[some, :1], turned[some, heads : heads + 1]
                    probs = jnp.exp(jnp.where(mine, raw[slot, some, :] * score_scale - log, dead_score))
                    slopes[slot, some, :] = (probs * (products[slot, some, :] - delta)).astype(
                        jnp.bfloat16
                    )
            for slot in range(len(starts)):
                found = jnp.dot(
                    slopes[slot], k_ref[here[slot], :], preferred_element_type=jnp.float32
                )
                sums[:, columns[slot]] = found if least is None else sums[:, columns[slot]] + found

        window(
            list(range(heads)),
            [window_of(bounds_ref, source, head, heads, span, capacity)[0] for head in range(heads)],
            None,
        )

        @pl.loop(0, heads)
        def _(head):
            start, extra = window_of(bounds_ref, source, head, heads, span, capacity)

            @pl.loop(0, extra)
            def _(turn):
                least = start + (turn + 1) * span
                window([head], [jnp.minimum(least, capacity - span)], least)

        out_ref[...] = sums[...].astype(jnp.bfloat16)

    return pl.pallas_call(
        kernel,
        grid_spec=pltpu.PrefetchScalarGridSpec(
            num_scalar_prefetch=1,
            grid=(sources,),
            in_specs=[
                pl.BlockSpec((rows, width), lambda i, *_: (i, 0)),
                pl.BlockSpec((rows, width + 128), lambda i, *_: (i, 0)),
                pl.BlockSpec((capacity, head_dim), lambda i, *_: (i, 0)),
                pl.BlockSpec((capacity, head_dim), lambda i, *_: (i, 0)),
                pl.BlockSpec((1, *row_ids.shape[1:]), lambda i, *_: (i, 0, 0)),
            ],
            out_specs=pl.BlockSpec((rows, width), lambda i, *_: (i, 0)),
            scratch_shapes=[
                pltpu.VMEM((rows, width), jnp.float32),
                pltpu.VMEM((rows, 128), jnp.float32),
                pltpu.VMEM((heads, rows, span), jnp.float32),
                pltpu.VMEM((heads, rows, span), jnp.float32),
                pltpu.VMEM((heads, rows, span), jnp.bfloat16),
            ],
        ),
        out_shape=jax.ShapeDtypeStruct((sources * rows, width), jnp.bfloat16),
        compiler_params=pltpu.CompilerParams(vmem_limit_bytes=VMEM_LIMIT),
        cost_estimate=lasting(25),
        name="memory_backward",
    )(bounds, queries, grads, key_rows, value_rows, row_ids)


def remote(source, target, send_sem, recv_sem, device):
    return pltpu.make_async_remote_copy(
        src_ref=source,
        dst_ref=target,
        send_sem=send_sem,
        recv_sem=recv_sem,
        device_id={"mem": device},
        device_id_type=pl.DeviceIdType.MESH,
    )


def grid_place(depth):
    me = lax.axis_index("mem")
    layer, column = me // 4, me % 4
    beside_x = column + 1 - 2 * (column % 2)
    beside_y = column + 2 - 4 * (column // 2)
    across = 3 - column

    def index_of(step, place):
        return (layer + step + depth) % depth * 4 + place

    return me, column, beside_x, beside_y, across, index_of


def greet(devices):
    barrier = pltpu.get_barrier_semaphore()
    for device in devices:
        pl.semaphore_signal(
            barrier, inc=1, device_id={"mem": device}, device_id_type=pl.DeviceIdType.MESH
        )
    pl.semaphore_wait(barrier, len(devices))


def gather_group(block, sources, collective_id):
    rows, width = block.shape
    depth, half = sources // 4, rows // 2
    slots = 2 * depth - 1

    def kernel(x_ref, out_ref, own_sem, send, recv):
        me = lax.axis_index("mem")
        layer, column = me // 4, me % 4
        to_x = me + 1 - 2 * (column % 2)
        to_y = me + 2 - 4 * (column // 2)
        across = layer * 4 + 3 - column
        has_above, has_below = layer + 1 < depth, layer > 0
        barrier = pltpu.get_barrier_semaphore()

        def signal(device):
            pl.semaphore_signal(
                barrier, inc=1, device_id={"mem": device}, device_id_type=pl.DeviceIdType.MESH
            )

        signal(to_x)
        signal(to_y)
        pl.when(has_above)(lambda: signal(me + 4))
        pl.when(has_below)(lambda: signal(me - 4))
        pl.semaphore_wait(barrier, 2 + has_above.astype(jnp.int32) + has_below.astype(jnp.int32))

        def part_of(index, part):
            start = pl.multiple_of(index * rows + part * half, half)
            return out_ref.at[pl.ds(start, half), :]

        own = pltpu.make_async_copy(x_ref, out_ref.at[pl.ds(pl.multiple_of(me * rows, rows), rows), :], own_sem)
        own.start()
        sent = []

        def push(condition, source, target, kind, slot, to_slot, part, device):
            copy = remote(source, target, send.at[kind, slot, part], recv.at[kind, to_slot, part], device)
            if condition is None:
                copy.start()
            else:
                pl.when(condition)(copy.start)
            sent.append((condition, copy))

        def arrived(index, kind, slot, part):
            target = part_of(index, part)
            remote(target, target, send.at[kind, slot, part], recv.at[kind, slot, part], to_x).wait_recv()

        def up_slot(distance):
            return distance

        def down_slot(distance):
            return depth - 1 + distance

        for part in (0, 1):
            mine = x_ref.at[pl.ds(part * half, half), :]
            push(has_above, mine, part_of(me, part), 0, 0, down_slot(1), part, me + 4)
            push(has_below, mine, part_of(me, part), 1, 0, up_slot(1), part, me - 4)
            mine_y = x_ref.at[pl.ds((1 - part) * half, half), :]
            push(None, mine, part_of(me, part), 2, 0, 0, part, to_x)
            push(None, mine_y, part_of(me, 1 - part), 3, 0, 0, 1 - part, to_y)

        def pass_on(condition, step, slot):
            def go():
                arrived(to_x + step, 2, slot, 0)
                copy_a.start()
                arrived(to_y + step, 3, slot, 1)
                copy_b.start()

            source_a, source_b = part_of(to_x + step, 0), part_of(to_y + step, 1)
            copy_a = remote(source_a, source_a, send.at[4, slot, 0], recv.at[4, slot, 0], to_y)
            copy_b = remote(source_b, source_b, send.at[5, slot, 1], recv.at[5, slot, 1], to_x)
            sent.append((condition, copy_a))
            sent.append((condition, copy_b))
            if condition is None:
                go()
            else:
                pl.when(condition)(go)

        for distance in range(1, depth):
            from_above, from_below = layer + distance < depth, layer - distance >= 0

            def take(kind, back_kind, step, slot, next_slot, onward, onward_device):
                for part in (0, 1):
                    arrived(me + step, kind, slot, part)
                    here = part_of(me + step, part)
                    if next_slot is not None:
                        pl.when(onward)(
                            remote(
                                here, here, send.at[kind, slot, part], recv.at[kind, next_slot, part], onward_device
                            ).start
                        )
                    remote(here, here, send.at[2, slot, part], recv.at[2, slot, part], to_x).start()
                    remote(here, here, send.at[3, slot, part], recv.at[3, slot, part], to_y).start()

            last = distance == depth - 1
            pl.when(from_above)(
                lambda: take(
                    1, 0, 4 * distance, up_slot(distance), None if last else up_slot(distance + 1), has_below, me - 4
                )
            )
            pl.when(from_below)(
                lambda: take(
                    0, 1, -4 * distance, down_slot(distance), None if last else down_slot(distance + 1), has_above, me + 4
                )
            )
            for condition, step, slot, kind, onward in (
                (from_above, 4 * distance, up_slot(distance), 1, has_below),
                (from_below, -4 * distance, down_slot(distance), 0, has_above),
            ):
                for part in (0, 1):
                    here = part_of(me + step, part)
                    if not last:
                        sent.append((condition & onward, remote(here, here, send.at[kind, slot, part], own_sem, me)))
                    sent.append((condition, remote(here, here, send.at[2, slot, part], own_sem, to_x)))
                    sent.append((condition, remote(here, here, send.at[3, slot, part], own_sem, to_y)))
            if distance == 1:
                pass_on(None, 0, 0)
            else:
                pass_on(layer + distance - 1 < depth, 4 * (distance - 1), up_slot(distance - 1))
                pass_on(layer - distance + 1 >= 0, -4 * (distance - 1), down_slot(distance - 1))
        pass_on(layer + depth - 1 < depth, 4 * (depth - 1), up_slot(depth - 1))
        pass_on(layer - depth + 1 >= 0, -4 * (depth - 1), down_slot(depth - 1))

        def close(step, slot):
            arrived(to_x + step, 2, slot, 1)
            arrived(to_y + step, 3, slot, 0)
            arrived(across + step, 4, slot, 0)
            arrived(across + step, 5, slot, 1)

        close(0, 0)
        for distance in range(1, depth):
            pl.when(layer + distance < depth)(lambda: close(4 * distance, up_slot(distance)))
            pl.when(layer - distance >= 0)(lambda: close(-4 * distance, down_slot(distance)))
        for condition, copy in sent:
            if condition is None:
                copy.wait_send()
            else:
                pl.when(condition)(copy.wait_send)
        own.wait()

    return pl.pallas_call(
        kernel,
        in_specs=[pl.BlockSpec(memory_space=pl.ANY)],
        out_specs=pl.BlockSpec(memory_space=pl.ANY),
        out_shape=jax.ShapeDtypeStruct((sources * rows, width), block.dtype),
        scratch_shapes=[
            pltpu.SemaphoreType.DMA,
            pltpu.SemaphoreType.DMA((6, slots, 2)),
            pltpu.SemaphoreType.DMA((6, slots, 2)),
        ],
        compiler_params=pltpu.CompilerParams(
            collective_id=collective_id, has_side_effects=True, vmem_limit_bytes=VMEM_LIMIT
        ),
        cost_estimate=lasting(50),
        name="gather_group",
    )(block)


def reduce_steps(parts_ref, sources, refs, sems, merge, pack):
    half_a, half_b, from_x, from_y, from_z, out_x, out_y, out_z = refs
    send, recv_a, recv_b, recv_x, recv_y, recv_z = sems
    rows = parts_ref.shape[0] // sources
    depth, half = sources // 4, rows // 2
    me, column, beside_x, beside_y, across, index_of = grid_place(depth)
    to_x, to_y = index_of(0, beside_x), index_of(0, beside_y)
    order = [*range(1, depth), 0]
    queues, sent = {"x": [], "y": [], "z": []}, []

    def piece(index, part):
        return parts_ref.at[pl.ds(pl.multiple_of(index * rows + part * half, half), half), :]

    def part_rows(part):
        return pl.ds(part * half, half)

    def push(link, source, target, kind, k, recv_sem, device):
        queue = queues[link]
        if link != "z" and len(queue) >= 2:
            queue.pop(0).wait_send()
        copy = remote(source, target, send.at[kind, k], recv_sem, device)
        copy.start()
        queue.append(copy)

    def arrived(target, recv_sem):
        remote(target, target, send.at[0, 0], recv_sem, to_x).wait_recv()

    def plane_rest(k):
        push("x", piece(index_of(k, beside_x), 0), from_x.at[k, part_rows(0)], 2, k, recv_x.at[0, k], to_x)
        push("y", piece(index_of(k, beside_y), 1), from_y.at[k, part_rows(1)], 3, k, recv_y.at[1, k], to_y)

    def plane_merged(k):
        arrived(half_a.at[k], recv_a.at[k])
        pack(out_y.at[k], merge([piece(index_of(k, beside_y), 0), half_a.at[k]]))
        push("y", out_y.at[k], from_y.at[k, part_rows(0)], 4, k, recv_y.at[0, k], to_y)
        arrived(half_b.at[k], recv_b.at[k])
        pack(out_x.at[k], merge([piece(index_of(k, beside_x), 1), half_b.at[k]]))
        push("x", out_x.at[k], from_x.at[k, part_rows(1)], 5, k, recv_x.at[1, k], to_x)

    def column_step(k):
        for part in (0, 1):
            here = part_rows(part)
            arrived(from_x.at[k, here], recv_x.at[part, k])
            arrived(from_y.at[k, here], recv_y.at[part, k])
            if k:
                blocks = [piece(index_of(k, column), part), from_x.at[k, here], from_y.at[k, here]]
                pack(out_z.at[k, here], merge(blocks))
        if k:
            push("z", out_z.at[k], from_z.at[k], 6, k, recv_z.at[k], index_of(k, column))

    for k in order:
        far = index_of(k, across)
        push("x", piece(far, 0), half_a.at[k], 0, k, recv_a.at[k], to_x)
        push("y", piece(far, 1), half_b.at[k], 1, k, recv_b.at[k], to_y)
    for i, k in enumerate(order):
        plane_rest(k)
        plane_merged(k)
        if i:
            column_step(order[i - 1])
    column_step(order[-1])
    for k in range(1, depth):
        arrived(from_z.at[k], recv_z.at[k])
    final = []
    for part in (0, 1):
        here = part_rows(part)
        blocks = [piece(me, part), from_x.at[0, here], from_y.at[0, here]]
        final.append((here, blocks + [from_z.at[k, here] for k in range(1, depth)]))
    return final, [copy for queue in queues.values() for copy in queue]


def reduce_scratch(rows, width, dtype, sources):
    depth, half = sources // 4, rows // 2

    def slots(size):
        return pltpu.VMEM((depth, size, width), dtype)

    refs = [slots(half), slots(half), slots(rows), slots(rows), slots(rows)]
    refs += [slots(half), slots(half), slots(rows)]
    sems = [pltpu.SemaphoreType.DMA((7, depth))]
    sems += [pltpu.SemaphoreType.DMA((depth,))] * 2
    sems += [pltpu.SemaphoreType.DMA((2, depth))] * 2
    sems += [pltpu.SemaphoreType.DMA((depth,))]
    return refs, sems


def reduce_group(parts, sources, collective_id, merge, pack, finish, out_shape):
    rows, width = parts.shape[0] // sources, parts.shape[1]
    depth = sources // 4
    outs = len(out_shape)
    ref_shapes, sem_shapes = reduce_scratch(rows, width, parts.dtype, sources)

    def kernel(parts_ref, *refs):
        out_refs, refs = refs[:outs], refs[outs:]
        me, column, beside_x, beside_y, across, index_of = grid_place(depth)
        greet(
            [index_of(0, beside_x), index_of(0, beside_y)]
            + [index_of(-k, column) for k in range(1, depth)]
        )
        final, still_open = reduce_steps(
            parts_ref, sources, refs[: len(ref_shapes)], refs[len(ref_shapes) :], merge, pack
        )
        for here, blocks in final:
            finish([out.at[here] for out in out_refs], merge(blocks))
        for copy in still_open:
            copy.wait_send()

    return pl.pallas_call(
        kernel,
        in_specs=[pl.BlockSpec(memory_space=pltpu.VMEM)],
        out_specs=[pl.BlockSpec(memory_space=pltpu.VMEM)] * outs,
        out_shape=out_shape,
        scratch_shapes=ref_shapes + sem_shapes,
        compiler_params=pltpu.CompilerParams(
            collective_id=collective_id, has_side_effects=True, vmem_limit_bytes=VMEM_LIMIT
        ),
        cost_estimate=lasting(55),
        name="reduce_group",
    )(parts)


def sum_blocks(parts, sources, collective_id):
    rows, width = parts.shape[0] // sources, parts.shape[1]

    def merge(blocks):
        total = blocks[0][...].astype(jnp.float32)
        for block in blocks[1:]:
            total = total + block[...].astype(jnp.float32)
        return total

    def pack(target, total):
        target[...] = total.astype(parts.dtype)

    def finish(targets, total):
        targets[0][...] = total

    out_shape = [jax.ShapeDtypeStruct((rows, width), jnp.float32)]
    return reduce_group(parts, sources, collective_id, merge, pack, finish, out_shape)[0]


def merge_partials(parts, sources, collective_id, heads):
    rows, width = parts.shape[0] // sources, parts.shape[1] - 128
    head_dim = width // heads

    def merge(blocks):
        stats = []
        for block in blocks:
            stat = block[:, width:].astype(jnp.float32)
            stats.append(stat + pltpu.roll(stat, 128 - 16, 1) + pltpu.roll(stat, 128 - 32, 1))
        top = stats[0]
        for stat in stats[1:]:
            top = jnp.maximum(top, stat)
        fades = [jnp.exp(stat - top) for stat in stats]
        total = sum(fade * pltpu.roll(stat, 128 - heads, 1) for fade, stat in zip(fades, stats))
        sums = []
        for head in range(heads):
            columns = slice(head * head_dim, (head + 1) * head_dim)
            sums.append(
                sum(
                    block[:, columns].astype(jnp.float32) * fade[:, head : head + 1]
                    for block, fade in zip(blocks, fades)
                )
            )
        return sums, top, total

    def pack(target, merged):
        sums, top, total = merged
        for head in range(heads):
            target[:, head * head_dim : (head + 1) * head_dim] = sums[head].astype(parts.dtype)
        lane = lax.broadcasted_iota(jnp.int32, top.shape, 1)
        stat = jnp.where(lane < heads, top, jnp.where(lane < 16, pltpu.roll(total, heads, 1), 0.0))
        target[:, width:] = triple(stat + pltpu.roll(stat, 16, 1) + pltpu.roll(stat, 32, 1))

    def finish(targets, merged):
        sums, top, total = merged
        live = total > 0
        total = jnp.where(live, total, 1.0)
        targets[1][...] = jnp.where(live, top + jnp.log(total), 0.0)
        for head in range(heads):
            targets[0][:, head * head_dim : (head + 1) * head_dim] = sums[head] / total[:, head : head + 1]

    out_shape = [
        jax.ShapeDtypeStruct((rows, width), jnp.float32),
        jax.ShapeDtypeStruct((rows, 128), jnp.float32),
    ]
    return reduce_group(parts, sources, collective_id, merge, pack, finish, out_shape)


def scattered(halves):
    return lax.psum_scatter(halves, "mem", scatter_dimension=0, tiled=True)


def whole_grads(both, widths):
    both = both.astype(jnp.float32)
    grads, at = [], 0
    for size in widths:
        half = size // 2
        grads.append(jnp.concatenate([both[0, :, at : at + half], both[1, :, at : at + half]], 1))
        at += half
    return grads


def lane_tile(columns, rows):
    lane = lax.broadcasted_iota(jnp.int32, (rows, 128), 1)
    tile = jnp.zeros((rows, 128), jnp.float32)
    for i, column in enumerate(columns):
        tile = jnp.where(lane == i, column, tile)
    return tile


def split_tile(tile):
    lane = lax.broadcasted_iota(jnp.int32, tile.shape, 1)
    kept = jnp.where(lane < 32, tile, 0.0)
    kept = kept + pltpu.roll(kept, 32, 1) + pltpu.roll(kept, 64, 1)
    high = kept.astype(jnp.bfloat16).astype(jnp.float32)
    middle = (kept - high).astype(jnp.bfloat16).astype(jnp.float32)
    low = kept - high - middle
    part = lane // 32
    return jnp.where(part == 0, high, jnp.where(part == 1, middle, low)).astype(jnp.bfloat16)


def joined_tile(tile):
    tile = tile.astype(jnp.float32)
    return tile + pltpu.roll(tile, 128 - 32, 1) + pltpu.roll(tile, 128 - 64, 1)


def slanted(base, rows):
    return pltpu.roll(jnp.broadcast_to(base, (rows, base.shape[1])), 0, 1, stride=1, stride_axis=0)


def local_forward(base, book_column, book_row, own, halos, heads, score_scale):
    rows, width = own.shape[0], own.shape[1] // 3
    head_dim = width // heads
    count = len(halos) + 1

    def kernel(base_ref, column_ref, row_ref, own_ref, *refs):
        halo_refs, (out_ref, log_ref) = refs[: count - 1], refs[count - 1 :]
        same = column_ref[:, :1] == row_ref[:1, :]
        logs = []
        for head in range(heads):
            columns = slice(head * head_dim, (head + 1) * head_dim)
            above = slice(width + head * head_dim, width + (head + 1) * head_dim)
            twice = slice(2 * width + head * head_dim, 2 * width + (head + 1) * head_dim)
            keys = [ref[:, columns] for ref in halo_refs] + [own_ref[:, above]]
            values = [ref[:, above] for ref in halo_refs] + [own_ref[:, twice]]
            q = own_ref[:, columns]
            raw = [
                lax.dot_general(q, k, contract_cols, preferred_element_type=jnp.float32) for k in keys
            ]
            bias = slanted(base_ref[head : head + 1, :], rows)[:, : count * rows]
            scores = jnp.concatenate(raw, axis=1) * score_scale + bias
            scores = jnp.where(same, scores, masked_score)
            top = jnp.max(scores, axis=1, keepdims=True)
            weights = jnp.exp(scores - top)
            total = jnp.sum(weights, axis=1, keepdims=True)
            weights = (weights / total).astype(jnp.bfloat16)
            out_ref[:, columns] = sum(
                jnp.dot(
                    weights[:, i * rows : (i + 1) * rows], v, preferred_element_type=jnp.float32
                )
                for i, v in enumerate(values)
            )
            logs.append(top + jnp.log(total))
        log_ref[...] = lane_tile(logs, rows)

    return pl.pallas_call(
        kernel,
        out_shape=[
            jax.ShapeDtypeStruct((rows, width), jnp.float32),
            jax.ShapeDtypeStruct((rows, 128), jnp.float32),
        ],
        compiler_params=pltpu.CompilerParams(vmem_limit_bytes=VMEM_LIMIT),
        cost_estimate=lasting(10),
        name="local_forward",
    )(base, book_column, book_row, own, *halos)


def local_queries(
    base, book_column, book_row, own, halos, d_mixed, memory_out, local_out, mem_log, local_log, share, heads, score_scale
):
    rows, width = d_mixed.shape
    head_dim = width // heads
    count = len(halos) + 1
    span = base.shape[1]

    def kernel(
        base_ref, column_ref, row_ref, own_ref, mix_ref, mem_ref, loc_ref, mem_log_ref, log_ref, share_ref, *refs
    ):
        halo_refs, (dq_ref, diagonal_ref, gate_ref, sent_ref) = refs[: count - 1], refs[count - 1 :]
        same = column_ref[:, :1] == row_ref[:1, :]
        turned = (
            lax.broadcasted_iota(jnp.int32, (rows, rows), 0)
            + lax.broadcasted_iota(jnp.int32, (rows, rows), 1)
            == rows - 1
        ).astype(jnp.bfloat16)
        mem_deltas, deltas = [], []
        for head in range(heads):
            columns = slice(head * head_dim, (head + 1) * head_dim)
            above = slice(width + head * head_dim, width + (head + 1) * head_dim)
            twice = slice(2 * width + head * head_dim, 2 * width + (head + 1) * head_dim)
            keys = [ref[:, columns] for ref in halo_refs] + [own_ref[:, above]]
            values = [ref[:, above] for ref in halo_refs] + [own_ref[:, twice]]
            q = own_ref[:, columns]
            share_here = share_ref[head]
            d_mix, mem_here, loc_here = mix_ref[:, columns], mem_ref[:, columns], loc_ref[:, columns]
            d_mem = (share_here * d_mix).astype(jnp.bfloat16)
            d_out = ((1.0 - share_here) * d_mix).astype(jnp.bfloat16)
            sent_ref[:, columns] = d_mem
            mem_deltas.append(
                jnp.sum(d_mem.astype(jnp.float32) * mem_here, axis=1, keepdims=True)
            )
            delta = jnp.sum(d_out.astype(jnp.float32) * loc_here, axis=1, keepdims=True)
            deltas.append(delta)
            gate_ref[head : head + 1, :] = jnp.sum(
                d_mix * (mem_here - loc_here), axis=0, keepdims=True
            )
            raw = [
                lax.dot_general(q, k, contract_cols, preferred_element_type=jnp.float32) for k in keys
            ]
            bias = slanted(base_ref[head : head + 1, :], rows)[:, : count * rows]
            scores = jnp.concatenate(raw, axis=1) * score_scale + bias
            probs = jnp.exp(jnp.where(same, scores - log_ref[:, head : head + 1], masked_score))
            products = [
                lax.dot_general(d_out, v, contract_cols, preferred_element_type=jnp.float32)
                for v in values
            ]
            slopes = (probs * (jnp.concatenate(products, axis=1) - delta)).astype(jnp.bfloat16)
            slope_blocks = [slopes[:, i * rows : (i + 1) * rows] for i in range(count)]
            dq_ref[:, columns] = score_scale * sum(
                jnp.dot(s, k, preferred_element_type=jnp.float32) for s, k in zip(slope_blocks, keys)
            )
            mirrored = [
                jnp.dot(s, turned, preferred_element_type=jnp.float32) for s in slope_blocks[::-1]
            ]
            mirrored.append(jnp.zeros((rows, span - count * rows), jnp.float32))
            leaned = pltpu.roll(jnp.concatenate(mirrored, axis=1), 0, 1, stride=1, stride_axis=0)
            diagonal_ref[head : head + 1, :] = jnp.sum(leaned, axis=0, keepdims=True)
        mem_logs = [mem_log_ref[:, head : head + 1] for head in range(heads)]
        logs = [log_ref[:, head : head + 1] for head in range(heads)]
        sent_ref[:, width:] = split_tile(lane_tile(mem_logs + mem_deltas + logs + deltas, rows))

    vmem = pl.BlockSpec(memory_space=pltpu.VMEM)
    return pl.pallas_call(
        kernel,
        in_specs=[vmem] * 9 + [pl.BlockSpec(memory_space=pltpu.SMEM)] + [vmem] * len(halos),
        out_shape=[
            jax.ShapeDtypeStruct((rows, width), jnp.float32),
            jax.ShapeDtypeStruct((heads, span), jnp.float32),
            jax.ShapeDtypeStruct((heads, head_dim), jnp.float32),
            jax.ShapeDtypeStruct((rows, width + 128), jnp.bfloat16),
        ],
        compiler_params=pltpu.CompilerParams(vmem_limit_bytes=VMEM_LIMIT),
        cost_estimate=lasting(15),
        name="local_queries",
    )(base, book_column, book_row, own, d_mixed, memory_out, local_out, mem_log, local_log, share, *halos)


def local_keys(base, book_column, book_row, own, queries, sent, ratio, me, count, heads, score_scale):
    rows, width = own.shape[0], own.shape[1] // 3
    head_dim = width // heads
    groups = queries.shape[0] // rows

    def kernel(me_ref, base_ref, column_ref, row_ref, own_ref, ratio_ref, *refs):
        q_refs, g_refs, out_ref = refs[:count], refs[count : 2 * count], refs[2 * count]
        same = column_ref[:, :1] == row_ref[:1, :]
        stats = jnp.concatenate([joined_tile(ref[:, width:]).T for ref in g_refs], axis=1)
        for head in range(heads):
            columns = slice(head * head_dim, (head + 1) * head_dim)
            above = slice(width + head * head_dim, width + (head + 1) * head_dim)
            twice = slice(2 * width + head * head_dim, 2 * width + (head + 1) * head_dim)
            k, v = own_ref[:, above], own_ref[:, twice]
            qs = [ref[:, columns] for ref in q_refs]
            gs = [
                (ref[:, columns].astype(jnp.float32) * ratio_ref[head]).astype(jnp.bfloat16)
                for ref in g_refs
            ]
            raw = [
                lax.dot_general(k, q, contract_cols, preferred_element_type=jnp.float32) for q in qs
            ]
            bias = slanted(base_ref[head : head + 1, :], rows)[:, : count * rows]
            scores = jnp.concatenate(raw, axis=1) * score_scale + bias
            log = stats[2 * heads + head : 2 * heads + head + 1, :]
            delta = stats[3 * heads + head : 3 * heads + head + 1, :]
            probs = jnp.exp(jnp.where(same, scores - log, masked_score))
            products = [
                lax.dot_general(v, g, contract_cols, preferred_element_type=jnp.float32) for g in gs
            ]
            slopes = (probs * (jnp.concatenate(products, axis=1) - delta)).astype(jnp.bfloat16)
            weights = probs.astype(jnp.bfloat16)
            blocks = [slice(i * rows, (i + 1) * rows) for i in range(count)]
            d_key = sum(
                jnp.dot(slopes[:, b], q, preferred_element_type=jnp.float32) for b, q in zip(blocks, qs)
            )
            d_value = sum(
                jnp.dot(weights[:, b], g, preferred_element_type=jnp.float32)
                for b, g in zip(blocks, gs)
            )
            out_ref[:, columns] = (d_key * score_scale).astype(jnp.bfloat16)
            out_ref[:, above] = d_value.astype(jnp.bfloat16)

    def whole(array):
        return pl.BlockSpec(array.shape, lambda i, *_: (0, 0))

    def later(distance, size):
        return pl.BlockSpec((rows, size), lambda i, m: (jnp.minimum(m[0] + distance, groups - 1), 0))

    return pl.pallas_call(
        kernel,
        grid_spec=pltpu.PrefetchScalarGridSpec(
            num_scalar_prefetch=1,
            grid=(1,),
            in_specs=[whole(base), whole(book_column), whole(book_row), whole(own)]
            + [pl.BlockSpec(memory_space=pltpu.SMEM)]
            + [later(i, width) for i in range(count)]
            + [later(i, width + 128) for i in range(count)],
            out_specs=pl.BlockSpec((rows, 2 * width), lambda i, *_: (0, 0)),
        ),
        out_shape=jax.ShapeDtypeStruct((rows, 2 * width), jnp.bfloat16),
        compiler_params=pltpu.CompilerParams(vmem_limit_bytes=VMEM_LIMIT),
        cost_estimate=lasting(15),
        name="local_keys",
    )(me, base, book_column, book_row, own, ratio, *([queries] * count), *([sent] * count))


def feed_forward(normed_mid, cotangent, up_weight, down_weight):
    rows, width = normed_mid.shape
    hidden = up_weight.shape[1]
    block = math.gcd(hidden, 1024)

    def kernel(mid_ref, cot_ref, up_ref, down_ref, act_ref, d_up_ref, branch_ref, d_mid_ref):
        first = pl.program_id(0) == 0
        up = jnp.dot(mid_ref[...], up_ref[...], preferred_element_type=jnp.float32)
        d_act = jnp.dot(cot_ref[...], down_ref[...], preferred_element_type=jnp.float32)
        below = 0.5 * (1.0 + lax.erf(up * math.sqrt(0.5)))
        density = jnp.exp(-0.5 * up * up) * (1.0 / math.sqrt(2.0 * math.pi))
        act = (up * below).astype(jnp.bfloat16)
        d_up = (d_act * (below + up * density)).astype(jnp.bfloat16)
        act_ref[...] = act
        d_up_ref[...] = d_up
        branch = lax.dot_general(act, down_ref[...], contract_cols, preferred_element_type=jnp.float32)
        d_mid = lax.dot_general(d_up, up_ref[...], contract_cols, preferred_element_type=jnp.float32)
        branch_ref[...] = jnp.where(first, branch, branch_ref[...] + branch)
        d_mid_ref[...] = jnp.where(first, d_mid, d_mid_ref[...] + d_mid)

    whole = pl.BlockSpec((rows, width), lambda i: (0, 0))
    weight = pl.BlockSpec((width, block), lambda i: (0, i))
    middle = pl.BlockSpec((rows, block), lambda i: (0, i))
    return pl.pallas_call(
        kernel,
        grid=(hidden // block,),
        in_specs=[whole, whole, weight, weight],
        out_specs=[middle, middle, whole, whole],
        out_shape=[
            jax.ShapeDtypeStruct((rows, hidden), jnp.bfloat16),
            jax.ShapeDtypeStruct((rows, hidden), jnp.bfloat16),
            jax.ShapeDtypeStruct((rows, width), jnp.float32),
            jax.ShapeDtypeStruct((rows, width), jnp.float32),
        ],
        compiler_params=pltpu.CompilerParams(vmem_limit_bytes=VMEM_LIMIT),
        cost_estimate=lasting(15),
        name="feed_forward",
    )(normed_mid, cotangent, up_weight, down_weight)


def exchange_pairs(lefts, rights, other_lefts, other_right, send, recv):
    core = lax.axis_index("dp")
    copies, at = [], 0

    def push(source, target):
        i = len(copies)
        copy = pltpu.make_async_remote_copy(
            src_ref=source,
            dst_ref=target,
            send_sem=send.at[i],
            recv_sem=recv.at[i],
            device_id={"dp": 1 - core},
            device_id_type=pl.DeviceIdType.MESH,
        )
        copy.start()
        copies.append(copy)

    for i, (left, right) in enumerate(zip(lefts, rights)):
        half = right.shape[1] // 2
        push(left, other_lefts.at[i])
        there = pl.ds(pl.multiple_of((1 - core) * half, 128), half)
        push(right.at[:, there], other_right.at[:, pl.ds(at, half)])
        at += half
    return copies


def pair_products(lefts, rights, other_lefts, other_right, turned, store):
    core = lax.axis_index("dp")
    rows = lefts[0].shape[0]
    at = 0
    for i, (left, right) in enumerate(zip(lefts, rights)):
        half = right.shape[1] // 2
        turned[:, :rows] = left[...].T
        turned[:, rows:] = other_lefts[i].T
        block = math.gcd(half, 512)
        for column in range(0, half, block):
            kept = right[:, pl.ds(pl.multiple_of(core * half + column, 128), block)]
            both = jnp.concatenate([kept, other_right[:, at + column : at + column + block]], axis=0)
            store(
                at + column,
                jnp.dot(turned[...], both, preferred_element_type=jnp.float32).astype(jnp.bfloat16),
            )
        at += half


def pair_scratch(lefts, rights):
    rows, width = lefts[0].shape
    count = len(lefts)
    return [
        pltpu.VMEM((count, rows, width), jnp.bfloat16),
        pltpu.VMEM((rows, sum(right.shape[1] for right in rights) // 2), jnp.bfloat16),
        pltpu.VMEM((width, 2 * rows), jnp.bfloat16),
        pltpu.SemaphoreType.DMA((2 * count,)),
        pltpu.SemaphoreType.DMA((2 * count,)),
    ]


def pair_grads(lefts, rights, collective_id):
    count, width = len(lefts), lefts[0].shape[1]
    total = sum(right.shape[1] for right in rights) // 2
    block = math.gcd(*[right.shape[1] // 2 for right in rights], 512)

    def kernel(*refs):
        left_refs, right_refs, out_ref = refs[:count], refs[count : 2 * count], refs[2 * count]
        other_lefts, other_right, turned, send, recv, staged, out_sem = refs[2 * count + 1 :]
        barrier = pltpu.get_barrier_semaphore()
        partner = {"dp": 1 - lax.axis_index("dp")}
        pl.semaphore_signal(barrier, inc=1, device_id=partner, device_id_type=pl.DeviceIdType.MESH)
        pl.semaphore_wait(barrier, 1)
        copies = exchange_pairs(left_refs, right_refs, other_lefts, other_right, send, recv)
        for copy in copies:
            copy.wait_recv()
        written = []

        def store(column, value):
            slot = len(written) % 2
            if len(written) >= 2:
                written[-2].wait()
            staged[slot] = value
            copy = pltpu.make_async_copy(
                staged.at[slot], out_ref.at[:, pl.ds(column, block)], out_sem.at[slot]
            )
            copy.start()
            written.append(copy)

        pair_products(left_refs, right_refs, other_lefts, other_right, turned, store)
        for copy in written[-2:]:
            copy.wait()
        for copy in copies:
            copy.wait_send()

    vmem = pl.BlockSpec(memory_space=pltpu.VMEM)
    return pl.pallas_call(
        kernel,
        in_specs=[vmem] * (2 * count),
        out_specs=pl.BlockSpec(memory_space=pl.ANY),
        out_shape=jax.ShapeDtypeStruct((width, total), jnp.bfloat16),
        scratch_shapes=pair_scratch(lefts, rights)
        + [pltpu.VMEM((2, width, block), jnp.bfloat16), pltpu.SemaphoreType.DMA((2,))],
        compiler_params=pltpu.CompilerParams(
            collective_id=collective_id, has_side_effects=True, vmem_limit_bytes=VMEM_LIMIT
        ),
        cost_estimate=lasting(10),
        name="pair_grads",
    )(*lefts, *rights)


def finish_grads(left, right, early, early_widths, small, sources, collective_id):
    width, total = left.shape[1], right.shape[1] // 2
    rows = width // sources
    mesh_type = pl.DeviceIdType.MESH
    ref_shapes, sem_shapes = reduce_scratch(rows, total, jnp.bfloat16, sources)
    pair_shapes = pair_scratch([left], [right])
    outs = len(early_widths) + 2

    def kernel(left_ref, right_ref, early_ref, small_ref, *refs):
        (late_out, *early_outs, small_out), refs = refs[:outs], refs[outs:]
        steps_refs, refs = refs[: len(ref_shapes)], refs[len(ref_shapes) :]
        steps_sems, refs = refs[: len(sem_shapes)], refs[len(sem_shapes) :]
        (other_left, other_right, turned, pair_send, pair_recv), refs = refs[:5], refs[5:]
        parts, late, both, smalls, core_small, small_send, small_recv, core_send, core_recv = refs
        me, core = lax.axis_index("mem"), lax.axis_index("dp")
        barrier = pltpu.get_barrier_semaphore()
        peers = [lax.rem(me + k, sources) for k in range(1, sources)]
        for peer in peers:
            pl.semaphore_signal(barrier, inc=1, device_id={"mem": peer}, device_id_type=mesh_type)
        pl.semaphore_signal(barrier, inc=1, device_id={"dp": 1 - core}, device_id_type=mesh_type)
        pl.semaphore_wait(barrier, sources)

        def merge(blocks):
            total = blocks[0][...].astype(jnp.float32)
            for block in blocks[1:]:
                total = total + block[...].astype(jnp.float32)
            return total

        def pack(target, total):
            target[...] = total.astype(jnp.bfloat16)

        def across_cores(source, target, i):
            copy = pltpu.make_async_remote_copy(
                src_ref=source,
                dst_ref=target,
                send_sem=core_send.at[i],
                recv_sem=core_recv.at[i],
                device_id={"dp": 1 - core},
                device_id_type=mesh_type,
            )
            copy.start()
            return copy

        pair_copies = exchange_pairs([left_ref], [right_ref], other_left, other_right, pair_send, pair_recv)
        smalls[me] = small_ref[...]
        small_copies = [
            remote(small_ref, smalls.at[me], small_send.at[i], small_recv.at[me], peer)
            for i, peer in enumerate(peers)
        ]
        for copy in small_copies:
            copy.start()
        for copy in pair_copies:
            copy.wait_recv()

        def store(column, value):
            parts[:, column : column + value.shape[1]] = value

        pair_products([left_ref], [right_ref], other_left, other_right, turned, store)
        early_copy = across_cores(early_ref, both.at[core], 0)
        both[core] = early_ref[...]
        final, still_open = reduce_steps(parts, sources, steps_refs, steps_sems, merge, pack)
        for here, blocks in final:
            late[core, here] = merge(blocks).astype(jnp.bfloat16)
        late_copy = across_cores(late.at[core], late.at[core], 2)
        for peer in peers:
            remote(
                smalls.at[peer], smalls.at[peer], small_send.at[0], small_recv.at[peer], peer
            ).wait_recv()
        group_small = smalls[0]
        for i in range(1, sources):
            group_small = group_small + smalls[i]
        core_small[0] = group_small
        small_copy = across_cores(core_small.at[0], core_small.at[1], 1)
        early_copy.wait()
        at = 0
        for out, size in zip(early_outs, early_widths):
            half = size // 2
            for c in (0, 1):
                out[:, c * half : (c + 1) * half] = both[c, :, at : at + half].astype(jnp.float32)
            at += half
        for copy in (late_copy, small_copy):
            copy.wait()
        for c in (0, 1):
            late_out[:, c * total : (c + 1) * total] = late[c].astype(jnp.float32)
        small_out[...] = core_small[0] + core_small[1]
        for copy in still_open + small_copies + pair_copies:
            copy.wait_send()

    vmem = pl.BlockSpec(memory_space=pltpu.VMEM)
    return pl.pallas_call(
        kernel,
        in_specs=[vmem] * 4,
        out_specs=[vmem] * outs,
        out_shape=[jax.ShapeDtypeStruct((rows, size), jnp.float32) for size in (2 * total, *early_widths)]
        + [jax.ShapeDtypeStruct(small.shape, small.dtype)],
        scratch_shapes=ref_shapes
        + sem_shapes
        + pair_shapes
        + [
            pltpu.VMEM((width, total), jnp.bfloat16),
            pltpu.VMEM((2, rows, total), jnp.bfloat16),
            pltpu.VMEM((2, *early.shape), early.dtype),
            pltpu.VMEM((sources, *small.shape), small.dtype),
            pltpu.VMEM((2, *small.shape), small.dtype),
        ]
        + [pltpu.SemaphoreType.DMA((sources,))] * 2
        + [pltpu.SemaphoreType.DMA((3,))] * 2,
        compiler_params=pltpu.CompilerParams(
            collective_id=collective_id, has_side_effects=True, vmem_limit_bytes=VMEM_LIMIT
        ),
        cost_estimate=lasting(45),
        name="finish_grads",
    )(left, right, early, small)


def on_device(
    tokens,
    attn_gain,
    qkv_weight,
    out_weight,
    bias_table,
    gate_logit,
    ffn_gain,
    up_weight,
    down_weight,
    memory_keys,
    memory_values,
    book_lengths,
    slot_shard,
    slot_index,
    slot_live,
    cotangent,
):
    rows, width = tokens.shape
    heads, buckets = bias_table.shape
    head_dim = width // heads
    top_count = slot_index.shape[2]
    hidden = up_weight.shape[1]
    groups = lax.axis_size("mem")
    capacity = -(-3 * rows * heads * top_count // (2 * groups) // 128) * 128
    score_scale = 1.0 / math.sqrt(head_dim)
    repeats = W // rows
    span = W + 2 * rows
    me = lax.axis_index("mem")
    first_pos = me * rows
    lengths = book_lengths[0]
    window = jnp.arange(W + rows, dtype=jnp.int32)
    key_pos = first_pos - W + window
    key_book = jnp.where(key_pos >= 0, book_of(key_pos, lengths), -1)
    later_book = book_of(first_pos + window, lengths)
    own_book = jnp.broadcast_to(later_book[:rows, None], (rows, 128))
    key_book = jnp.broadcast_to(key_book[None, :], (8, W + rows))
    later_book = jnp.broadcast_to(later_book[None, :], (8, W + rows))
    bucket = bucket_of(jnp.arange(W, dtype=jnp.int32))
    one_hot = (bucket[:, None] == jnp.arange(buckets, dtype=jnp.int32)).astype(jnp.float32)
    offset_bias = jnp.einsum("rb,hb->hr", one_hot, bias_table, precision=lax.Precision.HIGHEST)
    after_bias = jnp.pad(offset_bias, ((0, 0), (0, span - W)), constant_values=masked_score)
    before_bias = jnp.pad(
        offset_bias[:, ::-1], ((0, 0), (1, span - W - 1)), constant_values=masked_score
    )
    tokens_f = tokens.astype(jnp.float32)
    normed_f, norm_in_back = jax.vjp(normed, tokens_f, attn_gain)
    normed_in = normed_f.astype(jnp.bfloat16)
    projected = jnp.dot(normed_in, qkv_weight, preferred_element_type=jnp.float32).astype(
        jnp.bfloat16
    )
    slots = memory_keys.shape[0]
    requests = place_requests(slot_shard, slot_index, slot_live, groups, capacity, slots)
    incoming = lax.all_to_all(requests, "mem", split_axis=0, concat_axis=0, tiled=True)
    keys_values, _ = lax.optimization_barrier((projected[:, width:], requests))
    halos = [passed_along(keys_values, "mem", distance) for distance in range(repeats, 0, -1)]
    row_ids = incoming // slots
    limits = jnp.arange(heads + 1, dtype=jnp.int32) * (rows * slots)
    bounds = jnp.sum((incoming[:, None] < limits[None, :, None, None]).astype(jnp.int32), axis=(2, 3))
    index = jnp.where(row_ids < heads * rows, row_ids // rows * slots + incoming % slots, 0)
    padded_ids = jnp.pad(row_ids, ((0, 0), (0, 1), (0, 0)), constant_values=heads * rows)
    key_rows, value_rows = gather_rows(
        index.reshape(-1), bounds[:, heads], memory_keys, memory_values, heads, groups, capacity
    )
    all_queries = lax.all_gather(projected[:, :width], "mem", axis=0, tiled=True)
    local_out, local_log = local_forward(
        before_bias, own_book, key_book, projected, halos, heads, score_scale
    )
    partial = memory_forward(
        bounds.reshape(-1),
        all_queries,
        key_rows,
        value_rows,
        padded_ids,
        heads,
        groups,
        rows,
        score_scale,
    )
    if groups == 16:
        memory_out, mem_log = merge_partials(partial, groups, 1, heads)
    else:
        partial = lax.all_to_all(
            partial.reshape(groups, rows, width + 128),
            "mem",
            split_axis=0,
            concat_axis=0,
            tiled=True,
        ).reshape(groups * rows, width + 128)
        memory_out, mem_log = combine_partials(partial, heads, groups, rows)
    gate_share = jax.nn.sigmoid(gate_logit)
    share_wide = jnp.repeat(gate_share, head_dim)[None, :]
    mixed_heads = (share_wide * memory_out + (1.0 - share_wide) * local_out).astype(jnp.bfloat16)
    residual = tokens_f + jnp.dot(mixed_heads, out_weight, preferred_element_type=jnp.float32)
    normed_mid_f, norm_mid_back = jax.vjp(normed, residual, ffn_gain)
    normed_mid = normed_mid_f.astype(jnp.bfloat16)
    activated, d_up, ffn_branch, d_mid = feed_forward(normed_mid, cotangent, up_weight, down_weight)
    block_out = (residual + ffn_branch).astype(jnp.bfloat16)
    d_resid_part, ffn_gain_part = norm_mid_back(d_mid)
    d_residual = cotangent.astype(jnp.float32) + d_resid_part
    d_branch = d_residual.astype(jnp.bfloat16)
    d_mixed = lax.dot_general(
        d_branch, out_weight, contract_cols, preferred_element_type=jnp.float32
    )
    early_halves = pair_grads(
        [mixed_heads, normed_mid, cotangent], [d_branch, d_up, activated], 5
    )
    d_queries, diagonals, gate_products, sent_grads = local_queries(
        before_bias,
        own_book,
        key_book,
        projected,
        halos,
        d_mixed,
        memory_out,
        local_out,
        mem_log,
        local_log,
        gate_share,
        heads,
        score_scale,
    )
    gate_part = jnp.sum(gate_products, axis=1) * gate_share * (1.0 - gate_share)
    bias_part = jnp.dot(diagonals[:, rows - 1 : rows - 1 + W], one_hot, precision=lax.Precision.HIGHEST)
    sent_grads, early_halves = lax.optimization_barrier((sent_grads, early_halves))
    early_sums = scattered(early_halves)
    if groups == 16:
        all_grads = gather_group(sent_grads, groups, 2)
    else:
        all_grads = lax.all_gather(sent_grads, "mem", axis=0, tiled=True)
    d_partial = memory_backward(
        bounds.reshape(-1),
        all_queries,
        all_grads,
        key_rows,
        value_rows,
        padded_ids,
        heads,
        groups,
        rows,
        score_scale,
    )
    d_keys_values = local_keys(
        after_bias,
        own_book,
        later_book,
        projected,
        all_queries,
        all_grads,
        (1.0 - gate_share) / gate_share,
        me[None],
        repeats + 1,
        heads,
        score_scale,
    )
    if groups == 16:
        d_partial = sum_blocks(d_partial, groups, 3)
    else:
        d_partial, d_keys_values = lax.optimization_barrier((d_partial, d_keys_values))
        d_partial = jnp.sum(
            lax.all_to_all(
                d_partial.reshape(groups, rows, width), "mem", split_axis=0, concat_axis=0, tiled=True
            ).astype(jnp.float32),
            axis=0,
        )
    d_queries = (d_queries + d_partial * score_scale).astype(jnp.bfloat16)
    d_projected = jnp.concatenate([d_queries, d_keys_values], axis=1)
    d_in = lax.dot_general(
        d_projected, qkv_weight, contract_cols, preferred_element_type=jnp.float32
    )
    d_tokens_part, attn_gain_part = norm_in_back(d_in)
    tokens_grad = d_residual + d_tokens_part
    small = jnp.concatenate(
        [attn_gain_part, ffn_gain_part, bias_part.reshape(-1), gate_part], axis=0
    )
    small = jnp.pad(small, (0, -small.shape[0] % 1024)).reshape(-1, 128)
    early_widths = [width, hidden, hidden]
    if groups == 16:
        qkv_grad, out_grad, up_grad, down_grad, small = finish_grads(
            normed_in, d_projected, early_sums, early_widths, small, groups, 4
        )
    else:
        late_halves = pair_grads([normed_in], [d_projected], 6)
        late_halves, early_sums = lax.optimization_barrier((late_halves, early_sums))
        late_both = lax.all_gather(scattered(late_halves), "dp", axis=0)
        early_both = lax.all_gather(early_sums, "dp", axis=0)
        small = lax.psum(small, ("dp", "mem"))
        out_grad, up_grad, down_grad = whole_grads(early_both, early_widths)
        qkv_grad = whole_grads(late_both, [3 * width])[0]
    small = small.reshape(-1)
    at_bias = 2 * width + heads * buckets
    return (
        block_out,
        tokens_grad,
        qkv_grad,
        out_grad,
        up_grad,
        down_grad,
        small[:width],
        small[width : 2 * width],
        small[2 * width : at_bias].reshape(heads, buckets),
        small[at_bias : at_bias + heads],
    )


def solution(mesh):
    in_specs = (
        P(("dp", "mem"), None),
        P(),
        P(),
        P(),
        P(),
        P(),
        P(),
        P(),
        P(),
        P("mem", None),
        P("mem", None),
        P("dp", None),
        P(("dp", "mem"), None, None, None),
        P(("dp", "mem"), None, None),
        P(("dp", "mem"), None, None),
        P(("dp", "mem"), None),
    )
    out_specs = (
        P(("dp", "mem"), None),
        P(("dp", "mem"), None),
        P("mem", None),
        P("mem", None),
        P("mem", None),
        P("mem", None),
        P(),
        P(),
        P(),
        P(),
    )
    return jax.shard_map(
        on_device, mesh=mesh, in_specs=in_specs, out_specs=out_specs, check_vma=False
    )
```

```python
import math

import jax
import jax.numpy as jnp
from jax import lax
from jax.experimental import pallas as pl
from jax.experimental.pallas import tpu as pltpu
from jax.sharding import PartitionSpec as P

W = 512
VMEM_LIMIT = 56 * 1024 * 1024


eps_norm = 1e-06
bucket_edges = tuple((math.ceil(16 * 8 ** (edge_step / 16)) for edge_step in range(1, 16)))
masked_score = -1e30
dead_score = -10000.0
contract_rows = (((0,), (0,)), ((), ()))
contract_cols = (((1,), (1,)), ((), ()))


def passed_along(value, axis, by):
    size = lax.axis_size(axis)
    pairs = [(i, i + by) for i in range(size) if 0 <= i + by < size]
    return lax.ppermute(value, axis, pairs)


def bucket_of(offset):
    past_edges = sum(((offset >= edge_pos).astype(jnp.int32) for edge_pos in bucket_edges))
    return jnp.where(offset < 16, offset, 16 + past_edges)


def normed(values, gain_vec):
    return (
        values * lax.rsqrt(jnp.mean(values * values, axis=-1, keepdims=True) + eps_norm) * gain_vec
    )


def book_of(positions, lengths):
    book_ends = jnp.cumsum(lengths, dtype=jnp.int32)
    return jnp.sum((positions[..., None] >= book_ends).astype(jnp.int32), axis=-1)


def place_requests(slot_shard, slot_index, slot_live, owners, capacity, slots):
    rows, heads, top_count = slot_index.shape
    entries = rows * heads * top_count
    row_of = (
        jnp.arange(heads, dtype=jnp.int32)[None, :] * rows
        + jnp.arange(rows, dtype=jnp.int32)[:, None]
    )
    place = row_of[:, :, None] * top_count + jnp.arange(top_count, dtype=jnp.int32)
    owner = jnp.where(slot_live > 0, slot_shard[..., 0], owners)
    keys, picked = lax.sort(
        ((owner * entries + place).reshape(-1), slot_index.reshape(-1)), num_keys=1
    )
    ends = jnp.sum(
        (keys[None, :] < (jnp.arange(owners, dtype=jnp.int32) + 1)[:, None] * entries).astype(jnp.int32),
        axis=1,
    )
    starts = jnp.concatenate([jnp.zeros((1,), jnp.int32), ends[:-1]])
    codes = keys % entries // top_count * slots + picked
    tall = -(-entries // 128)
    codes = jnp.pad(codes, (0, tall * 128 - entries)).reshape(tall, 128)
    long = capacity // 128
    empty = heads * rows * slots

    def kernel(starts_ref, ends_ref, codes_ref, lists_ref, padded):
        padded[:tall, :] = codes_ref[...]
        padded[tall:, :] = jnp.zeros((long + 8, 128), jnp.int32)
        lane = lax.broadcasted_iota(jnp.int32, (long, 128), 1)
        place = lax.broadcasted_iota(jnp.int32, (long, 128), 0) * 128 + lane

        @pl.loop(0, owners)
        def _(i):
            start, end = starts_ref[i], ends_ref[i]
            shift = start % 128
            lines = padded[pl.ds(start // 128, long + 1), :]
            turned = pltpu.roll(lines, (128 - shift) % 128, 1)
            joined = jnp.where(lane < 128 - shift, turned[:long], turned[1:])
            lists_ref[i] = jnp.where(place < end - start, joined, empty)

    return pl.pallas_call(
        kernel,
        in_specs=[pl.BlockSpec(memory_space=pltpu.SMEM)] * 2 + [pl.BlockSpec(memory_space=pltpu.VMEM)],
        out_shape=jax.ShapeDtypeStruct((owners, long, 128), jnp.int32),
        scratch_shapes=[pltpu.VMEM((tall + long + 8, 128), jnp.int32)],
        cost_estimate=lasting(3),
        name="make_lists",
    )(starts, ends, codes)


def gather_rows(index, counts, memory_keys, memory_values, heads, sources, capacity):
    slots, width = memory_keys.shape
    head_dim = width // heads
    step, part = 128, 16

    def kernel(index_ref, counts_ref, keys, values, out_keys, out_values, key_table, value_table, key_rows, value_rows):
        i = pl.program_id(0)

        @pl.when(i < heads)
        def _():
            place = pl.ds(pl.multiple_of(i * slots, slots), slots)
            key_table[place, :] = keys[...].astype(jnp.float32)
            value_table[place, :] = values[...].astype(jnp.float32)

        @pl.when(i >= heads)
        def _():
            source = i - heads

            used = (counts_ref[source] + step - 1) // step

            def store(group):
                for at in range(0, step, part):
                    here = pl.ds(pl.multiple_of(group * step, step) + at, part)
                    out_keys[here, :] = key_rows[at : at + part, :].astype(jnp.bfloat16)
                    out_values[here, :] = value_rows[at : at + part, :].astype(jnp.bfloat16)

            @pl.loop(0, used)
            def _(group):
                store(jnp.maximum(group - 1, 0))
                first = source * capacity + group * step
                for u in range(step):
                    row = index_ref[first + u]
                    key_rows[u : u + 1, :] = key_table[pl.ds(row, 1), :]
                    value_rows[u : u + 1, :] = value_table[pl.ds(row, 1), :]

            pl.when(used > 0)(lambda: store(used - 1))

            @pl.loop(used, capacity // step)
            def _(group):
                here = pl.ds(pl.multiple_of(group * step, step), step)
                out_keys[here, :] = jnp.zeros((step, head_dim), jnp.bfloat16)
                out_values[here, :] = jnp.zeros((step, head_dim), jnp.bfloat16)

    table_spec = pl.BlockSpec((slots, head_dim), lambda i, *_: (0, jnp.minimum(i, heads - 1)))
    out_spec = pl.BlockSpec((capacity, head_dim), lambda i, *_: (jnp.maximum(i - heads, 0), 0))
    out_shape = jax.ShapeDtypeStruct((sources * capacity, head_dim), jnp.bfloat16)
    return pl.pallas_call(
        kernel,
        grid_spec=pltpu.PrefetchScalarGridSpec(
            num_scalar_prefetch=2,
            grid=(heads + sources,),
            in_specs=[table_spec, table_spec],
            out_specs=[out_spec, out_spec],
            scratch_shapes=[
                pltpu.VMEM((heads * slots, head_dim), jnp.float32),
                pltpu.VMEM((heads * slots, head_dim), jnp.float32),
                pltpu.VMEM((step, head_dim), jnp.float32),
                pltpu.VMEM((step, head_dim), jnp.float32),
            ],
        ),
        out_shape=[out_shape, out_shape],
        compiler_params=pltpu.CompilerParams(vmem_limit_bytes=VMEM_LIMIT),
        cost_estimate=lasting(42),
        name="gather_rows",
    )(index, counts, memory_keys, memory_values)


def lasting(microseconds):
    return pl.CostEstimate(flops=0, bytes_accessed=3_000_000 * microseconds, transcendentals=0)


def triple(stat):
    part = lax.broadcasted_iota(jnp.int32, stat.shape, 1) // 16
    high = stat.astype(jnp.bfloat16).astype(jnp.float32)
    rest = stat - high
    middle = rest.astype(jnp.bfloat16).astype(jnp.float32)
    low = rest - middle
    chosen = jnp.where(part == 0, high, jnp.where(part == 1, middle, jnp.where(part == 2, low, 0.0)))
    return chosen.astype(jnp.bfloat16)


def window_of(bounds, source, head, heads, span, capacity):
    first = bounds[source * (heads + 1) + head]
    last = bounds[source * (heads + 1) + head + 1]
    start = jnp.minimum(first // 16 * 16, capacity - span)
    extra = jnp.maximum(last - start - 1, 0) // span
    return start, extra


def columns_of(head, head_dim):
    if isinstance(head, int):
        return slice(head * head_dim, (head + 1) * head_dim)
    return pl.ds(pl.multiple_of(head * head_dim, head_dim), head_dim)


def window_ids(id_ref, start, span):
    lines = id_ref[0, pl.ds(start // 128, span // 128 + 1), :]
    shift = start % 128
    turned = pltpu.roll(lines, (128 - shift) % 128, 1)
    lane = lax.broadcasted_iota(jnp.int32, (span // 128, 128), 1)
    return jnp.where(lane < 128 - shift, turned[:-1], turned[1:])


def owned(lines, first_row, count, start, least):
    row = lax.broadcasted_iota(jnp.int32, (count, 128), 0) + first_row
    masks = []
    for i in range(lines.shape[0]):
        mask = lines[i : i + 1, :] == row
        if least is not None:
            place = lax.broadcasted_iota(jnp.int32, (1, 128), 1) + start + i * 128
            mask = mask & (place >= least)
        masks.append(mask)
    return jnp.concatenate(masks, axis=1)


def memory_forward(bounds, queries, key_rows, value_rows, row_ids, heads, sources, rows, score_scale):
    capacity, head_dim = key_rows.shape[0] // sources, key_rows.shape[1]
    width = heads * head_dim
    span = min(384, capacity)
    chunk = math.gcd(rows, 32)

    def kernel(bounds_ref, q_ref, k_ref, v_ref, id_ref, out_ref, sums, tops, totals, raw, weights):
        source = pl.program_id(0)
        lane = lax.broadcasted_iota(jnp.int32, (chunk, 128), 1) % 16

        def window(heads_here, starts, least):
            here = [pl.ds(pl.multiple_of(start, 16), span) for start in starts]
            columns = [columns_of(head, head_dim) for head in heads_here]
            for slot in range(len(starts)):
                raw[slot] = lax.dot_general(
                    q_ref[:, columns[slot]],
                    k_ref[here[slot], :],
                    contract_cols,
                    preferred_element_type=jnp.float32,
                )
            for slot, (head, start) in enumerate(zip(heads_here, starts)):
                lines = window_ids(id_ref, start, span)
                for at in range(0, rows, chunk):
                    some = slice(at, at + chunk)
                    mine = owned(lines, head * rows + at, chunk, start, least)
                    scores = jnp.where(mine, raw[slot, some, :], masked_score)
                    top = jnp.maximum(jnp.max(scores, axis=1, keepdims=True), 0.1 * masked_score)
                    if least is not None:
                        old_top = jnp.max(
                            jnp.where(lane == head, tops[some, :], masked_score), axis=1, keepdims=True
                        )
                        top = jnp.maximum(top, old_top)
                    exps = jnp.exp((scores - top) * score_scale)
                    weights[slot, some, :] = exps.astype(jnp.bfloat16)
                    total = jnp.sum(exps, axis=1, keepdims=True)
                    if least is not None:
                        faded = jnp.exp((old_top - top) * score_scale)
                        sums[some, columns[slot]] = sums[some, columns[slot]] * faded
                        total = total + totals[some, :] * faded
                    tops[some, :] = jnp.where(lane == head, top, tops[some, :])
                    totals[some, :] = jnp.where(lane == heads + head, total, totals[some, :])
            for slot in range(len(starts)):
                found = jnp.dot(
                    weights[slot], v_ref[here[slot], :], preferred_element_type=jnp.float32
                )
                sums[:, columns[slot]] = found if least is None else sums[:, columns[slot]] + found

        tops[...] = jnp.zeros_like(tops)
        totals[...] = jnp.zeros_like(totals)

        window(
            list(range(heads)),
            [window_of(bounds_ref, source, head, heads, span, capacity)[0] for head in range(heads)],
            None,
        )

        @pl.loop(0, heads)
        def _(head):
            start, extra = window_of(bounds_ref, source, head, heads, span, capacity)

            @pl.loop(0, extra)
            def _(turn):
                least = start + (turn + 1) * span
                window([head], [jnp.minimum(least, capacity - span)], least)

        out_ref[:, :width] = sums[...].astype(jnp.bfloat16)
        wide = lax.broadcasted_iota(jnp.int32, (rows, 128), 1) % 16
        out_ref[:, width:] = triple(jnp.where(wide < heads, tops[...] * score_scale, totals[...]))

    return pl.pallas_call(
        kernel,
        grid_spec=pltpu.PrefetchScalarGridSpec(
            num_scalar_prefetch=1,
            grid=(sources,),
            in_specs=[
                pl.BlockSpec((rows, width), lambda i, *_: (i, 0)),
                pl.BlockSpec((capacity, head_dim), lambda i, *_: (i, 0)),
                pl.BlockSpec((capacity, head_dim), lambda i, *_: (i, 0)),
                pl.BlockSpec((1, *row_ids.shape[1:]), lambda i, *_: (i, 0, 0)),
            ],
            out_specs=pl.BlockSpec((rows, width + 128), lambda i, *_: (i, 0)),
            scratch_shapes=[
                pltpu.VMEM((rows, width), jnp.float32),
                pltpu.VMEM((rows, 128), jnp.float32),
                pltpu.VMEM((rows, 128), jnp.float32),
                pltpu.VMEM((heads, rows, span), jnp.float32),
                pltpu.VMEM((heads, rows, span), jnp.bfloat16),
            ],
        ),
        out_shape=jax.ShapeDtypeStruct((sources * rows, width + 128), jnp.bfloat16),
        compiler_params=pltpu.CompilerParams(vmem_limit_bytes=VMEM_LIMIT),
        cost_estimate=lasting(25),
        name="memory_forward",
    )(bounds, queries, key_rows, value_rows, row_ids)


def combine_partials(partial, heads, sources, rows):
    width = partial.shape[1] - 128
    head_dim = width // heads

    def kernel(part_ref, out_ref, log_ref, sums, tops, totals):
        i = pl.program_id(0)

        @pl.when(i == 0)
        def _():
            sums[...] = jnp.zeros_like(sums)
            tops[...] = jnp.full_like(tops, masked_score)
            totals[...] = jnp.zeros_like(totals)

        stat = part_ref[:, width:].astype(jnp.float32)
        stat = stat + pltpu.roll(stat, 128 - 16, 1) + pltpu.roll(stat, 128 - 32, 1)
        new_total = pltpu.roll(stat, 128 - heads, 1)
        top = jnp.maximum(tops[...], stat)
        old_fade, new_fade = jnp.exp(tops[...] - top), jnp.exp(stat - top)
        tops[...] = top
        totals[...] = totals[...] * old_fade + new_total * new_fade
        for head in range(heads):
            columns = slice(head * head_dim, (head + 1) * head_dim)
            sums[:, columns] = (
                sums[:, columns] * old_fade[:, head : head + 1]
                + part_ref[:, columns].astype(jnp.float32) * new_fade[:, head : head + 1]
            )

        @pl.when(i == sources - 1)
        def _():
            live = totals[...] > 0
            total = jnp.where(live, totals[...], 1.0)
            log_ref[...] = jnp.where(live, tops[...] + jnp.log(total), 0.0)
            for head in range(heads):
                columns = slice(head * head_dim, (head + 1) * head_dim)
                out_ref[:, columns] = sums[:, columns] / total[:, head : head + 1]

    return pl.pallas_call(
        kernel,
        grid=(sources,),
        in_specs=[pl.BlockSpec((rows, width + 128), lambda i: (i, 0))],
        out_specs=[
            pl.BlockSpec((rows, width), lambda i: (0, 0)),
            pl.BlockSpec((rows, 128), lambda i: (0, 0)),
        ],
        scratch_shapes=[
            pltpu.VMEM((rows, width), jnp.float32),
            pltpu.VMEM((rows, 128), jnp.float32),
            pltpu.VMEM((rows, 128), jnp.float32),
        ],
        out_shape=[
            jax.ShapeDtypeStruct((rows, width), jnp.float32),
            jax.ShapeDtypeStruct((rows, 128), jnp.float32),
        ],
        compiler_params=pltpu.CompilerParams(vmem_limit_bytes=VMEM_LIMIT),
        cost_estimate=lasting(13),
        name="combine_partials",
    )(partial)


def memory_backward(bounds, queries, grads, key_rows, value_rows, row_ids, heads, sources, rows, score_scale):
    capacity, head_dim = key_rows.shape[0] // sources, key_rows.shape[1]
    width = heads * head_dim
    span = min(384, capacity)
    chunk = math.gcd(rows, 32)

    def kernel(bounds_ref, q_ref, g_ref, k_ref, v_ref, id_ref, out_ref, sums, stats, raw, products, slopes):
        source = pl.program_id(0)
        stats[...] = joined_tile(g_ref[:, width : width + 128])

        def window(heads_here, starts, least):
            here = [pl.ds(pl.multiple_of(start, 16), span) for start in starts]
            columns = [columns_of(head, head_dim) for head in heads_here]
            for slot in range(len(starts)):
                raw[slot] = lax.dot_general(
                    q_ref[:, columns[slot]],
                    k_ref[here[slot], :],
                    contract_cols,
                    preferred_element_type=jnp.float32,
                )
                products[slot] = lax.dot_general(
                    g_ref[:, columns[slot]],
                    v_ref[here[slot], :],
                    contract_cols,
                    preferred_element_type=jnp.float32,
                )
            for slot, (head, start) in enumerate(zip(heads_here, starts)):
                lines = window_ids(id_ref, start, span)
                turned = stats[...]
                if least is not None:
                    turned = pltpu.roll(turned, 128 - head, 1)
                elif head:
                    turned = turned[:, head:]
                for at in range(0, rows, chunk):
                    some = slice(at, at + chunk)
                    mine = owned(lines, head * rows + at, chunk, start, least)
                    log, delta = turned[some, :1], turned[some, heads : heads + 1]
                    probs = jnp.exp(jnp.where(mine, raw[slot, some, :] * score_scale - log, dead_score))
                    slopes[slot, some, :] = (probs * (products[slot, some, :] - delta)).astype(
                        jnp.bfloat16
                    )
            for slot in range(len(starts)):
                found = jnp.dot(
                    slopes[slot], k_ref[here[slot], :], preferred_element_type=jnp.float32
                )
                sums[:, columns[slot]] = found if least is None else sums[:, columns[slot]] + found

        window(
            list(range(heads)),
            [window_of(bounds_ref, source, head, heads, span, capacity)[0] for head in range(heads)],
            None,
        )

        @pl.loop(0, heads)
        def _(head):
            start, extra = window_of(bounds_ref, source, head, heads, span, capacity)

            @pl.loop(0, extra)
            def _(turn):
                least = start + (turn + 1) * span
                window([head], [jnp.minimum(least, capacity - span)], least)

        out_ref[...] = sums[...].astype(jnp.bfloat16)

    return pl.pallas_call(
        kernel,
        grid_spec=pltpu.PrefetchScalarGridSpec(
            num_scalar_prefetch=1,
            grid=(sources,),
            in_specs=[
                pl.BlockSpec((rows, width), lambda i, *_: (i, 0)),
                pl.BlockSpec((rows, width + 128), lambda i, *_: (i, 0)),
                pl.BlockSpec((capacity, head_dim), lambda i, *_: (i, 0)),
                pl.BlockSpec((capacity, head_dim), lambda i, *_: (i, 0)),
                pl.BlockSpec((1, *row_ids.shape[1:]), lambda i, *_: (i, 0, 0)),
            ],
            out_specs=pl.BlockSpec((rows, width), lambda i, *_: (i, 0)),
            scratch_shapes=[
                pltpu.VMEM((rows, width), jnp.float32),
                pltpu.VMEM((rows, 128), jnp.float32),
                pltpu.VMEM((heads, rows, span), jnp.float32),
                pltpu.VMEM((heads, rows, span), jnp.float32),
                pltpu.VMEM((heads, rows, span), jnp.bfloat16),
            ],
        ),
        out_shape=jax.ShapeDtypeStruct((sources * rows, width), jnp.bfloat16),
        compiler_params=pltpu.CompilerParams(vmem_limit_bytes=VMEM_LIMIT),
        cost_estimate=lasting(25),
        name="memory_backward",
    )(bounds, queries, grads, key_rows, value_rows, row_ids)


def remote(source, target, send_sem, recv_sem, device):
    return pltpu.make_async_remote_copy(
        src_ref=source,
        dst_ref=target,
        send_sem=send_sem,
        recv_sem=recv_sem,
        device_id={"mem": device},
        device_id_type=pl.DeviceIdType.MESH,
    )


def grid_place(depth):
    me = lax.axis_index("mem")
    layer, column = me // 4, me % 4
    beside_x = column + 1 - 2 * (column % 2)
    beside_y = column + 2 - 4 * (column // 2)
    across = 3 - column

    def index_of(step, place):
        return (layer + step + depth) % depth * 4 + place

    return me, column, beside_x, beside_y, across, index_of


def greet(devices):
    barrier = pltpu.get_barrier_semaphore()
    for device in devices:
        pl.semaphore_signal(
            barrier, inc=1, device_id={"mem": device}, device_id_type=pl.DeviceIdType.MESH
        )
    pl.semaphore_wait(barrier, len(devices))


def gather_group(block, sources, collective_id):
    rows, width = block.shape
    depth, half = sources // 4, rows // 2
    slots = 2 * depth - 1

    def kernel(x_ref, out_ref, own_sem, send, recv):
        me = lax.axis_index("mem")
        layer, column = me // 4, me % 4
        to_x = me + 1 - 2 * (column % 2)
        to_y = me + 2 - 4 * (column // 2)
        across = layer * 4 + 3 - column
        has_above, has_below = layer + 1 < depth, layer > 0
        barrier = pltpu.get_barrier_semaphore()

        def signal(device):
            pl.semaphore_signal(
                barrier, inc=1, device_id={"mem": device}, device_id_type=pl.DeviceIdType.MESH
            )

        signal(to_x)
        signal(to_y)
        pl.when(has_above)(lambda: signal(me + 4))
        pl.when(has_below)(lambda: signal(me - 4))
        pl.semaphore_wait(barrier, 2 + has_above.astype(jnp.int32) + has_below.astype(jnp.int32))

        def part_of(index, part):
            start = pl.multiple_of(index * rows + part * half, half)
            return out_ref.at[pl.ds(start, half), :]

        own = pltpu.make_async_copy(x_ref, out_ref.at[pl.ds(pl.multiple_of(me * rows, rows), rows), :], own_sem)
        own.start()
        sent = []

        def push(condition, source, target, kind, slot, to_slot, part, device):
            copy = remote(source, target, send.at[kind, slot, part], recv.at[kind, to_slot, part], device)
            if condition is None:
                copy.start()
            else:
                pl.when(condition)(copy.start)
            sent.append((condition, copy))

        def arrived(index, kind, slot, part):
            target = part_of(index, part)
            remote(target, target, send.at[kind, slot, part], recv.at[kind, slot, part], to_x).wait_recv()

        def up_slot(distance):
            return distance

        def down_slot(distance):
            return depth - 1 + distance

        for part in (0, 1):
            mine = x_ref.at[pl.ds(part * half, half), :]
            push(has_above, mine, part_of(me, part), 0, 0, down_slot(1), part, me + 4)
            push(has_below, mine, part_of(me, part), 1, 0, up_slot(1), part, me - 4)
            mine_y = x_ref.at[pl.ds((1 - part) * half, half), :]
            push(None, mine, part_of(me, part), 2, 0, 0, part, to_x)
            push(None, mine_y, part_of(me, 1 - part), 3, 0, 0, 1 - part, to_y)

        def pass_on(condition, step, slot):
            def go():
                arrived(to_x + step, 2, slot, 0)
                copy_a.start()
                arrived(to_y + step, 3, slot, 1)
                copy_b.start()

            source_a, source_b = part_of(to_x + step, 0), part_of(to_y + step, 1)
            copy_a = remote(source_a, source_a, send.at[4, slot, 0], recv.at[4, slot, 0], to_y)
            copy_b = remote(source_b, source_b, send.at[5, slot, 1], recv.at[5, slot, 1], to_x)
            sent.append((condition, copy_a))
            sent.append((condition, copy_b))
            if condition is None:
                go()
            else:
                pl.when(condition)(go)

        for distance in range(1, depth):
            from_above, from_below = layer + distance < depth, layer - distance >= 0

            def take(kind, back_kind, step, slot, next_slot, onward, onward_device):
                for part in (0, 1):
                    arrived(me + step, kind, slot, part)
                    here = part_of(me + step, part)
                    if next_slot is not None:
                        pl.when(onward)(
                            remote(
                                here, here, send.at[kind, slot, part], recv.at[kind, next_slot, part], onward_device
                            ).start
                        )
                    remote(here, here, send.at[2, slot, part], recv.at[2, slot, part], to_x).start()
                    remote(here, here, send.at[3, slot, part], recv.at[3, slot, part], to_y).start()

            last = distance == depth - 1
            pl.when(from_above)(
                lambda: take(
                    1, 0, 4 * distance, up_slot(distance), None if last else up_slot(distance + 1), has_below, me - 4
                )
            )
            pl.when(from_below)(
                lambda: take(
                    0, 1, -4 * distance, down_slot(distance), None if last else down_slot(distance + 1), has_above, me + 4
                )
            )
            for condition, step, slot, kind, onward in (
                (from_above, 4 * distance, up_slot(distance), 1, has_below),
                (from_below, -4 * distance, down_slot(distance), 0, has_above),
            ):
                for part in (0, 1):
                    here = part_of(me + step, part)
                    if not last:
                        sent.append((condition & onward, remote(here, here, send.at[kind, slot, part], own_sem, me)))
                    sent.append((condition, remote(here, here, send.at[2, slot, part], own_sem, to_x)))
                    sent.append((condition, remote(here, here, send.at[3, slot, part], own_sem, to_y)))
            if distance == 1:
                pass_on(None, 0, 0)
            else:
                pass_on(layer + distance - 1 < depth, 4 * (distance - 1), up_slot(distance - 1))
                pass_on(layer - distance + 1 >= 0, -4 * (distance - 1), down_slot(distance - 1))
        pass_on(layer + depth - 1 < depth, 4 * (depth - 1), up_slot(depth - 1))
        pass_on(layer - depth + 1 >= 0, -4 * (depth - 1), down_slot(depth - 1))

        def close(step, slot):
            arrived(to_x + step, 2, slot, 1)
            arrived(to_y + step, 3, slot, 0)
            arrived(across + step, 4, slot, 0)
            arrived(across + step, 5, slot, 1)

        close(0, 0)
        for distance in range(1, depth):
            pl.when(layer + distance < depth)(lambda: close(4 * distance, up_slot(distance)))
            pl.when(layer - distance >= 0)(lambda: close(-4 * distance, down_slot(distance)))
        for condition, copy in sent:
            if condition is None:
                copy.wait_send()
            else:
                pl.when(condition)(copy.wait_send)
        own.wait()

    return pl.pallas_call(
        kernel,
        in_specs=[pl.BlockSpec(memory_space=pl.ANY)],
        out_specs=pl.BlockSpec(memory_space=pl.ANY),
        out_shape=jax.ShapeDtypeStruct((sources * rows, width), block.dtype),
        scratch_shapes=[
            pltpu.SemaphoreType.DMA,
            pltpu.SemaphoreType.DMA((6, slots, 2)),
            pltpu.SemaphoreType.DMA((6, slots, 2)),
        ],
        compiler_params=pltpu.CompilerParams(
            collective_id=collective_id, has_side_effects=True, vmem_limit_bytes=VMEM_LIMIT
        ),
        cost_estimate=lasting(50),
        name="gather_group",
    )(block)


def reduce_steps(parts_ref, sources, refs, sems, merge, pack, beside=None):
    half_a, half_b, from_x, from_y, from_z, out_x, out_y, out_z = refs
    send, recv_a, recv_b, recv_x, recv_y, recv_z = sems
    rows = parts_ref.shape[0] // sources
    depth, half = sources // 4, rows // 2
    me, column, beside_x, beside_y, across, index_of = grid_place(depth)
    to_x, to_y = index_of(0, beside_x), index_of(0, beside_y)
    order = [*range(1, depth), 0]
    queues = {"x": [], "y": [], "z": []}
    first_limit = 2 if beside is None else depth

    def piece(index, part):
        return parts_ref.at[pl.ds(pl.multiple_of(index * rows + part * half, half), half), :]

    def part_rows(part):
        return pl.ds(part * half, half)

    def push(link, source, target, kind, k, recv_sem, device, limit=2):
        queue = queues[link]
        while link != "z" and len(queue) >= limit:
            queue.pop(0).wait_send()
        copy = remote(source, target, send.at[kind, k], recv_sem, device)
        copy.start()
        queue.append(copy)

    def arrived(target, recv_sem):
        remote(target, target, send.at[0, 0], recv_sem, to_x).wait_recv()

    def plane_rest(k):
        push("x", piece(index_of(k, beside_x), 0), from_x.at[k, part_rows(0)], 2, k, recv_x.at[0, k], to_x)
        push("y", piece(index_of(k, beside_y), 1), from_y.at[k, part_rows(1)], 3, k, recv_y.at[1, k], to_y)

    def plane_merged(k):
        arrived(half_a.at[k], recv_a.at[k])
        pack(out_y.at[k], merge([piece(index_of(k, beside_y), 0), half_a.at[k]]))
        push("y", out_y.at[k], from_y.at[k, part_rows(0)], 4, k, recv_y.at[0, k], to_y)
        arrived(half_b.at[k], recv_b.at[k])
        pack(out_x.at[k], merge([piece(index_of(k, beside_x), 1), half_b.at[k]]))
        push("x", out_x.at[k], from_x.at[k, part_rows(1)], 5, k, recv_x.at[1, k], to_x)

    def column_step(k):
        for part in (0, 1):
            here = part_rows(part)
            arrived(from_x.at[k, here], recv_x.at[part, k])
            arrived(from_y.at[k, here], recv_y.at[part, k])
            if k:
                blocks = [piece(index_of(k, column), part), from_x.at[k, here], from_y.at[k, here]]
                pack(out_z.at[k, here], merge(blocks))
        if k:
            push("z", out_z.at[k], from_z.at[k], 6, k, recv_z.at[k], index_of(k, column))

    for k in order:
        far = index_of(k, across)
        push("x", piece(far, 0), half_a.at[k], 0, k, recv_a.at[k], to_x, first_limit)
        push("y", piece(far, 1), half_b.at[k], 1, k, recv_b.at[k], to_y, first_limit)
    if beside is not None:
        beside()
    for i, k in enumerate(order):
        plane_rest(k)
        plane_merged(k)
        if i:
            column_step(order[i - 1])
    column_step(order[-1])
    for k in range(1, depth):
        arrived(from_z.at[k], recv_z.at[k])
    final = []
    for part in (0, 1):
        here = part_rows(part)
        blocks = [piece(me, part), from_x.at[0, here], from_y.at[0, here]]
        final.append((here, blocks + [from_z.at[k, here] for k in range(1, depth)]))
    return final, [copy for queue in queues.values() for copy in queue]


def reduce_scratch(rows, width, dtype, sources):
    depth, half = sources // 4, rows // 2

    def slots(size):
        return pltpu.VMEM((depth, size, width), dtype)

    refs = [slots(half), slots(half), slots(rows), slots(rows), slots(rows)]
    refs += [slots(half), slots(half), slots(rows)]
    sems = [pltpu.SemaphoreType.DMA((7, depth))]
    sems += [pltpu.SemaphoreType.DMA((depth,))] * 2
    sems += [pltpu.SemaphoreType.DMA((2, depth))] * 2
    sems += [pltpu.SemaphoreType.DMA((depth,))]
    return refs, sems


def run_alone(name, beside):
    arrays, specs, out_shape, scratch, begin = beside
    ins, outs = len(arrays), len(out_shape)

    def kernel(*refs):
        begin(refs[:ins], refs[ins : ins + outs], refs[ins + outs :])()

    return pl.pallas_call(
        kernel,
        in_specs=specs,
        out_specs=[pl.BlockSpec(memory_space=pltpu.VMEM)] * outs,
        out_shape=out_shape,
        scratch_shapes=scratch,
        compiler_params=pltpu.CompilerParams(vmem_limit_bytes=VMEM_LIMIT),
        cost_estimate=lasting(8),
        name=name,
    )(*arrays)


def reduce_group(parts, sources, collective_id, merge, pack, finish, out_shape, beside):
    rows, width = parts.shape[0] // sources, parts.shape[1]
    depth = sources // 4
    arrays, specs, more_out, more_scratch, begin = beside
    ref_shapes, sem_shapes = reduce_scratch(rows, width, parts.dtype, sources)
    sizes = [len(arrays), len(out_shape), len(more_out), len(ref_shapes), len(sem_shapes), len(more_scratch)]

    def kernel(parts_ref, *refs):
        groups, at = [], 0
        for size in sizes:
            groups.append(refs[at : at + size])
            at += size
        ins, out_refs, more_refs, steps_refs, steps_sems, scratch = groups
        meanwhile = begin(ins, more_refs, scratch)
        me, column, beside_x, beside_y, across, index_of = grid_place(depth)
        greet(
            [index_of(0, beside_x), index_of(0, beside_y)]
            + [index_of(-k, column) for k in range(1, depth)]
        )
        final, still_open = reduce_steps(
            parts_ref, sources, steps_refs, steps_sems, merge, pack, meanwhile
        )
        for here, blocks in final:
            finish([out.at[here] for out in out_refs], merge(blocks))
        for copy in still_open:
            copy.wait_send()

    vmem = pl.BlockSpec(memory_space=pltpu.VMEM)
    return pl.pallas_call(
        kernel,
        in_specs=[vmem, *specs],
        out_specs=[vmem] * (len(out_shape) + len(more_out)),
        out_shape=[*out_shape, *more_out],
        scratch_shapes=[*ref_shapes, *sem_shapes, *more_scratch],
        compiler_params=pltpu.CompilerParams(
            collective_id=collective_id, has_side_effects=True, vmem_limit_bytes=VMEM_LIMIT
        ),
        cost_estimate=lasting(50),
        name="reduce_group",
    )(parts, *arrays)


def sum_blocks(parts, sources, collective_id, beside):
    rows, width = parts.shape[0] // sources, parts.shape[1]

    def merge(blocks):
        total = blocks[0][...].astype(jnp.float32)
        for block in blocks[1:]:
            total = total + block[...].astype(jnp.float32)
        return total

    def pack(target, total):
        target[...] = total.astype(parts.dtype)

    def finish(targets, total):
        targets[0][...] = total

    out_shape = [jax.ShapeDtypeStruct((rows, width), jnp.float32)]
    return reduce_group(parts, sources, collective_id, merge, pack, finish, out_shape, beside)


def merge_partials(parts, sources, collective_id, heads, beside):
    rows, width = parts.shape[0] // sources, parts.shape[1] - 128
    head_dim = width // heads

    def merge(blocks):
        stats = []
        for block in blocks:
            stat = block[:, width:].astype(jnp.float32)
            stats.append(stat + pltpu.roll(stat, 128 - 16, 1) + pltpu.roll(stat, 128 - 32, 1))
        top = stats[0]
        for stat in stats[1:]:
            top = jnp.maximum(top, stat)
        fades = [jnp.exp(stat - top) for stat in stats]
        total = sum(fade * pltpu.roll(stat, 128 - heads, 1) for fade, stat in zip(fades, stats))
        sums = []
        for head in range(heads):
            columns = slice(head * head_dim, (head + 1) * head_dim)
            sums.append(
                sum(
                    block[:, columns].astype(jnp.float32) * fade[:, head : head + 1]
                    for block, fade in zip(blocks, fades)
                )
            )
        return sums, top, total

    def pack(target, merged):
        sums, top, total = merged
        for head in range(heads):
            target[:, head * head_dim : (head + 1) * head_dim] = sums[head].astype(parts.dtype)
        lane = lax.broadcasted_iota(jnp.int32, top.shape, 1)
        stat = jnp.where(lane < heads, top, jnp.where(lane < 16, pltpu.roll(total, heads, 1), 0.0))
        target[:, width:] = triple(stat + pltpu.roll(stat, 16, 1) + pltpu.roll(stat, 32, 1))

    def finish(targets, merged):
        sums, top, total = merged
        live = total > 0
        total = jnp.where(live, total, 1.0)
        targets[1][...] = jnp.where(live, top + jnp.log(total), 0.0)
        for head in range(heads):
            targets[0][:, head * head_dim : (head + 1) * head_dim] = sums[head] / total[:, head : head + 1]

    out_shape = [
        jax.ShapeDtypeStruct((rows, width), jnp.float32),
        jax.ShapeDtypeStruct((rows, 128), jnp.float32),
    ]
    return reduce_group(parts, sources, collective_id, merge, pack, finish, out_shape, beside)


def scattered(halves):
    return lax.psum_scatter(halves, "mem", scatter_dimension=0, tiled=True)


def whole_grads(both, widths):
    both = both.astype(jnp.float32)
    grads, at = [], 0
    for size in widths:
        half = size // 2
        grads.append(jnp.concatenate([both[0, :, at : at + half], both[1, :, at : at + half]], 1))
        at += half
    return grads


def lane_tile(columns, rows):
    lane = lax.broadcasted_iota(jnp.int32, (rows, 128), 1)
    tile = jnp.zeros((rows, 128), jnp.float32)
    for i, column in enumerate(columns):
        tile = jnp.where(lane == i, column, tile)
    return tile


def split_tile(tile):
    lane = lax.broadcasted_iota(jnp.int32, tile.shape, 1)
    kept = jnp.where(lane < 32, tile, 0.0)
    kept = kept + pltpu.roll(kept, 32, 1) + pltpu.roll(kept, 64, 1)
    high = kept.astype(jnp.bfloat16).astype(jnp.float32)
    middle = (kept - high).astype(jnp.bfloat16).astype(jnp.float32)
    low = kept - high - middle
    part = lane // 32
    return jnp.where(part == 0, high, jnp.where(part == 1, middle, low)).astype(jnp.bfloat16)


def joined_tile(tile):
    tile = tile.astype(jnp.float32)
    return tile + pltpu.roll(tile, 128 - 32, 1) + pltpu.roll(tile, 128 - 64, 1)


def slanted(base, rows):
    return pltpu.roll(jnp.broadcast_to(base, (rows, base.shape[1])), 0, 1, stride=1, stride_axis=0)


def local_forward(base, book_column, book_row, own, halos, heads, score_scale):
    rows, width = own.shape[0], own.shape[1] // 3
    head_dim = width // heads
    count = len(halos) + 1

    def begin(ins, outs, scratch):
        base_ref, column_ref, row_ref, own_ref, *halo_refs = ins
        out_ref, log_ref = outs

        def run():
            same = column_ref[:, :1] == row_ref[:1, :]
            logs = []
            for head in range(heads):
                columns = slice(head * head_dim, (head + 1) * head_dim)
                above = slice(width + head * head_dim, width + (head + 1) * head_dim)
                twice = slice(2 * width + head * head_dim, 2 * width + (head + 1) * head_dim)
                keys = [ref[:, columns] for ref in halo_refs] + [own_ref[:, above]]
                values = [ref[:, above] for ref in halo_refs] + [own_ref[:, twice]]
                q = own_ref[:, columns]
                raw = [
                    lax.dot_general(q, k, contract_cols, preferred_element_type=jnp.float32) for k in keys
                ]
                bias = slanted(base_ref[head : head + 1, :], rows)[:, : count * rows]
                scores = jnp.concatenate(raw, axis=1) * score_scale + bias
                scores = jnp.where(same, scores, masked_score)
                top = jnp.max(scores, axis=1, keepdims=True)
                weights = jnp.exp(scores - top)
                total = jnp.sum(weights, axis=1, keepdims=True)
                weights = (weights / total).astype(jnp.bfloat16)
                out_ref[:, columns] = sum(
                    jnp.dot(
                        weights[:, i * rows : (i + 1) * rows], v, preferred_element_type=jnp.float32
                    )
                    for i, v in enumerate(values)
                )
                logs.append(top + jnp.log(total))
            log_ref[...] = lane_tile(logs, rows)

        return run

    arrays = [base, book_column, book_row, own, *halos]
    specs = [pl.BlockSpec(memory_space=pltpu.VMEM)] * len(arrays)
    out_shape = [
        jax.ShapeDtypeStruct((rows, width), jnp.float32),
        jax.ShapeDtypeStruct((rows, 128), jnp.float32),
    ]
    return arrays, specs, out_shape, [], begin


def local_queries(
    base, book_column, book_row, own, halos, d_mixed, memory_out, local_out, mem_log, local_log, share, heads, score_scale
):
    rows, width = d_mixed.shape
    head_dim = width // heads
    count = len(halos) + 1
    span = base.shape[1]

    def kernel(
        base_ref, column_ref, row_ref, own_ref, mix_ref, mem_ref, loc_ref, mem_log_ref, log_ref, share_ref, *refs
    ):
        halo_refs, (dq_ref, diagonal_ref, gate_ref, sent_ref) = refs[: count - 1], refs[count - 1 :]
        same = column_ref[:, :1] == row_ref[:1, :]
        turned = (
            lax.broadcasted_iota(jnp.int32, (rows, rows), 0)
            + lax.broadcasted_iota(jnp.int32, (rows, rows), 1)
            == rows - 1
        ).astype(jnp.bfloat16)
        mem_deltas, deltas = [], []
        for head in range(heads):
            columns = slice(head * head_dim, (head + 1) * head_dim)
            above = slice(width + head * head_dim, width + (head + 1) * head_dim)
            twice = slice(2 * width + head * head_dim, 2 * width + (head + 1) * head_dim)
            keys = [ref[:, columns] for ref in halo_refs] + [own_ref[:, above]]
            values = [ref[:, above] for ref in halo_refs] + [own_ref[:, twice]]
            q = own_ref[:, columns]
            share_here = share_ref[head]
            d_mix, mem_here, loc_here = mix_ref[:, columns], mem_ref[:, columns], loc_ref[:, columns]
            d_mem = (share_here * d_mix).astype(jnp.bfloat16)
            d_out = ((1.0 - share_here) * d_mix).astype(jnp.bfloat16)
            sent_ref[:, columns] = d_mem
            mem_deltas.append(
                jnp.sum(d_mem.astype(jnp.float32) * mem_here, axis=1, keepdims=True)
            )
            delta = jnp.sum(d_out.astype(jnp.float32) * loc_here, axis=1, keepdims=True)
            deltas.append(delta)
            gate_ref[head : head + 1, :] = jnp.sum(
                d_mix * (mem_here - loc_here), axis=0, keepdims=True
            )
            raw = [
                lax.dot_general(q, k, contract_cols, preferred_element_type=jnp.float32) for k in keys
            ]
            bias = slanted(base_ref[head : head + 1, :], rows)[:, : count * rows]
            scores = jnp.concatenate(raw, axis=1) * score_scale + bias
            probs = jnp.exp(jnp.where(same, scores - log_ref[:, head : head + 1], masked_score))
            products = [
                lax.dot_general(d_out, v, contract_cols, preferred_element_type=jnp.float32)
                for v in values
            ]
            slopes = (probs * (jnp.concatenate(products, axis=1) - delta)).astype(jnp.bfloat16)
            slope_blocks = [slopes[:, i * rows : (i + 1) * rows] for i in range(count)]
            dq_ref[:, columns] = score_scale * sum(
                jnp.dot(s, k, preferred_element_type=jnp.float32) for s, k in zip(slope_blocks, keys)
            )
            mirrored = [
                jnp.dot(s, turned, preferred_element_type=jnp.float32) for s in slope_blocks[::-1]
            ]
            mirrored.append(jnp.zeros((rows, span - count * rows), jnp.float32))
            leaned = pltpu.roll(jnp.concatenate(mirrored, axis=1), 0, 1, stride=1, stride_axis=0)
            diagonal_ref[head : head + 1, :] = jnp.sum(leaned, axis=0, keepdims=True)
        mem_logs = [mem_log_ref[:, head : head + 1] for head in range(heads)]
        logs = [log_ref[:, head : head + 1] for head in range(heads)]
        sent_ref[:, width:] = split_tile(lane_tile(mem_logs + mem_deltas + logs + deltas, rows))

    vmem = pl.BlockSpec(memory_space=pltpu.VMEM)
    return pl.pallas_call(
        kernel,
        in_specs=[vmem] * 9 + [pl.BlockSpec(memory_space=pltpu.SMEM)] + [vmem] * len(halos),
        out_shape=[
            jax.ShapeDtypeStruct((rows, width), jnp.float32),
            jax.ShapeDtypeStruct((heads, span), jnp.float32),
            jax.ShapeDtypeStruct((heads, head_dim), jnp.float32),
            jax.ShapeDtypeStruct((rows, width + 128), jnp.bfloat16),
        ],
        compiler_params=pltpu.CompilerParams(vmem_limit_bytes=VMEM_LIMIT),
        cost_estimate=lasting(15),
        name="local_queries",
    )(base, book_column, book_row, own, d_mixed, memory_out, local_out, mem_log, local_log, share, *halos)


def local_keys(base, book_column, book_row, own, queries, sent, ratio, count, heads, score_scale):
    rows, width = own.shape[0], own.shape[1] // 3
    head_dim = width // heads
    groups = queries.shape[0] // rows

    def begin(ins, outs, scratch):
        base_ref, column_ref, row_ref, own_ref, ratio_ref, queries_ref, sent_ref = ins
        (out_ref,) = outs
        queries_here, sent_here, sems = scratch
        copies = []
        for i in range(count):
            index = jnp.minimum(lax.axis_index("mem") + i, groups - 1)
            there = pl.ds(pl.multiple_of(index * rows, rows), rows)
            copies.append(
                pltpu.make_async_copy(queries_ref.at[there, :], queries_here.at[i], sems.at[0, i])
            )
            copies.append(pltpu.make_async_copy(sent_ref.at[there, :], sent_here.at[i], sems.at[1, i]))
        for copy in copies:
            copy.start()

        def run():
            for copy in copies:
                copy.wait()
            same = column_ref[:, :1] == row_ref[:1, :]
            stats = jnp.concatenate([joined_tile(sent_here[i, :, width:]).T for i in range(count)], axis=1)
            for head in range(heads):
                columns = slice(head * head_dim, (head + 1) * head_dim)
                above = slice(width + head * head_dim, width + (head + 1) * head_dim)
                twice = slice(2 * width + head * head_dim, 2 * width + (head + 1) * head_dim)
                k, v = own_ref[:, above], own_ref[:, twice]
                qs = [queries_here[i, :, columns] for i in range(count)]
                gs = [
                    (sent_here[i, :, columns].astype(jnp.float32) * ratio_ref[head]).astype(jnp.bfloat16)
                    for i in range(count)
                ]
                raw = [
                    lax.dot_general(k, q, contract_cols, preferred_element_type=jnp.float32) for q in qs
                ]
                bias = slanted(base_ref[head : head + 1, :], rows)[:, : count * rows]
                scores = jnp.concatenate(raw, axis=1) * score_scale + bias
                log = stats[2 * heads + head : 2 * heads + head + 1, :]
                delta = stats[3 * heads + head : 3 * heads + head + 1, :]
                probs = jnp.exp(jnp.where(same, scores - log, masked_score))
                products = [
                    lax.dot_general(v, g, contract_cols, preferred_element_type=jnp.float32) for g in gs
                ]
                slopes = (probs * (jnp.concatenate(products, axis=1) - delta)).astype(jnp.bfloat16)
                weights = probs.astype(jnp.bfloat16)
                blocks = [slice(i * rows, (i + 1) * rows) for i in range(count)]
                d_key = sum(
                    jnp.dot(slopes[:, b], q, preferred_element_type=jnp.float32) for b, q in zip(blocks, qs)
                )
                d_value = sum(
                    jnp.dot(weights[:, b], g, preferred_element_type=jnp.float32)
                    for b, g in zip(blocks, gs)
                )
                out_ref[:, columns] = (d_key * score_scale).astype(jnp.bfloat16)
                out_ref[:, above] = d_value.astype(jnp.bfloat16)

        return run

    vmem, anywhere = pl.BlockSpec(memory_space=pltpu.VMEM), pl.BlockSpec(memory_space=pl.ANY)
    arrays = [base, book_column, book_row, own, ratio, queries, sent]
    specs = [vmem] * 4 + [pl.BlockSpec(memory_space=pltpu.SMEM), anywhere, anywhere]
    scratch = [
        pltpu.VMEM((count, rows, width), jnp.bfloat16),
        pltpu.VMEM((count, rows, width + 128), jnp.bfloat16),
        pltpu.SemaphoreType.DMA((2, count)),
    ]
    return arrays, specs, [jax.ShapeDtypeStruct((rows, 2 * width), jnp.bfloat16)], scratch, begin


def feed_forward(normed_mid, cotangent, up_weight, down_weight):
    rows, width = normed_mid.shape
    hidden = up_weight.shape[1]
    block = math.gcd(hidden, 1024)

    def kernel(mid_ref, cot_ref, up_ref, down_ref, act_ref, d_up_ref, branch_ref, d_mid_ref):
        first = pl.program_id(0) == 0
        up = jnp.dot(mid_ref[...], up_ref[...], preferred_element_type=jnp.float32)
        d_act = jnp.dot(cot_ref[...], down_ref[...], preferred_element_type=jnp.float32)
        below = 0.5 * (1.0 + lax.erf(up * math.sqrt(0.5)))
        density = jnp.exp(-0.5 * up * up) * (1.0 / math.sqrt(2.0 * math.pi))
        act = (up * below).astype(jnp.bfloat16)
        d_up = (d_act * (below + up * density)).astype(jnp.bfloat16)
        act_ref[...] = act
        d_up_ref[...] = d_up
        branch = lax.dot_general(act, down_ref[...], contract_cols, preferred_element_type=jnp.float32)
        d_mid = lax.dot_general(d_up, up_ref[...], contract_cols, preferred_element_type=jnp.float32)
        branch_ref[...] = jnp.where(first, branch, branch_ref[...] + branch)
        d_mid_ref[...] = jnp.where(first, d_mid, d_mid_ref[...] + d_mid)

    whole = pl.BlockSpec((rows, width), lambda i: (0, 0))
    weight = pl.BlockSpec((width, block), lambda i: (0, i))
    middle = pl.BlockSpec((rows, block), lambda i: (0, i))
    return pl.pallas_call(
        kernel,
        grid=(hidden // block,),
        in_specs=[whole, whole, weight, weight],
        out_specs=[middle, middle, whole, whole],
        out_shape=[
            jax.ShapeDtypeStruct((rows, hidden), jnp.bfloat16),
            jax.ShapeDtypeStruct((rows, hidden), jnp.bfloat16),
            jax.ShapeDtypeStruct((rows, width), jnp.float32),
            jax.ShapeDtypeStruct((rows, width), jnp.float32),
        ],
        compiler_params=pltpu.CompilerParams(vmem_limit_bytes=VMEM_LIMIT),
        cost_estimate=lasting(15),
        name="feed_forward",
    )(normed_mid, cotangent, up_weight, down_weight)


def exchange_pairs(lefts, rights, other_lefts, other_right, send, recv):
    core = lax.axis_index("dp")
    copies, at = [], 0

    def push(source, target):
        i = len(copies)
        copy = pltpu.make_async_remote_copy(
            src_ref=source,
            dst_ref=target,
            send_sem=send.at[i],
            recv_sem=recv.at[i],
            device_id={"dp": 1 - core},
            device_id_type=pl.DeviceIdType.MESH,
        )
        copy.start()
        copies.append(copy)

    for i, (left, right) in enumerate(zip(lefts, rights)):
        half = right.shape[1] // 2
        push(left, other_lefts.at[i])
        there = pl.ds(pl.multiple_of((1 - core) * half, 128), half)
        push(right.at[:, there], other_right.at[:, pl.ds(at, half)])
        at += half
    return copies


def pair_products(lefts, rights, other_lefts, other_right, turned, store):
    core = lax.axis_index("dp")
    rows = lefts[0].shape[0]
    at = 0
    for i, (left, right) in enumerate(zip(lefts, rights)):
        half = right.shape[1] // 2
        turned[:, :rows] = left[...].T
        turned[:, rows:] = other_lefts[i].T
        block = math.gcd(half, 512)
        for column in range(0, half, block):
            kept = right[:, pl.ds(pl.multiple_of(core * half + column, 128), block)]
            both = jnp.concatenate([kept, other_right[:, at + column : at + column + block]], axis=0)
            store(
                at + column,
                jnp.dot(turned[...], both, preferred_element_type=jnp.float32).astype(jnp.bfloat16),
            )
        at += half


def pair_scratch(lefts, rights):
    rows, width = lefts[0].shape
    count = len(lefts)
    return [
        pltpu.VMEM((count, rows, width), jnp.bfloat16),
        pltpu.VMEM((rows, sum(right.shape[1] for right in rights) // 2), jnp.bfloat16),
        pltpu.VMEM((width, 2 * rows), jnp.bfloat16),
        pltpu.SemaphoreType.DMA((2 * count,)),
        pltpu.SemaphoreType.DMA((2 * count,)),
    ]


def pair_grads(lefts, rights, collective_id):
    count, width = len(lefts), lefts[0].shape[1]
    total = sum(right.shape[1] for right in rights) // 2
    block = math.gcd(*[right.shape[1] // 2 for right in rights], 512)

    def kernel(*refs):
        left_refs, right_refs, out_ref = refs[:count], refs[count : 2 * count], refs[2 * count]
        other_lefts, other_right, turned, send, recv, staged, out_sem = refs[2 * count + 1 :]
        barrier = pltpu.get_barrier_semaphore()
        partner = {"dp": 1 - lax.axis_index("dp")}
        pl.semaphore_signal(barrier, inc=1, device_id=partner, device_id_type=pl.DeviceIdType.MESH)
        pl.semaphore_wait(barrier, 1)
        copies = exchange_pairs(left_refs, right_refs, other_lefts, other_right, send, recv)
        for copy in copies:
            copy.wait_recv()
        written = []

        def store(column, value):
            slot = len(written) % 2
            if len(written) >= 2:
                written[-2].wait()
            staged[slot] = value
            copy = pltpu.make_async_copy(
                staged.at[slot], out_ref.at[:, pl.ds(column, block)], out_sem.at[slot]
            )
            copy.start()
            written.append(copy)

        pair_products(left_refs, right_refs, other_lefts, other_right, turned, store)
        for copy in written[-2:]:
            copy.wait()
        for copy in copies:
            copy.wait_send()

    vmem = pl.BlockSpec(memory_space=pltpu.VMEM)
    return pl.pallas_call(
        kernel,
        in_specs=[vmem] * (2 * count),
        out_specs=pl.BlockSpec(memory_space=pl.ANY),
        out_shape=jax.ShapeDtypeStruct((width, total), jnp.bfloat16),
        scratch_shapes=pair_scratch(lefts, rights)
        + [pltpu.VMEM((2, width, block), jnp.bfloat16), pltpu.SemaphoreType.DMA((2,))],
        compiler_params=pltpu.CompilerParams(
            collective_id=collective_id, has_side_effects=True, vmem_limit_bytes=VMEM_LIMIT
        ),
        cost_estimate=lasting(10),
        name="pair_grads",
    )(*lefts, *rights)


def input_backward(tokens, attn_gain, d_projected, qkv_weight, d_residual):
    rows, width = tokens.shape

    def begin(ins, outs, scratch):
        tokens_ref, gain_ref, d_ref, weight_ref, residual_ref = ins
        grad_ref, part_ref = outs
        weight_here, sem = scratch
        copy = pltpu.make_async_copy(weight_ref, weight_here, sem)
        copy.start()

        def run():
            copy.wait()
            d_in = lax.dot_general(
                d_ref[...], weight_here[...], contract_cols, preferred_element_type=jnp.float32
            )
            x = tokens_ref[...].astype(jnp.float32)
            scale = lax.rsqrt(jnp.mean(x * x, axis=1, keepdims=True) + eps_norm)
            wanted = d_in * gain_ref[...]
            slope = jnp.mean(x * wanted, axis=1, keepdims=True) * scale * scale * scale
            grad_ref[...] = residual_ref[...] + scale * wanted - x * slope
            part_ref[...] = jnp.sum(d_in * x * scale, axis=0, keepdims=True)

        return run

    vmem = pl.BlockSpec(memory_space=pltpu.VMEM)
    arrays = [tokens, attn_gain[None, :], d_projected, qkv_weight, d_residual]
    specs = [vmem, vmem, vmem, pl.BlockSpec(memory_space=pl.ANY), vmem]
    out_shape = [
        jax.ShapeDtypeStruct((rows, width), jnp.float32),
        jax.ShapeDtypeStruct((1, width), jnp.float32),
    ]
    scratch = [pltpu.VMEM(qkv_weight.shape, qkv_weight.dtype), pltpu.SemaphoreType.DMA]
    return arrays, specs, out_shape, scratch, begin


def finish_grads(lefts, rights, early, early_widths, small, sources, collective_id, beside):
    width, total = lefts[0].shape[1], sum(right.shape[1] for right in rights) // 2
    rows = width // sources
    count = len(lefts)
    late_widths = [right.shape[1] for right in rights]
    arrays, specs, more_out, more_scratch, begin = beside
    mesh_type = pl.DeviceIdType.MESH
    ref_shapes, sem_shapes = reduce_scratch(rows, total, jnp.bfloat16, sources)
    pair_shapes = pair_scratch(lefts, rights)
    sizes = [count, count, len(arrays), 2, count, len(early_widths), 1, len(more_out)]
    sizes += [len(ref_shapes), len(sem_shapes), len(pair_shapes), len(more_scratch), 10]

    def kernel(*refs):
        groups, at = [], 0
        for size in sizes:
            groups.append(refs[at : at + size])
            at += size
        left_refs, right_refs, ins, (early_ref, small_ref), late_outs, early_outs, (small_out,), more_refs = groups[:8]
        steps_refs, steps_sems, (other_lefts, other_right, turned, pair_send, pair_recv), scratch, own = groups[8:]
        parts, late, both, small_mine, smalls, core_small, small_send, small_recv, core_send, core_recv = own
        meanwhile = begin(ins, more_refs, scratch)
        me, core = lax.axis_index("mem"), lax.axis_index("dp")
        barrier = pltpu.get_barrier_semaphore()
        peers = [lax.rem(me + k, sources) for k in range(1, sources)]
        for peer in peers:
            pl.semaphore_signal(barrier, inc=1, device_id={"mem": peer}, device_id_type=mesh_type)
        pl.semaphore_signal(barrier, inc=1, device_id={"dp": 1 - core}, device_id_type=mesh_type)
        pl.semaphore_wait(barrier, sources)

        def merge(blocks):
            total = blocks[0][...].astype(jnp.float32)
            for block in blocks[1:]:
                total = total + block[...].astype(jnp.float32)
            return total

        def pack(target, total):
            target[...] = total.astype(jnp.bfloat16)

        def across_cores(source, target, i):
            copy = pltpu.make_async_remote_copy(
                src_ref=source,
                dst_ref=target,
                send_sem=core_send.at[i],
                recv_sem=core_recv.at[i],
                device_id={"dp": 1 - core},
                device_id_type=mesh_type,
            )
            copy.start()
            return copy

        pair_copies = exchange_pairs(
            left_refs, right_refs, other_lefts, other_right, pair_send, pair_recv
        )
        for copy in pair_copies:
            copy.wait_recv()

        def store(column, value):
            parts[:, column : column + value.shape[1]] = value

        pair_products(left_refs, right_refs, other_lefts, other_right, turned, store)
        small_copies = [
            remote(small_mine, smalls.at[me], small_send.at[i], small_recv.at[me], peer)
            for i, peer in enumerate(peers)
        ]

        def between():
            meanwhile()
            small_mine[...] = small_ref[...]
            for i in range(width // 128):
                small_mine[i : i + 1, :] = more_refs[-1][:, i * 128 : (i + 1) * 128]
            smalls[me] = small_mine[...]
            for copy in small_copies:
                copy.start()

        early_copy = across_cores(early_ref, both.at[core], 0)
        both[core] = early_ref[...]
        final, still_open = reduce_steps(parts, sources, steps_refs, steps_sems, merge, pack, between)
        for here, blocks in final:
            late[core, here] = merge(blocks).astype(jnp.bfloat16)
        late_copy = across_cores(late.at[core], late.at[core], 2)
        for peer in peers:
            remote(
                smalls.at[peer], smalls.at[peer], small_send.at[0], small_recv.at[peer], peer
            ).wait_recv()
        group_small = smalls[0]
        for i in range(1, sources):
            group_small = group_small + smalls[i]
        core_small[0] = group_small
        small_copy = across_cores(core_small.at[0], core_small.at[1], 1)
        early_copy.wait()

        def spread(halves, outs):
            at = 0
            for out in outs:
                half = out.shape[1] // 2
                for c in (0, 1):
                    out[:, c * half : (c + 1) * half] = halves[c, :, at : at + half].astype(jnp.float32)
                at += half

        spread(both, early_outs)
        for copy in (late_copy, small_copy):
            copy.wait()
        spread(late, late_outs)
        small_out[...] = core_small[0] + core_small[1]
        for copy in still_open + small_copies + pair_copies:
            copy.wait_send()

    vmem = pl.BlockSpec(memory_space=pltpu.VMEM)
    return pl.pallas_call(
        kernel,
        in_specs=[vmem] * (2 * count) + specs + [vmem] * 2,
        out_specs=[vmem] * (count + len(early_widths) + 1 + len(more_out)),
        out_shape=[jax.ShapeDtypeStruct((rows, size), jnp.float32) for size in late_widths + early_widths]
        + [jax.ShapeDtypeStruct(small.shape, small.dtype)]
        + more_out,
        scratch_shapes=ref_shapes
        + sem_shapes
        + pair_shapes
        + more_scratch
        + [
            pltpu.VMEM((width, total), jnp.bfloat16),
            pltpu.VMEM((2, rows, total), jnp.bfloat16),
            pltpu.VMEM((2, *early.shape), early.dtype),
            pltpu.VMEM(small.shape, small.dtype),
            pltpu.VMEM((sources, *small.shape), small.dtype),
            pltpu.VMEM((2, *small.shape), small.dtype),
        ]
        + [pltpu.SemaphoreType.DMA((sources,))] * 2
        + [pltpu.SemaphoreType.DMA((3,))] * 2,
        compiler_params=pltpu.CompilerParams(
            collective_id=collective_id, has_side_effects=True, vmem_limit_bytes=VMEM_LIMIT
        ),
        cost_estimate=lasting(45),
        name="finish_grads",
    )(*lefts, *rights, *arrays, early, small)


def on_device(
    tokens,
    attn_gain,
    qkv_weight,
    out_weight,
    bias_table,
    gate_logit,
    ffn_gain,
    up_weight,
    down_weight,
    memory_keys,
    memory_values,
    book_lengths,
    slot_shard,
    slot_index,
    slot_live,
    cotangent,
):
    rows, width = tokens.shape
    heads, buckets = bias_table.shape
    head_dim = width // heads
    top_count = slot_index.shape[2]
    hidden = up_weight.shape[1]
    groups = lax.axis_size("mem")
    capacity = -(-3 * rows * heads * top_count // (2 * groups) // 128) * 128
    score_scale = 1.0 / math.sqrt(head_dim)
    repeats = W // rows
    span = W + 2 * rows
    me = lax.axis_index("mem")
    first_pos = me * rows
    lengths = book_lengths[0]
    window = jnp.arange(W + rows, dtype=jnp.int32)
    key_pos = first_pos - W + window
    key_book = jnp.where(key_pos >= 0, book_of(key_pos, lengths), -1)
    later_book = book_of(first_pos + window, lengths)
    own_book = jnp.broadcast_to(later_book[:rows, None], (rows, 128))
    key_book = jnp.broadcast_to(key_book[None, :], (8, W + rows))
    later_book = jnp.broadcast_to(later_book[None, :], (8, W + rows))
    bucket = bucket_of(jnp.arange(W, dtype=jnp.int32))
    one_hot = (bucket[:, None] == jnp.arange(buckets, dtype=jnp.int32)).astype(jnp.float32)
    offset_bias = jnp.einsum("rb,hb->hr", one_hot, bias_table, precision=lax.Precision.HIGHEST)
    after_bias = jnp.pad(offset_bias, ((0, 0), (0, span - W)), constant_values=masked_score)
    before_bias = jnp.pad(
        offset_bias[:, ::-1], ((0, 0), (1, span - W - 1)), constant_values=masked_score
    )
    tokens_f = tokens.astype(jnp.float32)
    normed_in = normed(tokens_f, attn_gain).astype(jnp.bfloat16)
    projected = jnp.dot(normed_in, qkv_weight, preferred_element_type=jnp.float32).astype(
        jnp.bfloat16
    )
    slots = memory_keys.shape[0]
    requests = place_requests(slot_shard, slot_index, slot_live, groups, capacity, slots)
    incoming = lax.all_to_all(requests, "mem", split_axis=0, concat_axis=0, tiled=True)
    keys_values, _ = lax.optimization_barrier((projected[:, width:], requests))
    halos = [passed_along(keys_values, "mem", distance) for distance in range(repeats, 0, -1)]
    row_ids = incoming // slots
    limits = jnp.arange(heads + 1, dtype=jnp.int32) * (rows * slots)
    bounds = jnp.sum((incoming[:, None] < limits[None, :, None, None]).astype(jnp.int32), axis=(2, 3))
    index = jnp.where(row_ids < heads * rows, row_ids // rows * slots + incoming % slots, 0)
    padded_ids = jnp.pad(row_ids, ((0, 0), (0, 1), (0, 0)), constant_values=heads * rows)
    key_rows, value_rows = gather_rows(
        index.reshape(-1), bounds[:, heads], memory_keys, memory_values, heads, groups, capacity
    )
    all_queries = lax.all_gather(projected[:, :width], "mem", axis=0, tiled=True)
    local = local_forward(before_bias, own_book, key_book, projected, halos, heads, score_scale)
    partial = memory_forward(
        bounds.reshape(-1),
        all_queries,
        key_rows,
        value_rows,
        padded_ids,
        heads,
        groups,
        rows,
        score_scale,
    )
    if groups == 16:
        memory_out, mem_log, local_out, local_log = merge_partials(partial, groups, 1, heads, local)
    else:
        local_out, local_log = run_alone("local_forward", local)
        partial = lax.all_to_all(
            partial.reshape(groups, rows, width + 128),
            "mem",
            split_axis=0,
            concat_axis=0,
            tiled=True,
        ).reshape(groups * rows, width + 128)
        memory_out, mem_log = combine_partials(partial, heads, groups, rows)
    gate_share = jax.nn.sigmoid(gate_logit)
    share_wide = jnp.repeat(gate_share, head_dim)[None, :]
    mixed_heads = (share_wide * memory_out + (1.0 - share_wide) * local_out).astype(jnp.bfloat16)
    residual = tokens_f + jnp.dot(mixed_heads, out_weight, preferred_element_type=jnp.float32)
    normed_mid_f, norm_mid_back = jax.vjp(normed, residual, ffn_gain)
    normed_mid = normed_mid_f.astype(jnp.bfloat16)
    activated, d_up, ffn_branch, d_mid = feed_forward(normed_mid, cotangent, up_weight, down_weight)
    block_out = (residual + ffn_branch).astype(jnp.bfloat16)
    d_resid_part, ffn_gain_part = norm_mid_back(d_mid)
    d_residual = cotangent.astype(jnp.float32) + d_resid_part
    d_branch = d_residual.astype(jnp.bfloat16)
    d_mixed = lax.dot_general(
        d_branch, out_weight, contract_cols, preferred_element_type=jnp.float32
    )
    early_halves = pair_grads(
        [normed_mid, cotangent], [d_up, activated], 5
    )
    d_queries, diagonals, gate_products, sent_grads = local_queries(
        before_bias,
        own_book,
        key_book,
        projected,
        halos,
        d_mixed,
        memory_out,
        local_out,
        mem_log,
        local_log,
        gate_share,
        heads,
        score_scale,
    )
    gate_part = jnp.sum(gate_products, axis=1) * gate_share * (1.0 - gate_share)
    bias_part = jnp.dot(diagonals[:, rows - 1 : rows - 1 + W], one_hot, precision=lax.Precision.HIGHEST)
    sent_grads, early_halves = lax.optimization_barrier((sent_grads, early_halves))
    early_sums = scattered(early_halves)
    if groups == 16:
        all_grads = gather_group(sent_grads, groups, 2)
    else:
        all_grads = lax.all_gather(sent_grads, "mem", axis=0, tiled=True)
    d_partial = memory_backward(
        bounds.reshape(-1),
        all_queries,
        all_grads,
        key_rows,
        value_rows,
        padded_ids,
        heads,
        groups,
        rows,
        score_scale,
    )
    local = local_keys(
        after_bias,
        own_book,
        later_book,
        projected,
        all_queries,
        all_grads,
        (1.0 - gate_share) / gate_share,
        repeats + 1,
        heads,
        score_scale,
    )
    if groups == 16:
        d_partial, d_keys_values = sum_blocks(d_partial, groups, 3, local)
    else:
        (d_keys_values,) = run_alone("local_keys", local)
        d_partial, d_keys_values = lax.optimization_barrier((d_partial, d_keys_values))
        d_partial = jnp.sum(
            lax.all_to_all(
                d_partial.reshape(groups, rows, width), "mem", split_axis=0, concat_axis=0, tiled=True
            ).astype(jnp.float32),
            axis=0,
        )
    d_queries = (d_queries + d_partial * score_scale).astype(jnp.bfloat16)
    d_projected = jnp.concatenate([d_queries, d_keys_values], axis=1)
    beside = input_backward(tokens, attn_gain, d_projected, qkv_weight, d_residual)
    small = jnp.concatenate([ffn_gain_part, bias_part.reshape(-1), gate_part], axis=0)
    small = jnp.pad(small, (width, -small.shape[0] % 1024)).reshape(-1, 128)
    early_widths = [hidden, hidden]
    lefts, rights = [normed_in, mixed_heads], [d_projected, d_branch]
    if groups == 16:
        qkv_grad, out_grad, up_grad, down_grad, small, tokens_grad, _ = finish_grads(
            lefts, rights, early_sums, early_widths, small, groups, 4, beside
        )
    else:
        tokens_grad, attn_gain_part = run_alone("input_backward", beside)
        late_halves = pair_grads(lefts, rights, 6)
        late_halves, early_sums = lax.optimization_barrier((late_halves, early_sums))
        late_both = lax.all_gather(scattered(late_halves), "dp", axis=0)
        early_both = lax.all_gather(early_sums, "dp", axis=0)
        small = lax.psum(small.at[: width // 128].set(attn_gain_part.reshape(-1, 128)), ("dp", "mem"))
        up_grad, down_grad = whole_grads(early_both, early_widths)
        qkv_grad, out_grad = whole_grads(late_both, [3 * width, width])
    small = small.reshape(-1)
    at_bias = 2 * width + heads * buckets
    return (
        block_out,
        tokens_grad,
        qkv_grad,
        out_grad,
        up_grad,
        down_grad,
        small[:width],
        small[width : 2 * width],
        small[2 * width : at_bias].reshape(heads, buckets),
        small[at_bias : at_bias + heads],
    )


def solution(mesh):
    in_specs = (
        P(("dp", "mem"), None),
        P(),
        P(),
        P(),
        P(),
        P(),
        P(),
        P(),
        P(),
        P("mem", None),
        P("mem", None),
        P("dp", None),
        P(("dp", "mem"), None, None, None),
        P(("dp", "mem"), None, None),
        P(("dp", "mem"), None, None),
        P(("dp", "mem"), None),
    )
    out_specs = (
        P(("dp", "mem"), None),
        P(("dp", "mem"), None),
        P("mem", None),
        P("mem", None),
        P("mem", None),
        P("mem", None),
        P(),
        P(),
        P(),
        P(),
    )
    return jax.shard_map(
        on_device, mesh=mesh, in_specs=in_specs, out_specs=out_specs, check_vma=False
    )
```

```python
import math

import jax
import jax.numpy as jnp
from jax import lax
from jax.experimental import pallas as pl
from jax.experimental.pallas import tpu as pltpu
from jax.sharding import PartitionSpec as P

W = 512
VMEM_LIMIT = 56 * 1024 * 1024


eps_norm = 1e-06
bucket_edges = tuple((math.ceil(16 * 8 ** (edge_step / 16)) for edge_step in range(1, 16)))
masked_score = -1e30
dead_score = -10000.0
contract_rows = (((0,), (0,)), ((), ()))
contract_cols = (((1,), (1,)), ((), ()))


def passed_along(value, axis, by):
    size = lax.axis_size(axis)
    pairs = [(i, i + by) for i in range(size) if 0 <= i + by < size]
    return lax.ppermute(value, axis, pairs)


def bucket_of(offset):
    past_edges = sum(((offset >= edge_pos).astype(jnp.int32) for edge_pos in bucket_edges))
    return jnp.where(offset < 16, offset, 16 + past_edges)


def normed(values, gain_vec):
    return (
        values * lax.rsqrt(jnp.mean(values * values, axis=-1, keepdims=True) + eps_norm) * gain_vec
    )


def book_of(positions, lengths):
    book_ends = jnp.cumsum(lengths, dtype=jnp.int32)
    return jnp.sum((positions[..., None] >= book_ends).astype(jnp.int32), axis=-1)


def place_requests(slot_shard, slot_index, slot_live, owners, capacity, slots):
    rows, heads, top_count = slot_index.shape
    entries = rows * heads * top_count
    row_of = (
        jnp.arange(heads, dtype=jnp.int32)[None, :] * rows
        + jnp.arange(rows, dtype=jnp.int32)[:, None]
    )
    place = row_of[:, :, None] * top_count + jnp.arange(top_count, dtype=jnp.int32)
    owner = jnp.where(slot_live > 0, slot_shard[..., 0], owners)
    keys, picked = lax.sort(
        ((owner * entries + place).reshape(-1), slot_index.reshape(-1)), num_keys=1
    )
    ends = jnp.sum(
        (keys[None, :] < (jnp.arange(owners, dtype=jnp.int32) + 1)[:, None] * entries).astype(jnp.int32),
        axis=1,
    )
    starts = jnp.concatenate([jnp.zeros((1,), jnp.int32), ends[:-1]])
    codes = keys % entries // top_count * slots + picked
    tall = -(-entries // 128)
    codes = jnp.pad(codes, (0, tall * 128 - entries)).reshape(tall, 128)
    long = capacity // 128
    empty = heads * rows * slots

    def kernel(starts_ref, ends_ref, codes_ref, lists_ref, padded):
        padded[:tall, :] = codes_ref[...]
        padded[tall:, :] = jnp.zeros((long + 8, 128), jnp.int32)
        lane = lax.broadcasted_iota(jnp.int32, (long, 128), 1)
        place = lax.broadcasted_iota(jnp.int32, (long, 128), 0) * 128 + lane

        @pl.loop(0, owners)
        def _(i):
            start, end = starts_ref[i], ends_ref[i]
            shift = start % 128
            lines = padded[pl.ds(start // 128, long + 1), :]
            turned = pltpu.roll(lines, (128 - shift) % 128, 1)
            joined = jnp.where(lane < 128 - shift, turned[:long], turned[1:])
            lists_ref[i] = jnp.where(place < end - start, joined, empty)

    return pl.pallas_call(
        kernel,
        in_specs=[pl.BlockSpec(memory_space=pltpu.SMEM)] * 2 + [pl.BlockSpec(memory_space=pltpu.VMEM)],
        out_shape=jax.ShapeDtypeStruct((owners, long, 128), jnp.int32),
        scratch_shapes=[pltpu.VMEM((tall + long + 8, 128), jnp.int32)],
        cost_estimate=lasting(3),
        name="make_lists",
    )(starts, ends, codes)


def gather_rows(index, counts, memory_keys, memory_values, heads, sources, capacity):
    slots, width = memory_keys.shape
    head_dim = width // heads
    step, part = 128, 16

    def kernel(index_ref, counts_ref, keys, values, out_keys, out_values, key_table, value_table, key_rows, value_rows):
        i = pl.program_id(0)

        @pl.when(i < heads)
        def _():
            place = pl.ds(pl.multiple_of(i * slots, slots), slots)
            key_table[place, :] = keys[...].astype(jnp.float32)
            value_table[place, :] = values[...].astype(jnp.float32)

        @pl.when(i >= heads)
        def _():
            source = i - heads

            used = (counts_ref[source] + step - 1) // step

            def store(group):
                for at in range(0, step, part):
                    here = pl.ds(pl.multiple_of(group * step, step) + at, part)
                    out_keys[here, :] = key_rows[at : at + part, :].astype(jnp.bfloat16)
                    out_values[here, :] = value_rows[at : at + part, :].astype(jnp.bfloat16)

            @pl.loop(0, used)
            def _(group):
                store(jnp.maximum(group - 1, 0))
                first = source * capacity + group * step
                for u in range(step):
                    row = index_ref[first + u]
                    key_rows[u : u + 1, :] = key_table[pl.ds(row, 1), :]
                    value_rows[u : u + 1, :] = value_table[pl.ds(row, 1), :]

            pl.when(used > 0)(lambda: store(used - 1))

            @pl.loop(used, capacity // step)
            def _(group):
                here = pl.ds(pl.multiple_of(group * step, step), step)
                out_keys[here, :] = jnp.zeros((step, head_dim), jnp.bfloat16)
                out_values[here, :] = jnp.zeros((step, head_dim), jnp.bfloat16)

    table_spec = pl.BlockSpec((slots, head_dim), lambda i, *_: (0, jnp.minimum(i, heads - 1)))
    out_spec = pl.BlockSpec((capacity, head_dim), lambda i, *_: (jnp.maximum(i - heads, 0), 0))
    out_shape = jax.ShapeDtypeStruct((sources * capacity, head_dim), jnp.bfloat16)
    return pl.pallas_call(
        kernel,
        grid_spec=pltpu.PrefetchScalarGridSpec(
            num_scalar_prefetch=2,
            grid=(heads + sources,),
            in_specs=[table_spec, table_spec],
            out_specs=[out_spec, out_spec],
            scratch_shapes=[
                pltpu.VMEM((heads * slots, head_dim), jnp.float32),
                pltpu.VMEM((heads * slots, head_dim), jnp.float32),
                pltpu.VMEM((step, head_dim), jnp.float32),
                pltpu.VMEM((step, head_dim), jnp.float32),
            ],
        ),
        out_shape=[out_shape, out_shape],
        compiler_params=pltpu.CompilerParams(vmem_limit_bytes=VMEM_LIMIT),
        cost_estimate=lasting(42),
        name="gather_rows",
    )(index, counts, memory_keys, memory_values)


def lasting(microseconds):
    return pl.CostEstimate(flops=0, bytes_accessed=3_000_000 * microseconds, transcendentals=0)


def triple(stat):
    part = lax.broadcasted_iota(jnp.int32, stat.shape, 1) // 16
    high = stat.astype(jnp.bfloat16).astype(jnp.float32)
    rest = stat - high
    middle = rest.astype(jnp.bfloat16).astype(jnp.float32)
    low = rest - middle
    chosen = jnp.where(part == 0, high, jnp.where(part == 1, middle, jnp.where(part == 2, low, 0.0)))
    return chosen.astype(jnp.bfloat16)


def window_of(bounds, source, head, heads, span, capacity):
    first = bounds[source * (heads + 1) + head]
    last = bounds[source * (heads + 1) + head + 1]
    start = jnp.minimum(first // 16 * 16, capacity - span)
    extra = jnp.maximum(last - start - 1, 0) // span
    return start, extra


def columns_of(head, head_dim):
    if isinstance(head, int):
        return slice(head * head_dim, (head + 1) * head_dim)
    return pl.ds(pl.multiple_of(head * head_dim, head_dim), head_dim)


def window_ids(id_ref, start, span):
    lines = id_ref[0, pl.ds(start // 128, span // 128 + 1), :]
    shift = start % 128
    turned = pltpu.roll(lines, (128 - shift) % 128, 1)
    lane = lax.broadcasted_iota(jnp.int32, (span // 128, 128), 1)
    return jnp.where(lane < 128 - shift, turned[:-1], turned[1:])


def owned(lines, first_row, count, start, least):
    row = lax.broadcasted_iota(jnp.int32, (count, 128), 0) + first_row
    masks = []
    for i in range(lines.shape[0]):
        mask = lines[i : i + 1, :] == row
        if least is not None:
            place = lax.broadcasted_iota(jnp.int32, (1, 128), 1) + start + i * 128
            mask = mask & (place >= least)
        masks.append(mask)
    return jnp.concatenate(masks, axis=1)


def memory_forward(bounds, queries, key_rows, value_rows, row_ids, heads, sources, rows, score_scale):
    capacity, head_dim = key_rows.shape[0] // sources, key_rows.shape[1]
    width = heads * head_dim
    span = min(384, capacity)
    chunk = math.gcd(rows, 32)

    def kernel(bounds_ref, q_ref, k_ref, v_ref, id_ref, out_ref, sums, tops, totals, raw, weights):
        source = pl.program_id(0)
        lane = lax.broadcasted_iota(jnp.int32, (chunk, 128), 1) % 16

        def window(heads_here, starts, least):
            here = [pl.ds(pl.multiple_of(start, 16), span) for start in starts]
            columns = [columns_of(head, head_dim) for head in heads_here]
            for slot in range(len(starts)):
                raw[slot] = lax.dot_general(
                    q_ref[:, columns[slot]],
                    k_ref[here[slot], :],
                    contract_cols,
                    preferred_element_type=jnp.float32,
                )
            for slot, (head, start) in enumerate(zip(heads_here, starts)):
                lines = window_ids(id_ref, start, span)
                for at in range(0, rows, chunk):
                    some = slice(at, at + chunk)
                    mine = owned(lines, head * rows + at, chunk, start, least)
                    scores = jnp.where(mine, raw[slot, some, :], masked_score)
                    top = jnp.maximum(jnp.max(scores, axis=1, keepdims=True), 0.1 * masked_score)
                    if least is not None:
                        old_top = jnp.max(
                            jnp.where(lane == head, tops[some, :], masked_score), axis=1, keepdims=True
                        )
                        top = jnp.maximum(top, old_top)
                    exps = jnp.exp((scores - top) * score_scale)
                    weights[slot, some, :] = exps.astype(jnp.bfloat16)
                    total = jnp.sum(exps, axis=1, keepdims=True)
                    if least is not None:
                        faded = jnp.exp((old_top - top) * score_scale)
                        sums[some, columns[slot]] = sums[some, columns[slot]] * faded
                        total = total + totals[some, :] * faded
                    tops[some, :] = jnp.where(lane == head, top, tops[some, :])
                    totals[some, :] = jnp.where(lane == heads + head, total, totals[some, :])
            for slot in range(len(starts)):
                found = jnp.dot(
                    weights[slot], v_ref[here[slot], :], preferred_element_type=jnp.float32
                )
                sums[:, columns[slot]] = found if least is None else sums[:, columns[slot]] + found

        tops[...] = jnp.zeros_like(tops)
        totals[...] = jnp.zeros_like(totals)

        window(
            list(range(heads)),
            [window_of(bounds_ref, source, head, heads, span, capacity)[0] for head in range(heads)],
            None,
        )

        @pl.loop(0, heads)
        def _(head):
            start, extra = window_of(bounds_ref, source, head, heads, span, capacity)

            @pl.loop(0, extra)
            def _(turn):
                least = start + (turn + 1) * span
                window([head], [jnp.minimum(least, capacity - span)], least)

        out_ref[:, :width] = sums[...].astype(jnp.bfloat16)
        wide = lax.broadcasted_iota(jnp.int32, (rows, 128), 1) % 16
        out_ref[:, width:] = triple(jnp.where(wide < heads, tops[...] * score_scale, totals[...]))

    return pl.pallas_call(
        kernel,
        grid_spec=pltpu.PrefetchScalarGridSpec(
            num_scalar_prefetch=1,
            grid=(sources,),
            in_specs=[
                pl.BlockSpec((rows, width), lambda i, *_: (i, 0)),
                pl.BlockSpec((capacity, head_dim), lambda i, *_: (i, 0)),
                pl.BlockSpec((capacity, head_dim), lambda i, *_: (i, 0)),
                pl.BlockSpec((1, *row_ids.shape[1:]), lambda i, *_: (i, 0, 0)),
            ],
            out_specs=pl.BlockSpec((rows, width + 128), lambda i, *_: (i, 0)),
            scratch_shapes=[
                pltpu.VMEM((rows, width), jnp.float32),
                pltpu.VMEM((rows, 128), jnp.float32),
                pltpu.VMEM((rows, 128), jnp.float32),
                pltpu.VMEM((heads, rows, span), jnp.float32),
                pltpu.VMEM((heads, rows, span), jnp.bfloat16),
            ],
        ),
        out_shape=jax.ShapeDtypeStruct((sources * rows, width + 128), jnp.bfloat16),
        compiler_params=pltpu.CompilerParams(vmem_limit_bytes=VMEM_LIMIT),
        cost_estimate=lasting(25),
        name="memory_forward",
    )(bounds, queries, key_rows, value_rows, row_ids)


def combine_partials(partial, heads, sources, rows):
    width = partial.shape[1] - 128
    head_dim = width // heads

    def kernel(part_ref, out_ref, log_ref, sums, tops, totals):
        i = pl.program_id(0)

        @pl.when(i == 0)
        def _():
            sums[...] = jnp.zeros_like(sums)
            tops[...] = jnp.full_like(tops, masked_score)
            totals[...] = jnp.zeros_like(totals)

        stat = part_ref[:, width:].astype(jnp.float32)
        stat = stat + pltpu.roll(stat, 128 - 16, 1) + pltpu.roll(stat, 128 - 32, 1)
        new_total = pltpu.roll(stat, 128 - heads, 1)
        top = jnp.maximum(tops[...], stat)
        old_fade, new_fade = jnp.exp(tops[...] - top), jnp.exp(stat - top)
        tops[...] = top
        totals[...] = totals[...] * old_fade + new_total * new_fade
        for head in range(heads):
            columns = slice(head * head_dim, (head + 1) * head_dim)
            sums[:, columns] = (
                sums[:, columns] * old_fade[:, head : head + 1]
                + part_ref[:, columns].astype(jnp.float32) * new_fade[:, head : head + 1]
            )

        @pl.when(i == sources - 1)
        def _():
            live = totals[...] > 0
            total = jnp.where(live, totals[...], 1.0)
            log_ref[...] = jnp.where(live, tops[...] + jnp.log(total), 0.0)
            for head in range(heads):
                columns = slice(head * head_dim, (head + 1) * head_dim)
                out_ref[:, columns] = sums[:, columns] / total[:, head : head + 1]

    return pl.pallas_call(
        kernel,
        grid=(sources,),
        in_specs=[pl.BlockSpec((rows, width + 128), lambda i: (i, 0))],
        out_specs=[
            pl.BlockSpec((rows, width), lambda i: (0, 0)),
            pl.BlockSpec((rows, 128), lambda i: (0, 0)),
        ],
        scratch_shapes=[
            pltpu.VMEM((rows, width), jnp.float32),
            pltpu.VMEM((rows, 128), jnp.float32),
            pltpu.VMEM((rows, 128), jnp.float32),
        ],
        out_shape=[
            jax.ShapeDtypeStruct((rows, width), jnp.float32),
            jax.ShapeDtypeStruct((rows, 128), jnp.float32),
        ],
        compiler_params=pltpu.CompilerParams(vmem_limit_bytes=VMEM_LIMIT),
        cost_estimate=lasting(13),
        name="combine_partials",
    )(partial)


def memory_backward(bounds, queries, grads, key_rows, value_rows, row_ids, heads, sources, rows, score_scale):
    capacity, head_dim = key_rows.shape[0] // sources, key_rows.shape[1]
    width = heads * head_dim
    span = min(384, capacity)
    chunk = math.gcd(rows, 32)

    def kernel(bounds_ref, q_ref, g_ref, k_ref, v_ref, id_ref, out_ref, sums, stats, raw, products, slopes):
        source = pl.program_id(0)
        stats[...] = joined_tile(g_ref[:, width : width + 128])

        def window(heads_here, starts, least):
            here = [pl.ds(pl.multiple_of(start, 16), span) for start in starts]
            columns = [columns_of(head, head_dim) for head in heads_here]
            for slot in range(len(starts)):
                raw[slot] = lax.dot_general(
                    q_ref[:, columns[slot]],
                    k_ref[here[slot], :],
                    contract_cols,
                    preferred_element_type=jnp.float32,
                )
                products[slot] = lax.dot_general(
                    g_ref[:, columns[slot]],
                    v_ref[here[slot], :],
                    contract_cols,
                    preferred_element_type=jnp.float32,
                )
            for slot, (head, start) in enumerate(zip(heads_here, starts)):
                lines = window_ids(id_ref, start, span)
                turned = stats[...]
                if least is not None:
                    turned = pltpu.roll(turned, 128 - head, 1)
                elif head:
                    turned = turned[:, head:]
                for at in range(0, rows, chunk):
                    some = slice(at, at + chunk)
                    mine = owned(lines, head * rows + at, chunk, start, least)
                    log, delta = turned[some, :1], turned[some, heads : heads + 1]
                    probs = jnp.exp(jnp.where(mine, raw[slot, some, :] * score_scale - log, dead_score))
                    slopes[slot, some, :] = (probs * (products[slot, some, :] - delta)).astype(
                        jnp.bfloat16
                    )
            for slot in range(len(starts)):
                found = jnp.dot(
                    slopes[slot], k_ref[here[slot], :], preferred_element_type=jnp.float32
                )
                sums[:, columns[slot]] = found if least is None else sums[:, columns[slot]] + found

        window(
            list(range(heads)),
            [window_of(bounds_ref, source, head, heads, span, capacity)[0] for head in range(heads)],
            None,
        )

        @pl.loop(0, heads)
        def _(head):
            start, extra = window_of(bounds_ref, source, head, heads, span, capacity)

            @pl.loop(0, extra)
            def _(turn):
                least = start + (turn + 1) * span
                window([head], [jnp.minimum(least, capacity - span)], least)

        out_ref[...] = sums[...].astype(jnp.bfloat16)

    return pl.pallas_call(
        kernel,
        grid_spec=pltpu.PrefetchScalarGridSpec(
            num_scalar_prefetch=1,
            grid=(sources,),
            in_specs=[
                pl.BlockSpec((rows, width), lambda i, *_: (i, 0)),
                pl.BlockSpec((rows, width + 128), lambda i, *_: (i, 0)),
                pl.BlockSpec((capacity, head_dim), lambda i, *_: (i, 0)),
                pl.BlockSpec((capacity, head_dim), lambda i, *_: (i, 0)),
                pl.BlockSpec((1, *row_ids.shape[1:]), lambda i, *_: (i, 0, 0)),
            ],
            out_specs=pl.BlockSpec((rows, width), lambda i, *_: (i, 0)),
            scratch_shapes=[
                pltpu.VMEM((rows, width), jnp.float32),
                pltpu.VMEM((rows, 128), jnp.float32),
                pltpu.VMEM((heads, rows, span), jnp.float32),
                pltpu.VMEM((heads, rows, span), jnp.float32),
                pltpu.VMEM((heads, rows, span), jnp.bfloat16),
            ],
        ),
        out_shape=jax.ShapeDtypeStruct((sources * rows, width), jnp.bfloat16),
        compiler_params=pltpu.CompilerParams(vmem_limit_bytes=VMEM_LIMIT),
        cost_estimate=lasting(25),
        name="memory_backward",
    )(bounds, queries, grads, key_rows, value_rows, row_ids)


def remote(source, target, send_sem, recv_sem, device):
    return pltpu.make_async_remote_copy(
        src_ref=source,
        dst_ref=target,
        send_sem=send_sem,
        recv_sem=recv_sem,
        device_id={"mem": device},
        device_id_type=pl.DeviceIdType.MESH,
    )


def grid_place(depth):
    me = lax.axis_index("mem")
    layer, column = me // 4, me % 4
    beside_x = column + 1 - 2 * (column % 2)
    beside_y = column + 2 - 4 * (column // 2)
    across = 3 - column

    def index_of(step, place):
        return (layer + step + depth) % depth * 4 + place

    return me, column, beside_x, beside_y, across, index_of


def greet(devices):
    barrier = pltpu.get_barrier_semaphore()
    for device in devices:
        pl.semaphore_signal(
            barrier, inc=1, device_id={"mem": device}, device_id_type=pl.DeviceIdType.MESH
        )
    pl.semaphore_wait(barrier, len(devices))


def gather_group(block, sources, collective_id):
    rows, width = block.shape
    depth, half = sources // 4, rows // 2
    slots = 2 * depth - 1

    def kernel(x_ref, out_ref, own_sem, send, recv):
        me = lax.axis_index("mem")
        layer, column = me // 4, me % 4
        to_x = me + 1 - 2 * (column % 2)
        to_y = me + 2 - 4 * (column // 2)
        across = layer * 4 + 3 - column
        has_above, has_below = layer + 1 < depth, layer > 0
        barrier = pltpu.get_barrier_semaphore()

        def signal(device):
            pl.semaphore_signal(
                barrier, inc=1, device_id={"mem": device}, device_id_type=pl.DeviceIdType.MESH
            )

        signal(to_x)
        signal(to_y)
        pl.when(has_above)(lambda: signal(me + 4))
        pl.when(has_below)(lambda: signal(me - 4))
        pl.semaphore_wait(barrier, 2 + has_above.astype(jnp.int32) + has_below.astype(jnp.int32))

        def part_of(index, part):
            start = pl.multiple_of(index * rows + part * half, half)
            return out_ref.at[pl.ds(start, half), :]

        own = pltpu.make_async_copy(x_ref, out_ref.at[pl.ds(pl.multiple_of(me * rows, rows), rows), :], own_sem)
        own.start()
        sent = []

        def push(condition, source, target, kind, slot, to_slot, part, device):
            copy = remote(source, target, send.at[kind, slot, part], recv.at[kind, to_slot, part], device)
            if condition is None:
                copy.start()
            else:
                pl.when(condition)(copy.start)
            sent.append((condition, copy))

        def arrived(index, kind, slot, part):
            target = part_of(index, part)
            remote(target, target, send.at[kind, slot, part], recv.at[kind, slot, part], to_x).wait_recv()

        def up_slot(distance):
            return distance

        def down_slot(distance):
            return depth - 1 + distance

        for part in (0, 1):
            mine = x_ref.at[pl.ds(part * half, half), :]
            push(has_above, mine, part_of(me, part), 0, 0, down_slot(1), part, me + 4)
            push(has_below, mine, part_of(me, part), 1, 0, up_slot(1), part, me - 4)
            mine_y = x_ref.at[pl.ds((1 - part) * half, half), :]
            push(None, mine, part_of(me, part), 2, 0, 0, part, to_x)
            push(None, mine_y, part_of(me, 1 - part), 3, 0, 0, 1 - part, to_y)

        def pass_on(condition, step, slot):
            def go():
                arrived(to_x + step, 2, slot, 0)
                copy_a.start()
                arrived(to_y + step, 3, slot, 1)
                copy_b.start()

            source_a, source_b = part_of(to_x + step, 0), part_of(to_y + step, 1)
            copy_a = remote(source_a, source_a, send.at[4, slot, 0], recv.at[4, slot, 0], to_y)
            copy_b = remote(source_b, source_b, send.at[5, slot, 1], recv.at[5, slot, 1], to_x)
            sent.append((condition, copy_a))
            sent.append((condition, copy_b))
            if condition is None:
                go()
            else:
                pl.when(condition)(go)

        for distance in range(1, depth):
            from_above, from_below = layer + distance < depth, layer - distance >= 0

            def take(kind, back_kind, step, slot, next_slot, onward, onward_device):
                for part in (0, 1):
                    arrived(me + step, kind, slot, part)
                    here = part_of(me + step, part)
                    if next_slot is not None:
                        pl.when(onward)(
                            remote(
                                here, here, send.at[kind, slot, part], recv.at[kind, next_slot, part], onward_device
                            ).start
                        )
                    remote(here, here, send.at[2, slot, part], recv.at[2, slot, part], to_x).start()
                    remote(here, here, send.at[3, slot, part], recv.at[3, slot, part], to_y).start()

            last = distance == depth - 1
            pl.when(from_above)(
                lambda: take(
                    1, 0, 4 * distance, up_slot(distance), None if last else up_slot(distance + 1), has_below, me - 4
                )
            )
            pl.when(from_below)(
                lambda: take(
                    0, 1, -4 * distance, down_slot(distance), None if last else down_slot(distance + 1), has_above, me + 4
                )
            )
            for condition, step, slot, kind, onward in (
                (from_above, 4 * distance, up_slot(distance), 1, has_below),
                (from_below, -4 * distance, down_slot(distance), 0, has_above),
            ):
                for part in (0, 1):
                    here = part_of(me + step, part)
                    if not last:
                        sent.append((condition & onward, remote(here, here, send.at[kind, slot, part], own_sem, me)))
                    sent.append((condition, remote(here, here, send.at[2, slot, part], own_sem, to_x)))
                    sent.append((condition, remote(here, here, send.at[3, slot, part], own_sem, to_y)))
            if distance == 1:
                pass_on(None, 0, 0)
            else:
                pass_on(layer + distance - 1 < depth, 4 * (distance - 1), up_slot(distance - 1))
                pass_on(layer - distance + 1 >= 0, -4 * (distance - 1), down_slot(distance - 1))
        pass_on(layer + depth - 1 < depth, 4 * (depth - 1), up_slot(depth - 1))
        pass_on(layer - depth + 1 >= 0, -4 * (depth - 1), down_slot(depth - 1))

        def close(step, slot):
            arrived(to_x + step, 2, slot, 1)
            arrived(to_y + step, 3, slot, 0)
            arrived(across + step, 4, slot, 0)
            arrived(across + step, 5, slot, 1)

        close(0, 0)
        for distance in range(1, depth):
            pl.when(layer + distance < depth)(lambda: close(4 * distance, up_slot(distance)))
            pl.when(layer - distance >= 0)(lambda: close(-4 * distance, down_slot(distance)))
        for condition, copy in sent:
            if condition is None:
                copy.wait_send()
            else:
                pl.when(condition)(copy.wait_send)
        own.wait()

    return pl.pallas_call(
        kernel,
        in_specs=[pl.BlockSpec(memory_space=pl.ANY)],
        out_specs=pl.BlockSpec(memory_space=pl.ANY),
        out_shape=jax.ShapeDtypeStruct((sources * rows, width), block.dtype),
        scratch_shapes=[
            pltpu.SemaphoreType.DMA,
            pltpu.SemaphoreType.DMA((6, slots, 2)),
            pltpu.SemaphoreType.DMA((6, slots, 2)),
        ],
        compiler_params=pltpu.CompilerParams(
            collective_id=collective_id, has_side_effects=True, vmem_limit_bytes=VMEM_LIMIT
        ),
        cost_estimate=lasting(50),
        name="gather_group",
    )(block)


def reduce_steps(parts_ref, sources, refs, sems, merge, pack, beside=None):
    half_a, half_b, from_x, from_y, from_z, out_x, out_y, out_z = refs
    send, recv_a, recv_b, recv_x, recv_y, recv_z = sems
    rows = parts_ref.shape[0] // sources
    depth, half = sources // 4, rows // 2
    me, column, beside_x, beside_y, across, index_of = grid_place(depth)
    to_x, to_y = index_of(0, beside_x), index_of(0, beside_y)
    order = [*range(1, depth), 0]
    queues = {"x": [], "y": [], "z": []}
    first_limit = 2 if beside is None else depth

    def piece(index, part):
        return parts_ref.at[pl.ds(pl.multiple_of(index * rows + part * half, half), half), :]

    def part_rows(part):
        return pl.ds(part * half, half)

    def push(link, source, target, kind, k, recv_sem, device, limit=2):
        queue = queues[link]
        while link != "z" and len(queue) >= limit:
            queue.pop(0).wait_send()
        copy = remote(source, target, send.at[kind, k], recv_sem, device)
        copy.start()
        queue.append(copy)

    def arrived(target, recv_sem):
        remote(target, target, send.at[0, 0], recv_sem, to_x).wait_recv()

    def plane_rest(k):
        push("x", piece(index_of(k, beside_x), 0), from_x.at[k, part_rows(0)], 2, k, recv_x.at[0, k], to_x)
        push("y", piece(index_of(k, beside_y), 1), from_y.at[k, part_rows(1)], 3, k, recv_y.at[1, k], to_y)

    def plane_merged(k):
        arrived(half_a.at[k], recv_a.at[k])
        pack(out_y.at[k], merge([piece(index_of(k, beside_y), 0), half_a.at[k]]))
        push("y", out_y.at[k], from_y.at[k, part_rows(0)], 4, k, recv_y.at[0, k], to_y)
        arrived(half_b.at[k], recv_b.at[k])
        pack(out_x.at[k], merge([piece(index_of(k, beside_x), 1), half_b.at[k]]))
        push("x", out_x.at[k], from_x.at[k, part_rows(1)], 5, k, recv_x.at[1, k], to_x)

    def column_step(k):
        for part in (0, 1):
            here = part_rows(part)
            arrived(from_x.at[k, here], recv_x.at[part, k])
            arrived(from_y.at[k, here], recv_y.at[part, k])
            if k:
                blocks = [piece(index_of(k, column), part), from_x.at[k, here], from_y.at[k, here]]
                pack(out_z.at[k, here], merge(blocks))
        if k:
            push("z", out_z.at[k], from_z.at[k], 6, k, recv_z.at[k], index_of(k, column))

    for k in order:
        far = index_of(k, across)
        push("x", piece(far, 0), half_a.at[k], 0, k, recv_a.at[k], to_x, first_limit)
        push("y", piece(far, 1), half_b.at[k], 1, k, recv_b.at[k], to_y, first_limit)
    if beside is not None:
        beside()
    for i, k in enumerate(order):
        plane_rest(k)
        plane_merged(k)
        if i:
            column_step(order[i - 1])
    column_step(order[-1])
    for k in range(1, depth):
        arrived(from_z.at[k], recv_z.at[k])
    final = []
    for part in (0, 1):
        here = part_rows(part)
        blocks = [piece(me, part), from_x.at[0, here], from_y.at[0, here]]
        final.append((here, blocks + [from_z.at[k, here] for k in range(1, depth)]))
    return final, [copy for queue in queues.values() for copy in queue]


def reduce_scratch(rows, width, dtype, sources):
    depth, half = sources // 4, rows // 2

    def slots(size):
        return pltpu.VMEM((depth, size, width), dtype)

    refs = [slots(half), slots(half), slots(rows), slots(rows), slots(rows)]
    refs += [slots(half), slots(half), slots(rows)]
    sems = [pltpu.SemaphoreType.DMA((7, depth))]
    sems += [pltpu.SemaphoreType.DMA((depth,))] * 2
    sems += [pltpu.SemaphoreType.DMA((2, depth))] * 2
    sems += [pltpu.SemaphoreType.DMA((depth,))]
    return refs, sems


def run_alone(name, beside):
    arrays, specs, out_shape, scratch, begin = beside
    ins, outs = len(arrays), len(out_shape)

    def kernel(*refs):
        begin(refs[:ins], refs[ins : ins + outs], refs[ins + outs :])()

    return pl.pallas_call(
        kernel,
        in_specs=specs,
        out_specs=[pl.BlockSpec(memory_space=pltpu.VMEM)] * outs,
        out_shape=out_shape,
        scratch_shapes=scratch,
        compiler_params=pltpu.CompilerParams(vmem_limit_bytes=VMEM_LIMIT),
        cost_estimate=lasting(8),
        name=name,
    )(*arrays)


def reduce_group(parts, sources, collective_id, merge, pack, finish, out_shape, beside):
    rows, width = parts.shape[0] // sources, parts.shape[1]
    depth = sources // 4
    arrays, specs, more_out, more_scratch, begin = beside
    ref_shapes, sem_shapes = reduce_scratch(rows, width, parts.dtype, sources)
    sizes = [len(arrays), len(out_shape), len(more_out), len(ref_shapes), len(sem_shapes), len(more_scratch)]

    def kernel(parts_ref, *refs):
        groups, at = [], 0
        for size in sizes:
            groups.append(refs[at : at + size])
            at += size
        ins, out_refs, more_refs, steps_refs, steps_sems, scratch = groups
        meanwhile = begin(ins, more_refs, scratch)
        me, column, beside_x, beside_y, across, index_of = grid_place(depth)
        greet(
            [index_of(0, beside_x), index_of(0, beside_y)]
            + [index_of(-k, column) for k in range(1, depth)]
        )
        final, still_open = reduce_steps(
            parts_ref, sources, steps_refs, steps_sems, merge, pack, meanwhile
        )
        for here, blocks in final:
            finish([out.at[here] for out in out_refs], merge(blocks))
        for copy in still_open:
            copy.wait_send()

    vmem = pl.BlockSpec(memory_space=pltpu.VMEM)
    return pl.pallas_call(
        kernel,
        in_specs=[vmem, *specs],
        out_specs=[vmem] * (len(out_shape) + len(more_out)),
        out_shape=[*out_shape, *more_out],
        scratch_shapes=[*ref_shapes, *sem_shapes, *more_scratch],
        compiler_params=pltpu.CompilerParams(
            collective_id=collective_id, has_side_effects=True, vmem_limit_bytes=VMEM_LIMIT
        ),
        cost_estimate=lasting(50),
        name="reduce_group",
    )(parts, *arrays)


def sum_blocks(parts, sources, collective_id, beside):
    rows, width = parts.shape[0] // sources, parts.shape[1]

    def merge(blocks):
        total = blocks[0][...].astype(jnp.float32)
        for block in blocks[1:]:
            total = total + block[...].astype(jnp.float32)
        return total

    def pack(target, total):
        target[...] = total.astype(parts.dtype)

    def finish(targets, total):
        targets[0][...] = total

    out_shape = [jax.ShapeDtypeStruct((rows, width), jnp.float32)]
    return reduce_group(parts, sources, collective_id, merge, pack, finish, out_shape, beside)


def merge_partials(parts, sources, collective_id, heads, beside):
    rows, width = parts.shape[0] // sources, parts.shape[1] - 128
    head_dim = width // heads

    def merge(blocks):
        stats = []
        for block in blocks:
            stat = block[:, width:].astype(jnp.float32)
            stats.append(stat + pltpu.roll(stat, 128 - 16, 1) + pltpu.roll(stat, 128 - 32, 1))
        top = stats[0]
        for stat in stats[1:]:
            top = jnp.maximum(top, stat)
        fades = [jnp.exp(stat - top) for stat in stats]
        total = sum(fade * pltpu.roll(stat, 128 - heads, 1) for fade, stat in zip(fades, stats))
        sums = []
        for head in range(heads):
            columns = slice(head * head_dim, (head + 1) * head_dim)
            sums.append(
                sum(
                    block[:, columns].astype(jnp.float32) * fade[:, head : head + 1]
                    for block, fade in zip(blocks, fades)
                )
            )
        return sums, top, total

    def pack(target, merged):
        sums, top, total = merged
        for head in range(heads):
            target[:, head * head_dim : (head + 1) * head_dim] = sums[head].astype(parts.dtype)
        lane = lax.broadcasted_iota(jnp.int32, top.shape, 1)
        stat = jnp.where(lane < heads, top, jnp.where(lane < 16, pltpu.roll(total, heads, 1), 0.0))
        target[:, width:] = triple(stat + pltpu.roll(stat, 16, 1) + pltpu.roll(stat, 32, 1))

    def finish(targets, merged):
        sums, top, total = merged
        live = total > 0
        total = jnp.where(live, total, 1.0)
        targets[1][...] = jnp.where(live, top + jnp.log(total), 0.0)
        for head in range(heads):
            targets[0][:, head * head_dim : (head + 1) * head_dim] = sums[head] / total[:, head : head + 1]

    out_shape = [
        jax.ShapeDtypeStruct((rows, width), jnp.float32),
        jax.ShapeDtypeStruct((rows, 128), jnp.float32),
    ]
    return reduce_group(parts, sources, collective_id, merge, pack, finish, out_shape, beside)


def scattered(halves):
    return lax.psum_scatter(halves, "mem", scatter_dimension=0, tiled=True)


def whole_grads(both, widths):
    both = both.astype(jnp.float32)
    grads, at = [], 0
    for size in widths:
        half = size // 2
        grads.append(jnp.concatenate([both[0, :, at : at + half], both[1, :, at : at + half]], 1))
        at += half
    return grads


def lane_tile(columns, rows):
    lane = lax.broadcasted_iota(jnp.int32, (rows, 128), 1)
    tile = jnp.zeros((rows, 128), jnp.float32)
    for i, column in enumerate(columns):
        tile = jnp.where(lane == i, column, tile)
    return tile


def split_tile(tile):
    lane = lax.broadcasted_iota(jnp.int32, tile.shape, 1)
    kept = jnp.where(lane < 32, tile, 0.0)
    kept = kept + pltpu.roll(kept, 32, 1) + pltpu.roll(kept, 64, 1)
    high = kept.astype(jnp.bfloat16).astype(jnp.float32)
    middle = (kept - high).astype(jnp.bfloat16).astype(jnp.float32)
    low = kept - high - middle
    part = lane // 32
    return jnp.where(part == 0, high, jnp.where(part == 1, middle, low)).astype(jnp.bfloat16)


def joined_tile(tile):
    tile = tile.astype(jnp.float32)
    return tile + pltpu.roll(tile, 128 - 32, 1) + pltpu.roll(tile, 128 - 64, 1)


def slanted(base, rows):
    return pltpu.roll(jnp.broadcast_to(base, (rows, base.shape[1])), 0, 1, stride=1, stride_axis=0)


def local_forward(base, book_column, book_row, own, halos, heads, score_scale):
    rows, width = own.shape[0], own.shape[1] // 3
    head_dim = width // heads
    count = len(halos) + 1

    def begin(ins, outs, scratch):
        base_ref, column_ref, row_ref, own_ref, *halo_refs = ins
        out_ref, log_ref = outs

        def run():
            same = column_ref[:, :1] == row_ref[:1, :]
            logs = []
            for head in range(heads):
                columns = slice(head * head_dim, (head + 1) * head_dim)
                above = slice(width + head * head_dim, width + (head + 1) * head_dim)
                twice = slice(2 * width + head * head_dim, 2 * width + (head + 1) * head_dim)
                keys = [ref[:, columns] for ref in halo_refs] + [own_ref[:, above]]
                values = [ref[:, above] for ref in halo_refs] + [own_ref[:, twice]]
                q = own_ref[:, columns]
                raw = [
                    lax.dot_general(q, k, contract_cols, preferred_element_type=jnp.float32) for k in keys
                ]
                bias = slanted(base_ref[head : head + 1, :], rows)[:, : count * rows]
                scores = jnp.concatenate(raw, axis=1) * score_scale + bias
                scores = jnp.where(same, scores, masked_score)
                top = jnp.max(scores, axis=1, keepdims=True)
                weights = jnp.exp(scores - top)
                total = jnp.sum(weights, axis=1, keepdims=True)
                weights = (weights / total).astype(jnp.bfloat16)
                out_ref[:, columns] = sum(
                    jnp.dot(
                        weights[:, i * rows : (i + 1) * rows], v, preferred_element_type=jnp.float32
                    )
                    for i, v in enumerate(values)
                )
                logs.append(top + jnp.log(total))
            log_ref[...] = lane_tile(logs, rows)

        return run

    arrays = [base, book_column, book_row, own, *halos]
    specs = [pl.BlockSpec(memory_space=pltpu.VMEM)] * len(arrays)
    out_shape = [
        jax.ShapeDtypeStruct((rows, width), jnp.float32),
        jax.ShapeDtypeStruct((rows, 128), jnp.float32),
    ]
    return arrays, specs, out_shape, [], begin


def local_queries(
    base, book_column, book_row, own, halos, d_mixed, memory_out, local_out, mem_log, local_log, share, heads, score_scale
):
    rows, width = d_mixed.shape
    head_dim = width // heads
    count = len(halos) + 1
    span = base.shape[1]

    def kernel(
        base_ref, column_ref, row_ref, own_ref, mix_ref, mem_ref, loc_ref, mem_log_ref, log_ref, share_ref, *refs
    ):
        halo_refs, (dq_ref, diagonal_ref, gate_ref, sent_ref) = refs[: count - 1], refs[count - 1 :]
        same = column_ref[:, :1] == row_ref[:1, :]
        turned = (
            lax.broadcasted_iota(jnp.int32, (rows, rows), 0)
            + lax.broadcasted_iota(jnp.int32, (rows, rows), 1)
            == rows - 1
        ).astype(jnp.bfloat16)
        mem_deltas, deltas = [], []
        for head in range(heads):
            columns = slice(head * head_dim, (head + 1) * head_dim)
            above = slice(width + head * head_dim, width + (head + 1) * head_dim)
            twice = slice(2 * width + head * head_dim, 2 * width + (head + 1) * head_dim)
            keys = [ref[:, columns] for ref in halo_refs] + [own_ref[:, above]]
            values = [ref[:, above] for ref in halo_refs] + [own_ref[:, twice]]
            q = own_ref[:, columns]
            share_here = share_ref[head]
            d_mix, mem_here, loc_here = mix_ref[:, columns], mem_ref[:, columns], loc_ref[:, columns]
            d_mem = (share_here * d_mix).astype(jnp.bfloat16)
            d_out = ((1.0 - share_here) * d_mix).astype(jnp.bfloat16)
            sent_ref[:, columns] = d_mem
            mem_deltas.append(
                jnp.sum(d_mem.astype(jnp.float32) * mem_here, axis=1, keepdims=True)
            )
            delta = jnp.sum(d_out.astype(jnp.float32) * loc_here, axis=1, keepdims=True)
            deltas.append(delta)
            gate_ref[head : head + 1, :] = jnp.sum(
                d_mix * (mem_here - loc_here), axis=0, keepdims=True
            )
            raw = [
                lax.dot_general(q, k, contract_cols, preferred_element_type=jnp.float32) for k in keys
            ]
            bias = slanted(base_ref[head : head + 1, :], rows)[:, : count * rows]
            scores = jnp.concatenate(raw, axis=1) * score_scale + bias
            probs = jnp.exp(jnp.where(same, scores - log_ref[:, head : head + 1], masked_score))
            products = [
                lax.dot_general(d_out, v, contract_cols, preferred_element_type=jnp.float32)
                for v in values
            ]
            slopes = (probs * (jnp.concatenate(products, axis=1) - delta)).astype(jnp.bfloat16)
            slope_blocks = [slopes[:, i * rows : (i + 1) * rows] for i in range(count)]
            dq_ref[:, columns] = score_scale * sum(
                jnp.dot(s, k, preferred_element_type=jnp.float32) for s, k in zip(slope_blocks, keys)
            )
            mirrored = [
                jnp.dot(s, turned, preferred_element_type=jnp.float32) for s in slope_blocks[::-1]
            ]
            mirrored.append(jnp.zeros((rows, span - count * rows), jnp.float32))
            leaned = pltpu.roll(jnp.concatenate(mirrored, axis=1), 0, 1, stride=1, stride_axis=0)
            diagonal_ref[head : head + 1, :] = jnp.sum(leaned, axis=0, keepdims=True)
        mem_logs = [mem_log_ref[:, head : head + 1] for head in range(heads)]
        logs = [log_ref[:, head : head + 1] for head in range(heads)]
        sent_ref[:, width:] = split_tile(lane_tile(mem_logs + mem_deltas + logs + deltas, rows))

    vmem = pl.BlockSpec(memory_space=pltpu.VMEM)
    return pl.pallas_call(
        kernel,
        in_specs=[vmem] * 9 + [pl.BlockSpec(memory_space=pltpu.SMEM)] + [vmem] * len(halos),
        out_shape=[
            jax.ShapeDtypeStruct((rows, width), jnp.float32),
            jax.ShapeDtypeStruct((heads, span), jnp.float32),
            jax.ShapeDtypeStruct((heads, head_dim), jnp.float32),
            jax.ShapeDtypeStruct((rows, width + 128), jnp.bfloat16),
        ],
        compiler_params=pltpu.CompilerParams(vmem_limit_bytes=VMEM_LIMIT),
        cost_estimate=lasting(15),
        name="local_queries",
    )(base, book_column, book_row, own, d_mixed, memory_out, local_out, mem_log, local_log, share, *halos)


def local_keys(base, book_column, book_row, own, queries, sent, ratio, count, heads, score_scale):
    rows, width = own.shape[0], own.shape[1] // 3
    head_dim = width // heads
    groups = queries.shape[0] // rows

    def begin(ins, outs, scratch):
        base_ref, column_ref, row_ref, own_ref, ratio_ref, queries_ref, sent_ref = ins
        (out_ref,) = outs
        queries_here, sent_here, sems = scratch
        copies = []
        for i in range(count):
            index = jnp.minimum(lax.axis_index("mem") + i, groups - 1)
            there = pl.ds(pl.multiple_of(index * rows, rows), rows)
            copies.append(
                pltpu.make_async_copy(queries_ref.at[there, :], queries_here.at[i], sems.at[0, i])
            )
            copies.append(pltpu.make_async_copy(sent_ref.at[there, :], sent_here.at[i], sems.at[1, i]))
        for copy in copies:
            copy.start()

        def run():
            for copy in copies:
                copy.wait()
            same = column_ref[:, :1] == row_ref[:1, :]
            stats = jnp.concatenate([joined_tile(sent_here[i, :, width:]).T for i in range(count)], axis=1)
            for head in range(heads):
                columns = slice(head * head_dim, (head + 1) * head_dim)
                above = slice(width + head * head_dim, width + (head + 1) * head_dim)
                twice = slice(2 * width + head * head_dim, 2 * width + (head + 1) * head_dim)
                k, v = own_ref[:, above], own_ref[:, twice]
                qs = [queries_here[i, :, columns] for i in range(count)]
                gs = [
                    (sent_here[i, :, columns].astype(jnp.float32) * ratio_ref[head]).astype(jnp.bfloat16)
                    for i in range(count)
                ]
                raw = [
                    lax.dot_general(k, q, contract_cols, preferred_element_type=jnp.float32) for q in qs
                ]
                bias = slanted(base_ref[head : head + 1, :], rows)[:, : count * rows]
                scores = jnp.concatenate(raw, axis=1) * score_scale + bias
                log = stats[2 * heads + head : 2 * heads + head + 1, :]
                delta = stats[3 * heads + head : 3 * heads + head + 1, :]
                probs = jnp.exp(jnp.where(same, scores - log, masked_score))
                products = [
                    lax.dot_general(v, g, contract_cols, preferred_element_type=jnp.float32) for g in gs
                ]
                slopes = (probs * (jnp.concatenate(products, axis=1) - delta)).astype(jnp.bfloat16)
                weights = probs.astype(jnp.bfloat16)
                blocks = [slice(i * rows, (i + 1) * rows) for i in range(count)]
                d_key = sum(
                    jnp.dot(slopes[:, b], q, preferred_element_type=jnp.float32) for b, q in zip(blocks, qs)
                )
                d_value = sum(
                    jnp.dot(weights[:, b], g, preferred_element_type=jnp.float32)
                    for b, g in zip(blocks, gs)
                )
                out_ref[:, columns] = (d_key * score_scale).astype(jnp.bfloat16)
                out_ref[:, above] = d_value.astype(jnp.bfloat16)

        return run

    vmem, anywhere = pl.BlockSpec(memory_space=pltpu.VMEM), pl.BlockSpec(memory_space=pl.ANY)
    arrays = [base, book_column, book_row, own, ratio, queries, sent]
    specs = [vmem] * 4 + [pl.BlockSpec(memory_space=pltpu.SMEM), anywhere, anywhere]
    scratch = [
        pltpu.VMEM((count, rows, width), jnp.bfloat16),
        pltpu.VMEM((count, rows, width + 128), jnp.bfloat16),
        pltpu.SemaphoreType.DMA((2, count)),
    ]
    return arrays, specs, [jax.ShapeDtypeStruct((rows, 2 * width), jnp.bfloat16)], scratch, begin


def feed_forward(normed_mid, cotangent, up_weight, down_weight):
    rows, width = normed_mid.shape
    hidden = up_weight.shape[1]
    block = math.gcd(hidden, 1024)

    def kernel(mid_ref, cot_ref, up_ref, down_ref, act_ref, d_up_ref, branch_ref, d_mid_ref):
        first = pl.program_id(0) == 0
        up = jnp.dot(mid_ref[...], up_ref[...], preferred_element_type=jnp.float32)
        d_act = jnp.dot(cot_ref[...], down_ref[...], preferred_element_type=jnp.float32)
        below = 0.5 * (1.0 + lax.erf(up * math.sqrt(0.5)))
        density = jnp.exp(-0.5 * up * up) * (1.0 / math.sqrt(2.0 * math.pi))
        act = (up * below).astype(jnp.bfloat16)
        d_up = (d_act * (below + up * density)).astype(jnp.bfloat16)
        act_ref[...] = act
        d_up_ref[...] = d_up
        branch = lax.dot_general(act, down_ref[...], contract_cols, preferred_element_type=jnp.float32)
        d_mid = lax.dot_general(d_up, up_ref[...], contract_cols, preferred_element_type=jnp.float32)
        branch_ref[...] = jnp.where(first, branch, branch_ref[...] + branch)
        d_mid_ref[...] = jnp.where(first, d_mid, d_mid_ref[...] + d_mid)

    whole = pl.BlockSpec((rows, width), lambda i: (0, 0))
    weight = pl.BlockSpec((width, block), lambda i: (0, i))
    middle = pl.BlockSpec((rows, block), lambda i: (0, i))
    return pl.pallas_call(
        kernel,
        grid=(hidden // block,),
        in_specs=[whole, whole, weight, weight],
        out_specs=[middle, middle, whole, whole],
        out_shape=[
            jax.ShapeDtypeStruct((rows, hidden), jnp.bfloat16),
            jax.ShapeDtypeStruct((rows, hidden), jnp.bfloat16),
            jax.ShapeDtypeStruct((rows, width), jnp.float32),
            jax.ShapeDtypeStruct((rows, width), jnp.float32),
        ],
        compiler_params=pltpu.CompilerParams(vmem_limit_bytes=VMEM_LIMIT),
        cost_estimate=lasting(15),
        name="feed_forward",
    )(normed_mid, cotangent, up_weight, down_weight)


def exchange_pairs(lefts, rights, other_lefts, other_right, send, recv):
    core = lax.axis_index("dp")
    copies, at = [], 0

    def push(source, target):
        i = len(copies)
        copy = pltpu.make_async_remote_copy(
            src_ref=source,
            dst_ref=target,
            send_sem=send.at[i],
            recv_sem=recv.at[i],
            device_id={"dp": 1 - core},
            device_id_type=pl.DeviceIdType.MESH,
        )
        copy.start()
        copies.append(copy)

    for i, (left, right) in enumerate(zip(lefts, rights)):
        half = right.shape[1] // 2
        push(left, other_lefts.at[i])
        there = pl.ds(pl.multiple_of((1 - core) * half, 128), half)
        push(right.at[:, there], other_right.at[:, pl.ds(at, half)])
        at += half
    return copies


def pair_products(lefts, rights, other_lefts, other_right, turned, store):
    core = lax.axis_index("dp")
    rows = lefts[0].shape[0]
    at = 0
    for i, (left, right) in enumerate(zip(lefts, rights)):
        half = right.shape[1] // 2
        turned[:, :rows] = left[...].T
        turned[:, rows:] = other_lefts[i].T
        block = math.gcd(half, 512)
        for column in range(0, half, block):
            kept = right[:, pl.ds(pl.multiple_of(core * half + column, 128), block)]
            both = jnp.concatenate([kept, other_right[:, at + column : at + column + block]], axis=0)
            store(
                at + column,
                jnp.dot(turned[...], both, preferred_element_type=jnp.float32).astype(jnp.bfloat16),
            )
        at += half


def pair_scratch(lefts, rights):
    rows, width = lefts[0].shape
    count = len(lefts)
    return [
        pltpu.VMEM((count, rows, width), jnp.bfloat16),
        pltpu.VMEM((rows, sum(right.shape[1] for right in rights) // 2), jnp.bfloat16),
        pltpu.VMEM((width, 2 * rows), jnp.bfloat16),
        pltpu.SemaphoreType.DMA((2 * count,)),
        pltpu.SemaphoreType.DMA((2 * count,)),
    ]


def pair_grads(lefts, rights, collective_id):
    count, width = len(lefts), lefts[0].shape[1]
    total = sum(right.shape[1] for right in rights) // 2
    block = math.gcd(*[right.shape[1] // 2 for right in rights], 512)

    def kernel(*refs):
        left_refs, right_refs, out_ref = refs[:count], refs[count : 2 * count], refs[2 * count]
        other_lefts, other_right, turned, send, recv, staged, out_sem = refs[2 * count + 1 :]
        barrier = pltpu.get_barrier_semaphore()
        partner = {"dp": 1 - lax.axis_index("dp")}
        pl.semaphore_signal(barrier, inc=1, device_id=partner, device_id_type=pl.DeviceIdType.MESH)
        pl.semaphore_wait(barrier, 1)
        copies = exchange_pairs(left_refs, right_refs, other_lefts, other_right, send, recv)
        for copy in copies:
            copy.wait_recv()
        written = []

        def store(column, value):
            slot = len(written) % 2
            if len(written) >= 2:
                written[-2].wait()
            staged[slot] = value
            copy = pltpu.make_async_copy(
                staged.at[slot], out_ref.at[:, pl.ds(column, block)], out_sem.at[slot]
            )
            copy.start()
            written.append(copy)

        pair_products(left_refs, right_refs, other_lefts, other_right, turned, store)
        for copy in written[-2:]:
            copy.wait()
        for copy in copies:
            copy.wait_send()

    vmem = pl.BlockSpec(memory_space=pltpu.VMEM)
    return pl.pallas_call(
        kernel,
        in_specs=[vmem] * (2 * count),
        out_specs=pl.BlockSpec(memory_space=pl.ANY),
        out_shape=jax.ShapeDtypeStruct((width, total), jnp.bfloat16),
        scratch_shapes=pair_scratch(lefts, rights)
        + [pltpu.VMEM((2, width, block), jnp.bfloat16), pltpu.SemaphoreType.DMA((2,))],
        compiler_params=pltpu.CompilerParams(
            collective_id=collective_id, has_side_effects=True, vmem_limit_bytes=VMEM_LIMIT
        ),
        cost_estimate=lasting(10),
        name="pair_grads",
    )(*lefts, *rights)


def input_backward(tokens, attn_gain, d_projected, qkv_weight, d_residual):
    rows, width = tokens.shape

    def begin(ins, outs, scratch):
        tokens_ref, gain_ref, d_ref, weight_ref, residual_ref = ins
        grad_ref, part_ref = outs
        weight_here, sem = scratch
        copy = pltpu.make_async_copy(weight_ref, weight_here, sem)
        copy.start()

        def run():
            copy.wait()
            d_in = lax.dot_general(
                d_ref[...], weight_here[...], contract_cols, preferred_element_type=jnp.float32
            )
            x = tokens_ref[...].astype(jnp.float32)
            scale = lax.rsqrt(jnp.mean(x * x, axis=1, keepdims=True) + eps_norm)
            wanted = d_in * gain_ref[...]
            slope = jnp.mean(x * wanted, axis=1, keepdims=True) * scale * scale * scale
            grad_ref[...] = residual_ref[...] + scale * wanted - x * slope
            part_ref[...] = jnp.sum(d_in * x * scale, axis=0, keepdims=True)

        return run

    vmem = pl.BlockSpec(memory_space=pltpu.VMEM)
    arrays = [tokens, attn_gain[None, :], d_projected, qkv_weight, d_residual]
    specs = [vmem, vmem, vmem, pl.BlockSpec(memory_space=pl.ANY), vmem]
    out_shape = [
        jax.ShapeDtypeStruct((rows, width), jnp.float32),
        jax.ShapeDtypeStruct((1, width), jnp.float32),
    ]
    scratch = [pltpu.VMEM(qkv_weight.shape, qkv_weight.dtype), pltpu.SemaphoreType.DMA]
    return arrays, specs, out_shape, scratch, begin


def spread_halves(halves, outs):
    at = 0
    for out in outs:
        half = out.shape[1] // 2
        for c in (0, 1):
            out[:, c * half : (c + 1) * half] = halves[c, :, at : at + half].astype(jnp.float32)
        at += half


def join_halves(sums, widths, collective_id):
    def kernel(sums_ref, *refs):
        outs, (both, send, recv) = refs[: len(widths)], refs[len(widths) :]
        core = lax.axis_index("dp")
        partner = {"dp": 1 - core}
        barrier = pltpu.get_barrier_semaphore()
        pl.semaphore_signal(barrier, inc=1, device_id=partner, device_id_type=pl.DeviceIdType.MESH)
        pl.semaphore_wait(barrier, 1)
        copy = pltpu.make_async_remote_copy(
            src_ref=sums_ref,
            dst_ref=both.at[core],
            send_sem=send,
            recv_sem=recv,
            device_id=partner,
            device_id_type=pl.DeviceIdType.MESH,
        )
        copy.start()
        both[core] = sums_ref[...]
        copy.wait()
        spread_halves(both, outs)

    vmem = pl.BlockSpec(memory_space=pltpu.VMEM)
    return pl.pallas_call(
        kernel,
        in_specs=[vmem],
        out_specs=[vmem] * len(widths),
        out_shape=[jax.ShapeDtypeStruct((sums.shape[0], size), jnp.float32) for size in widths],
        scratch_shapes=[
            pltpu.VMEM((2, *sums.shape), sums.dtype),
            pltpu.SemaphoreType.DMA,
            pltpu.SemaphoreType.DMA,
        ],
        compiler_params=pltpu.CompilerParams(
            collective_id=collective_id, has_side_effects=True, vmem_limit_bytes=VMEM_LIMIT
        ),
        cost_estimate=lasting(5),
        name="join_halves",
    )(sums)


def finish_grads(lefts, rights, small, sources, collective_id, beside):
    width, total = lefts[0].shape[1], sum(right.shape[1] for right in rights) // 2
    rows = width // sources
    count = len(lefts)
    late_widths = [right.shape[1] for right in rights]
    arrays, specs, more_out, more_scratch, begin = beside
    mesh_type = pl.DeviceIdType.MESH
    ref_shapes, sem_shapes = reduce_scratch(rows, total, jnp.bfloat16, sources)
    pair_shapes = pair_scratch(lefts, rights)
    sizes = [count, count, len(arrays), 1, count, 1, len(more_out)]
    sizes += [len(ref_shapes), len(sem_shapes), len(pair_shapes), len(more_scratch), 9]

    def kernel(*refs):
        groups, at = [], 0
        for size in sizes:
            groups.append(refs[at : at + size])
            at += size
        left_refs, right_refs, ins, (small_ref,), late_outs, (small_out,), more_refs = groups[:7]
        steps_refs, steps_sems, (other_lefts, other_right, turned, pair_send, pair_recv), scratch, own = groups[7:]
        parts, late, small_mine, smalls, core_small, small_send, small_recv, core_send, core_recv = own
        meanwhile = begin(ins, more_refs, scratch)
        me, core = lax.axis_index("mem"), lax.axis_index("dp")
        barrier = pltpu.get_barrier_semaphore()
        peers = [lax.rem(me + k, sources) for k in range(1, sources)]
        for peer in peers:
            pl.semaphore_signal(barrier, inc=1, device_id={"mem": peer}, device_id_type=mesh_type)
        pl.semaphore_signal(barrier, inc=1, device_id={"dp": 1 - core}, device_id_type=mesh_type)
        pl.semaphore_wait(barrier, sources)

        def merge(blocks):
            total = blocks[0][...].astype(jnp.float32)
            for block in blocks[1:]:
                total = total + block[...].astype(jnp.float32)
            return total

        def pack(target, total):
            target[...] = total.astype(jnp.bfloat16)

        def across_cores(source, target, i):
            copy = pltpu.make_async_remote_copy(
                src_ref=source,
                dst_ref=target,
                send_sem=core_send.at[i],
                recv_sem=core_recv.at[i],
                device_id={"dp": 1 - core},
                device_id_type=mesh_type,
            )
            copy.start()
            return copy

        pair_copies = exchange_pairs(
            left_refs, right_refs, other_lefts, other_right, pair_send, pair_recv
        )
        for copy in pair_copies:
            copy.wait_recv()

        def store(column, value):
            parts[:, column : column + value.shape[1]] = value

        pair_products(left_refs, right_refs, other_lefts, other_right, turned, store)
        small_copies = [
            remote(small_mine, smalls.at[me], small_send.at[i], small_recv.at[me], peer)
            for i, peer in enumerate(peers)
        ]

        def between():
            meanwhile()
            small_mine[...] = small_ref[...]
            for i in range(width // 128):
                small_mine[i : i + 1, :] = more_refs[-1][:, i * 128 : (i + 1) * 128]
            smalls[me] = small_mine[...]
            for copy in small_copies:
                copy.start()

        final, still_open = reduce_steps(parts, sources, steps_refs, steps_sems, merge, pack, between)
        for here, blocks in final:
            late[core, here] = merge(blocks).astype(jnp.bfloat16)
        late_copy = across_cores(late.at[core], late.at[core], 0)
        for peer in peers:
            remote(
                smalls.at[peer], smalls.at[peer], small_send.at[0], small_recv.at[peer], peer
            ).wait_recv()
        group_small = smalls[0]
        for i in range(1, sources):
            group_small = group_small + smalls[i]
        core_small[0] = group_small
        small_copy = across_cores(core_small.at[0], core_small.at[1], 1)
        for copy in (late_copy, small_copy):
            copy.wait()
        spread_halves(late, late_outs)
        small_out[...] = core_small[0] + core_small[1]
        for copy in still_open + small_copies + pair_copies:
            copy.wait_send()

    vmem = pl.BlockSpec(memory_space=pltpu.VMEM)
    return pl.pallas_call(
        kernel,
        in_specs=[vmem] * (2 * count) + specs + [vmem],
        out_specs=[vmem] * (count + 1 + len(more_out)),
        out_shape=[jax.ShapeDtypeStruct((rows, size), jnp.float32) for size in late_widths]
        + [jax.ShapeDtypeStruct(small.shape, small.dtype)]
        + more_out,
        scratch_shapes=ref_shapes
        + sem_shapes
        + pair_shapes
        + more_scratch
        + [
            pltpu.VMEM((width, total), jnp.bfloat16),
            pltpu.VMEM((2, rows, total), jnp.bfloat16),
            pltpu.VMEM(small.shape, small.dtype),
            pltpu.VMEM((sources, *small.shape), small.dtype),
            pltpu.VMEM((2, *small.shape), small.dtype),
        ]
        + [pltpu.SemaphoreType.DMA((sources,))] * 2
        + [pltpu.SemaphoreType.DMA((2,))] * 2,
        compiler_params=pltpu.CompilerParams(
            collective_id=collective_id, has_side_effects=True, vmem_limit_bytes=VMEM_LIMIT
        ),
        cost_estimate=lasting(45),
        name="finish_grads",
    )(*lefts, *rights, *arrays, small)


def on_device(
    tokens,
    attn_gain,
    qkv_weight,
    out_weight,
    bias_table,
    gate_logit,
    ffn_gain,
    up_weight,
    down_weight,
    memory_keys,
    memory_values,
    book_lengths,
    slot_shard,
    slot_index,
    slot_live,
    cotangent,
):
    rows, width = tokens.shape
    heads, buckets = bias_table.shape
    head_dim = width // heads
    top_count = slot_index.shape[2]
    hidden = up_weight.shape[1]
    groups = lax.axis_size("mem")
    capacity = -(-3 * rows * heads * top_count // (2 * groups) // 128) * 128
    score_scale = 1.0 / math.sqrt(head_dim)
    repeats = W // rows
    span = W + 2 * rows
    me = lax.axis_index("mem")
    first_pos = me * rows
    lengths = book_lengths[0]
    window = jnp.arange(W + rows, dtype=jnp.int32)
    key_pos = first_pos - W + window
    key_book = jnp.where(key_pos >= 0, book_of(key_pos, lengths), -1)
    later_book = book_of(first_pos + window, lengths)
    own_book = jnp.broadcast_to(later_book[:rows, None], (rows, 128))
    key_book = jnp.broadcast_to(key_book[None, :], (8, W + rows))
    later_book = jnp.broadcast_to(later_book[None, :], (8, W + rows))
    bucket = bucket_of(jnp.arange(W, dtype=jnp.int32))
    one_hot = (bucket[:, None] == jnp.arange(buckets, dtype=jnp.int32)).astype(jnp.float32)
    offset_bias = jnp.einsum("rb,hb->hr", one_hot, bias_table, precision=lax.Precision.HIGHEST)
    after_bias = jnp.pad(offset_bias, ((0, 0), (0, span - W)), constant_values=masked_score)
    before_bias = jnp.pad(
        offset_bias[:, ::-1], ((0, 0), (1, span - W - 1)), constant_values=masked_score
    )
    tokens_f = tokens.astype(jnp.float32)
    normed_in = normed(tokens_f, attn_gain).astype(jnp.bfloat16)
    projected = jnp.dot(normed_in, qkv_weight, preferred_element_type=jnp.float32).astype(
        jnp.bfloat16
    )
    slots = memory_keys.shape[0]
    requests = place_requests(slot_shard, slot_index, slot_live, groups, capacity, slots)
    incoming = lax.all_to_all(requests, "mem", split_axis=0, concat_axis=0, tiled=True)
    keys_values, _ = lax.optimization_barrier((projected[:, width:], requests))
    halos = [passed_along(keys_values, "mem", distance) for distance in range(repeats, 0, -1)]
    row_ids = incoming // slots
    limits = jnp.arange(heads + 1, dtype=jnp.int32) * (rows * slots)
    bounds = jnp.sum((incoming[:, None] < limits[None, :, None, None]).astype(jnp.int32), axis=(2, 3))
    index = jnp.where(row_ids < heads * rows, row_ids // rows * slots + incoming % slots, 0)
    padded_ids = jnp.pad(row_ids, ((0, 0), (0, 1), (0, 0)), constant_values=heads * rows)
    key_rows, value_rows = gather_rows(
        index.reshape(-1), bounds[:, heads], memory_keys, memory_values, heads, groups, capacity
    )
    all_queries = lax.all_gather(projected[:, :width], "mem", axis=0, tiled=True)
    local = local_forward(before_bias, own_book, key_book, projected, halos, heads, score_scale)
    partial = memory_forward(
        bounds.reshape(-1),
        all_queries,
        key_rows,
        value_rows,
        padded_ids,
        heads,
        groups,
        rows,
        score_scale,
    )
    if groups == 16:
        memory_out, mem_log, local_out, local_log = merge_partials(partial, groups, 1, heads, local)
    else:
        local_out, local_log = run_alone("local_forward", local)
        partial = lax.all_to_all(
            partial.reshape(groups, rows, width + 128),
            "mem",
            split_axis=0,
            concat_axis=0,
            tiled=True,
        ).reshape(groups * rows, width + 128)
        memory_out, mem_log = combine_partials(partial, heads, groups, rows)
    gate_share = jax.nn.sigmoid(gate_logit)
    share_wide = jnp.repeat(gate_share, head_dim)[None, :]
    mixed_heads = (share_wide * memory_out + (1.0 - share_wide) * local_out).astype(jnp.bfloat16)
    residual = tokens_f + jnp.dot(mixed_heads, out_weight, preferred_element_type=jnp.float32)
    normed_mid_f, norm_mid_back = jax.vjp(normed, residual, ffn_gain)
    normed_mid = normed_mid_f.astype(jnp.bfloat16)
    activated, d_up, ffn_branch, d_mid = feed_forward(normed_mid, cotangent, up_weight, down_weight)
    block_out = (residual + ffn_branch).astype(jnp.bfloat16)
    d_resid_part, ffn_gain_part = norm_mid_back(d_mid)
    d_residual = cotangent.astype(jnp.float32) + d_resid_part
    d_branch = d_residual.astype(jnp.bfloat16)
    early_halves = pair_grads(
        [mixed_heads, normed_mid, cotangent], [d_branch, d_up, activated], 5
    )
    early_sums = scattered(early_halves)
    d_after, _ = lax.optimization_barrier((d_branch, early_halves))
    d_mixed = lax.dot_general(
        d_after, out_weight, contract_cols, preferred_element_type=jnp.float32
    )
    d_queries, diagonals, gate_products, sent_grads = local_queries(
        before_bias,
        own_book,
        key_book,
        projected,
        halos,
        d_mixed,
        memory_out,
        local_out,
        mem_log,
        local_log,
        gate_share,
        heads,
        score_scale,
    )
    gate_part = jnp.sum(gate_products, axis=1) * gate_share * (1.0 - gate_share)
    bias_part = jnp.dot(diagonals[:, rows - 1 : rows - 1 + W], one_hot, precision=lax.Precision.HIGHEST)
    if groups == 16:
        all_grads = gather_group(sent_grads, groups, 2)
    else:
        all_grads = lax.all_gather(sent_grads, "mem", axis=0, tiled=True)
    d_partial = memory_backward(
        bounds.reshape(-1),
        all_queries,
        all_grads,
        key_rows,
        value_rows,
        padded_ids,
        heads,
        groups,
        rows,
        score_scale,
    )
    local = local_keys(
        after_bias,
        own_book,
        later_book,
        projected,
        all_queries,
        all_grads,
        (1.0 - gate_share) / gate_share,
        repeats + 1,
        heads,
        score_scale,
    )
    if groups == 16:
        d_partial, d_keys_values = sum_blocks(d_partial, groups, 3, local)
    else:
        (d_keys_values,) = run_alone("local_keys", local)
        d_partial, d_keys_values = lax.optimization_barrier((d_partial, d_keys_values))
        d_partial = jnp.sum(
            lax.all_to_all(
                d_partial.reshape(groups, rows, width), "mem", split_axis=0, concat_axis=0, tiled=True
            ).astype(jnp.float32),
            axis=0,
        )
    d_queries = (d_queries + d_partial * score_scale).astype(jnp.bfloat16)
    d_projected = jnp.concatenate([d_queries, d_keys_values], axis=1)
    beside = input_backward(tokens, attn_gain, d_projected, qkv_weight, d_residual)
    small = jnp.concatenate([ffn_gain_part, bias_part.reshape(-1), gate_part], axis=0)
    small = jnp.pad(small, (width, -small.shape[0] % 1024)).reshape(-1, 128)
    early_widths = [width, hidden, hidden]
    if groups == 16:
        qkv_grad, small, tokens_grad, _ = finish_grads(
            [normed_in], [d_projected], small, groups, 4, beside
        )
        early_sums, small = lax.optimization_barrier((early_sums, small))
        out_grad, up_grad, down_grad = join_halves(early_sums, early_widths, 7)
    else:
        tokens_grad, attn_gain_part = run_alone("input_backward", beside)
        late_halves = pair_grads([normed_in], [d_projected], 6)
        late_halves, early_sums = lax.optimization_barrier((late_halves, early_sums))
        late_both = lax.all_gather(scattered(late_halves), "dp", axis=0)
        early_both = lax.all_gather(early_sums, "dp", axis=0)
        small = lax.psum(small.at[: width // 128].set(attn_gain_part.reshape(-1, 128)), ("dp", "mem"))
        out_grad, up_grad, down_grad = whole_grads(early_both, early_widths)
        qkv_grad = whole_grads(late_both, [3 * width])[0]
    small = small.reshape(-1)
    at_bias = 2 * width + heads * buckets
    return (
        block_out,
        tokens_grad,
        qkv_grad,
        out_grad,
        up_grad,
        down_grad,
        small[:width],
        small[width : 2 * width],
        small[2 * width : at_bias].reshape(heads, buckets),
        small[at_bias : at_bias + heads],
    )


def solution(mesh):
    in_specs = (
        P(("dp", "mem"), None),
        P(),
        P(),
        P(),
        P(),
        P(),
        P(),
        P(),
        P(),
        P("mem", None),
        P("mem", None),
        P("dp", None),
        P(("dp", "mem"), None, None, None),
        P(("dp", "mem"), None, None),
        P(("dp", "mem"), None, None),
        P(("dp", "mem"), None),
    )
    out_specs = (
        P(("dp", "mem"), None),
        P(("dp", "mem"), None),
        P("mem", None),
        P("mem", None),
        P("mem", None),
        P("mem", None),
        P(),
        P(),
        P(),
        P(),
    )
    return jax.shard_map(
        on_device, mesh=mesh, in_specs=in_specs, out_specs=out_specs, check_vma=False
    )
```

```python
import math

import jax
import jax.numpy as jnp
from jax import lax
from jax.experimental import pallas as pl
from jax.experimental.pallas import tpu as pltpu
from jax.sharding import PartitionSpec as P

W = 512
VMEM_LIMIT = 56 * 1024 * 1024


eps_norm = 1e-06
bucket_edges = tuple((math.ceil(16 * 8 ** (edge_step / 16)) for edge_step in range(1, 16)))
masked_score = -1e30
dead_score = -10000.0
contract_rows = (((0,), (0,)), ((), ()))
contract_cols = (((1,), (1,)), ((), ()))


def passed_along(value, axis, by):
    size = lax.axis_size(axis)
    pairs = [(i, i + by) for i in range(size) if 0 <= i + by < size]
    return lax.ppermute(value, axis, pairs)


def bucket_of(offset):
    past_edges = sum(((offset >= edge_pos).astype(jnp.int32) for edge_pos in bucket_edges))
    return jnp.where(offset < 16, offset, 16 + past_edges)


def normed(values, gain_vec):
    return (
        values * lax.rsqrt(jnp.mean(values * values, axis=-1, keepdims=True) + eps_norm) * gain_vec
    )


def book_of(positions, lengths):
    book_ends = jnp.cumsum(lengths, dtype=jnp.int32)
    return jnp.sum((positions[..., None] >= book_ends).astype(jnp.int32), axis=-1)


def place_requests(slot_shard, slot_index, slot_live, owners, capacity, slots):
    rows, heads, top_count = slot_index.shape
    entries, empty = rows * heads * top_count, heads * rows * slots
    if (owners + 1) * empty >= 2**31:
        raise ValueError("codes exceed int32")
    row_of = (
        jnp.arange(heads, dtype=jnp.int32)[None, :] * rows
        + jnp.arange(rows, dtype=jnp.int32)[:, None]
    )
    owner = jnp.where(slot_live > 0, slot_shard[..., 0], owners)
    codes = owner * empty + row_of[:, :, None] * slots + slot_index
    codes = lax.sort(codes.reshape(-1), is_stable=False)
    ends = jnp.sum(
        (codes[None, :] < (jnp.arange(owners, dtype=jnp.int32) + 1)[:, None] * empty).astype(jnp.int32),
        axis=1,
    )
    starts = jnp.concatenate([jnp.zeros((1,), jnp.int32), ends[:-1]])
    tall = -(-entries // 128)
    codes = jnp.pad(codes, (0, tall * 128 - entries)).reshape(tall, 128)
    long = capacity // 128

    def kernel(starts_ref, ends_ref, codes_ref, lists_ref, padded):
        padded[:tall, :] = codes_ref[...]
        padded[tall:, :] = jnp.zeros((long + 8, 128), jnp.int32)
        lane = lax.broadcasted_iota(jnp.int32, (long, 128), 1)
        place = lax.broadcasted_iota(jnp.int32, (long, 128), 0) * 128 + lane

        @pl.loop(0, owners)
        def _(i):
            start, end = starts_ref[i], ends_ref[i]
            shift = start % 128
            lines = padded[pl.ds(start // 128, long + 1), :]
            turned = pltpu.roll(lines, (128 - shift) % 128, 1)
            joined = jnp.where(lane < 128 - shift, turned[:long], turned[1:])
            lists_ref[i] = jnp.where(place < end - start, joined - i * empty, empty)

    return pl.pallas_call(
        kernel,
        in_specs=[pl.BlockSpec(memory_space=pltpu.SMEM)] * 2 + [pl.BlockSpec(memory_space=pltpu.VMEM)],
        out_shape=jax.ShapeDtypeStruct((owners, long, 128), jnp.int32),
        scratch_shapes=[pltpu.VMEM((tall + long + 8, 128), jnp.int32)],
        cost_estimate=lasting(3),
        name="make_lists",
    )(starts, ends, codes)


def read_lists(incoming, heads, rows, slots):
    sources, long, _ = incoming.shape

    def kernel(lists_ref, index_ref, ids_ref, bounds_ref):
        lane = lax.broadcasted_iota(jnp.int32, (1, 128), 1)

        def read(source):
            codes = lists_ref[source]
            ids = lax.div(codes, slots)
            index = lax.div(ids, rows) * slots + lax.rem(codes, slots)
            index_ref[source] = jnp.where(ids < heads * rows, index, 0)
            ids_ref[source, :long, :] = ids
            ids_ref[source, long:, :] = jnp.full((1, 128), heads * rows, jnp.int32)
            bounds = jnp.zeros((1, 128), jnp.int32)
            for head in range(1, heads + 1):
                below = jnp.sum(
                    jnp.where(codes < head * rows * slots, 1.0, 0.0), axis=0, keepdims=True
                )
                below = jnp.sum(below, axis=1, keepdims=True).astype(jnp.int32)
                bounds = jnp.where(lane == head, below, bounds)
            bounds_ref[pl.ds(source, 1), :] = bounds

        if sources > 16:
            pl.loop(0, sources)(read)
        else:
            for source in range(sources):
                read(source)

    return pl.pallas_call(
        kernel,
        out_shape=[
            jax.ShapeDtypeStruct((sources, long, 128), jnp.int32),
            jax.ShapeDtypeStruct((sources, long + 1, 128), jnp.int32),
            jax.ShapeDtypeStruct((sources, 128), jnp.int32),
        ],
        cost_estimate=lasting(3),
        name="read_lists",
    )(incoming)


def gather_rows(index, bounds, memory_keys, memory_values, heads, sources, capacity):
    slots, width = memory_keys.shape
    head_dim = width // heads
    step, part = 128, 16

    def kernel(index_ref, bounds_ref, keys, values, out_keys, out_values, key_table, value_table, key_rows, value_rows):
        i = pl.program_id(0)

        @pl.when(i < heads)
        def _():
            place = pl.ds(pl.multiple_of(i * slots, slots), slots)
            key_table[place, :] = keys[...].astype(jnp.float32)
            value_table[place, :] = values[...].astype(jnp.float32)

        @pl.when(i >= heads)
        def _():
            source = i - heads

            used = (bounds_ref[source * 128 + heads] + step - 1) // step

            def store(group):
                for at in range(0, step, part):
                    here = pl.ds(pl.multiple_of(group * step, step) + at, part)
                    out_keys[here, :] = key_rows[at : at + part, :].astype(jnp.bfloat16)
                    out_values[here, :] = value_rows[at : at + part, :].astype(jnp.bfloat16)

            @pl.loop(0, used)
            def _(group):
                store(jnp.maximum(group - 1, 0))
                first = source * capacity + group * step
                for u in range(step):
                    row = index_ref[first + u]
                    key_rows[u : u + 1, :] = key_table[pl.ds(row, 1), :]
                    value_rows[u : u + 1, :] = value_table[pl.ds(row, 1), :]

            pl.when(used > 0)(lambda: store(used - 1))

            @pl.loop(used, capacity // step)
            def _(group):
                here = pl.ds(pl.multiple_of(group * step, step), step)
                out_keys[here, :] = jnp.zeros((step, head_dim), jnp.bfloat16)
                out_values[here, :] = jnp.zeros((step, head_dim), jnp.bfloat16)

    table_spec = pl.BlockSpec((slots, head_dim), lambda i, *_: (0, jnp.minimum(i, heads - 1)))
    out_spec = pl.BlockSpec((capacity, head_dim), lambda i, *_: (jnp.maximum(i - heads, 0), 0))
    out_shape = jax.ShapeDtypeStruct((sources * capacity, head_dim), jnp.bfloat16)
    return pl.pallas_call(
        kernel,
        grid_spec=pltpu.PrefetchScalarGridSpec(
            num_scalar_prefetch=2,
            grid=(heads + sources,),
            in_specs=[table_spec, table_spec],
            out_specs=[out_spec, out_spec],
            scratch_shapes=[
                pltpu.VMEM((heads * slots, head_dim), jnp.float32),
                pltpu.VMEM((heads * slots, head_dim), jnp.float32),
                pltpu.VMEM((step, head_dim), jnp.float32),
                pltpu.VMEM((step, head_dim), jnp.float32),
            ],
        ),
        out_shape=[out_shape, out_shape],
        compiler_params=pltpu.CompilerParams(vmem_limit_bytes=VMEM_LIMIT),
        cost_estimate=lasting(42),
        name="gather_rows",
    )(index, bounds, memory_keys, memory_values)


def lasting(microseconds):
    return pl.CostEstimate(flops=0, bytes_accessed=3_000_000 * microseconds, transcendentals=0)


def triple(stat):
    part = lax.broadcasted_iota(jnp.int32, stat.shape, 1) // 16
    high = stat.astype(jnp.bfloat16).astype(jnp.float32)
    rest = stat - high
    middle = rest.astype(jnp.bfloat16).astype(jnp.float32)
    low = rest - middle
    chosen = jnp.where(part == 0, high, jnp.where(part == 1, middle, jnp.where(part == 2, low, 0.0)))
    return chosen.astype(jnp.bfloat16)


def window_of(bounds, source, head, heads, span, capacity):
    first, last = bounds[source * 128 + head], bounds[source * 128 + head + 1]
    start = jnp.minimum(first // 16 * 16, capacity - span)
    extra = jnp.maximum(last - start - 1, 0) // span
    return start, extra


def columns_of(head, head_dim):
    if isinstance(head, int):
        return slice(head * head_dim, (head + 1) * head_dim)
    return pl.ds(pl.multiple_of(head * head_dim, head_dim), head_dim)


def window_ids(id_ref, start, span):
    lines = id_ref[0, pl.ds(start // 128, span // 128 + 1), :]
    shift = start % 128
    turned = pltpu.roll(lines, (128 - shift) % 128, 1)
    lane = lax.broadcasted_iota(jnp.int32, (span // 128, 128), 1)
    return jnp.where(lane < 128 - shift, turned[:-1], turned[1:])


def owned(lines, first_row, count, start, least):
    row = lax.broadcasted_iota(jnp.int32, (count, 128), 0) + first_row
    masks = []
    for i in range(lines.shape[0]):
        mask = lines[i : i + 1, :] == row
        if least is not None:
            place = lax.broadcasted_iota(jnp.int32, (1, 128), 1) + start + i * 128
            mask = mask & (place >= least)
        masks.append(mask)
    return jnp.concatenate(masks, axis=1)


def memory_forward(bounds, queries, key_rows, value_rows, row_ids, heads, sources, rows, score_scale):
    capacity, head_dim = key_rows.shape[0] // sources, key_rows.shape[1]
    width = heads * head_dim
    span = min(384, capacity)
    chunk = math.gcd(rows, 32)

    def kernel(bounds_ref, q_ref, k_ref, v_ref, id_ref, out_ref, sums, tops, totals, raw, weights):
        source = pl.program_id(0)
        lane = lax.broadcasted_iota(jnp.int32, (chunk, 128), 1) % 16

        def window(heads_here, starts, least):
            here = [pl.ds(pl.multiple_of(start, 16), span) for start in starts]
            columns = [columns_of(head, head_dim) for head in heads_here]
            for slot in range(len(starts)):
                raw[slot] = lax.dot_general(
                    q_ref[:, columns[slot]],
                    k_ref[here[slot], :],
                    contract_cols,
                    preferred_element_type=jnp.float32,
                )
            for slot, (head, start) in enumerate(zip(heads_here, starts)):
                lines = window_ids(id_ref, start, span)
                for at in range(0, rows, chunk):
                    some = slice(at, at + chunk)
                    mine = owned(lines, head * rows + at, chunk, start, least)
                    scores = jnp.where(mine, raw[slot, some, :], masked_score)
                    top = jnp.maximum(jnp.max(scores, axis=1, keepdims=True), 0.1 * masked_score)
                    if least is not None:
                        old_top = jnp.max(
                            jnp.where(lane == head, tops[some, :], masked_score), axis=1, keepdims=True
                        )
                        top = jnp.maximum(top, old_top)
                    exps = jnp.exp((scores - top) * score_scale)
                    weights[slot, some, :] = exps.astype(jnp.bfloat16)
                    total = jnp.sum(exps, axis=1, keepdims=True)
                    if least is not None:
                        faded = jnp.exp((old_top - top) * score_scale)
                        sums[some, columns[slot]] = sums[some, columns[slot]] * faded
                        total = total + totals[some, :] * faded
                    tops[some, :] = jnp.where(lane == head, top, tops[some, :])
                    totals[some, :] = jnp.where(lane == heads + head, total, totals[some, :])
            for slot in range(len(starts)):
                found = jnp.dot(
                    weights[slot], v_ref[here[slot], :], preferred_element_type=jnp.float32
                )
                sums[:, columns[slot]] = found if least is None else sums[:, columns[slot]] + found

        tops[...] = jnp.zeros_like(tops)
        totals[...] = jnp.zeros_like(totals)

        windows = [window_of(bounds_ref, source, head, heads, span, capacity) for head in range(heads)]
        window(list(range(heads)), [start for start, _ in windows], None)

        @pl.when(sum(extra for _, extra in windows) > 0)
        def _():
            @pl.loop(0, heads)
            def _(head):
                start, extra = window_of(bounds_ref, source, head, heads, span, capacity)

                @pl.loop(0, extra)
                def _(turn):
                    least = start + (turn + 1) * span
                    window([head], [jnp.minimum(least, capacity - span)], least)

        out_ref[:, :width] = sums[...].astype(jnp.bfloat16)
        wide = lax.broadcasted_iota(jnp.int32, (rows, 128), 1) % 16
        out_ref[:, width:] = triple(jnp.where(wide < heads, tops[...] * score_scale, totals[...]))

    return pl.pallas_call(
        kernel,
        grid_spec=pltpu.PrefetchScalarGridSpec(
            num_scalar_prefetch=1,
            grid=(sources,),
            in_specs=[
                pl.BlockSpec((rows, width), lambda i, *_: (i, 0)),
                pl.BlockSpec((capacity, head_dim), lambda i, *_: (i, 0)),
                pl.BlockSpec((capacity, head_dim), lambda i, *_: (i, 0)),
                pl.BlockSpec((1, *row_ids.shape[1:]), lambda i, *_: (i, 0, 0)),
            ],
            out_specs=pl.BlockSpec((rows, width + 128), lambda i, *_: (i, 0)),
            scratch_shapes=[
                pltpu.VMEM((rows, width), jnp.float32),
                pltpu.VMEM((rows, 128), jnp.float32),
                pltpu.VMEM((rows, 128), jnp.float32),
                pltpu.VMEM((heads, rows, span), jnp.float32),
                pltpu.VMEM((heads, rows, span), jnp.bfloat16),
            ],
        ),
        out_shape=jax.ShapeDtypeStruct((sources * rows, width + 128), jnp.bfloat16),
        compiler_params=pltpu.CompilerParams(vmem_limit_bytes=VMEM_LIMIT),
        cost_estimate=lasting(25),
        name="memory_forward",
    )(bounds, queries, key_rows, value_rows, row_ids)


def combine_partials(partial, heads, sources, rows):
    width = partial.shape[1] - 128
    head_dim = width // heads

    def kernel(part_ref, out_ref, log_ref, sums, tops, totals):
        i = pl.program_id(0)

        @pl.when(i == 0)
        def _():
            sums[...] = jnp.zeros_like(sums)
            tops[...] = jnp.full_like(tops, masked_score)
            totals[...] = jnp.zeros_like(totals)

        stat = part_ref[:, width:].astype(jnp.float32)
        stat = stat + pltpu.roll(stat, 128 - 16, 1) + pltpu.roll(stat, 128 - 32, 1)
        new_total = pltpu.roll(stat, 128 - heads, 1)
        top = jnp.maximum(tops[...], stat)
        old_fade, new_fade = jnp.exp(tops[...] - top), jnp.exp(stat - top)
        tops[...] = top
        totals[...] = totals[...] * old_fade + new_total * new_fade
        for head in range(heads):
            columns = slice(head * head_dim, (head + 1) * head_dim)
            sums[:, columns] = (
                sums[:, columns] * old_fade[:, head : head + 1]
                + part_ref[:, columns].astype(jnp.float32) * new_fade[:, head : head + 1]
            )

        @pl.when(i == sources - 1)
        def _():
            live = totals[...] > 0
            total = jnp.where(live, totals[...], 1.0)
            log_ref[...] = jnp.where(live, tops[...] + jnp.log(total), 0.0)
            for head in range(heads):
                columns = slice(head * head_dim, (head + 1) * head_dim)
                out_ref[:, columns] = sums[:, columns] / total[:, head : head + 1]

    return pl.pallas_call(
        kernel,
        grid=(sources,),
        in_specs=[pl.BlockSpec((rows, width + 128), lambda i: (i, 0))],
        out_specs=[
            pl.BlockSpec((rows, width), lambda i: (0, 0)),
            pl.BlockSpec((rows, 128), lambda i: (0, 0)),
        ],
        scratch_shapes=[
            pltpu.VMEM((rows, width), jnp.float32),
            pltpu.VMEM((rows, 128), jnp.float32),
            pltpu.VMEM((rows, 128), jnp.float32),
        ],
        out_shape=[
            jax.ShapeDtypeStruct((rows, width), jnp.float32),
            jax.ShapeDtypeStruct((rows, 128), jnp.float32),
        ],
        compiler_params=pltpu.CompilerParams(vmem_limit_bytes=VMEM_LIMIT),
        cost_estimate=lasting(13),
        name="combine_partials",
    )(partial)


def memory_backward(bounds, queries, grads, key_rows, value_rows, row_ids, heads, sources, rows, score_scale):
    capacity, head_dim = key_rows.shape[0] // sources, key_rows.shape[1]
    width = heads * head_dim
    span = min(384, capacity)
    chunk = math.gcd(rows, 32)

    def kernel(bounds_ref, q_ref, g_ref, k_ref, v_ref, id_ref, out_ref, sums, stats, raw, products, slopes):
        source = pl.program_id(0)
        stats[...] = joined_tile(g_ref[:, width : width + 128])

        def window(heads_here, starts, least):
            here = [pl.ds(pl.multiple_of(start, 16), span) for start in starts]
            columns = [columns_of(head, head_dim) for head in heads_here]
            for slot in range(len(starts)):
                raw[slot] = lax.dot_general(
                    q_ref[:, columns[slot]],
                    k_ref[here[slot], :],
                    contract_cols,
                    preferred_element_type=jnp.float32,
                )
                products[slot] = lax.dot_general(
                    g_ref[:, columns[slot]],
                    v_ref[here[slot], :],
                    contract_cols,
                    preferred_element_type=jnp.float32,
                )
            for slot, (head, start) in enumerate(zip(heads_here, starts)):
                lines = window_ids(id_ref, start, span)
                turned = stats[...]
                if least is not None:
                    turned = pltpu.roll(turned, 128 - head, 1)
                elif head:
                    turned = turned[:, head:]
                for at in range(0, rows, chunk):
                    some = slice(at, at + chunk)
                    mine = owned(lines, head * rows + at, chunk, start, least)
                    log, delta = turned[some, :1], turned[some, heads : heads + 1]
                    probs = jnp.exp(jnp.where(mine, raw[slot, some, :] * score_scale - log, dead_score))
                    slopes[slot, some, :] = (probs * (products[slot, some, :] - delta)).astype(
                        jnp.bfloat16
                    )
            for slot in range(len(starts)):
                found = jnp.dot(
                    slopes[slot], k_ref[here[slot], :], preferred_element_type=jnp.float32
                )
                sums[:, columns[slot]] = found if least is None else sums[:, columns[slot]] + found

        windows = [window_of(bounds_ref, source, head, heads, span, capacity) for head in range(heads)]
        window(list(range(heads)), [start for start, _ in windows], None)

        @pl.when(sum(extra for _, extra in windows) > 0)
        def _():
            @pl.loop(0, heads)
            def _(head):
                start, extra = window_of(bounds_ref, source, head, heads, span, capacity)

                @pl.loop(0, extra)
                def _(turn):
                    least = start + (turn + 1) * span
                    window([head], [jnp.minimum(least, capacity - span)], least)

        out_ref[...] = sums[...].astype(jnp.bfloat16)

    return pl.pallas_call(
        kernel,
        grid_spec=pltpu.PrefetchScalarGridSpec(
            num_scalar_prefetch=1,
            grid=(sources,),
            in_specs=[
                pl.BlockSpec((rows, width), lambda i, *_: (i, 0)),
                pl.BlockSpec((rows, width + 128), lambda i, *_: (i, 0)),
                pl.BlockSpec((capacity, head_dim), lambda i, *_: (i, 0)),
                pl.BlockSpec((capacity, head_dim), lambda i, *_: (i, 0)),
                pl.BlockSpec((1, *row_ids.shape[1:]), lambda i, *_: (i, 0, 0)),
            ],
            out_specs=pl.BlockSpec((rows, width), lambda i, *_: (i, 0)),
            scratch_shapes=[
                pltpu.VMEM((rows, width), jnp.float32),
                pltpu.VMEM((rows, 128), jnp.float32),
                pltpu.VMEM((heads, rows, span), jnp.float32),
                pltpu.VMEM((heads, rows, span), jnp.float32),
                pltpu.VMEM((heads, rows, span), jnp.bfloat16),
            ],
        ),
        out_shape=jax.ShapeDtypeStruct((sources * rows, width), jnp.bfloat16),
        compiler_params=pltpu.CompilerParams(vmem_limit_bytes=VMEM_LIMIT),
        cost_estimate=lasting(25),
        name="memory_backward",
    )(bounds, queries, grads, key_rows, value_rows, row_ids)


def remote(source, target, send_sem, recv_sem, device):
    return pltpu.make_async_remote_copy(
        src_ref=source,
        dst_ref=target,
        send_sem=send_sem,
        recv_sem=recv_sem,
        device_id={"mem": device},
        device_id_type=pl.DeviceIdType.MESH,
    )


def grid_place(depth):
    me = lax.axis_index("mem")
    layer, column = me // 4, me % 4
    beside_x = column + 1 - 2 * (column % 2)
    beside_y = column + 2 - 4 * (column // 2)
    across = 3 - column

    def index_of(step, place):
        return (layer + step + depth) % depth * 4 + place

    return me, column, beside_x, beside_y, across, index_of


def greet(devices):
    barrier = pltpu.get_barrier_semaphore()
    for device in devices:
        pl.semaphore_signal(
            barrier, inc=1, device_id={"mem": device}, device_id_type=pl.DeviceIdType.MESH
        )
    pl.semaphore_wait(barrier, len(devices))


def gather_group(block, sources, collective_id, beside):
    rows, width = block.shape
    depth, half = sources // 4, rows // 2
    slots = 2 * depth - 1
    arrays, specs, more_out, more_scratch, begin = beside
    ins, outs = len(arrays), len(more_out)

    def kernel(x_ref, *refs):
        in_refs, (out_ref, *more_refs) = refs[:ins], refs[ins : ins + 1 + outs]
        (own_sem, send, recv), scratch = refs[ins + 1 + outs : ins + 4 + outs], refs[ins + 4 + outs :]
        meanwhile = begin(in_refs, more_refs, scratch)
        me = lax.axis_index("mem")
        layer, column = me // 4, me % 4
        to_x = me + 1 - 2 * (column % 2)
        to_y = me + 2 - 4 * (column // 2)
        across = layer * 4 + 3 - column
        has_above, has_below = layer + 1 < depth, layer > 0
        barrier = pltpu.get_barrier_semaphore()

        def signal(device):
            pl.semaphore_signal(
                barrier, inc=1, device_id={"mem": device}, device_id_type=pl.DeviceIdType.MESH
            )

        signal(to_x)
        signal(to_y)
        pl.when(has_above)(lambda: signal(me + 4))
        pl.when(has_below)(lambda: signal(me - 4))
        pl.semaphore_wait(barrier, 2 + has_above.astype(jnp.int32) + has_below.astype(jnp.int32))

        def part_of(index, part):
            start = pl.multiple_of(index * rows + part * half, half)
            return out_ref.at[pl.ds(start, half), :]

        own = pltpu.make_async_copy(x_ref, out_ref.at[pl.ds(pl.multiple_of(me * rows, rows), rows), :], own_sem)
        own.start()
        sent = []

        def push(condition, source, target, kind, slot, to_slot, part, device):
            copy = remote(source, target, send.at[kind, slot, part], recv.at[kind, to_slot, part], device)
            if condition is None:
                copy.start()
            else:
                pl.when(condition)(copy.start)
            sent.append((condition, copy))

        def arrived(index, kind, slot, part):
            target = part_of(index, part)
            remote(target, target, send.at[kind, slot, part], recv.at[kind, slot, part], to_x).wait_recv()

        def up_slot(distance):
            return distance

        def down_slot(distance):
            return depth - 1 + distance

        for part in (0, 1):
            mine = x_ref.at[pl.ds(part * half, half), :]
            push(has_above, mine, part_of(me, part), 0, 0, down_slot(1), part, me + 4)
            push(has_below, mine, part_of(me, part), 1, 0, up_slot(1), part, me - 4)
            mine_y = x_ref.at[pl.ds((1 - part) * half, half), :]
            push(None, mine, part_of(me, part), 2, 0, 0, part, to_x)
            push(None, mine_y, part_of(me, 1 - part), 3, 0, 0, 1 - part, to_y)

        meanwhile()

        def pass_on(condition, step, slot):
            def go():
                arrived(to_x + step, 2, slot, 0)
                copy_a.start()
                arrived(to_y + step, 3, slot, 1)
                copy_b.start()

            source_a, source_b = part_of(to_x + step, 0), part_of(to_y + step, 1)
            copy_a = remote(source_a, source_a, send.at[4, slot, 0], recv.at[4, slot, 0], to_y)
            copy_b = remote(source_b, source_b, send.at[5, slot, 1], recv.at[5, slot, 1], to_x)
            sent.append((condition, copy_a))
            sent.append((condition, copy_b))
            if condition is None:
                go()
            else:
                pl.when(condition)(go)

        for distance in range(1, depth):
            from_above, from_below = layer + distance < depth, layer - distance >= 0

            def take(kind, back_kind, step, slot, next_slot, onward, onward_device):
                for part in (0, 1):
                    arrived(me + step, kind, slot, part)
                    here = part_of(me + step, part)
                    if next_slot is not None:
                        pl.when(onward)(
                            remote(
                                here, here, send.at[kind, slot, part], recv.at[kind, next_slot, part], onward_device
                            ).start
                        )
                    remote(here, here, send.at[2, slot, part], recv.at[2, slot, part], to_x).start()
                    remote(here, here, send.at[3, slot, part], recv.at[3, slot, part], to_y).start()

            last = distance == depth - 1
            pl.when(from_above)(
                lambda: take(
                    1, 0, 4 * distance, up_slot(distance), None if last else up_slot(distance + 1), has_below, me - 4
                )
            )
            pl.when(from_below)(
                lambda: take(
                    0, 1, -4 * distance, down_slot(distance), None if last else down_slot(distance + 1), has_above, me + 4
                )
            )
            for condition, step, slot, kind, onward in (
                (from_above, 4 * distance, up_slot(distance), 1, has_below),
                (from_below, -4 * distance, down_slot(distance), 0, has_above),
            ):
                for part in (0, 1):
                    here = part_of(me + step, part)
                    if not last:
                        sent.append((condition & onward, remote(here, here, send.at[kind, slot, part], own_sem, me)))
                    sent.append((condition, remote(here, here, send.at[2, slot, part], own_sem, to_x)))
                    sent.append((condition, remote(here, here, send.at[3, slot, part], own_sem, to_y)))
            if distance == 1:
                pass_on(None, 0, 0)
            else:
                pass_on(layer + distance - 1 < depth, 4 * (distance - 1), up_slot(distance - 1))
                pass_on(layer - distance + 1 >= 0, -4 * (distance - 1), down_slot(distance - 1))
        pass_on(layer + depth - 1 < depth, 4 * (depth - 1), up_slot(depth - 1))
        pass_on(layer - depth + 1 >= 0, -4 * (depth - 1), down_slot(depth - 1))

        def close(step, slot):
            arrived(to_x + step, 2, slot, 1)
            arrived(to_y + step, 3, slot, 0)
            arrived(across + step, 4, slot, 0)
            arrived(across + step, 5, slot, 1)

        close(0, 0)
        for distance in range(1, depth):
            pl.when(layer + distance < depth)(lambda: close(4 * distance, up_slot(distance)))
            pl.when(layer - distance >= 0)(lambda: close(-4 * distance, down_slot(distance)))
        for condition, copy in sent:
            if condition is None:
                copy.wait_send()
            else:
                pl.when(condition)(copy.wait_send)
        own.wait()

    return pl.pallas_call(
        kernel,
        in_specs=[pl.BlockSpec(memory_space=pl.ANY), *specs],
        out_specs=[pl.BlockSpec(memory_space=pl.ANY)] + [pl.BlockSpec(memory_space=pltpu.VMEM)] * outs,
        out_shape=[jax.ShapeDtypeStruct((sources * rows, width), block.dtype), *more_out],
        scratch_shapes=[
            pltpu.SemaphoreType.DMA,
            pltpu.SemaphoreType.DMA((6, slots, 2)),
            pltpu.SemaphoreType.DMA((6, slots, 2)),
            *more_scratch,
        ],
        compiler_params=pltpu.CompilerParams(
            collective_id=collective_id, has_side_effects=True, vmem_limit_bytes=VMEM_LIMIT
        ),
        cost_estimate=lasting(50),
        name="gather_group",
    )(block, *arrays)


def reduce_steps(parts_ref, sources, refs, sems, merge, pack, beside=None):
    half_a, half_b, from_x, from_y, from_z, out_x, out_y, out_z = refs
    send, recv_a, recv_b, recv_x, recv_y, recv_z = sems
    rows = parts_ref.shape[0] // sources
    depth, half = sources // 4, rows // 2
    me, column, beside_x, beside_y, across, index_of = grid_place(depth)
    to_x, to_y = index_of(0, beside_x), index_of(0, beside_y)
    order = [*range(1, depth), 0]
    queues = {"x": [], "y": [], "z": []}
    first_limit = 2 if beside is None else depth

    def piece(index, part):
        return parts_ref.at[pl.ds(pl.multiple_of(index * rows + part * half, half), half), :]

    def part_rows(part):
        return pl.ds(part * half, half)

    def push(link, source, target, kind, k, recv_sem, device, limit=2):
        queue = queues[link]
        while link != "z" and len(queue) >= limit:
            queue.pop(0).wait_send()
        copy = remote(source, target, send.at[kind, k], recv_sem, device)
        copy.start()
        queue.append(copy)

    def arrived(target, recv_sem):
        remote(target, target, send.at[0, 0], recv_sem, to_x).wait_recv()

    def plane_rest(k):
        push("x", piece(index_of(k, beside_x), 0), from_x.at[k, part_rows(0)], 2, k, recv_x.at[0, k], to_x)
        push("y", piece(index_of(k, beside_y), 1), from_y.at[k, part_rows(1)], 3, k, recv_y.at[1, k], to_y)

    def plane_merged(k):
        arrived(half_a.at[k], recv_a.at[k])
        pack(out_y.at[k], merge([piece(index_of(k, beside_y), 0), half_a.at[k]]))
        push("y", out_y.at[k], from_y.at[k, part_rows(0)], 4, k, recv_y.at[0, k], to_y)
        arrived(half_b.at[k], recv_b.at[k])
        pack(out_x.at[k], merge([piece(index_of(k, beside_x), 1), half_b.at[k]]))
        push("x", out_x.at[k], from_x.at[k, part_rows(1)], 5, k, recv_x.at[1, k], to_x)

    def column_step(k):
        for part in (0, 1):
            here = part_rows(part)
            arrived(from_x.at[k, here], recv_x.at[part, k])
            arrived(from_y.at[k, here], recv_y.at[part, k])
            if k:
                blocks = [piece(index_of(k, column), part), from_x.at[k, here], from_y.at[k, here]]
                pack(out_z.at[k, here], merge(blocks))
        if k:
            push("z", out_z.at[k], from_z.at[k], 6, k, recv_z.at[k], index_of(k, column))

    for k in order:
        far = index_of(k, across)
        push("x", piece(far, 0), half_a.at[k], 0, k, recv_a.at[k], to_x, first_limit)
        push("y", piece(far, 1), half_b.at[k], 1, k, recv_b.at[k], to_y, first_limit)
    if beside is not None:
        beside()
    for i, k in enumerate(order):
        plane_rest(k)
        plane_merged(k)
        if i:
            column_step(order[i - 1])
    column_step(order[-1])
    for k in range(1, depth):
        arrived(from_z.at[k], recv_z.at[k])
    final = []
    for part in (0, 1):
        here = part_rows(part)
        blocks = [piece(me, part), from_x.at[0, here], from_y.at[0, here]]
        final.append((here, blocks + [from_z.at[k, here] for k in range(1, depth)]))
    return final, [copy for queue in queues.values() for copy in queue]


def reduce_scratch(rows, width, dtype, sources):
    depth, half = sources // 4, rows // 2

    def slots(size):
        return pltpu.VMEM((depth, size, width), dtype)

    refs = [slots(half), slots(half), slots(rows), slots(rows), slots(rows)]
    refs += [slots(half), slots(half), slots(rows)]
    sems = [pltpu.SemaphoreType.DMA((7, depth))]
    sems += [pltpu.SemaphoreType.DMA((depth,))] * 2
    sems += [pltpu.SemaphoreType.DMA((2, depth))] * 2
    sems += [pltpu.SemaphoreType.DMA((depth,))]
    return refs, sems


def run_alone(name, beside):
    arrays, specs, out_shape, scratch, begin = beside
    ins, outs = len(arrays), len(out_shape)

    def kernel(*refs):
        begin(refs[:ins], refs[ins : ins + outs], refs[ins + outs :])()

    return pl.pallas_call(
        kernel,
        in_specs=specs,
        out_specs=[pl.BlockSpec(memory_space=pltpu.VMEM)] * outs,
        out_shape=out_shape,
        scratch_shapes=scratch,
        compiler_params=pltpu.CompilerParams(vmem_limit_bytes=VMEM_LIMIT),
        cost_estimate=lasting(8),
        name=name,
    )(*arrays)


def reduce_group(parts, sources, collective_id, merge, pack, finish, out_shape, beside):
    rows, width = parts.shape[0] // sources, parts.shape[1]
    depth = sources // 4
    arrays, specs, more_out, more_scratch, begin = beside
    ref_shapes, sem_shapes = reduce_scratch(rows, width, parts.dtype, sources)
    sizes = [len(arrays), len(out_shape), len(more_out), len(ref_shapes), len(sem_shapes), len(more_scratch)]

    def kernel(parts_ref, *refs):
        groups, at = [], 0
        for size in sizes:
            groups.append(refs[at : at + size])
            at += size
        ins, out_refs, more_refs, steps_refs, steps_sems, scratch = groups
        meanwhile = begin(ins, more_refs, scratch)
        me, column, beside_x, beside_y, across, index_of = grid_place(depth)
        greet(
            [index_of(0, beside_x), index_of(0, beside_y)]
            + [index_of(-k, column) for k in range(1, depth)]
        )
        final, still_open = reduce_steps(
            parts_ref, sources, steps_refs, steps_sems, merge, pack, meanwhile
        )
        for here, blocks in final:
            finish([out.at[here] for out in out_refs], merge(blocks))
        for copy in still_open:
            copy.wait_send()

    vmem = pl.BlockSpec(memory_space=pltpu.VMEM)
    return pl.pallas_call(
        kernel,
        in_specs=[vmem, *specs],
        out_specs=[vmem] * (len(out_shape) + len(more_out)),
        out_shape=[*out_shape, *more_out],
        scratch_shapes=[*ref_shapes, *sem_shapes, *more_scratch],
        compiler_params=pltpu.CompilerParams(
            collective_id=collective_id, has_side_effects=True, vmem_limit_bytes=VMEM_LIMIT
        ),
        cost_estimate=lasting(50),
        name="reduce_group",
    )(parts, *arrays)


def sum_blocks(parts, sources, collective_id, beside):
    rows, width = parts.shape[0] // sources, parts.shape[1]

    def merge(blocks):
        total = blocks[0][...].astype(jnp.float32)
        for block in blocks[1:]:
            total = total + block[...].astype(jnp.float32)
        return total

    def pack(target, total):
        target[...] = total.astype(parts.dtype)

    def finish(targets, total):
        targets[0][...] = total

    out_shape = [jax.ShapeDtypeStruct((rows, width), jnp.float32)]
    return reduce_group(parts, sources, collective_id, merge, pack, finish, out_shape, beside)


def merge_partials(parts, sources, collective_id, heads, beside):
    rows, width = parts.shape[0] // sources, parts.shape[1] - 128
    head_dim = width // heads

    def merge(blocks):
        stats = []
        for block in blocks:
            stat = block[:, width:].astype(jnp.float32)
            stats.append(stat + pltpu.roll(stat, 128 - 16, 1) + pltpu.roll(stat, 128 - 32, 1))
        top = stats[0]
        for stat in stats[1:]:
            top = jnp.maximum(top, stat)
        fades = [jnp.exp(stat - top) for stat in stats]
        total = sum(fade * pltpu.roll(stat, 128 - heads, 1) for fade, stat in zip(fades, stats))
        sums = []
        for head in range(heads):
            columns = slice(head * head_dim, (head + 1) * head_dim)
            sums.append(
                sum(
                    block[:, columns].astype(jnp.float32) * fade[:, head : head + 1]
                    for block, fade in zip(blocks, fades)
                )
            )
        return sums, top, total

    def pack(target, merged):
        sums, top, total = merged
        for head in range(heads):
            target[:, head * head_dim : (head + 1) * head_dim] = sums[head].astype(parts.dtype)
        lane = lax.broadcasted_iota(jnp.int32, top.shape, 1)
        stat = jnp.where(lane < heads, top, jnp.where(lane < 16, pltpu.roll(total, heads, 1), 0.0))
        target[:, width:] = triple(stat + pltpu.roll(stat, 16, 1) + pltpu.roll(stat, 32, 1))

    def finish(targets, merged):
        sums, top, total = merged
        live = total > 0
        total = jnp.where(live, total, 1.0)
        targets[1][...] = jnp.where(live, top + jnp.log(total), 0.0)
        for head in range(heads):
            targets[0][:, head * head_dim : (head + 1) * head_dim] = sums[head] / total[:, head : head + 1]

    out_shape = [
        jax.ShapeDtypeStruct((rows, width), jnp.float32),
        jax.ShapeDtypeStruct((rows, 128), jnp.float32),
    ]
    return reduce_group(parts, sources, collective_id, merge, pack, finish, out_shape, beside)


def scattered(halves):
    return lax.psum_scatter(halves, "mem", scatter_dimension=0, tiled=True)


def whole_grads(both, widths):
    both = both.astype(jnp.float32)
    grads, at = [], 0
    for size in widths:
        half = size // 2
        grads.append(jnp.concatenate([both[0, :, at : at + half], both[1, :, at : at + half]], 1))
        at += half
    return grads


def lane_tile(columns, rows):
    lane = lax.broadcasted_iota(jnp.int32, (rows, 128), 1)
    tile = jnp.zeros((rows, 128), jnp.float32)
    for i, column in enumerate(columns):
        tile = jnp.where(lane == i, column, tile)
    return tile


def split_tile(tile):
    lane = lax.broadcasted_iota(jnp.int32, tile.shape, 1)
    kept = jnp.where(lane < 32, tile, 0.0)
    kept = kept + pltpu.roll(kept, 32, 1) + pltpu.roll(kept, 64, 1)
    high = kept.astype(jnp.bfloat16).astype(jnp.float32)
    middle = (kept - high).astype(jnp.bfloat16).astype(jnp.float32)
    low = kept - high - middle
    part = lane // 32
    return jnp.where(part == 0, high, jnp.where(part == 1, middle, low)).astype(jnp.bfloat16)


def joined_tile(tile):
    tile = tile.astype(jnp.float32)
    return tile + pltpu.roll(tile, 128 - 32, 1) + pltpu.roll(tile, 128 - 64, 1)


def slanted(base, rows):
    return pltpu.roll(jnp.broadcast_to(base, (rows, base.shape[1])), 0, 1, stride=1, stride_axis=0)


def local_forward(base, book_column, book_row, own, halos, heads, score_scale):
    rows, width = own.shape[0], own.shape[1] // 3
    head_dim = width // heads
    count = len(halos) + 1

    def begin(ins, outs, scratch):
        base_ref, column_ref, row_ref, own_ref, *halo_refs = ins
        out_ref, log_ref = outs

        def run():
            same = column_ref[:, :1] == row_ref[:1, :]
            logs = []
            for head in range(heads):
                columns = slice(head * head_dim, (head + 1) * head_dim)
                above = slice(width + head * head_dim, width + (head + 1) * head_dim)
                twice = slice(2 * width + head * head_dim, 2 * width + (head + 1) * head_dim)
                keys = [ref[:, columns] for ref in halo_refs] + [own_ref[:, above]]
                values = [ref[:, above] for ref in halo_refs] + [own_ref[:, twice]]
                q = own_ref[:, columns]
                raw = [
                    lax.dot_general(q, k, contract_cols, preferred_element_type=jnp.float32) for k in keys
                ]
                bias = slanted(base_ref[head : head + 1, :], rows)[:, : count * rows]
                scores = jnp.concatenate(raw, axis=1) * score_scale + bias
                scores = jnp.where(same, scores, masked_score)
                top = jnp.max(scores, axis=1, keepdims=True)
                weights = jnp.exp(scores - top)
                total = jnp.sum(weights, axis=1, keepdims=True)
                weights = (weights / total).astype(jnp.bfloat16)
                out_ref[:, columns] = sum(
                    jnp.dot(
                        weights[:, i * rows : (i + 1) * rows], v, preferred_element_type=jnp.float32
                    )
                    for i, v in enumerate(values)
                )
                logs.append(top + jnp.log(total))
            log_ref[...] = lane_tile(logs, rows)

        return run

    arrays = [base, book_column, book_row, own, *halos]
    specs = [pl.BlockSpec(memory_space=pltpu.VMEM)] * len(arrays)
    out_shape = [
        jax.ShapeDtypeStruct((rows, width), jnp.float32),
        jax.ShapeDtypeStruct((rows, 128), jnp.float32),
    ]
    return arrays, specs, out_shape, [], begin


def sent_gradients(d_mixed, memory_out, local_out, mem_log, local_log, share, heads):
    rows, width = d_mixed.shape
    head_dim = width // heads

    def kernel(mix_ref, mem_ref, loc_ref, mem_log_ref, log_ref, share_ref, gate_ref, sent_ref):
        mem_deltas, deltas = [], []
        for head in range(heads):
            columns = slice(head * head_dim, (head + 1) * head_dim)
            share_here = share_ref[head]
            d_mix, mem_here, loc_here = mix_ref[:, columns], mem_ref[:, columns], loc_ref[:, columns]
            d_mem = (share_here * d_mix).astype(jnp.bfloat16)
            d_out = ((1.0 - share_here) * d_mix).astype(jnp.bfloat16)
            sent_ref[:, columns] = d_mem
            mem_deltas.append(jnp.sum(d_mem.astype(jnp.float32) * mem_here, axis=1, keepdims=True))
            deltas.append(jnp.sum(d_out.astype(jnp.float32) * loc_here, axis=1, keepdims=True))
            gate_ref[head : head + 1, :] = jnp.sum(
                d_mix * (mem_here - loc_here), axis=0, keepdims=True
            )
        mem_logs = [mem_log_ref[:, head : head + 1] for head in range(heads)]
        logs = [log_ref[:, head : head + 1] for head in range(heads)]
        sent_ref[:, width:] = split_tile(lane_tile(mem_logs + mem_deltas + logs + deltas, rows))

    vmem = pl.BlockSpec(memory_space=pltpu.VMEM)
    return pl.pallas_call(
        kernel,
        in_specs=[vmem] * 5 + [pl.BlockSpec(memory_space=pltpu.SMEM)],
        out_shape=[
            jax.ShapeDtypeStruct((heads, head_dim), jnp.float32),
            jax.ShapeDtypeStruct((rows, width + 128), jnp.bfloat16),
        ],
        compiler_params=pltpu.CompilerParams(vmem_limit_bytes=VMEM_LIMIT),
        cost_estimate=lasting(3),
        name="sent_gradients",
    )(d_mixed, memory_out, local_out, mem_log, local_log, share)


def local_queries(
    base, book_column, book_row, own, halos, d_mixed, local_out, local_log, share, heads, score_scale
):
    rows, width = d_mixed.shape
    head_dim = width // heads
    count = len(halos) + 1
    span = base.shape[1]

    def begin(ins, outs, scratch):
        base_ref, column_ref, row_ref, own_ref, mix_ref, loc_ref, log_ref, share_ref, *halo_refs = ins
        dq_ref, diagonal_ref = outs

        def run():
            same = column_ref[:, :1] == row_ref[:1, :]
            turned = (
                lax.broadcasted_iota(jnp.int32, (rows, rows), 0)
                + lax.broadcasted_iota(jnp.int32, (rows, rows), 1)
                == rows - 1
            ).astype(jnp.bfloat16)
            for head in range(heads):
                columns = slice(head * head_dim, (head + 1) * head_dim)
                above = slice(width + head * head_dim, width + (head + 1) * head_dim)
                twice = slice(2 * width + head * head_dim, 2 * width + (head + 1) * head_dim)
                keys = [ref[:, columns] for ref in halo_refs] + [own_ref[:, above]]
                values = [ref[:, above] for ref in halo_refs] + [own_ref[:, twice]]
                q = own_ref[:, columns]
                d_out = ((1.0 - share_ref[head]) * mix_ref[:, columns]).astype(jnp.bfloat16)
                delta = jnp.sum(
                    d_out.astype(jnp.float32) * loc_ref[:, columns], axis=1, keepdims=True
                )
                raw = [
                    lax.dot_general(q, k, contract_cols, preferred_element_type=jnp.float32)
                    for k in keys
                ]
                bias = slanted(base_ref[head : head + 1, :], rows)[:, : count * rows]
                scores = jnp.concatenate(raw, axis=1) * score_scale + bias
                probs = jnp.exp(jnp.where(same, scores - log_ref[:, head : head + 1], masked_score))
                products = [
                    lax.dot_general(d_out, v, contract_cols, preferred_element_type=jnp.float32)
                    for v in values
                ]
                slopes = (probs * (jnp.concatenate(products, axis=1) - delta)).astype(jnp.bfloat16)
                slope_blocks = [slopes[:, i * rows : (i + 1) * rows] for i in range(count)]
                dq_ref[:, columns] = score_scale * sum(
                    jnp.dot(s, k, preferred_element_type=jnp.float32)
                    for s, k in zip(slope_blocks, keys)
                )
                mirrored = [
                    jnp.dot(s, turned, preferred_element_type=jnp.float32) for s in slope_blocks[::-1]
                ]
                mirrored.append(jnp.zeros((rows, span - count * rows), jnp.float32))
                leaned = pltpu.roll(jnp.concatenate(mirrored, axis=1), 0, 1, stride=1, stride_axis=0)
                diagonal_ref[head : head + 1, :] = jnp.sum(leaned, axis=0, keepdims=True)

        return run

    vmem = pl.BlockSpec(memory_space=pltpu.VMEM)
    arrays = [base, book_column, book_row, own, d_mixed, local_out, local_log, share, *halos]
    specs = [vmem] * 7 + [pl.BlockSpec(memory_space=pltpu.SMEM)] + [vmem] * len(halos)
    out_shape = [
        jax.ShapeDtypeStruct((rows, width), jnp.float32),
        jax.ShapeDtypeStruct((heads, span), jnp.float32),
    ]
    return arrays, specs, out_shape, [], begin


def local_keys(base, book_column, book_row, own, queries, sent, ratio, count, heads, score_scale):
    rows, width = own.shape[0], own.shape[1] // 3
    head_dim = width // heads
    groups = queries.shape[0] // rows

    def begin(ins, outs, scratch):
        base_ref, column_ref, row_ref, own_ref, ratio_ref, queries_ref, sent_ref = ins
        (out_ref,) = outs
        queries_here, sent_here, sems = scratch
        copies = []
        for i in range(count):
            index = jnp.minimum(lax.axis_index("mem") + i, groups - 1)
            there = pl.ds(pl.multiple_of(index * rows, rows), rows)
            copies.append(
                pltpu.make_async_copy(queries_ref.at[there, :], queries_here.at[i], sems.at[0, i])
            )
            copies.append(pltpu.make_async_copy(sent_ref.at[there, :], sent_here.at[i], sems.at[1, i]))
        for copy in copies:
            copy.start()

        def run():
            for copy in copies:
                copy.wait()
            same = column_ref[:, :1] == row_ref[:1, :]
            stats = jnp.concatenate([joined_tile(sent_here[i, :, width:]).T for i in range(count)], axis=1)
            for head in range(heads):
                columns = slice(head * head_dim, (head + 1) * head_dim)
                above = slice(width + head * head_dim, width + (head + 1) * head_dim)
                twice = slice(2 * width + head * head_dim, 2 * width + (head + 1) * head_dim)
                k, v = own_ref[:, above], own_ref[:, twice]
                qs = [queries_here[i, :, columns] for i in range(count)]
                gs = [
                    (sent_here[i, :, columns].astype(jnp.float32) * ratio_ref[head]).astype(jnp.bfloat16)
                    for i in range(count)
                ]
                raw = [
                    lax.dot_general(k, q, contract_cols, preferred_element_type=jnp.float32) for q in qs
                ]
                bias = slanted(base_ref[head : head + 1, :], rows)[:, : count * rows]
                scores = jnp.concatenate(raw, axis=1) * score_scale + bias
                log = stats[2 * heads + head : 2 * heads + head + 1, :]
                delta = stats[3 * heads + head : 3 * heads + head + 1, :]
                probs = jnp.exp(jnp.where(same, scores - log, masked_score))
                products = [
                    lax.dot_general(v, g, contract_cols, preferred_element_type=jnp.float32) for g in gs
                ]
                slopes = (probs * (jnp.concatenate(products, axis=1) - delta)).astype(jnp.bfloat16)
                weights = probs.astype(jnp.bfloat16)
                blocks = [slice(i * rows, (i + 1) * rows) for i in range(count)]
                d_key = sum(
                    jnp.dot(slopes[:, b], q, preferred_element_type=jnp.float32) for b, q in zip(blocks, qs)
                )
                d_value = sum(
                    jnp.dot(weights[:, b], g, preferred_element_type=jnp.float32)
                    for b, g in zip(blocks, gs)
                )
                out_ref[:, columns] = (d_key * score_scale).astype(jnp.bfloat16)
                out_ref[:, above] = d_value.astype(jnp.bfloat16)

        return run

    vmem, anywhere = pl.BlockSpec(memory_space=pltpu.VMEM), pl.BlockSpec(memory_space=pl.ANY)
    arrays = [base, book_column, book_row, own, ratio, queries, sent]
    specs = [vmem] * 4 + [pl.BlockSpec(memory_space=pltpu.SMEM), anywhere, anywhere]
    scratch = [
        pltpu.VMEM((count, rows, width), jnp.bfloat16),
        pltpu.VMEM((count, rows, width + 128), jnp.bfloat16),
        pltpu.SemaphoreType.DMA((2, count)),
    ]
    return arrays, specs, [jax.ShapeDtypeStruct((rows, 2 * width), jnp.bfloat16)], scratch, begin


def feed_forward(normed_mid, cotangent, up_weight, down_weight):
    rows, width = normed_mid.shape
    hidden = up_weight.shape[1]
    block = math.gcd(hidden, 1024)

    def kernel(mid_ref, cot_ref, up_ref, down_ref, act_ref, d_up_ref, branch_ref, d_mid_ref):
        first = pl.program_id(0) == 0
        up = jnp.dot(mid_ref[...], up_ref[...], preferred_element_type=jnp.float32)
        d_act = jnp.dot(cot_ref[...], down_ref[...], preferred_element_type=jnp.float32)
        below = 0.5 * (1.0 + lax.erf(up * math.sqrt(0.5)))
        density = jnp.exp(-0.5 * up * up) * (1.0 / math.sqrt(2.0 * math.pi))
        act = (up * below).astype(jnp.bfloat16)
        d_up = (d_act * (below + up * density)).astype(jnp.bfloat16)
        act_ref[...] = act
        d_up_ref[...] = d_up
        branch = lax.dot_general(act, down_ref[...], contract_cols, preferred_element_type=jnp.float32)
        d_mid = lax.dot_general(d_up, up_ref[...], contract_cols, preferred_element_type=jnp.float32)
        branch_ref[...] = jnp.where(first, branch, branch_ref[...] + branch)
        d_mid_ref[...] = jnp.where(first, d_mid, d_mid_ref[...] + d_mid)

    whole = pl.BlockSpec((rows, width), lambda i: (0, 0))
    weight = pl.BlockSpec((width, block), lambda i: (0, i))
    middle = pl.BlockSpec((rows, block), lambda i: (0, i))
    return pl.pallas_call(
        kernel,
        grid=(hidden // block,),
        in_specs=[whole, whole, weight, weight],
        out_specs=[middle, middle, whole, whole],
        out_shape=[
            jax.ShapeDtypeStruct((rows, hidden), jnp.bfloat16),
            jax.ShapeDtypeStruct((rows, hidden), jnp.bfloat16),
            jax.ShapeDtypeStruct((rows, width), jnp.float32),
            jax.ShapeDtypeStruct((rows, width), jnp.float32),
        ],
        compiler_params=pltpu.CompilerParams(vmem_limit_bytes=VMEM_LIMIT),
        cost_estimate=lasting(15),
        name="feed_forward",
    )(normed_mid, cotangent, up_weight, down_weight)


def exchange_pairs(lefts, rights, other_lefts, other_right, send, recv):
    core = lax.axis_index("dp")
    copies, at = [], 0

    def push(source, target):
        i = len(copies)
        copy = pltpu.make_async_remote_copy(
            src_ref=source,
            dst_ref=target,
            send_sem=send.at[i],
            recv_sem=recv.at[i],
            device_id={"dp": 1 - core},
            device_id_type=pl.DeviceIdType.MESH,
        )
        copy.start()
        copies.append(copy)

    for i, (left, right) in enumerate(zip(lefts, rights)):
        half = right.shape[1] // 2
        push(left, other_lefts.at[i])
        there = pl.ds(pl.multiple_of((1 - core) * half, 128), half)
        push(right.at[:, there], other_right.at[:, pl.ds(at, half)])
        at += half
    return copies


def pair_products(lefts, rights, other_lefts, other_right, turned, store):
    core = lax.axis_index("dp")
    rows = lefts[0].shape[0]
    at = 0
    for i, (left, right) in enumerate(zip(lefts, rights)):
        half = right.shape[1] // 2
        turned[:, :rows] = left[...].T
        turned[:, rows:] = other_lefts[i].T
        block = math.gcd(half, 512)
        for column in range(0, half, block):
            kept = right[:, pl.ds(pl.multiple_of(core * half + column, 128), block)]
            both = jnp.concatenate([kept, other_right[:, at + column : at + column + block]], axis=0)
            store(
                at + column,
                jnp.dot(turned[...], both, preferred_element_type=jnp.float32).astype(jnp.bfloat16),
            )
        at += half


def pair_scratch(lefts, rights):
    rows, width = lefts[0].shape
    count = len(lefts)
    return [
        pltpu.VMEM((count, rows, width), jnp.bfloat16),
        pltpu.VMEM((rows, sum(right.shape[1] for right in rights) // 2), jnp.bfloat16),
        pltpu.VMEM((width, 2 * rows), jnp.bfloat16),
        pltpu.SemaphoreType.DMA((2 * count,)),
        pltpu.SemaphoreType.DMA((2 * count,)),
    ]


def pair_grads(lefts, rights, collective_id):
    count, width = len(lefts), lefts[0].shape[1]
    total = sum(right.shape[1] for right in rights) // 2
    block = math.gcd(*[right.shape[1] // 2 for right in rights], 512)

    def kernel(*refs):
        left_refs, right_refs, out_ref = refs[:count], refs[count : 2 * count], refs[2 * count]
        other_lefts, other_right, turned, send, recv, staged, out_sem = refs[2 * count + 1 :]
        barrier = pltpu.get_barrier_semaphore()
        partner = {"dp": 1 - lax.axis_index("dp")}
        pl.semaphore_signal(barrier, inc=1, device_id=partner, device_id_type=pl.DeviceIdType.MESH)
        pl.semaphore_wait(barrier, 1)
        copies = exchange_pairs(left_refs, right_refs, other_lefts, other_right, send, recv)
        for copy in copies:
            copy.wait_recv()
        written = []

        def store(column, value):
            slot = len(written) % 2
            if len(written) >= 2:
                written[-2].wait()
            staged[slot] = value
            copy = pltpu.make_async_copy(
                staged.at[slot], out_ref.at[:, pl.ds(column, block)], out_sem.at[slot]
            )
            copy.start()
            written.append(copy)

        pair_products(left_refs, right_refs, other_lefts, other_right, turned, store)
        for copy in written[-2:]:
            copy.wait()
        for copy in copies:
            copy.wait_send()

    vmem = pl.BlockSpec(memory_space=pltpu.VMEM)
    return pl.pallas_call(
        kernel,
        in_specs=[vmem] * (2 * count),
        out_specs=pl.BlockSpec(memory_space=pl.ANY),
        out_shape=jax.ShapeDtypeStruct((width, total), jnp.bfloat16),
        scratch_shapes=pair_scratch(lefts, rights)
        + [pltpu.VMEM((2, width, block), jnp.bfloat16), pltpu.SemaphoreType.DMA((2,))],
        compiler_params=pltpu.CompilerParams(
            collective_id=collective_id, has_side_effects=True, vmem_limit_bytes=VMEM_LIMIT
        ),
        cost_estimate=lasting(10),
        name="pair_grads",
    )(*lefts, *rights)


def input_backward(tokens, attn_gain, d_projected, qkv_weight, d_residual):
    rows, width = tokens.shape

    def begin(ins, outs, scratch):
        tokens_ref, gain_ref, d_ref, weight_ref, residual_ref = ins
        grad_ref, part_ref = outs
        weight_here, sem = scratch
        copy = pltpu.make_async_copy(weight_ref, weight_here, sem)
        copy.start()

        def run():
            copy.wait()
            d_in = lax.dot_general(
                d_ref[...], weight_here[...], contract_cols, preferred_element_type=jnp.float32
            )
            x = tokens_ref[...].astype(jnp.float32)
            scale = lax.rsqrt(jnp.mean(x * x, axis=1, keepdims=True) + eps_norm)
            wanted = d_in * gain_ref[...]
            slope = jnp.mean(x * wanted, axis=1, keepdims=True) * scale * scale * scale
            grad_ref[...] = residual_ref[...] + scale * wanted - x * slope
            part_ref[...] = jnp.sum(d_in * x * scale, axis=0, keepdims=True)

        return run

    vmem = pl.BlockSpec(memory_space=pltpu.VMEM)
    arrays = [tokens, attn_gain[None, :], d_projected, qkv_weight, d_residual]
    specs = [vmem, vmem, vmem, pl.BlockSpec(memory_space=pl.ANY), vmem]
    out_shape = [
        jax.ShapeDtypeStruct((rows, width), jnp.float32),
        jax.ShapeDtypeStruct((1, width), jnp.float32),
    ]
    scratch = [pltpu.VMEM(qkv_weight.shape, qkv_weight.dtype), pltpu.SemaphoreType.DMA]
    return arrays, specs, out_shape, scratch, begin


def spread_halves(halves, outs):
    at = 0
    for out in outs:
        half = out.shape[1] // 2
        for c in (0, 1):
            out[:, c * half : (c + 1) * half] = halves[c, :, at : at + half].astype(jnp.float32)
        at += half


def join_halves(sums, widths, collective_id):
    def kernel(sums_ref, *refs):
        outs, (both, send, recv) = refs[: len(widths)], refs[len(widths) :]
        core = lax.axis_index("dp")
        partner = {"dp": 1 - core}
        barrier = pltpu.get_barrier_semaphore()
        pl.semaphore_signal(barrier, inc=1, device_id=partner, device_id_type=pl.DeviceIdType.MESH)
        pl.semaphore_wait(barrier, 1)
        copy = pltpu.make_async_remote_copy(
            src_ref=sums_ref,
            dst_ref=both.at[core],
            send_sem=send,
            recv_sem=recv,
            device_id=partner,
            device_id_type=pl.DeviceIdType.MESH,
        )
        copy.start()
        both[core] = sums_ref[...]
        copy.wait()
        spread_halves(both, outs)

    vmem = pl.BlockSpec(memory_space=pltpu.VMEM)
    return pl.pallas_call(
        kernel,
        in_specs=[vmem],
        out_specs=[vmem] * len(widths),
        out_shape=[jax.ShapeDtypeStruct((sums.shape[0], size), jnp.float32) for size in widths],
        scratch_shapes=[
            pltpu.VMEM((2, *sums.shape), sums.dtype),
            pltpu.SemaphoreType.DMA,
            pltpu.SemaphoreType.DMA,
        ],
        compiler_params=pltpu.CompilerParams(
            collective_id=collective_id, has_side_effects=True, vmem_limit_bytes=VMEM_LIMIT
        ),
        cost_estimate=lasting(5),
        name="join_halves",
    )(sums)


def finish_grads(lefts, rights, small, sources, collective_id, beside):
    width, total = lefts[0].shape[1], sum(right.shape[1] for right in rights) // 2
    rows = width // sources
    count = len(lefts)
    late_widths = [right.shape[1] for right in rights]
    arrays, specs, more_out, more_scratch, begin = beside
    mesh_type = pl.DeviceIdType.MESH
    ref_shapes, sem_shapes = reduce_scratch(rows, total, jnp.bfloat16, sources)
    pair_shapes = pair_scratch(lefts, rights)
    sizes = [count, count, len(arrays), 1, count, 1, len(more_out)]
    sizes += [len(ref_shapes), len(sem_shapes), len(pair_shapes), len(more_scratch), 9]

    def kernel(*refs):
        groups, at = [], 0
        for size in sizes:
            groups.append(refs[at : at + size])
            at += size
        left_refs, right_refs, ins, (small_ref,), late_outs, (small_out,), more_refs = groups[:7]
        steps_refs, steps_sems, (other_lefts, other_right, turned, pair_send, pair_recv), scratch, own = groups[7:]
        parts, late, small_mine, smalls, core_small, small_send, small_recv, core_send, core_recv = own
        meanwhile = begin(ins, more_refs, scratch)
        me, core = lax.axis_index("mem"), lax.axis_index("dp")
        barrier = pltpu.get_barrier_semaphore()
        peers = [lax.rem(me + k, sources) for k in range(1, sources)]
        for peer in peers:
            pl.semaphore_signal(barrier, inc=1, device_id={"mem": peer}, device_id_type=mesh_type)
        pl.semaphore_signal(barrier, inc=1, device_id={"dp": 1 - core}, device_id_type=mesh_type)
        pl.semaphore_wait(barrier, sources)

        def merge(blocks):
            total = blocks[0][...].astype(jnp.float32)
            for block in blocks[1:]:
                total = total + block[...].astype(jnp.float32)
            return total

        def pack(target, total):
            target[...] = total.astype(jnp.bfloat16)

        def across_cores(source, target, i):
            copy = pltpu.make_async_remote_copy(
                src_ref=source,
                dst_ref=target,
                send_sem=core_send.at[i],
                recv_sem=core_recv.at[i],
                device_id={"dp": 1 - core},
                device_id_type=mesh_type,
            )
            copy.start()
            return copy

        pair_copies = exchange_pairs(
            left_refs, right_refs, other_lefts, other_right, pair_send, pair_recv
        )
        for copy in pair_copies:
            copy.wait_recv()

        def store(column, value):
            parts[:, column : column + value.shape[1]] = value

        pair_products(left_refs, right_refs, other_lefts, other_right, turned, store)
        small_copies = [
            remote(small_mine, smalls.at[me], small_send.at[i], small_recv.at[me], peer)
            for i, peer in enumerate(peers)
        ]

        def between():
            meanwhile()
            small_mine[...] = small_ref[...]
            for i in range(width // 128):
                small_mine[i : i + 1, :] = more_refs[-1][:, i * 128 : (i + 1) * 128]
            smalls[me] = small_mine[...]
            for copy in small_copies:
                copy.start()

        final, still_open = reduce_steps(parts, sources, steps_refs, steps_sems, merge, pack, between)
        for here, blocks in final:
            late[core, here] = merge(blocks).astype(jnp.bfloat16)
        late_copy = across_cores(late.at[core], late.at[core], 0)
        for peer in peers:
            remote(
                smalls.at[peer], smalls.at[peer], small_send.at[0], small_recv.at[peer], peer
            ).wait_recv()
        group_small = smalls[0]
        for i in range(1, sources):
            group_small = group_small + smalls[i]
        core_small[0] = group_small
        small_copy = across_cores(core_small.at[0], core_small.at[1], 1)
        for copy in (late_copy, small_copy):
            copy.wait()
        spread_halves(late, late_outs)
        small_out[...] = core_small[0] + core_small[1]
        for copy in still_open + small_copies + pair_copies:
            copy.wait_send()

    vmem = pl.BlockSpec(memory_space=pltpu.VMEM)
    return pl.pallas_call(
        kernel,
        in_specs=[vmem] * (2 * count) + specs + [vmem],
        out_specs=[vmem] * (count + 1 + len(more_out)),
        out_shape=[jax.ShapeDtypeStruct((rows, size), jnp.float32) for size in late_widths]
        + [jax.ShapeDtypeStruct(small.shape, small.dtype)]
        + more_out,
        scratch_shapes=ref_shapes
        + sem_shapes
        + pair_shapes
        + more_scratch
        + [
            pltpu.VMEM((width, total), jnp.bfloat16),
            pltpu.VMEM((2, rows, total), jnp.bfloat16),
            pltpu.VMEM(small.shape, small.dtype),
            pltpu.VMEM((sources, *small.shape), small.dtype),
            pltpu.VMEM((2, *small.shape), small.dtype),
        ]
        + [pltpu.SemaphoreType.DMA((sources,))] * 2
        + [pltpu.SemaphoreType.DMA((2,))] * 2,
        compiler_params=pltpu.CompilerParams(
            collective_id=collective_id, has_side_effects=True, vmem_limit_bytes=VMEM_LIMIT
        ),
        cost_estimate=lasting(45),
        name="finish_grads",
    )(*lefts, *rights, *arrays, small)


def on_device(
    tokens,
    attn_gain,
    qkv_weight,
    out_weight,
    bias_table,
    gate_logit,
    ffn_gain,
    up_weight,
    down_weight,
    memory_keys,
    memory_values,
    book_lengths,
    slot_shard,
    slot_index,
    slot_live,
    cotangent,
):
    rows, width = tokens.shape
    heads, buckets = bias_table.shape
    head_dim = width // heads
    top_count = slot_index.shape[2]
    hidden = up_weight.shape[1]
    groups = lax.axis_size("mem")
    capacity = -(-3 * rows * heads * top_count // (2 * groups) // 128) * 128
    score_scale = 1.0 / math.sqrt(head_dim)
    repeats = W // rows
    span = W + 2 * rows
    me = lax.axis_index("mem")
    first_pos = me * rows
    lengths = book_lengths[0]
    window = jnp.arange(W + rows, dtype=jnp.int32)
    key_pos = first_pos - W + window
    key_book = jnp.where(key_pos >= 0, book_of(key_pos, lengths), -1)
    later_book = book_of(first_pos + window, lengths)
    own_book = jnp.broadcast_to(later_book[:rows, None], (rows, 128))
    key_book = jnp.broadcast_to(key_book[None, :], (8, W + rows))
    later_book = jnp.broadcast_to(later_book[None, :], (8, W + rows))
    bucket = bucket_of(jnp.arange(W, dtype=jnp.int32))
    one_hot = (bucket[:, None] == jnp.arange(buckets, dtype=jnp.int32)).astype(jnp.float32)
    offset_bias = jnp.einsum("rb,hb->hr", one_hot, bias_table, precision=lax.Precision.HIGHEST)
    after_bias = jnp.pad(offset_bias, ((0, 0), (0, span - W)), constant_values=masked_score)
    before_bias = jnp.pad(
        offset_bias[:, ::-1], ((0, 0), (1, span - W - 1)), constant_values=masked_score
    )
    tokens_f = tokens.astype(jnp.float32)
    normed_in = normed(tokens_f, attn_gain).astype(jnp.bfloat16)
    projected = jnp.dot(normed_in, qkv_weight, preferred_element_type=jnp.float32).astype(
        jnp.bfloat16
    )
    slots = memory_keys.shape[0]
    requests = place_requests(slot_shard, slot_index, slot_live, groups, capacity, slots)
    incoming = lax.all_to_all(requests, "mem", split_axis=0, concat_axis=0, tiled=True)
    keys_values, _ = lax.optimization_barrier((projected[:, width:], requests))
    halos = [passed_along(keys_values, "mem", distance) for distance in range(repeats, 0, -1)]
    index, row_ids, bounds = read_lists(incoming, heads, rows, slots)
    bounds = bounds.reshape(-1)
    key_rows, value_rows = gather_rows(
        index.reshape(-1), bounds, memory_keys, memory_values, heads, groups, capacity
    )
    all_queries = lax.all_gather(projected[:, :width], "mem", axis=0, tiled=True)
    local = local_forward(before_bias, own_book, key_book, projected, halos, heads, score_scale)
    partial = memory_forward(
        bounds,
        all_queries,
        key_rows,
        value_rows,
        row_ids,
        heads,
        groups,
        rows,
        score_scale,
    )
    if groups == 16:
        memory_out, mem_log, local_out, local_log = merge_partials(partial, groups, 1, heads, local)
    else:
        local_out, local_log = run_alone("local_forward", local)
        partial = lax.all_to_all(
            partial.reshape(groups, rows, width + 128),
            "mem",
            split_axis=0,
            concat_axis=0,
            tiled=True,
        ).reshape(groups * rows, width + 128)
        memory_out, mem_log = combine_partials(partial, heads, groups, rows)
    gate_share = jax.nn.sigmoid(gate_logit)
    share_wide = jnp.repeat(gate_share, head_dim)[None, :]
    mixed_heads = (share_wide * memory_out + (1.0 - share_wide) * local_out).astype(jnp.bfloat16)
    residual = tokens_f + jnp.dot(mixed_heads, out_weight, preferred_element_type=jnp.float32)
    normed_mid_f, norm_mid_back = jax.vjp(normed, residual, ffn_gain)
    normed_mid = normed_mid_f.astype(jnp.bfloat16)
    activated, d_up, ffn_branch, d_mid = feed_forward(normed_mid, cotangent, up_weight, down_weight)
    block_out = (residual + ffn_branch).astype(jnp.bfloat16)
    d_resid_part, ffn_gain_part = norm_mid_back(d_mid)
    d_residual = cotangent.astype(jnp.float32) + d_resid_part
    d_branch = d_residual.astype(jnp.bfloat16)
    early_halves = pair_grads(
        [mixed_heads, normed_mid, cotangent], [d_branch, d_up, activated], 5
    )
    early_sums = scattered(early_halves)
    d_after, _ = lax.optimization_barrier((d_branch, early_halves))
    d_mixed = lax.dot_general(
        d_after, out_weight, contract_cols, preferred_element_type=jnp.float32
    )
    gate_products, sent_grads = sent_gradients(
        d_mixed, memory_out, local_out, mem_log, local_log, gate_share, heads
    )
    gate_part = jnp.sum(gate_products, axis=1) * gate_share * (1.0 - gate_share)
    local = local_queries(
        before_bias,
        own_book,
        key_book,
        projected,
        halos,
        d_mixed,
        local_out,
        local_log,
        gate_share,
        heads,
        score_scale,
    )
    if groups == 16:
        all_grads, d_queries, diagonals = gather_group(sent_grads, groups, 2, local)
    else:
        all_grads = lax.all_gather(sent_grads, "mem", axis=0, tiled=True)
        d_queries, diagonals = run_alone("local_queries", local)
    bias_part = jnp.dot(diagonals[:, rows - 1 : rows - 1 + W], one_hot, precision=lax.Precision.HIGHEST)
    d_partial = memory_backward(
        bounds,
        all_queries,
        all_grads,
        key_rows,
        value_rows,
        row_ids,
        heads,
        groups,
        rows,
        score_scale,
    )
    local = local_keys(
        after_bias,
        own_book,
        later_book,
        projected,
        all_queries,
        all_grads,
        (1.0 - gate_share) / gate_share,
        repeats + 1,
        heads,
        score_scale,
    )
    if groups == 16:
        d_partial, d_keys_values = sum_blocks(d_partial, groups, 3, local)
    else:
        (d_keys_values,) = run_alone("local_keys", local)
        d_partial, d_keys_values = lax.optimization_barrier((d_partial, d_keys_values))
        d_partial = jnp.sum(
            lax.all_to_all(
                d_partial.reshape(groups, rows, width), "mem", split_axis=0, concat_axis=0, tiled=True
            ).astype(jnp.float32),
            axis=0,
        )
    d_queries = (d_queries + d_partial * score_scale).astype(jnp.bfloat16)
    d_projected = jnp.concatenate([d_queries, d_keys_values], axis=1)
    beside = input_backward(tokens, attn_gain, d_projected, qkv_weight, d_residual)
    small = jnp.concatenate([ffn_gain_part, bias_part.reshape(-1), gate_part], axis=0)
    small = jnp.pad(small, (width, -small.shape[0] % 1024)).reshape(-1, 128)
    early_widths = [width, hidden, hidden]
    if groups == 16:
        qkv_grad, small, tokens_grad, _ = finish_grads(
            [normed_in], [d_projected], small, groups, 4, beside
        )
        early_sums, small = lax.optimization_barrier((early_sums, small))
        out_grad, up_grad, down_grad = join_halves(early_sums, early_widths, 7)
    else:
        tokens_grad, attn_gain_part = run_alone("input_backward", beside)
        late_halves = pair_grads([normed_in], [d_projected], 6)
        late_halves, early_sums = lax.optimization_barrier((late_halves, early_sums))
        late_both = lax.all_gather(scattered(late_halves), "dp", axis=0)
        early_both = lax.all_gather(early_sums, "dp", axis=0)
        small = lax.psum(small.at[: width // 128].set(attn_gain_part.reshape(-1, 128)), ("dp", "mem"))
        out_grad, up_grad, down_grad = whole_grads(early_both, early_widths)
        qkv_grad = whole_grads(late_both, [3 * width])[0]
    small = small.reshape(-1)
    at_bias = 2 * width + heads * buckets
    return (
        block_out,
        tokens_grad,
        qkv_grad,
        out_grad,
        up_grad,
        down_grad,
        small[:width],
        small[width : 2 * width],
        small[2 * width : at_bias].reshape(heads, buckets),
        small[at_bias : at_bias + heads],
    )


def solution(mesh):
    in_specs = (
        P(("dp", "mem"), None),
        P(),
        P(),
        P(),
        P(),
        P(),
        P(),
        P(),
        P(),
        P("mem", None),
        P("mem", None),
        P("dp", None),
        P(("dp", "mem"), None, None, None),
        P(("dp", "mem"), None, None),
        P(("dp", "mem"), None, None),
        P(("dp", "mem"), None),
    )
    out_specs = (
        P(("dp", "mem"), None),
        P(("dp", "mem"), None),
        P("mem", None),
        P("mem", None),
        P("mem", None),
        P("mem", None),
        P(),
        P(),
        P(),
        P(),
    )
    return jax.shard_map(
        on_device, mesh=mesh, in_specs=in_specs, out_specs=out_specs, check_vma=False
    )
```

```python
import math

import jax
import jax.numpy as jnp
from jax import lax
from jax.experimental import pallas as pl
from jax.experimental.pallas import tpu as pltpu
from jax.sharding import PartitionSpec as P

W = 512
VMEM_LIMIT = 56 * 1024 * 1024


eps_norm = 1e-06
bucket_edges = tuple((math.ceil(16 * 8 ** (edge_step / 16)) for edge_step in range(1, 16)))
masked_score = -1e30
dead_score = -10000.0
contract_rows = (((0,), (0,)), ((), ()))
contract_cols = (((1,), (1,)), ((), ()))


def passed_along(value, axis, by):
    size = lax.axis_size(axis)
    pairs = [(i, i + by) for i in range(size) if 0 <= i + by < size]
    return lax.ppermute(value, axis, pairs)


def bucket_of(offset):
    past_edges = sum(((offset >= edge_pos).astype(jnp.int32) for edge_pos in bucket_edges))
    return jnp.where(offset < 16, offset, 16 + past_edges)


def normed(values, gain_vec):
    return (
        values * lax.rsqrt(jnp.mean(values * values, axis=-1, keepdims=True) + eps_norm) * gain_vec
    )


def place_requests(slot_shard, slot_index, slot_live, owners, capacity, slots):
    rows, heads, top_count = slot_index.shape
    entries, empty = rows * heads * top_count, heads * rows * slots
    if (owners + 1) * empty >= 2**31:
        raise ValueError("codes exceed int32")
    row_of = (
        jnp.arange(heads, dtype=jnp.int32)[None, :] * rows
        + jnp.arange(rows, dtype=jnp.int32)[:, None]
    )
    owner = jnp.where(slot_live > 0, slot_shard[..., 0], owners)
    codes = owner * empty + row_of[:, :, None] * slots + slot_index
    codes = lax.sort(codes.reshape(-1), is_stable=False)
    ends = jnp.sum(
        (codes[None, :] < (jnp.arange(owners, dtype=jnp.int32) + 1)[:, None] * empty).astype(jnp.int32),
        axis=1,
    )
    starts = jnp.concatenate([jnp.zeros((1,), jnp.int32), ends[:-1]])
    tall = -(-entries // 128)
    codes = jnp.pad(codes, (0, tall * 128 - entries)).reshape(tall, 128)
    long = capacity // 128

    def kernel(starts_ref, ends_ref, codes_ref, lists_ref, padded):
        padded[:tall, :] = codes_ref[...]
        padded[tall:, :] = jnp.zeros((long + 8, 128), jnp.int32)
        lane = lax.broadcasted_iota(jnp.int32, (long, 128), 1)
        place = lax.broadcasted_iota(jnp.int32, (long, 128), 0) * 128 + lane

        @pl.loop(0, owners)
        def _(i):
            start, end = starts_ref[i], ends_ref[i]
            shift = start % 128
            lines = padded[pl.ds(start // 128, long + 1), :]
            turned = pltpu.roll(lines, (128 - shift) % 128, 1)
            joined = jnp.where(lane < 128 - shift, turned[:long], turned[1:])
            lists_ref[i] = jnp.where(place < end - start, joined - i * empty, empty)

    return pl.pallas_call(
        kernel,
        in_specs=[pl.BlockSpec(memory_space=pltpu.SMEM)] * 2 + [pl.BlockSpec(memory_space=pltpu.VMEM)],
        out_shape=jax.ShapeDtypeStruct((owners, long, 128), jnp.int32),
        scratch_shapes=[pltpu.VMEM((tall + long + 8, 128), jnp.int32)],
        cost_estimate=lasting(3),
        name="make_lists",
    )(starts, ends, codes)


def read_lists(incoming, heads, rows, slots):
    sources, long, _ = incoming.shape

    def kernel(lists_ref, index_ref, ids_ref, bounds_ref):
        lane = lax.broadcasted_iota(jnp.int32, (1, 128), 1)

        def read(source):
            codes = lists_ref[source]
            ids = lax.div(codes, slots)
            index = lax.div(ids, rows) * slots + lax.rem(codes, slots)
            index_ref[source] = jnp.where(ids < heads * rows, index, 0)
            ids_ref[source, :long, :] = ids
            ids_ref[source, long:, :] = jnp.full((1, 128), heads * rows, jnp.int32)
            bounds = jnp.zeros((1, 128), jnp.int32)
            for head in range(1, heads + 1):
                below = jnp.sum(
                    jnp.where(codes < head * rows * slots, 1.0, 0.0), axis=0, keepdims=True
                )
                below = jnp.sum(below, axis=1, keepdims=True).astype(jnp.int32)
                bounds = jnp.where(lane == head, below, bounds)
            bounds_ref[pl.ds(source, 1), :] = bounds

        if sources > 16:
            pl.loop(0, sources)(read)
        else:
            for source in range(sources):
                read(source)

    return pl.pallas_call(
        kernel,
        out_shape=[
            jax.ShapeDtypeStruct((sources, long, 128), jnp.int32),
            jax.ShapeDtypeStruct((sources, long + 1, 128), jnp.int32),
            jax.ShapeDtypeStruct((sources, 128), jnp.int32),
        ],
        cost_estimate=lasting(3),
        name="read_lists",
    )(incoming)


def gather_rows(index, bounds, memory_keys, memory_values, heads, sources, capacity):
    slots, width = memory_keys.shape
    head_dim = width // heads
    step, part = 128, 16

    def kernel(index_ref, bounds_ref, keys, values, out_keys, out_values, key_table, value_table, key_rows, value_rows):
        i = pl.program_id(0)

        @pl.when(i < heads)
        def _():
            place = pl.ds(pl.multiple_of(i * slots, slots), slots)
            key_table[place, :] = keys[...].astype(jnp.float32)
            value_table[place, :] = values[...].astype(jnp.float32)

        @pl.when(i >= heads)
        def _():
            source = i - heads

            used = (bounds_ref[source * 128 + heads] + step - 1) // step

            def store(group):
                for at in range(0, step, part):
                    here = pl.ds(pl.multiple_of(group * step, step) + at, part)
                    out_keys[here, :] = key_rows[at : at + part, :].astype(jnp.bfloat16)
                    out_values[here, :] = value_rows[at : at + part, :].astype(jnp.bfloat16)

            @pl.loop(0, used)
            def _(group):
                store(jnp.maximum(group - 1, 0))
                first = source * capacity + group * step
                for u in range(step):
                    row = index_ref[first + u]
                    key_rows[u : u + 1, :] = key_table[pl.ds(row, 1), :]
                    value_rows[u : u + 1, :] = value_table[pl.ds(row, 1), :]

            pl.when(used > 0)(lambda: store(used - 1))

            @pl.loop(used, capacity // step)
            def _(group):
                here = pl.ds(pl.multiple_of(group * step, step), step)
                out_keys[here, :] = jnp.zeros((step, head_dim), jnp.bfloat16)
                out_values[here, :] = jnp.zeros((step, head_dim), jnp.bfloat16)

    table_spec = pl.BlockSpec((slots, head_dim), lambda i, *_: (0, jnp.minimum(i, heads - 1)))
    out_spec = pl.BlockSpec((capacity, head_dim), lambda i, *_: (jnp.maximum(i - heads, 0), 0))
    out_shape = jax.ShapeDtypeStruct((sources * capacity, head_dim), jnp.bfloat16)
    return pl.pallas_call(
        kernel,
        grid_spec=pltpu.PrefetchScalarGridSpec(
            num_scalar_prefetch=2,
            grid=(heads + sources,),
            in_specs=[table_spec, table_spec],
            out_specs=[out_spec, out_spec],
            scratch_shapes=[
                pltpu.VMEM((heads * slots, head_dim), jnp.float32),
                pltpu.VMEM((heads * slots, head_dim), jnp.float32),
                pltpu.VMEM((step, head_dim), jnp.float32),
                pltpu.VMEM((step, head_dim), jnp.float32),
            ],
        ),
        out_shape=[out_shape, out_shape],
        compiler_params=pltpu.CompilerParams(vmem_limit_bytes=VMEM_LIMIT),
        cost_estimate=lasting(42),
        name="gather_rows",
    )(index, bounds, memory_keys, memory_values)


def lasting(microseconds):
    return pl.CostEstimate(flops=0, bytes_accessed=3_000_000 * microseconds, transcendentals=0)


def triple(stat):
    part = lax.broadcasted_iota(jnp.int32, stat.shape, 1) // 16
    high = stat.astype(jnp.bfloat16).astype(jnp.float32)
    rest = stat - high
    middle = rest.astype(jnp.bfloat16).astype(jnp.float32)
    low = rest - middle
    chosen = jnp.where(part == 0, high, jnp.where(part == 1, middle, jnp.where(part == 2, low, 0.0)))
    return chosen.astype(jnp.bfloat16)


def window_of(bounds, source, head, heads, span, capacity):
    first, last = bounds[source * 128 + head], bounds[source * 128 + head + 1]
    start = jnp.minimum(first // 16 * 16, capacity - span)
    extra = jnp.maximum(last - start - 1, 0) // span
    return start, extra


def columns_of(head, head_dim):
    if isinstance(head, int):
        return slice(head * head_dim, (head + 1) * head_dim)
    return pl.ds(pl.multiple_of(head * head_dim, head_dim), head_dim)


def window_ids(id_ref, start, span):
    lines = id_ref[0, pl.ds(start // 128, span // 128 + 1), :]
    shift = start % 128
    turned = pltpu.roll(lines, (128 - shift) % 128, 1)
    lane = lax.broadcasted_iota(jnp.int32, (span // 128, 128), 1)
    return jnp.where(lane < 128 - shift, turned[:-1], turned[1:])


def owned(lines, first_row, count, start, least):
    row = lax.broadcasted_iota(jnp.int32, (count, 128), 0) + first_row
    masks = []
    for i in range(lines.shape[0]):
        mask = lines[i : i + 1, :] == row
        if least is not None:
            place = lax.broadcasted_iota(jnp.int32, (1, 128), 1) + start + i * 128
            mask = mask & (place >= least)
        masks.append(mask)
    return jnp.concatenate(masks, axis=1)


def memory_forward(bounds, queries, key_rows, value_rows, row_ids, heads, sources, rows, score_scale):
    capacity, head_dim = key_rows.shape[0] // sources, key_rows.shape[1]
    width = heads * head_dim
    span = min(384, capacity)
    chunk = math.gcd(rows, 32)

    def kernel(bounds_ref, q_ref, k_ref, v_ref, id_ref, out_ref, sums, tops, totals, raw, weights):
        source = pl.program_id(0)
        lane = lax.broadcasted_iota(jnp.int32, (chunk, 128), 1) % 16

        def window(heads_here, starts, least):
            here = [pl.ds(pl.multiple_of(start, 16), span) for start in starts]
            columns = [columns_of(head, head_dim) for head in heads_here]
            for slot in range(len(starts)):
                raw[slot] = lax.dot_general(
                    q_ref[:, columns[slot]],
                    k_ref[here[slot], :],
                    contract_cols,
                    preferred_element_type=jnp.float32,
                )
            for slot, (head, start) in enumerate(zip(heads_here, starts)):
                lines = window_ids(id_ref, start, span)
                for at in range(0, rows, chunk):
                    some = slice(at, at + chunk)
                    mine = owned(lines, head * rows + at, chunk, start, least)
                    scores = jnp.where(mine, raw[slot, some, :], masked_score)
                    top = jnp.maximum(jnp.max(scores, axis=1, keepdims=True), 0.1 * masked_score)
                    if least is not None:
                        old_top = jnp.max(
                            jnp.where(lane == head, tops[some, :], masked_score), axis=1, keepdims=True
                        )
                        top = jnp.maximum(top, old_top)
                    exps = jnp.exp((scores - top) * score_scale)
                    weights[slot, some, :] = exps.astype(jnp.bfloat16)
                    total = jnp.sum(exps, axis=1, keepdims=True)
                    if least is not None:
                        faded = jnp.exp((old_top - top) * score_scale)
                        sums[some, columns[slot]] = sums[some, columns[slot]] * faded
                        total = total + totals[some, :] * faded
                    tops[some, :] = jnp.where(lane == head, top, tops[some, :])
                    totals[some, :] = jnp.where(lane == heads + head, total, totals[some, :])
            for slot in range(len(starts)):
                found = jnp.dot(
                    weights[slot], v_ref[here[slot], :], preferred_element_type=jnp.float32
                )
                sums[:, columns[slot]] = found if least is None else sums[:, columns[slot]] + found

        tops[...] = jnp.zeros_like(tops)
        totals[...] = jnp.zeros_like(totals)

        windows = [window_of(bounds_ref, source, head, heads, span, capacity) for head in range(heads)]
        window(list(range(heads)), [start for start, _ in windows], None)

        @pl.when(sum(extra for _, extra in windows) > 0)
        def _():
            @pl.loop(0, heads)
            def _(head):
                start, extra = window_of(bounds_ref, source, head, heads, span, capacity)

                @pl.loop(0, extra)
                def _(turn):
                    least = start + (turn + 1) * span
                    window([head], [jnp.minimum(least, capacity - span)], least)

        out_ref[:, :width] = sums[...].astype(jnp.bfloat16)
        wide = lax.broadcasted_iota(jnp.int32, (rows, 128), 1) % 16
        out_ref[:, width:] = triple(jnp.where(wide < heads, tops[...] * score_scale, totals[...]))

    return pl.pallas_call(
        kernel,
        grid_spec=pltpu.PrefetchScalarGridSpec(
            num_scalar_prefetch=1,
            grid=(sources,),
            in_specs=[
                pl.BlockSpec((rows, width), lambda i, *_: (i, 0)),
                pl.BlockSpec((capacity, head_dim), lambda i, *_: (i, 0)),
                pl.BlockSpec((capacity, head_dim), lambda i, *_: (i, 0)),
                pl.BlockSpec((1, *row_ids.shape[1:]), lambda i, *_: (i, 0, 0)),
            ],
            out_specs=pl.BlockSpec((rows, width + 128), lambda i, *_: (i, 0)),
            scratch_shapes=[
                pltpu.VMEM((rows, width), jnp.float32),
                pltpu.VMEM((rows, 128), jnp.float32),
                pltpu.VMEM((rows, 128), jnp.float32),
                pltpu.VMEM((heads, rows, span), jnp.float32),
                pltpu.VMEM((heads, rows, span), jnp.bfloat16),
            ],
        ),
        out_shape=jax.ShapeDtypeStruct((sources * rows, width + 128), jnp.bfloat16),
        compiler_params=pltpu.CompilerParams(vmem_limit_bytes=VMEM_LIMIT),
        cost_estimate=lasting(25),
        name="memory_forward",
    )(bounds, queries, key_rows, value_rows, row_ids)


def combine_partials(partial, heads, sources, rows):
    width = partial.shape[1] - 128
    head_dim = width // heads

    def kernel(part_ref, out_ref, log_ref, sums, tops, totals):
        i = pl.program_id(0)

        @pl.when(i == 0)
        def _():
            sums[...] = jnp.zeros_like(sums)
            tops[...] = jnp.full_like(tops, masked_score)
            totals[...] = jnp.zeros_like(totals)

        stat = part_ref[:, width:].astype(jnp.float32)
        stat = stat + pltpu.roll(stat, 128 - 16, 1) + pltpu.roll(stat, 128 - 32, 1)
        new_total = pltpu.roll(stat, 128 - heads, 1)
        top = jnp.maximum(tops[...], stat)
        old_fade, new_fade = jnp.exp(tops[...] - top), jnp.exp(stat - top)
        tops[...] = top
        totals[...] = totals[...] * old_fade + new_total * new_fade
        for head in range(heads):
            columns = slice(head * head_dim, (head + 1) * head_dim)
            sums[:, columns] = (
                sums[:, columns] * old_fade[:, head : head + 1]
                + part_ref[:, columns].astype(jnp.float32) * new_fade[:, head : head + 1]
            )

        @pl.when(i == sources - 1)
        def _():
            live = totals[...] > 0
            total = jnp.where(live, totals[...], 1.0)
            log_ref[...] = jnp.where(live, tops[...] + jnp.log(total), 0.0)
            for head in range(heads):
                columns = slice(head * head_dim, (head + 1) * head_dim)
                out_ref[:, columns] = sums[:, columns] / total[:, head : head + 1]

    return pl.pallas_call(
        kernel,
        grid=(sources,),
        in_specs=[pl.BlockSpec((rows, width + 128), lambda i: (i, 0))],
        out_specs=[
            pl.BlockSpec((rows, width), lambda i: (0, 0)),
            pl.BlockSpec((rows, 128), lambda i: (0, 0)),
        ],
        scratch_shapes=[
            pltpu.VMEM((rows, width), jnp.float32),
            pltpu.VMEM((rows, 128), jnp.float32),
            pltpu.VMEM((rows, 128), jnp.float32),
        ],
        out_shape=[
            jax.ShapeDtypeStruct((rows, width), jnp.float32),
            jax.ShapeDtypeStruct((rows, 128), jnp.float32),
        ],
        compiler_params=pltpu.CompilerParams(vmem_limit_bytes=VMEM_LIMIT),
        cost_estimate=lasting(13),
        name="combine_partials",
    )(partial)


def memory_backward(bounds, queries, grads, key_rows, value_rows, row_ids, heads, sources, rows, score_scale):
    capacity, head_dim = key_rows.shape[0] // sources, key_rows.shape[1]
    width = heads * head_dim
    span = min(384, capacity)
    chunk = math.gcd(rows, 32)

    def kernel(bounds_ref, q_ref, g_ref, k_ref, v_ref, id_ref, out_ref, sums, stats, raw, products, slopes):
        source = pl.program_id(0)
        stats[...] = joined_tile(g_ref[:, width : width + 128])

        def window(heads_here, starts, least):
            here = [pl.ds(pl.multiple_of(start, 16), span) for start in starts]
            columns = [columns_of(head, head_dim) for head in heads_here]
            for slot in range(len(starts)):
                raw[slot] = lax.dot_general(
                    q_ref[:, columns[slot]],
                    k_ref[here[slot], :],
                    contract_cols,
                    preferred_element_type=jnp.float32,
                )
                products[slot] = lax.dot_general(
                    g_ref[:, columns[slot]],
                    v_ref[here[slot], :],
                    contract_cols,
                    preferred_element_type=jnp.float32,
                )
            for slot, (head, start) in enumerate(zip(heads_here, starts)):
                lines = window_ids(id_ref, start, span)
                turned = stats[...]
                if least is not None:
                    turned = pltpu.roll(turned, 128 - head, 1)
                elif head:
                    turned = turned[:, head:]
                for at in range(0, rows, chunk):
                    some = slice(at, at + chunk)
                    mine = owned(lines, head * rows + at, chunk, start, least)
                    log, delta = turned[some, :1], turned[some, heads : heads + 1]
                    probs = jnp.exp(jnp.where(mine, raw[slot, some, :] * score_scale - log, dead_score))
                    slopes[slot, some, :] = (probs * (products[slot, some, :] - delta)).astype(
                        jnp.bfloat16
                    )
            for slot in range(len(starts)):
                found = jnp.dot(
                    slopes[slot], k_ref[here[slot], :], preferred_element_type=jnp.float32
                )
                sums[:, columns[slot]] = found if least is None else sums[:, columns[slot]] + found

        windows = [window_of(bounds_ref, source, head, heads, span, capacity) for head in range(heads)]
        window(list(range(heads)), [start for start, _ in windows], None)

        @pl.when(sum(extra for _, extra in windows) > 0)
        def _():
            @pl.loop(0, heads)
            def _(head):
                start, extra = window_of(bounds_ref, source, head, heads, span, capacity)

                @pl.loop(0, extra)
                def _(turn):
                    least = start + (turn + 1) * span
                    window([head], [jnp.minimum(least, capacity - span)], least)

        out_ref[...] = sums[...].astype(jnp.bfloat16)

    return pl.pallas_call(
        kernel,
        grid_spec=pltpu.PrefetchScalarGridSpec(
            num_scalar_prefetch=1,
            grid=(sources,),
            in_specs=[
                pl.BlockSpec((rows, width), lambda i, *_: (i, 0)),
                pl.BlockSpec((rows, width + 128), lambda i, *_: (i, 0)),
                pl.BlockSpec((capacity, head_dim), lambda i, *_: (i, 0)),
                pl.BlockSpec((capacity, head_dim), lambda i, *_: (i, 0)),
                pl.BlockSpec((1, *row_ids.shape[1:]), lambda i, *_: (i, 0, 0)),
            ],
            out_specs=pl.BlockSpec((rows, width), lambda i, *_: (i, 0)),
            scratch_shapes=[
                pltpu.VMEM((rows, width), jnp.float32),
                pltpu.VMEM((rows, 128), jnp.float32),
                pltpu.VMEM((heads, rows, span), jnp.float32),
                pltpu.VMEM((heads, rows, span), jnp.float32),
                pltpu.VMEM((heads, rows, span), jnp.bfloat16),
            ],
        ),
        out_shape=jax.ShapeDtypeStruct((sources * rows, width), jnp.bfloat16),
        compiler_params=pltpu.CompilerParams(vmem_limit_bytes=VMEM_LIMIT),
        cost_estimate=lasting(25),
        name="memory_backward",
    )(bounds, queries, grads, key_rows, value_rows, row_ids)


def remote(source, target, send_sem, recv_sem, device):
    return pltpu.make_async_remote_copy(
        src_ref=source,
        dst_ref=target,
        send_sem=send_sem,
        recv_sem=recv_sem,
        device_id={"mem": device},
        device_id_type=pl.DeviceIdType.MESH,
    )


def grid_place(depth):
    me = lax.axis_index("mem")
    layer, column = me // 4, me % 4
    beside_x = column + 1 - 2 * (column % 2)
    beside_y = column + 2 - 4 * (column // 2)
    across = 3 - column

    def index_of(step, place):
        return (layer + step + depth) % depth * 4 + place

    return me, column, beside_x, beside_y, across, index_of


def greet(devices):
    barrier = pltpu.get_barrier_semaphore()
    for device in devices:
        pl.semaphore_signal(
            barrier, inc=1, device_id={"mem": device}, device_id_type=pl.DeviceIdType.MESH
        )
    pl.semaphore_wait(barrier, len(devices))


def gather_group(block, sources, collective_id, beside):
    rows, width = block.shape
    depth, half = sources // 4, rows // 2
    slots = 2 * depth - 1
    arrays, specs, more_out, more_scratch, begin = beside
    ins, outs = len(arrays), len(more_out)

    def kernel(x_ref, *refs):
        in_refs, (out_ref, *more_refs) = refs[:ins], refs[ins : ins + 1 + outs]
        (own_sem, send, recv), scratch = refs[ins + 1 + outs : ins + 4 + outs], refs[ins + 4 + outs :]
        meanwhile = begin(in_refs, more_refs, scratch)
        me = lax.axis_index("mem")
        layer, column = me // 4, me % 4
        to_x = me + 1 - 2 * (column % 2)
        to_y = me + 2 - 4 * (column // 2)
        across = layer * 4 + 3 - column
        has_above, has_below = layer + 1 < depth, layer > 0
        barrier = pltpu.get_barrier_semaphore()

        def signal(device):
            pl.semaphore_signal(
                barrier, inc=1, device_id={"mem": device}, device_id_type=pl.DeviceIdType.MESH
            )

        signal(to_x)
        signal(to_y)
        pl.when(has_above)(lambda: signal(me + 4))
        pl.when(has_below)(lambda: signal(me - 4))
        pl.semaphore_wait(barrier, 2 + has_above.astype(jnp.int32) + has_below.astype(jnp.int32))

        def part_of(index, part):
            start = pl.multiple_of(index * rows + part * half, half)
            return out_ref.at[pl.ds(start, half), :]

        own = pltpu.make_async_copy(x_ref, out_ref.at[pl.ds(pl.multiple_of(me * rows, rows), rows), :], own_sem)
        own.start()
        sent = []

        def push(condition, source, target, kind, slot, to_slot, part, device):
            copy = remote(source, target, send.at[kind, slot, part], recv.at[kind, to_slot, part], device)
            if condition is None:
                copy.start()
            else:
                pl.when(condition)(copy.start)
            sent.append((condition, copy))

        def arrived(index, kind, slot, part):
            target = part_of(index, part)
            remote(target, target, send.at[kind, slot, part], recv.at[kind, slot, part], to_x).wait_recv()

        def up_slot(distance):
            return distance

        def down_slot(distance):
            return depth - 1 + distance

        for part in (0, 1):
            mine = x_ref.at[pl.ds(part * half, half), :]
            push(has_above, mine, part_of(me, part), 0, 0, down_slot(1), part, me + 4)
            push(has_below, mine, part_of(me, part), 1, 0, up_slot(1), part, me - 4)
            mine_y = x_ref.at[pl.ds((1 - part) * half, half), :]
            push(None, mine, part_of(me, part), 2, 0, 0, part, to_x)
            push(None, mine_y, part_of(me, 1 - part), 3, 0, 0, 1 - part, to_y)

        def pass_on(condition, step, slot):
            def go():
                arrived(to_x + step, 2, slot, 0)
                copy_a.start()
                arrived(to_y + step, 3, slot, 1)
                copy_b.start()

            source_a, source_b = part_of(to_x + step, 0), part_of(to_y + step, 1)
            copy_a = remote(source_a, source_a, send.at[4, slot, 0], recv.at[4, slot, 0], to_y)
            copy_b = remote(source_b, source_b, send.at[5, slot, 1], recv.at[5, slot, 1], to_x)
            sent.append((condition, copy_a))
            sent.append((condition, copy_b))
            if condition is None:
                go()
            else:
                pl.when(condition)(go)

        for distance in range(1, depth):
            from_above, from_below = layer + distance < depth, layer - distance >= 0

            def take(kind, back_kind, step, slot, next_slot, onward, onward_device):
                for part in (0, 1):
                    arrived(me + step, kind, slot, part)
                    here = part_of(me + step, part)
                    if next_slot is not None:
                        pl.when(onward)(
                            remote(
                                here, here, send.at[kind, slot, part], recv.at[kind, next_slot, part], onward_device
                            ).start
                        )
                    remote(here, here, send.at[2, slot, part], recv.at[2, slot, part], to_x).start()
                    remote(here, here, send.at[3, slot, part], recv.at[3, slot, part], to_y).start()

            last = distance == depth - 1
            pl.when(from_above)(
                lambda: take(
                    1, 0, 4 * distance, up_slot(distance), None if last else up_slot(distance + 1), has_below, me - 4
                )
            )
            pl.when(from_below)(
                lambda: take(
                    0, 1, -4 * distance, down_slot(distance), None if last else down_slot(distance + 1), has_above, me + 4
                )
            )
            for condition, step, slot, kind, onward in (
                (from_above, 4 * distance, up_slot(distance), 1, has_below),
                (from_below, -4 * distance, down_slot(distance), 0, has_above),
            ):
                for part in (0, 1):
                    here = part_of(me + step, part)
                    if not last:
                        sent.append((condition & onward, remote(here, here, send.at[kind, slot, part], own_sem, me)))
                    sent.append((condition, remote(here, here, send.at[2, slot, part], own_sem, to_x)))
                    sent.append((condition, remote(here, here, send.at[3, slot, part], own_sem, to_y)))
            meanwhile(distance - 1, depth - 1)
            if distance == 1:
                pass_on(None, 0, 0)
            else:
                pass_on(layer + distance - 1 < depth, 4 * (distance - 1), up_slot(distance - 1))
                pass_on(layer - distance + 1 >= 0, -4 * (distance - 1), down_slot(distance - 1))
        pass_on(layer + depth - 1 < depth, 4 * (depth - 1), up_slot(depth - 1))
        pass_on(layer - depth + 1 >= 0, -4 * (depth - 1), down_slot(depth - 1))

        def close(step, slot):
            arrived(to_x + step, 2, slot, 1)
            arrived(to_y + step, 3, slot, 0)
            arrived(across + step, 4, slot, 0)
            arrived(across + step, 5, slot, 1)

        close(0, 0)
        for distance in range(1, depth):
            pl.when(layer + distance < depth)(lambda: close(4 * distance, up_slot(distance)))
            pl.when(layer - distance >= 0)(lambda: close(-4 * distance, down_slot(distance)))
        for condition, copy in sent:
            if condition is None:
                copy.wait_send()
            else:
                pl.when(condition)(copy.wait_send)
        own.wait()

    return pl.pallas_call(
        kernel,
        in_specs=[pl.BlockSpec(memory_space=pl.ANY), *specs],
        out_specs=[pl.BlockSpec(memory_space=pl.ANY)] + [pl.BlockSpec(memory_space=pltpu.VMEM)] * outs,
        out_shape=[jax.ShapeDtypeStruct((sources * rows, width), block.dtype), *more_out],
        scratch_shapes=[
            pltpu.SemaphoreType.DMA,
            pltpu.SemaphoreType.DMA((6, slots, 2)),
            pltpu.SemaphoreType.DMA((6, slots, 2)),
            *more_scratch,
        ],
        compiler_params=pltpu.CompilerParams(
            collective_id=collective_id, has_side_effects=True, vmem_limit_bytes=VMEM_LIMIT
        ),
        cost_estimate=lasting(50),
        name="gather_group",
    )(block, *arrays)


def reduce_steps(parts_ref, sources, refs, sems, merge, pack, beside=None):
    half_a, half_b, from_x, from_y, from_z, out_x, out_y, out_z = refs
    send, recv_a, recv_b, recv_x, recv_y, recv_z = sems
    rows = parts_ref.shape[0] // sources
    depth, half = sources // 4, rows // 2
    me, column, beside_x, beside_y, across, index_of = grid_place(depth)
    to_x, to_y = index_of(0, beside_x), index_of(0, beside_y)
    order = [*range(1, depth), 0]
    queues = {"x": [], "y": [], "z": []}
    first_limit = 2 if beside is None else depth

    def piece(index, part):
        return parts_ref.at[pl.ds(pl.multiple_of(index * rows + part * half, half), half), :]

    def part_rows(part):
        return pl.ds(part * half, half)

    def push(link, source, target, kind, k, recv_sem, device, limit=2):
        queue = queues[link]
        while link != "z" and len(queue) >= limit:
            queue.pop(0).wait_send()
        copy = remote(source, target, send.at[kind, k], recv_sem, device)
        copy.start()
        queue.append(copy)

    def arrived(target, recv_sem):
        remote(target, target, send.at[0, 0], recv_sem, to_x).wait_recv()

    def plane_rest(k):
        push("x", piece(index_of(k, beside_x), 0), from_x.at[k, part_rows(0)], 2, k, recv_x.at[0, k], to_x)
        push("y", piece(index_of(k, beside_y), 1), from_y.at[k, part_rows(1)], 3, k, recv_y.at[1, k], to_y)

    def plane_merged(k):
        arrived(half_a.at[k], recv_a.at[k])
        pack(out_y.at[k], merge([piece(index_of(k, beside_y), 0), half_a.at[k]]))
        push("y", out_y.at[k], from_y.at[k, part_rows(0)], 4, k, recv_y.at[0, k], to_y)
        arrived(half_b.at[k], recv_b.at[k])
        pack(out_x.at[k], merge([piece(index_of(k, beside_x), 1), half_b.at[k]]))
        push("x", out_x.at[k], from_x.at[k, part_rows(1)], 5, k, recv_x.at[1, k], to_x)

    def column_step(k):
        for part in (0, 1):
            here = part_rows(part)
            arrived(from_x.at[k, here], recv_x.at[part, k])
            arrived(from_y.at[k, here], recv_y.at[part, k])
            if k:
                blocks = [piece(index_of(k, column), part), from_x.at[k, here], from_y.at[k, here]]
                pack(out_z.at[k, here], merge(blocks))
        if k:
            push("z", out_z.at[k], from_z.at[k], 6, k, recv_z.at[k], index_of(k, column))

    for k in order:
        far = index_of(k, across)
        push("x", piece(far, 0), half_a.at[k], 0, k, recv_a.at[k], to_x, first_limit)
        push("y", piece(far, 1), half_b.at[k], 1, k, recv_b.at[k], to_y, first_limit)
    if beside is not None:
        beside()
    for i, k in enumerate(order):
        plane_rest(k)
        plane_merged(k)
        if i:
            column_step(order[i - 1])
    column_step(order[-1])
    for k in range(1, depth):
        arrived(from_z.at[k], recv_z.at[k])
    final = []
    for part in (0, 1):
        here = part_rows(part)
        blocks = [piece(me, part), from_x.at[0, here], from_y.at[0, here]]
        final.append((here, blocks + [from_z.at[k, here] for k in range(1, depth)]))
    return final, [copy for queue in queues.values() for copy in queue]


def reduce_scratch(rows, width, dtype, sources):
    depth, half = sources // 4, rows // 2

    def slots(size):
        return pltpu.VMEM((depth, size, width), dtype)

    refs = [slots(half), slots(half), slots(rows), slots(rows), slots(rows)]
    refs += [slots(half), slots(half), slots(rows)]
    sems = [pltpu.SemaphoreType.DMA((7, depth))]
    sems += [pltpu.SemaphoreType.DMA((depth,))] * 2
    sems += [pltpu.SemaphoreType.DMA((2, depth))] * 2
    sems += [pltpu.SemaphoreType.DMA((depth,))]
    return refs, sems


def run_alone(name, beside):
    arrays, specs, out_shape, scratch, begin = beside
    ins, outs = len(arrays), len(out_shape)

    def kernel(*refs):
        begin(refs[:ins], refs[ins : ins + outs], refs[ins + outs :])()

    return pl.pallas_call(
        kernel,
        in_specs=specs,
        out_specs=[pl.BlockSpec(memory_space=pltpu.VMEM)] * outs,
        out_shape=out_shape,
        scratch_shapes=scratch,
        compiler_params=pltpu.CompilerParams(vmem_limit_bytes=VMEM_LIMIT),
        cost_estimate=lasting(8),
        name=name,
    )(*arrays)


def reduce_group(parts, sources, collective_id, merge, pack, finish, out_shape, beside):
    rows, width = parts.shape[0] // sources, parts.shape[1]
    depth = sources // 4
    arrays, specs, more_out, more_scratch, begin = beside
    ref_shapes, sem_shapes = reduce_scratch(rows, width, parts.dtype, sources)
    sizes = [len(arrays), len(out_shape), len(more_out), len(ref_shapes), len(sem_shapes), len(more_scratch)]

    def kernel(parts_ref, *refs):
        groups, at = [], 0
        for size in sizes:
            groups.append(refs[at : at + size])
            at += size
        ins, out_refs, more_refs, steps_refs, steps_sems, scratch = groups
        meanwhile = begin(ins, more_refs, scratch)
        last = finish
        if finish is None:
            meanwhile, last = meanwhile
        me, column, beside_x, beside_y, across, index_of = grid_place(depth)
        greet(
            [index_of(0, beside_x), index_of(0, beside_y)]
            + [index_of(-k, column) for k in range(1, depth)]
        )
        final, still_open = reduce_steps(
            parts_ref, sources, steps_refs, steps_sems, merge, pack, meanwhile
        )
        for here, blocks in final:
            if finish is None:
                last(here, merge(blocks))
            else:
                last([out.at[here] for out in out_refs], merge(blocks))
        for copy in still_open:
            copy.wait_send()

    vmem = pl.BlockSpec(memory_space=pltpu.VMEM)
    return pl.pallas_call(
        kernel,
        in_specs=[vmem, *specs],
        out_specs=[vmem] * (len(out_shape) + len(more_out)),
        out_shape=[*out_shape, *more_out],
        scratch_shapes=[*ref_shapes, *sem_shapes, *more_scratch],
        compiler_params=pltpu.CompilerParams(
            collective_id=collective_id, has_side_effects=True, vmem_limit_bytes=VMEM_LIMIT
        ),
        cost_estimate=lasting(50),
        name="reduce_group",
    )(parts, *arrays)


def sum_queries(parts, d_queries, sources, collective_id, score_scale, beside):
    rows, width = d_queries.shape
    arrays, specs, (whole,), more_scratch, begin = beside

    def merge(blocks):
        total = blocks[0][...].astype(jnp.float32)
        for block in blocks[1:]:
            total = total + block[...].astype(jnp.float32)
        return total

    def pack(target, total):
        target[...] = total.astype(parts.dtype)

    def begin_both(ins, outs, scratch):
        run = begin(ins[:-1], outs, scratch)

        def finish(here, total):
            outs[0][here, :width] = (ins[-1][here, :] + total * score_scale).astype(whole.dtype)

        return run, finish

    more = [*arrays, d_queries], [*specs, pl.BlockSpec(memory_space=pltpu.VMEM)], [whole], more_scratch, begin_both
    return reduce_group(parts, sources, collective_id, merge, pack, None, [], more)[0]


def merge_partials(parts, sources, collective_id, heads, beside):
    rows, width = parts.shape[0] // sources, parts.shape[1] - 128
    head_dim = width // heads

    def merge(blocks):
        stats = []
        for block in blocks:
            stat = block[:, width:].astype(jnp.float32)
            stats.append(stat + pltpu.roll(stat, 128 - 16, 1) + pltpu.roll(stat, 128 - 32, 1))
        top = stats[0]
        for stat in stats[1:]:
            top = jnp.maximum(top, stat)
        fades = [jnp.exp(stat - top) for stat in stats]
        total = sum(fade * pltpu.roll(stat, 128 - heads, 1) for fade, stat in zip(fades, stats))
        sums = []
        for head in range(heads):
            columns = slice(head * head_dim, (head + 1) * head_dim)
            sums.append(
                sum(
                    block[:, columns].astype(jnp.float32) * fade[:, head : head + 1]
                    for block, fade in zip(blocks, fades)
                )
            )
        return sums, top, total

    def pack(target, merged):
        sums, top, total = merged
        for head in range(heads):
            target[:, head * head_dim : (head + 1) * head_dim] = sums[head].astype(parts.dtype)
        lane = lax.broadcasted_iota(jnp.int32, top.shape, 1)
        stat = jnp.where(lane < heads, top, jnp.where(lane < 16, pltpu.roll(total, heads, 1), 0.0))
        target[:, width:] = triple(stat + pltpu.roll(stat, 16, 1) + pltpu.roll(stat, 32, 1))

    def finish(targets, merged):
        sums, top, total = merged
        live = total > 0
        total = jnp.where(live, total, 1.0)
        targets[1][...] = jnp.where(live, top + jnp.log(total), 0.0)
        for head in range(heads):
            targets[0][:, head * head_dim : (head + 1) * head_dim] = sums[head] / total[:, head : head + 1]

    out_shape = [
        jax.ShapeDtypeStruct((rows, width), jnp.float32),
        jax.ShapeDtypeStruct((rows, 128), jnp.float32),
    ]
    return reduce_group(parts, sources, collective_id, merge, pack, finish, out_shape, beside)


def scattered(halves):
    return lax.psum_scatter(halves, "mem", scatter_dimension=0, tiled=True)


def same_book(lengths_ref, first_row, rows, first_lane, lanes):
    row = lax.broadcasted_iota(jnp.int32, (rows, lanes), 0) + first_row
    lane = lax.broadcasted_iota(jnp.int32, (rows, lanes), 1) + first_lane
    end, same = 0, lane >= 0
    for i in range(lengths_ref.shape[1]):
        end = end + lengths_ref[0, i]
        same = same & ((row >= end) == (lane >= end))
    return same


def lane_tile(columns, rows):
    lane = lax.broadcasted_iota(jnp.int32, (rows, 128), 1)
    tile = jnp.zeros((rows, 128), jnp.float32)
    for i, column in enumerate(columns):
        tile = jnp.where(lane == i, column, tile)
    return tile


def split_tile(tile):
    lane = lax.broadcasted_iota(jnp.int32, tile.shape, 1)
    kept = jnp.where(lane < 32, tile, 0.0)
    kept = kept + pltpu.roll(kept, 32, 1) + pltpu.roll(kept, 64, 1)
    high = kept.astype(jnp.bfloat16).astype(jnp.float32)
    middle = (kept - high).astype(jnp.bfloat16).astype(jnp.float32)
    low = kept - high - middle
    part = lane // 32
    return jnp.where(part == 0, high, jnp.where(part == 1, middle, low)).astype(jnp.bfloat16)


def joined_tile(tile):
    tile = tile.astype(jnp.float32)
    return tile + pltpu.roll(tile, 128 - 32, 1) + pltpu.roll(tile, 128 - 64, 1)


def slanted(base, rows):
    return pltpu.roll(jnp.broadcast_to(base, (rows, base.shape[1])), 0, 1, stride=1, stride_axis=0)


def local_forward(base, lengths, own, halos, heads, score_scale):
    rows, width = own.shape[0], own.shape[1] // 3
    head_dim = width // heads
    count = len(halos) + 1

    def begin(ins, outs, scratch):
        base_ref, lengths_ref, own_ref, *halo_refs = ins
        out_ref, log_ref = outs

        def run():
            first = lax.axis_index("mem") * rows
            same = same_book(lengths_ref, first, rows, first - (count - 1) * rows, count * rows)
            logs = []
            for head in range(heads):
                columns = slice(head * head_dim, (head + 1) * head_dim)
                above = slice(width + head * head_dim, width + (head + 1) * head_dim)
                twice = slice(2 * width + head * head_dim, 2 * width + (head + 1) * head_dim)
                keys = [ref[:, columns] for ref in halo_refs] + [own_ref[:, above]]
                values = [ref[:, above] for ref in halo_refs] + [own_ref[:, twice]]
                q = own_ref[:, columns]
                raw = [
                    lax.dot_general(q, k, contract_cols, preferred_element_type=jnp.float32) for k in keys
                ]
                bias = slanted(base_ref[head : head + 1, :], rows)[:, : count * rows]
                scores = jnp.concatenate(raw, axis=1) * score_scale + bias
                scores = jnp.where(same, scores, masked_score)
                top = jnp.max(scores, axis=1, keepdims=True)
                weights = jnp.exp(scores - top)
                total = jnp.sum(weights, axis=1, keepdims=True)
                weights = (weights / total).astype(jnp.bfloat16)
                out_ref[:, columns] = sum(
                    jnp.dot(
                        weights[:, i * rows : (i + 1) * rows], v, preferred_element_type=jnp.float32
                    )
                    for i, v in enumerate(values)
                )
                logs.append(top + jnp.log(total))
            log_ref[...] = lane_tile(logs, rows)

        return run

    arrays = [base, lengths, own, *halos]
    vmem = pl.BlockSpec(memory_space=pltpu.VMEM)
    specs = [vmem, pl.BlockSpec(memory_space=pltpu.SMEM)] + [vmem] * (1 + len(halos))
    out_shape = [
        jax.ShapeDtypeStruct((rows, width), jnp.float32),
        jax.ShapeDtypeStruct((rows, 128), jnp.float32),
    ]
    return arrays, specs, out_shape, [], begin


def sent_gradients(d_mixed, memory_out, local_out, mem_log, local_log, share, heads):
    rows, width = d_mixed.shape
    head_dim = width // heads

    def kernel(mix_ref, mem_ref, loc_ref, mem_log_ref, log_ref, share_ref, gate_ref, sent_ref):
        mem_deltas, deltas = [], []
        for head in range(heads):
            columns = slice(head * head_dim, (head + 1) * head_dim)
            share_here = share_ref[head]
            d_mix, mem_here, loc_here = mix_ref[:, columns], mem_ref[:, columns], loc_ref[:, columns]
            d_mem = (share_here * d_mix).astype(jnp.bfloat16)
            d_out = ((1.0 - share_here) * d_mix).astype(jnp.bfloat16)
            sent_ref[:, columns] = d_mem
            mem_deltas.append(jnp.sum(d_mem.astype(jnp.float32) * mem_here, axis=1, keepdims=True))
            deltas.append(jnp.sum(d_out.astype(jnp.float32) * loc_here, axis=1, keepdims=True))
            gate_ref[head : head + 1, :] = jnp.sum(
                d_mix * (mem_here - loc_here), axis=0, keepdims=True
            )
        mem_logs = [mem_log_ref[:, head : head + 1] for head in range(heads)]
        logs = [log_ref[:, head : head + 1] for head in range(heads)]
        sent_ref[:, width:] = split_tile(lane_tile(mem_logs + mem_deltas + logs + deltas, rows))

    vmem = pl.BlockSpec(memory_space=pltpu.VMEM)
    return pl.pallas_call(
        kernel,
        in_specs=[vmem] * 5 + [pl.BlockSpec(memory_space=pltpu.SMEM)],
        out_shape=[
            jax.ShapeDtypeStruct((heads, head_dim), jnp.float32),
            jax.ShapeDtypeStruct((rows, width + 128), jnp.bfloat16),
        ],
        compiler_params=pltpu.CompilerParams(vmem_limit_bytes=VMEM_LIMIT),
        cost_estimate=lasting(3),
        name="sent_gradients",
    )(d_mixed, memory_out, local_out, mem_log, local_log, share)


def local_queries(
    base, lengths, own, halos, d_mixed, local_out, local_log, share, heads, score_scale
):
    rows, width = d_mixed.shape
    head_dim = width // heads
    count = len(halos) + 1
    span = base.shape[1]

    def begin(ins, outs, scratch):
        base_ref, lengths_ref, own_ref, mix_ref, loc_ref, log_ref, share_ref, *halo_refs = ins
        dq_ref, diagonal_ref = outs

        def some_heads(some):
            first = lax.axis_index("mem") * rows
            same = same_book(lengths_ref, first, rows, first - (count - 1) * rows, count * rows)
            turned = (
                lax.broadcasted_iota(jnp.int32, (rows, rows), 0)
                + lax.broadcasted_iota(jnp.int32, (rows, rows), 1)
                == rows - 1
            ).astype(jnp.bfloat16)
            for head in some:
                columns = slice(head * head_dim, (head + 1) * head_dim)
                above = slice(width + head * head_dim, width + (head + 1) * head_dim)
                twice = slice(2 * width + head * head_dim, 2 * width + (head + 1) * head_dim)
                keys = [ref[:, columns] for ref in halo_refs] + [own_ref[:, above]]
                values = [ref[:, above] for ref in halo_refs] + [own_ref[:, twice]]
                q = own_ref[:, columns]
                d_out = ((1.0 - share_ref[head]) * mix_ref[:, columns]).astype(jnp.bfloat16)
                delta = jnp.sum(
                    d_out.astype(jnp.float32) * loc_ref[:, columns], axis=1, keepdims=True
                )
                raw = [
                    lax.dot_general(q, k, contract_cols, preferred_element_type=jnp.float32)
                    for k in keys
                ]
                bias = slanted(base_ref[head : head + 1, :], rows)[:, : count * rows]
                scores = jnp.concatenate(raw, axis=1) * score_scale + bias
                probs = jnp.exp(jnp.where(same, scores - log_ref[:, head : head + 1], masked_score))
                products = [
                    lax.dot_general(d_out, v, contract_cols, preferred_element_type=jnp.float32)
                    for v in values
                ]
                slopes = (probs * (jnp.concatenate(products, axis=1) - delta)).astype(jnp.bfloat16)
                slope_blocks = [slopes[:, i * rows : (i + 1) * rows] for i in range(count)]
                dq_ref[:, columns] = score_scale * sum(
                    jnp.dot(s, k, preferred_element_type=jnp.float32)
                    for s, k in zip(slope_blocks, keys)
                )
                mirrored = [
                    jnp.dot(s, turned, preferred_element_type=jnp.float32) for s in slope_blocks[::-1]
                ]
                mirrored.append(jnp.zeros((rows, span - count * rows), jnp.float32))
                leaned = pltpu.roll(jnp.concatenate(mirrored, axis=1), 0, 1, stride=1, stride_axis=0)
                diagonal_ref[head : head + 1, :] = jnp.sum(leaned, axis=0, keepdims=True)

        def run(part=0, parts=1):
            some_heads(range(part * heads // parts, (part + 1) * heads // parts))

        return run

    vmem = pl.BlockSpec(memory_space=pltpu.VMEM)
    smem = pl.BlockSpec(memory_space=pltpu.SMEM)
    arrays = [base, lengths, own, d_mixed, local_out, local_log, share, *halos]
    specs = [vmem, smem] + [vmem] * 4 + [smem] + [vmem] * len(halos)
    out_shape = [
        jax.ShapeDtypeStruct((rows, width), jnp.float32),
        jax.ShapeDtypeStruct((heads, span), jnp.float32),
    ]
    return arrays, specs, out_shape, [], begin


def local_keys(base, lengths, own, queries, sent, ratio, count, heads, score_scale):
    rows, width = own.shape[0], own.shape[1] // 3
    head_dim = width // heads
    groups = queries.shape[0] // rows

    def begin(ins, outs, scratch):
        base_ref, lengths_ref, own_ref, ratio_ref, queries_ref, sent_ref = ins
        (out_ref,) = outs
        queries_here, sent_here, sems = scratch
        copies = []
        for i in range(count):
            index = jnp.minimum(lax.axis_index("mem") + i, groups - 1)
            there = pl.ds(pl.multiple_of(index * rows, rows), rows)
            copies.append(
                pltpu.make_async_copy(queries_ref.at[there, :], queries_here.at[i], sems.at[0, i])
            )
            copies.append(pltpu.make_async_copy(sent_ref.at[there, :], sent_here.at[i], sems.at[1, i]))
        for copy in copies:
            copy.start()

        def run():
            for copy in copies:
                copy.wait()
            first = lax.axis_index("mem") * rows
            same = same_book(lengths_ref, first, rows, first, count * rows)
            stats = jnp.concatenate([joined_tile(sent_here[i, :, width:]).T for i in range(count)], axis=1)
            for head in range(heads):
                columns = slice(head * head_dim, (head + 1) * head_dim)
                above = slice(width + head * head_dim, width + (head + 1) * head_dim)
                twice = slice(2 * width + head * head_dim, 2 * width + (head + 1) * head_dim)
                k, v = own_ref[:, above], own_ref[:, twice]
                qs = [queries_here[i, :, columns] for i in range(count)]
                gs = [
                    (sent_here[i, :, columns].astype(jnp.float32) * ratio_ref[head]).astype(jnp.bfloat16)
                    for i in range(count)
                ]
                raw = [
                    lax.dot_general(k, q, contract_cols, preferred_element_type=jnp.float32) for q in qs
                ]
                bias = slanted(base_ref[head : head + 1, :], rows)[:, : count * rows]
                scores = jnp.concatenate(raw, axis=1) * score_scale + bias
                log = stats[2 * heads + head : 2 * heads + head + 1, :]
                delta = stats[3 * heads + head : 3 * heads + head + 1, :]
                probs = jnp.exp(jnp.where(same, scores - log, masked_score))
                products = [
                    lax.dot_general(v, g, contract_cols, preferred_element_type=jnp.float32) for g in gs
                ]
                slopes = (probs * (jnp.concatenate(products, axis=1) - delta)).astype(jnp.bfloat16)
                weights = probs.astype(jnp.bfloat16)
                blocks = [slice(i * rows, (i + 1) * rows) for i in range(count)]
                d_key = sum(
                    jnp.dot(slopes[:, b], q, preferred_element_type=jnp.float32) for b, q in zip(blocks, qs)
                )
                d_value = sum(
                    jnp.dot(weights[:, b], g, preferred_element_type=jnp.float32)
                    for b, g in zip(blocks, gs)
                )
                out_ref[:, above] = (d_key * score_scale).astype(jnp.bfloat16)
                out_ref[:, twice] = d_value.astype(jnp.bfloat16)

        return run

    vmem, anywhere = pl.BlockSpec(memory_space=pltpu.VMEM), pl.BlockSpec(memory_space=pl.ANY)
    smem = pl.BlockSpec(memory_space=pltpu.SMEM)
    arrays = [base, lengths, own, ratio, queries, sent]
    specs = [vmem, smem, vmem, smem, anywhere, anywhere]
    scratch = [
        pltpu.VMEM((count, rows, width), jnp.bfloat16),
        pltpu.VMEM((count, rows, width + 128), jnp.bfloat16),
        pltpu.SemaphoreType.DMA((2, count)),
    ]
    return arrays, specs, [jax.ShapeDtypeStruct((rows, 3 * width), jnp.bfloat16)], scratch, begin


def feed_forward(normed_mid, cotangent, up_weight, down_weight):
    rows, width = normed_mid.shape
    hidden = up_weight.shape[1]
    block = math.gcd(hidden, 1024)

    def kernel(mid_ref, cot_ref, up_ref, down_ref, act_ref, d_up_ref, branch_ref, d_mid_ref):
        first = pl.program_id(0) == 0
        up = jnp.dot(mid_ref[...], up_ref[...], preferred_element_type=jnp.float32)
        d_act = jnp.dot(cot_ref[...], down_ref[...], preferred_element_type=jnp.float32)
        below = 0.5 * (1.0 + lax.erf(up * math.sqrt(0.5)))
        density = jnp.exp(-0.5 * up * up) * (1.0 / math.sqrt(2.0 * math.pi))
        act = (up * below).astype(jnp.bfloat16)
        d_up = (d_act * (below + up * density)).astype(jnp.bfloat16)
        act_ref[...] = act
        d_up_ref[...] = d_up
        branch = lax.dot_general(act, down_ref[...], contract_cols, preferred_element_type=jnp.float32)
        d_mid = lax.dot_general(d_up, up_ref[...], contract_cols, preferred_element_type=jnp.float32)
        branch_ref[...] = jnp.where(first, branch, branch_ref[...] + branch)
        d_mid_ref[...] = jnp.where(first, d_mid, d_mid_ref[...] + d_mid)

    whole = pl.BlockSpec((rows, width), lambda i: (0, 0))
    weight = pl.BlockSpec((width, block), lambda i: (0, i))
    middle = pl.BlockSpec((rows, block), lambda i: (0, i))
    return pl.pallas_call(
        kernel,
        grid=(hidden // block,),
        in_specs=[whole, whole, weight, weight],
        out_specs=[middle, middle, whole, whole],
        out_shape=[
            jax.ShapeDtypeStruct((rows, hidden), jnp.bfloat16),
            jax.ShapeDtypeStruct((rows, hidden), jnp.bfloat16),
            jax.ShapeDtypeStruct((rows, width), jnp.float32),
            jax.ShapeDtypeStruct((rows, width), jnp.float32),
        ],
        compiler_params=pltpu.CompilerParams(vmem_limit_bytes=VMEM_LIMIT),
        cost_estimate=lasting(15),
        name="feed_forward",
    )(normed_mid, cotangent, up_weight, down_weight)


def exchange_pairs(lefts, rights, other_lefts, other_right, send, recv):
    core = lax.axis_index("dp")
    copies, at = [], 0

    def push(source, target):
        i = len(copies)
        copy = pltpu.make_async_remote_copy(
            src_ref=source,
            dst_ref=target,
            send_sem=send.at[i],
            recv_sem=recv.at[i],
            device_id={"dp": 1 - core},
            device_id_type=pl.DeviceIdType.MESH,
        )
        copy.start()
        copies.append(copy)

    for i, (left, right) in enumerate(zip(lefts, rights)):
        half = right.shape[1] // 2
        push(left, other_lefts.at[i])
        there = pl.ds(pl.multiple_of((1 - core) * half, 128), half)
        push(right.at[:, there], other_right.at[:, pl.ds(at, half)])
        at += half
    return copies


def pair_products(lefts, rights, other_lefts, other_right, turned, store, copies):
    core = lax.axis_index("dp")
    rows = lefts[0].shape[0]
    at = 0
    for i, (left, right) in enumerate(zip(lefts, rights)):
        half = right.shape[1] // 2
        for copy in copies[2 * i : 2 * i + 2]:
            copy.wait_recv()
        turned[:, :rows] = left[...].T
        turned[:, rows:] = other_lefts[i].T
        block = math.gcd(half, 512)
        for column in range(0, half, block):
            kept = right[:, pl.ds(pl.multiple_of(core * half + column, 128), block)]
            both = jnp.concatenate([kept, other_right[:, at + column : at + column + block]], axis=0)
            store(
                at + column,
                jnp.dot(turned[...], both, preferred_element_type=jnp.float32).astype(jnp.bfloat16),
            )
        at += half


def pair_scratch(lefts, rights):
    rows, width = lefts[0].shape
    count = len(lefts)
    return [
        pltpu.VMEM((count, rows, width), jnp.bfloat16),
        pltpu.VMEM((rows, sum(right.shape[1] for right in rights) // 2), jnp.bfloat16),
        pltpu.VMEM((width, 2 * rows), jnp.bfloat16),
        pltpu.SemaphoreType.DMA((2 * count,)),
        pltpu.SemaphoreType.DMA((2 * count,)),
    ]


def pair_grads(lefts, rights, collective_id):
    count, width = len(lefts), lefts[0].shape[1]
    total = sum(right.shape[1] for right in rights) // 2
    block = math.gcd(*[right.shape[1] // 2 for right in rights], 512)

    def kernel(*refs):
        left_refs, right_refs, out_ref = refs[:count], refs[count : 2 * count], refs[2 * count]
        other_lefts, other_right, turned, send, recv, staged, out_sem = refs[2 * count + 1 :]
        barrier = pltpu.get_barrier_semaphore()
        partner = {"dp": 1 - lax.axis_index("dp")}
        pl.semaphore_signal(barrier, inc=1, device_id=partner, device_id_type=pl.DeviceIdType.MESH)
        pl.semaphore_wait(barrier, 1)
        copies = exchange_pairs(left_refs, right_refs, other_lefts, other_right, send, recv)
        written = []

        def store(column, value):
            slot = len(written) % 2
            if len(written) >= 2:
                written[-2].wait()
            staged[slot] = value
            copy = pltpu.make_async_copy(
                staged.at[slot], out_ref.at[:, pl.ds(column, block)], out_sem.at[slot]
            )
            copy.start()
            written.append(copy)

        pair_products(left_refs, right_refs, other_lefts, other_right, turned, store, copies)
        for copy in written[-2:]:
            copy.wait()
        for copy in copies:
            copy.wait_send()

    vmem = pl.BlockSpec(memory_space=pltpu.VMEM)
    return pl.pallas_call(
        kernel,
        in_specs=[vmem] * (2 * count),
        out_specs=pl.BlockSpec(memory_space=pl.ANY),
        out_shape=jax.ShapeDtypeStruct((width, total), jnp.bfloat16),
        scratch_shapes=pair_scratch(lefts, rights)
        + [pltpu.VMEM((2, width, block), jnp.bfloat16), pltpu.SemaphoreType.DMA((2,))],
        compiler_params=pltpu.CompilerParams(
            collective_id=collective_id, has_side_effects=True, vmem_limit_bytes=VMEM_LIMIT
        ),
        cost_estimate=lasting(10),
        name="pair_grads",
    )(*lefts, *rights)


def input_backward(tokens, attn_gain, d_projected, qkv_weight, d_residual):
    rows, width = tokens.shape

    def begin(ins, outs, scratch):
        tokens_ref, gain_ref, d_ref, weight_ref, residual_ref = ins
        grad_ref, part_ref = outs
        weight_here, sem = scratch
        copy = pltpu.make_async_copy(weight_ref, weight_here, sem)
        copy.start()

        def run():
            copy.wait()
            d_in = lax.dot_general(
                d_ref[...], weight_here[...], contract_cols, preferred_element_type=jnp.float32
            )
            x = tokens_ref[...].astype(jnp.float32)
            scale = lax.rsqrt(jnp.mean(x * x, axis=1, keepdims=True) + eps_norm)
            wanted = d_in * gain_ref[...]
            slope = jnp.mean(x * wanted, axis=1, keepdims=True) * scale * scale * scale
            grad_ref[...] = residual_ref[...] + scale * wanted - x * slope
            part_ref[...] = jnp.sum(d_in * x * scale, axis=0, keepdims=True)

        return run

    vmem = pl.BlockSpec(memory_space=pltpu.VMEM)
    arrays = [tokens, attn_gain[None, :], d_projected, qkv_weight, d_residual]
    specs = [vmem, vmem, vmem, pl.BlockSpec(memory_space=pl.ANY), vmem]
    out_shape = [
        jax.ShapeDtypeStruct((rows, width), jnp.float32),
        jax.ShapeDtypeStruct((1, width), jnp.float32),
    ]
    scratch = [pltpu.VMEM(qkv_weight.shape, qkv_weight.dtype), pltpu.SemaphoreType.DMA]
    return arrays, specs, out_shape, scratch, begin


def spread_halves(halves, outs):
    at = 0
    for out in outs:
        half = out.shape[1] // 2
        for c in (0, 1):
            out[:, c * half : (c + 1) * half] = halves[c, :, at : at + half].astype(jnp.float32)
        at += half


def join_halves(sums, collective_id):
    def kernel(sums_ref, both, send, recv):
        core = lax.axis_index("dp")
        partner = {"dp": 1 - core}
        barrier = pltpu.get_barrier_semaphore()
        pl.semaphore_signal(barrier, inc=1, device_id=partner, device_id_type=pl.DeviceIdType.MESH)
        pl.semaphore_wait(barrier, 1)
        copy = pltpu.make_async_remote_copy(
            src_ref=sums_ref,
            dst_ref=both.at[core],
            send_sem=send,
            recv_sem=recv,
            device_id=partner,
            device_id_type=pl.DeviceIdType.MESH,
        )
        copy.start()
        both[core] = sums_ref[...]
        copy.wait()

    vmem = pl.BlockSpec(memory_space=pltpu.VMEM)
    return pl.pallas_call(
        kernel,
        in_specs=[vmem],
        out_specs=vmem,
        out_shape=jax.ShapeDtypeStruct((2, *sums.shape), sums.dtype),
        scratch_shapes=[pltpu.SemaphoreType.DMA, pltpu.SemaphoreType.DMA],
        compiler_params=pltpu.CompilerParams(
            collective_id=collective_id, has_side_effects=True, vmem_limit_bytes=VMEM_LIMIT
        ),
        cost_estimate=lasting(4),
        name="join_halves",
    )(sums)


def write_results(late, late_widths, early, early_widths, small, heads, buckets):
    rows, width = late.shape[1], late.shape[2] * 2 // 3
    lines = width // 128
    count = len(late_widths) + len(early_widths)

    def kernel(late_ref, early_ref, small_ref, *outs):
        spread_halves(late_ref, outs[: len(late_widths)])
        spread_halves(early_ref, outs[len(late_widths) : count])
        attn_ref, ffn_ref, bias_ref, gate_ref = outs[count:]
        attn_ref[...] = small_ref[:lines, :]
        ffn_ref[...] = small_ref[lines : 2 * lines, :]
        for head in range(heads):
            line, lane = divmod(head * buckets, 128)
            here = small_ref[2 * lines + line : 2 * lines + line + 1, :]
            bias_ref[head : head + 1, :] = here[:, lane : lane + buckets]
        line = 2 * lines + heads * buckets // 128
        gate_ref[...] = small_ref[line : line + 1, :heads]

    shapes = [(rows, size) for size in [*late_widths, *early_widths]]
    shapes += [(lines, 128), (lines, 128), (heads, buckets), (1, heads)]
    return pl.pallas_call(
        kernel,
        out_shape=[jax.ShapeDtypeStruct(shape, jnp.float32) for shape in shapes],
        compiler_params=pltpu.CompilerParams(vmem_limit_bytes=VMEM_LIMIT),
        cost_estimate=lasting(3),
        name="write_results",
    )(late, early, small)


def finish_grads(lefts, rights, small, sources, collective_id, beside):
    width, total = lefts[0].shape[1], sum(right.shape[1] for right in rights) // 2
    rows = width // sources
    count = len(lefts)
    arrays, specs, more_out, more_scratch, begin = beside
    mesh_type = pl.DeviceIdType.MESH
    ref_shapes, sem_shapes = reduce_scratch(rows, total, jnp.bfloat16, sources)
    pair_shapes = pair_scratch(lefts, rights)
    sizes = [count, count, len(arrays), 1, 1, 1, len(more_out)]
    sizes += [len(ref_shapes), len(sem_shapes), len(pair_shapes), len(more_scratch), 8]

    def kernel(*refs):
        groups, at = [], 0
        for size in sizes:
            groups.append(refs[at : at + size])
            at += size
        left_refs, right_refs, ins, (small_ref,), (late,), (small_out,), more_refs = groups[:7]
        steps_refs, steps_sems, (other_lefts, other_right, turned, pair_send, pair_recv), scratch, own = groups[7:]
        parts, small_mine, smalls, core_small, small_send, small_recv, core_send, core_recv = own
        meanwhile = begin(ins, more_refs, scratch)
        me, core = lax.axis_index("mem"), lax.axis_index("dp")
        barrier = pltpu.get_barrier_semaphore()
        peers = [lax.rem(me + k, sources) for k in range(1, sources)]
        for peer in peers:
            pl.semaphore_signal(barrier, inc=1, device_id={"mem": peer}, device_id_type=mesh_type)
        pl.semaphore_signal(barrier, inc=1, device_id={"dp": 1 - core}, device_id_type=mesh_type)
        pl.semaphore_wait(barrier, sources)

        def merge(blocks):
            total = blocks[0][...].astype(jnp.float32)
            for block in blocks[1:]:
                total = total + block[...].astype(jnp.float32)
            return total

        def pack(target, total):
            target[...] = total.astype(jnp.bfloat16)

        def across_cores(source, target, i):
            copy = pltpu.make_async_remote_copy(
                src_ref=source,
                dst_ref=target,
                send_sem=core_send.at[i],
                recv_sem=core_recv.at[i],
                device_id={"dp": 1 - core},
                device_id_type=mesh_type,
            )
            copy.start()
            return copy

        pair_copies = exchange_pairs(
            left_refs, right_refs, other_lefts, other_right, pair_send, pair_recv
        )

        def store(column, value):
            parts[:, column : column + value.shape[1]] = value

        pair_products(
            left_refs, right_refs, other_lefts, other_right, turned, store, pair_copies
        )
        small_copies = [
            remote(small_mine, smalls.at[me], small_send.at[i], small_recv.at[me], peer)
            for i, peer in enumerate(peers)
        ]

        def between():
            meanwhile()
            small_mine[...] = small_ref[...]
            for i in range(width // 128):
                small_mine[i : i + 1, :] = more_refs[-1][:, i * 128 : (i + 1) * 128]
            smalls[me] = small_mine[...]
            for copy in small_copies:
                copy.start()

        final, still_open = reduce_steps(parts, sources, steps_refs, steps_sems, merge, pack, between)
        for here, blocks in final:
            late[core, here] = merge(blocks).astype(jnp.bfloat16)
        late_copy = across_cores(late.at[core], late.at[core], 0)
        for peer in peers:
            remote(
                smalls.at[peer], smalls.at[peer], small_send.at[0], small_recv.at[peer], peer
            ).wait_recv()
        group_small = smalls[0]
        for i in range(1, sources):
            group_small = group_small + smalls[i]
        core_small[0] = group_small
        small_copy = across_cores(core_small.at[0], core_small.at[1], 1)
        for copy in (late_copy, small_copy):
            copy.wait()
        small_out[...] = core_small[0] + core_small[1]
        for copy in still_open + small_copies + pair_copies:
            copy.wait_send()

    vmem = pl.BlockSpec(memory_space=pltpu.VMEM)
    return pl.pallas_call(
        kernel,
        in_specs=[vmem] * (2 * count) + specs + [vmem],
        out_specs=[vmem] * (2 + len(more_out)),
        out_shape=[jax.ShapeDtypeStruct((2, rows, total), jnp.bfloat16)]
        + [jax.ShapeDtypeStruct(small.shape, small.dtype)]
        + more_out,
        scratch_shapes=ref_shapes
        + sem_shapes
        + pair_shapes
        + more_scratch
        + [
            pltpu.VMEM((width, total), jnp.bfloat16),
            pltpu.VMEM(small.shape, small.dtype),
            pltpu.VMEM((sources, *small.shape), small.dtype),
            pltpu.VMEM((2, *small.shape), small.dtype),
        ]
        + [pltpu.SemaphoreType.DMA((sources,))] * 2
        + [pltpu.SemaphoreType.DMA((2,))] * 2,
        compiler_params=pltpu.CompilerParams(
            collective_id=collective_id, has_side_effects=True, vmem_limit_bytes=VMEM_LIMIT
        ),
        cost_estimate=lasting(45),
        name="finish_grads",
    )(*lefts, *rights, *arrays, small)


def on_device(
    tokens,
    attn_gain,
    qkv_weight,
    out_weight,
    bias_table,
    gate_logit,
    ffn_gain,
    up_weight,
    down_weight,
    memory_keys,
    memory_values,
    book_lengths,
    slot_shard,
    slot_index,
    slot_live,
    cotangent,
):
    rows, width = tokens.shape
    heads, buckets = bias_table.shape
    head_dim = width // heads
    top_count = slot_index.shape[2]
    hidden = up_weight.shape[1]
    groups = lax.axis_size("mem")
    capacity = -(-3 * rows * heads * top_count // (2 * groups) // 128) * 128
    score_scale = 1.0 / math.sqrt(head_dim)
    repeats = W // rows
    span = W + 2 * rows
    before = W - jnp.arange(span, dtype=jnp.int32)
    after = jnp.arange(span, dtype=jnp.int32)

    def bias_rows(offset):
        reached = (offset >= 0) & (offset < W)
        hot = (bucket_of(offset)[:, None] == jnp.arange(buckets, dtype=jnp.int32)) & reached[:, None]
        rows_of_bias = jnp.einsum(
            "rb,hb->hr", hot.astype(jnp.float32), bias_table, precision=lax.Precision.HIGHEST
        )
        return rows_of_bias + jnp.where(reached, 0.0, masked_score)

    before_bias, after_bias = bias_rows(before), bias_rows(after)
    bucket = bucket_of(jnp.arange(W, dtype=jnp.int32))
    one_hot = (bucket[:, None] == jnp.arange(buckets, dtype=jnp.int32)).astype(jnp.float32)
    tokens_f = tokens.astype(jnp.float32)
    normed_in = normed(tokens_f, attn_gain).astype(jnp.bfloat16)
    projected = jnp.dot(normed_in, qkv_weight, preferred_element_type=jnp.float32).astype(
        jnp.bfloat16
    )
    slots = memory_keys.shape[0]
    requests = place_requests(slot_shard, slot_index, slot_live, groups, capacity, slots)
    incoming = lax.all_to_all(requests, "mem", split_axis=0, concat_axis=0, tiled=True)
    keys_values, _ = lax.optimization_barrier((projected[:, width:], requests))
    halos = [passed_along(keys_values, "mem", distance) for distance in range(repeats, 0, -1)]
    index, row_ids, bounds = read_lists(incoming, heads, rows, slots)
    bounds = bounds.reshape(-1)
    key_rows, value_rows = gather_rows(
        index.reshape(-1), bounds, memory_keys, memory_values, heads, groups, capacity
    )
    all_queries = lax.all_gather(projected[:, :width], "mem", axis=0, tiled=True)
    local = local_forward(before_bias, book_lengths, projected, halos, heads, score_scale)
    partial = memory_forward(
        bounds,
        all_queries,
        key_rows,
        value_rows,
        row_ids,
        heads,
        groups,
        rows,
        score_scale,
    )
    if groups == 16:
        memory_out, mem_log, local_out, local_log = merge_partials(partial, groups, 1, heads, local)
    else:
        local_out, local_log = run_alone("local_forward", local)
        partial = lax.all_to_all(
            partial.reshape(groups, rows, width + 128),
            "mem",
            split_axis=0,
            concat_axis=0,
            tiled=True,
        ).reshape(groups * rows, width + 128)
        memory_out, mem_log = combine_partials(partial, heads, groups, rows)
    gate_share = jax.nn.sigmoid(gate_logit)
    share_wide = jnp.repeat(gate_share, head_dim)[None, :]
    mixed_heads = (share_wide * memory_out + (1.0 - share_wide) * local_out).astype(jnp.bfloat16)
    residual = tokens_f + jnp.dot(mixed_heads, out_weight, preferred_element_type=jnp.float32)
    normed_mid_f, norm_mid_back = jax.vjp(normed, residual, ffn_gain)
    normed_mid = normed_mid_f.astype(jnp.bfloat16)
    activated, d_up, ffn_branch, d_mid = feed_forward(normed_mid, cotangent, up_weight, down_weight)
    block_out = (residual + ffn_branch).astype(jnp.bfloat16)
    d_resid_part, ffn_gain_part = norm_mid_back(d_mid)
    d_residual = cotangent.astype(jnp.float32) + d_resid_part
    d_branch = d_residual.astype(jnp.bfloat16)
    early_halves = pair_grads(
        [mixed_heads, normed_mid, cotangent], [d_branch, d_up, activated], 5
    )
    early_sums = scattered(early_halves)
    d_after, _ = lax.optimization_barrier((d_branch, early_halves))
    d_mixed = lax.dot_general(
        d_after, out_weight, contract_cols, preferred_element_type=jnp.float32
    )
    gate_products, sent_grads = sent_gradients(
        d_mixed, memory_out, local_out, mem_log, local_log, gate_share, heads
    )
    gate_part = jnp.sum(gate_products, axis=1) * gate_share * (1.0 - gate_share)
    local = local_queries(
        before_bias,
        book_lengths,
        projected,
        halos,
        d_mixed,
        local_out,
        local_log,
        gate_share,
        heads,
        score_scale,
    )
    if groups == 16:
        all_grads, d_queries, diagonals = gather_group(sent_grads, groups, 2, local)
    else:
        all_grads = lax.all_gather(sent_grads, "mem", axis=0, tiled=True)
        d_queries, diagonals = run_alone("local_queries", local)
    bias_part = jnp.dot(diagonals[:, rows - 1 : rows - 1 + W], one_hot, precision=lax.Precision.HIGHEST)
    d_partial = memory_backward(
        bounds,
        all_queries,
        all_grads,
        key_rows,
        value_rows,
        row_ids,
        heads,
        groups,
        rows,
        score_scale,
    )
    local = local_keys(
        after_bias,
        book_lengths,
        projected,
        all_queries,
        all_grads,
        (1.0 - gate_share) / gate_share,
        repeats + 1,
        heads,
        score_scale,
    )
    if groups == 16:
        d_projected = sum_queries(d_partial, d_queries, groups, 3, score_scale, local)
    else:
        (d_projected,) = run_alone("local_keys", local)
        d_partial, d_projected = lax.optimization_barrier((d_partial, d_projected))
        d_partial = jnp.sum(
            lax.all_to_all(
                d_partial.reshape(groups, rows, width), "mem", split_axis=0, concat_axis=0, tiled=True
            ).astype(jnp.float32),
            axis=0,
        )
        d_queries = (d_queries + d_partial * score_scale).astype(jnp.bfloat16)
        d_projected = jnp.concatenate([d_queries, d_projected[:, width:]], axis=1)
    beside = input_backward(tokens, attn_gain, d_projected, qkv_weight, d_residual)
    small = jnp.concatenate([ffn_gain_part, bias_part.reshape(-1), gate_part], axis=0)
    small = jnp.pad(small, (width, -small.shape[0] % 1024)).reshape(-1, 128)
    early_widths = [width, hidden, hidden]
    if groups == 16:
        late_both, small, tokens_grad, _ = finish_grads(
            [normed_in], [d_projected], small, groups, 4, beside
        )
        early_sums, small = lax.optimization_barrier((early_sums, small))
        early_both = join_halves(early_sums, 7)
    else:
        tokens_grad, attn_gain_part = run_alone("input_backward", beside)
        late_halves = pair_grads([normed_in], [d_projected], 6)
        late_halves, early_sums = lax.optimization_barrier((late_halves, early_sums))
        late_both = lax.all_gather(scattered(late_halves), "dp", axis=0)
        early_both = lax.all_gather(early_sums, "dp", axis=0)
        small = lax.psum(small.at[: width // 128].set(attn_gain_part.reshape(-1, 128)), ("dp", "mem"))
    qkv_grad, out_grad, up_grad, down_grad, attn_sum, ffn_sum, bias_sum, gate_sum = write_results(
        late_both, [3 * width], early_both, early_widths, small, heads, buckets
    )
    return (
        block_out,
        tokens_grad,
        qkv_grad,
        out_grad,
        up_grad,
        down_grad,
        attn_sum.reshape(-1),
        ffn_sum.reshape(-1),
        bias_sum,
        gate_sum.reshape(-1),
    )


def solution(mesh):
    in_specs = (
        P(("dp", "mem"), None),
        P(),
        P(),
        P(),
        P(),
        P(),
        P(),
        P(),
        P(),
        P("mem", None),
        P("mem", None),
        P("dp", None),
        P(("dp", "mem"), None, None, None),
        P(("dp", "mem"), None, None),
        P(("dp", "mem"), None, None),
        P(("dp", "mem"), None),
    )
    out_specs = (
        P(("dp", "mem"), None),
        P(("dp", "mem"), None),
        P("mem", None),
        P("mem", None),
        P("mem", None),
        P("mem", None),
        P(),
        P(),
        P(),
        P(),
    )
    return jax.shard_map(
        on_device, mesh=mesh, in_specs=in_specs, out_specs=out_specs, check_vma=False
    )
```

```python
import math

import jax
import jax.numpy as jnp
from jax import lax
from jax.experimental import pallas as pl
from jax.experimental.pallas import tpu as pltpu
from jax.sharding import PartitionSpec as P

W = 512
VMEM_LIMIT = 56 * 1024 * 1024


eps_norm = 1e-06
bucket_edges = tuple((math.ceil(16 * 8 ** (edge_step / 16)) for edge_step in range(1, 16)))
masked_score = -1e30
dead_score = -10000.0
contract_rows = (((0,), (0,)), ((), ()))
contract_cols = (((1,), (1,)), ((), ()))


def passed_along(value, axis, by):
    size = lax.axis_size(axis)
    pairs = [(i, i + by) for i in range(size) if 0 <= i + by < size]
    return lax.ppermute(value, axis, pairs)


def bucket_of(offset):
    past_edges = sum(((offset >= edge_pos).astype(jnp.int32) for edge_pos in bucket_edges))
    return jnp.where(offset < 16, offset, 16 + past_edges)


def normed(values, gain_vec):
    return (
        values * lax.rsqrt(jnp.mean(values * values, axis=-1, keepdims=True) + eps_norm) * gain_vec
    )


def place_requests(slot_shard, slot_index, slot_live, owners, capacity, slots):
    rows, heads, top_count = slot_index.shape
    entries, empty = rows * heads * top_count, heads * rows * slots
    if (owners + 1) * empty >= 2**31:
        raise ValueError("codes exceed int32")
    row_of = (
        jnp.arange(heads, dtype=jnp.int32)[None, :] * rows
        + jnp.arange(rows, dtype=jnp.int32)[:, None]
    )
    owner = jnp.where(slot_live > 0, slot_shard[..., 0], owners)
    codes = owner * empty + row_of[:, :, None] * slots + slot_index
    codes = lax.sort(codes.reshape(-1), is_stable=False)
    ends = jnp.sum(
        (codes[None, :] < (jnp.arange(owners, dtype=jnp.int32) + 1)[:, None] * empty).astype(jnp.int32),
        axis=1,
    )
    starts = jnp.concatenate([jnp.zeros((1,), jnp.int32), ends[:-1]])
    tall = -(-entries // 128)
    codes = jnp.pad(codes, (0, tall * 128 - entries)).reshape(tall, 128)
    long = capacity // 128

    def kernel(starts_ref, ends_ref, codes_ref, lists_ref, padded):
        padded[:tall, :] = codes_ref[...]
        padded[tall:, :] = jnp.zeros((long + 8, 128), jnp.int32)
        lane = lax.broadcasted_iota(jnp.int32, (long, 128), 1)
        place = lax.broadcasted_iota(jnp.int32, (long, 128), 0) * 128 + lane

        @pl.loop(0, owners)
        def _(i):
            start, end = starts_ref[i], ends_ref[i]
            shift = start % 128
            lines = padded[pl.ds(start // 128, long + 1), :]
            turned = pltpu.roll(lines, (128 - shift) % 128, 1)
            joined = jnp.where(lane < 128 - shift, turned[:long], turned[1:])
            lists_ref[i] = jnp.where(place < end - start, joined - i * empty, empty)

    return pl.pallas_call(
        kernel,
        in_specs=[pl.BlockSpec(memory_space=pltpu.SMEM)] * 2 + [pl.BlockSpec(memory_space=pltpu.VMEM)],
        out_shape=jax.ShapeDtypeStruct((owners, long, 128), jnp.int32),
        scratch_shapes=[pltpu.VMEM((tall + long + 8, 128), jnp.int32)],
        cost_estimate=lasting(3),
        name="make_lists",
    )(starts, ends, codes)


def read_lists(incoming, heads, rows, slots):
    sources, long, _ = incoming.shape

    def kernel(lists_ref, index_ref, ids_ref, bounds_ref):
        lane = lax.broadcasted_iota(jnp.int32, (1, 128), 1)

        def read(source):
            codes = lists_ref[source]
            ids = lax.div(codes, slots)
            index = lax.div(ids, rows) * slots + lax.rem(codes, slots)
            index_ref[source] = jnp.where(ids < heads * rows, index, 0)
            ids_ref[source, :long, :] = ids
            ids_ref[source, long:, :] = jnp.full((1, 128), heads * rows, jnp.int32)
            bounds = jnp.zeros((1, 128), jnp.int32)
            for head in range(1, heads + 1):
                below = jnp.sum(
                    jnp.where(codes < head * rows * slots, 1.0, 0.0), axis=0, keepdims=True
                )
                below = jnp.sum(below, axis=1, keepdims=True).astype(jnp.int32)
                bounds = jnp.where(lane == head, below, bounds)
            bounds_ref[pl.ds(source, 1), :] = bounds

        if sources > 16:
            pl.loop(0, sources)(read)
        else:
            for source in range(sources):
                read(source)

    return pl.pallas_call(
        kernel,
        out_shape=[
            jax.ShapeDtypeStruct((sources, long, 128), jnp.int32),
            jax.ShapeDtypeStruct((sources, long + 1, 128), jnp.int32),
            jax.ShapeDtypeStruct((sources, 128), jnp.int32),
        ],
        cost_estimate=lasting(3),
        name="read_lists",
    )(incoming)


def gather_rows(index, bounds, memory_keys, memory_values, heads, sources, capacity):
    slots, width = memory_keys.shape
    head_dim = width // heads
    step, part = 128, 16

    def kernel(index_ref, bounds_ref, keys, values, out_keys, out_values, key_table, value_table, key_rows, value_rows):
        i = pl.program_id(0)

        @pl.when(i < heads)
        def _():
            place = pl.ds(pl.multiple_of(i * slots, slots), slots)
            key_table[place, :] = keys[...].astype(jnp.float32)
            value_table[place, :] = values[...].astype(jnp.float32)

        @pl.when(i >= heads)
        def _():
            source = i - heads

            used = (bounds_ref[source * 128 + heads] + step - 1) // step

            def store(group):
                for at in range(0, step, part):
                    here = pl.ds(pl.multiple_of(group * step, step) + at, part)
                    out_keys[here, :] = key_rows[at : at + part, :].astype(jnp.bfloat16)
                    out_values[here, :] = value_rows[at : at + part, :].astype(jnp.bfloat16)

            @pl.loop(0, used)
            def _(group):
                store(jnp.maximum(group - 1, 0))
                first = source * capacity + group * step
                for u in range(step):
                    row = index_ref[first + u]
                    key_rows[u : u + 1, :] = key_table[pl.ds(row, 1), :]
                    value_rows[u : u + 1, :] = value_table[pl.ds(row, 1), :]

            pl.when(used > 0)(lambda: store(used - 1))

            @pl.loop(used, capacity // step)
            def _(group):
                here = pl.ds(pl.multiple_of(group * step, step), step)
                out_keys[here, :] = jnp.zeros((step, head_dim), jnp.bfloat16)
                out_values[here, :] = jnp.zeros((step, head_dim), jnp.bfloat16)

    table_spec = pl.BlockSpec((slots, head_dim), lambda i, *_: (0, jnp.minimum(i, heads - 1)))
    out_spec = pl.BlockSpec((capacity, head_dim), lambda i, *_: (jnp.maximum(i - heads, 0), 0))
    out_shape = jax.ShapeDtypeStruct((sources * capacity, head_dim), jnp.bfloat16)
    return pl.pallas_call(
        kernel,
        grid_spec=pltpu.PrefetchScalarGridSpec(
            num_scalar_prefetch=2,
            grid=(heads + sources,),
            in_specs=[table_spec, table_spec],
            out_specs=[out_spec, out_spec],
            scratch_shapes=[
                pltpu.VMEM((heads * slots, head_dim), jnp.float32),
                pltpu.VMEM((heads * slots, head_dim), jnp.float32),
                pltpu.VMEM((step, head_dim), jnp.float32),
                pltpu.VMEM((step, head_dim), jnp.float32),
            ],
        ),
        out_shape=[out_shape, out_shape],
        compiler_params=pltpu.CompilerParams(vmem_limit_bytes=VMEM_LIMIT),
        cost_estimate=lasting(42),
        name="gather_rows",
    )(index, bounds, memory_keys, memory_values)


def lasting(microseconds):
    return pl.CostEstimate(flops=0, bytes_accessed=3_000_000 * microseconds, transcendentals=0)


def triple(stat):
    part = lax.broadcasted_iota(jnp.int32, stat.shape, 1) // 16
    high = stat.astype(jnp.bfloat16).astype(jnp.float32)
    rest = stat - high
    middle = rest.astype(jnp.bfloat16).astype(jnp.float32)
    low = rest - middle
    chosen = jnp.where(part == 0, high, jnp.where(part == 1, middle, jnp.where(part == 2, low, 0.0)))
    return chosen.astype(jnp.bfloat16)


def window_of(bounds, source, head, heads, span, capacity):
    first, last = bounds[source * 128 + head], bounds[source * 128 + head + 1]
    start = jnp.minimum(first // 16 * 16, capacity - span)
    extra = jnp.maximum(last - start - 1, 0) // span
    return start, extra


def columns_of(head, head_dim):
    if isinstance(head, int):
        return slice(head * head_dim, (head + 1) * head_dim)
    return pl.ds(pl.multiple_of(head * head_dim, head_dim), head_dim)


def window_ids(id_ref, start, span):
    lines = id_ref[0, pl.ds(start // 128, span // 128 + 1), :]
    shift = start % 128
    turned = pltpu.roll(lines, (128 - shift) % 128, 1)
    lane = lax.broadcasted_iota(jnp.int32, (span // 128, 128), 1)
    return jnp.where(lane < 128 - shift, turned[:-1], turned[1:])


def owned(lines, first_row, count, start, least):
    row = lax.broadcasted_iota(jnp.int32, (count, 128), 0) + first_row
    masks = []
    for i in range(lines.shape[0]):
        mask = lines[i : i + 1, :] == row
        if least is not None:
            place = lax.broadcasted_iota(jnp.int32, (1, 128), 1) + start + i * 128
            mask = mask & (place >= least)
        masks.append(mask)
    return jnp.concatenate(masks, axis=1)


def memory_forward(bounds, queries, key_rows, value_rows, row_ids, heads, sources, rows, score_scale):
    capacity, head_dim = key_rows.shape[0] // sources, key_rows.shape[1]
    width = heads * head_dim
    span = min(384, capacity)
    chunk = math.gcd(rows, 32)

    def kernel(bounds_ref, q_ref, k_ref, v_ref, id_ref, out_ref, sums, tops, totals, raw, weights):
        source = pl.program_id(0)
        lane = lax.broadcasted_iota(jnp.int32, (chunk, 128), 1) % 16

        def window(heads_here, starts, least):
            here = [pl.ds(pl.multiple_of(start, 16), span) for start in starts]
            columns = [columns_of(head, head_dim) for head in heads_here]
            for slot in range(len(starts)):
                raw[slot] = lax.dot_general(
                    q_ref[:, columns[slot]],
                    k_ref[here[slot], :],
                    contract_cols,
                    preferred_element_type=jnp.float32,
                )
            for slot, (head, start) in enumerate(zip(heads_here, starts)):
                lines = window_ids(id_ref, start, span)
                for at in range(0, rows, chunk):
                    some = slice(at, at + chunk)
                    mine = owned(lines, head * rows + at, chunk, start, least)
                    scores = jnp.where(mine, raw[slot, some, :], masked_score)
                    top = jnp.maximum(jnp.max(scores, axis=1, keepdims=True), 0.1 * masked_score)
                    if least is not None:
                        old_top = jnp.max(
                            jnp.where(lane == head, tops[some, :], masked_score), axis=1, keepdims=True
                        )
                        top = jnp.maximum(top, old_top)
                    exps = jnp.exp((scores - top) * score_scale)
                    weights[slot, some, :] = exps.astype(jnp.bfloat16)
                    total = jnp.sum(exps, axis=1, keepdims=True)
                    if least is not None:
                        faded = jnp.exp((old_top - top) * score_scale)
                        sums[some, columns[slot]] = sums[some, columns[slot]] * faded
                        total = total + totals[some, :] * faded
                    tops[some, :] = jnp.where(lane == head, top, tops[some, :])
                    totals[some, :] = jnp.where(lane == heads + head, total, totals[some, :])
            for slot in range(len(starts)):
                found = jnp.dot(
                    weights[slot], v_ref[here[slot], :], preferred_element_type=jnp.float32
                )
                sums[:, columns[slot]] = found if least is None else sums[:, columns[slot]] + found

        tops[...] = jnp.zeros_like(tops)
        totals[...] = jnp.zeros_like(totals)

        windows = [window_of(bounds_ref, source, head, heads, span, capacity) for head in range(heads)]
        window(list(range(heads)), [start for start, _ in windows], None)

        @pl.when(sum(extra for _, extra in windows) > 0)
        def _():
            @pl.loop(0, heads)
            def _(head):
                start, extra = window_of(bounds_ref, source, head, heads, span, capacity)

                @pl.loop(0, extra)
                def _(turn):
                    least = start + (turn + 1) * span
                    window([head], [jnp.minimum(least, capacity - span)], least)

        out_ref[:, :width] = sums[...].astype(jnp.bfloat16)
        wide = lax.broadcasted_iota(jnp.int32, (rows, 128), 1) % 16
        out_ref[:, width:] = triple(jnp.where(wide < heads, tops[...] * score_scale, totals[...]))

    return pl.pallas_call(
        kernel,
        grid_spec=pltpu.PrefetchScalarGridSpec(
            num_scalar_prefetch=1,
            grid=(sources,),
            in_specs=[
                pl.BlockSpec((rows, width), lambda i, *_: (i, 0)),
                pl.BlockSpec((capacity, head_dim), lambda i, *_: (i, 0)),
                pl.BlockSpec((capacity, head_dim), lambda i, *_: (i, 0)),
                pl.BlockSpec((1, *row_ids.shape[1:]), lambda i, *_: (i, 0, 0)),
            ],
            out_specs=pl.BlockSpec((rows, width + 128), lambda i, *_: (i, 0)),
            scratch_shapes=[
                pltpu.VMEM((rows, width), jnp.float32),
                pltpu.VMEM((rows, 128), jnp.float32),
                pltpu.VMEM((rows, 128), jnp.float32),
                pltpu.VMEM((heads, rows, span), jnp.float32),
                pltpu.VMEM((heads, rows, span), jnp.bfloat16),
            ],
        ),
        out_shape=jax.ShapeDtypeStruct((sources * rows, width + 128), jnp.bfloat16),
        compiler_params=pltpu.CompilerParams(vmem_limit_bytes=VMEM_LIMIT),
        cost_estimate=lasting(25),
        name="memory_forward",
    )(bounds, queries, key_rows, value_rows, row_ids)


def combine_partials(partial, heads, sources, rows):
    width = partial.shape[1] - 128
    head_dim = width // heads

    def kernel(part_ref, out_ref, log_ref, sums, tops, totals):
        i = pl.program_id(0)

        @pl.when(i == 0)
        def _():
            sums[...] = jnp.zeros_like(sums)
            tops[...] = jnp.full_like(tops, masked_score)
            totals[...] = jnp.zeros_like(totals)

        stat = part_ref[:, width:].astype(jnp.float32)
        stat = stat + pltpu.roll(stat, 128 - 16, 1) + pltpu.roll(stat, 128 - 32, 1)
        new_total = pltpu.roll(stat, 128 - heads, 1)
        top = jnp.maximum(tops[...], stat)
        old_fade, new_fade = jnp.exp(tops[...] - top), jnp.exp(stat - top)
        tops[...] = top
        totals[...] = totals[...] * old_fade + new_total * new_fade
        for head in range(heads):
            columns = slice(head * head_dim, (head + 1) * head_dim)
            sums[:, columns] = (
                sums[:, columns] * old_fade[:, head : head + 1]
                + part_ref[:, columns].astype(jnp.float32) * new_fade[:, head : head + 1]
            )

        @pl.when(i == sources - 1)
        def _():
            live = totals[...] > 0
            total = jnp.where(live, totals[...], 1.0)
            log_ref[...] = jnp.where(live, tops[...] + jnp.log(total), 0.0)
            for head in range(heads):
                columns = slice(head * head_dim, (head + 1) * head_dim)
                out_ref[:, columns] = sums[:, columns] / total[:, head : head + 1]

    return pl.pallas_call(
        kernel,
        grid=(sources,),
        in_specs=[pl.BlockSpec((rows, width + 128), lambda i: (i, 0))],
        out_specs=[
            pl.BlockSpec((rows, width), lambda i: (0, 0)),
            pl.BlockSpec((rows, 128), lambda i: (0, 0)),
        ],
        scratch_shapes=[
            pltpu.VMEM((rows, width), jnp.float32),
            pltpu.VMEM((rows, 128), jnp.float32),
            pltpu.VMEM((rows, 128), jnp.float32),
        ],
        out_shape=[
            jax.ShapeDtypeStruct((rows, width), jnp.float32),
            jax.ShapeDtypeStruct((rows, 128), jnp.float32),
        ],
        compiler_params=pltpu.CompilerParams(vmem_limit_bytes=VMEM_LIMIT),
        cost_estimate=lasting(13),
        name="combine_partials",
    )(partial)


def memory_backward(bounds, queries, grads, key_rows, value_rows, row_ids, heads, sources, rows, score_scale):
    capacity, head_dim = key_rows.shape[0] // sources, key_rows.shape[1]
    width = heads * head_dim
    span = min(384, capacity)
    chunk = math.gcd(rows, 32)

    def kernel(bounds_ref, q_ref, g_ref, k_ref, v_ref, id_ref, out_ref, sums, stats, raw, products, slopes):
        source = pl.program_id(0)
        stats[...] = joined_tile(g_ref[:, width : width + 128])

        def window(heads_here, starts, least):
            here = [pl.ds(pl.multiple_of(start, 16), span) for start in starts]
            columns = [columns_of(head, head_dim) for head in heads_here]
            for slot in range(len(starts)):
                raw[slot] = lax.dot_general(
                    q_ref[:, columns[slot]],
                    k_ref[here[slot], :],
                    contract_cols,
                    preferred_element_type=jnp.float32,
                )
                products[slot] = lax.dot_general(
                    g_ref[:, columns[slot]],
                    v_ref[here[slot], :],
                    contract_cols,
                    preferred_element_type=jnp.float32,
                )
            for slot, (head, start) in enumerate(zip(heads_here, starts)):
                lines = window_ids(id_ref, start, span)
                turned = stats[...]
                if least is not None:
                    turned = pltpu.roll(turned, 128 - head, 1)
                elif head:
                    turned = turned[:, head:]
                for at in range(0, rows, chunk):
                    some = slice(at, at + chunk)
                    mine = owned(lines, head * rows + at, chunk, start, least)
                    log, delta = turned[some, :1], turned[some, heads : heads + 1]
                    probs = jnp.exp(jnp.where(mine, raw[slot, some, :] * score_scale - log, dead_score))
                    slopes[slot, some, :] = (probs * (products[slot, some, :] - delta)).astype(
                        jnp.bfloat16
                    )
            for slot in range(len(starts)):
                found = jnp.dot(
                    slopes[slot], k_ref[here[slot], :], preferred_element_type=jnp.float32
                )
                sums[:, columns[slot]] = found if least is None else sums[:, columns[slot]] + found

        windows = [window_of(bounds_ref, source, head, heads, span, capacity) for head in range(heads)]
        window(list(range(heads)), [start for start, _ in windows], None)

        @pl.when(sum(extra for _, extra in windows) > 0)
        def _():
            @pl.loop(0, heads)
            def _(head):
                start, extra = window_of(bounds_ref, source, head, heads, span, capacity)

                @pl.loop(0, extra)
                def _(turn):
                    least = start + (turn + 1) * span
                    window([head], [jnp.minimum(least, capacity - span)], least)

        out_ref[...] = sums[...].astype(jnp.bfloat16)

    return pl.pallas_call(
        kernel,
        grid_spec=pltpu.PrefetchScalarGridSpec(
            num_scalar_prefetch=1,
            grid=(sources,),
            in_specs=[
                pl.BlockSpec((rows, width), lambda i, *_: (i, 0)),
                pl.BlockSpec((rows, width + 128), lambda i, *_: (i, 0)),
                pl.BlockSpec((capacity, head_dim), lambda i, *_: (i, 0)),
                pl.BlockSpec((capacity, head_dim), lambda i, *_: (i, 0)),
                pl.BlockSpec((1, *row_ids.shape[1:]), lambda i, *_: (i, 0, 0)),
            ],
            out_specs=pl.BlockSpec((rows, width), lambda i, *_: (i, 0)),
            scratch_shapes=[
                pltpu.VMEM((rows, width), jnp.float32),
                pltpu.VMEM((rows, 128), jnp.float32),
                pltpu.VMEM((heads, rows, span), jnp.float32),
                pltpu.VMEM((heads, rows, span), jnp.float32),
                pltpu.VMEM((heads, rows, span), jnp.bfloat16),
            ],
        ),
        out_shape=jax.ShapeDtypeStruct((sources * rows, width), jnp.bfloat16),
        compiler_params=pltpu.CompilerParams(vmem_limit_bytes=VMEM_LIMIT),
        cost_estimate=lasting(25),
        name="memory_backward",
    )(bounds, queries, grads, key_rows, value_rows, row_ids)


def remote(source, target, send_sem, recv_sem, device):
    return pltpu.make_async_remote_copy(
        src_ref=source,
        dst_ref=target,
        send_sem=send_sem,
        recv_sem=recv_sem,
        device_id={"mem": device},
        device_id_type=pl.DeviceIdType.MESH,
    )


def grid_place(depth):
    me = lax.axis_index("mem")
    layer, column = me // 4, me % 4
    beside_x = column + 1 - 2 * (column % 2)
    beside_y = column + 2 - 4 * (column // 2)
    across = 3 - column

    def index_of(step, place):
        return (layer + step + depth) % depth * 4 + place

    return me, column, beside_x, beside_y, across, index_of


def greet(devices):
    barrier = pltpu.get_barrier_semaphore()
    for device in devices:
        pl.semaphore_signal(
            barrier, inc=1, device_id={"mem": device}, device_id_type=pl.DeviceIdType.MESH
        )
    pl.semaphore_wait(barrier, len(devices))


def gather_group(block, sources, collective_id, beside):
    rows, width = block.shape
    depth, half = sources // 4, rows // 2
    slots = 2 * depth - 1
    arrays, specs, more_out, more_scratch, begin = beside
    ins, outs = len(arrays), len(more_out)

    def kernel(x_ref, *refs):
        in_refs, (out_ref, *more_refs) = refs[:ins], refs[ins : ins + 1 + outs]
        (own_sem, send, recv), scratch = refs[ins + 1 + outs : ins + 4 + outs], refs[ins + 4 + outs :]
        meanwhile = begin(in_refs, more_refs, scratch)
        me = lax.axis_index("mem")
        layer, column = me // 4, me % 4
        to_x = me + 1 - 2 * (column % 2)
        to_y = me + 2 - 4 * (column // 2)
        across = layer * 4 + 3 - column
        has_above, has_below = layer + 1 < depth, layer > 0
        barrier = pltpu.get_barrier_semaphore()

        def signal(device):
            pl.semaphore_signal(
                barrier, inc=1, device_id={"mem": device}, device_id_type=pl.DeviceIdType.MESH
            )

        signal(to_x)
        signal(to_y)
        pl.when(has_above)(lambda: signal(me + 4))
        pl.when(has_below)(lambda: signal(me - 4))
        pl.semaphore_wait(barrier, 2 + has_above.astype(jnp.int32) + has_below.astype(jnp.int32))

        def part_of(index, part):
            start = pl.multiple_of(index * rows + part * half, half)
            return out_ref.at[pl.ds(start, half), :]

        own = pltpu.make_async_copy(x_ref, out_ref.at[pl.ds(pl.multiple_of(me * rows, rows), rows), :], own_sem)
        own.start()
        sent = []

        def push(condition, source, target, kind, slot, to_slot, part, device):
            copy = remote(source, target, send.at[kind, slot, part], recv.at[kind, to_slot, part], device)
            if condition is None:
                copy.start()
            else:
                pl.when(condition)(copy.start)
            sent.append((condition, copy))

        def arrived(index, kind, slot, part):
            target = part_of(index, part)
            remote(target, target, send.at[kind, slot, part], recv.at[kind, slot, part], to_x).wait_recv()

        def up_slot(distance):
            return distance

        def down_slot(distance):
            return depth - 1 + distance

        for part in (0, 1):
            mine = x_ref.at[pl.ds(part * half, half), :]
            push(has_above, mine, part_of(me, part), 0, 0, down_slot(1), part, me + 4)
            push(has_below, mine, part_of(me, part), 1, 0, up_slot(1), part, me - 4)
            mine_y = x_ref.at[pl.ds((1 - part) * half, half), :]
            push(None, mine, part_of(me, part), 2, 0, 0, part, to_x)
            push(None, mine_y, part_of(me, 1 - part), 3, 0, 0, 1 - part, to_y)

        def pass_on(condition, step, slot):
            def go():
                arrived(to_x + step, 2, slot, 0)
                copy_a.start()
                arrived(to_y + step, 3, slot, 1)
                copy_b.start()

            source_a, source_b = part_of(to_x + step, 0), part_of(to_y + step, 1)
            copy_a = remote(source_a, source_a, send.at[4, slot, 0], recv.at[4, slot, 0], to_y)
            copy_b = remote(source_b, source_b, send.at[5, slot, 1], recv.at[5, slot, 1], to_x)
            sent.append((condition, copy_a))
            sent.append((condition, copy_b))
            if condition is None:
                go()
            else:
                pl.when(condition)(go)

        for distance in range(1, depth):
            from_above, from_below = layer + distance < depth, layer - distance >= 0

            def take(kind, back_kind, step, slot, next_slot, onward, onward_device):
                for part in (0, 1):
                    arrived(me + step, kind, slot, part)
                    here = part_of(me + step, part)
                    if next_slot is not None:
                        pl.when(onward)(
                            remote(
                                here, here, send.at[kind, slot, part], recv.at[kind, next_slot, part], onward_device
                            ).start
                        )
                    remote(here, here, send.at[2, slot, part], recv.at[2, slot, part], to_x).start()
                    remote(here, here, send.at[3, slot, part], recv.at[3, slot, part], to_y).start()

            last = distance == depth - 1
            pl.when(from_above)(
                lambda: take(
                    1, 0, 4 * distance, up_slot(distance), None if last else up_slot(distance + 1), has_below, me - 4
                )
            )
            pl.when(from_below)(
                lambda: take(
                    0, 1, -4 * distance, down_slot(distance), None if last else down_slot(distance + 1), has_above, me + 4
                )
            )
            for condition, step, slot, kind, onward in (
                (from_above, 4 * distance, up_slot(distance), 1, has_below),
                (from_below, -4 * distance, down_slot(distance), 0, has_above),
            ):
                for part in (0, 1):
                    here = part_of(me + step, part)
                    if not last:
                        sent.append((condition & onward, remote(here, here, send.at[kind, slot, part], own_sem, me)))
                    sent.append((condition, remote(here, here, send.at[2, slot, part], own_sem, to_x)))
                    sent.append((condition, remote(here, here, send.at[3, slot, part], own_sem, to_y)))
            meanwhile(distance - 1, depth - 1)
            if distance == 1:
                pass_on(None, 0, 0)
            else:
                pass_on(layer + distance - 1 < depth, 4 * (distance - 1), up_slot(distance - 1))
                pass_on(layer - distance + 1 >= 0, -4 * (distance - 1), down_slot(distance - 1))
        pass_on(layer + depth - 1 < depth, 4 * (depth - 1), up_slot(depth - 1))
        pass_on(layer - depth + 1 >= 0, -4 * (depth - 1), down_slot(depth - 1))

        def close(step, slot):
            arrived(to_x + step, 2, slot, 1)
            arrived(to_y + step, 3, slot, 0)
            arrived(across + step, 4, slot, 0)
            arrived(across + step, 5, slot, 1)

        close(0, 0)
        for distance in range(1, depth):
            pl.when(layer + distance < depth)(lambda: close(4 * distance, up_slot(distance)))
            pl.when(layer - distance >= 0)(lambda: close(-4 * distance, down_slot(distance)))
        for condition, copy in sent:
            if condition is None:
                copy.wait_send()
            else:
                pl.when(condition)(copy.wait_send)
        own.wait()

    return pl.pallas_call(
        kernel,
        in_specs=[pl.BlockSpec(memory_space=pl.ANY), *specs],
        out_specs=[pl.BlockSpec(memory_space=pl.ANY)] + [pl.BlockSpec(memory_space=pltpu.VMEM)] * outs,
        out_shape=[jax.ShapeDtypeStruct((sources * rows, width), block.dtype), *more_out],
        scratch_shapes=[
            pltpu.SemaphoreType.DMA,
            pltpu.SemaphoreType.DMA((6, slots, 2)),
            pltpu.SemaphoreType.DMA((6, slots, 2)),
            *more_scratch,
        ],
        compiler_params=pltpu.CompilerParams(
            collective_id=collective_id, has_side_effects=True, vmem_limit_bytes=VMEM_LIMIT
        ),
        cost_estimate=lasting(50),
        name="gather_group",
    )(block, *arrays)


def reduce_steps(parts_ref, sources, refs, sems, merge, pack, beside=None):
    half_a, half_b, from_x, from_y, from_z, out_x, out_y, out_z = refs
    send, recv_a, recv_b, recv_x, recv_y, recv_z = sems
    rows = parts_ref.shape[0] // sources
    depth, half = sources // 4, rows // 2
    me, column, beside_x, beside_y, across, index_of = grid_place(depth)
    to_x, to_y = index_of(0, beside_x), index_of(0, beside_y)
    order = [*range(1, depth), 0]
    queues = {"x": [], "y": [], "z": []}
    first_limit = 2 if beside is None else depth

    def piece(index, part):
        return parts_ref.at[pl.ds(pl.multiple_of(index * rows + part * half, half), half), :]

    def part_rows(part):
        return pl.ds(part * half, half)

    def push(link, source, target, kind, k, recv_sem, device, limit=2):
        queue = queues[link]
        while link != "z" and len(queue) >= limit:
            queue.pop(0).wait_send()
        copy = remote(source, target, send.at[kind, k], recv_sem, device)
        copy.start()
        queue.append(copy)

    def arrived(target, recv_sem):
        remote(target, target, send.at[0, 0], recv_sem, to_x).wait_recv()

    def plane_rest(k):
        push("x", piece(index_of(k, beside_x), 0), from_x.at[k, part_rows(0)], 2, k, recv_x.at[0, k], to_x)
        push("y", piece(index_of(k, beside_y), 1), from_y.at[k, part_rows(1)], 3, k, recv_y.at[1, k], to_y)

    def plane_merged(k):
        arrived(half_a.at[k], recv_a.at[k])
        pack(out_y.at[k], merge([piece(index_of(k, beside_y), 0), half_a.at[k]]))
        push("y", out_y.at[k], from_y.at[k, part_rows(0)], 4, k, recv_y.at[0, k], to_y)
        arrived(half_b.at[k], recv_b.at[k])
        pack(out_x.at[k], merge([piece(index_of(k, beside_x), 1), half_b.at[k]]))
        push("x", out_x.at[k], from_x.at[k, part_rows(1)], 5, k, recv_x.at[1, k], to_x)

    def column_step(k):
        for part in (0, 1):
            here = part_rows(part)
            arrived(from_x.at[k, here], recv_x.at[part, k])
            arrived(from_y.at[k, here], recv_y.at[part, k])
            if k:
                blocks = [piece(index_of(k, column), part), from_x.at[k, here], from_y.at[k, here]]
                pack(out_z.at[k, here], merge(blocks))
        if k:
            push("z", out_z.at[k], from_z.at[k], 6, k, recv_z.at[k], index_of(k, column))

    for k in order:
        far = index_of(k, across)
        push("x", piece(far, 0), half_a.at[k], 0, k, recv_a.at[k], to_x, first_limit)
        push("y", piece(far, 1), half_b.at[k], 1, k, recv_b.at[k], to_y, first_limit)
    if beside is not None:
        beside()
    for i, k in enumerate(order):
        plane_rest(k)
        plane_merged(k)
        if i:
            column_step(order[i - 1])
    column_step(order[-1])
    for k in range(1, depth):
        arrived(from_z.at[k], recv_z.at[k])
    final = []
    for part in (0, 1):
        here = part_rows(part)
        blocks = [piece(me, part), from_x.at[0, here], from_y.at[0, here]]
        final.append((here, blocks + [from_z.at[k, here] for k in range(1, depth)]))
    return final, [copy for queue in queues.values() for copy in queue]


def reduce_scratch(rows, width, dtype, sources):
    depth, half = sources // 4, rows // 2

    def slots(size):
        return pltpu.VMEM((depth, size, width), dtype)

    refs = [slots(half), slots(half), slots(rows), slots(rows), slots(rows)]
    refs += [slots(half), slots(half), slots(rows)]
    sems = [pltpu.SemaphoreType.DMA((7, depth))]
    sems += [pltpu.SemaphoreType.DMA((depth,))] * 2
    sems += [pltpu.SemaphoreType.DMA((2, depth))] * 2
    sems += [pltpu.SemaphoreType.DMA((depth,))]
    return refs, sems


def run_alone(name, beside):
    arrays, specs, out_shape, scratch, begin = beside
    ins, outs = len(arrays), len(out_shape)

    def kernel(*refs):
        begin(refs[:ins], refs[ins : ins + outs], refs[ins + outs :])()

    return pl.pallas_call(
        kernel,
        in_specs=specs,
        out_specs=[pl.BlockSpec(memory_space=pltpu.VMEM)] * outs,
        out_shape=out_shape,
        scratch_shapes=scratch,
        compiler_params=pltpu.CompilerParams(vmem_limit_bytes=VMEM_LIMIT),
        cost_estimate=lasting(8),
        name=name,
    )(*arrays)


def reduce_group(parts, sources, collective_id, merge, pack, finish, out_shape, beside):
    rows, width = parts.shape[0] // sources, parts.shape[1]
    depth = sources // 4
    arrays, specs, more_out, more_scratch, begin = beside
    ref_shapes, sem_shapes = reduce_scratch(rows, width, parts.dtype, sources)
    sizes = [len(arrays), len(out_shape), len(more_out), len(ref_shapes), len(sem_shapes), len(more_scratch)]

    def kernel(parts_ref, *refs):
        groups, at = [], 0
        for size in sizes:
            groups.append(refs[at : at + size])
            at += size
        ins, out_refs, more_refs, steps_refs, steps_sems, scratch = groups
        meanwhile = begin(ins, more_refs, scratch)
        last = finish
        if finish is None:
            meanwhile, last = meanwhile
        me, column, beside_x, beside_y, across, index_of = grid_place(depth)
        greet(
            [index_of(0, beside_x), index_of(0, beside_y)]
            + [index_of(-k, column) for k in range(1, depth)]
        )
        final, still_open = reduce_steps(
            parts_ref, sources, steps_refs, steps_sems, merge, pack, meanwhile
        )
        for here, blocks in final:
            if finish is None:
                last(here, merge(blocks))
            else:
                last([out.at[here] for out in out_refs], merge(blocks))
        for copy in still_open:
            copy.wait_send()

    vmem = pl.BlockSpec(memory_space=pltpu.VMEM)
    return pl.pallas_call(
        kernel,
        in_specs=[vmem, *specs],
        out_specs=[vmem] * (len(out_shape) + len(more_out)),
        out_shape=[*out_shape, *more_out],
        scratch_shapes=[*ref_shapes, *sem_shapes, *more_scratch],
        compiler_params=pltpu.CompilerParams(
            collective_id=collective_id, has_side_effects=True, vmem_limit_bytes=VMEM_LIMIT
        ),
        cost_estimate=lasting(50),
        name="reduce_group",
    )(parts, *arrays)


def sum_queries(parts, d_queries, sources, collective_id, score_scale, beside):
    rows, width = d_queries.shape
    arrays, specs, (whole,), more_scratch, begin = beside

    def merge(blocks):
        total = blocks[0][...].astype(jnp.float32)
        for block in blocks[1:]:
            total = total + block[...].astype(jnp.float32)
        return total

    def pack(target, total):
        target[...] = total.astype(parts.dtype)

    def begin_both(ins, outs, scratch):
        run = begin(ins[:-1], outs, scratch)

        def finish(here, total):
            outs[0][here, :width] = (ins[-1][here, :] + total * score_scale).astype(whole.dtype)

        return run, finish

    more = [*arrays, d_queries], [*specs, pl.BlockSpec(memory_space=pltpu.VMEM)], [whole], more_scratch, begin_both
    return reduce_group(parts, sources, collective_id, merge, pack, None, [], more)[0]


def merge_partials(parts, sources, collective_id, heads, beside):
    rows, width = parts.shape[0] // sources, parts.shape[1] - 128
    head_dim = width // heads

    def merge(blocks):
        stats = []
        for block in blocks:
            stat = block[:, width:].astype(jnp.float32)
            stats.append(stat + pltpu.roll(stat, 128 - 16, 1) + pltpu.roll(stat, 128 - 32, 1))
        top = stats[0]
        for stat in stats[1:]:
            top = jnp.maximum(top, stat)
        fades = [jnp.exp(stat - top) for stat in stats]
        total = sum(fade * pltpu.roll(stat, 128 - heads, 1) for fade, stat in zip(fades, stats))
        sums = []
        for head in range(heads):
            columns = slice(head * head_dim, (head + 1) * head_dim)
            sums.append(
                sum(
                    block[:, columns].astype(jnp.float32) * fade[:, head : head + 1]
                    for block, fade in zip(blocks, fades)
                )
            )
        return sums, top, total

    def pack(target, merged):
        sums, top, total = merged
        for head in range(heads):
            target[:, head * head_dim : (head + 1) * head_dim] = sums[head].astype(parts.dtype)
        lane = lax.broadcasted_iota(jnp.int32, top.shape, 1)
        stat = jnp.where(lane < heads, top, jnp.where(lane < 16, pltpu.roll(total, heads, 1), 0.0))
        target[:, width:] = triple(stat + pltpu.roll(stat, 16, 1) + pltpu.roll(stat, 32, 1))

    def finish(targets, merged):
        sums, top, total = merged
        live = total > 0
        total = jnp.where(live, total, 1.0)
        targets[1][...] = jnp.where(live, top + jnp.log(total), 0.0)
        for head in range(heads):
            targets[0][:, head * head_dim : (head + 1) * head_dim] = sums[head] / total[:, head : head + 1]

    out_shape = [
        jax.ShapeDtypeStruct((rows, width), jnp.float32),
        jax.ShapeDtypeStruct((rows, 128), jnp.float32),
    ]
    return reduce_group(parts, sources, collective_id, merge, pack, finish, out_shape, beside)


def scattered(halves):
    return lax.psum_scatter(halves, "mem", scatter_dimension=0, tiled=True)


def same_book(lengths_ref, first_row, rows, first_lane, lanes):
    row = lax.broadcasted_iota(jnp.int32, (rows, lanes), 0) + first_row
    lane = lax.broadcasted_iota(jnp.int32, (rows, lanes), 1) + first_lane
    end, same = 0, lane >= 0
    for i in range(lengths_ref.shape[1]):
        end = end + lengths_ref[0, i]
        same = same & ((row >= end) == (lane >= end))
    return same


def lane_tile(columns, rows):
    lane = lax.broadcasted_iota(jnp.int32, (rows, 128), 1)
    tile = jnp.zeros((rows, 128), jnp.float32)
    for i, column in enumerate(columns):
        tile = jnp.where(lane == i, column, tile)
    return tile


def split_tile(tile):
    lane = lax.broadcasted_iota(jnp.int32, tile.shape, 1)
    kept = jnp.where(lane < 32, tile, 0.0)
    kept = kept + pltpu.roll(kept, 32, 1) + pltpu.roll(kept, 64, 1)
    high = kept.astype(jnp.bfloat16).astype(jnp.float32)
    middle = (kept - high).astype(jnp.bfloat16).astype(jnp.float32)
    low = kept - high - middle
    part = lane // 32
    return jnp.where(part == 0, high, jnp.where(part == 1, middle, low)).astype(jnp.bfloat16)


def joined_tile(tile):
    tile = tile.astype(jnp.float32)
    return tile + pltpu.roll(tile, 128 - 32, 1) + pltpu.roll(tile, 128 - 64, 1)


def slanted(base, rows):
    return pltpu.roll(jnp.broadcast_to(base, (rows, base.shape[1])), 0, 1, stride=1, stride_axis=0)


def local_forward(base, lengths, own, halos, heads, score_scale):
    rows, width = own.shape[0], own.shape[1] // 3
    head_dim = width // heads
    count = len(halos) + 1

    def begin(ins, outs, scratch):
        base_ref, lengths_ref, own_ref, *halo_refs = ins
        out_ref, log_ref = outs

        def run():
            first = lax.axis_index("mem") * rows
            same = same_book(lengths_ref, first, rows, first - (count - 1) * rows, count * rows)
            logs = []
            for head in range(heads):
                columns = slice(head * head_dim, (head + 1) * head_dim)
                above = slice(width + head * head_dim, width + (head + 1) * head_dim)
                twice = slice(2 * width + head * head_dim, 2 * width + (head + 1) * head_dim)
                keys = [ref[:, columns] for ref in halo_refs] + [own_ref[:, above]]
                values = [ref[:, above] for ref in halo_refs] + [own_ref[:, twice]]
                q = own_ref[:, columns]
                raw = [
                    lax.dot_general(q, k, contract_cols, preferred_element_type=jnp.float32) for k in keys
                ]
                bias = slanted(base_ref[head : head + 1, :], rows)[:, : count * rows]
                scores = jnp.concatenate(raw, axis=1) * score_scale + bias
                scores = jnp.where(same, scores, masked_score)
                top = jnp.max(scores, axis=1, keepdims=True)
                weights = jnp.exp(scores - top)
                total = jnp.sum(weights, axis=1, keepdims=True)
                weights = (weights / total).astype(jnp.bfloat16)
                out_ref[:, columns] = sum(
                    jnp.dot(
                        weights[:, i * rows : (i + 1) * rows], v, preferred_element_type=jnp.float32
                    )
                    for i, v in enumerate(values)
                )
                logs.append(top + jnp.log(total))
            log_ref[...] = lane_tile(logs, rows)

        return run

    arrays = [base, lengths, own, *halos]
    vmem = pl.BlockSpec(memory_space=pltpu.VMEM)
    specs = [vmem, pl.BlockSpec(memory_space=pltpu.SMEM)] + [vmem] * (1 + len(halos))
    out_shape = [
        jax.ShapeDtypeStruct((rows, width), jnp.float32),
        jax.ShapeDtypeStruct((rows, 128), jnp.float32),
    ]
    return arrays, specs, out_shape, [], begin


def sent_gradients(d_mixed, memory_out, local_out, mem_log, local_log, share, heads):
    rows, width = d_mixed.shape
    head_dim = width // heads

    def kernel(mix_ref, mem_ref, loc_ref, mem_log_ref, log_ref, share_ref, gate_ref, sent_ref):
        mem_deltas, deltas = [], []
        for head in range(heads):
            columns = slice(head * head_dim, (head + 1) * head_dim)
            share_here = share_ref[head]
            d_mix, mem_here, loc_here = mix_ref[:, columns], mem_ref[:, columns], loc_ref[:, columns]
            d_mem = (share_here * d_mix).astype(jnp.bfloat16)
            d_out = ((1.0 - share_here) * d_mix).astype(jnp.bfloat16)
            sent_ref[:, columns] = d_mem
            mem_deltas.append(jnp.sum(d_mem.astype(jnp.float32) * mem_here, axis=1, keepdims=True))
            deltas.append(jnp.sum(d_out.astype(jnp.float32) * loc_here, axis=1, keepdims=True))
            gate_ref[head : head + 1, :] = jnp.sum(
                d_mix * (mem_here - loc_here), axis=0, keepdims=True
            )
        mem_logs = [mem_log_ref[:, head : head + 1] for head in range(heads)]
        logs = [log_ref[:, head : head + 1] for head in range(heads)]
        sent_ref[:, width:] = split_tile(lane_tile(mem_logs + mem_deltas + logs + deltas, rows))

    vmem = pl.BlockSpec(memory_space=pltpu.VMEM)
    return pl.pallas_call(
        kernel,
        in_specs=[vmem] * 5 + [pl.BlockSpec(memory_space=pltpu.SMEM)],
        out_shape=[
            jax.ShapeDtypeStruct((heads, head_dim), jnp.float32),
            jax.ShapeDtypeStruct((rows, width + 128), jnp.bfloat16),
        ],
        compiler_params=pltpu.CompilerParams(vmem_limit_bytes=VMEM_LIMIT),
        cost_estimate=lasting(3),
        name="sent_gradients",
    )(d_mixed, memory_out, local_out, mem_log, local_log, share)


def local_queries(
    base, lengths, own, halos, d_mixed, local_out, local_log, share, heads, score_scale
):
    rows, width = d_mixed.shape
    head_dim = width // heads
    count = len(halos) + 1
    span = base.shape[1]

    def begin(ins, outs, scratch):
        base_ref, lengths_ref, own_ref, mix_ref, loc_ref, log_ref, share_ref, *halo_refs = ins
        dq_ref, diagonal_ref = outs

        def some_heads(some):
            first = lax.axis_index("mem") * rows
            same = same_book(lengths_ref, first, rows, first - (count - 1) * rows, count * rows)
            turned = (
                lax.broadcasted_iota(jnp.int32, (rows, rows), 0)
                + lax.broadcasted_iota(jnp.int32, (rows, rows), 1)
                == rows - 1
            ).astype(jnp.bfloat16)
            for head in some:
                columns = slice(head * head_dim, (head + 1) * head_dim)
                above = slice(width + head * head_dim, width + (head + 1) * head_dim)
                twice = slice(2 * width + head * head_dim, 2 * width + (head + 1) * head_dim)
                keys = [ref[:, columns] for ref in halo_refs] + [own_ref[:, above]]
                values = [ref[:, above] for ref in halo_refs] + [own_ref[:, twice]]
                q = own_ref[:, columns]
                d_out = ((1.0 - share_ref[head]) * mix_ref[:, columns]).astype(jnp.bfloat16)
                delta = jnp.sum(
                    d_out.astype(jnp.float32) * loc_ref[:, columns], axis=1, keepdims=True
                )
                raw = [
                    lax.dot_general(q, k, contract_cols, preferred_element_type=jnp.float32)
                    for k in keys
                ]
                bias = slanted(base_ref[head : head + 1, :], rows)[:, : count * rows]
                scores = jnp.concatenate(raw, axis=1) * score_scale + bias
                probs = jnp.exp(jnp.where(same, scores - log_ref[:, head : head + 1], masked_score))
                products = [
                    lax.dot_general(d_out, v, contract_cols, preferred_element_type=jnp.float32)
                    for v in values
                ]
                slopes = (probs * (jnp.concatenate(products, axis=1) - delta)).astype(jnp.bfloat16)
                slope_blocks = [slopes[:, i * rows : (i + 1) * rows] for i in range(count)]
                dq_ref[:, columns] = score_scale * sum(
                    jnp.dot(s, k, preferred_element_type=jnp.float32)
                    for s, k in zip(slope_blocks, keys)
                )
                mirrored = [
                    jnp.dot(s, turned, preferred_element_type=jnp.float32) for s in slope_blocks[::-1]
                ]
                mirrored.append(jnp.zeros((rows, span - count * rows), jnp.float32))
                leaned = pltpu.roll(jnp.concatenate(mirrored, axis=1), 0, 1, stride=1, stride_axis=0)
                diagonal_ref[head : head + 1, :] = jnp.sum(leaned, axis=0, keepdims=True)

        def run(part=0, parts=1):
            some_heads(range(part * heads // parts, (part + 1) * heads // parts))

        return run

    vmem = pl.BlockSpec(memory_space=pltpu.VMEM)
    smem = pl.BlockSpec(memory_space=pltpu.SMEM)
    arrays = [base, lengths, own, d_mixed, local_out, local_log, share, *halos]
    specs = [vmem, smem] + [vmem] * 4 + [smem] + [vmem] * len(halos)
    out_shape = [
        jax.ShapeDtypeStruct((rows, width), jnp.float32),
        jax.ShapeDtypeStruct((heads, span), jnp.float32),
    ]
    return arrays, specs, out_shape, [], begin


def local_keys(base, lengths, own, queries, sent, ratio, count, heads, score_scale):
    rows, width = own.shape[0], own.shape[1] // 3
    head_dim = width // heads
    groups = queries.shape[0] // rows

    def begin(ins, outs, scratch):
        base_ref, lengths_ref, own_ref, ratio_ref, queries_ref, sent_ref = ins
        (out_ref,) = outs
        queries_here, sent_here, sems = scratch
        copies = []
        for i in range(count):
            index = jnp.minimum(lax.axis_index("mem") + i, groups - 1)
            there = pl.ds(pl.multiple_of(index * rows, rows), rows)
            copies.append(
                pltpu.make_async_copy(queries_ref.at[there, :], queries_here.at[i], sems.at[0, i])
            )
            copies.append(pltpu.make_async_copy(sent_ref.at[there, :], sent_here.at[i], sems.at[1, i]))
        for copy in copies:
            copy.start()

        def run():
            for copy in copies:
                copy.wait()
            first = lax.axis_index("mem") * rows
            same = same_book(lengths_ref, first, rows, first, count * rows)
            stats = jnp.concatenate([joined_tile(sent_here[i, :, width:]).T for i in range(count)], axis=1)
            for head in range(heads):
                columns = slice(head * head_dim, (head + 1) * head_dim)
                above = slice(width + head * head_dim, width + (head + 1) * head_dim)
                twice = slice(2 * width + head * head_dim, 2 * width + (head + 1) * head_dim)
                k, v = own_ref[:, above], own_ref[:, twice]
                qs = [queries_here[i, :, columns] for i in range(count)]
                gs = [
                    (sent_here[i, :, columns].astype(jnp.float32) * ratio_ref[head]).astype(jnp.bfloat16)
                    for i in range(count)
                ]
                raw = [
                    lax.dot_general(k, q, contract_cols, preferred_element_type=jnp.float32) for q in qs
                ]
                bias = slanted(base_ref[head : head + 1, :], rows)[:, : count * rows]
                scores = jnp.concatenate(raw, axis=1) * score_scale + bias
                log = stats[2 * heads + head : 2 * heads + head + 1, :]
                delta = stats[3 * heads + head : 3 * heads + head + 1, :]
                probs = jnp.exp(jnp.where(same, scores - log, masked_score))
                products = [
                    lax.dot_general(v, g, contract_cols, preferred_element_type=jnp.float32) for g in gs
                ]
                slopes = (probs * (jnp.concatenate(products, axis=1) - delta)).astype(jnp.bfloat16)
                weights = probs.astype(jnp.bfloat16)
                blocks = [slice(i * rows, (i + 1) * rows) for i in range(count)]
                d_key = sum(
                    jnp.dot(slopes[:, b], q, preferred_element_type=jnp.float32) for b, q in zip(blocks, qs)
                )
                d_value = sum(
                    jnp.dot(weights[:, b], g, preferred_element_type=jnp.float32)
                    for b, g in zip(blocks, gs)
                )
                out_ref[:, above] = (d_key * score_scale).astype(jnp.bfloat16)
                out_ref[:, twice] = d_value.astype(jnp.bfloat16)

        return run

    vmem, anywhere = pl.BlockSpec(memory_space=pltpu.VMEM), pl.BlockSpec(memory_space=pl.ANY)
    smem = pl.BlockSpec(memory_space=pltpu.SMEM)
    arrays = [base, lengths, own, ratio, queries, sent]
    specs = [vmem, smem, vmem, smem, anywhere, anywhere]
    scratch = [
        pltpu.VMEM((count, rows, width), jnp.bfloat16),
        pltpu.VMEM((count, rows, width + 128), jnp.bfloat16),
        pltpu.SemaphoreType.DMA((2, count)),
    ]
    return arrays, specs, [jax.ShapeDtypeStruct((rows, 3 * width), jnp.bfloat16)], scratch, begin


def feed_forward(normed_mid, cotangent, up_weight, down_weight):
    rows, width = normed_mid.shape
    hidden = up_weight.shape[1]
    block = math.gcd(hidden, 1024)

    def kernel(mid_ref, cot_ref, up_ref, down_ref, act_ref, d_up_ref, branch_ref, d_mid_ref):
        first = pl.program_id(0) == 0
        up = jnp.dot(mid_ref[...], up_ref[...], preferred_element_type=jnp.float32)
        d_act = jnp.dot(cot_ref[...], down_ref[...], preferred_element_type=jnp.float32)
        below = 0.5 * (1.0 + lax.erf(up * math.sqrt(0.5)))
        density = jnp.exp(-0.5 * up * up) * (1.0 / math.sqrt(2.0 * math.pi))
        act = (up * below).astype(jnp.bfloat16)
        d_up = (d_act * (below + up * density)).astype(jnp.bfloat16)
        act_ref[...] = act
        d_up_ref[...] = d_up
        branch = lax.dot_general(act, down_ref[...], contract_cols, preferred_element_type=jnp.float32)
        d_mid = lax.dot_general(d_up, up_ref[...], contract_cols, preferred_element_type=jnp.float32)
        branch_ref[...] = jnp.where(first, branch, branch_ref[...] + branch)
        d_mid_ref[...] = jnp.where(first, d_mid, d_mid_ref[...] + d_mid)

    whole = pl.BlockSpec((rows, width), lambda i: (0, 0))
    weight = pl.BlockSpec((width, block), lambda i: (0, i))
    middle = pl.BlockSpec((rows, block), lambda i: (0, i))
    return pl.pallas_call(
        kernel,
        grid=(hidden // block,),
        in_specs=[whole, whole, weight, weight],
        out_specs=[middle, middle, whole, whole],
        out_shape=[
            jax.ShapeDtypeStruct((rows, hidden), jnp.bfloat16),
            jax.ShapeDtypeStruct((rows, hidden), jnp.bfloat16),
            jax.ShapeDtypeStruct((rows, width), jnp.float32),
            jax.ShapeDtypeStruct((rows, width), jnp.float32),
        ],
        compiler_params=pltpu.CompilerParams(vmem_limit_bytes=VMEM_LIMIT),
        cost_estimate=lasting(15),
        name="feed_forward",
    )(normed_mid, cotangent, up_weight, down_weight)


def exchange_pairs(lefts, rights, other_lefts, other_right, send, recv):
    core = lax.axis_index("dp")
    copies, at = [], 0

    def push(source, target):
        i = len(copies)
        copy = pltpu.make_async_remote_copy(
            src_ref=source,
            dst_ref=target,
            send_sem=send.at[i],
            recv_sem=recv.at[i],
            device_id={"dp": 1 - core},
            device_id_type=pl.DeviceIdType.MESH,
        )
        copy.start()
        copies.append(copy)

    for i, (left, right) in enumerate(zip(lefts, rights)):
        half = right.shape[1] // 2
        push(left, other_lefts.at[i])
        there = pl.ds(pl.multiple_of((1 - core) * half, 128), half)
        push(right.at[:, there], other_right.at[:, pl.ds(at, half)])
        at += half
    return copies


def pair_products(lefts, rights, other_lefts, other_right, turned, store, copies):
    core = lax.axis_index("dp")
    rows = lefts[0].shape[0]
    at = 0
    for i, (left, right) in enumerate(zip(lefts, rights)):
        half = right.shape[1] // 2
        for copy in copies[2 * i : 2 * i + 2]:
            copy.wait_recv()
        turned[:, :rows] = left[...].T
        turned[:, rows:] = other_lefts[i].T
        block = math.gcd(half, 512)
        for column in range(0, half, block):
            kept = right[:, pl.ds(pl.multiple_of(core * half + column, 128), block)]
            both = jnp.concatenate([kept, other_right[:, at + column : at + column + block]], axis=0)
            store(
                at + column,
                jnp.dot(turned[...], both, preferred_element_type=jnp.float32).astype(jnp.bfloat16),
            )
        at += half


def pair_scratch(lefts, rights):
    rows, width = lefts[0].shape
    count = len(lefts)
    return [
        pltpu.VMEM((count, rows, width), jnp.bfloat16),
        pltpu.VMEM((rows, sum(right.shape[1] for right in rights) // 2), jnp.bfloat16),
        pltpu.VMEM((width, 2 * rows), jnp.bfloat16),
        pltpu.SemaphoreType.DMA((2 * count,)),
        pltpu.SemaphoreType.DMA((2 * count,)),
    ]


def pair_grads(lefts, rights, collective_id):
    count, width = len(lefts), lefts[0].shape[1]
    total = sum(right.shape[1] for right in rights) // 2
    block = math.gcd(*[right.shape[1] // 2 for right in rights], 512)

    def kernel(*refs):
        left_refs, right_refs, out_ref = refs[:count], refs[count : 2 * count], refs[2 * count]
        other_lefts, other_right, turned, send, recv, staged, out_sem = refs[2 * count + 1 :]
        barrier = pltpu.get_barrier_semaphore()
        partner = {"dp": 1 - lax.axis_index("dp")}
        pl.semaphore_signal(barrier, inc=1, device_id=partner, device_id_type=pl.DeviceIdType.MESH)
        pl.semaphore_wait(barrier, 1)
        copies = exchange_pairs(left_refs, right_refs, other_lefts, other_right, send, recv)
        written = []

        def store(column, value):
            slot = len(written) % 2
            if len(written) >= 2:
                written[-2].wait()
            staged[slot] = value
            copy = pltpu.make_async_copy(
                staged.at[slot], out_ref.at[:, pl.ds(column, block)], out_sem.at[slot]
            )
            copy.start()
            written.append(copy)

        pair_products(left_refs, right_refs, other_lefts, other_right, turned, store, copies)
        for copy in written[-2:]:
            copy.wait()
        for copy in copies:
            copy.wait_send()

    vmem = pl.BlockSpec(memory_space=pltpu.VMEM)
    return pl.pallas_call(
        kernel,
        in_specs=[vmem] * (2 * count),
        out_specs=pl.BlockSpec(memory_space=pl.ANY),
        out_shape=jax.ShapeDtypeStruct((width, total), jnp.bfloat16),
        scratch_shapes=pair_scratch(lefts, rights)
        + [pltpu.VMEM((2, width, block), jnp.bfloat16), pltpu.SemaphoreType.DMA((2,))],
        compiler_params=pltpu.CompilerParams(
            collective_id=collective_id, has_side_effects=True, vmem_limit_bytes=VMEM_LIMIT
        ),
        cost_estimate=lasting(10),
        name="pair_grads",
    )(*lefts, *rights)


def input_backward(tokens, attn_gain, d_projected, qkv_weight, d_residual):
    rows, width = tokens.shape

    def begin(ins, outs, scratch):
        tokens_ref, gain_ref, d_ref, weight_ref, residual_ref = ins
        grad_ref, part_ref = outs
        weight_here, sem = scratch
        copy = pltpu.make_async_copy(weight_ref, weight_here, sem)
        copy.start()

        def run():
            copy.wait()
            d_in = lax.dot_general(
                d_ref[...], weight_here[...], contract_cols, preferred_element_type=jnp.float32
            )
            x = tokens_ref[...].astype(jnp.float32)
            scale = lax.rsqrt(jnp.mean(x * x, axis=1, keepdims=True) + eps_norm)
            wanted = d_in * gain_ref[...]
            slope = jnp.mean(x * wanted, axis=1, keepdims=True) * scale * scale * scale
            grad_ref[...] = residual_ref[...] + scale * wanted - x * slope
            part_ref[...] = jnp.sum(d_in * x * scale, axis=0, keepdims=True)

        return run

    vmem = pl.BlockSpec(memory_space=pltpu.VMEM)
    arrays = [tokens, attn_gain[None, :], d_projected, qkv_weight, d_residual]
    specs = [vmem, vmem, vmem, pl.BlockSpec(memory_space=pl.ANY), vmem]
    out_shape = [
        jax.ShapeDtypeStruct((rows, width), jnp.float32),
        jax.ShapeDtypeStruct((1, width), jnp.float32),
    ]
    scratch = [pltpu.VMEM(qkv_weight.shape, qkv_weight.dtype), pltpu.SemaphoreType.DMA]
    return arrays, specs, out_shape, scratch, begin


def spread_halves(halves, outs):
    at = 0
    for out in outs:
        half = out.shape[1] // 2
        for c in (0, 1):
            out[:, c * half : (c + 1) * half] = halves[c, :, at : at + half].astype(jnp.float32)
        at += half


def join_halves(sums, collective_id):
    def kernel(sums_ref, both, send, recv):
        core = lax.axis_index("dp")
        partner = {"dp": 1 - core}
        barrier = pltpu.get_barrier_semaphore()
        pl.semaphore_signal(barrier, inc=1, device_id=partner, device_id_type=pl.DeviceIdType.MESH)
        pl.semaphore_wait(barrier, 1)
        copy = pltpu.make_async_remote_copy(
            src_ref=sums_ref,
            dst_ref=both.at[core],
            send_sem=send,
            recv_sem=recv,
            device_id=partner,
            device_id_type=pl.DeviceIdType.MESH,
        )
        copy.start()
        both[core] = sums_ref[...]
        copy.wait()

    vmem = pl.BlockSpec(memory_space=pltpu.VMEM)
    return pl.pallas_call(
        kernel,
        in_specs=[vmem],
        out_specs=vmem,
        out_shape=jax.ShapeDtypeStruct((2, *sums.shape), sums.dtype),
        scratch_shapes=[pltpu.SemaphoreType.DMA, pltpu.SemaphoreType.DMA],
        compiler_params=pltpu.CompilerParams(
            collective_id=collective_id, has_side_effects=True, vmem_limit_bytes=VMEM_LIMIT
        ),
        cost_estimate=lasting(4),
        name="join_halves",
    )(sums)


def write_results(late, late_widths, early, early_widths, small, heads, buckets):
    rows, lines = late.shape[1], late.shape[1] * lax.axis_size("mem") // 128
    count = len(late_widths) + len(early_widths)

    def kernel(late_ref, early_ref, small_ref, *outs):
        spread_halves(late_ref, outs[: len(late_widths)])
        spread_halves(early_ref, outs[len(late_widths) : count])
        attn_ref, ffn_ref, bias_ref, gate_ref = outs[count:]
        attn_ref[...] = small_ref[:lines, :]
        ffn_ref[...] = small_ref[lines : 2 * lines, :]
        for head in range(heads):
            line, lane = divmod(head * buckets, 128)
            here = small_ref[2 * lines + line : 2 * lines + line + 1, :]
            bias_ref[head : head + 1, :] = here[:, lane : lane + buckets]
        line = 2 * lines + heads * buckets // 128
        gate_ref[...] = small_ref[line : line + 1, :heads]

    shapes = [(rows, size) for size in [*late_widths, *early_widths]]
    shapes += [(lines, 128), (lines, 128), (heads, buckets), (1, heads)]
    return pl.pallas_call(
        kernel,
        out_shape=[jax.ShapeDtypeStruct(shape, jnp.float32) for shape in shapes],
        compiler_params=pltpu.CompilerParams(vmem_limit_bytes=VMEM_LIMIT),
        cost_estimate=lasting(3),
        name="write_results",
    )(late, early, small)


def finish_grads(lefts, rights, small, sources, collective_id, beside):
    width, total = lefts[0].shape[1], sum(right.shape[1] for right in rights) // 2
    rows = width // sources
    count = len(lefts)
    arrays, specs, more_out, more_scratch, begin = beside
    mesh_type = pl.DeviceIdType.MESH
    ref_shapes, sem_shapes = reduce_scratch(rows, total, jnp.bfloat16, sources)
    pair_shapes = pair_scratch(lefts, rights)
    sizes = [count, count, len(arrays), 1, 1, 1, len(more_out)]
    sizes += [len(ref_shapes), len(sem_shapes), len(pair_shapes), len(more_scratch), 8]

    def kernel(*refs):
        groups, at = [], 0
        for size in sizes:
            groups.append(refs[at : at + size])
            at += size
        left_refs, right_refs, ins, (small_ref,), (late,), (small_out,), more_refs = groups[:7]
        steps_refs, steps_sems, (other_lefts, other_right, turned, pair_send, pair_recv), scratch, own = groups[7:]
        parts, small_mine, smalls, core_small, small_send, small_recv, core_send, core_recv = own
        meanwhile = begin(ins, more_refs, scratch)
        me, core = lax.axis_index("mem"), lax.axis_index("dp")
        barrier = pltpu.get_barrier_semaphore()
        peers = [lax.rem(me + k, sources) for k in range(1, sources)]
        for peer in peers:
            pl.semaphore_signal(barrier, inc=1, device_id={"mem": peer}, device_id_type=mesh_type)
        pl.semaphore_signal(barrier, inc=1, device_id={"dp": 1 - core}, device_id_type=mesh_type)
        pl.semaphore_wait(barrier, sources)

        def merge(blocks):
            total = blocks[0][...].astype(jnp.float32)
            for block in blocks[1:]:
                total = total + block[...].astype(jnp.float32)
            return total

        def pack(target, total):
            target[...] = total.astype(jnp.bfloat16)

        def across_cores(source, target, i):
            copy = pltpu.make_async_remote_copy(
                src_ref=source,
                dst_ref=target,
                send_sem=core_send.at[i],
                recv_sem=core_recv.at[i],
                device_id={"dp": 1 - core},
                device_id_type=mesh_type,
            )
            copy.start()
            return copy

        pair_copies = exchange_pairs(
            left_refs, right_refs, other_lefts, other_right, pair_send, pair_recv
        )

        def store(column, value):
            parts[:, column : column + value.shape[1]] = value

        pair_products(
            left_refs, right_refs, other_lefts, other_right, turned, store, pair_copies
        )
        small_copies = [
            remote(small_mine, smalls.at[me], small_send.at[i], small_recv.at[me], peer)
            for i, peer in enumerate(peers)
        ]

        def between():
            meanwhile()
            small_mine[...] = small_ref[...]
            for i in range(width // 128):
                small_mine[i : i + 1, :] = more_refs[-1][:, i * 128 : (i + 1) * 128]
            smalls[me] = small_mine[...]
            for copy in small_copies:
                copy.start()

        final, still_open = reduce_steps(parts, sources, steps_refs, steps_sems, merge, pack, between)
        for here, blocks in final:
            late[core, here] = merge(blocks).astype(jnp.bfloat16)
        late_copy = across_cores(late.at[core], late.at[core], 0)
        for peer in peers:
            remote(
                smalls.at[peer], smalls.at[peer], small_send.at[0], small_recv.at[peer], peer
            ).wait_recv()
        group_small = smalls[0]
        for i in range(1, sources):
            group_small = group_small + smalls[i]
        core_small[0] = group_small
        small_copy = across_cores(core_small.at[0], core_small.at[1], 1)
        for copy in (late_copy, small_copy):
            copy.wait()
        small_out[...] = core_small[0] + core_small[1]
        for copy in still_open + small_copies + pair_copies:
            copy.wait_send()

    vmem = pl.BlockSpec(memory_space=pltpu.VMEM)
    return pl.pallas_call(
        kernel,
        in_specs=[vmem] * (2 * count) + specs + [vmem],
        out_specs=[vmem] * (2 + len(more_out)),
        out_shape=[jax.ShapeDtypeStruct((2, rows, total), jnp.bfloat16)]
        + [jax.ShapeDtypeStruct(small.shape, small.dtype)]
        + more_out,
        scratch_shapes=ref_shapes
        + sem_shapes
        + pair_shapes
        + more_scratch
        + [
            pltpu.VMEM((width, total), jnp.bfloat16),
            pltpu.VMEM(small.shape, small.dtype),
            pltpu.VMEM((sources, *small.shape), small.dtype),
            pltpu.VMEM((2, *small.shape), small.dtype),
        ]
        + [pltpu.SemaphoreType.DMA((sources,))] * 2
        + [pltpu.SemaphoreType.DMA((2,))] * 2,
        compiler_params=pltpu.CompilerParams(
            collective_id=collective_id, has_side_effects=True, vmem_limit_bytes=VMEM_LIMIT
        ),
        cost_estimate=lasting(45),
        name="finish_grads",
    )(*lefts, *rights, *arrays, small)


def on_device(
    tokens,
    attn_gain,
    qkv_weight,
    out_weight,
    bias_table,
    gate_logit,
    ffn_gain,
    up_weight,
    down_weight,
    memory_keys,
    memory_values,
    book_lengths,
    slot_shard,
    slot_index,
    slot_live,
    cotangent,
):
    rows, width = tokens.shape
    heads, buckets = bias_table.shape
    head_dim = width // heads
    top_count = slot_index.shape[2]
    hidden = up_weight.shape[1]
    groups = lax.axis_size("mem")
    capacity = -(-3 * rows * heads * top_count // (2 * groups) // 128) * 128
    score_scale = 1.0 / math.sqrt(head_dim)
    repeats = W // rows
    span = W + 2 * rows
    before = W - jnp.arange(span, dtype=jnp.int32)
    after = jnp.arange(span, dtype=jnp.int32)

    def bias_rows(offset):
        reached = (offset >= 0) & (offset < W)
        hot = (bucket_of(offset)[:, None] == jnp.arange(buckets, dtype=jnp.int32)) & reached[:, None]
        rows_of_bias = jnp.einsum(
            "rb,hb->hr", hot.astype(jnp.float32), bias_table, precision=lax.Precision.HIGHEST
        )
        return rows_of_bias + jnp.where(reached, 0.0, masked_score)

    before_bias, after_bias = bias_rows(before), bias_rows(after)
    bucket = bucket_of(jnp.arange(W, dtype=jnp.int32))
    one_hot = (bucket[:, None] == jnp.arange(buckets, dtype=jnp.int32)).astype(jnp.float32)
    tokens_f = tokens.astype(jnp.float32)
    normed_in = normed(tokens_f, attn_gain).astype(jnp.bfloat16)
    projected = jnp.dot(normed_in, qkv_weight, preferred_element_type=jnp.float32).astype(
        jnp.bfloat16
    )
    slots = memory_keys.shape[0]
    requests = place_requests(slot_shard, slot_index, slot_live, groups, capacity, slots)
    incoming = lax.all_to_all(requests, "mem", split_axis=0, concat_axis=0, tiled=True)
    keys_values, _ = lax.optimization_barrier((projected[:, width:], requests))
    halos = [passed_along(keys_values, "mem", distance) for distance in range(repeats, 0, -1)]
    index, row_ids, bounds = read_lists(incoming, heads, rows, slots)
    bounds = bounds.reshape(-1)
    key_rows, value_rows = gather_rows(
        index.reshape(-1), bounds, memory_keys, memory_values, heads, groups, capacity
    )
    all_queries = lax.all_gather(projected[:, :width], "mem", axis=0, tiled=True)
    local = local_forward(before_bias, book_lengths, projected, halos, heads, score_scale)
    partial = memory_forward(
        bounds,
        all_queries,
        key_rows,
        value_rows,
        row_ids,
        heads,
        groups,
        rows,
        score_scale,
    )
    if groups == 16:
        memory_out, mem_log, local_out, local_log = merge_partials(partial, groups, 1, heads, local)
    else:
        local_out, local_log = run_alone("local_forward", local)
        partial = lax.all_to_all(
            partial.reshape(groups, rows, width + 128),
            "mem",
            split_axis=0,
            concat_axis=0,
            tiled=True,
        ).reshape(groups * rows, width + 128)
        memory_out, mem_log = combine_partials(partial, heads, groups, rows)
    gate_share = jax.nn.sigmoid(gate_logit)
    share_wide = jnp.repeat(gate_share, head_dim)[None, :]
    mixed_heads = (share_wide * memory_out + (1.0 - share_wide) * local_out).astype(jnp.bfloat16)
    residual = tokens_f + jnp.dot(mixed_heads, out_weight, preferred_element_type=jnp.float32)
    normed_mid_f, norm_mid_back = jax.vjp(normed, residual, ffn_gain)
    normed_mid = normed_mid_f.astype(jnp.bfloat16)
    activated, d_up, ffn_branch, d_mid = feed_forward(normed_mid, cotangent, up_weight, down_weight)
    block_out = (residual + ffn_branch).astype(jnp.bfloat16)
    early_halves = pair_grads([cotangent], [activated], 5)
    early_sums = scattered(early_halves)
    d_mid, _ = lax.optimization_barrier((d_mid, early_halves))
    d_resid_part, ffn_gain_part = norm_mid_back(d_mid)
    d_residual = cotangent.astype(jnp.float32) + d_resid_part
    d_branch = d_residual.astype(jnp.bfloat16)
    d_mixed = lax.dot_general(
        d_branch, out_weight, contract_cols, preferred_element_type=jnp.float32
    )
    gate_products, sent_grads = sent_gradients(
        d_mixed, memory_out, local_out, mem_log, local_log, gate_share, heads
    )
    gate_part = jnp.sum(gate_products, axis=1) * gate_share * (1.0 - gate_share)
    local = local_queries(
        before_bias,
        book_lengths,
        projected,
        halos,
        d_mixed,
        local_out,
        local_log,
        gate_share,
        heads,
        score_scale,
    )
    if groups == 16:
        all_grads, d_queries, diagonals = gather_group(sent_grads, groups, 2, local)
    else:
        all_grads = lax.all_gather(sent_grads, "mem", axis=0, tiled=True)
        d_queries, diagonals = run_alone("local_queries", local)
    bias_part = jnp.dot(diagonals[:, rows - 1 : rows - 1 + W], one_hot, precision=lax.Precision.HIGHEST)
    d_partial = memory_backward(
        bounds,
        all_queries,
        all_grads,
        key_rows,
        value_rows,
        row_ids,
        heads,
        groups,
        rows,
        score_scale,
    )
    local = local_keys(
        after_bias,
        book_lengths,
        projected,
        all_queries,
        all_grads,
        (1.0 - gate_share) / gate_share,
        repeats + 1,
        heads,
        score_scale,
    )
    if groups == 16:
        d_projected = sum_queries(d_partial, d_queries, groups, 3, score_scale, local)
    else:
        (d_projected,) = run_alone("local_keys", local)
        d_partial, d_projected = lax.optimization_barrier((d_partial, d_projected))
        d_partial = jnp.sum(
            lax.all_to_all(
                d_partial.reshape(groups, rows, width), "mem", split_axis=0, concat_axis=0, tiled=True
            ).astype(jnp.float32),
            axis=0,
        )
        d_queries = (d_queries + d_partial * score_scale).astype(jnp.bfloat16)
        d_projected = jnp.concatenate([d_queries, d_projected[:, width:]], axis=1)
    beside = input_backward(tokens, attn_gain, d_projected, qkv_weight, d_residual)
    small = jnp.concatenate([ffn_gain_part, bias_part.reshape(-1), gate_part], axis=0)
    small = jnp.pad(small, (width, -small.shape[0] % 1024)).reshape(-1, 128)
    lefts, rights = [normed_in, mixed_heads, normed_mid], [d_projected, d_branch, d_up]
    if groups == 16:
        late_both, small, tokens_grad, _ = finish_grads(
            lefts, rights, small, groups, 4, beside
        )
        early_sums, small = lax.optimization_barrier((early_sums, small))
        early_both = join_halves(early_sums, 7)
    else:
        tokens_grad, attn_gain_part = run_alone("input_backward", beside)
        late_halves = pair_grads(lefts, rights, 6)
        late_halves, early_sums = lax.optimization_barrier((late_halves, early_sums))
        late_both = lax.all_gather(scattered(late_halves), "dp", axis=0)
        early_both = lax.all_gather(early_sums, "dp", axis=0)
        small = lax.psum(small.at[: width // 128].set(attn_gain_part.reshape(-1, 128)), ("dp", "mem"))
    qkv_grad, out_grad, up_grad, down_grad, attn_sum, ffn_sum, bias_sum, gate_sum = write_results(
        late_both, [right.shape[1] for right in rights], early_both, [hidden], small, heads, buckets
    )
    return (
        block_out,
        tokens_grad,
        qkv_grad,
        out_grad,
        up_grad,
        down_grad,
        attn_sum.reshape(-1),
        ffn_sum.reshape(-1),
        bias_sum,
        gate_sum.reshape(-1),
    )


def solution(mesh):
    in_specs = (
        P(("dp", "mem"), None),
        P(),
        P(),
        P(),
        P(),
        P(),
        P(),
        P(),
        P(),
        P("mem", None),
        P("mem", None),
        P("dp", None),
        P(("dp", "mem"), None, None, None),
        P(("dp", "mem"), None, None),
        P(("dp", "mem"), None, None),
        P(("dp", "mem"), None),
    )
    out_specs = (
        P(("dp", "mem"), None),
        P(("dp", "mem"), None),
        P("mem", None),
        P("mem", None),
        P("mem", None),
        P("mem", None),
        P(),
        P(),
        P(),
        P(),
    )
    return jax.shard_map(
        on_device, mesh=mesh, in_specs=in_specs, out_specs=out_specs, check_vma=False
    )
```

```python
import math

import jax
import jax.numpy as jnp
from jax import lax
from jax.experimental import pallas as pl
from jax.experimental.pallas import tpu as pltpu
from jax.sharding import PartitionSpec as P

W = 512
VMEM_LIMIT = 56 * 1024 * 1024


eps_norm = 1e-06
bucket_edges = tuple((math.ceil(16 * 8 ** (edge_step / 16)) for edge_step in range(1, 16)))
masked_score = -1e30
dead_score = -10000.0
contract_rows = (((0,), (0,)), ((), ()))
contract_cols = (((1,), (1,)), ((), ()))


def passed_along(value, axis, by):
    size = lax.axis_size(axis)
    pairs = [(i, i + by) for i in range(size) if 0 <= i + by < size]
    return lax.ppermute(value, axis, pairs)


def bucket_of(offset):
    past_edges = sum(((offset >= edge_pos).astype(jnp.int32) for edge_pos in bucket_edges))
    return jnp.where(offset < 16, offset, 16 + past_edges)


def normed(values, gain_vec):
    return (
        values * lax.rsqrt(jnp.mean(values * values, axis=-1, keepdims=True) + eps_norm) * gain_vec
    )


def place_requests(slot_shard, slot_index, slot_live, owners, capacity, slots):
    rows, heads, top_count = slot_index.shape
    entries, empty = rows * heads * top_count, heads * rows * slots
    if (owners + 1) * empty >= 2**31:
        raise ValueError("codes exceed int32")
    row_of = (
        jnp.arange(heads, dtype=jnp.int32)[None, :] * rows
        + jnp.arange(rows, dtype=jnp.int32)[:, None]
    )
    owner = jnp.where(slot_live > 0, slot_shard[..., 0], owners)
    codes = owner * empty + row_of[:, :, None] * slots + slot_index
    codes = lax.sort(codes.reshape(-1), is_stable=False)
    ends = jnp.sum(
        (codes[None, :] < (jnp.arange(owners, dtype=jnp.int32) + 1)[:, None] * empty).astype(jnp.int32),
        axis=1,
    )
    starts = jnp.concatenate([jnp.zeros((1,), jnp.int32), ends[:-1]])
    tall = -(-entries // 128)
    codes = jnp.pad(codes, (0, tall * 128 - entries)).reshape(tall, 128)
    long = capacity // 128

    def kernel(starts_ref, ends_ref, codes_ref, lists_ref, padded):
        padded[:tall, :] = codes_ref[...]
        padded[tall:, :] = jnp.zeros((long + 8, 128), jnp.int32)
        lane = lax.broadcasted_iota(jnp.int32, (long, 128), 1)
        place = lax.broadcasted_iota(jnp.int32, (long, 128), 0) * 128 + lane

        @pl.loop(0, owners)
        def _(i):
            start, end = starts_ref[i], ends_ref[i]
            shift = start % 128
            lines = padded[pl.ds(start // 128, long + 1), :]
            turned = pltpu.roll(lines, (128 - shift) % 128, 1)
            joined = jnp.where(lane < 128 - shift, turned[:long], turned[1:])
            lists_ref[i] = jnp.where(place < end - start, joined - i * empty, empty)

    return pl.pallas_call(
        kernel,
        in_specs=[pl.BlockSpec(memory_space=pltpu.SMEM)] * 2 + [pl.BlockSpec(memory_space=pltpu.VMEM)],
        out_shape=jax.ShapeDtypeStruct((owners, long, 128), jnp.int32),
        scratch_shapes=[pltpu.VMEM((tall + long + 8, 128), jnp.int32)],
        cost_estimate=lasting(3),
        name="make_lists",
    )(starts, ends, codes)


def read_lists(incoming, heads, rows, slots):
    sources, long, _ = incoming.shape

    def kernel(lists_ref, index_ref, ids_ref, bounds_ref):
        lane = lax.broadcasted_iota(jnp.int32, (1, 128), 1)

        def read(source):
            codes = lists_ref[source]
            ids = lax.div(codes, slots)
            index = lax.div(ids, rows) * slots + lax.rem(codes, slots)
            index_ref[source] = jnp.where(ids < heads * rows, index, 0)
            ids_ref[source, :long, :] = ids
            ids_ref[source, long:, :] = jnp.full((1, 128), heads * rows, jnp.int32)
            bounds = jnp.zeros((1, 128), jnp.int32)
            for head in range(1, heads + 1):
                below = jnp.sum(
                    jnp.where(codes < head * rows * slots, 1.0, 0.0), axis=0, keepdims=True
                )
                below = jnp.sum(below, axis=1, keepdims=True).astype(jnp.int32)
                bounds = jnp.where(lane == head, below, bounds)
            bounds_ref[pl.ds(source, 1), :] = bounds

        if sources > 16:
            pl.loop(0, sources)(read)
        else:
            for source in range(sources):
                read(source)

    return pl.pallas_call(
        kernel,
        out_shape=[
            jax.ShapeDtypeStruct((sources, long, 128), jnp.int32),
            jax.ShapeDtypeStruct((sources, long + 1, 128), jnp.int32),
            jax.ShapeDtypeStruct((sources, 128), jnp.int32),
        ],
        cost_estimate=lasting(3),
        name="read_lists",
    )(incoming)


def gather_rows(index, bounds, memory_keys, memory_values, heads, sources, capacity):
    slots, width = memory_keys.shape
    head_dim = width // heads
    step, part = 128, 16

    def kernel(index_ref, bounds_ref, keys, values, out_keys, out_values, key_table, value_table, key_rows, value_rows):
        i = pl.program_id(0)

        @pl.when(i < heads)
        def _():
            place = pl.ds(pl.multiple_of(i * slots, slots), slots)
            key_table[place, :] = keys[...].astype(jnp.float32)
            value_table[place, :] = values[...].astype(jnp.float32)

        @pl.when(i >= heads)
        def _():
            source = i - heads

            used = (bounds_ref[source * 128 + heads] + step - 1) // step

            def store(group):
                for at in range(0, step, part):
                    here = pl.ds(pl.multiple_of(group * step, step) + at, part)
                    out_keys[here, :] = key_rows[at : at + part, :].astype(jnp.bfloat16)
                    out_values[here, :] = value_rows[at : at + part, :].astype(jnp.bfloat16)

            @pl.loop(0, used)
            def _(group):
                store(jnp.maximum(group - 1, 0))
                first = source * capacity + group * step
                for u in range(step):
                    row = index_ref[first + u]
                    key_rows[u : u + 1, :] = key_table[pl.ds(row, 1), :]
                    value_rows[u : u + 1, :] = value_table[pl.ds(row, 1), :]

            pl.when(used > 0)(lambda: store(used - 1))

            @pl.loop(used, capacity // step)
            def _(group):
                here = pl.ds(pl.multiple_of(group * step, step), step)
                out_keys[here, :] = jnp.zeros((step, head_dim), jnp.bfloat16)
                out_values[here, :] = jnp.zeros((step, head_dim), jnp.bfloat16)

    table_spec = pl.BlockSpec((slots, head_dim), lambda i, *_: (0, jnp.minimum(i, heads - 1)))
    out_spec = pl.BlockSpec((capacity, head_dim), lambda i, *_: (jnp.maximum(i - heads, 0), 0))
    out_shape = jax.ShapeDtypeStruct((sources * capacity, head_dim), jnp.bfloat16)
    return pl.pallas_call(
        kernel,
        grid_spec=pltpu.PrefetchScalarGridSpec(
            num_scalar_prefetch=2,
            grid=(heads + sources,),
            in_specs=[table_spec, table_spec],
            out_specs=[out_spec, out_spec],
            scratch_shapes=[
                pltpu.VMEM((heads * slots, head_dim), jnp.float32),
                pltpu.VMEM((heads * slots, head_dim), jnp.float32),
                pltpu.VMEM((step, head_dim), jnp.float32),
                pltpu.VMEM((step, head_dim), jnp.float32),
            ],
        ),
        out_shape=[out_shape, out_shape],
        compiler_params=pltpu.CompilerParams(vmem_limit_bytes=VMEM_LIMIT),
        cost_estimate=lasting(42),
        name="gather_rows",
    )(index, bounds, memory_keys, memory_values)


def lasting(microseconds):
    return pl.CostEstimate(flops=0, bytes_accessed=3_000_000 * microseconds, transcendentals=0)


def triple(stat):
    part = lax.broadcasted_iota(jnp.int32, stat.shape, 1) // 16
    high = stat.astype(jnp.bfloat16).astype(jnp.float32)
    rest = stat - high
    middle = rest.astype(jnp.bfloat16).astype(jnp.float32)
    low = rest - middle
    chosen = jnp.where(part == 0, high, jnp.where(part == 1, middle, jnp.where(part == 2, low, 0.0)))
    return chosen.astype(jnp.bfloat16)


def window_of(bounds, source, head, heads, span, capacity):
    first, last = bounds[source * 128 + head], bounds[source * 128 + head + 1]
    start = jnp.minimum(first // 16 * 16, capacity - span)
    extra = jnp.maximum(last - start - 1, 0) // span
    return start, extra


def columns_of(head, head_dim):
    if isinstance(head, int):
        return slice(head * head_dim, (head + 1) * head_dim)
    return pl.ds(pl.multiple_of(head * head_dim, head_dim), head_dim)


def window_ids(id_ref, start, span):
    lines = id_ref[0, pl.ds(start // 128, span // 128 + 1), :]
    shift = start % 128
    turned = pltpu.roll(lines, (128 - shift) % 128, 1)
    lane = lax.broadcasted_iota(jnp.int32, (span // 128, 128), 1)
    return jnp.where(lane < 128 - shift, turned[:-1], turned[1:])


def owned(lines, first_row, count, start, least):
    row = lax.broadcasted_iota(jnp.int32, (count, 128), 0) + first_row
    masks = []
    for i in range(lines.shape[0]):
        mask = lines[i : i + 1, :] == row
        if least is not None:
            place = lax.broadcasted_iota(jnp.int32, (1, 128), 1) + start + i * 128
            mask = mask & (place >= least)
        masks.append(mask)
    return jnp.concatenate(masks, axis=1)


def memory_forward(bounds, queries, key_rows, value_rows, row_ids, heads, sources, rows, score_scale):
    capacity, head_dim = key_rows.shape[0] // sources, key_rows.shape[1]
    width = heads * head_dim
    span = min(384, capacity)
    chunk = math.gcd(rows, 32)

    def kernel(bounds_ref, q_ref, k_ref, v_ref, id_ref, out_ref, sums, tops, totals, raw, weights):
        source = pl.program_id(0)
        lane = lax.broadcasted_iota(jnp.int32, (chunk, 128), 1) % 16

        def window(heads_here, starts, least):
            here = [pl.ds(pl.multiple_of(start, 16), span) for start in starts]
            columns = [columns_of(head, head_dim) for head in heads_here]
            for slot in range(len(starts)):
                raw[slot] = lax.dot_general(
                    q_ref[:, columns[slot]],
                    k_ref[here[slot], :],
                    contract_cols,
                    preferred_element_type=jnp.float32,
                )
            for slot, (head, start) in enumerate(zip(heads_here, starts)):
                lines = window_ids(id_ref, start, span)
                for at in range(0, rows, chunk):
                    some = slice(at, at + chunk)
                    mine = owned(lines, head * rows + at, chunk, start, least)
                    scores = jnp.where(mine, raw[slot, some, :], masked_score)
                    top = jnp.maximum(jnp.max(scores, axis=1, keepdims=True), 0.1 * masked_score)
                    if least is not None:
                        old_top = jnp.max(
                            jnp.where(lane == head, tops[some, :], masked_score), axis=1, keepdims=True
                        )
                        top = jnp.maximum(top, old_top)
                    exps = jnp.exp((scores - top) * score_scale)
                    weights[slot, some, :] = exps.astype(jnp.bfloat16)
                    total = jnp.sum(exps, axis=1, keepdims=True)
                    if least is not None:
                        faded = jnp.exp((old_top - top) * score_scale)
                        sums[some, columns[slot]] = sums[some, columns[slot]] * faded
                        total = total + totals[some, :] * faded
                    tops[some, :] = jnp.where(lane == head, top, tops[some, :])
                    totals[some, :] = jnp.where(lane == heads + head, total, totals[some, :])
            for slot in range(len(starts)):
                found = jnp.dot(
                    weights[slot], v_ref[here[slot], :], preferred_element_type=jnp.float32
                )
                sums[:, columns[slot]] = found if least is None else sums[:, columns[slot]] + found

        tops[...] = jnp.zeros_like(tops)
        totals[...] = jnp.zeros_like(totals)

        windows = [window_of(bounds_ref, source, head, heads, span, capacity) for head in range(heads)]
        window(list(range(heads)), [start for start, _ in windows], None)

        @pl.when(sum(extra for _, extra in windows) > 0)
        def _():
            @pl.loop(0, heads)
            def _(head):
                start, extra = window_of(bounds_ref, source, head, heads, span, capacity)

                @pl.loop(0, extra)
                def _(turn):
                    least = start + (turn + 1) * span
                    window([head], [jnp.minimum(least, capacity - span)], least)

        out_ref[:, :width] = sums[...].astype(jnp.bfloat16)
        wide = lax.broadcasted_iota(jnp.int32, (rows, 128), 1) % 16
        out_ref[:, width:] = triple(jnp.where(wide < heads, tops[...] * score_scale, totals[...]))

    return pl.pallas_call(
        kernel,
        grid_spec=pltpu.PrefetchScalarGridSpec(
            num_scalar_prefetch=1,
            grid=(sources,),
            in_specs=[
                pl.BlockSpec((rows, width), lambda i, *_: (i, 0)),
                pl.BlockSpec((capacity, head_dim), lambda i, *_: (i, 0)),
                pl.BlockSpec((capacity, head_dim), lambda i, *_: (i, 0)),
                pl.BlockSpec((1, *row_ids.shape[1:]), lambda i, *_: (i, 0, 0)),
            ],
            out_specs=pl.BlockSpec((rows, width + 128), lambda i, *_: (i, 0)),
            scratch_shapes=[
                pltpu.VMEM((rows, width), jnp.float32),
                pltpu.VMEM((rows, 128), jnp.float32),
                pltpu.VMEM((rows, 128), jnp.float32),
                pltpu.VMEM((heads, rows, span), jnp.float32),
                pltpu.VMEM((heads, rows, span), jnp.bfloat16),
            ],
        ),
        out_shape=jax.ShapeDtypeStruct((sources * rows, width + 128), jnp.bfloat16),
        compiler_params=pltpu.CompilerParams(vmem_limit_bytes=VMEM_LIMIT),
        cost_estimate=lasting(25),
        name="memory_forward",
    )(bounds, queries, key_rows, value_rows, row_ids)


def combine_partials(partial, heads, sources, rows):
    width = partial.shape[1] - 128
    head_dim = width // heads

    def kernel(part_ref, out_ref, log_ref, sums, tops, totals):
        i = pl.program_id(0)

        @pl.when(i == 0)
        def _():
            sums[...] = jnp.zeros_like(sums)
            tops[...] = jnp.full_like(tops, masked_score)
            totals[...] = jnp.zeros_like(totals)

        stat = part_ref[:, width:].astype(jnp.float32)
        stat = stat + pltpu.roll(stat, 128 - 16, 1) + pltpu.roll(stat, 128 - 32, 1)
        new_total = pltpu.roll(stat, 128 - heads, 1)
        top = jnp.maximum(tops[...], stat)
        old_fade, new_fade = jnp.exp(tops[...] - top), jnp.exp(stat - top)
        tops[...] = top
        totals[...] = totals[...] * old_fade + new_total * new_fade
        for head in range(heads):
            columns = slice(head * head_dim, (head + 1) * head_dim)
            sums[:, columns] = (
                sums[:, columns] * old_fade[:, head : head + 1]
                + part_ref[:, columns].astype(jnp.float32) * new_fade[:, head : head + 1]
            )

        @pl.when(i == sources - 1)
        def _():
            live = totals[...] > 0
            total = jnp.where(live, totals[...], 1.0)
            log_ref[...] = jnp.where(live, tops[...] + jnp.log(total), 0.0)
            for head in range(heads):
                columns = slice(head * head_dim, (head + 1) * head_dim)
                out_ref[:, columns] = sums[:, columns] / total[:, head : head + 1]

    return pl.pallas_call(
        kernel,
        grid=(sources,),
        in_specs=[pl.BlockSpec((rows, width + 128), lambda i: (i, 0))],
        out_specs=[
            pl.BlockSpec((rows, width), lambda i: (0, 0)),
            pl.BlockSpec((rows, 128), lambda i: (0, 0)),
        ],
        scratch_shapes=[
            pltpu.VMEM((rows, width), jnp.float32),
            pltpu.VMEM((rows, 128), jnp.float32),
            pltpu.VMEM((rows, 128), jnp.float32),
        ],
        out_shape=[
            jax.ShapeDtypeStruct((rows, width), jnp.float32),
            jax.ShapeDtypeStruct((rows, 128), jnp.float32),
        ],
        compiler_params=pltpu.CompilerParams(vmem_limit_bytes=VMEM_LIMIT),
        cost_estimate=lasting(13),
        name="combine_partials",
    )(partial)


def memory_backward(bounds, queries, grads, key_rows, value_rows, row_ids, heads, sources, rows, score_scale):
    capacity, head_dim = key_rows.shape[0] // sources, key_rows.shape[1]
    width = heads * head_dim
    span = min(384, capacity)
    chunk = math.gcd(rows, 32)

    def kernel(bounds_ref, q_ref, g_ref, k_ref, v_ref, id_ref, out_ref, sums, stats, raw, products, slopes):
        source = pl.program_id(0)
        stats[...] = joined_tile(g_ref[:, width : width + 128])

        def window(heads_here, starts, least):
            here = [pl.ds(pl.multiple_of(start, 16), span) for start in starts]
            columns = [columns_of(head, head_dim) for head in heads_here]
            for slot in range(len(starts)):
                raw[slot] = lax.dot_general(
                    q_ref[:, columns[slot]],
                    k_ref[here[slot], :],
                    contract_cols,
                    preferred_element_type=jnp.float32,
                )
                products[slot] = lax.dot_general(
                    g_ref[:, columns[slot]],
                    v_ref[here[slot], :],
                    contract_cols,
                    preferred_element_type=jnp.float32,
                )
            for slot, (head, start) in enumerate(zip(heads_here, starts)):
                lines = window_ids(id_ref, start, span)
                turned = stats[...]
                if least is not None:
                    turned = pltpu.roll(turned, 128 - head, 1)
                elif head:
                    turned = turned[:, head:]
                for at in range(0, rows, chunk):
                    some = slice(at, at + chunk)
                    mine = owned(lines, head * rows + at, chunk, start, least)
                    log, delta = turned[some, :1], turned[some, heads : heads + 1]
                    probs = jnp.exp(jnp.where(mine, raw[slot, some, :] * score_scale - log, dead_score))
                    slopes[slot, some, :] = (probs * (products[slot, some, :] - delta)).astype(
                        jnp.bfloat16
                    )
            for slot in range(len(starts)):
                found = jnp.dot(
                    slopes[slot], k_ref[here[slot], :], preferred_element_type=jnp.float32
                )
                sums[:, columns[slot]] = found if least is None else sums[:, columns[slot]] + found

        windows = [window_of(bounds_ref, source, head, heads, span, capacity) for head in range(heads)]
        window(list(range(heads)), [start for start, _ in windows], None)

        @pl.when(sum(extra for _, extra in windows) > 0)
        def _():
            @pl.loop(0, heads)
            def _(head):
                start, extra = window_of(bounds_ref, source, head, heads, span, capacity)

                @pl.loop(0, extra)
                def _(turn):
                    least = start + (turn + 1) * span
                    window([head], [jnp.minimum(least, capacity - span)], least)

        out_ref[...] = sums[...].astype(jnp.bfloat16)

    return pl.pallas_call(
        kernel,
        grid_spec=pltpu.PrefetchScalarGridSpec(
            num_scalar_prefetch=1,
            grid=(sources,),
            in_specs=[
                pl.BlockSpec((rows, width), lambda i, *_: (i, 0)),
                pl.BlockSpec((rows, width + 128), lambda i, *_: (i, 0)),
                pl.BlockSpec((capacity, head_dim), lambda i, *_: (i, 0)),
                pl.BlockSpec((capacity, head_dim), lambda i, *_: (i, 0)),
                pl.BlockSpec((1, *row_ids.shape[1:]), lambda i, *_: (i, 0, 0)),
            ],
            out_specs=pl.BlockSpec((rows, width), lambda i, *_: (i, 0)),
            scratch_shapes=[
                pltpu.VMEM((rows, width), jnp.float32),
                pltpu.VMEM((rows, 128), jnp.float32),
                pltpu.VMEM((heads, rows, span), jnp.float32),
                pltpu.VMEM((heads, rows, span), jnp.float32),
                pltpu.VMEM((heads, rows, span), jnp.bfloat16),
            ],
        ),
        out_shape=jax.ShapeDtypeStruct((sources * rows, width), jnp.bfloat16),
        compiler_params=pltpu.CompilerParams(vmem_limit_bytes=VMEM_LIMIT),
        cost_estimate=lasting(25),
        name="memory_backward",
    )(bounds, queries, grads, key_rows, value_rows, row_ids)


def remote(source, target, send_sem, recv_sem, device):
    return pltpu.make_async_remote_copy(
        src_ref=source,
        dst_ref=target,
        send_sem=send_sem,
        recv_sem=recv_sem,
        device_id={"mem": device},
        device_id_type=pl.DeviceIdType.MESH,
    )


def grid_place(depth):
    me = lax.axis_index("mem")
    layer, column = me // 4, me % 4
    beside_x = column + 1 - 2 * (column % 2)
    beside_y = column + 2 - 4 * (column // 2)
    across = 3 - column

    def index_of(step, place):
        return (layer + step + depth) % depth * 4 + place

    return me, column, beside_x, beside_y, across, index_of


def greet(devices):
    barrier = pltpu.get_barrier_semaphore()
    for device in devices:
        pl.semaphore_signal(
            barrier, inc=1, device_id={"mem": device}, device_id_type=pl.DeviceIdType.MESH
        )
    pl.semaphore_wait(barrier, len(devices))


def gather_group(block, sources, collective_id, beside):
    rows, width = block.shape
    depth, half = sources // 4, rows // 2
    slots = 2 * depth - 1
    arrays, specs, more_out, more_scratch, begin = beside
    ins, outs = len(arrays), len(more_out)

    def kernel(x_ref, *refs):
        in_refs, (out_ref, *more_refs) = refs[:ins], refs[ins : ins + 1 + outs]
        (own_sem, send, recv), scratch = refs[ins + 1 + outs : ins + 4 + outs], refs[ins + 4 + outs :]
        meanwhile = begin(in_refs, more_refs, scratch)
        me = lax.axis_index("mem")
        layer, column = me // 4, me % 4
        to_x = me + 1 - 2 * (column % 2)
        to_y = me + 2 - 4 * (column // 2)
        across = layer * 4 + 3 - column
        has_above, has_below = layer + 1 < depth, layer > 0
        barrier = pltpu.get_barrier_semaphore()

        def signal(device):
            pl.semaphore_signal(
                barrier, inc=1, device_id={"mem": device}, device_id_type=pl.DeviceIdType.MESH
            )

        signal(to_x)
        signal(to_y)
        pl.when(has_above)(lambda: signal(me + 4))
        pl.when(has_below)(lambda: signal(me - 4))
        pl.semaphore_wait(barrier, 2 + has_above.astype(jnp.int32) + has_below.astype(jnp.int32))

        def part_of(index, part):
            start = pl.multiple_of(index * rows + part * half, half)
            return out_ref.at[pl.ds(start, half), :]

        own = pltpu.make_async_copy(x_ref, out_ref.at[pl.ds(pl.multiple_of(me * rows, rows), rows), :], own_sem)
        own.start()
        sent = []

        def push(condition, source, target, kind, slot, to_slot, part, device):
            copy = remote(source, target, send.at[kind, slot, part], recv.at[kind, to_slot, part], device)
            if condition is None:
                copy.start()
            else:
                pl.when(condition)(copy.start)
            sent.append((condition, copy))

        def arrived(index, kind, slot, part):
            target = part_of(index, part)
            remote(target, target, send.at[kind, slot, part], recv.at[kind, slot, part], to_x).wait_recv()

        def up_slot(distance):
            return distance

        def down_slot(distance):
            return depth - 1 + distance

        for part in (0, 1):
            mine = x_ref.at[pl.ds(part * half, half), :]
            push(has_above, mine, part_of(me, part), 0, 0, down_slot(1), part, me + 4)
            push(has_below, mine, part_of(me, part), 1, 0, up_slot(1), part, me - 4)
            mine_y = x_ref.at[pl.ds((1 - part) * half, half), :]
            push(None, mine, part_of(me, part), 2, 0, 0, part, to_x)
            push(None, mine_y, part_of(me, 1 - part), 3, 0, 0, 1 - part, to_y)

        def pass_on(condition, step, slot):
            def go():
                arrived(to_x + step, 2, slot, 0)
                copy_a.start()
                arrived(to_y + step, 3, slot, 1)
                copy_b.start()

            source_a, source_b = part_of(to_x + step, 0), part_of(to_y + step, 1)
            copy_a = remote(source_a, source_a, send.at[4, slot, 0], recv.at[4, slot, 0], to_y)
            copy_b = remote(source_b, source_b, send.at[5, slot, 1], recv.at[5, slot, 1], to_x)
            sent.append((condition, copy_a))
            sent.append((condition, copy_b))
            if condition is None:
                go()
            else:
                pl.when(condition)(go)

        for distance in range(1, depth):
            from_above, from_below = layer + distance < depth, layer - distance >= 0

            def take(kind, back_kind, step, slot, next_slot, onward, onward_device):
                for part in (0, 1):
                    arrived(me + step, kind, slot, part)
                    here = part_of(me + step, part)
                    if next_slot is not None:
                        pl.when(onward)(
                            remote(
                                here, here, send.at[kind, slot, part], recv.at[kind, next_slot, part], onward_device
                            ).start
                        )
                    remote(here, here, send.at[2, slot, part], recv.at[2, slot, part], to_x).start()
                    remote(here, here, send.at[3, slot, part], recv.at[3, slot, part], to_y).start()

            last = distance == depth - 1
            pl.when(from_above)(
                lambda: take(
                    1, 0, 4 * distance, up_slot(distance), None if last else up_slot(distance + 1), has_below, me - 4
                )
            )
            pl.when(from_below)(
                lambda: take(
                    0, 1, -4 * distance, down_slot(distance), None if last else down_slot(distance + 1), has_above, me + 4
                )
            )
            for condition, step, slot, kind, onward in (
                (from_above, 4 * distance, up_slot(distance), 1, has_below),
                (from_below, -4 * distance, down_slot(distance), 0, has_above),
            ):
                for part in (0, 1):
                    here = part_of(me + step, part)
                    if not last:
                        sent.append((condition & onward, remote(here, here, send.at[kind, slot, part], own_sem, me)))
                    sent.append((condition, remote(here, here, send.at[2, slot, part], own_sem, to_x)))
                    sent.append((condition, remote(here, here, send.at[3, slot, part], own_sem, to_y)))
            meanwhile(distance - 1, depth - 1)
            if distance == 1:
                pass_on(None, 0, 0)
            else:
                pass_on(layer + distance - 1 < depth, 4 * (distance - 1), up_slot(distance - 1))
                pass_on(layer - distance + 1 >= 0, -4 * (distance - 1), down_slot(distance - 1))
        pass_on(layer + depth - 1 < depth, 4 * (depth - 1), up_slot(depth - 1))
        pass_on(layer - depth + 1 >= 0, -4 * (depth - 1), down_slot(depth - 1))

        def close(step, slot):
            arrived(to_x + step, 2, slot, 1)
            arrived(to_y + step, 3, slot, 0)
            arrived(across + step, 4, slot, 0)
            arrived(across + step, 5, slot, 1)

        close(0, 0)
        for distance in range(1, depth):
            pl.when(layer + distance < depth)(lambda: close(4 * distance, up_slot(distance)))
            pl.when(layer - distance >= 0)(lambda: close(-4 * distance, down_slot(distance)))
        for condition, copy in sent:
            if condition is None:
                copy.wait_send()
            else:
                pl.when(condition)(copy.wait_send)
        own.wait()

    return pl.pallas_call(
        kernel,
        in_specs=[pl.BlockSpec(memory_space=pl.ANY), *specs],
        out_specs=[pl.BlockSpec(memory_space=pl.ANY)] + [pl.BlockSpec(memory_space=pltpu.VMEM)] * outs,
        out_shape=[jax.ShapeDtypeStruct((sources * rows, width), block.dtype), *more_out],
        scratch_shapes=[
            pltpu.SemaphoreType.DMA,
            pltpu.SemaphoreType.DMA((6, slots, 2)),
            pltpu.SemaphoreType.DMA((6, slots, 2)),
            *more_scratch,
        ],
        compiler_params=pltpu.CompilerParams(
            collective_id=collective_id, has_side_effects=True, vmem_limit_bytes=VMEM_LIMIT
        ),
        cost_estimate=lasting(50),
        name="gather_group",
    )(block, *arrays)


def reduce_steps(parts_ref, sources, refs, sems, merge, pack, beside=None):
    half_a, half_b, from_x, from_y, from_z, out_x, out_y, out_z = refs
    send, recv_a, recv_b, recv_x, recv_y, recv_z = sems
    rows = parts_ref.shape[0] // sources
    depth, half = sources // 4, rows // 2
    me, column, beside_x, beside_y, across, index_of = grid_place(depth)
    to_x, to_y = index_of(0, beside_x), index_of(0, beside_y)
    order = [*range(1, depth), 0]
    queues = {"x": [], "y": [], "z": []}
    first_limit = 2 if beside is None else depth

    def piece(index, part):
        return parts_ref.at[pl.ds(pl.multiple_of(index * rows + part * half, half), half), :]

    def part_rows(part):
        return pl.ds(part * half, half)

    def push(link, source, target, kind, k, recv_sem, device, limit=2):
        queue = queues[link]
        while link != "z" and len(queue) >= limit:
            queue.pop(0).wait_send()
        copy = remote(source, target, send.at[kind, k], recv_sem, device)
        copy.start()
        queue.append(copy)

    def arrived(target, recv_sem):
        remote(target, target, send.at[0, 0], recv_sem, to_x).wait_recv()

    def plane_rest(k):
        push("x", piece(index_of(k, beside_x), 0), from_x.at[k, part_rows(0)], 2, k, recv_x.at[0, k], to_x)
        push("y", piece(index_of(k, beside_y), 1), from_y.at[k, part_rows(1)], 3, k, recv_y.at[1, k], to_y)

    def plane_merged(k):
        arrived(half_a.at[k], recv_a.at[k])
        pack(out_y.at[k], merge([piece(index_of(k, beside_y), 0), half_a.at[k]]))
        push("y", out_y.at[k], from_y.at[k, part_rows(0)], 4, k, recv_y.at[0, k], to_y)
        arrived(half_b.at[k], recv_b.at[k])
        pack(out_x.at[k], merge([piece(index_of(k, beside_x), 1), half_b.at[k]]))
        push("x", out_x.at[k], from_x.at[k, part_rows(1)], 5, k, recv_x.at[1, k], to_x)

    def column_step(k):
        for part in (0, 1):
            here = part_rows(part)
            arrived(from_x.at[k, here], recv_x.at[part, k])
            arrived(from_y.at[k, here], recv_y.at[part, k])
            if k:
                blocks = [piece(index_of(k, column), part), from_x.at[k, here], from_y.at[k, here]]
                pack(out_z.at[k, here], merge(blocks))
        if k:
            push("z", out_z.at[k], from_z.at[k], 6, k, recv_z.at[k], index_of(k, column))

    for k in order:
        far = index_of(k, across)
        push("x", piece(far, 0), half_a.at[k], 0, k, recv_a.at[k], to_x, first_limit)
        push("y", piece(far, 1), half_b.at[k], 1, k, recv_b.at[k], to_y, first_limit)
    if beside is not None:
        beside()
    for i, k in enumerate(order):
        plane_rest(k)
        plane_merged(k)
        if i:
            column_step(order[i - 1])
    column_step(order[-1])
    for k in range(1, depth):
        arrived(from_z.at[k], recv_z.at[k])
    final = []
    for part in (0, 1):
        here = part_rows(part)
        blocks = [piece(me, part), from_x.at[0, here], from_y.at[0, here]]
        final.append((here, blocks + [from_z.at[k, here] for k in range(1, depth)]))
    return final, [copy for queue in queues.values() for copy in queue]


def reduce_scratch(rows, width, dtype, sources):
    depth, half = sources // 4, rows // 2

    def slots(size):
        return pltpu.VMEM((depth, size, width), dtype)

    refs = [slots(half), slots(half), slots(rows), slots(rows), slots(rows)]
    refs += [slots(half), slots(half), slots(rows)]
    sems = [pltpu.SemaphoreType.DMA((7, depth))]
    sems += [pltpu.SemaphoreType.DMA((depth,))] * 2
    sems += [pltpu.SemaphoreType.DMA((2, depth))] * 2
    sems += [pltpu.SemaphoreType.DMA((depth,))]
    return refs, sems


def run_alone(name, beside):
    arrays, specs, out_shape, scratch, begin = beside
    ins, outs = len(arrays), len(out_shape)

    def kernel(*refs):
        begin(refs[:ins], refs[ins : ins + outs], refs[ins + outs :])()

    return pl.pallas_call(
        kernel,
        in_specs=specs,
        out_specs=[pl.BlockSpec(memory_space=pltpu.VMEM)] * outs,
        out_shape=out_shape,
        scratch_shapes=scratch,
        compiler_params=pltpu.CompilerParams(vmem_limit_bytes=VMEM_LIMIT),
        cost_estimate=lasting(8),
        name=name,
    )(*arrays)


def reduce_group(parts, sources, collective_id, merge, pack, finish, out_shape, beside):
    rows, width = parts.shape[0] // sources, parts.shape[1]
    depth = sources // 4
    arrays, specs, more_out, more_scratch, begin = beside
    ref_shapes, sem_shapes = reduce_scratch(rows, width, parts.dtype, sources)
    sizes = [len(arrays), len(out_shape), len(more_out), len(ref_shapes), len(sem_shapes), len(more_scratch)]

    def kernel(parts_ref, *refs):
        groups, at = [], 0
        for size in sizes:
            groups.append(refs[at : at + size])
            at += size
        ins, out_refs, more_refs, steps_refs, steps_sems, scratch = groups
        meanwhile = begin(ins, more_refs, scratch)
        last = finish
        if finish is None:
            meanwhile, last = meanwhile
        me, column, beside_x, beside_y, across, index_of = grid_place(depth)
        greet(
            [index_of(0, beside_x), index_of(0, beside_y)]
            + [index_of(-k, column) for k in range(1, depth)]
        )
        final, still_open = reduce_steps(
            parts_ref, sources, steps_refs, steps_sems, merge, pack, meanwhile
        )
        for here, blocks in final:
            if finish is None:
                last(here, merge(blocks))
            else:
                last([out.at[here] for out in out_refs], merge(blocks))
        for copy in still_open:
            copy.wait_send()

    vmem = pl.BlockSpec(memory_space=pltpu.VMEM)
    return pl.pallas_call(
        kernel,
        in_specs=[vmem, *specs],
        out_specs=[vmem] * (len(out_shape) + len(more_out)),
        out_shape=[*out_shape, *more_out],
        scratch_shapes=[*ref_shapes, *sem_shapes, *more_scratch],
        compiler_params=pltpu.CompilerParams(
            collective_id=collective_id, has_side_effects=True, vmem_limit_bytes=VMEM_LIMIT
        ),
        cost_estimate=lasting(50),
        name="reduce_group",
    )(parts, *arrays)


def sum_queries(parts, d_queries, sources, collective_id, score_scale, beside):
    rows, width = d_queries.shape
    arrays, specs, (whole,), more_scratch, begin = beside

    def merge(blocks):
        total = blocks[0][...].astype(jnp.float32)
        for block in blocks[1:]:
            total = total + block[...].astype(jnp.float32)
        return total

    def pack(target, total):
        target[...] = total.astype(parts.dtype)

    def begin_both(ins, outs, scratch):
        run = begin(ins[:-1], outs, scratch)

        def finish(here, total):
            outs[0][here, :width] = (ins[-1][here, :] + total * score_scale).astype(whole.dtype)

        return run, finish

    more = [*arrays, d_queries], [*specs, pl.BlockSpec(memory_space=pltpu.VMEM)], [whole], more_scratch, begin_both
    return reduce_group(parts, sources, collective_id, merge, pack, None, [], more)[0]


def merge_partials(parts, sources, collective_id, heads, beside):
    rows, width = parts.shape[0] // sources, parts.shape[1] - 128
    head_dim = width // heads

    def merge(blocks):
        stats = []
        for block in blocks:
            stat = block[:, width:].astype(jnp.float32)
            stats.append(stat + pltpu.roll(stat, 128 - 16, 1) + pltpu.roll(stat, 128 - 32, 1))
        top = stats[0]
        for stat in stats[1:]:
            top = jnp.maximum(top, stat)
        fades = [jnp.exp(stat - top) for stat in stats]
        total = sum(fade * pltpu.roll(stat, 128 - heads, 1) for fade, stat in zip(fades, stats))
        sums = []
        for head in range(heads):
            columns = slice(head * head_dim, (head + 1) * head_dim)
            sums.append(
                sum(
                    block[:, columns].astype(jnp.float32) * fade[:, head : head + 1]
                    for block, fade in zip(blocks, fades)
                )
            )
        return sums, top, total

    def pack(target, merged):
        sums, top, total = merged
        for head in range(heads):
            target[:, head * head_dim : (head + 1) * head_dim] = sums[head].astype(parts.dtype)
        lane = lax.broadcasted_iota(jnp.int32, top.shape, 1)
        stat = jnp.where(lane < heads, top, jnp.where(lane < 16, pltpu.roll(total, heads, 1), 0.0))
        target[:, width:] = triple(stat + pltpu.roll(stat, 16, 1) + pltpu.roll(stat, 32, 1))

    def finish(targets, merged):
        sums, top, total = merged
        live = total > 0
        total = jnp.where(live, total, 1.0)
        targets[1][...] = jnp.where(live, top + jnp.log(total), 0.0)
        for head in range(heads):
            targets[0][:, head * head_dim : (head + 1) * head_dim] = sums[head] / total[:, head : head + 1]

    out_shape = [
        jax.ShapeDtypeStruct((rows, width), jnp.float32),
        jax.ShapeDtypeStruct((rows, 128), jnp.float32),
    ]
    return reduce_group(parts, sources, collective_id, merge, pack, finish, out_shape, beside)


def scattered(halves):
    return lax.psum_scatter(halves, "mem", scatter_dimension=0, tiled=True)


def same_book(lengths_ref, first_row, rows, first_lane, lanes):
    row = lax.broadcasted_iota(jnp.int32, (rows, lanes), 0) + first_row
    lane = lax.broadcasted_iota(jnp.int32, (rows, lanes), 1) + first_lane
    end, same = 0, lane >= 0
    for i in range(lengths_ref.shape[1]):
        end = end + lengths_ref[0, i]
        same = same & ((row >= end) == (lane >= end))
    return same


def lane_tile(columns, rows):
    lane = lax.broadcasted_iota(jnp.int32, (rows, 128), 1)
    tile = jnp.zeros((rows, 128), jnp.float32)
    for i, column in enumerate(columns):
        tile = jnp.where(lane == i, column, tile)
    return tile


def split_tile(tile):
    lane = lax.broadcasted_iota(jnp.int32, tile.shape, 1)
    kept = jnp.where(lane < 32, tile, 0.0)
    kept = kept + pltpu.roll(kept, 32, 1) + pltpu.roll(kept, 64, 1)
    high = kept.astype(jnp.bfloat16).astype(jnp.float32)
    middle = (kept - high).astype(jnp.bfloat16).astype(jnp.float32)
    low = kept - high - middle
    part = lane // 32
    return jnp.where(part == 0, high, jnp.where(part == 1, middle, low)).astype(jnp.bfloat16)


def joined_tile(tile):
    tile = tile.astype(jnp.float32)
    return tile + pltpu.roll(tile, 128 - 32, 1) + pltpu.roll(tile, 128 - 64, 1)


def slanted(base, rows):
    return pltpu.roll(jnp.broadcast_to(base, (rows, base.shape[1])), 0, 1, stride=1, stride_axis=0)


def local_forward(base, lengths, own, halos, heads, score_scale):
    rows, width = own.shape[0], own.shape[1] // 3
    head_dim = width // heads
    count = len(halos) + 1

    def begin(ins, outs, scratch):
        base_ref, lengths_ref, own_ref, *halo_refs = ins
        out_ref, log_ref = outs

        def run():
            first = lax.axis_index("mem") * rows
            same = same_book(lengths_ref, first, rows, first - (count - 1) * rows, count * rows)
            logs = []
            for head in range(heads):
                columns = slice(head * head_dim, (head + 1) * head_dim)
                above = slice(width + head * head_dim, width + (head + 1) * head_dim)
                twice = slice(2 * width + head * head_dim, 2 * width + (head + 1) * head_dim)
                keys = [ref[:, columns] for ref in halo_refs] + [own_ref[:, above]]
                values = [ref[:, above] for ref in halo_refs] + [own_ref[:, twice]]
                q = own_ref[:, columns]
                raw = [
                    lax.dot_general(q, k, contract_cols, preferred_element_type=jnp.float32) for k in keys
                ]
                bias = slanted(base_ref[head : head + 1, :], rows)[:, : count * rows]
                scores = jnp.concatenate(raw, axis=1) * score_scale + bias
                scores = jnp.where(same, scores, masked_score)
                top = jnp.max(scores, axis=1, keepdims=True)
                weights = jnp.exp(scores - top)
                total = jnp.sum(weights, axis=1, keepdims=True)
                weights = (weights / total).astype(jnp.bfloat16)
                out_ref[:, columns] = sum(
                    jnp.dot(
                        weights[:, i * rows : (i + 1) * rows], v, preferred_element_type=jnp.float32
                    )
                    for i, v in enumerate(values)
                )
                logs.append(top + jnp.log(total))
            log_ref[...] = lane_tile(logs, rows)

        return run

    arrays = [base, lengths, own, *halos]
    vmem = pl.BlockSpec(memory_space=pltpu.VMEM)
    specs = [vmem, pl.BlockSpec(memory_space=pltpu.SMEM)] + [vmem] * (1 + len(halos))
    out_shape = [
        jax.ShapeDtypeStruct((rows, width), jnp.float32),
        jax.ShapeDtypeStruct((rows, 128), jnp.float32),
    ]
    return arrays, specs, out_shape, [], begin


def local_queries(
    base, lengths, own, halos, d_mixed, local_out, local_log, share, heads, score_scale
):
    rows, width = d_mixed.shape
    head_dim = width // heads
    count = len(halos) + 1
    span = base.shape[1]

    def begin(ins, outs, scratch):
        base_ref, lengths_ref, own_ref, mix_ref, loc_ref, log_ref, share_ref, *halo_refs = ins
        dq_ref, diagonal_ref = outs

        def some_heads(some):
            first = lax.axis_index("mem") * rows
            same = same_book(lengths_ref, first, rows, first - (count - 1) * rows, count * rows)
            turned = (
                lax.broadcasted_iota(jnp.int32, (rows, rows), 0)
                + lax.broadcasted_iota(jnp.int32, (rows, rows), 1)
                == rows - 1
            ).astype(jnp.bfloat16)
            for head in some:
                columns = slice(head * head_dim, (head + 1) * head_dim)
                above = slice(width + head * head_dim, width + (head + 1) * head_dim)
                twice = slice(2 * width + head * head_dim, 2 * width + (head + 1) * head_dim)
                keys = [ref[:, columns] for ref in halo_refs] + [own_ref[:, above]]
                values = [ref[:, above] for ref in halo_refs] + [own_ref[:, twice]]
                q = own_ref[:, columns]
                d_out = ((1.0 - share_ref[head]) * mix_ref[:, columns]).astype(jnp.bfloat16)
                delta = jnp.sum(
                    d_out.astype(jnp.float32) * loc_ref[:, columns], axis=1, keepdims=True
                )
                raw = [
                    lax.dot_general(q, k, contract_cols, preferred_element_type=jnp.float32)
                    for k in keys
                ]
                bias = slanted(base_ref[head : head + 1, :], rows)[:, : count * rows]
                scores = jnp.concatenate(raw, axis=1) * score_scale + bias
                probs = jnp.exp(jnp.where(same, scores - log_ref[:, head : head + 1], masked_score))
                products = [
                    lax.dot_general(d_out, v, contract_cols, preferred_element_type=jnp.float32)
                    for v in values
                ]
                slopes = (probs * (jnp.concatenate(products, axis=1) - delta)).astype(jnp.bfloat16)
                slope_blocks = [slopes[:, i * rows : (i + 1) * rows] for i in range(count)]
                dq_ref[:, columns] = score_scale * sum(
                    jnp.dot(s, k, preferred_element_type=jnp.float32)
                    for s, k in zip(slope_blocks, keys)
                )
                mirrored = [
                    jnp.dot(s, turned, preferred_element_type=jnp.float32) for s in slope_blocks[::-1]
                ]
                mirrored.append(jnp.zeros((rows, span - count * rows), jnp.float32))
                leaned = pltpu.roll(jnp.concatenate(mirrored, axis=1), 0, 1, stride=1, stride_axis=0)
                diagonal_ref[head : head + 1, :] = jnp.sum(leaned, axis=0, keepdims=True)

        def run(part=0, parts=1):
            some_heads(range(part * heads // parts, (part + 1) * heads // parts))

        return run

    vmem = pl.BlockSpec(memory_space=pltpu.VMEM)
    smem = pl.BlockSpec(memory_space=pltpu.SMEM)
    arrays = [base, lengths, own, d_mixed, local_out, local_log, share, *halos]
    specs = [vmem, smem] + [vmem] * 4 + [smem] + [vmem] * len(halos)
    out_shape = [
        jax.ShapeDtypeStruct((rows, width), jnp.float32),
        jax.ShapeDtypeStruct((heads, span), jnp.float32),
    ]
    return arrays, specs, out_shape, [], begin


def local_keys(base, lengths, own, queries, sent, ratio, count, heads, score_scale):
    rows, width = own.shape[0], own.shape[1] // 3
    head_dim = width // heads
    groups = queries.shape[0] // rows

    def begin(ins, outs, scratch):
        base_ref, lengths_ref, own_ref, ratio_ref, queries_ref, sent_ref = ins
        (out_ref,) = outs
        queries_here, sent_here, sems = scratch
        copies = []
        for i in range(count):
            index = jnp.minimum(lax.axis_index("mem") + i, groups - 1)
            there = pl.ds(pl.multiple_of(index * rows, rows), rows)
            copies.append(
                pltpu.make_async_copy(queries_ref.at[there, :], queries_here.at[i], sems.at[0, i])
            )
            copies.append(pltpu.make_async_copy(sent_ref.at[there, :], sent_here.at[i], sems.at[1, i]))
        for copy in copies:
            copy.start()

        def run():
            for copy in copies:
                copy.wait()
            first = lax.axis_index("mem") * rows
            same = same_book(lengths_ref, first, rows, first, count * rows)
            stats = jnp.concatenate([joined_tile(sent_here[i, :, width:]).T for i in range(count)], axis=1)
            for head in range(heads):
                columns = slice(head * head_dim, (head + 1) * head_dim)
                above = slice(width + head * head_dim, width + (head + 1) * head_dim)
                twice = slice(2 * width + head * head_dim, 2 * width + (head + 1) * head_dim)
                k, v = own_ref[:, above], own_ref[:, twice]
                qs = [queries_here[i, :, columns] for i in range(count)]
                gs = [
                    (sent_here[i, :, columns].astype(jnp.float32) * ratio_ref[head]).astype(jnp.bfloat16)
                    for i in range(count)
                ]
                raw = [
                    lax.dot_general(k, q, contract_cols, preferred_element_type=jnp.float32) for q in qs
                ]
                bias = slanted(base_ref[head : head + 1, :], rows)[:, : count * rows]
                scores = jnp.concatenate(raw, axis=1) * score_scale + bias
                log = stats[2 * heads + head : 2 * heads + head + 1, :]
                delta = stats[3 * heads + head : 3 * heads + head + 1, :]
                probs = jnp.exp(jnp.where(same, scores - log, masked_score))
                products = [
                    lax.dot_general(v, g, contract_cols, preferred_element_type=jnp.float32) for g in gs
                ]
                slopes = (probs * (jnp.concatenate(products, axis=1) - delta)).astype(jnp.bfloat16)
                weights = probs.astype(jnp.bfloat16)
                blocks = [slice(i * rows, (i + 1) * rows) for i in range(count)]
                d_key = sum(
                    jnp.dot(slopes[:, b], q, preferred_element_type=jnp.float32) for b, q in zip(blocks, qs)
                )
                d_value = sum(
                    jnp.dot(weights[:, b], g, preferred_element_type=jnp.float32)
                    for b, g in zip(blocks, gs)
                )
                out_ref[:, above] = (d_key * score_scale).astype(jnp.bfloat16)
                out_ref[:, twice] = d_value.astype(jnp.bfloat16)

        return run

    vmem, anywhere = pl.BlockSpec(memory_space=pltpu.VMEM), pl.BlockSpec(memory_space=pl.ANY)
    smem = pl.BlockSpec(memory_space=pltpu.SMEM)
    arrays = [base, lengths, own, ratio, queries, sent]
    specs = [vmem, smem, vmem, smem, anywhere, anywhere]
    scratch = [
        pltpu.VMEM((count, rows, width), jnp.bfloat16),
        pltpu.VMEM((count, rows, width + 128), jnp.bfloat16),
        pltpu.SemaphoreType.DMA((2, count)),
    ]
    return arrays, specs, [jax.ShapeDtypeStruct((rows, 3 * width), jnp.bfloat16)], scratch, begin


def middle(
    tokens,
    memory_out,
    local_out,
    mem_log,
    local_log,
    share,
    out_weight,
    ffn_gain,
    up_weight,
    down_weight,
    cotangent,
    heads,
):
    rows, width = tokens.shape
    head_dim = width // heads
    hidden = up_weight.shape[1]
    block = math.gcd(hidden, 1024)
    steps = hidden // block

    def kernel(
        tokens_ref, mem_ref, loc_ref, mem_log_ref, log_ref, share_ref, out_w_ref, gain_ref, up_ref, down_ref, cot_ref, *refs
    ):
        mixed_ref, mid_ref, act_ref, d_up_ref, block_ref, d_res_ref, gain_part_ref, d_branch_ref, d_mix_ref = refs[:9]
        gate_ref, sent_ref, residual, branch_sum, d_mid_sum = refs[9:]
        i = pl.program_id(0)

        def scale_of(values):
            return lax.rsqrt(jnp.mean(values * values, axis=1, keepdims=True) + eps_norm)

        @pl.when(i == 0)
        def _():
            for head in range(heads):
                columns = slice(head * head_dim, (head + 1) * head_dim)
                part = share_ref[head]
                mixed_ref[:, columns] = (
                    part * mem_ref[:, columns] + (1.0 - part) * loc_ref[:, columns]
                ).astype(jnp.bfloat16)
            values = tokens_ref[...].astype(jnp.float32) + jnp.dot(
                mixed_ref[...], out_w_ref[...], preferred_element_type=jnp.float32
            )
            residual[...] = values
            mid_ref[...] = (values * scale_of(values) * gain_ref[...]).astype(jnp.bfloat16)
            branch_sum[...] = jnp.zeros_like(branch_sum)
            d_mid_sum[...] = jnp.zeros_like(d_mid_sum)

        up = jnp.dot(mid_ref[...], up_ref[...], preferred_element_type=jnp.float32)
        d_act = jnp.dot(cot_ref[...], down_ref[...], preferred_element_type=jnp.float32)
        below = 0.5 * (1.0 + lax.erf(up * math.sqrt(0.5)))
        density = jnp.exp(-0.5 * up * up) * (1.0 / math.sqrt(2.0 * math.pi))
        act = (up * below).astype(jnp.bfloat16)
        d_up = (d_act * (below + up * density)).astype(jnp.bfloat16)
        act_ref[...] = act
        d_up_ref[...] = d_up
        branch_sum[...] += lax.dot_general(
            act, down_ref[...], contract_cols, preferred_element_type=jnp.float32
        )
        d_mid_sum[...] += lax.dot_general(
            d_up, up_ref[...], contract_cols, preferred_element_type=jnp.float32
        )

        @pl.when(i == steps - 1)
        def _():
            values, d_mid = residual[...], d_mid_sum[...]
            block_ref[...] = (values + branch_sum[...]).astype(jnp.bfloat16)
            scale = scale_of(values)
            wanted = d_mid * gain_ref[...]
            slope = jnp.mean(values * wanted, axis=1, keepdims=True) * scale * scale * scale
            d_res = cot_ref[...].astype(jnp.float32) + scale * wanted - values * slope
            d_res_ref[...] = d_res
            gain_part_ref[...] = jnp.sum(d_mid * values * scale, axis=0, keepdims=True)
            d_branch_ref[...] = d_res.astype(jnp.bfloat16)
            d_mix_ref[...] = lax.dot_general(
                d_branch_ref[...], out_w_ref[...], contract_cols, preferred_element_type=jnp.float32
            )
            mem_deltas, deltas = [], []
            for head in range(heads):
                columns = slice(head * head_dim, (head + 1) * head_dim)
                part = share_ref[head]
                d_mix, mem_here, loc_here = d_mix_ref[:, columns], mem_ref[:, columns], loc_ref[:, columns]
                d_mem = (part * d_mix).astype(jnp.bfloat16)
                d_out = ((1.0 - part) * d_mix).astype(jnp.bfloat16)
                sent_ref[:, columns] = d_mem
                mem_deltas.append(
                    jnp.sum(d_mem.astype(jnp.float32) * mem_here, axis=1, keepdims=True)
                )
                deltas.append(jnp.sum(d_out.astype(jnp.float32) * loc_here, axis=1, keepdims=True))
                gate_ref[head : head + 1, :] = jnp.sum(
                    d_mix * (mem_here - loc_here), axis=0, keepdims=True
                )
            mem_logs = [mem_log_ref[:, head : head + 1] for head in range(heads)]
            logs = [log_ref[:, head : head + 1] for head in range(heads)]
            sent_ref[:, width:] = split_tile(lane_tile(mem_logs + mem_deltas + logs + deltas, rows))

    def whole(*shape):
        return pl.BlockSpec(shape, lambda i: (0, 0))

    weight = pl.BlockSpec((width, block), lambda i: (0, i))
    column = pl.BlockSpec((rows, block), lambda i: (0, i))
    full = whole(rows, width)
    low, high = jnp.bfloat16, jnp.float32
    outs = [
        (full, (rows, width), low),
        (full, (rows, width), low),
        (column, (rows, hidden), low),
        (column, (rows, hidden), low),
        (full, (rows, width), low),
        (full, (rows, width), high),
        (whole(1, width), (1, width), high),
        (full, (rows, width), low),
        (full, (rows, width), high),
        (whole(heads, head_dim), (heads, head_dim), high),
        (whole(rows, width + 128), (rows, width + 128), low),
    ]
    return pl.pallas_call(
        kernel,
        grid=(steps,),
        in_specs=[full, full, full, whole(rows, 128), whole(rows, 128)]
        + [pl.BlockSpec(memory_space=pltpu.SMEM)]
        + [whole(width, width), whole(1, width), weight, weight, full],
        out_specs=[spec for spec, _, _ in outs],
        out_shape=[jax.ShapeDtypeStruct(shape, dtype) for _, shape, dtype in outs],
        scratch_shapes=[pltpu.VMEM((rows, width), jnp.float32)] * 3,
        compiler_params=pltpu.CompilerParams(vmem_limit_bytes=VMEM_LIMIT),
        cost_estimate=lasting(18),
        name="middle",
    )(
        tokens,
        memory_out,
        local_out,
        mem_log,
        local_log,
        share,
        out_weight,
        ffn_gain[None, :],
        up_weight,
        down_weight,
        cotangent,
    )


def exchange_pairs(lefts, rights, other_lefts, other_right, send, recv):
    core = lax.axis_index("dp")
    copies, at = [], 0

    def push(source, target):
        i = len(copies)
        copy = pltpu.make_async_remote_copy(
            src_ref=source,
            dst_ref=target,
            send_sem=send.at[i],
            recv_sem=recv.at[i],
            device_id={"dp": 1 - core},
            device_id_type=pl.DeviceIdType.MESH,
        )
        copy.start()
        copies.append(copy)

    for i, (left, right) in enumerate(zip(lefts, rights)):
        half = right.shape[1] // 2
        push(left, other_lefts.at[i])
        there = pl.ds(pl.multiple_of((1 - core) * half, 128), half)
        push(right.at[:, there], other_right.at[:, pl.ds(at, half)])
        at += half
    return copies


def pair_products(lefts, rights, other_lefts, other_right, turned, store, copies):
    core = lax.axis_index("dp")
    rows = lefts[0].shape[0]
    at = 0
    for i, (left, right) in enumerate(zip(lefts, rights)):
        half = right.shape[1] // 2
        for copy in copies[2 * i : 2 * i + 2]:
            copy.wait_recv()
        turned[:, :rows] = left[...].T
        turned[:, rows:] = other_lefts[i].T
        block = math.gcd(half, 512)
        for column in range(0, half, block):
            kept = right[:, pl.ds(pl.multiple_of(core * half + column, 128), block)]
            both = jnp.concatenate([kept, other_right[:, at + column : at + column + block]], axis=0)
            store(
                at + column,
                jnp.dot(turned[...], both, preferred_element_type=jnp.float32).astype(jnp.bfloat16),
            )
        at += half


def pair_scratch(lefts, rights):
    rows, width = lefts[0].shape
    count = len(lefts)
    return [
        pltpu.VMEM((count, rows, width), jnp.bfloat16),
        pltpu.VMEM((rows, sum(right.shape[1] for right in rights) // 2), jnp.bfloat16),
        pltpu.VMEM((width, 2 * rows), jnp.bfloat16),
        pltpu.SemaphoreType.DMA((2 * count,)),
        pltpu.SemaphoreType.DMA((2 * count,)),
    ]


def pair_grads(lefts, rights, collective_id):
    count, width = len(lefts), lefts[0].shape[1]
    total = sum(right.shape[1] for right in rights) // 2
    block = math.gcd(*[right.shape[1] // 2 for right in rights], 512)

    def kernel(*refs):
        left_refs, right_refs, out_ref = refs[:count], refs[count : 2 * count], refs[2 * count]
        other_lefts, other_right, turned, send, recv, staged, out_sem = refs[2 * count + 1 :]
        barrier = pltpu.get_barrier_semaphore()
        partner = {"dp": 1 - lax.axis_index("dp")}
        pl.semaphore_signal(barrier, inc=1, device_id=partner, device_id_type=pl.DeviceIdType.MESH)
        pl.semaphore_wait(barrier, 1)
        copies = exchange_pairs(left_refs, right_refs, other_lefts, other_right, send, recv)
        written = []

        def store(column, value):
            slot = len(written) % 2
            if len(written) >= 2:
                written[-2].wait()
            staged[slot] = value
            copy = pltpu.make_async_copy(
                staged.at[slot], out_ref.at[:, pl.ds(column, block)], out_sem.at[slot]
            )
            copy.start()
            written.append(copy)

        pair_products(left_refs, right_refs, other_lefts, other_right, turned, store, copies)
        for copy in written[-2:]:
            copy.wait()
        for copy in copies:
            copy.wait_send()

    vmem = pl.BlockSpec(memory_space=pltpu.VMEM)
    return pl.pallas_call(
        kernel,
        in_specs=[vmem] * (2 * count),
        out_specs=pl.BlockSpec(memory_space=pl.ANY),
        out_shape=jax.ShapeDtypeStruct((width, total), jnp.bfloat16),
        scratch_shapes=pair_scratch(lefts, rights)
        + [pltpu.VMEM((2, width, block), jnp.bfloat16), pltpu.SemaphoreType.DMA((2,))],
        compiler_params=pltpu.CompilerParams(
            collective_id=collective_id, has_side_effects=True, vmem_limit_bytes=VMEM_LIMIT
        ),
        cost_estimate=lasting(10),
        name="pair_grads",
    )(*lefts, *rights)


def input_backward(tokens, attn_gain, d_projected, qkv_weight, d_residual):
    rows, width = tokens.shape

    def begin(ins, outs, scratch):
        tokens_ref, gain_ref, d_ref, weight_ref, residual_ref = ins
        grad_ref, part_ref = outs
        weight_here, sem = scratch
        copy = pltpu.make_async_copy(weight_ref, weight_here, sem)
        copy.start()

        def run():
            copy.wait()
            d_in = lax.dot_general(
                d_ref[...], weight_here[...], contract_cols, preferred_element_type=jnp.float32
            )
            x = tokens_ref[...].astype(jnp.float32)
            scale = lax.rsqrt(jnp.mean(x * x, axis=1, keepdims=True) + eps_norm)
            wanted = d_in * gain_ref[...]
            slope = jnp.mean(x * wanted, axis=1, keepdims=True) * scale * scale * scale
            grad_ref[...] = residual_ref[...] + scale * wanted - x * slope
            part_ref[...] = jnp.sum(d_in * x * scale, axis=0, keepdims=True)

        return run

    vmem = pl.BlockSpec(memory_space=pltpu.VMEM)
    arrays = [tokens, attn_gain[None, :], d_projected, qkv_weight, d_residual]
    specs = [vmem, vmem, vmem, pl.BlockSpec(memory_space=pl.ANY), vmem]
    out_shape = [
        jax.ShapeDtypeStruct((rows, width), jnp.float32),
        jax.ShapeDtypeStruct((1, width), jnp.float32),
    ]
    scratch = [pltpu.VMEM(qkv_weight.shape, qkv_weight.dtype), pltpu.SemaphoreType.DMA]
    return arrays, specs, out_shape, scratch, begin


def spread_halves(halves, outs):
    at = 0
    for out in outs:
        half = out.shape[1] // 2
        for c in (0, 1):
            out[:, c * half : (c + 1) * half] = halves[c, :, at : at + half].astype(jnp.float32)
        at += half


def join_halves(sums, collective_id):
    def kernel(sums_ref, both, send, recv):
        core = lax.axis_index("dp")
        partner = {"dp": 1 - core}
        barrier = pltpu.get_barrier_semaphore()
        pl.semaphore_signal(barrier, inc=1, device_id=partner, device_id_type=pl.DeviceIdType.MESH)
        pl.semaphore_wait(barrier, 1)
        copy = pltpu.make_async_remote_copy(
            src_ref=sums_ref,
            dst_ref=both.at[core],
            send_sem=send,
            recv_sem=recv,
            device_id=partner,
            device_id_type=pl.DeviceIdType.MESH,
        )
        copy.start()
        both[core] = sums_ref[...]
        copy.wait()

    vmem = pl.BlockSpec(memory_space=pltpu.VMEM)
    return pl.pallas_call(
        kernel,
        in_specs=[vmem],
        out_specs=vmem,
        out_shape=jax.ShapeDtypeStruct((2, *sums.shape), sums.dtype),
        scratch_shapes=[pltpu.SemaphoreType.DMA, pltpu.SemaphoreType.DMA],
        compiler_params=pltpu.CompilerParams(
            collective_id=collective_id, has_side_effects=True, vmem_limit_bytes=VMEM_LIMIT
        ),
        cost_estimate=lasting(4),
        name="join_halves",
    )(sums)


def write_results(late, late_widths, early, early_widths, small, heads, buckets):
    rows, width = late.shape[1], late.shape[2] * 2 // 3
    lines = width // 128
    count = len(late_widths) + len(early_widths)

    def kernel(late_ref, early_ref, small_ref, *outs):
        spread_halves(late_ref, outs[: len(late_widths)])
        spread_halves(early_ref, outs[len(late_widths) : count])
        attn_ref, ffn_ref, bias_ref, gate_ref = outs[count:]
        attn_ref[...] = small_ref[:lines, :]
        ffn_ref[...] = small_ref[lines : 2 * lines, :]
        for head in range(heads):
            line, lane = divmod(head * buckets, 128)
            here = small_ref[2 * lines + line : 2 * lines + line + 1, :]
            bias_ref[head : head + 1, :] = here[:, lane : lane + buckets]
        line = 2 * lines + heads * buckets // 128
        gate_ref[...] = small_ref[line : line + 1, :heads]

    shapes = [(rows, size) for size in [*late_widths, *early_widths]]
    shapes += [(lines, 128), (lines, 128), (heads, buckets), (1, heads)]
    return pl.pallas_call(
        kernel,
        out_shape=[jax.ShapeDtypeStruct(shape, jnp.float32) for shape in shapes],
        compiler_params=pltpu.CompilerParams(vmem_limit_bytes=VMEM_LIMIT),
        cost_estimate=lasting(3),
        name="write_results",
    )(late, early, small)


def finish_grads(lefts, rights, small, sources, collective_id, beside):
    width, total = lefts[0].shape[1], sum(right.shape[1] for right in rights) // 2
    rows = width // sources
    count = len(lefts)
    arrays, specs, more_out, more_scratch, begin = beside
    mesh_type = pl.DeviceIdType.MESH
    ref_shapes, sem_shapes = reduce_scratch(rows, total, jnp.bfloat16, sources)
    pair_shapes = pair_scratch(lefts, rights)
    sizes = [count, count, len(arrays), 1, 1, 1, len(more_out)]
    sizes += [len(ref_shapes), len(sem_shapes), len(pair_shapes), len(more_scratch), 8]

    def kernel(*refs):
        groups, at = [], 0
        for size in sizes:
            groups.append(refs[at : at + size])
            at += size
        left_refs, right_refs, ins, (small_ref,), (late,), (small_out,), more_refs = groups[:7]
        steps_refs, steps_sems, (other_lefts, other_right, turned, pair_send, pair_recv), scratch, own = groups[7:]
        parts, small_mine, smalls, core_small, small_send, small_recv, core_send, core_recv = own
        meanwhile = begin(ins, more_refs, scratch)
        me, core = lax.axis_index("mem"), lax.axis_index("dp")
        barrier = pltpu.get_barrier_semaphore()
        peers = [lax.rem(me + k, sources) for k in range(1, sources)]
        for peer in peers:
            pl.semaphore_signal(barrier, inc=1, device_id={"mem": peer}, device_id_type=mesh_type)
        pl.semaphore_signal(barrier, inc=1, device_id={"dp": 1 - core}, device_id_type=mesh_type)
        pl.semaphore_wait(barrier, sources)

        def merge(blocks):
            total = blocks[0][...].astype(jnp.float32)
            for block in blocks[1:]:
                total = total + block[...].astype(jnp.float32)
            return total

        def pack(target, total):
            target[...] = total.astype(jnp.bfloat16)

        def across_cores(source, target, i):
            copy = pltpu.make_async_remote_copy(
                src_ref=source,
                dst_ref=target,
                send_sem=core_send.at[i],
                recv_sem=core_recv.at[i],
                device_id={"dp": 1 - core},
                device_id_type=mesh_type,
            )
            copy.start()
            return copy

        pair_copies = exchange_pairs(
            left_refs, right_refs, other_lefts, other_right, pair_send, pair_recv
        )

        def store(column, value):
            parts[:, column : column + value.shape[1]] = value

        pair_products(
            left_refs, right_refs, other_lefts, other_right, turned, store, pair_copies
        )
        small_copies = [
            remote(small_mine, smalls.at[me], small_send.at[i], small_recv.at[me], peer)
            for i, peer in enumerate(peers)
        ]

        def between():
            meanwhile()
            small_mine[...] = small_ref[...]
            for i in range(width // 128):
                small_mine[i : i + 1, :] = more_refs[-1][:, i * 128 : (i + 1) * 128]
            smalls[me] = small_mine[...]
            for copy in small_copies:
                copy.start()

        final, still_open = reduce_steps(parts, sources, steps_refs, steps_sems, merge, pack, between)
        for here, blocks in final:
            late[core, here] = merge(blocks).astype(jnp.bfloat16)
        late_copy = across_cores(late.at[core], late.at[core], 0)
        for peer in peers:
            remote(
                smalls.at[peer], smalls.at[peer], small_send.at[0], small_recv.at[peer], peer
            ).wait_recv()
        group_small = smalls[0]
        for i in range(1, sources):
            group_small = group_small + smalls[i]
        core_small[0] = group_small
        small_copy = across_cores(core_small.at[0], core_small.at[1], 1)
        for copy in (late_copy, small_copy):
            copy.wait()
        small_out[...] = core_small[0] + core_small[1]
        for copy in still_open + small_copies + pair_copies:
            copy.wait_send()

    vmem = pl.BlockSpec(memory_space=pltpu.VMEM)
    return pl.pallas_call(
        kernel,
        in_specs=[vmem] * (2 * count) + specs + [vmem],
        out_specs=[vmem] * (2 + len(more_out)),
        out_shape=[jax.ShapeDtypeStruct((2, rows, total), jnp.bfloat16)]
        + [jax.ShapeDtypeStruct(small.shape, small.dtype)]
        + more_out,
        scratch_shapes=ref_shapes
        + sem_shapes
        + pair_shapes
        + more_scratch
        + [
            pltpu.VMEM((width, total), jnp.bfloat16),
            pltpu.VMEM(small.shape, small.dtype),
            pltpu.VMEM((sources, *small.shape), small.dtype),
            pltpu.VMEM((2, *small.shape), small.dtype),
        ]
        + [pltpu.SemaphoreType.DMA((sources,))] * 2
        + [pltpu.SemaphoreType.DMA((2,))] * 2,
        compiler_params=pltpu.CompilerParams(
            collective_id=collective_id, has_side_effects=True, vmem_limit_bytes=VMEM_LIMIT
        ),
        cost_estimate=lasting(45),
        name="finish_grads",
    )(*lefts, *rights, *arrays, small)


def on_device(
    tokens,
    attn_gain,
    qkv_weight,
    out_weight,
    bias_table,
    gate_logit,
    ffn_gain,
    up_weight,
    down_weight,
    memory_keys,
    memory_values,
    book_lengths,
    slot_shard,
    slot_index,
    slot_live,
    cotangent,
):
    rows, width = tokens.shape
    heads, buckets = bias_table.shape
    head_dim = width // heads
    top_count = slot_index.shape[2]
    hidden = up_weight.shape[1]
    groups = lax.axis_size("mem")
    capacity = -(-3 * rows * heads * top_count // (2 * groups) // 128) * 128
    score_scale = 1.0 / math.sqrt(head_dim)
    repeats = W // rows
    span = W + 2 * rows
    before = W - jnp.arange(span, dtype=jnp.int32)
    after = jnp.arange(span, dtype=jnp.int32)

    def bias_rows(offset):
        reached = (offset >= 0) & (offset < W)
        hot = (bucket_of(offset)[:, None] == jnp.arange(buckets, dtype=jnp.int32)) & reached[:, None]
        rows_of_bias = jnp.einsum(
            "rb,hb->hr", hot.astype(jnp.float32), bias_table, precision=lax.Precision.HIGHEST
        )
        return rows_of_bias + jnp.where(reached, 0.0, masked_score)

    before_bias, after_bias = bias_rows(before), bias_rows(after)
    bucket = bucket_of(jnp.arange(W, dtype=jnp.int32))
    one_hot = (bucket[:, None] == jnp.arange(buckets, dtype=jnp.int32)).astype(jnp.float32)
    tokens_f = tokens.astype(jnp.float32)
    normed_in = normed(tokens_f, attn_gain).astype(jnp.bfloat16)
    projected = jnp.dot(normed_in, qkv_weight, preferred_element_type=jnp.float32).astype(
        jnp.bfloat16
    )
    slots = memory_keys.shape[0]
    requests = place_requests(slot_shard, slot_index, slot_live, groups, capacity, slots)
    incoming = lax.all_to_all(requests, "mem", split_axis=0, concat_axis=0, tiled=True)
    keys_values, _ = lax.optimization_barrier((projected[:, width:], requests))
    halos = [passed_along(keys_values, "mem", distance) for distance in range(repeats, 0, -1)]
    index, row_ids, bounds = read_lists(incoming, heads, rows, slots)
    bounds = bounds.reshape(-1)
    key_rows, value_rows = gather_rows(
        index.reshape(-1), bounds, memory_keys, memory_values, heads, groups, capacity
    )
    all_queries = lax.all_gather(projected[:, :width], "mem", axis=0, tiled=True)
    local = local_forward(before_bias, book_lengths, projected, halos, heads, score_scale)
    partial = memory_forward(
        bounds,
        all_queries,
        key_rows,
        value_rows,
        row_ids,
        heads,
        groups,
        rows,
        score_scale,
    )
    if groups == 16:
        memory_out, mem_log, local_out, local_log = merge_partials(partial, groups, 1, heads, local)
    else:
        local_out, local_log = run_alone("local_forward", local)
        partial = lax.all_to_all(
            partial.reshape(groups, rows, width + 128),
            "mem",
            split_axis=0,
            concat_axis=0,
            tiled=True,
        ).reshape(groups * rows, width + 128)
        memory_out, mem_log = combine_partials(partial, heads, groups, rows)
    gate_share = jax.nn.sigmoid(gate_logit)
    (
        mixed_heads,
        normed_mid,
        activated,
        d_up,
        block_out,
        d_residual,
        ffn_gain_part,
        d_branch,
        d_mixed,
        gate_products,
        sent_grads,
    ) = middle(
        tokens,
        memory_out,
        local_out,
        mem_log,
        local_log,
        gate_share,
        out_weight,
        ffn_gain,
        up_weight,
        down_weight,
        cotangent,
        heads,
    )
    ffn_gain_part = ffn_gain_part.reshape(-1)
    early_halves = pair_grads(
        [mixed_heads, normed_mid, cotangent], [d_branch, d_up, activated], 5
    )
    early_sums = scattered(early_halves)
    sent_grads, _ = lax.optimization_barrier((sent_grads, early_halves))
    gate_part = jnp.sum(gate_products, axis=1) * gate_share * (1.0 - gate_share)
    local = local_queries(
        before_bias,
        book_lengths,
        projected,
        halos,
        d_mixed,
        local_out,
        local_log,
        gate_share,
        heads,
        score_scale,
    )
    if groups == 16:
        all_grads, d_queries, diagonals = gather_group(sent_grads, groups, 2, local)
    else:
        all_grads = lax.all_gather(sent_grads, "mem", axis=0, tiled=True)
        d_queries, diagonals = run_alone("local_queries", local)
    bias_part = jnp.dot(diagonals[:, rows - 1 : rows - 1 + W], one_hot, precision=lax.Precision.HIGHEST)
    d_partial = memory_backward(
        bounds,
        all_queries,
        all_grads,
        key_rows,
        value_rows,
        row_ids,
        heads,
        groups,
        rows,
        score_scale,
    )
    local = local_keys(
        after_bias,
        book_lengths,
        projected,
        all_queries,
        all_grads,
        (1.0 - gate_share) / gate_share,
        repeats + 1,
        heads,
        score_scale,
    )
    if groups == 16:
        d_projected = sum_queries(d_partial, d_queries, groups, 3, score_scale, local)
    else:
        (d_projected,) = run_alone("local_keys", local)
        d_partial, d_projected = lax.optimization_barrier((d_partial, d_projected))
        d_partial = jnp.sum(
            lax.all_to_all(
                d_partial.reshape(groups, rows, width), "mem", split_axis=0, concat_axis=0, tiled=True
            ).astype(jnp.float32),
            axis=0,
        )
        d_queries = (d_queries + d_partial * score_scale).astype(jnp.bfloat16)
        d_projected = jnp.concatenate([d_queries, d_projected[:, width:]], axis=1)
    beside = input_backward(tokens, attn_gain, d_projected, qkv_weight, d_residual)
    small = jnp.concatenate([ffn_gain_part, bias_part.reshape(-1), gate_part], axis=0)
    small = jnp.pad(small, (width, -small.shape[0] % 1024)).reshape(-1, 128)
    early_widths = [width, hidden, hidden]
    if groups == 16:
        late_both, small, tokens_grad, _ = finish_grads(
            [normed_in], [d_projected], small, groups, 4, beside
        )
        early_sums, small = lax.optimization_barrier((early_sums, small))
        early_both = join_halves(early_sums, 7)
    else:
        tokens_grad, attn_gain_part = run_alone("input_backward", beside)
        late_halves = pair_grads([normed_in], [d_projected], 6)
        late_halves, early_sums = lax.optimization_barrier((late_halves, early_sums))
        late_both = lax.all_gather(scattered(late_halves), "dp", axis=0)
        early_both = lax.all_gather(early_sums, "dp", axis=0)
        small = lax.psum(small.at[: width // 128].set(attn_gain_part.reshape(-1, 128)), ("dp", "mem"))
    qkv_grad, out_grad, up_grad, down_grad, attn_sum, ffn_sum, bias_sum, gate_sum = write_results(
        late_both, [3 * width], early_both, early_widths, small, heads, buckets
    )
    return (
        block_out,
        tokens_grad,
        qkv_grad,
        out_grad,
        up_grad,
        down_grad,
        attn_sum.reshape(-1),
        ffn_sum.reshape(-1),
        bias_sum,
        gate_sum.reshape(-1),
    )


def solution(mesh):
    in_specs = (
        P(("dp", "mem"), None),
        P(),
        P(),
        P(),
        P(),
        P(),
        P(),
        P(),
        P(),
        P("mem", None),
        P("mem", None),
        P("dp", None),
        P(("dp", "mem"), None, None, None),
        P(("dp", "mem"), None, None),
        P(("dp", "mem"), None, None),
        P(("dp", "mem"), None),
    )
    out_specs = (
        P(("dp", "mem"), None),
        P(("dp", "mem"), None),
        P("mem", None),
        P("mem", None),
        P("mem", None),
        P("mem", None),
        P(),
        P(),
        P(),
        P(),
    )
    return jax.shard_map(
        on_device, mesh=mesh, in_specs=in_specs, out_specs=out_specs, check_vma=False
    )
```

```python
import math

import jax
import jax.numpy as jnp
from jax import lax
from jax.experimental import pallas as pl
from jax.experimental.pallas import tpu as pltpu
from jax.sharding import PartitionSpec as P

W = 512
VMEM_LIMIT = 56 * 1024 * 1024


eps_norm = 1e-06
bucket_edges = tuple((math.ceil(16 * 8 ** (edge_step / 16)) for edge_step in range(1, 16)))
masked_score = -1e30
dead_score = -10000.0
contract_rows = (((0,), (0,)), ((), ()))
contract_cols = (((1,), (1,)), ((), ()))


def passed_along(value, axis, by):
    size = lax.axis_size(axis)
    pairs = [(i, i + by) for i in range(size) if 0 <= i + by < size]
    return lax.ppermute(value, axis, pairs)


def bucket_of(offset):
    past_edges = sum(((offset >= edge_pos).astype(jnp.int32) for edge_pos in bucket_edges))
    return jnp.where(offset < 16, offset, 16 + past_edges)


def normed(values, gain_vec):
    return (
        values * lax.rsqrt(jnp.mean(values * values, axis=-1, keepdims=True) + eps_norm) * gain_vec
    )


def place_requests(slot_shard, slot_index, slot_live, owners, capacity, slots):
    rows, heads, top_count = slot_index.shape
    entries, empty = rows * heads * top_count, heads * rows * slots
    if (owners + 1) * empty >= 2**31:
        raise ValueError("codes exceed int32")
    row_of = (
        jnp.arange(heads, dtype=jnp.int32)[None, :] * rows
        + jnp.arange(rows, dtype=jnp.int32)[:, None]
    )
    owner = jnp.where(slot_live > 0, slot_shard[..., 0], owners)
    codes = owner * empty + row_of[:, :, None] * slots + slot_index
    codes = lax.sort(codes.reshape(-1), is_stable=False)
    ends = jnp.sum(
        (codes[None, :] < (jnp.arange(owners, dtype=jnp.int32) + 1)[:, None] * empty).astype(jnp.int32),
        axis=1,
    )
    starts = jnp.concatenate([jnp.zeros((1,), jnp.int32), ends[:-1]])
    tall = -(-entries // 128)
    codes = jnp.pad(codes, (0, tall * 128 - entries)).reshape(tall, 128)
    long = capacity // 128

    def kernel(starts_ref, ends_ref, codes_ref, lists_ref, padded):
        padded[:tall, :] = codes_ref[...]
        padded[tall:, :] = jnp.zeros((long + 8, 128), jnp.int32)
        lane = lax.broadcasted_iota(jnp.int32, (long, 128), 1)
        place = lax.broadcasted_iota(jnp.int32, (long, 128), 0) * 128 + lane

        @pl.loop(0, owners)
        def _(i):
            start, end = starts_ref[i], ends_ref[i]
            shift = start % 128
            lines = padded[pl.ds(start // 128, long + 1), :]
            turned = pltpu.roll(lines, (128 - shift) % 128, 1)
            joined = jnp.where(lane < 128 - shift, turned[:long], turned[1:])
            lists_ref[i] = jnp.where(place < end - start, joined - i * empty, empty)

    return pl.pallas_call(
        kernel,
        in_specs=[pl.BlockSpec(memory_space=pltpu.SMEM)] * 2 + [pl.BlockSpec(memory_space=pltpu.VMEM)],
        out_shape=jax.ShapeDtypeStruct((owners, long, 128), jnp.int32),
        scratch_shapes=[pltpu.VMEM((tall + long + 8, 128), jnp.int32)],
        cost_estimate=lasting(3),
        name="make_lists",
    )(starts, ends, codes)


def read_lists(incoming, heads, rows, slots):
    sources, long, _ = incoming.shape

    def kernel(lists_ref, index_ref, ids_ref, bounds_ref):
        lane = lax.broadcasted_iota(jnp.int32, (1, 128), 1)

        def read(source):
            codes = lists_ref[source]
            ids = lax.div(codes, slots)
            index = lax.div(ids, rows) * slots + lax.rem(codes, slots)
            index_ref[source] = jnp.where(ids < heads * rows, index, 0)
            ids_ref[source, :long, :] = ids
            ids_ref[source, long:, :] = jnp.full((1, 128), heads * rows, jnp.int32)
            bounds = jnp.zeros((1, 128), jnp.int32)
            for head in range(1, heads + 1):
                below = jnp.sum(
                    jnp.where(codes < head * rows * slots, 1.0, 0.0), axis=0, keepdims=True
                )
                below = jnp.sum(below, axis=1, keepdims=True).astype(jnp.int32)
                bounds = jnp.where(lane == head, below, bounds)
            bounds_ref[pl.ds(source, 1), :] = bounds

        if sources > 16:
            pl.loop(0, sources)(read)
        else:
            for source in range(sources):
                read(source)

    return pl.pallas_call(
        kernel,
        out_shape=[
            jax.ShapeDtypeStruct((sources, long, 128), jnp.int32),
            jax.ShapeDtypeStruct((sources, long + 1, 128), jnp.int32),
            jax.ShapeDtypeStruct((sources, 128), jnp.int32),
        ],
        cost_estimate=lasting(3),
        name="read_lists",
    )(incoming)


def gather_rows(index, bounds, memory_keys, memory_values, heads, sources, capacity):
    slots, width = memory_keys.shape
    head_dim = width // heads
    step, part = 128, 16

    def kernel(index_ref, bounds_ref, keys, values, out_keys, out_values, key_table, value_table, key_rows, value_rows):
        i = pl.program_id(0)

        @pl.when(i < heads)
        def _():
            place = pl.ds(pl.multiple_of(i * slots, slots), slots)
            key_table[place, :] = keys[...].astype(jnp.float32)
            value_table[place, :] = values[...].astype(jnp.float32)

        @pl.when(i >= heads)
        def _():
            source = i - heads

            used = (bounds_ref[source * 128 + heads] + step - 1) // step

            def store(group):
                for at in range(0, step, part):
                    here = pl.ds(pl.multiple_of(group * step, step) + at, part)
                    out_keys[here, :] = key_rows[at : at + part, :].astype(jnp.bfloat16)
                    out_values[here, :] = value_rows[at : at + part, :].astype(jnp.bfloat16)

            @pl.loop(0, used)
            def _(group):
                store(jnp.maximum(group - 1, 0))
                first = source * capacity + group * step
                for u in range(step):
                    row = index_ref[first + u]
                    key_rows[u : u + 1, :] = key_table[pl.ds(row, 1), :]
                    value_rows[u : u + 1, :] = value_table[pl.ds(row, 1), :]

            pl.when(used > 0)(lambda: store(used - 1))

            @pl.loop(used, capacity // step)
            def _(group):
                here = pl.ds(pl.multiple_of(group * step, step), step)
                out_keys[here, :] = jnp.zeros((step, head_dim), jnp.bfloat16)
                out_values[here, :] = jnp.zeros((step, head_dim), jnp.bfloat16)

    table_spec = pl.BlockSpec((slots, head_dim), lambda i, *_: (0, jnp.minimum(i, heads - 1)))
    out_spec = pl.BlockSpec((capacity, head_dim), lambda i, *_: (jnp.maximum(i - heads, 0), 0))
    out_shape = jax.ShapeDtypeStruct((sources * capacity, head_dim), jnp.bfloat16)
    return pl.pallas_call(
        kernel,
        grid_spec=pltpu.PrefetchScalarGridSpec(
            num_scalar_prefetch=2,
            grid=(heads + sources,),
            in_specs=[table_spec, table_spec],
            out_specs=[out_spec, out_spec],
            scratch_shapes=[
                pltpu.VMEM((heads * slots, head_dim), jnp.float32),
                pltpu.VMEM((heads * slots, head_dim), jnp.float32),
                pltpu.VMEM((step, head_dim), jnp.float32),
                pltpu.VMEM((step, head_dim), jnp.float32),
            ],
        ),
        out_shape=[out_shape, out_shape],
        compiler_params=pltpu.CompilerParams(vmem_limit_bytes=VMEM_LIMIT),
        cost_estimate=lasting(42),
        name="gather_rows",
    )(index, bounds, memory_keys, memory_values)


def lasting(microseconds):
    return pl.CostEstimate(flops=0, bytes_accessed=3_000_000 * microseconds, transcendentals=0)


def triple(stat):
    part = lax.broadcasted_iota(jnp.int32, stat.shape, 1) // 16
    high = stat.astype(jnp.bfloat16).astype(jnp.float32)
    rest = stat - high
    middle = rest.astype(jnp.bfloat16).astype(jnp.float32)
    low = rest - middle
    chosen = jnp.where(part == 0, high, jnp.where(part == 1, middle, jnp.where(part == 2, low, 0.0)))
    return chosen.astype(jnp.bfloat16)


def window_of(bounds, source, head, heads, span, capacity):
    first, last = bounds[source * 128 + head], bounds[source * 128 + head + 1]
    start = jnp.minimum(first // 16 * 16, capacity - span)
    extra = jnp.maximum(last - start - 1, 0) // span
    return start, extra


def columns_of(head, head_dim):
    if isinstance(head, int):
        return slice(head * head_dim, (head + 1) * head_dim)
    return pl.ds(pl.multiple_of(head * head_dim, head_dim), head_dim)


def window_ids(id_ref, start, span):
    lines = id_ref[0, pl.ds(start // 128, span // 128 + 1), :]
    shift = start % 128
    turned = pltpu.roll(lines, (128 - shift) % 128, 1)
    lane = lax.broadcasted_iota(jnp.int32, (span // 128, 128), 1)
    return jnp.where(lane < 128 - shift, turned[:-1], turned[1:])


def owned(lines, first_row, count, start, least):
    row = lax.broadcasted_iota(jnp.int32, (count, 128), 0) + first_row
    masks = []
    for i in range(lines.shape[0]):
        mask = lines[i : i + 1, :] == row
        if least is not None:
            place = lax.broadcasted_iota(jnp.int32, (1, 128), 1) + start + i * 128
            mask = mask & (place >= least)
        masks.append(mask)
    return jnp.concatenate(masks, axis=1)


def memory_forward(bounds, queries, key_rows, value_rows, row_ids, heads, sources, rows, score_scale):
    capacity, head_dim = key_rows.shape[0] // sources, key_rows.shape[1]
    width = heads * head_dim
    span = min(384, capacity)
    chunk = math.gcd(rows, 32)

    def kernel(bounds_ref, q_ref, k_ref, v_ref, id_ref, out_ref, sums, tops, totals, raw, weights):
        source = pl.program_id(0)
        lane = lax.broadcasted_iota(jnp.int32, (chunk, 128), 1) % 16

        def window(heads_here, starts, least):
            here = [pl.ds(pl.multiple_of(start, 16), span) for start in starts]
            columns = [columns_of(head, head_dim) for head in heads_here]
            for slot in range(len(starts)):
                raw[slot] = lax.dot_general(
                    q_ref[:, columns[slot]],
                    k_ref[here[slot], :],
                    contract_cols,
                    preferred_element_type=jnp.float32,
                )
            for slot, (head, start) in enumerate(zip(heads_here, starts)):
                lines = window_ids(id_ref, start, span)
                for at in range(0, rows, chunk):
                    some = slice(at, at + chunk)
                    mine = owned(lines, head * rows + at, chunk, start, least)
                    scores = jnp.where(mine, raw[slot, some, :], masked_score)
                    top = jnp.maximum(jnp.max(scores, axis=1, keepdims=True), 0.1 * masked_score)
                    if least is not None:
                        old_top = jnp.max(
                            jnp.where(lane == head, tops[some, :], masked_score), axis=1, keepdims=True
                        )
                        top = jnp.maximum(top, old_top)
                    exps = jnp.exp((scores - top) * score_scale)
                    weights[slot, some, :] = exps.astype(jnp.bfloat16)
                    total = jnp.sum(exps, axis=1, keepdims=True)
                    if least is not None:
                        faded = jnp.exp((old_top - top) * score_scale)
                        sums[some, columns[slot]] = sums[some, columns[slot]] * faded
                        total = total + totals[some, :] * faded
                    tops[some, :] = jnp.where(lane == head, top, tops[some, :])
                    totals[some, :] = jnp.where(lane == heads + head, total, totals[some, :])
            for slot in range(len(starts)):
                found = jnp.dot(
                    weights[slot], v_ref[here[slot], :], preferred_element_type=jnp.float32
                )
                sums[:, columns[slot]] = found if least is None else sums[:, columns[slot]] + found

        tops[...] = jnp.zeros_like(tops)
        totals[...] = jnp.zeros_like(totals)

        windows = [window_of(bounds_ref, source, head, heads, span, capacity) for head in range(heads)]
        window(list(range(heads)), [start for start, _ in windows], None)

        @pl.when(sum(extra for _, extra in windows) > 0)
        def _():
            @pl.loop(0, heads)
            def _(head):
                start, extra = window_of(bounds_ref, source, head, heads, span, capacity)

                @pl.loop(0, extra)
                def _(turn):
                    least = start + (turn + 1) * span
                    window([head], [jnp.minimum(least, capacity - span)], least)

        out_ref[:, :width] = sums[...].astype(jnp.bfloat16)
        wide = lax.broadcasted_iota(jnp.int32, (rows, 128), 1) % 16
        out_ref[:, width:] = triple(jnp.where(wide < heads, tops[...] * score_scale, totals[...]))

    return pl.pallas_call(
        kernel,
        grid_spec=pltpu.PrefetchScalarGridSpec(
            num_scalar_prefetch=1,
            grid=(sources,),
            in_specs=[
                pl.BlockSpec((rows, width), lambda i, *_: (i, 0)),
                pl.BlockSpec((capacity, head_dim), lambda i, *_: (i, 0)),
                pl.BlockSpec((capacity, head_dim), lambda i, *_: (i, 0)),
                pl.BlockSpec((1, *row_ids.shape[1:]), lambda i, *_: (i, 0, 0)),
            ],
            out_specs=pl.BlockSpec((rows, width + 128), lambda i, *_: (i, 0)),
            scratch_shapes=[
                pltpu.VMEM((rows, width), jnp.float32),
                pltpu.VMEM((rows, 128), jnp.float32),
                pltpu.VMEM((rows, 128), jnp.float32),
                pltpu.VMEM((heads, rows, span), jnp.float32),
                pltpu.VMEM((heads, rows, span), jnp.bfloat16),
            ],
        ),
        out_shape=jax.ShapeDtypeStruct((sources * rows, width + 128), jnp.bfloat16),
        compiler_params=pltpu.CompilerParams(vmem_limit_bytes=VMEM_LIMIT),
        cost_estimate=lasting(25),
        name="memory_forward",
    )(bounds, queries, key_rows, value_rows, row_ids)


def combine_partials(partial, heads, sources, rows):
    width = partial.shape[1] - 128
    head_dim = width // heads

    def kernel(part_ref, out_ref, log_ref, sums, tops, totals):
        i = pl.program_id(0)

        @pl.when(i == 0)
        def _():
            sums[...] = jnp.zeros_like(sums)
            tops[...] = jnp.full_like(tops, masked_score)
            totals[...] = jnp.zeros_like(totals)

        stat = part_ref[:, width:].astype(jnp.float32)
        stat = stat + pltpu.roll(stat, 128 - 16, 1) + pltpu.roll(stat, 128 - 32, 1)
        new_total = pltpu.roll(stat, 128 - heads, 1)
        top = jnp.maximum(tops[...], stat)
        old_fade, new_fade = jnp.exp(tops[...] - top), jnp.exp(stat - top)
        tops[...] = top
        totals[...] = totals[...] * old_fade + new_total * new_fade
        for head in range(heads):
            columns = slice(head * head_dim, (head + 1) * head_dim)
            sums[:, columns] = (
                sums[:, columns] * old_fade[:, head : head + 1]
                + part_ref[:, columns].astype(jnp.float32) * new_fade[:, head : head + 1]
            )

        @pl.when(i == sources - 1)
        def _():
            live = totals[...] > 0
            total = jnp.where(live, totals[...], 1.0)
            log_ref[...] = jnp.where(live, tops[...] + jnp.log(total), 0.0)
            for head in range(heads):
                columns = slice(head * head_dim, (head + 1) * head_dim)
                out_ref[:, columns] = sums[:, columns] / total[:, head : head + 1]

    return pl.pallas_call(
        kernel,
        grid=(sources,),
        in_specs=[pl.BlockSpec((rows, width + 128), lambda i: (i, 0))],
        out_specs=[
            pl.BlockSpec((rows, width), lambda i: (0, 0)),
            pl.BlockSpec((rows, 128), lambda i: (0, 0)),
        ],
        scratch_shapes=[
            pltpu.VMEM((rows, width), jnp.float32),
            pltpu.VMEM((rows, 128), jnp.float32),
            pltpu.VMEM((rows, 128), jnp.float32),
        ],
        out_shape=[
            jax.ShapeDtypeStruct((rows, width), jnp.float32),
            jax.ShapeDtypeStruct((rows, 128), jnp.float32),
        ],
        compiler_params=pltpu.CompilerParams(vmem_limit_bytes=VMEM_LIMIT),
        cost_estimate=lasting(13),
        name="combine_partials",
    )(partial)


def memory_backward(bounds, queries, grads, key_rows, value_rows, row_ids, heads, sources, rows, score_scale):
    capacity, head_dim = key_rows.shape[0] // sources, key_rows.shape[1]
    width = heads * head_dim
    span = min(384, capacity)
    chunk = math.gcd(rows, 32)

    def kernel(bounds_ref, q_ref, g_ref, k_ref, v_ref, id_ref, out_ref, sums, stats, raw, products, slopes):
        source = pl.program_id(0)
        stats[...] = joined_tile(g_ref[:, width : width + 128])

        def window(heads_here, starts, least):
            here = [pl.ds(pl.multiple_of(start, 16), span) for start in starts]
            columns = [columns_of(head, head_dim) for head in heads_here]
            for slot in range(len(starts)):
                raw[slot] = lax.dot_general(
                    q_ref[:, columns[slot]],
                    k_ref[here[slot], :],
                    contract_cols,
                    preferred_element_type=jnp.float32,
                )
                products[slot] = lax.dot_general(
                    g_ref[:, columns[slot]],
                    v_ref[here[slot], :],
                    contract_cols,
                    preferred_element_type=jnp.float32,
                )
            for slot, (head, start) in enumerate(zip(heads_here, starts)):
                lines = window_ids(id_ref, start, span)
                turned = stats[...]
                if least is not None:
                    turned = pltpu.roll(turned, 128 - head, 1)
                elif head:
                    turned = turned[:, head:]
                for at in range(0, rows, chunk):
                    some = slice(at, at + chunk)
                    mine = owned(lines, head * rows + at, chunk, start, least)
                    log, delta = turned[some, :1], turned[some, heads : heads + 1]
                    probs = jnp.exp(jnp.where(mine, raw[slot, some, :] * score_scale - log, dead_score))
                    slopes[slot, some, :] = (probs * (products[slot, some, :] - delta)).astype(
                        jnp.bfloat16
                    )
            for slot in range(len(starts)):
                found = jnp.dot(
                    slopes[slot], k_ref[here[slot], :], preferred_element_type=jnp.float32
                )
                sums[:, columns[slot]] = found if least is None else sums[:, columns[slot]] + found

        windows = [window_of(bounds_ref, source, head, heads, span, capacity) for head in range(heads)]
        window(list(range(heads)), [start for start, _ in windows], None)

        @pl.when(sum(extra for _, extra in windows) > 0)
        def _():
            @pl.loop(0, heads)
            def _(head):
                start, extra = window_of(bounds_ref, source, head, heads, span, capacity)

                @pl.loop(0, extra)
                def _(turn):
                    least = start + (turn + 1) * span
                    window([head], [jnp.minimum(least, capacity - span)], least)

        out_ref[...] = sums[...].astype(jnp.bfloat16)

    return pl.pallas_call(
        kernel,
        grid_spec=pltpu.PrefetchScalarGridSpec(
            num_scalar_prefetch=1,
            grid=(sources,),
            in_specs=[
                pl.BlockSpec((rows, width), lambda i, *_: (i, 0)),
                pl.BlockSpec((rows, width + 128), lambda i, *_: (i, 0)),
                pl.BlockSpec((capacity, head_dim), lambda i, *_: (i, 0)),
                pl.BlockSpec((capacity, head_dim), lambda i, *_: (i, 0)),
                pl.BlockSpec((1, *row_ids.shape[1:]), lambda i, *_: (i, 0, 0)),
            ],
            out_specs=pl.BlockSpec((rows, width), lambda i, *_: (i, 0)),
            scratch_shapes=[
                pltpu.VMEM((rows, width), jnp.float32),
                pltpu.VMEM((rows, 128), jnp.float32),
                pltpu.VMEM((heads, rows, span), jnp.float32),
                pltpu.VMEM((heads, rows, span), jnp.float32),
                pltpu.VMEM((heads, rows, span), jnp.bfloat16),
            ],
        ),
        out_shape=jax.ShapeDtypeStruct((sources * rows, width), jnp.bfloat16),
        compiler_params=pltpu.CompilerParams(vmem_limit_bytes=VMEM_LIMIT),
        cost_estimate=lasting(25),
        name="memory_backward",
    )(bounds, queries, grads, key_rows, value_rows, row_ids)


def remote(source, target, send_sem, recv_sem, device):
    return pltpu.make_async_remote_copy(
        src_ref=source,
        dst_ref=target,
        send_sem=send_sem,
        recv_sem=recv_sem,
        device_id={"mem": device},
        device_id_type=pl.DeviceIdType.MESH,
    )


def grid_place(depth):
    me = lax.axis_index("mem")
    layer, column = me // 4, me % 4
    beside_x = column + 1 - 2 * (column % 2)
    beside_y = column + 2 - 4 * (column // 2)
    across = 3 - column

    def index_of(step, place):
        return (layer + step + depth) % depth * 4 + place

    return me, column, beside_x, beside_y, across, index_of


def greet(devices):
    barrier = pltpu.get_barrier_semaphore()
    for device in devices:
        pl.semaphore_signal(
            barrier, inc=1, device_id={"mem": device}, device_id_type=pl.DeviceIdType.MESH
        )
    pl.semaphore_wait(barrier, len(devices))


def gather_group(block, sources, collective_id, beside):
    rows, width = block.shape
    depth, half = sources // 4, rows // 2
    slots = 2 * depth - 1
    arrays, specs, more_out, more_scratch, begin = beside
    ins, outs = len(arrays), len(more_out)

    def kernel(x_ref, *refs):
        in_refs, (out_ref, *more_refs) = refs[:ins], refs[ins : ins + 1 + outs]
        (own_sem, send, recv), scratch = refs[ins + 1 + outs : ins + 4 + outs], refs[ins + 4 + outs :]
        meanwhile = begin(in_refs, more_refs, scratch)
        me = lax.axis_index("mem")
        layer, column = me // 4, me % 4
        to_x = me + 1 - 2 * (column % 2)
        to_y = me + 2 - 4 * (column // 2)
        across = layer * 4 + 3 - column
        has_above, has_below = layer + 1 < depth, layer > 0
        barrier = pltpu.get_barrier_semaphore()

        def signal(device):
            pl.semaphore_signal(
                barrier, inc=1, device_id={"mem": device}, device_id_type=pl.DeviceIdType.MESH
            )

        signal(to_x)
        signal(to_y)
        pl.when(has_above)(lambda: signal(me + 4))
        pl.when(has_below)(lambda: signal(me - 4))
        pl.semaphore_wait(barrier, 2 + has_above.astype(jnp.int32) + has_below.astype(jnp.int32))

        def part_of(index, part):
            start = pl.multiple_of(index * rows + part * half, half)
            return out_ref.at[pl.ds(start, half), :]

        own = pltpu.make_async_copy(x_ref, out_ref.at[pl.ds(pl.multiple_of(me * rows, rows), rows), :], own_sem)
        own.start()
        sent = []

        def push(condition, source, target, kind, slot, to_slot, part, device):
            copy = remote(source, target, send.at[kind, slot, part], recv.at[kind, to_slot, part], device)
            if condition is None:
                copy.start()
            else:
                pl.when(condition)(copy.start)
            sent.append((condition, copy))

        def arrived(index, kind, slot, part):
            target = part_of(index, part)
            remote(target, target, send.at[kind, slot, part], recv.at[kind, slot, part], to_x).wait_recv()

        def up_slot(distance):
            return distance

        def down_slot(distance):
            return depth - 1 + distance

        for part in (0, 1):
            mine = x_ref.at[pl.ds(part * half, half), :]
            push(has_above, mine, part_of(me, part), 0, 0, down_slot(1), part, me + 4)
            push(has_below, mine, part_of(me, part), 1, 0, up_slot(1), part, me - 4)
            mine_y = x_ref.at[pl.ds((1 - part) * half, half), :]
            push(None, mine, part_of(me, part), 2, 0, 0, part, to_x)
            push(None, mine_y, part_of(me, 1 - part), 3, 0, 0, 1 - part, to_y)

        def pass_on(condition, step, slot):
            def go():
                arrived(to_x + step, 2, slot, 0)
                copy_a.start()
                arrived(to_y + step, 3, slot, 1)
                copy_b.start()

            source_a, source_b = part_of(to_x + step, 0), part_of(to_y + step, 1)
            copy_a = remote(source_a, source_a, send.at[4, slot, 0], recv.at[4, slot, 0], to_y)
            copy_b = remote(source_b, source_b, send.at[5, slot, 1], recv.at[5, slot, 1], to_x)
            sent.append((condition, copy_a))
            sent.append((condition, copy_b))
            if condition is None:
                go()
            else:
                pl.when(condition)(go)

        for distance in range(1, depth):
            from_above, from_below = layer + distance < depth, layer - distance >= 0

            def take(kind, back_kind, step, slot, next_slot, onward, onward_device):
                for part in (0, 1):
                    arrived(me + step, kind, slot, part)
                    here = part_of(me + step, part)
                    if next_slot is not None:
                        pl.when(onward)(
                            remote(
                                here, here, send.at[kind, slot, part], recv.at[kind, next_slot, part], onward_device
                            ).start
                        )
                    remote(here, here, send.at[2, slot, part], recv.at[2, slot, part], to_x).start()
                    remote(here, here, send.at[3, slot, part], recv.at[3, slot, part], to_y).start()

            last = distance == depth - 1
            pl.when(from_above)(
                lambda: take(
                    1, 0, 4 * distance, up_slot(distance), None if last else up_slot(distance + 1), has_below, me - 4
                )
            )
            pl.when(from_below)(
                lambda: take(
                    0, 1, -4 * distance, down_slot(distance), None if last else down_slot(distance + 1), has_above, me + 4
                )
            )
            for condition, step, slot, kind, onward in (
                (from_above, 4 * distance, up_slot(distance), 1, has_below),
                (from_below, -4 * distance, down_slot(distance), 0, has_above),
            ):
                for part in (0, 1):
                    here = part_of(me + step, part)
                    if not last:
                        sent.append((condition & onward, remote(here, here, send.at[kind, slot, part], own_sem, me)))
                    sent.append((condition, remote(here, here, send.at[2, slot, part], own_sem, to_x)))
                    sent.append((condition, remote(here, here, send.at[3, slot, part], own_sem, to_y)))
            meanwhile(distance - 1, depth - 1)
            if distance == 1:
                pass_on(None, 0, 0)
            else:
                pass_on(layer + distance - 1 < depth, 4 * (distance - 1), up_slot(distance - 1))
                pass_on(layer - distance + 1 >= 0, -4 * (distance - 1), down_slot(distance - 1))
        pass_on(layer + depth - 1 < depth, 4 * (depth - 1), up_slot(depth - 1))
        pass_on(layer - depth + 1 >= 0, -4 * (depth - 1), down_slot(depth - 1))

        def close(step, slot):
            arrived(to_x + step, 2, slot, 1)
            arrived(to_y + step, 3, slot, 0)
            arrived(across + step, 4, slot, 0)
            arrived(across + step, 5, slot, 1)

        close(0, 0)
        for distance in range(1, depth):
            pl.when(layer + distance < depth)(lambda: close(4 * distance, up_slot(distance)))
            pl.when(layer - distance >= 0)(lambda: close(-4 * distance, down_slot(distance)))
        for condition, copy in sent:
            if condition is None:
                copy.wait_send()
            else:
                pl.when(condition)(copy.wait_send)
        own.wait()

    return pl.pallas_call(
        kernel,
        in_specs=[pl.BlockSpec(memory_space=pl.ANY), *specs],
        out_specs=[pl.BlockSpec(memory_space=pl.ANY)] + [pl.BlockSpec(memory_space=pltpu.VMEM)] * outs,
        out_shape=[jax.ShapeDtypeStruct((sources * rows, width), block.dtype), *more_out],
        scratch_shapes=[
            pltpu.SemaphoreType.DMA,
            pltpu.SemaphoreType.DMA((6, slots, 2)),
            pltpu.SemaphoreType.DMA((6, slots, 2)),
            *more_scratch,
        ],
        compiler_params=pltpu.CompilerParams(
            collective_id=collective_id, has_side_effects=True, vmem_limit_bytes=VMEM_LIMIT
        ),
        cost_estimate=lasting(50),
        name="gather_group",
    )(block, *arrays)


def reduce_steps(parts_ref, sources, refs, sems, merge, pack, beside=None):
    half_a, half_b, from_x, from_y, from_z, out_x, out_y, out_z = refs
    send, recv_a, recv_b, recv_x, recv_y, recv_z = sems
    rows = parts_ref.shape[0] // sources
    depth, half = sources // 4, rows // 2
    me, column, beside_x, beside_y, across, index_of = grid_place(depth)
    to_x, to_y = index_of(0, beside_x), index_of(0, beside_y)
    order = [*range(1, depth), 0]
    queues = {"x": [], "y": [], "z": []}
    first_limit = 2 if beside is None else depth

    def piece(index, part):
        return parts_ref.at[pl.ds(pl.multiple_of(index * rows + part * half, half), half), :]

    def part_rows(part):
        return pl.ds(part * half, half)

    def push(link, source, target, kind, k, recv_sem, device, limit=2):
        queue = queues[link]
        while link != "z" and len(queue) >= limit:
            queue.pop(0).wait_send()
        copy = remote(source, target, send.at[kind, k], recv_sem, device)
        copy.start()
        queue.append(copy)

    def arrived(target, recv_sem):
        remote(target, target, send.at[0, 0], recv_sem, to_x).wait_recv()

    def plane_rest(k):
        push("x", piece(index_of(k, beside_x), 0), from_x.at[k, part_rows(0)], 2, k, recv_x.at[0, k], to_x)
        push("y", piece(index_of(k, beside_y), 1), from_y.at[k, part_rows(1)], 3, k, recv_y.at[1, k], to_y)

    def plane_merged(k):
        arrived(half_a.at[k], recv_a.at[k])
        pack(out_y.at[k], merge([piece(index_of(k, beside_y), 0), half_a.at[k]]))
        push("y", out_y.at[k], from_y.at[k, part_rows(0)], 4, k, recv_y.at[0, k], to_y)
        arrived(half_b.at[k], recv_b.at[k])
        pack(out_x.at[k], merge([piece(index_of(k, beside_x), 1), half_b.at[k]]))
        push("x", out_x.at[k], from_x.at[k, part_rows(1)], 5, k, recv_x.at[1, k], to_x)

    def column_step(k):
        for part in (0, 1):
            here = part_rows(part)
            arrived(from_x.at[k, here], recv_x.at[part, k])
            arrived(from_y.at[k, here], recv_y.at[part, k])
            if k:
                blocks = [piece(index_of(k, column), part), from_x.at[k, here], from_y.at[k, here]]
                pack(out_z.at[k, here], merge(blocks))
        if k:
            push("z", out_z.at[k], from_z.at[k], 6, k, recv_z.at[k], index_of(k, column))

    for k in order:
        far = index_of(k, across)
        push("x", piece(far, 0), half_a.at[k], 0, k, recv_a.at[k], to_x, first_limit)
        push("y", piece(far, 1), half_b.at[k], 1, k, recv_b.at[k], to_y, first_limit)
    if beside is not None:
        beside()
    for i, k in enumerate(order):
        plane_rest(k)
        plane_merged(k)
        if i:
            column_step(order[i - 1])
    column_step(order[-1])
    for k in range(1, depth):
        arrived(from_z.at[k], recv_z.at[k])
    final = []
    for part in (0, 1):
        here = part_rows(part)
        blocks = [piece(me, part), from_x.at[0, here], from_y.at[0, here]]
        final.append((here, blocks + [from_z.at[k, here] for k in range(1, depth)]))
    return final, [copy for queue in queues.values() for copy in queue]


def reduce_scratch(rows, width, dtype, sources):
    depth, half = sources // 4, rows // 2

    def slots(size):
        return pltpu.VMEM((depth, size, width), dtype)

    refs = [slots(half), slots(half), slots(rows), slots(rows), slots(rows)]
    refs += [slots(half), slots(half), slots(rows)]
    sems = [pltpu.SemaphoreType.DMA((7, depth))]
    sems += [pltpu.SemaphoreType.DMA((depth,))] * 2
    sems += [pltpu.SemaphoreType.DMA((2, depth))] * 2
    sems += [pltpu.SemaphoreType.DMA((depth,))]
    return refs, sems


def run_alone(name, beside):
    arrays, specs, out_shape, scratch, begin = beside
    ins, outs = len(arrays), len(out_shape)

    def kernel(*refs):
        begin(refs[:ins], refs[ins : ins + outs], refs[ins + outs :])()

    return pl.pallas_call(
        kernel,
        in_specs=specs,
        out_specs=[pl.BlockSpec(memory_space=pltpu.VMEM)] * outs,
        out_shape=out_shape,
        scratch_shapes=scratch,
        compiler_params=pltpu.CompilerParams(vmem_limit_bytes=VMEM_LIMIT),
        cost_estimate=lasting(8),
        name=name,
    )(*arrays)


def reduce_group(parts, sources, collective_id, merge, pack, finish, out_shape, beside):
    rows, width = parts.shape[0] // sources, parts.shape[1]
    depth = sources // 4
    arrays, specs, more_out, more_scratch, begin = beside
    ref_shapes, sem_shapes = reduce_scratch(rows, width, parts.dtype, sources)
    sizes = [len(arrays), len(out_shape), len(more_out), len(ref_shapes), len(sem_shapes), len(more_scratch)]

    def kernel(parts_ref, *refs):
        groups, at = [], 0
        for size in sizes:
            groups.append(refs[at : at + size])
            at += size
        ins, out_refs, more_refs, steps_refs, steps_sems, scratch = groups
        meanwhile = begin(ins, more_refs, scratch)
        last = finish
        if finish is None:
            meanwhile, last = meanwhile
        me, column, beside_x, beside_y, across, index_of = grid_place(depth)
        greet(
            [index_of(0, beside_x), index_of(0, beside_y)]
            + [index_of(-k, column) for k in range(1, depth)]
        )
        final, still_open = reduce_steps(
            parts_ref, sources, steps_refs, steps_sems, merge, pack, meanwhile
        )
        for here, blocks in final:
            if finish is None:
                last(here, merge(blocks))
            else:
                last([out.at[here] for out in out_refs], merge(blocks))
        for copy in still_open:
            copy.wait_send()

    vmem = pl.BlockSpec(memory_space=pltpu.VMEM)
    return pl.pallas_call(
        kernel,
        in_specs=[vmem, *specs],
        out_specs=[vmem] * (len(out_shape) + len(more_out)),
        out_shape=[*out_shape, *more_out],
        scratch_shapes=[*ref_shapes, *sem_shapes, *more_scratch],
        compiler_params=pltpu.CompilerParams(
            collective_id=collective_id, has_side_effects=True, vmem_limit_bytes=VMEM_LIMIT
        ),
        cost_estimate=lasting(50),
        name="reduce_group",
    )(parts, *arrays)


def sum_queries(parts, d_queries, sources, collective_id, score_scale, beside):
    rows, width = d_queries.shape
    arrays, specs, (whole,), more_scratch, begin = beside

    def merge(blocks):
        total = blocks[0][...].astype(jnp.float32)
        for block in blocks[1:]:
            total = total + block[...].astype(jnp.float32)
        return total

    def pack(target, total):
        target[...] = total.astype(parts.dtype)

    def begin_both(ins, outs, scratch):
        run = begin(ins[:-1], outs, scratch)

        def finish(here, total):
            outs[0][here, :width] = (ins[-1][here, :] + total * score_scale).astype(whole.dtype)

        return run, finish

    more = [*arrays, d_queries], [*specs, pl.BlockSpec(memory_space=pltpu.VMEM)], [whole], more_scratch, begin_both
    return reduce_group(parts, sources, collective_id, merge, pack, None, [], more)[0]


def merge_partials(parts, sources, collective_id, heads, beside):
    rows, width = parts.shape[0] // sources, parts.shape[1] - 128
    head_dim = width // heads

    def merge(blocks):
        stats = []
        for block in blocks:
            stat = block[:, width:].astype(jnp.float32)
            stats.append(stat + pltpu.roll(stat, 128 - 16, 1) + pltpu.roll(stat, 128 - 32, 1))
        top = stats[0]
        for stat in stats[1:]:
            top = jnp.maximum(top, stat)
        fades = [jnp.exp(stat - top) for stat in stats]
        total = sum(fade * pltpu.roll(stat, 128 - heads, 1) for fade, stat in zip(fades, stats))
        sums = []
        for head in range(heads):
            columns = slice(head * head_dim, (head + 1) * head_dim)
            sums.append(
                sum(
                    block[:, columns].astype(jnp.float32) * fade[:, head : head + 1]
                    for block, fade in zip(blocks, fades)
                )
            )
        return sums, top, total

    def pack(target, merged):
        sums, top, total = merged
        for head in range(heads):
            target[:, head * head_dim : (head + 1) * head_dim] = sums[head].astype(parts.dtype)
        lane = lax.broadcasted_iota(jnp.int32, top.shape, 1)
        stat = jnp.where(lane < heads, top, jnp.where(lane < 16, pltpu.roll(total, heads, 1), 0.0))
        target[:, width:] = triple(stat + pltpu.roll(stat, 16, 1) + pltpu.roll(stat, 32, 1))

    def finish(targets, merged):
        sums, top, total = merged
        live = total > 0
        total = jnp.where(live, total, 1.0)
        targets[1][...] = jnp.where(live, top + jnp.log(total), 0.0)
        for head in range(heads):
            targets[0][:, head * head_dim : (head + 1) * head_dim] = sums[head] / total[:, head : head + 1]

    out_shape = [
        jax.ShapeDtypeStruct((rows, width), jnp.float32),
        jax.ShapeDtypeStruct((rows, 128), jnp.float32),
    ]
    return reduce_group(parts, sources, collective_id, merge, pack, finish, out_shape, beside)


def scattered(halves):
    return lax.psum_scatter(halves, "mem", scatter_dimension=0, tiled=True)


def same_book(lengths_ref, first_row, rows, first_lane, lanes):
    row = lax.broadcasted_iota(jnp.int32, (rows, lanes), 0) + first_row
    lane = lax.broadcasted_iota(jnp.int32, (rows, lanes), 1) + first_lane
    end, same = 0, lane >= 0
    for i in range(lengths_ref.shape[1]):
        end = end + lengths_ref[0, i]
        same = same & ((row >= end) == (lane >= end))
    return same


def lane_tile(columns, rows):
    lane = lax.broadcasted_iota(jnp.int32, (rows, 128), 1)
    tile = jnp.zeros((rows, 128), jnp.float32)
    for i, column in enumerate(columns):
        tile = jnp.where(lane == i, column, tile)
    return tile


def split_tile(tile):
    lane = lax.broadcasted_iota(jnp.int32, tile.shape, 1)
    kept = jnp.where(lane < 32, tile, 0.0)
    kept = kept + pltpu.roll(kept, 32, 1) + pltpu.roll(kept, 64, 1)
    high = kept.astype(jnp.bfloat16).astype(jnp.float32)
    middle = (kept - high).astype(jnp.bfloat16).astype(jnp.float32)
    low = kept - high - middle
    part = lane // 32
    return jnp.where(part == 0, high, jnp.where(part == 1, middle, low)).astype(jnp.bfloat16)


def joined_tile(tile):
    tile = tile.astype(jnp.float32)
    return tile + pltpu.roll(tile, 128 - 32, 1) + pltpu.roll(tile, 128 - 64, 1)


def slanted(base, rows):
    return pltpu.roll(jnp.broadcast_to(base, (rows, base.shape[1])), 0, 1, stride=1, stride_axis=0)


def local_forward(base, lengths, own, halos, heads, score_scale):
    rows, width = own.shape[0], own.shape[1] // 3
    head_dim = width // heads
    count = len(halos) + 1

    def begin(ins, outs, scratch):
        base_ref, lengths_ref, own_ref, *halo_refs = ins
        out_ref, log_ref = outs

        def run():
            first = lax.axis_index("mem") * rows
            same = same_book(lengths_ref, first, rows, first - (count - 1) * rows, count * rows)
            logs = []
            for head in range(heads):
                columns = slice(head * head_dim, (head + 1) * head_dim)
                above = slice(width + head * head_dim, width + (head + 1) * head_dim)
                twice = slice(2 * width + head * head_dim, 2 * width + (head + 1) * head_dim)
                keys = [ref[:, columns] for ref in halo_refs] + [own_ref[:, above]]
                values = [ref[:, above] for ref in halo_refs] + [own_ref[:, twice]]
                q = own_ref[:, columns]
                raw = [
                    lax.dot_general(q, k, contract_cols, preferred_element_type=jnp.float32) for k in keys
                ]
                bias = slanted(base_ref[head : head + 1, :], rows)[:, : count * rows]
                scores = jnp.concatenate(raw, axis=1) * score_scale + bias
                scores = jnp.where(same, scores, masked_score)
                top = jnp.max(scores, axis=1, keepdims=True)
                weights = jnp.exp(scores - top)
                total = jnp.sum(weights, axis=1, keepdims=True)
                weights = (weights / total).astype(jnp.bfloat16)
                out_ref[:, columns] = sum(
                    jnp.dot(
                        weights[:, i * rows : (i + 1) * rows], v, preferred_element_type=jnp.float32
                    )
                    for i, v in enumerate(values)
                )
                logs.append(top + jnp.log(total))
            log_ref[...] = lane_tile(logs, rows)

        return run

    arrays = [base, lengths, own, *halos]
    vmem = pl.BlockSpec(memory_space=pltpu.VMEM)
    specs = [vmem, pl.BlockSpec(memory_space=pltpu.SMEM)] + [vmem] * (1 + len(halos))
    out_shape = [
        jax.ShapeDtypeStruct((rows, width), jnp.float32),
        jax.ShapeDtypeStruct((rows, 128), jnp.float32),
    ]
    return arrays, specs, out_shape, [], begin


def local_queries(
    base, lengths, own, halos, d_mixed, local_out, local_log, share, heads, score_scale
):
    rows, width = d_mixed.shape
    head_dim = width // heads
    count = len(halos) + 1
    span = base.shape[1]

    def begin(ins, outs, scratch):
        base_ref, lengths_ref, own_ref, mix_ref, loc_ref, log_ref, share_ref, *halo_refs = ins
        dq_ref, diagonal_ref = outs

        def some_heads(some):
            first = lax.axis_index("mem") * rows
            same = same_book(lengths_ref, first, rows, first - (count - 1) * rows, count * rows)
            turned = (
                lax.broadcasted_iota(jnp.int32, (rows, rows), 0)
                + lax.broadcasted_iota(jnp.int32, (rows, rows), 1)
                == rows - 1
            ).astype(jnp.bfloat16)
            for head in some:
                columns = slice(head * head_dim, (head + 1) * head_dim)
                above = slice(width + head * head_dim, width + (head + 1) * head_dim)
                twice = slice(2 * width + head * head_dim, 2 * width + (head + 1) * head_dim)
                keys = [ref[:, columns] for ref in halo_refs] + [own_ref[:, above]]
                values = [ref[:, above] for ref in halo_refs] + [own_ref[:, twice]]
                q = own_ref[:, columns]
                d_out = ((1.0 - share_ref[head]) * mix_ref[:, columns]).astype(jnp.bfloat16)
                delta = jnp.sum(
                    d_out.astype(jnp.float32) * loc_ref[:, columns], axis=1, keepdims=True
                )
                raw = [
                    lax.dot_general(q, k, contract_cols, preferred_element_type=jnp.float32)
                    for k in keys
                ]
                bias = slanted(base_ref[head : head + 1, :], rows)[:, : count * rows]
                scores = jnp.concatenate(raw, axis=1) * score_scale + bias
                probs = jnp.exp(jnp.where(same, scores - log_ref[:, head : head + 1], masked_score))
                products = [
                    lax.dot_general(d_out, v, contract_cols, preferred_element_type=jnp.float32)
                    for v in values
                ]
                slopes = (probs * (jnp.concatenate(products, axis=1) - delta)).astype(jnp.bfloat16)
                slope_blocks = [slopes[:, i * rows : (i + 1) * rows] for i in range(count)]
                dq_ref[:, columns] = score_scale * sum(
                    jnp.dot(s, k, preferred_element_type=jnp.float32)
                    for s, k in zip(slope_blocks, keys)
                )
                mirrored = [
                    jnp.dot(s, turned, preferred_element_type=jnp.float32) for s in slope_blocks[::-1]
                ]
                mirrored.append(jnp.zeros((rows, span - count * rows), jnp.float32))
                leaned = pltpu.roll(jnp.concatenate(mirrored, axis=1), 0, 1, stride=1, stride_axis=0)
                diagonal_ref[head : head + 1, :] = jnp.sum(leaned, axis=0, keepdims=True)

        def run(part=0, parts=1):
            some_heads(range(part * heads // parts, (part + 1) * heads // parts))

        return run

    vmem = pl.BlockSpec(memory_space=pltpu.VMEM)
    smem = pl.BlockSpec(memory_space=pltpu.SMEM)
    arrays = [base, lengths, own, d_mixed, local_out, local_log, share, *halos]
    specs = [vmem, smem] + [vmem] * 4 + [smem] + [vmem] * len(halos)
    out_shape = [
        jax.ShapeDtypeStruct((rows, width), jnp.float32),
        jax.ShapeDtypeStruct((heads, span), jnp.float32),
    ]
    return arrays, specs, out_shape, [], begin


def local_keys(base, lengths, own, queries, sent, ratio, count, heads, score_scale):
    rows, width = own.shape[0], own.shape[1] // 3
    head_dim = width // heads
    groups = queries.shape[0] // rows

    def begin(ins, outs, scratch):
        base_ref, lengths_ref, own_ref, ratio_ref, queries_ref, sent_ref = ins
        (out_ref,) = outs
        queries_here, sent_here, sems = scratch
        copies = []
        for i in range(count):
            index = jnp.minimum(lax.axis_index("mem") + i, groups - 1)
            there = pl.ds(pl.multiple_of(index * rows, rows), rows)
            copies.append(
                pltpu.make_async_copy(queries_ref.at[there, :], queries_here.at[i], sems.at[0, i])
            )
            copies.append(pltpu.make_async_copy(sent_ref.at[there, :], sent_here.at[i], sems.at[1, i]))
        for copy in copies:
            copy.start()

        def run():
            for copy in copies:
                copy.wait()
            first = lax.axis_index("mem") * rows
            same = same_book(lengths_ref, first, rows, first, count * rows)
            stats = jnp.concatenate([joined_tile(sent_here[i, :, width:]).T for i in range(count)], axis=1)
            for head in range(heads):
                columns = slice(head * head_dim, (head + 1) * head_dim)
                above = slice(width + head * head_dim, width + (head + 1) * head_dim)
                twice = slice(2 * width + head * head_dim, 2 * width + (head + 1) * head_dim)
                k, v = own_ref[:, above], own_ref[:, twice]
                qs = [queries_here[i, :, columns] for i in range(count)]
                gs = [
                    (sent_here[i, :, columns].astype(jnp.float32) * ratio_ref[head]).astype(jnp.bfloat16)
                    for i in range(count)
                ]
                raw = [
                    lax.dot_general(k, q, contract_cols, preferred_element_type=jnp.float32) for q in qs
                ]
                bias = slanted(base_ref[head : head + 1, :], rows)[:, : count * rows]
                scores = jnp.concatenate(raw, axis=1) * score_scale + bias
                log = stats[2 * heads + head : 2 * heads + head + 1, :]
                delta = stats[3 * heads + head : 3 * heads + head + 1, :]
                probs = jnp.exp(jnp.where(same, scores - log, masked_score))
                products = [
                    lax.dot_general(v, g, contract_cols, preferred_element_type=jnp.float32) for g in gs
                ]
                slopes = (probs * (jnp.concatenate(products, axis=1) - delta)).astype(jnp.bfloat16)
                weights = probs.astype(jnp.bfloat16)
                blocks = [slice(i * rows, (i + 1) * rows) for i in range(count)]
                d_key = sum(
                    jnp.dot(slopes[:, b], q, preferred_element_type=jnp.float32) for b, q in zip(blocks, qs)
                )
                d_value = sum(
                    jnp.dot(weights[:, b], g, preferred_element_type=jnp.float32)
                    for b, g in zip(blocks, gs)
                )
                out_ref[:, above] = (d_key * score_scale).astype(jnp.bfloat16)
                out_ref[:, twice] = d_value.astype(jnp.bfloat16)

        return run

    vmem, anywhere = pl.BlockSpec(memory_space=pltpu.VMEM), pl.BlockSpec(memory_space=pl.ANY)
    smem = pl.BlockSpec(memory_space=pltpu.SMEM)
    arrays = [base, lengths, own, ratio, queries, sent]
    specs = [vmem, smem, vmem, smem, anywhere, anywhere]
    scratch = [
        pltpu.VMEM((count, rows, width), jnp.bfloat16),
        pltpu.VMEM((count, rows, width + 128), jnp.bfloat16),
        pltpu.SemaphoreType.DMA((2, count)),
    ]
    return arrays, specs, [jax.ShapeDtypeStruct((rows, 3 * width), jnp.bfloat16)], scratch, begin


def middle(
    tokens,
    memory_out,
    local_out,
    mem_log,
    local_log,
    share,
    out_weight,
    ffn_gain,
    up_weight,
    down_weight,
    cotangent,
    heads,
):
    rows, width = tokens.shape
    head_dim = width // heads
    hidden = up_weight.shape[1]
    block = math.gcd(hidden, 1024)
    steps = hidden // block

    def kernel(
        tokens_ref, mem_ref, loc_ref, mem_log_ref, log_ref, share_ref, out_w_ref, gain_ref, up_ref, down_ref, cot_ref, *refs
    ):
        mixed_ref, mid_ref, act_ref, d_up_ref, block_ref, d_res_ref, gain_part_ref, d_branch_ref, d_mix_ref = refs[:9]
        gate_ref, sent_ref, residual, branch_sum, d_mid_sum = refs[9:]
        i = pl.program_id(0)

        def scale_of(values):
            return lax.rsqrt(jnp.mean(values * values, axis=1, keepdims=True) + eps_norm)

        @pl.when(i == 0)
        def _():
            for head in range(heads):
                columns = slice(head * head_dim, (head + 1) * head_dim)
                part = share_ref[head]
                mixed_ref[:, columns] = (
                    part * mem_ref[:, columns] + (1.0 - part) * loc_ref[:, columns]
                ).astype(jnp.bfloat16)
            values = tokens_ref[...].astype(jnp.float32) + jnp.dot(
                mixed_ref[...], out_w_ref[...], preferred_element_type=jnp.float32
            )
            residual[...] = values
            mid_ref[...] = (values * scale_of(values) * gain_ref[...]).astype(jnp.bfloat16)
            branch_sum[...] = jnp.zeros_like(branch_sum)
            d_mid_sum[...] = jnp.zeros_like(d_mid_sum)

        up = jnp.dot(mid_ref[...], up_ref[...], preferred_element_type=jnp.float32)
        d_act = jnp.dot(cot_ref[...], down_ref[...], preferred_element_type=jnp.float32)
        below = 0.5 * (1.0 + lax.erf(up * math.sqrt(0.5)))
        density = jnp.exp(-0.5 * up * up) * (1.0 / math.sqrt(2.0 * math.pi))
        act = (up * below).astype(jnp.bfloat16)
        d_up = (d_act * (below + up * density)).astype(jnp.bfloat16)
        act_ref[...] = act
        d_up_ref[...] = d_up
        branch_sum[...] += lax.dot_general(
            act, down_ref[...], contract_cols, preferred_element_type=jnp.float32
        )
        d_mid_sum[...] += lax.dot_general(
            d_up, up_ref[...], contract_cols, preferred_element_type=jnp.float32
        )

        @pl.when(i == steps - 1)
        def _():
            values, d_mid = residual[...], d_mid_sum[...]
            block_ref[...] = (values + branch_sum[...]).astype(jnp.bfloat16)
            scale = scale_of(values)
            wanted = d_mid * gain_ref[...]
            slope = jnp.mean(values * wanted, axis=1, keepdims=True) * scale * scale * scale
            d_res = cot_ref[...].astype(jnp.float32) + scale * wanted - values * slope
            d_res_ref[...] = d_res
            gain_part_ref[...] = jnp.sum(d_mid * values * scale, axis=0, keepdims=True)
            d_branch_ref[...] = d_res.astype(jnp.bfloat16)
            d_mix_ref[...] = lax.dot_general(
                d_branch_ref[...], out_w_ref[...], contract_cols, preferred_element_type=jnp.float32
            )
            mem_deltas, deltas = [], []
            for head in range(heads):
                columns = slice(head * head_dim, (head + 1) * head_dim)
                part = share_ref[head]
                d_mix, mem_here, loc_here = d_mix_ref[:, columns], mem_ref[:, columns], loc_ref[:, columns]
                d_mem = (part * d_mix).astype(jnp.bfloat16)
                d_out = ((1.0 - part) * d_mix).astype(jnp.bfloat16)
                sent_ref[:, columns] = d_mem
                mem_deltas.append(
                    jnp.sum(d_mem.astype(jnp.float32) * mem_here, axis=1, keepdims=True)
                )
                deltas.append(jnp.sum(d_out.astype(jnp.float32) * loc_here, axis=1, keepdims=True))
                gate_ref[head : head + 1, :] = jnp.sum(
                    d_mix * (mem_here - loc_here), axis=0, keepdims=True
                )
            mem_logs = [mem_log_ref[:, head : head + 1] for head in range(heads)]
            logs = [log_ref[:, head : head + 1] for head in range(heads)]
            sent_ref[:, width:] = split_tile(lane_tile(mem_logs + mem_deltas + logs + deltas, rows))

    def whole(*shape):
        return pl.BlockSpec(shape, lambda i: (0, 0))

    weight = pl.BlockSpec((width, block), lambda i: (0, i))
    column = pl.BlockSpec((rows, block), lambda i: (0, i))
    full = whole(rows, width)
    low, high = jnp.bfloat16, jnp.float32
    outs = [
        (full, (rows, width), low),
        (full, (rows, width), low),
        (column, (rows, hidden), low),
        (column, (rows, hidden), low),
        (full, (rows, width), low),
        (full, (rows, width), high),
        (whole(1, width), (1, width), high),
        (full, (rows, width), low),
        (full, (rows, width), high),
        (whole(heads, head_dim), (heads, head_dim), high),
        (whole(rows, width + 128), (rows, width + 128), low),
    ]
    return pl.pallas_call(
        kernel,
        grid=(steps,),
        in_specs=[full, full, full, whole(rows, 128), whole(rows, 128)]
        + [pl.BlockSpec(memory_space=pltpu.SMEM)]
        + [whole(width, width), whole(1, width), weight, weight, full],
        out_specs=[spec for spec, _, _ in outs],
        out_shape=[jax.ShapeDtypeStruct(shape, dtype) for _, shape, dtype in outs],
        scratch_shapes=[pltpu.VMEM((rows, width), jnp.float32)] * 3,
        compiler_params=pltpu.CompilerParams(vmem_limit_bytes=VMEM_LIMIT),
        cost_estimate=lasting(18),
        name="middle",
    )(
        tokens,
        memory_out,
        local_out,
        mem_log,
        local_log,
        share,
        out_weight,
        ffn_gain[None, :],
        up_weight,
        down_weight,
        cotangent,
    )


def exchange_pairs(lefts, rights, other_lefts, other_right, send, recv):
    core = lax.axis_index("dp")
    copies, at = [], 0

    def push(source, target):
        i = len(copies)
        copy = pltpu.make_async_remote_copy(
            src_ref=source,
            dst_ref=target,
            send_sem=send.at[i],
            recv_sem=recv.at[i],
            device_id={"dp": 1 - core},
            device_id_type=pl.DeviceIdType.MESH,
        )
        copy.start()
        copies.append(copy)

    for i, (left, right) in enumerate(zip(lefts, rights)):
        half = right.shape[1] // 2
        push(left, other_lefts.at[i])
        there = pl.ds(pl.multiple_of((1 - core) * half, 128), half)
        push(right.at[:, there], other_right.at[:, pl.ds(at, half)])
        at += half
    return copies


def pair_products(lefts, rights, other_lefts, other_right, turned, store, copies):
    core = lax.axis_index("dp")
    rows = lefts[0].shape[0]
    at = 0
    for i, (left, right) in enumerate(zip(lefts, rights)):
        half = right.shape[1] // 2
        for copy in copies[2 * i : 2 * i + 2]:
            copy.wait_recv()
        turned[:, :rows] = left[...].T
        turned[:, rows:] = other_lefts[i].T
        block = math.gcd(half, 512)
        for column in range(0, half, block):
            kept = right[:, pl.ds(pl.multiple_of(core * half + column, 128), block)]
            both = jnp.concatenate([kept, other_right[:, at + column : at + column + block]], axis=0)
            store(
                at + column,
                jnp.dot(turned[...], both, preferred_element_type=jnp.float32).astype(jnp.bfloat16),
            )
        at += half


def pair_scratch(lefts, rights):
    rows, width = lefts[0].shape
    count = len(lefts)
    return [
        pltpu.VMEM((count, rows, width), jnp.bfloat16),
        pltpu.VMEM((rows, sum(right.shape[1] for right in rights) // 2), jnp.bfloat16),
        pltpu.VMEM((width, 2 * rows), jnp.bfloat16),
        pltpu.SemaphoreType.DMA((2 * count,)),
        pltpu.SemaphoreType.DMA((2 * count,)),
    ]


def pair_grads(lefts, rights, collective_id):
    count, width = len(lefts), lefts[0].shape[1]
    total = sum(right.shape[1] for right in rights) // 2
    block = math.gcd(*[right.shape[1] // 2 for right in rights], 512)

    def kernel(*refs):
        left_refs, right_refs, out_ref = refs[:count], refs[count : 2 * count], refs[2 * count]
        other_lefts, other_right, turned, send, recv, staged, out_sem = refs[2 * count + 1 :]
        barrier = pltpu.get_barrier_semaphore()
        partner = {"dp": 1 - lax.axis_index("dp")}
        pl.semaphore_signal(barrier, inc=1, device_id=partner, device_id_type=pl.DeviceIdType.MESH)
        pl.semaphore_wait(barrier, 1)
        copies = exchange_pairs(left_refs, right_refs, other_lefts, other_right, send, recv)
        written = []

        def store(column, value):
            slot = len(written) % 2
            if len(written) >= 2:
                written[-2].wait()
            staged[slot] = value
            copy = pltpu.make_async_copy(
                staged.at[slot], out_ref.at[:, pl.ds(column, block)], out_sem.at[slot]
            )
            copy.start()
            written.append(copy)

        pair_products(left_refs, right_refs, other_lefts, other_right, turned, store, copies)
        for copy in written[-2:]:
            copy.wait()
        for copy in copies:
            copy.wait_send()

    vmem = pl.BlockSpec(memory_space=pltpu.VMEM)
    return pl.pallas_call(
        kernel,
        in_specs=[vmem] * (2 * count),
        out_specs=pl.BlockSpec(memory_space=pl.ANY),
        out_shape=jax.ShapeDtypeStruct((width, total), jnp.bfloat16),
        scratch_shapes=pair_scratch(lefts, rights)
        + [pltpu.VMEM((2, width, block), jnp.bfloat16), pltpu.SemaphoreType.DMA((2,))],
        compiler_params=pltpu.CompilerParams(
            collective_id=collective_id, has_side_effects=True, vmem_limit_bytes=VMEM_LIMIT
        ),
        cost_estimate=lasting(10),
        name="pair_grads",
    )(*lefts, *rights)


def input_backward(tokens, attn_gain, d_projected, qkv_weight, d_residual):
    rows, width = tokens.shape

    def begin(ins, outs, scratch):
        tokens_ref, gain_ref, d_ref, weight_ref, residual_ref = ins
        grad_ref, part_ref = outs
        weight_here, sem = scratch
        copy = pltpu.make_async_copy(weight_ref, weight_here, sem)
        copy.start()

        def run():
            copy.wait()
            d_in = lax.dot_general(
                d_ref[...], weight_here[...], contract_cols, preferred_element_type=jnp.float32
            )
            x = tokens_ref[...].astype(jnp.float32)
            scale = lax.rsqrt(jnp.mean(x * x, axis=1, keepdims=True) + eps_norm)
            wanted = d_in * gain_ref[...]
            slope = jnp.mean(x * wanted, axis=1, keepdims=True) * scale * scale * scale
            grad_ref[...] = residual_ref[...] + scale * wanted - x * slope
            part_ref[...] = jnp.sum(d_in * x * scale, axis=0, keepdims=True)

        return run

    vmem = pl.BlockSpec(memory_space=pltpu.VMEM)
    arrays = [tokens, attn_gain[None, :], d_projected, qkv_weight, d_residual]
    specs = [vmem, vmem, vmem, pl.BlockSpec(memory_space=pl.ANY), vmem]
    out_shape = [
        jax.ShapeDtypeStruct((rows, width), jnp.float32),
        jax.ShapeDtypeStruct((1, width), jnp.float32),
    ]
    scratch = [pltpu.VMEM(qkv_weight.shape, qkv_weight.dtype), pltpu.SemaphoreType.DMA]
    return arrays, specs, out_shape, scratch, begin


def spread_halves(halves, outs):
    at = 0
    for out in outs:
        half = out.shape[1] // 2
        for c in (0, 1):
            out[:, c * half : (c + 1) * half] = halves[c, :, at : at + half].astype(jnp.float32)
        at += half


def join_halves(sums, collective_id):
    def kernel(sums_ref, both, send, recv):
        core = lax.axis_index("dp")
        partner = {"dp": 1 - core}
        barrier = pltpu.get_barrier_semaphore()
        pl.semaphore_signal(barrier, inc=1, device_id=partner, device_id_type=pl.DeviceIdType.MESH)
        pl.semaphore_wait(barrier, 1)
        copy = pltpu.make_async_remote_copy(
            src_ref=sums_ref,
            dst_ref=both.at[core],
            send_sem=send,
            recv_sem=recv,
            device_id=partner,
            device_id_type=pl.DeviceIdType.MESH,
        )
        copy.start()
        both[core] = sums_ref[...]
        copy.wait()

    vmem = pl.BlockSpec(memory_space=pltpu.VMEM)
    return pl.pallas_call(
        kernel,
        in_specs=[vmem],
        out_specs=vmem,
        out_shape=jax.ShapeDtypeStruct((2, *sums.shape), sums.dtype),
        scratch_shapes=[pltpu.SemaphoreType.DMA, pltpu.SemaphoreType.DMA],
        compiler_params=pltpu.CompilerParams(
            collective_id=collective_id, has_side_effects=True, vmem_limit_bytes=VMEM_LIMIT
        ),
        cost_estimate=lasting(4),
        name="join_halves",
    )(sums)


def write_results(late, late_widths, early, early_widths, small, heads, buckets):
    rows, width = late.shape[1], late.shape[2] * 2 // 3
    lines = width // 128
    count = len(late_widths) + len(early_widths)

    def kernel(late_ref, early_ref, small_ref, *outs):
        spread_halves(late_ref, outs[: len(late_widths)])
        spread_halves(early_ref, outs[len(late_widths) : count])
        attn_ref, ffn_ref, bias_ref, gate_ref = outs[count:]
        attn_ref[...] = small_ref[:lines, :]
        ffn_ref[...] = small_ref[lines : 2 * lines, :]
        for head in range(heads):
            line, lane = divmod(head * buckets, 128)
            here = small_ref[2 * lines + line : 2 * lines + line + 1, :]
            bias_ref[head : head + 1, :] = here[:, lane : lane + buckets]
        line = 2 * lines + heads * buckets // 128
        gate_ref[...] = small_ref[line : line + 1, :heads]

    shapes = [(rows, size) for size in [*late_widths, *early_widths]]
    shapes += [(lines, 128), (lines, 128), (heads, buckets), (1, heads)]
    return pl.pallas_call(
        kernel,
        out_shape=[jax.ShapeDtypeStruct(shape, jnp.float32) for shape in shapes],
        compiler_params=pltpu.CompilerParams(vmem_limit_bytes=VMEM_LIMIT),
        cost_estimate=lasting(3),
        name="write_results",
    )(late, early, small)


def finish_grads(lefts, rights, small, sources, collective_id, beside):
    width, total = lefts[0].shape[1], sum(right.shape[1] for right in rights) // 2
    rows = width // sources
    count = len(lefts)
    arrays, specs, more_out, more_scratch, begin = beside
    mesh_type = pl.DeviceIdType.MESH
    ref_shapes, sem_shapes = reduce_scratch(rows, total, jnp.bfloat16, sources)
    pair_shapes = pair_scratch(lefts, rights)
    sizes = [count, count, len(arrays), 1, 1, 1, len(more_out)]
    sizes += [len(ref_shapes), len(sem_shapes), len(pair_shapes), len(more_scratch), 8]

    def kernel(*refs):
        groups, at = [], 0
        for size in sizes:
            groups.append(refs[at : at + size])
            at += size
        left_refs, right_refs, ins, (small_ref,), (late,), (small_out,), more_refs = groups[:7]
        steps_refs, steps_sems, (other_lefts, other_right, turned, pair_send, pair_recv), scratch, own = groups[7:]
        parts, small_mine, smalls, core_small, small_send, small_recv, core_send, core_recv = own
        meanwhile = begin(ins, more_refs, scratch)
        me, core = lax.axis_index("mem"), lax.axis_index("dp")
        barrier = pltpu.get_barrier_semaphore()
        peers = [lax.rem(me + k, sources) for k in range(1, sources)]
        for peer in peers:
            pl.semaphore_signal(barrier, inc=1, device_id={"mem": peer}, device_id_type=mesh_type)
        pl.semaphore_signal(barrier, inc=1, device_id={"dp": 1 - core}, device_id_type=mesh_type)
        pl.semaphore_wait(barrier, sources)

        def merge(blocks):
            total = blocks[0][...].astype(jnp.float32)
            for block in blocks[1:]:
                total = total + block[...].astype(jnp.float32)
            return total

        def pack(target, total):
            target[...] = total.astype(jnp.bfloat16)

        def across_cores(source, target, i):
            copy = pltpu.make_async_remote_copy(
                src_ref=source,
                dst_ref=target,
                send_sem=core_send.at[i],
                recv_sem=core_recv.at[i],
                device_id={"dp": 1 - core},
                device_id_type=mesh_type,
            )
            copy.start()
            return copy

        pair_copies = exchange_pairs(
            left_refs, right_refs, other_lefts, other_right, pair_send, pair_recv
        )

        def store(column, value):
            parts[:, column : column + value.shape[1]] = value

        pair_products(
            left_refs, right_refs, other_lefts, other_right, turned, store, pair_copies
        )
        small_copies = [
            remote(small_mine, smalls.at[me], small_send.at[i], small_recv.at[me], peer)
            for i, peer in enumerate(peers)
        ]

        def between():
            meanwhile()
            small_mine[...] = small_ref[...]
            for i in range(width // 128):
                small_mine[i : i + 1, :] = more_refs[-1][:, i * 128 : (i + 1) * 128]
            smalls[me] = small_mine[...]
            for copy in small_copies:
                copy.start()

        final, still_open = reduce_steps(parts, sources, steps_refs, steps_sems, merge, pack, between)
        for here, blocks in final:
            late[core, here] = merge(blocks).astype(jnp.bfloat16)
        late_copy = across_cores(late.at[core], late.at[core], 0)
        for peer in peers:
            remote(
                smalls.at[peer], smalls.at[peer], small_send.at[0], small_recv.at[peer], peer
            ).wait_recv()
        group_small = smalls[0]
        for i in range(1, sources):
            group_small = group_small + smalls[i]
        core_small[0] = group_small
        small_copy = across_cores(core_small.at[0], core_small.at[1], 1)
        for copy in (late_copy, small_copy):
            copy.wait()
        small_out[...] = core_small[0] + core_small[1]
        for copy in still_open + small_copies + pair_copies:
            copy.wait_send()

    vmem = pl.BlockSpec(memory_space=pltpu.VMEM)
    return pl.pallas_call(
        kernel,
        in_specs=[vmem] * (2 * count) + specs + [vmem],
        out_specs=[vmem] * (2 + len(more_out)),
        out_shape=[jax.ShapeDtypeStruct((2, rows, total), jnp.bfloat16)]
        + [jax.ShapeDtypeStruct(small.shape, small.dtype)]
        + more_out,
        scratch_shapes=ref_shapes
        + sem_shapes
        + pair_shapes
        + more_scratch
        + [
            pltpu.VMEM((width, total), jnp.bfloat16),
            pltpu.VMEM(small.shape, small.dtype),
            pltpu.VMEM((sources, *small.shape), small.dtype),
            pltpu.VMEM((2, *small.shape), small.dtype),
        ]
        + [pltpu.SemaphoreType.DMA((sources,))] * 2
        + [pltpu.SemaphoreType.DMA((2,))] * 2,
        compiler_params=pltpu.CompilerParams(
            collective_id=collective_id, has_side_effects=True, vmem_limit_bytes=VMEM_LIMIT
        ),
        cost_estimate=lasting(45),
        name="finish_grads",
    )(*lefts, *rights, *arrays, small)


def on_device(
    tokens,
    attn_gain,
    qkv_weight,
    out_weight,
    bias_table,
    gate_logit,
    ffn_gain,
    up_weight,
    down_weight,
    memory_keys,
    memory_values,
    book_lengths,
    slot_shard,
    slot_index,
    slot_live,
    cotangent,
):
    rows, width = tokens.shape
    heads, buckets = bias_table.shape
    head_dim = width // heads
    top_count = slot_index.shape[2]
    hidden = up_weight.shape[1]
    groups = lax.axis_size("mem")
    capacity = -(-3 * rows * heads * top_count // (2 * groups) // 128) * 128
    score_scale = 1.0 / math.sqrt(head_dim)
    repeats = W // rows
    span = W + 2 * rows
    before = W - jnp.arange(span, dtype=jnp.int32)
    after = jnp.arange(span, dtype=jnp.int32)

    def bias_rows(offset):
        reached = (offset >= 0) & (offset < W)
        hot = (bucket_of(offset)[:, None] == jnp.arange(buckets, dtype=jnp.int32)) & reached[:, None]
        rows_of_bias = jnp.einsum(
            "rb,hb->hr", hot.astype(jnp.float32), bias_table, precision=lax.Precision.HIGHEST
        )
        return rows_of_bias + jnp.where(reached, 0.0, masked_score)

    before_bias, after_bias = bias_rows(before), bias_rows(after)
    bucket = bucket_of(jnp.arange(W, dtype=jnp.int32))
    one_hot = (bucket[:, None] == jnp.arange(buckets, dtype=jnp.int32)).astype(jnp.float32)
    tokens_f = tokens.astype(jnp.float32)
    normed_in = normed(tokens_f, attn_gain).astype(jnp.bfloat16)
    projected = jnp.dot(normed_in, qkv_weight, preferred_element_type=jnp.float32).astype(
        jnp.bfloat16
    )
    slots = memory_keys.shape[0]
    requests = place_requests(slot_shard, slot_index, slot_live, groups, capacity, slots)
    incoming = lax.all_to_all(requests, "mem", split_axis=0, concat_axis=0, tiled=True)
    index, row_ids, bounds = read_lists(incoming, heads, rows, slots)
    bounds = bounds.reshape(-1)
    key_rows, value_rows = gather_rows(
        index.reshape(-1), bounds, memory_keys, memory_values, heads, groups, capacity
    )
    keys_values, key_rows = lax.optimization_barrier((projected[:, width:], key_rows))
    halos = [passed_along(keys_values, "mem", distance) for distance in range(repeats, 0, -1)]
    all_queries = lax.all_gather(projected[:, :width], "mem", axis=0, tiled=True)
    local = local_forward(before_bias, book_lengths, projected, halos, heads, score_scale)
    partial = memory_forward(
        bounds,
        all_queries,
        key_rows,
        value_rows,
        row_ids,
        heads,
        groups,
        rows,
        score_scale,
    )
    if groups == 16:
        memory_out, mem_log, local_out, local_log = merge_partials(partial, groups, 1, heads, local)
    else:
        local_out, local_log = run_alone("local_forward", local)
        partial = lax.all_to_all(
            partial.reshape(groups, rows, width + 128),
            "mem",
            split_axis=0,
            concat_axis=0,
            tiled=True,
        ).reshape(groups * rows, width + 128)
        memory_out, mem_log = combine_partials(partial, heads, groups, rows)
    gate_share = jax.nn.sigmoid(gate_logit)
    (
        mixed_heads,
        normed_mid,
        activated,
        d_up,
        block_out,
        d_residual,
        ffn_gain_part,
        d_branch,
        d_mixed,
        gate_products,
        sent_grads,
    ) = middle(
        tokens,
        memory_out,
        local_out,
        mem_log,
        local_log,
        gate_share,
        out_weight,
        ffn_gain,
        up_weight,
        down_weight,
        cotangent,
        heads,
    )
    ffn_gain_part = ffn_gain_part.reshape(-1)
    early_halves = pair_grads(
        [mixed_heads, normed_mid, cotangent], [d_branch, d_up, activated], 5
    )
    early_sums = scattered(early_halves)
    sent_grads, _ = lax.optimization_barrier((sent_grads, early_halves))
    gate_part = jnp.sum(gate_products, axis=1) * gate_share * (1.0 - gate_share)
    local = local_queries(
        before_bias,
        book_lengths,
        projected,
        halos,
        d_mixed,
        local_out,
        local_log,
        gate_share,
        heads,
        score_scale,
    )
    if groups == 16:
        all_grads, d_queries, diagonals = gather_group(sent_grads, groups, 2, local)
    else:
        all_grads = lax.all_gather(sent_grads, "mem", axis=0, tiled=True)
        d_queries, diagonals = run_alone("local_queries", local)
    bias_part = jnp.dot(diagonals[:, rows - 1 : rows - 1 + W], one_hot, precision=lax.Precision.HIGHEST)
    d_partial = memory_backward(
        bounds,
        all_queries,
        all_grads,
        key_rows,
        value_rows,
        row_ids,
        heads,
        groups,
        rows,
        score_scale,
    )
    local = local_keys(
        after_bias,
        book_lengths,
        projected,
        all_queries,
        all_grads,
        (1.0 - gate_share) / gate_share,
        repeats + 1,
        heads,
        score_scale,
    )
    if groups == 16:
        d_projected = sum_queries(d_partial, d_queries, groups, 3, score_scale, local)
    else:
        (d_projected,) = run_alone("local_keys", local)
        d_partial, d_projected = lax.optimization_barrier((d_partial, d_projected))
        d_partial = jnp.sum(
            lax.all_to_all(
                d_partial.reshape(groups, rows, width), "mem", split_axis=0, concat_axis=0, tiled=True
            ).astype(jnp.float32),
            axis=0,
        )
        d_queries = (d_queries + d_partial * score_scale).astype(jnp.bfloat16)
        d_projected = jnp.concatenate([d_queries, d_projected[:, width:]], axis=1)
    beside = input_backward(tokens, attn_gain, d_projected, qkv_weight, d_residual)
    small = jnp.concatenate([ffn_gain_part, bias_part.reshape(-1), gate_part], axis=0)
    small = jnp.pad(small, (width, -small.shape[0] % 1024)).reshape(-1, 128)
    early_widths = [width, hidden, hidden]
    if groups == 16:
        late_both, small, tokens_grad, _ = finish_grads(
            [normed_in], [d_projected], small, groups, 4, beside
        )
        early_sums, small = lax.optimization_barrier((early_sums, small))
        early_both = join_halves(early_sums, 7)
    else:
        tokens_grad, attn_gain_part = run_alone("input_backward", beside)
        late_halves = pair_grads([normed_in], [d_projected], 6)
        late_halves, early_sums = lax.optimization_barrier((late_halves, early_sums))
        late_both = lax.all_gather(scattered(late_halves), "dp", axis=0)
        early_both = lax.all_gather(early_sums, "dp", axis=0)
        small = lax.psum(small.at[: width // 128].set(attn_gain_part.reshape(-1, 128)), ("dp", "mem"))
    qkv_grad, out_grad, up_grad, down_grad, attn_sum, ffn_sum, bias_sum, gate_sum = write_results(
        late_both, [3 * width], early_both, early_widths, small, heads, buckets
    )
    return (
        block_out,
        tokens_grad,
        qkv_grad,
        out_grad,
        up_grad,
        down_grad,
        attn_sum.reshape(-1),
        ffn_sum.reshape(-1),
        bias_sum,
        gate_sum.reshape(-1),
    )


def solution(mesh):
    in_specs = (
        P(("dp", "mem"), None),
        P(),
        P(),
        P(),
        P(),
        P(),
        P(),
        P(),
        P(),
        P("mem", None),
        P("mem", None),
        P("dp", None),
        P(("dp", "mem"), None, None, None),
        P(("dp", "mem"), None, None),
        P(("dp", "mem"), None, None),
        P(("dp", "mem"), None),
    )
    out_specs = (
        P(("dp", "mem"), None),
        P(("dp", "mem"), None),
        P("mem", None),
        P("mem", None),
        P("mem", None),
        P("mem", None),
        P(),
        P(),
        P(),
        P(),
    )
    return jax.shard_map(
        on_device, mesh=mesh, in_specs=in_specs, out_specs=out_specs, check_vma=False
    )
```

```python
import math

import jax
import jax.numpy as jnp
from jax import lax
from jax.experimental import pallas as pl
from jax.experimental.pallas import tpu as pltpu
from jax.sharding import PartitionSpec as P

W = 512
VMEM_LIMIT = 56 * 1024 * 1024


eps_norm = 1e-06
bucket_edges = tuple((math.ceil(16 * 8 ** (edge_step / 16)) for edge_step in range(1, 16)))
masked_score = -1e30
dead_score = -10000.0
contract_rows = (((0,), (0,)), ((), ()))
contract_cols = (((1,), (1,)), ((), ()))


def passed_along(value, axis, by):
    size = lax.axis_size(axis)
    pairs = [(i, i + by) for i in range(size) if 0 <= i + by < size]
    return lax.ppermute(value, axis, pairs)


def bucket_of(offset):
    past_edges = sum(((offset >= edge_pos).astype(jnp.int32) for edge_pos in bucket_edges))
    return jnp.where(offset < 16, offset, 16 + past_edges)


def normed(values, gain_vec):
    return (
        values * lax.rsqrt(jnp.mean(values * values, axis=-1, keepdims=True) + eps_norm) * gain_vec
    )


def place_requests(slot_shard, slot_index, slot_live, owners, capacity, slots):
    rows, heads, top_count = slot_index.shape
    entries, empty = rows * heads * top_count, heads * rows * slots
    if (owners + 1) * empty >= 2**31:
        raise ValueError("codes exceed int32")
    row_of = (
        jnp.arange(heads, dtype=jnp.int32)[None, :] * rows
        + jnp.arange(rows, dtype=jnp.int32)[:, None]
    )
    owner = jnp.where(slot_live > 0, slot_shard[..., 0], owners)
    codes = owner * empty + row_of[:, :, None] * slots + slot_index
    codes = lax.sort(codes.reshape(-1), is_stable=False)
    ends = jnp.sum(
        (codes[None, :] < (jnp.arange(owners, dtype=jnp.int32) + 1)[:, None] * empty).astype(jnp.int32),
        axis=1,
    )
    starts = jnp.concatenate([jnp.zeros((1,), jnp.int32), ends[:-1]])
    tall = -(-entries // 128)
    codes = jnp.pad(codes, (0, tall * 128 - entries)).reshape(tall, 128)
    long = capacity // 128

    def kernel(starts_ref, ends_ref, codes_ref, lists_ref, padded):
        padded[:tall, :] = codes_ref[...]
        padded[tall:, :] = jnp.zeros((long + 8, 128), jnp.int32)
        lane = lax.broadcasted_iota(jnp.int32, (long, 128), 1)
        place = lax.broadcasted_iota(jnp.int32, (long, 128), 0) * 128 + lane

        @pl.loop(0, owners)
        def _(i):
            start, end = starts_ref[i], ends_ref[i]
            shift = start % 128
            lines = padded[pl.ds(start // 128, long + 1), :]
            turned = pltpu.roll(lines, (128 - shift) % 128, 1)
            joined = jnp.where(lane < 128 - shift, turned[:long], turned[1:])
            lists_ref[i] = jnp.where(place < end - start, joined - i * empty, empty)

    return pl.pallas_call(
        kernel,
        in_specs=[pl.BlockSpec(memory_space=pltpu.SMEM)] * 2 + [pl.BlockSpec(memory_space=pltpu.VMEM)],
        out_shape=jax.ShapeDtypeStruct((owners, long, 128), jnp.int32),
        scratch_shapes=[pltpu.VMEM((tall + long + 8, 128), jnp.int32)],
        cost_estimate=lasting(3),
        name="make_lists",
    )(starts, ends, codes)


def read_lists(incoming, heads, rows, slots):
    sources, long, _ = incoming.shape

    def kernel(lists_ref, index_ref, ids_ref, bounds_ref):
        lane = lax.broadcasted_iota(jnp.int32, (1, 128), 1)

        def read(source):
            codes = lists_ref[source]
            ids = lax.div(codes, slots)
            index = lax.div(ids, rows) * slots + lax.rem(codes, slots)
            index_ref[source] = jnp.where(ids < heads * rows, index, 0)
            ids_ref[source, :long, :] = ids
            ids_ref[source, long:, :] = jnp.full((1, 128), heads * rows, jnp.int32)
            bounds = jnp.zeros((1, 128), jnp.int32)
            for head in range(1, heads + 1):
                below = jnp.sum(
                    jnp.where(codes < head * rows * slots, 1.0, 0.0), axis=0, keepdims=True
                )
                below = jnp.sum(below, axis=1, keepdims=True).astype(jnp.int32)
                bounds = jnp.where(lane == head, below, bounds)
            bounds_ref[pl.ds(source, 1), :] = bounds

        if sources > 16:
            pl.loop(0, sources)(read)
        else:
            for source in range(sources):
                read(source)

    return pl.pallas_call(
        kernel,
        out_shape=[
            jax.ShapeDtypeStruct((sources, long, 128), jnp.int32),
            jax.ShapeDtypeStruct((sources, long + 1, 128), jnp.int32),
            jax.ShapeDtypeStruct((sources, 128), jnp.int32),
        ],
        cost_estimate=lasting(3),
        name="read_lists",
    )(incoming)


def gather_rows(index, bounds, memory_keys, memory_values, heads, sources, capacity):
    slots, width = memory_keys.shape
    head_dim = width // heads
    step, part = 128, 16

    def kernel(index_ref, bounds_ref, keys, values, out_keys, out_values, key_table, value_table, key_rows, value_rows):
        i = pl.program_id(0)

        @pl.when(i < heads)
        def _():
            place = pl.ds(pl.multiple_of(i * slots, slots), slots)
            key_table[place, :] = keys[...].astype(jnp.float32)
            value_table[place, :] = values[...].astype(jnp.float32)

        @pl.when(i >= heads)
        def _():
            source = i - heads

            used = (bounds_ref[source * 128 + heads] + step - 1) // step

            def store(group):
                for at in range(0, step, part):
                    here = pl.ds(pl.multiple_of(group * step, step) + at, part)
                    out_keys[here, :] = key_rows[at : at + part, :].astype(jnp.bfloat16)
                    out_values[here, :] = value_rows[at : at + part, :].astype(jnp.bfloat16)

            @pl.loop(0, used)
            def _(group):
                store(jnp.maximum(group - 1, 0))
                first = source * capacity + group * step
                for u in range(step):
                    row = index_ref[first + u]
                    key_rows[u : u + 1, :] = key_table[pl.ds(row, 1), :]
                    value_rows[u : u + 1, :] = value_table[pl.ds(row, 1), :]

            pl.when(used > 0)(lambda: store(used - 1))

            @pl.loop(used, capacity // step)
            def _(group):
                here = pl.ds(pl.multiple_of(group * step, step), step)
                out_keys[here, :] = jnp.zeros((step, head_dim), jnp.bfloat16)
                out_values[here, :] = jnp.zeros((step, head_dim), jnp.bfloat16)

    table_spec = pl.BlockSpec((slots, head_dim), lambda i, *_: (0, jnp.minimum(i, heads - 1)))
    out_spec = pl.BlockSpec((capacity, head_dim), lambda i, *_: (jnp.maximum(i - heads, 0), 0))
    out_shape = jax.ShapeDtypeStruct((sources * capacity, head_dim), jnp.bfloat16)
    return pl.pallas_call(
        kernel,
        grid_spec=pltpu.PrefetchScalarGridSpec(
            num_scalar_prefetch=2,
            grid=(heads + sources,),
            in_specs=[table_spec, table_spec],
            out_specs=[out_spec, out_spec],
            scratch_shapes=[
                pltpu.VMEM((heads * slots, head_dim), jnp.float32),
                pltpu.VMEM((heads * slots, head_dim), jnp.float32),
                pltpu.VMEM((step, head_dim), jnp.float32),
                pltpu.VMEM((step, head_dim), jnp.float32),
            ],
        ),
        out_shape=[out_shape, out_shape],
        compiler_params=pltpu.CompilerParams(vmem_limit_bytes=VMEM_LIMIT),
        cost_estimate=lasting(42),
        name="gather_rows",
    )(index, bounds, memory_keys, memory_values)


def lasting(microseconds):
    return pl.CostEstimate(flops=0, bytes_accessed=3_000_000 * microseconds, transcendentals=0)


def triple(stat):
    part = lax.broadcasted_iota(jnp.int32, stat.shape, 1) // 16
    high = stat.astype(jnp.bfloat16).astype(jnp.float32)
    rest = stat - high
    middle = rest.astype(jnp.bfloat16).astype(jnp.float32)
    low = rest - middle
    chosen = jnp.where(part == 0, high, jnp.where(part == 1, middle, jnp.where(part == 2, low, 0.0)))
    return chosen.astype(jnp.bfloat16)


def window_of(bounds, source, head, heads, span, capacity):
    first, last = bounds[source * 128 + head], bounds[source * 128 + head + 1]
    start = jnp.minimum(first // 16 * 16, capacity - span)
    extra = jnp.maximum(last - start - 1, 0) // span
    return start, extra


def columns_of(head, head_dim):
    if isinstance(head, int):
        return slice(head * head_dim, (head + 1) * head_dim)
    return pl.ds(pl.multiple_of(head * head_dim, head_dim), head_dim)


def window_ids(id_ref, start, span):
    lines = id_ref[0, pl.ds(start // 128, span // 128 + 1), :]
    shift = start % 128
    turned = pltpu.roll(lines, (128 - shift) % 128, 1)
    lane = lax.broadcasted_iota(jnp.int32, (span // 128, 128), 1)
    return jnp.where(lane < 128 - shift, turned[:-1], turned[1:])


def owned(lines, first_row, count, start, least):
    row = lax.broadcasted_iota(jnp.int32, (count, 128), 0) + first_row
    masks = []
    for i in range(lines.shape[0]):
        mask = lines[i : i + 1, :] == row
        if least is not None:
            place = lax.broadcasted_iota(jnp.int32, (1, 128), 1) + start + i * 128
            mask = mask & (place >= least)
        masks.append(mask)
    return jnp.concatenate(masks, axis=1)


def memory_forward(bounds, queries, key_rows, value_rows, row_ids, heads, sources, rows, score_scale):
    capacity, head_dim = key_rows.shape[0] // sources, key_rows.shape[1]
    width = heads * head_dim
    span = min(384, capacity)
    chunk = math.gcd(rows, 32)

    def kernel(bounds_ref, q_ref, k_ref, v_ref, id_ref, out_ref, sums, tops, totals, raw, weights):
        source = pl.program_id(0)
        lane = lax.broadcasted_iota(jnp.int32, (chunk, 128), 1) % 16

        def window(heads_here, starts, least):
            here = [pl.ds(pl.multiple_of(start, 16), span) for start in starts]
            columns = [columns_of(head, head_dim) for head in heads_here]
            for slot in range(len(starts)):
                raw[slot] = lax.dot_general(
                    q_ref[:, columns[slot]],
                    k_ref[here[slot], :],
                    contract_cols,
                    preferred_element_type=jnp.float32,
                )
            for slot, (head, start) in enumerate(zip(heads_here, starts)):
                lines = window_ids(id_ref, start, span)
                for at in range(0, rows, chunk):
                    some = slice(at, at + chunk)
                    mine = owned(lines, head * rows + at, chunk, start, least)
                    scores = jnp.where(mine, raw[slot, some, :], masked_score)
                    top = jnp.maximum(jnp.max(scores, axis=1, keepdims=True), 0.1 * masked_score)
                    if least is not None:
                        old_top = jnp.max(
                            jnp.where(lane == head, tops[some, :], masked_score), axis=1, keepdims=True
                        )
                        top = jnp.maximum(top, old_top)
                    exps = jnp.exp((scores - top) * score_scale)
                    weights[slot, some, :] = exps.astype(jnp.bfloat16)
                    total = jnp.sum(exps, axis=1, keepdims=True)
                    if least is not None:
                        faded = jnp.exp((old_top - top) * score_scale)
                        sums[some, columns[slot]] = sums[some, columns[slot]] * faded
                        total = total + totals[some, :] * faded
                    tops[some, :] = jnp.where(lane == head, top, tops[some, :])
                    totals[some, :] = jnp.where(lane == heads + head, total, totals[some, :])
            for slot in range(len(starts)):
                found = jnp.dot(
                    weights[slot], v_ref[here[slot], :], preferred_element_type=jnp.float32
                )
                sums[:, columns[slot]] = found if least is None else sums[:, columns[slot]] + found

        tops[...] = jnp.zeros_like(tops)
        totals[...] = jnp.zeros_like(totals)

        windows = [window_of(bounds_ref, source, head, heads, span, capacity) for head in range(heads)]
        window(list(range(heads)), [start for start, _ in windows], None)

        @pl.when(sum(extra for _, extra in windows) > 0)
        def _():
            @pl.loop(0, heads)
            def _(head):
                start, extra = window_of(bounds_ref, source, head, heads, span, capacity)

                @pl.loop(0, extra)
                def _(turn):
                    least = start + (turn + 1) * span
                    window([head], [jnp.minimum(least, capacity - span)], least)

        out_ref[:, :width] = sums[...].astype(jnp.bfloat16)
        wide = lax.broadcasted_iota(jnp.int32, (rows, 128), 1) % 16
        out_ref[:, width:] = triple(jnp.where(wide < heads, tops[...] * score_scale, totals[...]))

    return pl.pallas_call(
        kernel,
        grid_spec=pltpu.PrefetchScalarGridSpec(
            num_scalar_prefetch=1,
            grid=(sources,),
            in_specs=[
                pl.BlockSpec((rows, width), lambda i, *_: (i, 0)),
                pl.BlockSpec((capacity, head_dim), lambda i, *_: (i, 0)),
                pl.BlockSpec((capacity, head_dim), lambda i, *_: (i, 0)),
                pl.BlockSpec((1, *row_ids.shape[1:]), lambda i, *_: (i, 0, 0)),
            ],
            out_specs=pl.BlockSpec((rows, width + 128), lambda i, *_: (i, 0)),
            scratch_shapes=[
                pltpu.VMEM((rows, width), jnp.float32),
                pltpu.VMEM((rows, 128), jnp.float32),
                pltpu.VMEM((rows, 128), jnp.float32),
                pltpu.VMEM((heads, rows, span), jnp.float32),
                pltpu.VMEM((heads, rows, span), jnp.bfloat16),
            ],
        ),
        out_shape=jax.ShapeDtypeStruct((sources * rows, width + 128), jnp.bfloat16),
        compiler_params=pltpu.CompilerParams(vmem_limit_bytes=VMEM_LIMIT),
        cost_estimate=lasting(25),
        name="memory_forward",
    )(bounds, queries, key_rows, value_rows, row_ids)


def combine_partials(partial, heads, sources, rows):
    width = partial.shape[1] - 128
    head_dim = width // heads

    def kernel(part_ref, out_ref, log_ref, sums, tops, totals):
        i = pl.program_id(0)

        @pl.when(i == 0)
        def _():
            sums[...] = jnp.zeros_like(sums)
            tops[...] = jnp.full_like(tops, masked_score)
            totals[...] = jnp.zeros_like(totals)

        stat = part_ref[:, width:].astype(jnp.float32)
        stat = stat + pltpu.roll(stat, 128 - 16, 1) + pltpu.roll(stat, 128 - 32, 1)
        new_total = pltpu.roll(stat, 128 - heads, 1)
        top = jnp.maximum(tops[...], stat)
        old_fade, new_fade = jnp.exp(tops[...] - top), jnp.exp(stat - top)
        tops[...] = top
        totals[...] = totals[...] * old_fade + new_total * new_fade
        for head in range(heads):
            columns = slice(head * head_dim, (head + 1) * head_dim)
            sums[:, columns] = (
                sums[:, columns] * old_fade[:, head : head + 1]
                + part_ref[:, columns].astype(jnp.float32) * new_fade[:, head : head + 1]
            )

        @pl.when(i == sources - 1)
        def _():
            live = totals[...] > 0
            total = jnp.where(live, totals[...], 1.0)
            log_ref[...] = jnp.where(live, tops[...] + jnp.log(total), 0.0)
            for head in range(heads):
                columns = slice(head * head_dim, (head + 1) * head_dim)
                out_ref[:, columns] = sums[:, columns] / total[:, head : head + 1]

    return pl.pallas_call(
        kernel,
        grid=(sources,),
        in_specs=[pl.BlockSpec((rows, width + 128), lambda i: (i, 0))],
        out_specs=[
            pl.BlockSpec((rows, width), lambda i: (0, 0)),
            pl.BlockSpec((rows, 128), lambda i: (0, 0)),
        ],
        scratch_shapes=[
            pltpu.VMEM((rows, width), jnp.float32),
            pltpu.VMEM((rows, 128), jnp.float32),
            pltpu.VMEM((rows, 128), jnp.float32),
        ],
        out_shape=[
            jax.ShapeDtypeStruct((rows, width), jnp.float32),
            jax.ShapeDtypeStruct((rows, 128), jnp.float32),
        ],
        compiler_params=pltpu.CompilerParams(vmem_limit_bytes=VMEM_LIMIT),
        cost_estimate=lasting(13),
        name="combine_partials",
    )(partial)


def memory_backward(bounds, queries, grads, key_rows, value_rows, row_ids, heads, sources, rows, score_scale):
    capacity, head_dim = key_rows.shape[0] // sources, key_rows.shape[1]
    width = heads * head_dim
    span = min(384, capacity)
    chunk = math.gcd(rows, 32)

    def kernel(bounds_ref, q_ref, g_ref, k_ref, v_ref, id_ref, out_ref, sums, stats, raw, products, slopes):
        source = pl.program_id(0)
        stats[...] = joined_tile(g_ref[:, width : width + 128])

        def window(heads_here, starts, least):
            here = [pl.ds(pl.multiple_of(start, 16), span) for start in starts]
            columns = [columns_of(head, head_dim) for head in heads_here]
            for slot in range(len(starts)):
                raw[slot] = lax.dot_general(
                    q_ref[:, columns[slot]],
                    k_ref[here[slot], :],
                    contract_cols,
                    preferred_element_type=jnp.float32,
                )
                products[slot] = lax.dot_general(
                    g_ref[:, columns[slot]],
                    v_ref[here[slot], :],
                    contract_cols,
                    preferred_element_type=jnp.float32,
                )
            for slot, (head, start) in enumerate(zip(heads_here, starts)):
                lines = window_ids(id_ref, start, span)
                turned = stats[...]
                if least is not None:
                    turned = pltpu.roll(turned, 128 - head, 1)
                elif head:
                    turned = turned[:, head:]
                for at in range(0, rows, chunk):
                    some = slice(at, at + chunk)
                    mine = owned(lines, head * rows + at, chunk, start, least)
                    log, delta = turned[some, :1], turned[some, heads : heads + 1]
                    probs = jnp.exp(jnp.where(mine, raw[slot, some, :] * score_scale - log, dead_score))
                    slopes[slot, some, :] = (probs * (products[slot, some, :] - delta)).astype(
                        jnp.bfloat16
                    )
            for slot in range(len(starts)):
                found = jnp.dot(
                    slopes[slot], k_ref[here[slot], :], preferred_element_type=jnp.float32
                )
                sums[:, columns[slot]] = found if least is None else sums[:, columns[slot]] + found

        windows = [window_of(bounds_ref, source, head, heads, span, capacity) for head in range(heads)]
        window(list(range(heads)), [start for start, _ in windows], None)

        @pl.when(sum(extra for _, extra in windows) > 0)
        def _():
            @pl.loop(0, heads)
            def _(head):
                start, extra = window_of(bounds_ref, source, head, heads, span, capacity)

                @pl.loop(0, extra)
                def _(turn):
                    least = start + (turn + 1) * span
                    window([head], [jnp.minimum(least, capacity - span)], least)

        out_ref[...] = sums[...].astype(jnp.bfloat16)

    return pl.pallas_call(
        kernel,
        grid_spec=pltpu.PrefetchScalarGridSpec(
            num_scalar_prefetch=1,
            grid=(sources,),
            in_specs=[
                pl.BlockSpec((rows, width), lambda i, *_: (i, 0)),
                pl.BlockSpec((rows, width + 128), lambda i, *_: (i, 0)),
                pl.BlockSpec((capacity, head_dim), lambda i, *_: (i, 0)),
                pl.BlockSpec((capacity, head_dim), lambda i, *_: (i, 0)),
                pl.BlockSpec((1, *row_ids.shape[1:]), lambda i, *_: (i, 0, 0)),
            ],
            out_specs=pl.BlockSpec((rows, width), lambda i, *_: (i, 0)),
            scratch_shapes=[
                pltpu.VMEM((rows, width), jnp.float32),
                pltpu.VMEM((rows, 128), jnp.float32),
                pltpu.VMEM((heads, rows, span), jnp.float32),
                pltpu.VMEM((heads, rows, span), jnp.float32),
                pltpu.VMEM((heads, rows, span), jnp.bfloat16),
            ],
        ),
        out_shape=jax.ShapeDtypeStruct((sources * rows, width), jnp.bfloat16),
        compiler_params=pltpu.CompilerParams(vmem_limit_bytes=VMEM_LIMIT),
        cost_estimate=lasting(25),
        name="memory_backward",
    )(bounds, queries, grads, key_rows, value_rows, row_ids)


def remote(source, target, send_sem, recv_sem, device):
    return pltpu.make_async_remote_copy(
        src_ref=source,
        dst_ref=target,
        send_sem=send_sem,
        recv_sem=recv_sem,
        device_id={"mem": device},
        device_id_type=pl.DeviceIdType.MESH,
    )


def grid_place(depth):
    me = lax.axis_index("mem")
    layer, column = me // 4, me % 4
    beside_x = column + 1 - 2 * (column % 2)
    beside_y = column + 2 - 4 * (column // 2)
    across = 3 - column

    def index_of(step, place):
        return (layer + step + depth) % depth * 4 + place

    return me, column, beside_x, beside_y, across, index_of


def greet(devices):
    barrier = pltpu.get_barrier_semaphore()
    for device in devices:
        pl.semaphore_signal(
            barrier, inc=1, device_id={"mem": device}, device_id_type=pl.DeviceIdType.MESH
        )
    pl.semaphore_wait(barrier, len(devices))


def gather_group(block, sources, collective_id, beside):
    rows, width = block.shape
    depth, half = sources // 4, rows // 2
    slots = 2 * depth - 1
    arrays, specs, more_out, more_scratch, begin = beside
    ins, outs = len(arrays), len(more_out)

    def kernel(x_ref, *refs):
        in_refs, (out_ref, *more_refs) = refs[:ins], refs[ins : ins + 1 + outs]
        (own_sem, send, recv), scratch = refs[ins + 1 + outs : ins + 4 + outs], refs[ins + 4 + outs :]
        meanwhile = begin(in_refs, more_refs, scratch)
        me = lax.axis_index("mem")
        layer, column = me // 4, me % 4
        to_x = me + 1 - 2 * (column % 2)
        to_y = me + 2 - 4 * (column // 2)
        across = layer * 4 + 3 - column
        has_above, has_below = layer + 1 < depth, layer > 0
        barrier = pltpu.get_barrier_semaphore()

        def signal(device):
            pl.semaphore_signal(
                barrier, inc=1, device_id={"mem": device}, device_id_type=pl.DeviceIdType.MESH
            )

        signal(to_x)
        signal(to_y)
        pl.when(has_above)(lambda: signal(me + 4))
        pl.when(has_below)(lambda: signal(me - 4))
        pl.semaphore_wait(barrier, 2 + has_above.astype(jnp.int32) + has_below.astype(jnp.int32))

        def part_of(index, part):
            start = pl.multiple_of(index * rows + part * half, half)
            return out_ref.at[pl.ds(start, half), :]

        own = pltpu.make_async_copy(x_ref, out_ref.at[pl.ds(pl.multiple_of(me * rows, rows), rows), :], own_sem)
        own.start()
        sent = []

        def push(condition, source, target, kind, slot, to_slot, part, device):
            copy = remote(source, target, send.at[kind, slot, part], recv.at[kind, to_slot, part], device)
            if condition is None:
                copy.start()
            else:
                pl.when(condition)(copy.start)
            sent.append((condition, copy))

        def arrived(index, kind, slot, part):
            target = part_of(index, part)
            remote(target, target, send.at[kind, slot, part], recv.at[kind, slot, part], to_x).wait_recv()

        def up_slot(distance):
            return distance

        def down_slot(distance):
            return depth - 1 + distance

        for part in (0, 1):
            mine = x_ref.at[pl.ds(part * half, half), :]
            push(has_above, mine, part_of(me, part), 0, 0, down_slot(1), part, me + 4)
            push(has_below, mine, part_of(me, part), 1, 0, up_slot(1), part, me - 4)
            mine_y = x_ref.at[pl.ds((1 - part) * half, half), :]
            push(None, mine, part_of(me, part), 2, 0, 0, part, to_x)
            push(None, mine_y, part_of(me, 1 - part), 3, 0, 0, 1 - part, to_y)

        def pass_on(condition, step, slot):
            def go():
                arrived(to_x + step, 2, slot, 0)
                copy_a.start()
                arrived(to_y + step, 3, slot, 1)
                copy_b.start()

            source_a, source_b = part_of(to_x + step, 0), part_of(to_y + step, 1)
            copy_a = remote(source_a, source_a, send.at[4, slot, 0], recv.at[4, slot, 0], to_y)
            copy_b = remote(source_b, source_b, send.at[5, slot, 1], recv.at[5, slot, 1], to_x)
            sent.append((condition, copy_a))
            sent.append((condition, copy_b))
            if condition is None:
                go()
            else:
                pl.when(condition)(go)

        for distance in range(1, depth):
            from_above, from_below = layer + distance < depth, layer - distance >= 0

            def take(kind, back_kind, step, slot, next_slot, onward, onward_device):
                for part in (0, 1):
                    arrived(me + step, kind, slot, part)
                    here = part_of(me + step, part)
                    if next_slot is not None:
                        pl.when(onward)(
                            remote(
                                here, here, send.at[kind, slot, part], recv.at[kind, next_slot, part], onward_device
                            ).start
                        )
                    remote(here, here, send.at[2, slot, part], recv.at[2, slot, part], to_x).start()
                    remote(here, here, send.at[3, slot, part], recv.at[3, slot, part], to_y).start()

            last = distance == depth - 1
            pl.when(from_above)(
                lambda: take(
                    1, 0, 4 * distance, up_slot(distance), None if last else up_slot(distance + 1), has_below, me - 4
                )
            )
            pl.when(from_below)(
                lambda: take(
                    0, 1, -4 * distance, down_slot(distance), None if last else down_slot(distance + 1), has_above, me + 4
                )
            )
            for condition, step, slot, kind, onward in (
                (from_above, 4 * distance, up_slot(distance), 1, has_below),
                (from_below, -4 * distance, down_slot(distance), 0, has_above),
            ):
                for part in (0, 1):
                    here = part_of(me + step, part)
                    if not last:
                        sent.append((condition & onward, remote(here, here, send.at[kind, slot, part], own_sem, me)))
                    sent.append((condition, remote(here, here, send.at[2, slot, part], own_sem, to_x)))
                    sent.append((condition, remote(here, here, send.at[3, slot, part], own_sem, to_y)))
            meanwhile(distance - 1, depth - 1)
            if distance == 1:
                pass_on(None, 0, 0)
            else:
                pass_on(layer + distance - 1 < depth, 4 * (distance - 1), up_slot(distance - 1))
                pass_on(layer - distance + 1 >= 0, -4 * (distance - 1), down_slot(distance - 1))
        pass_on(layer + depth - 1 < depth, 4 * (depth - 1), up_slot(depth - 1))
        pass_on(layer - depth + 1 >= 0, -4 * (depth - 1), down_slot(depth - 1))

        def close(step, slot):
            arrived(to_x + step, 2, slot, 1)
            arrived(to_y + step, 3, slot, 0)
            arrived(across + step, 4, slot, 0)
            arrived(across + step, 5, slot, 1)

        close(0, 0)
        for distance in range(1, depth):
            pl.when(layer + distance < depth)(lambda: close(4 * distance, up_slot(distance)))
            pl.when(layer - distance >= 0)(lambda: close(-4 * distance, down_slot(distance)))
        for condition, copy in sent:
            if condition is None:
                copy.wait_send()
            else:
                pl.when(condition)(copy.wait_send)
        own.wait()

    return pl.pallas_call(
        kernel,
        in_specs=[pl.BlockSpec(memory_space=pl.ANY), *specs],
        out_specs=[pl.BlockSpec(memory_space=pl.ANY)] + [pl.BlockSpec(memory_space=pltpu.VMEM)] * outs,
        out_shape=[jax.ShapeDtypeStruct((sources * rows, width), block.dtype), *more_out],
        scratch_shapes=[
            pltpu.SemaphoreType.DMA,
            pltpu.SemaphoreType.DMA((6, slots, 2)),
            pltpu.SemaphoreType.DMA((6, slots, 2)),
            *more_scratch,
        ],
        compiler_params=pltpu.CompilerParams(
            collective_id=collective_id, has_side_effects=True, vmem_limit_bytes=VMEM_LIMIT
        ),
        cost_estimate=lasting(50),
        name="gather_group",
    )(block, *arrays)


def reduce_steps(parts_ref, sources, refs, sems, merge, pack, beside=None):
    half_a, half_b, from_x, from_y, from_z, out_x, out_y, out_z = refs
    send, recv_a, recv_b, recv_x, recv_y, recv_z = sems
    rows = parts_ref.shape[0] // sources
    depth, half = sources // 4, rows // 2
    me, column, beside_x, beside_y, across, index_of = grid_place(depth)
    to_x, to_y = index_of(0, beside_x), index_of(0, beside_y)
    order = [*range(1, depth), 0]
    queues = {"x": [], "y": [], "z": []}
    first_limit = 2 if beside is None else depth

    def piece(index, part):
        return parts_ref.at[pl.ds(pl.multiple_of(index * rows + part * half, half), half), :]

    def part_rows(part):
        return pl.ds(part * half, half)

    def push(link, source, target, kind, k, recv_sem, device, limit=2):
        queue = queues[link]
        while link != "z" and len(queue) >= limit:
            queue.pop(0).wait_send()
        copy = remote(source, target, send.at[kind, k], recv_sem, device)
        copy.start()
        queue.append(copy)

    def arrived(target, recv_sem):
        remote(target, target, send.at[0, 0], recv_sem, to_x).wait_recv()

    def plane_rest(k):
        push("x", piece(index_of(k, beside_x), 0), from_x.at[k, part_rows(0)], 2, k, recv_x.at[0, k], to_x)
        push("y", piece(index_of(k, beside_y), 1), from_y.at[k, part_rows(1)], 3, k, recv_y.at[1, k], to_y)

    def plane_merged(k):
        arrived(half_a.at[k], recv_a.at[k])
        pack(out_y.at[k], merge([piece(index_of(k, beside_y), 0), half_a.at[k]]))
        push("y", out_y.at[k], from_y.at[k, part_rows(0)], 4, k, recv_y.at[0, k], to_y)
        arrived(half_b.at[k], recv_b.at[k])
        pack(out_x.at[k], merge([piece(index_of(k, beside_x), 1), half_b.at[k]]))
        push("x", out_x.at[k], from_x.at[k, part_rows(1)], 5, k, recv_x.at[1, k], to_x)

    def column_step(k):
        for part in (0, 1):
            here = part_rows(part)
            arrived(from_x.at[k, here], recv_x.at[part, k])
            arrived(from_y.at[k, here], recv_y.at[part, k])
            if k:
                blocks = [piece(index_of(k, column), part), from_x.at[k, here], from_y.at[k, here]]
                pack(out_z.at[k, here], merge(blocks))
        if k:
            push("z", out_z.at[k], from_z.at[k], 6, k, recv_z.at[k], index_of(k, column))

    for k in order:
        far = index_of(k, across)
        push("x", piece(far, 0), half_a.at[k], 0, k, recv_a.at[k], to_x, first_limit)
        push("y", piece(far, 1), half_b.at[k], 1, k, recv_b.at[k], to_y, first_limit)
    if beside is not None:
        beside()
    for i, k in enumerate(order):
        plane_rest(k)
        plane_merged(k)
        if i:
            column_step(order[i - 1])
    column_step(order[-1])
    for k in range(1, depth):
        arrived(from_z.at[k], recv_z.at[k])
    final = []
    for part in (0, 1):
        here = part_rows(part)
        blocks = [piece(me, part), from_x.at[0, here], from_y.at[0, here]]
        final.append((here, blocks + [from_z.at[k, here] for k in range(1, depth)]))
    return final, [copy for queue in queues.values() for copy in queue]


def reduce_scratch(rows, width, dtype, sources):
    depth, half = sources // 4, rows // 2

    def slots(size):
        return pltpu.VMEM((depth, size, width), dtype)

    refs = [slots(half), slots(half), slots(rows), slots(rows), slots(rows)]
    refs += [slots(half), slots(half), slots(rows)]
    sems = [pltpu.SemaphoreType.DMA((7, depth))]
    sems += [pltpu.SemaphoreType.DMA((depth,))] * 2
    sems += [pltpu.SemaphoreType.DMA((2, depth))] * 2
    sems += [pltpu.SemaphoreType.DMA((depth,))]
    return refs, sems


def run_alone(name, beside):
    arrays, specs, out_shape, scratch, begin = beside
    ins, outs = len(arrays), len(out_shape)

    def kernel(*refs):
        begin(refs[:ins], refs[ins : ins + outs], refs[ins + outs :])()

    return pl.pallas_call(
        kernel,
        in_specs=specs,
        out_specs=[pl.BlockSpec(memory_space=pltpu.VMEM)] * outs,
        out_shape=out_shape,
        scratch_shapes=scratch,
        compiler_params=pltpu.CompilerParams(vmem_limit_bytes=VMEM_LIMIT),
        cost_estimate=lasting(8),
        name=name,
    )(*arrays)


def reduce_group(parts, sources, collective_id, merge, pack, finish, out_shape, beside):
    rows, width = parts.shape[0] // sources, parts.shape[1]
    depth = sources // 4
    arrays, specs, more_out, more_scratch, begin = beside
    ref_shapes, sem_shapes = reduce_scratch(rows, width, parts.dtype, sources)
    sizes = [len(arrays), len(out_shape), len(more_out), len(ref_shapes), len(sem_shapes), len(more_scratch)]

    def kernel(parts_ref, *refs):
        groups, at = [], 0
        for size in sizes:
            groups.append(refs[at : at + size])
            at += size
        ins, out_refs, more_refs, steps_refs, steps_sems, scratch = groups
        meanwhile = begin(ins, more_refs, scratch)
        last = finish
        if finish is None:
            meanwhile, last = meanwhile
        me, column, beside_x, beside_y, across, index_of = grid_place(depth)
        greet(
            [index_of(0, beside_x), index_of(0, beside_y)]
            + [index_of(-k, column) for k in range(1, depth)]
        )
        final, still_open = reduce_steps(
            parts_ref, sources, steps_refs, steps_sems, merge, pack, meanwhile
        )
        for here, blocks in final:
            if finish is None:
                last(here, merge(blocks))
            else:
                last([out.at[here] for out in out_refs], merge(blocks))
        for copy in still_open:
            copy.wait_send()

    vmem = pl.BlockSpec(memory_space=pltpu.VMEM)
    return pl.pallas_call(
        kernel,
        in_specs=[vmem, *specs],
        out_specs=[vmem] * (len(out_shape) + len(more_out)),
        out_shape=[*out_shape, *more_out],
        scratch_shapes=[*ref_shapes, *sem_shapes, *more_scratch],
        compiler_params=pltpu.CompilerParams(
            collective_id=collective_id, has_side_effects=True, vmem_limit_bytes=VMEM_LIMIT
        ),
        cost_estimate=lasting(50),
        name="reduce_group",
    )(parts, *arrays)


def sum_queries(parts, d_queries, sources, collective_id, score_scale, beside):
    rows, width = d_queries.shape
    arrays, specs, (whole,), more_scratch, begin = beside

    def merge(blocks):
        total = blocks[0][...].astype(jnp.float32)
        for block in blocks[1:]:
            total = total + block[...].astype(jnp.float32)
        return total

    def pack(target, total):
        target[...] = total.astype(parts.dtype)

    def begin_both(ins, outs, scratch):
        run = begin(ins[:-1], outs, scratch)

        def finish(here, total):
            outs[0][here, :width] = (ins[-1][here, :] + total * score_scale).astype(whole.dtype)

        return run, finish

    more = [*arrays, d_queries], [*specs, pl.BlockSpec(memory_space=pltpu.VMEM)], [whole], more_scratch, begin_both
    return reduce_group(parts, sources, collective_id, merge, pack, None, [], more)[0]


def merge_partials(parts, sources, collective_id, heads, beside):
    rows, width = parts.shape[0] // sources, parts.shape[1] - 128
    head_dim = width // heads

    def merge(blocks):
        stats = []
        for block in blocks:
            stat = block[:, width:].astype(jnp.float32)
            stats.append(stat + pltpu.roll(stat, 128 - 16, 1) + pltpu.roll(stat, 128 - 32, 1))
        top = stats[0]
        for stat in stats[1:]:
            top = jnp.maximum(top, stat)
        fades = [jnp.exp(stat - top) for stat in stats]
        total = sum(fade * pltpu.roll(stat, 128 - heads, 1) for fade, stat in zip(fades, stats))
        sums = []
        for head in range(heads):
            columns = slice(head * head_dim, (head + 1) * head_dim)
            sums.append(
                sum(
                    block[:, columns].astype(jnp.float32) * fade[:, head : head + 1]
                    for block, fade in zip(blocks, fades)
                )
            )
        return sums, top, total

    def pack(target, merged):
        sums, top, total = merged
        for head in range(heads):
            target[:, head * head_dim : (head + 1) * head_dim] = sums[head].astype(parts.dtype)
        lane = lax.broadcasted_iota(jnp.int32, top.shape, 1)
        stat = jnp.where(lane < heads, top, jnp.where(lane < 16, pltpu.roll(total, heads, 1), 0.0))
        target[:, width:] = triple(stat + pltpu.roll(stat, 16, 1) + pltpu.roll(stat, 32, 1))

    def finish(targets, merged):
        sums, top, total = merged
        live = total > 0
        total = jnp.where(live, total, 1.0)
        targets[1][...] = jnp.where(live, top + jnp.log(total), 0.0)
        for head in range(heads):
            targets[0][:, head * head_dim : (head + 1) * head_dim] = sums[head] / total[:, head : head + 1]

    out_shape = [
        jax.ShapeDtypeStruct((rows, width), jnp.float32),
        jax.ShapeDtypeStruct((rows, 128), jnp.float32),
    ]
    return reduce_group(parts, sources, collective_id, merge, pack, finish, out_shape, beside)


def scattered(halves):
    return lax.psum_scatter(halves, "mem", scatter_dimension=0, tiled=True)


def same_book(lengths_ref, first_row, rows, first_lane, lanes):
    row = lax.broadcasted_iota(jnp.int32, (rows, lanes), 0) + first_row
    lane = lax.broadcasted_iota(jnp.int32, (rows, lanes), 1) + first_lane
    end, same = 0, lane >= 0
    for i in range(lengths_ref.shape[1]):
        end = end + lengths_ref[0, i]
        same = same & ((row >= end) == (lane >= end))
    return same


def lane_tile(columns, rows):
    lane = lax.broadcasted_iota(jnp.int32, (rows, 128), 1)
    tile = jnp.zeros((rows, 128), jnp.float32)
    for i, column in enumerate(columns):
        tile = jnp.where(lane == i, column, tile)
    return tile


def split_tile(tile):
    lane = lax.broadcasted_iota(jnp.int32, tile.shape, 1)
    kept = jnp.where(lane < 32, tile, 0.0)
    kept = kept + pltpu.roll(kept, 32, 1) + pltpu.roll(kept, 64, 1)
    high = kept.astype(jnp.bfloat16).astype(jnp.float32)
    middle = (kept - high).astype(jnp.bfloat16).astype(jnp.float32)
    low = kept - high - middle
    part = lane // 32
    return jnp.where(part == 0, high, jnp.where(part == 1, middle, low)).astype(jnp.bfloat16)


def joined_tile(tile):
    tile = tile.astype(jnp.float32)
    return tile + pltpu.roll(tile, 128 - 32, 1) + pltpu.roll(tile, 128 - 64, 1)


def slanted(base, rows):
    return pltpu.roll(jnp.broadcast_to(base, (rows, base.shape[1])), 0, 1, stride=1, stride_axis=0)


def local_forward(base, lengths, own, halos, heads, score_scale):
    rows, width = own.shape[0], own.shape[1] // 3
    head_dim = width // heads
    count = len(halos) + 1

    def begin(ins, outs, scratch):
        base_ref, lengths_ref, own_ref, *halo_refs = ins
        out_ref, log_ref = outs

        def run():
            first = lax.axis_index("mem") * rows
            same = same_book(lengths_ref, first, rows, first - (count - 1) * rows, count * rows)
            logs = []
            for head in range(heads):
                columns = slice(head * head_dim, (head + 1) * head_dim)
                above = slice(width + head * head_dim, width + (head + 1) * head_dim)
                twice = slice(2 * width + head * head_dim, 2 * width + (head + 1) * head_dim)
                keys = [ref[:, columns] for ref in halo_refs] + [own_ref[:, above]]
                values = [ref[:, above] for ref in halo_refs] + [own_ref[:, twice]]
                q = own_ref[:, columns]
                raw = [
                    lax.dot_general(q, k, contract_cols, preferred_element_type=jnp.float32) for k in keys
                ]
                bias = slanted(base_ref[head : head + 1, :], rows)[:, : count * rows]
                scores = jnp.concatenate(raw, axis=1) * score_scale + bias
                scores = jnp.where(same, scores, masked_score)
                top = jnp.max(scores, axis=1, keepdims=True)
                weights = jnp.exp(scores - top)
                total = jnp.sum(weights, axis=1, keepdims=True)
                weights = (weights / total).astype(jnp.bfloat16)
                out_ref[:, columns] = sum(
                    jnp.dot(
                        weights[:, i * rows : (i + 1) * rows], v, preferred_element_type=jnp.float32
                    )
                    for i, v in enumerate(values)
                )
                logs.append(top + jnp.log(total))
            log_ref[...] = lane_tile(logs, rows)

        return run

    arrays = [base, lengths, own, *halos]
    vmem = pl.BlockSpec(memory_space=pltpu.VMEM)
    specs = [vmem, pl.BlockSpec(memory_space=pltpu.SMEM)] + [vmem] * (1 + len(halos))
    out_shape = [
        jax.ShapeDtypeStruct((rows, width), jnp.float32),
        jax.ShapeDtypeStruct((rows, 128), jnp.float32),
    ]
    return arrays, specs, out_shape, [], begin


def local_queries(
    base, lengths, own, halos, d_mixed, local_out, local_log, share, heads, score_scale
):
    rows, width = d_mixed.shape
    head_dim = width // heads
    count = len(halos) + 1
    span = base.shape[1]

    def begin(ins, outs, scratch):
        base_ref, lengths_ref, own_ref, mix_ref, loc_ref, log_ref, share_ref, *halo_refs = ins
        dq_ref, diagonal_ref = outs

        def some_heads(some):
            first = lax.axis_index("mem") * rows
            same = same_book(lengths_ref, first, rows, first - (count - 1) * rows, count * rows)
            turned = (
                lax.broadcasted_iota(jnp.int32, (rows, rows), 0)
                + lax.broadcasted_iota(jnp.int32, (rows, rows), 1)
                == rows - 1
            ).astype(jnp.bfloat16)
            for head in some:
                columns = slice(head * head_dim, (head + 1) * head_dim)
                above = slice(width + head * head_dim, width + (head + 1) * head_dim)
                twice = slice(2 * width + head * head_dim, 2 * width + (head + 1) * head_dim)
                keys = [ref[:, columns] for ref in halo_refs] + [own_ref[:, above]]
                values = [ref[:, above] for ref in halo_refs] + [own_ref[:, twice]]
                q = own_ref[:, columns]
                d_out = ((1.0 - share_ref[head]) * mix_ref[:, columns]).astype(jnp.bfloat16)
                delta = jnp.sum(
                    d_out.astype(jnp.float32) * loc_ref[:, columns], axis=1, keepdims=True
                )
                raw = [
                    lax.dot_general(q, k, contract_cols, preferred_element_type=jnp.float32)
                    for k in keys
                ]
                bias = slanted(base_ref[head : head + 1, :], rows)[:, : count * rows]
                scores = jnp.concatenate(raw, axis=1) * score_scale + bias
                probs = jnp.exp(jnp.where(same, scores - log_ref[:, head : head + 1], masked_score))
                products = [
                    lax.dot_general(d_out, v, contract_cols, preferred_element_type=jnp.float32)
                    for v in values
                ]
                slopes = (probs * (jnp.concatenate(products, axis=1) - delta)).astype(jnp.bfloat16)
                slope_blocks = [slopes[:, i * rows : (i + 1) * rows] for i in range(count)]
                dq_ref[:, columns] = score_scale * sum(
                    jnp.dot(s, k, preferred_element_type=jnp.float32)
                    for s, k in zip(slope_blocks, keys)
                )
                mirrored = [
                    jnp.dot(s, turned, preferred_element_type=jnp.float32) for s in slope_blocks[::-1]
                ]
                mirrored.append(jnp.zeros((rows, span - count * rows), jnp.float32))
                leaned = pltpu.roll(jnp.concatenate(mirrored, axis=1), 0, 1, stride=1, stride_axis=0)
                diagonal_ref[head : head + 1, :] = jnp.sum(leaned, axis=0, keepdims=True)

        def run(part=0, parts=1):
            some_heads(range(part * heads // parts, (part + 1) * heads // parts))

        return run

    vmem = pl.BlockSpec(memory_space=pltpu.VMEM)
    smem = pl.BlockSpec(memory_space=pltpu.SMEM)
    arrays = [base, lengths, own, d_mixed, local_out, local_log, share, *halos]
    specs = [vmem, smem] + [vmem] * 4 + [smem] + [vmem] * len(halos)
    out_shape = [
        jax.ShapeDtypeStruct((rows, width), jnp.float32),
        jax.ShapeDtypeStruct((heads, span), jnp.float32),
    ]
    return arrays, specs, out_shape, [], begin


def local_keys(base, lengths, own, queries, sent, ratio, count, heads, score_scale):
    rows, width = own.shape[0], own.shape[1] // 3
    head_dim = width // heads
    groups = queries.shape[0] // rows

    def begin(ins, outs, scratch):
        base_ref, lengths_ref, own_ref, ratio_ref, queries_ref, sent_ref = ins
        (out_ref,) = outs
        queries_here, sent_here, sems = scratch
        copies = []
        for i in range(count):
            index = jnp.minimum(lax.axis_index("mem") + i, groups - 1)
            there = pl.ds(pl.multiple_of(index * rows, rows), rows)
            copies.append(
                pltpu.make_async_copy(queries_ref.at[there, :], queries_here.at[i], sems.at[0, i])
            )
            copies.append(pltpu.make_async_copy(sent_ref.at[there, :], sent_here.at[i], sems.at[1, i]))
        for copy in copies:
            copy.start()

        def run():
            for copy in copies:
                copy.wait()
            first = lax.axis_index("mem") * rows
            same = same_book(lengths_ref, first, rows, first, count * rows)
            stats = jnp.concatenate([joined_tile(sent_here[i, :, width:]).T for i in range(count)], axis=1)
            for head in range(heads):
                columns = slice(head * head_dim, (head + 1) * head_dim)
                above = slice(width + head * head_dim, width + (head + 1) * head_dim)
                twice = slice(2 * width + head * head_dim, 2 * width + (head + 1) * head_dim)
                k, v = own_ref[:, above], own_ref[:, twice]
                qs = [queries_here[i, :, columns] for i in range(count)]
                gs = [
                    (sent_here[i, :, columns].astype(jnp.float32) * ratio_ref[head]).astype(jnp.bfloat16)
                    for i in range(count)
                ]
                raw = [
                    lax.dot_general(k, q, contract_cols, preferred_element_type=jnp.float32) for q in qs
                ]
                bias = slanted(base_ref[head : head + 1, :], rows)[:, : count * rows]
                scores = jnp.concatenate(raw, axis=1) * score_scale + bias
                log = stats[2 * heads + head : 2 * heads + head + 1, :]
                delta = stats[3 * heads + head : 3 * heads + head + 1, :]
                probs = jnp.exp(jnp.where(same, scores - log, masked_score))
                products = [
                    lax.dot_general(v, g, contract_cols, preferred_element_type=jnp.float32) for g in gs
                ]
                slopes = (probs * (jnp.concatenate(products, axis=1) - delta)).astype(jnp.bfloat16)
                weights = probs.astype(jnp.bfloat16)
                blocks = [slice(i * rows, (i + 1) * rows) for i in range(count)]
                d_key = sum(
                    jnp.dot(slopes[:, b], q, preferred_element_type=jnp.float32) for b, q in zip(blocks, qs)
                )
                d_value = sum(
                    jnp.dot(weights[:, b], g, preferred_element_type=jnp.float32)
                    for b, g in zip(blocks, gs)
                )
                out_ref[:, above] = (d_key * score_scale).astype(jnp.bfloat16)
                out_ref[:, twice] = d_value.astype(jnp.bfloat16)

        return run

    vmem, anywhere = pl.BlockSpec(memory_space=pltpu.VMEM), pl.BlockSpec(memory_space=pl.ANY)
    smem = pl.BlockSpec(memory_space=pltpu.SMEM)
    arrays = [base, lengths, own, ratio, queries, sent]
    specs = [vmem, smem, vmem, smem, anywhere, anywhere]
    scratch = [
        pltpu.VMEM((count, rows, width), jnp.bfloat16),
        pltpu.VMEM((count, rows, width + 128), jnp.bfloat16),
        pltpu.SemaphoreType.DMA((2, count)),
    ]
    return arrays, specs, [jax.ShapeDtypeStruct((rows, 3 * width), jnp.bfloat16)], scratch, begin


def middle(
    tokens,
    memory_out,
    local_out,
    mem_log,
    local_log,
    share,
    out_weight,
    ffn_gain,
    up_weight,
    down_weight,
    cotangent,
    heads,
):
    rows, width = tokens.shape
    head_dim = width // heads
    hidden = up_weight.shape[1]
    block = math.gcd(hidden, 1024)
    steps = hidden // block

    def kernel(
        tokens_ref, mem_ref, loc_ref, mem_log_ref, log_ref, share_ref, out_w_ref, gain_ref, up_ref, down_ref, cot_ref, *refs
    ):
        mixed_ref, mid_ref, act_ref, d_up_ref, block_ref, d_res_ref, gain_part_ref, d_branch_ref, d_mix_ref = refs[:9]
        gate_ref, sent_ref, residual, branch_sum, d_mid_sum = refs[9:]
        i = pl.program_id(0)

        def scale_of(values):
            return lax.rsqrt(jnp.mean(values * values, axis=1, keepdims=True) + eps_norm)

        @pl.when(i == 0)
        def _():
            for head in range(heads):
                columns = slice(head * head_dim, (head + 1) * head_dim)
                part = share_ref[head]
                mixed_ref[:, columns] = (
                    part * mem_ref[:, columns] + (1.0 - part) * loc_ref[:, columns]
                ).astype(jnp.bfloat16)
            values = tokens_ref[...].astype(jnp.float32) + jnp.dot(
                mixed_ref[...], out_w_ref[...], preferred_element_type=jnp.float32
            )
            residual[...] = values
            mid_ref[...] = (values * scale_of(values) * gain_ref[...]).astype(jnp.bfloat16)
            branch_sum[...] = jnp.zeros_like(branch_sum)
            d_mid_sum[...] = jnp.zeros_like(d_mid_sum)

        up = jnp.dot(mid_ref[...], up_ref[...], preferred_element_type=jnp.float32)
        d_act = jnp.dot(cot_ref[...], down_ref[...], preferred_element_type=jnp.float32)
        below = 0.5 * (1.0 + lax.erf(up * math.sqrt(0.5)))
        density = jnp.exp(-0.5 * up * up) * (1.0 / math.sqrt(2.0 * math.pi))
        act = (up * below).astype(jnp.bfloat16)
        d_up = (d_act * (below + up * density)).astype(jnp.bfloat16)
        act_ref[...] = act
        d_up_ref[...] = d_up
        branch_sum[...] += lax.dot_general(
            act, down_ref[...], contract_cols, preferred_element_type=jnp.float32
        )
        d_mid_sum[...] += lax.dot_general(
            d_up, up_ref[...], contract_cols, preferred_element_type=jnp.float32
        )

        @pl.when(i == steps - 1)
        def _():
            values, d_mid = residual[...], d_mid_sum[...]
            block_ref[...] = (values + branch_sum[...]).astype(jnp.bfloat16)
            scale = scale_of(values)
            wanted = d_mid * gain_ref[...]
            slope = jnp.mean(values * wanted, axis=1, keepdims=True) * scale * scale * scale
            d_res = cot_ref[...].astype(jnp.float32) + scale * wanted - values * slope
            d_res_ref[...] = d_res
            gain_part_ref[...] = jnp.sum(d_mid * values * scale, axis=0, keepdims=True)
            d_branch_ref[...] = d_res.astype(jnp.bfloat16)
            d_mix_ref[...] = lax.dot_general(
                d_branch_ref[...], out_w_ref[...], contract_cols, preferred_element_type=jnp.float32
            )
            mem_deltas, deltas = [], []
            for head in range(heads):
                columns = slice(head * head_dim, (head + 1) * head_dim)
                part = share_ref[head]
                d_mix, mem_here, loc_here = d_mix_ref[:, columns], mem_ref[:, columns], loc_ref[:, columns]
                d_mem = (part * d_mix).astype(jnp.bfloat16)
                d_out = ((1.0 - part) * d_mix).astype(jnp.bfloat16)
                sent_ref[:, columns] = d_mem
                mem_deltas.append(
                    jnp.sum(d_mem.astype(jnp.float32) * mem_here, axis=1, keepdims=True)
                )
                deltas.append(jnp.sum(d_out.astype(jnp.float32) * loc_here, axis=1, keepdims=True))
                gate_ref[head : head + 1, :] = jnp.sum(
                    d_mix * (mem_here - loc_here), axis=0, keepdims=True
                )
            mem_logs = [mem_log_ref[:, head : head + 1] for head in range(heads)]
            logs = [log_ref[:, head : head + 1] for head in range(heads)]
            sent_ref[:, width:] = split_tile(lane_tile(mem_logs + mem_deltas + logs + deltas, rows))

    def whole(*shape):
        return pl.BlockSpec(shape, lambda i: (0, 0))

    weight = pl.BlockSpec((width, block), lambda i: (0, i))
    column = pl.BlockSpec((rows, block), lambda i: (0, i))
    full = whole(rows, width)
    low, high = jnp.bfloat16, jnp.float32
    outs = [
        (full, (rows, width), low),
        (full, (rows, width), low),
        (column, (rows, hidden), low),
        (column, (rows, hidden), low),
        (full, (rows, width), low),
        (full, (rows, width), high),
        (whole(1, width), (1, width), high),
        (full, (rows, width), low),
        (full, (rows, width), high),
        (whole(heads, head_dim), (heads, head_dim), high),
        (whole(rows, width + 128), (rows, width + 128), low),
    ]
    return pl.pallas_call(
        kernel,
        grid=(steps,),
        in_specs=[full, full, full, whole(rows, 128), whole(rows, 128)]
        + [pl.BlockSpec(memory_space=pltpu.SMEM)]
        + [whole(width, width), whole(1, width), weight, weight, full],
        out_specs=[spec for spec, _, _ in outs],
        out_shape=[jax.ShapeDtypeStruct(shape, dtype) for _, shape, dtype in outs],
        scratch_shapes=[pltpu.VMEM((rows, width), jnp.float32)] * 3,
        compiler_params=pltpu.CompilerParams(vmem_limit_bytes=VMEM_LIMIT),
        cost_estimate=lasting(18),
        name="middle",
    )(
        tokens,
        memory_out,
        local_out,
        mem_log,
        local_log,
        share,
        out_weight,
        ffn_gain[None, :],
        up_weight,
        down_weight,
        cotangent,
    )


def exchange_pairs(lefts, rights, other_lefts, other_right, send, recv):
    core = lax.axis_index("dp")
    copies, at = [], 0

    def push(source, target):
        i = len(copies)
        copy = pltpu.make_async_remote_copy(
            src_ref=source,
            dst_ref=target,
            send_sem=send.at[i],
            recv_sem=recv.at[i],
            device_id={"dp": 1 - core},
            device_id_type=pl.DeviceIdType.MESH,
        )
        copy.start()
        copies.append(copy)

    for i, (left, right) in enumerate(zip(lefts, rights)):
        half = right.shape[1] // 2
        push(left, other_lefts.at[i])
        there = pl.ds(pl.multiple_of((1 - core) * half, 128), half)
        push(right.at[:, there], other_right.at[:, pl.ds(at, half)])
        at += half
    return copies


def pair_products(lefts, rights, other_lefts, other_right, turned, store, copies):
    core = lax.axis_index("dp")
    rows = lefts[0].shape[0]
    at = 0
    for i, (left, right) in enumerate(zip(lefts, rights)):
        half = right.shape[1] // 2
        for copy in copies[2 * i : 2 * i + 2]:
            copy.wait_recv()
        turned[:, :rows] = left[...].T
        turned[:, rows:] = other_lefts[i].T
        block = math.gcd(half, 512)
        for column in range(0, half, block):
            kept = right[:, pl.ds(pl.multiple_of(core * half + column, 128), block)]
            both = jnp.concatenate([kept, other_right[:, at + column : at + column + block]], axis=0)
            store(
                at + column,
                jnp.dot(turned[...], both, preferred_element_type=jnp.float32).astype(jnp.bfloat16),
            )
        at += half


def pair_scratch(lefts, rights):
    rows, width = lefts[0].shape
    count = len(lefts)
    return [
        pltpu.VMEM((count, rows, width), jnp.bfloat16),
        pltpu.VMEM((rows, sum(right.shape[1] for right in rights) // 2), jnp.bfloat16),
        pltpu.VMEM((width, 2 * rows), jnp.bfloat16),
        pltpu.SemaphoreType.DMA((2 * count,)),
        pltpu.SemaphoreType.DMA((2 * count,)),
    ]


def pair_grads(lefts, rights, collective_id):
    count, width = len(lefts), lefts[0].shape[1]
    total = sum(right.shape[1] for right in rights) // 2
    block = math.gcd(*[right.shape[1] // 2 for right in rights], 512)

    def kernel(*refs):
        left_refs, right_refs, out_ref = refs[:count], refs[count : 2 * count], refs[2 * count]
        other_lefts, other_right, turned, send, recv, staged, out_sem = refs[2 * count + 1 :]
        barrier = pltpu.get_barrier_semaphore()
        partner = {"dp": 1 - lax.axis_index("dp")}
        pl.semaphore_signal(barrier, inc=1, device_id=partner, device_id_type=pl.DeviceIdType.MESH)
        pl.semaphore_wait(barrier, 1)
        copies = exchange_pairs(left_refs, right_refs, other_lefts, other_right, send, recv)
        written = []

        def store(column, value):
            slot = len(written) % 2
            if len(written) >= 2:
                written[-2].wait()
            staged[slot] = value
            copy = pltpu.make_async_copy(
                staged.at[slot], out_ref.at[:, pl.ds(column, block)], out_sem.at[slot]
            )
            copy.start()
            written.append(copy)

        pair_products(left_refs, right_refs, other_lefts, other_right, turned, store, copies)
        for copy in written[-2:]:
            copy.wait()
        for copy in copies:
            copy.wait_send()

    vmem = pl.BlockSpec(memory_space=pltpu.VMEM)
    return pl.pallas_call(
        kernel,
        in_specs=[vmem] * (2 * count),
        out_specs=pl.BlockSpec(memory_space=pl.ANY),
        out_shape=jax.ShapeDtypeStruct((width, total), jnp.bfloat16),
        scratch_shapes=pair_scratch(lefts, rights)
        + [pltpu.VMEM((2, width, block), jnp.bfloat16), pltpu.SemaphoreType.DMA((2,))],
        compiler_params=pltpu.CompilerParams(
            collective_id=collective_id, has_side_effects=True, vmem_limit_bytes=VMEM_LIMIT
        ),
        cost_estimate=lasting(10),
        name="pair_grads",
    )(*lefts, *rights)


def input_backward(tokens, attn_gain, d_projected, qkv_weight, d_residual):
    rows, width = tokens.shape

    def begin(ins, outs, scratch):
        tokens_ref, gain_ref, d_ref, weight_ref, residual_ref = ins
        grad_ref, part_ref = outs
        weight_here, sem = scratch
        copy = pltpu.make_async_copy(weight_ref, weight_here, sem)
        copy.start()

        def run():
            copy.wait()
            d_in = lax.dot_general(
                d_ref[...], weight_here[...], contract_cols, preferred_element_type=jnp.float32
            )
            x = tokens_ref[...].astype(jnp.float32)
            scale = lax.rsqrt(jnp.mean(x * x, axis=1, keepdims=True) + eps_norm)
            wanted = d_in * gain_ref[...]
            slope = jnp.mean(x * wanted, axis=1, keepdims=True) * scale * scale * scale
            grad_ref[...] = residual_ref[...] + scale * wanted - x * slope
            part_ref[...] = jnp.sum(d_in * x * scale, axis=0, keepdims=True)

        return run

    vmem = pl.BlockSpec(memory_space=pltpu.VMEM)
    arrays = [tokens, attn_gain[None, :], d_projected, qkv_weight, d_residual]
    specs = [vmem, vmem, vmem, pl.BlockSpec(memory_space=pl.ANY), vmem]
    out_shape = [
        jax.ShapeDtypeStruct((rows, width), jnp.float32),
        jax.ShapeDtypeStruct((1, width), jnp.float32),
    ]
    scratch = [pltpu.VMEM(qkv_weight.shape, qkv_weight.dtype), pltpu.SemaphoreType.DMA]
    return arrays, specs, out_shape, scratch, begin


def spread_halves(halves, outs):
    at = 0
    for out in outs:
        half = out.shape[1] // 2
        for c in (0, 1):
            out[:, c * half : (c + 1) * half] = halves[c, :, at : at + half].astype(jnp.float32)
        at += half


def join_halves(sums, collective_id):
    def kernel(sums_ref, both, send, recv):
        core = lax.axis_index("dp")
        partner = {"dp": 1 - core}
        barrier = pltpu.get_barrier_semaphore()
        pl.semaphore_signal(barrier, inc=1, device_id=partner, device_id_type=pl.DeviceIdType.MESH)
        pl.semaphore_wait(barrier, 1)
        copy = pltpu.make_async_remote_copy(
            src_ref=sums_ref,
            dst_ref=both.at[core],
            send_sem=send,
            recv_sem=recv,
            device_id=partner,
            device_id_type=pl.DeviceIdType.MESH,
        )
        copy.start()
        both[core] = sums_ref[...]
        copy.wait()

    vmem = pl.BlockSpec(memory_space=pltpu.VMEM)
    return pl.pallas_call(
        kernel,
        in_specs=[vmem],
        out_specs=vmem,
        out_shape=jax.ShapeDtypeStruct((2, *sums.shape), sums.dtype),
        scratch_shapes=[pltpu.SemaphoreType.DMA, pltpu.SemaphoreType.DMA],
        compiler_params=pltpu.CompilerParams(
            collective_id=collective_id, has_side_effects=True, vmem_limit_bytes=VMEM_LIMIT
        ),
        cost_estimate=lasting(4),
        name="join_halves",
    )(sums)


def write_results(late, late_widths, early, early_widths, small, heads, buckets):
    rows, width = late.shape[1], late.shape[2] * 2 // 3
    lines = width // 128
    count = len(late_widths) + len(early_widths)

    def kernel(late_ref, early_ref, small_ref, *outs):
        spread_halves(late_ref, outs[: len(late_widths)])
        spread_halves(early_ref, outs[len(late_widths) : count])
        attn_ref, ffn_ref, bias_ref, gate_ref = outs[count:]
        attn_ref[...] = small_ref[:lines, :]
        ffn_ref[...] = small_ref[lines : 2 * lines, :]
        for head in range(heads):
            line, lane = divmod(head * buckets, 128)
            here = small_ref[2 * lines + line : 2 * lines + line + 1, :]
            bias_ref[head : head + 1, :] = here[:, lane : lane + buckets]
        line = 2 * lines + heads * buckets // 128
        gate_ref[...] = small_ref[line : line + 1, :heads]

    shapes = [(rows, size) for size in [*late_widths, *early_widths]]
    shapes += [(lines, 128), (lines, 128), (heads, buckets), (1, heads)]
    return pl.pallas_call(
        kernel,
        out_shape=[jax.ShapeDtypeStruct(shape, jnp.float32) for shape in shapes],
        compiler_params=pltpu.CompilerParams(vmem_limit_bytes=VMEM_LIMIT),
        cost_estimate=lasting(3),
        name="write_results",
    )(late, early, small)


def finish_grads(lefts, rights, small, sources, collective_id, beside):
    width, total = lefts[0].shape[1], sum(right.shape[1] for right in rights) // 2
    rows = width // sources
    count = len(lefts)
    arrays, specs, more_out, more_scratch, begin = beside
    mesh_type = pl.DeviceIdType.MESH
    ref_shapes, sem_shapes = reduce_scratch(rows, total, jnp.bfloat16, sources)
    pair_shapes = pair_scratch(lefts, rights)
    sizes = [count, count, len(arrays), 1, 1, 1, len(more_out)]
    sizes += [len(ref_shapes), len(sem_shapes), len(pair_shapes), len(more_scratch), 8]

    def kernel(*refs):
        groups, at = [], 0
        for size in sizes:
            groups.append(refs[at : at + size])
            at += size
        left_refs, right_refs, ins, (small_ref,), (late,), (small_out,), more_refs = groups[:7]
        steps_refs, steps_sems, (other_lefts, other_right, turned, pair_send, pair_recv), scratch, own = groups[7:]
        parts, small_mine, smalls, core_small, small_send, small_recv, core_send, core_recv = own
        meanwhile = begin(ins, more_refs, scratch)
        me, core = lax.axis_index("mem"), lax.axis_index("dp")
        barrier = pltpu.get_barrier_semaphore()
        peers = [lax.rem(me + k, sources) for k in range(1, sources)]
        for peer in peers:
            pl.semaphore_signal(barrier, inc=1, device_id={"mem": peer}, device_id_type=mesh_type)
        pl.semaphore_signal(barrier, inc=1, device_id={"dp": 1 - core}, device_id_type=mesh_type)
        pl.semaphore_wait(barrier, sources)

        def merge(blocks):
            total = blocks[0][...].astype(jnp.float32)
            for block in blocks[1:]:
                total = total + block[...].astype(jnp.float32)
            return total

        def pack(target, total):
            target[...] = total.astype(jnp.bfloat16)

        def across_cores(source, target, i):
            copy = pltpu.make_async_remote_copy(
                src_ref=source,
                dst_ref=target,
                send_sem=core_send.at[i],
                recv_sem=core_recv.at[i],
                device_id={"dp": 1 - core},
                device_id_type=mesh_type,
            )
            copy.start()
            return copy

        pair_copies = exchange_pairs(
            left_refs, right_refs, other_lefts, other_right, pair_send, pair_recv
        )

        def store(column, value):
            parts[:, column : column + value.shape[1]] = value

        pair_products(
            left_refs, right_refs, other_lefts, other_right, turned, store, pair_copies
        )
        small_copies = [
            remote(small_mine, smalls.at[me], small_send.at[i], small_recv.at[me], peer)
            for i, peer in enumerate(peers)
        ]

        def between():
            meanwhile()
            small_mine[...] = small_ref[...]
            for i in range(width // 128):
                small_mine[i : i + 1, :] = more_refs[-1][:, i * 128 : (i + 1) * 128]
            smalls[me] = small_mine[...]
            for copy in small_copies:
                copy.start()

        final, still_open = reduce_steps(parts, sources, steps_refs, steps_sems, merge, pack, between)
        for here, blocks in final:
            late[core, here] = merge(blocks).astype(jnp.bfloat16)
        late_copy = across_cores(late.at[core], late.at[core], 0)
        for peer in peers:
            remote(
                smalls.at[peer], smalls.at[peer], small_send.at[0], small_recv.at[peer], peer
            ).wait_recv()
        group_small = smalls[0]
        for i in range(1, sources):
            group_small = group_small + smalls[i]
        core_small[0] = group_small
        small_copy = across_cores(core_small.at[0], core_small.at[1], 1)
        for copy in (late_copy, small_copy):
            copy.wait()
        small_out[...] = core_small[0] + core_small[1]
        for copy in still_open + small_copies + pair_copies:
            copy.wait_send()

    vmem = pl.BlockSpec(memory_space=pltpu.VMEM)
    return pl.pallas_call(
        kernel,
        in_specs=[vmem] * (2 * count) + specs + [vmem],
        out_specs=[vmem] * (2 + len(more_out)),
        out_shape=[jax.ShapeDtypeStruct((2, rows, total), jnp.bfloat16)]
        + [jax.ShapeDtypeStruct(small.shape, small.dtype)]
        + more_out,
        scratch_shapes=ref_shapes
        + sem_shapes
        + pair_shapes
        + more_scratch
        + [
            pltpu.VMEM((width, total), jnp.bfloat16),
            pltpu.VMEM(small.shape, small.dtype),
            pltpu.VMEM((sources, *small.shape), small.dtype),
            pltpu.VMEM((2, *small.shape), small.dtype),
        ]
        + [pltpu.SemaphoreType.DMA((sources,))] * 2
        + [pltpu.SemaphoreType.DMA((2,))] * 2,
        compiler_params=pltpu.CompilerParams(
            collective_id=collective_id, has_side_effects=True, vmem_limit_bytes=VMEM_LIMIT
        ),
        cost_estimate=lasting(45),
        name="finish_grads",
    )(*lefts, *rights, *arrays, small)


def on_device(
    tokens,
    attn_gain,
    qkv_weight,
    out_weight,
    bias_table,
    gate_logit,
    ffn_gain,
    up_weight,
    down_weight,
    memory_keys,
    memory_values,
    book_lengths,
    slot_shard,
    slot_index,
    slot_live,
    cotangent,
):
    rows, width = tokens.shape
    heads, buckets = bias_table.shape
    head_dim = width // heads
    top_count = slot_index.shape[2]
    hidden = up_weight.shape[1]
    groups = lax.axis_size("mem")
    capacity = -(-3 * rows * heads * top_count // (2 * groups) // 128) * 128
    score_scale = 1.0 / math.sqrt(head_dim)
    repeats = W // rows
    span = W + 2 * rows
    before = W - jnp.arange(span, dtype=jnp.int32)
    after = jnp.arange(span, dtype=jnp.int32)

    def bias_rows(offset):
        reached = (offset >= 0) & (offset < W)
        hot = (bucket_of(offset)[:, None] == jnp.arange(buckets, dtype=jnp.int32)) & reached[:, None]
        rows_of_bias = jnp.einsum(
            "rb,hb->hr", hot.astype(jnp.float32), bias_table, precision=lax.Precision.HIGHEST
        )
        return rows_of_bias + jnp.where(reached, 0.0, masked_score)

    before_bias, after_bias = bias_rows(before), bias_rows(after)
    bucket = bucket_of(jnp.arange(W, dtype=jnp.int32))
    one_hot = (bucket[:, None] == jnp.arange(buckets, dtype=jnp.int32)).astype(jnp.float32)
    tokens_f = tokens.astype(jnp.float32)
    normed_in = normed(tokens_f, attn_gain).astype(jnp.bfloat16)
    projected = jnp.dot(normed_in, qkv_weight, preferred_element_type=jnp.float32).astype(
        jnp.bfloat16
    )
    slots = memory_keys.shape[0]
    requests = place_requests(slot_shard, slot_index, slot_live, groups, capacity, slots)
    incoming = lax.all_to_all(requests, "mem", split_axis=0, concat_axis=0, tiled=True)
    keys_values, _ = lax.optimization_barrier((projected[:, width:], requests))
    distances = list(range(repeats, 0, -1))
    halos = [passed_along(keys_values, "mem", distance) for distance in distances[: repeats // 2]]
    index, row_ids, bounds = read_lists(incoming, heads, rows, slots)
    bounds = bounds.reshape(-1)
    key_rows, value_rows = gather_rows(
        index.reshape(-1), bounds, memory_keys, memory_values, heads, groups, capacity
    )
    keys_values, key_rows = lax.optimization_barrier((keys_values, key_rows))
    halos += [passed_along(keys_values, "mem", distance) for distance in distances[repeats // 2 :]]
    all_queries = lax.all_gather(projected[:, :width], "mem", axis=0, tiled=True)
    local = local_forward(before_bias, book_lengths, projected, halos, heads, score_scale)
    partial = memory_forward(
        bounds,
        all_queries,
        key_rows,
        value_rows,
        row_ids,
        heads,
        groups,
        rows,
        score_scale,
    )
    if groups == 16:
        memory_out, mem_log, local_out, local_log = merge_partials(partial, groups, 1, heads, local)
    else:
        local_out, local_log = run_alone("local_forward", local)
        partial = lax.all_to_all(
            partial.reshape(groups, rows, width + 128),
            "mem",
            split_axis=0,
            concat_axis=0,
            tiled=True,
        ).reshape(groups * rows, width + 128)
        memory_out, mem_log = combine_partials(partial, heads, groups, rows)
    gate_share = jax.nn.sigmoid(gate_logit)
    (
        mixed_heads,
        normed_mid,
        activated,
        d_up,
        block_out,
        d_residual,
        ffn_gain_part,
        d_branch,
        d_mixed,
        gate_products,
        sent_grads,
    ) = middle(
        tokens,
        memory_out,
        local_out,
        mem_log,
        local_log,
        gate_share,
        out_weight,
        ffn_gain,
        up_weight,
        down_weight,
        cotangent,
        heads,
    )
    ffn_gain_part = ffn_gain_part.reshape(-1)
    early_halves = pair_grads(
        [mixed_heads, normed_mid, cotangent], [d_branch, d_up, activated], 5
    )
    early_sums = scattered(early_halves)
    sent_grads, _ = lax.optimization_barrier((sent_grads, early_halves))
    gate_part = jnp.sum(gate_products, axis=1) * gate_share * (1.0 - gate_share)
    local = local_queries(
        before_bias,
        book_lengths,
        projected,
        halos,
        d_mixed,
        local_out,
        local_log,
        gate_share,
        heads,
        score_scale,
    )
    if groups == 16:
        all_grads, d_queries, diagonals = gather_group(sent_grads, groups, 2, local)
    else:
        all_grads = lax.all_gather(sent_grads, "mem", axis=0, tiled=True)
        d_queries, diagonals = run_alone("local_queries", local)
    bias_part = jnp.dot(diagonals[:, rows - 1 : rows - 1 + W], one_hot, precision=lax.Precision.HIGHEST)
    d_partial = memory_backward(
        bounds,
        all_queries,
        all_grads,
        key_rows,
        value_rows,
        row_ids,
        heads,
        groups,
        rows,
        score_scale,
    )
    local = local_keys(
        after_bias,
        book_lengths,
        projected,
        all_queries,
        all_grads,
        (1.0 - gate_share) / gate_share,
        repeats + 1,
        heads,
        score_scale,
    )
    if groups == 16:
        d_projected = sum_queries(d_partial, d_queries, groups, 3, score_scale, local)
    else:
        (d_projected,) = run_alone("local_keys", local)
        d_partial, d_projected = lax.optimization_barrier((d_partial, d_projected))
        d_partial = jnp.sum(
            lax.all_to_all(
                d_partial.reshape(groups, rows, width), "mem", split_axis=0, concat_axis=0, tiled=True
            ).astype(jnp.float32),
            axis=0,
        )
        d_queries = (d_queries + d_partial * score_scale).astype(jnp.bfloat16)
        d_projected = jnp.concatenate([d_queries, d_projected[:, width:]], axis=1)
    beside = input_backward(tokens, attn_gain, d_projected, qkv_weight, d_residual)
    small = jnp.concatenate([ffn_gain_part, bias_part.reshape(-1), gate_part], axis=0)
    small = jnp.pad(small, (width, -small.shape[0] % 1024)).reshape(-1, 128)
    early_widths = [width, hidden, hidden]
    if groups == 16:
        late_both, small, tokens_grad, _ = finish_grads(
            [normed_in], [d_projected], small, groups, 4, beside
        )
        early_sums, small = lax.optimization_barrier((early_sums, small))
        early_both = join_halves(early_sums, 7)
    else:
        tokens_grad, attn_gain_part = run_alone("input_backward", beside)
        late_halves = pair_grads([normed_in], [d_projected], 6)
        late_halves, early_sums = lax.optimization_barrier((late_halves, early_sums))
        late_both = lax.all_gather(scattered(late_halves), "dp", axis=0)
        early_both = lax.all_gather(early_sums, "dp", axis=0)
        small = lax.psum(small.at[: width // 128].set(attn_gain_part.reshape(-1, 128)), ("dp", "mem"))
    qkv_grad, out_grad, up_grad, down_grad, attn_sum, ffn_sum, bias_sum, gate_sum = write_results(
        late_both, [3 * width], early_both, early_widths, small, heads, buckets
    )
    return (
        block_out,
        tokens_grad,
        qkv_grad,
        out_grad,
        up_grad,
        down_grad,
        attn_sum.reshape(-1),
        ffn_sum.reshape(-1),
        bias_sum,
        gate_sum.reshape(-1),
    )


def solution(mesh):
    in_specs = (
        P(("dp", "mem"), None),
        P(),
        P(),
        P(),
        P(),
        P(),
        P(),
        P(),
        P(),
        P("mem", None),
        P("mem", None),
        P("dp", None),
        P(("dp", "mem"), None, None, None),
        P(("dp", "mem"), None, None),
        P(("dp", "mem"), None, None),
        P(("dp", "mem"), None),
    )
    out_specs = (
        P(("dp", "mem"), None),
        P(("dp", "mem"), None),
        P("mem", None),
        P("mem", None),
        P("mem", None),
        P("mem", None),
        P(),
        P(),
        P(),
        P(),
    )
    return jax.shard_map(
        on_device, mesh=mesh, in_specs=in_specs, out_specs=out_specs, check_vma=False
    )
```

```python
import math

import jax
import jax.numpy as jnp
from jax import lax
from jax.experimental import pallas as pl
from jax.experimental.pallas import tpu as pltpu
from jax.sharding import PartitionSpec as P

W = 512
VMEM_LIMIT = 56 * 1024 * 1024


eps_norm = 1e-06
bucket_edges = tuple((math.ceil(16 * 8 ** (edge_step / 16)) for edge_step in range(1, 16)))
masked_score = -1e30
dead_score = -10000.0
contract_rows = (((0,), (0,)), ((), ()))
contract_cols = (((1,), (1,)), ((), ()))


def passed_along(value, axis, by):
    size = lax.axis_size(axis)
    pairs = [(i, i + by) for i in range(size) if 0 <= i + by < size]
    return lax.ppermute(value, axis, pairs)


def bucket_of(offset):
    past_edges = sum(((offset >= edge_pos).astype(jnp.int32) for edge_pos in bucket_edges))
    return jnp.where(offset < 16, offset, 16 + past_edges)


def normed(values, gain_vec):
    return (
        values * lax.rsqrt(jnp.mean(values * values, axis=-1, keepdims=True) + eps_norm) * gain_vec
    )


def place_requests(slot_shard, slot_index, slot_live, owners, capacity, slots):
    rows, heads, top_count = slot_index.shape
    entries, empty = rows * heads * top_count, heads * rows * slots
    if (owners + 1) * empty >= 2**31:
        raise ValueError("codes exceed int32")
    row_of = (
        jnp.arange(heads, dtype=jnp.int32)[None, :] * rows
        + jnp.arange(rows, dtype=jnp.int32)[:, None]
    )
    owner = jnp.where(slot_live > 0, slot_shard[..., 0], owners)
    codes = owner * empty + row_of[:, :, None] * slots + slot_index
    codes = lax.sort(codes.reshape(-1), is_stable=False)
    ends = jnp.sum(
        (codes[None, :] < (jnp.arange(owners, dtype=jnp.int32) + 1)[:, None] * empty).astype(jnp.int32),
        axis=1,
    )
    starts = jnp.concatenate([jnp.zeros((1,), jnp.int32), ends[:-1]])
    tall = -(-entries // 128)
    codes = jnp.pad(codes, (0, tall * 128 - entries)).reshape(tall, 128)
    long = capacity // 128

    def kernel(starts_ref, ends_ref, codes_ref, lists_ref, padded):
        padded[:tall, :] = codes_ref[...]
        padded[tall:, :] = jnp.zeros((long + 8, 128), jnp.int32)
        lane = lax.broadcasted_iota(jnp.int32, (long, 128), 1)
        place = lax.broadcasted_iota(jnp.int32, (long, 128), 0) * 128 + lane

        @pl.loop(0, owners)
        def _(i):
            start, end = starts_ref[i], ends_ref[i]
            shift = start % 128
            lines = padded[pl.ds(start // 128, long + 1), :]
            turned = pltpu.roll(lines, (128 - shift) % 128, 1)
            joined = jnp.where(lane < 128 - shift, turned[:long], turned[1:])
            lists_ref[i] = jnp.where(place < end - start, joined - i * empty, empty)

    return pl.pallas_call(
        kernel,
        in_specs=[pl.BlockSpec(memory_space=pltpu.SMEM)] * 2 + [pl.BlockSpec(memory_space=pltpu.VMEM)],
        out_shape=jax.ShapeDtypeStruct((owners, long, 128), jnp.int32),
        scratch_shapes=[pltpu.VMEM((tall + long + 8, 128), jnp.int32)],
        cost_estimate=lasting(3),
        name="make_lists",
    )(starts, ends, codes)


def read_lists(incoming, heads, rows, slots):
    sources, long, _ = incoming.shape

    def kernel(lists_ref, index_ref, ids_ref, bounds_ref):
        lane = lax.broadcasted_iota(jnp.int32, (1, 128), 1)

        def read(source):
            codes = lists_ref[source]
            ids = lax.div(codes, slots)
            index = lax.div(ids, rows) * slots + lax.rem(codes, slots)
            index_ref[source] = jnp.where(ids < heads * rows, index, 0)
            ids_ref[source, :long, :] = ids
            ids_ref[source, long:, :] = jnp.full((1, 128), heads * rows, jnp.int32)
            bounds = jnp.zeros((1, 128), jnp.int32)
            for head in range(1, heads + 1):
                below = jnp.sum(
                    jnp.where(codes < head * rows * slots, 1.0, 0.0), axis=0, keepdims=True
                )
                below = jnp.sum(below, axis=1, keepdims=True).astype(jnp.int32)
                bounds = jnp.where(lane == head, below, bounds)
            bounds_ref[pl.ds(source, 1), :] = bounds

        if sources > 16:
            pl.loop(0, sources)(read)
        else:
            for source in range(sources):
                read(source)

    return pl.pallas_call(
        kernel,
        out_shape=[
            jax.ShapeDtypeStruct((sources, long, 128), jnp.int32),
            jax.ShapeDtypeStruct((sources, long + 1, 128), jnp.int32),
            jax.ShapeDtypeStruct((sources, 128), jnp.int32),
        ],
        cost_estimate=lasting(3),
        name="read_lists",
    )(incoming)


def gather_rows(index, bounds, memory_keys, memory_values, heads, sources, capacity):
    slots, width = memory_keys.shape
    head_dim = width // heads
    step, part = 128, 16

    def kernel(index_ref, bounds_ref, keys, values, out_keys, out_values, key_table, value_table, key_rows, value_rows):
        i = pl.program_id(0)

        @pl.when(i < heads)
        def _():
            place = pl.ds(pl.multiple_of(i * slots, slots), slots)
            key_table[place, :] = keys[...].astype(jnp.float32)
            value_table[place, :] = values[...].astype(jnp.float32)

        @pl.when(i >= heads)
        def _():
            source = i - heads

            used = (bounds_ref[source * 128 + heads] + step - 1) // step

            def store(group):
                for at in range(0, step, part):
                    here = pl.ds(pl.multiple_of(group * step, step) + at, part)
                    out_keys[here, :] = key_rows[at : at + part, :].astype(jnp.bfloat16)
                    out_values[here, :] = value_rows[at : at + part, :].astype(jnp.bfloat16)

            @pl.loop(0, used)
            def _(group):
                store(jnp.maximum(group - 1, 0))
                first = source * capacity + group * step
                for u in range(step):
                    row = index_ref[first + u]
                    key_rows[u : u + 1, :] = key_table[pl.ds(row, 1), :]
                    value_rows[u : u + 1, :] = value_table[pl.ds(row, 1), :]

            pl.when(used > 0)(lambda: store(used - 1))

            @pl.loop(used, capacity // step)
            def _(group):
                here = pl.ds(pl.multiple_of(group * step, step), step)
                out_keys[here, :] = jnp.zeros((step, head_dim), jnp.bfloat16)
                out_values[here, :] = jnp.zeros((step, head_dim), jnp.bfloat16)

    table_spec = pl.BlockSpec((slots, head_dim), lambda i, *_: (0, jnp.minimum(i, heads - 1)))
    out_spec = pl.BlockSpec((capacity, head_dim), lambda i, *_: (jnp.maximum(i - heads, 0), 0))
    out_shape = jax.ShapeDtypeStruct((sources * capacity, head_dim), jnp.bfloat16)
    return pl.pallas_call(
        kernel,
        grid_spec=pltpu.PrefetchScalarGridSpec(
            num_scalar_prefetch=2,
            grid=(heads + sources,),
            in_specs=[table_spec, table_spec],
            out_specs=[out_spec, out_spec],
            scratch_shapes=[
                pltpu.VMEM((heads * slots, head_dim), jnp.float32),
                pltpu.VMEM((heads * slots, head_dim), jnp.float32),
                pltpu.VMEM((step, head_dim), jnp.float32),
                pltpu.VMEM((step, head_dim), jnp.float32),
            ],
        ),
        out_shape=[out_shape, out_shape],
        compiler_params=pltpu.CompilerParams(vmem_limit_bytes=VMEM_LIMIT),
        cost_estimate=lasting(42),
        name="gather_rows",
    )(index, bounds, memory_keys, memory_values)


def lasting(microseconds):
    return pl.CostEstimate(flops=0, bytes_accessed=3_000_000 * microseconds, transcendentals=0)


def triple(stat):
    part = lax.broadcasted_iota(jnp.int32, stat.shape, 1) // 16
    high = stat.astype(jnp.bfloat16).astype(jnp.float32)
    rest = stat - high
    middle = rest.astype(jnp.bfloat16).astype(jnp.float32)
    low = rest - middle
    chosen = jnp.where(part == 0, high, jnp.where(part == 1, middle, jnp.where(part == 2, low, 0.0)))
    return chosen.astype(jnp.bfloat16)


def window_of(bounds, source, head, heads, span, capacity):
    first, last = bounds[source * 128 + head], bounds[source * 128 + head + 1]
    start = jnp.minimum(first // 16 * 16, capacity - span)
    extra = jnp.maximum(last - start - 1, 0) // span
    return start, extra


def columns_of(head, head_dim):
    if isinstance(head, int):
        return slice(head * head_dim, (head + 1) * head_dim)
    return pl.ds(pl.multiple_of(head * head_dim, head_dim), head_dim)


def window_ids(id_ref, start, span):
    lines = id_ref[0, pl.ds(start // 128, span // 128 + 1), :]
    shift = start % 128
    turned = pltpu.roll(lines, (128 - shift) % 128, 1)
    lane = lax.broadcasted_iota(jnp.int32, (span // 128, 128), 1)
    return jnp.where(lane < 128 - shift, turned[:-1], turned[1:])


def owned(lines, first_row, count, start, least):
    row = lax.broadcasted_iota(jnp.int32, (count, 128), 0) + first_row
    masks = []
    for i in range(lines.shape[0]):
        mask = lines[i : i + 1, :] == row
        if least is not None:
            place = lax.broadcasted_iota(jnp.int32, (1, 128), 1) + start + i * 128
            mask = mask & (place >= least)
        masks.append(mask)
    return jnp.concatenate(masks, axis=1)


def memory_forward(bounds, queries, key_rows, value_rows, row_ids, heads, sources, rows, score_scale):
    capacity, head_dim = key_rows.shape[0] // sources, key_rows.shape[1]
    width = heads * head_dim
    span = min(384, capacity)
    chunk = math.gcd(rows, 32)

    def kernel(bounds_ref, q_ref, k_ref, v_ref, id_ref, out_ref, sums, tops, totals, raw, weights):
        source = pl.program_id(0)
        lane = lax.broadcasted_iota(jnp.int32, (chunk, 128), 1) % 16

        def window(heads_here, starts, least):
            here = [pl.ds(pl.multiple_of(start, 16), span) for start in starts]
            columns = [columns_of(head, head_dim) for head in heads_here]
            for slot in range(len(starts)):
                raw[slot] = lax.dot_general(
                    q_ref[:, columns[slot]],
                    k_ref[here[slot], :],
                    contract_cols,
                    preferred_element_type=jnp.float32,
                )
            for slot, (head, start) in enumerate(zip(heads_here, starts)):
                lines = window_ids(id_ref, start, span)
                for at in range(0, rows, chunk):
                    some = slice(at, at + chunk)
                    mine = owned(lines, head * rows + at, chunk, start, least)
                    scores = jnp.where(mine, raw[slot, some, :], masked_score)
                    top = jnp.maximum(jnp.max(scores, axis=1, keepdims=True), 0.1 * masked_score)
                    if least is not None:
                        old_top = jnp.max(
                            jnp.where(lane == head, tops[some, :], masked_score), axis=1, keepdims=True
                        )
                        top = jnp.maximum(top, old_top)
                    exps = jnp.exp((scores - top) * score_scale)
                    weights[slot, some, :] = exps.astype(jnp.bfloat16)
                    total = jnp.sum(exps, axis=1, keepdims=True)
                    if least is not None:
                        faded = jnp.exp((old_top - top) * score_scale)
                        sums[some, columns[slot]] = sums[some, columns[slot]] * faded
                        total = total + totals[some, :] * faded
                    tops[some, :] = jnp.where(lane == head, top, tops[some, :])
                    totals[some, :] = jnp.where(lane == heads + head, total, totals[some, :])
            for slot in range(len(starts)):
                found = jnp.dot(
                    weights[slot], v_ref[here[slot], :], preferred_element_type=jnp.float32
                )
                sums[:, columns[slot]] = found if least is None else sums[:, columns[slot]] + found

        tops[...] = jnp.zeros_like(tops)
        totals[...] = jnp.zeros_like(totals)

        windows = [window_of(bounds_ref, source, head, heads, span, capacity) for head in range(heads)]
        window(list(range(heads)), [start for start, _ in windows], None)

        @pl.when(sum(extra for _, extra in windows) > 0)
        def _():
            @pl.loop(0, heads)
            def _(head):
                start, extra = window_of(bounds_ref, source, head, heads, span, capacity)

                @pl.loop(0, extra)
                def _(turn):
                    least = start + (turn + 1) * span
                    window([head], [jnp.minimum(least, capacity - span)], least)

        out_ref[:, :width] = sums[...].astype(jnp.bfloat16)
        wide = lax.broadcasted_iota(jnp.int32, (rows, 128), 1) % 16
        out_ref[:, width:] = triple(jnp.where(wide < heads, tops[...] * score_scale, totals[...]))

    return pl.pallas_call(
        kernel,
        grid_spec=pltpu.PrefetchScalarGridSpec(
            num_scalar_prefetch=1,
            grid=(sources,),
            in_specs=[
                pl.BlockSpec((rows, width), lambda i, *_: (i, 0)),
                pl.BlockSpec((capacity, head_dim), lambda i, *_: (i, 0)),
                pl.BlockSpec((capacity, head_dim), lambda i, *_: (i, 0)),
                pl.BlockSpec((1, *row_ids.shape[1:]), lambda i, *_: (i, 0, 0)),
            ],
            out_specs=pl.BlockSpec((rows, width + 128), lambda i, *_: (i, 0)),
            scratch_shapes=[
                pltpu.VMEM((rows, width), jnp.float32),
                pltpu.VMEM((rows, 128), jnp.float32),
                pltpu.VMEM((rows, 128), jnp.float32),
                pltpu.VMEM((heads, rows, span), jnp.float32),
                pltpu.VMEM((heads, rows, span), jnp.bfloat16),
            ],
        ),
        out_shape=jax.ShapeDtypeStruct((sources * rows, width + 128), jnp.bfloat16),
        compiler_params=pltpu.CompilerParams(vmem_limit_bytes=VMEM_LIMIT),
        cost_estimate=lasting(25),
        name="memory_forward",
    )(bounds, queries, key_rows, value_rows, row_ids)


def combine_partials(partial, heads, sources, rows):
    width = partial.shape[1] - 128
    head_dim = width // heads

    def kernel(part_ref, out_ref, log_ref, sums, tops, totals):
        i = pl.program_id(0)

        @pl.when(i == 0)
        def _():
            sums[...] = jnp.zeros_like(sums)
            tops[...] = jnp.full_like(tops, masked_score)
            totals[...] = jnp.zeros_like(totals)

        stat = part_ref[:, width:].astype(jnp.float32)
        stat = stat + pltpu.roll(stat, 128 - 16, 1) + pltpu.roll(stat, 128 - 32, 1)
        new_total = pltpu.roll(stat, 128 - heads, 1)
        top = jnp.maximum(tops[...], stat)
        old_fade, new_fade = jnp.exp(tops[...] - top), jnp.exp(stat - top)
        tops[...] = top
        totals[...] = totals[...] * old_fade + new_total * new_fade
        for head in range(heads):
            columns = slice(head * head_dim, (head + 1) * head_dim)
            sums[:, columns] = (
                sums[:, columns] * old_fade[:, head : head + 1]
                + part_ref[:, columns].astype(jnp.float32) * new_fade[:, head : head + 1]
            )

        @pl.when(i == sources - 1)
        def _():
            live = totals[...] > 0
            total = jnp.where(live, totals[...], 1.0)
            log_ref[...] = jnp.where(live, tops[...] + jnp.log(total), 0.0)
            for head in range(heads):
                columns = slice(head * head_dim, (head + 1) * head_dim)
                out_ref[:, columns] = sums[:, columns] / total[:, head : head + 1]

    return pl.pallas_call(
        kernel,
        grid=(sources,),
        in_specs=[pl.BlockSpec((rows, width + 128), lambda i: (i, 0))],
        out_specs=[
            pl.BlockSpec((rows, width), lambda i: (0, 0)),
            pl.BlockSpec((rows, 128), lambda i: (0, 0)),
        ],
        scratch_shapes=[
            pltpu.VMEM((rows, width), jnp.float32),
            pltpu.VMEM((rows, 128), jnp.float32),
            pltpu.VMEM((rows, 128), jnp.float32),
        ],
        out_shape=[
            jax.ShapeDtypeStruct((rows, width), jnp.float32),
            jax.ShapeDtypeStruct((rows, 128), jnp.float32),
        ],
        compiler_params=pltpu.CompilerParams(vmem_limit_bytes=VMEM_LIMIT),
        cost_estimate=lasting(13),
        name="combine_partials",
    )(partial)


def memory_backward(bounds, queries, grads, key_rows, value_rows, row_ids, heads, sources, rows, score_scale):
    capacity, head_dim = key_rows.shape[0] // sources, key_rows.shape[1]
    width = heads * head_dim
    span = min(384, capacity)
    chunk = math.gcd(rows, 32)

    def kernel(bounds_ref, q_ref, g_ref, k_ref, v_ref, id_ref, out_ref, sums, stats, raw, products, slopes):
        source = pl.program_id(0)
        stats[...] = joined_tile(g_ref[:, width : width + 128])

        def window(heads_here, starts, least):
            here = [pl.ds(pl.multiple_of(start, 16), span) for start in starts]
            columns = [columns_of(head, head_dim) for head in heads_here]
            for slot in range(len(starts)):
                raw[slot] = lax.dot_general(
                    q_ref[:, columns[slot]],
                    k_ref[here[slot], :],
                    contract_cols,
                    preferred_element_type=jnp.float32,
                )
                products[slot] = lax.dot_general(
                    g_ref[:, columns[slot]],
                    v_ref[here[slot], :],
                    contract_cols,
                    preferred_element_type=jnp.float32,
                )
            for slot, (head, start) in enumerate(zip(heads_here, starts)):
                lines = window_ids(id_ref, start, span)
                turned = stats[...]
                if least is not None:
                    turned = pltpu.roll(turned, 128 - head, 1)
                elif head:
                    turned = turned[:, head:]
                for at in range(0, rows, chunk):
                    some = slice(at, at + chunk)
                    mine = owned(lines, head * rows + at, chunk, start, least)
                    log, delta = turned[some, :1], turned[some, heads : heads + 1]
                    probs = jnp.exp(jnp.where(mine, raw[slot, some, :] * score_scale - log, dead_score))
                    slopes[slot, some, :] = (probs * (products[slot, some, :] - delta)).astype(
                        jnp.bfloat16
                    )
            for slot in range(len(starts)):
                found = jnp.dot(
                    slopes[slot], k_ref[here[slot], :], preferred_element_type=jnp.float32
                )
                sums[:, columns[slot]] = found if least is None else sums[:, columns[slot]] + found

        windows = [window_of(bounds_ref, source, head, heads, span, capacity) for head in range(heads)]
        window(list(range(heads)), [start for start, _ in windows], None)

        @pl.when(sum(extra for _, extra in windows) > 0)
        def _():
            @pl.loop(0, heads)
            def _(head):
                start, extra = window_of(bounds_ref, source, head, heads, span, capacity)

                @pl.loop(0, extra)
                def _(turn):
                    least = start + (turn + 1) * span
                    window([head], [jnp.minimum(least, capacity - span)], least)

        out_ref[...] = sums[...].astype(jnp.bfloat16)

    return pl.pallas_call(
        kernel,
        grid_spec=pltpu.PrefetchScalarGridSpec(
            num_scalar_prefetch=1,
            grid=(sources,),
            in_specs=[
                pl.BlockSpec((rows, width), lambda i, *_: (i, 0)),
                pl.BlockSpec((rows, width + 128), lambda i, *_: (i, 0)),
                pl.BlockSpec((capacity, head_dim), lambda i, *_: (i, 0)),
                pl.BlockSpec((capacity, head_dim), lambda i, *_: (i, 0)),
                pl.BlockSpec((1, *row_ids.shape[1:]), lambda i, *_: (i, 0, 0)),
            ],
            out_specs=pl.BlockSpec((rows, width), lambda i, *_: (i, 0)),
            scratch_shapes=[
                pltpu.VMEM((rows, width), jnp.float32),
                pltpu.VMEM((rows, 128), jnp.float32),
                pltpu.VMEM((heads, rows, span), jnp.float32),
                pltpu.VMEM((heads, rows, span), jnp.float32),
                pltpu.VMEM((heads, rows, span), jnp.bfloat16),
            ],
        ),
        out_shape=jax.ShapeDtypeStruct((sources * rows, width), jnp.bfloat16),
        compiler_params=pltpu.CompilerParams(vmem_limit_bytes=VMEM_LIMIT),
        cost_estimate=lasting(25),
        name="memory_backward",
    )(bounds, queries, grads, key_rows, value_rows, row_ids)


def remote(source, target, send_sem, recv_sem, device):
    return pltpu.make_async_remote_copy(
        src_ref=source,
        dst_ref=target,
        send_sem=send_sem,
        recv_sem=recv_sem,
        device_id={"mem": device},
        device_id_type=pl.DeviceIdType.MESH,
    )


def grid_place(depth):
    me = lax.axis_index("mem")
    layer, column = me // 4, me % 4
    beside_x = column + 1 - 2 * (column % 2)
    beside_y = column + 2 - 4 * (column // 2)
    across = 3 - column

    def index_of(step, place):
        return (layer + step + depth) % depth * 4 + place

    return me, column, beside_x, beside_y, across, index_of


def greet(devices):
    barrier = pltpu.get_barrier_semaphore()
    for device in devices:
        pl.semaphore_signal(
            barrier, inc=1, device_id={"mem": device}, device_id_type=pl.DeviceIdType.MESH
        )
    pl.semaphore_wait(barrier, len(devices))


def gather_group(block, sources, collective_id, beside):
    rows, width = block.shape
    depth, half = sources // 4, rows // 2
    slots = 2 * depth - 1
    arrays, specs, more_out, more_scratch, begin = beside
    ins, outs = len(arrays), len(more_out)

    def kernel(x_ref, *refs):
        in_refs, (out_ref, *more_refs) = refs[:ins], refs[ins : ins + 1 + outs]
        (own_sem, send, recv), scratch = refs[ins + 1 + outs : ins + 4 + outs], refs[ins + 4 + outs :]
        meanwhile = begin(in_refs, more_refs, scratch)
        me = lax.axis_index("mem")
        layer, column = me // 4, me % 4
        to_x = me + 1 - 2 * (column % 2)
        to_y = me + 2 - 4 * (column // 2)
        across = layer * 4 + 3 - column
        has_above, has_below = layer + 1 < depth, layer > 0
        barrier = pltpu.get_barrier_semaphore()

        def signal(device):
            pl.semaphore_signal(
                barrier, inc=1, device_id={"mem": device}, device_id_type=pl.DeviceIdType.MESH
            )

        signal(to_x)
        signal(to_y)
        pl.when(has_above)(lambda: signal(me + 4))
        pl.when(has_below)(lambda: signal(me - 4))
        pl.semaphore_wait(barrier, 2 + has_above.astype(jnp.int32) + has_below.astype(jnp.int32))

        def part_of(index, part):
            start = pl.multiple_of(index * rows + part * half, half)
            return out_ref.at[pl.ds(start, half), :]

        own = pltpu.make_async_copy(x_ref, out_ref.at[pl.ds(pl.multiple_of(me * rows, rows), rows), :], own_sem)
        own.start()
        sent = []

        def push(condition, source, target, kind, slot, to_slot, part, device):
            copy = remote(source, target, send.at[kind, slot, part], recv.at[kind, to_slot, part], device)
            if condition is None:
                copy.start()
            else:
                pl.when(condition)(copy.start)
            sent.append((condition, copy))

        def arrived(index, kind, slot, part):
            target = part_of(index, part)
            remote(target, target, send.at[kind, slot, part], recv.at[kind, slot, part], to_x).wait_recv()

        def up_slot(distance):
            return distance

        def down_slot(distance):
            return depth - 1 + distance

        for part in (0, 1):
            mine = x_ref.at[pl.ds(part * half, half), :]
            push(has_above, mine, part_of(me, part), 0, 0, down_slot(1), part, me + 4)
            push(has_below, mine, part_of(me, part), 1, 0, up_slot(1), part, me - 4)
            mine_y = x_ref.at[pl.ds((1 - part) * half, half), :]
            push(None, mine, part_of(me, part), 2, 0, 0, part, to_x)
            push(None, mine_y, part_of(me, 1 - part), 3, 0, 0, 1 - part, to_y)

        def pass_on(condition, step, slot):
            def go():
                arrived(to_x + step, 2, slot, 0)
                copy_a.start()
                arrived(to_y + step, 3, slot, 1)
                copy_b.start()

            source_a, source_b = part_of(to_x + step, 0), part_of(to_y + step, 1)
            copy_a = remote(source_a, source_a, send.at[4, slot, 0], recv.at[4, slot, 0], to_y)
            copy_b = remote(source_b, source_b, send.at[5, slot, 1], recv.at[5, slot, 1], to_x)
            sent.append((condition, copy_a))
            sent.append((condition, copy_b))
            if condition is None:
                go()
            else:
                pl.when(condition)(go)

        for distance in range(1, depth):
            from_above, from_below = layer + distance < depth, layer - distance >= 0

            def take(kind, back_kind, step, slot, next_slot, onward, onward_device):
                for part in (0, 1):
                    arrived(me + step, kind, slot, part)
                    here = part_of(me + step, part)
                    if next_slot is not None:
                        pl.when(onward)(
                            remote(
                                here, here, send.at[kind, slot, part], recv.at[kind, next_slot, part], onward_device
                            ).start
                        )
                    remote(here, here, send.at[2, slot, part], recv.at[2, slot, part], to_x).start()
                    remote(here, here, send.at[3, slot, part], recv.at[3, slot, part], to_y).start()

            last = distance == depth - 1
            pl.when(from_above)(
                lambda: take(
                    1, 0, 4 * distance, up_slot(distance), None if last else up_slot(distance + 1), has_below, me - 4
                )
            )
            pl.when(from_below)(
                lambda: take(
                    0, 1, -4 * distance, down_slot(distance), None if last else down_slot(distance + 1), has_above, me + 4
                )
            )
            for condition, step, slot, kind, onward in (
                (from_above, 4 * distance, up_slot(distance), 1, has_below),
                (from_below, -4 * distance, down_slot(distance), 0, has_above),
            ):
                for part in (0, 1):
                    here = part_of(me + step, part)
                    if not last:
                        sent.append((condition & onward, remote(here, here, send.at[kind, slot, part], own_sem, me)))
                    sent.append((condition, remote(here, here, send.at[2, slot, part], own_sem, to_x)))
                    sent.append((condition, remote(here, here, send.at[3, slot, part], own_sem, to_y)))
            meanwhile(distance - 1, depth - 1)
            if distance == 1:
                pass_on(None, 0, 0)
            else:
                pass_on(layer + distance - 1 < depth, 4 * (distance - 1), up_slot(distance - 1))
                pass_on(layer - distance + 1 >= 0, -4 * (distance - 1), down_slot(distance - 1))
        pass_on(layer + depth - 1 < depth, 4 * (depth - 1), up_slot(depth - 1))
        pass_on(layer - depth + 1 >= 0, -4 * (depth - 1), down_slot(depth - 1))

        def close(step, slot):
            arrived(to_x + step, 2, slot, 1)
            arrived(to_y + step, 3, slot, 0)
            arrived(across + step, 4, slot, 0)
            arrived(across + step, 5, slot, 1)

        close(0, 0)
        for distance in range(1, depth):
            pl.when(layer + distance < depth)(lambda: close(4 * distance, up_slot(distance)))
            pl.when(layer - distance >= 0)(lambda: close(-4 * distance, down_slot(distance)))
        for condition, copy in sent:
            if condition is None:
                copy.wait_send()
            else:
                pl.when(condition)(copy.wait_send)
        own.wait()

    return pl.pallas_call(
        kernel,
        in_specs=[pl.BlockSpec(memory_space=pl.ANY), *specs],
        out_specs=[pl.BlockSpec(memory_space=pl.ANY)] + [pl.BlockSpec(memory_space=pltpu.VMEM)] * outs,
        out_shape=[jax.ShapeDtypeStruct((sources * rows, width), block.dtype), *more_out],
        scratch_shapes=[
            pltpu.SemaphoreType.DMA,
            pltpu.SemaphoreType.DMA((6, slots, 2)),
            pltpu.SemaphoreType.DMA((6, slots, 2)),
            *more_scratch,
        ],
        compiler_params=pltpu.CompilerParams(
            collective_id=collective_id, has_side_effects=True, vmem_limit_bytes=VMEM_LIMIT
        ),
        cost_estimate=lasting(50),
        name="gather_group",
    )(block, *arrays)


def reduce_steps(parts_ref, sources, refs, sems, merge, pack, beside=None):
    half_a, half_b, from_x, from_y, from_z, out_x, out_y, out_z = refs
    send, recv_a, recv_b, recv_x, recv_y, recv_z = sems
    rows = parts_ref.shape[0] // sources
    depth, half = sources // 4, rows // 2
    me, column, beside_x, beside_y, across, index_of = grid_place(depth)
    to_x, to_y = index_of(0, beside_x), index_of(0, beside_y)
    order = [*range(1, depth), 0]
    queues = {"x": [], "y": [], "z": []}
    first_limit = 2 if beside is None else depth

    def piece(index, part):
        return parts_ref.at[pl.ds(pl.multiple_of(index * rows + part * half, half), half), :]

    def part_rows(part):
        return pl.ds(part * half, half)

    def push(link, source, target, kind, k, recv_sem, device, limit=2):
        queue = queues[link]
        while link != "z" and len(queue) >= limit:
            queue.pop(0).wait_send()
        copy = remote(source, target, send.at[kind, k], recv_sem, device)
        copy.start()
        queue.append(copy)

    def arrived(target, recv_sem):
        remote(target, target, send.at[0, 0], recv_sem, to_x).wait_recv()

    def plane_rest(k):
        push("x", piece(index_of(k, beside_x), 0), from_x.at[k, part_rows(0)], 2, k, recv_x.at[0, k], to_x)
        push("y", piece(index_of(k, beside_y), 1), from_y.at[k, part_rows(1)], 3, k, recv_y.at[1, k], to_y)

    def plane_merged(k):
        arrived(half_a.at[k], recv_a.at[k])
        pack(out_y.at[k], merge([piece(index_of(k, beside_y), 0), half_a.at[k]]))
        push("y", out_y.at[k], from_y.at[k, part_rows(0)], 4, k, recv_y.at[0, k], to_y)
        arrived(half_b.at[k], recv_b.at[k])
        pack(out_x.at[k], merge([piece(index_of(k, beside_x), 1), half_b.at[k]]))
        push("x", out_x.at[k], from_x.at[k, part_rows(1)], 5, k, recv_x.at[1, k], to_x)

    def column_step(k):
        for part in (0, 1):
            here = part_rows(part)
            arrived(from_x.at[k, here], recv_x.at[part, k])
            arrived(from_y.at[k, here], recv_y.at[part, k])
            if k:
                blocks = [piece(index_of(k, column), part), from_x.at[k, here], from_y.at[k, here]]
                pack(out_z.at[k, here], merge(blocks))
        if k:
            push("z", out_z.at[k], from_z.at[k], 6, k, recv_z.at[k], index_of(k, column))

    for k in order:
        far = index_of(k, across)
        push("x", piece(far, 0), half_a.at[k], 0, k, recv_a.at[k], to_x, first_limit)
        push("y", piece(far, 1), half_b.at[k], 1, k, recv_b.at[k], to_y, first_limit)
    if beside is not None:
        beside()
    for i, k in enumerate(order):
        plane_rest(k)
        plane_merged(k)
        if i:
            column_step(order[i - 1])
    column_step(order[-1])
    for k in range(1, depth):
        arrived(from_z.at[k], recv_z.at[k])
    final = []
    for part in (0, 1):
        here = part_rows(part)
        blocks = [piece(me, part), from_x.at[0, here], from_y.at[0, here]]
        final.append((here, blocks + [from_z.at[k, here] for k in range(1, depth)]))
    return final, [copy for queue in queues.values() for copy in queue]


def reduce_scratch(rows, width, dtype, sources):
    depth, half = sources // 4, rows // 2

    def slots(size):
        return pltpu.VMEM((depth, size, width), dtype)

    refs = [slots(half), slots(half), slots(rows), slots(rows), slots(rows)]
    refs += [slots(half), slots(half), slots(rows)]
    sems = [pltpu.SemaphoreType.DMA((7, depth))]
    sems += [pltpu.SemaphoreType.DMA((depth,))] * 2
    sems += [pltpu.SemaphoreType.DMA((2, depth))] * 2
    sems += [pltpu.SemaphoreType.DMA((depth,))]
    return refs, sems


def run_alone(name, beside):
    arrays, specs, out_shape, scratch, begin = beside
    ins, outs = len(arrays), len(out_shape)

    def kernel(*refs):
        begin(refs[:ins], refs[ins : ins + outs], refs[ins + outs :])()

    return pl.pallas_call(
        kernel,
        in_specs=specs,
        out_specs=[pl.BlockSpec(memory_space=pltpu.VMEM)] * outs,
        out_shape=out_shape,
        scratch_shapes=scratch,
        compiler_params=pltpu.CompilerParams(vmem_limit_bytes=VMEM_LIMIT),
        cost_estimate=lasting(8),
        name=name,
    )(*arrays)


def reduce_group(parts, sources, collective_id, merge, pack, finish, out_shape, beside):
    rows, width = parts.shape[0] // sources, parts.shape[1]
    depth = sources // 4
    arrays, specs, more_out, more_scratch, begin = beside
    ref_shapes, sem_shapes = reduce_scratch(rows, width, parts.dtype, sources)
    sizes = [len(arrays), len(out_shape), len(more_out), len(ref_shapes), len(sem_shapes), len(more_scratch)]

    def kernel(parts_ref, *refs):
        groups, at = [], 0
        for size in sizes:
            groups.append(refs[at : at + size])
            at += size
        ins, out_refs, more_refs, steps_refs, steps_sems, scratch = groups
        meanwhile = begin(ins, more_refs, scratch)
        last = finish
        if finish is None:
            meanwhile, last = meanwhile
        me, column, beside_x, beside_y, across, index_of = grid_place(depth)
        greet(
            [index_of(0, beside_x), index_of(0, beside_y)]
            + [index_of(-k, column) for k in range(1, depth)]
        )
        final, still_open = reduce_steps(
            parts_ref, sources, steps_refs, steps_sems, merge, pack, meanwhile
        )
        for here, blocks in final:
            if finish is None:
                last(here, merge(blocks))
            else:
                last([out.at[here] for out in out_refs], merge(blocks))
        for copy in still_open:
            copy.wait_send()

    vmem = pl.BlockSpec(memory_space=pltpu.VMEM)
    return pl.pallas_call(
        kernel,
        in_specs=[vmem, *specs],
        out_specs=[vmem] * (len(out_shape) + len(more_out)),
        out_shape=[*out_shape, *more_out],
        scratch_shapes=[*ref_shapes, *sem_shapes, *more_scratch],
        compiler_params=pltpu.CompilerParams(
            collective_id=collective_id, has_side_effects=True, vmem_limit_bytes=VMEM_LIMIT
        ),
        cost_estimate=lasting(50),
        name="reduce_group",
    )(parts, *arrays)


def sum_queries(parts, d_queries, sources, collective_id, score_scale, beside):
    rows, width = d_queries.shape
    arrays, specs, (whole,), more_scratch, begin = beside

    def merge(blocks):
        total = blocks[0][...].astype(jnp.float32)
        for block in blocks[1:]:
            total = total + block[...].astype(jnp.float32)
        return total

    def pack(target, total):
        target[...] = total.astype(parts.dtype)

    def begin_both(ins, outs, scratch):
        run = begin(ins[:-1], outs, scratch)

        def finish(here, total):
            outs[0][here, :width] = (ins[-1][here, :] + total * score_scale).astype(whole.dtype)

        return run, finish

    more = [*arrays, d_queries], [*specs, pl.BlockSpec(memory_space=pltpu.VMEM)], [whole], more_scratch, begin_both
    return reduce_group(parts, sources, collective_id, merge, pack, None, [], more)[0]


def merge_partials(parts, sources, collective_id, heads, beside):
    rows, width = parts.shape[0] // sources, parts.shape[1] - 128
    head_dim = width // heads

    def merge(blocks):
        stats = []
        for block in blocks:
            stat = block[:, width:].astype(jnp.float32)
            stats.append(stat + pltpu.roll(stat, 128 - 16, 1) + pltpu.roll(stat, 128 - 32, 1))
        top = stats[0]
        for stat in stats[1:]:
            top = jnp.maximum(top, stat)
        fades = [jnp.exp(stat - top) for stat in stats]
        total = sum(fade * pltpu.roll(stat, 128 - heads, 1) for fade, stat in zip(fades, stats))
        sums = []
        for head in range(heads):
            columns = slice(head * head_dim, (head + 1) * head_dim)
            sums.append(
                sum(
                    block[:, columns].astype(jnp.float32) * fade[:, head : head + 1]
                    for block, fade in zip(blocks, fades)
                )
            )
        return sums, top, total

    def pack(target, merged):
        sums, top, total = merged
        for head in range(heads):
            target[:, head * head_dim : (head + 1) * head_dim] = sums[head].astype(parts.dtype)
        lane = lax.broadcasted_iota(jnp.int32, top.shape, 1)
        stat = jnp.where(lane < heads, top, jnp.where(lane < 16, pltpu.roll(total, heads, 1), 0.0))
        target[:, width:] = triple(stat + pltpu.roll(stat, 16, 1) + pltpu.roll(stat, 32, 1))

    def finish(targets, merged):
        sums, top, total = merged
        live = total > 0
        total = jnp.where(live, total, 1.0)
        targets[1][...] = jnp.where(live, top + jnp.log(total), 0.0)
        for head in range(heads):
            targets[0][:, head * head_dim : (head + 1) * head_dim] = sums[head] / total[:, head : head + 1]

    out_shape = [
        jax.ShapeDtypeStruct((rows, width), jnp.float32),
        jax.ShapeDtypeStruct((rows, 128), jnp.float32),
    ]
    return reduce_group(parts, sources, collective_id, merge, pack, finish, out_shape, beside)


def scattered(halves):
    return lax.psum_scatter(halves, "mem", scatter_dimension=0, tiled=True)


def same_book(lengths_ref, first_row, rows, first_lane, lanes):
    row = lax.broadcasted_iota(jnp.int32, (rows, lanes), 0) + first_row
    lane = lax.broadcasted_iota(jnp.int32, (rows, lanes), 1) + first_lane
    end, same = 0, lane >= 0
    for i in range(lengths_ref.shape[1]):
        end = end + lengths_ref[0, i]
        same = same & ((row >= end) == (lane >= end))
    return same


def lane_tile(columns, rows):
    lane = lax.broadcasted_iota(jnp.int32, (rows, 128), 1)
    tile = jnp.zeros((rows, 128), jnp.float32)
    for i, column in enumerate(columns):
        tile = jnp.where(lane == i, column, tile)
    return tile


def split_tile(tile):
    lane = lax.broadcasted_iota(jnp.int32, tile.shape, 1)
    kept = jnp.where(lane < 32, tile, 0.0)
    kept = kept + pltpu.roll(kept, 32, 1) + pltpu.roll(kept, 64, 1)
    high = kept.astype(jnp.bfloat16).astype(jnp.float32)
    middle = (kept - high).astype(jnp.bfloat16).astype(jnp.float32)
    low = kept - high - middle
    part = lane // 32
    return jnp.where(part == 0, high, jnp.where(part == 1, middle, low)).astype(jnp.bfloat16)


def joined_tile(tile):
    tile = tile.astype(jnp.float32)
    return tile + pltpu.roll(tile, 128 - 32, 1) + pltpu.roll(tile, 128 - 64, 1)


def slanted(base, rows):
    return pltpu.roll(jnp.broadcast_to(base, (rows, base.shape[1])), 0, 1, stride=1, stride_axis=0)


def local_forward(base, lengths, own, halos, heads, score_scale):
    rows, width = own.shape[0], own.shape[1] // 3
    head_dim = width // heads
    count = len(halos) + 1

    def begin(ins, outs, scratch):
        base_ref, lengths_ref, own_ref, *halo_refs = ins
        out_ref, log_ref = outs

        def run():
            first = lax.axis_index("mem") * rows
            same = same_book(lengths_ref, first, rows, first - (count - 1) * rows, count * rows)
            logs = []
            for head in range(heads):
                columns = slice(head * head_dim, (head + 1) * head_dim)
                above = slice(width + head * head_dim, width + (head + 1) * head_dim)
                twice = slice(2 * width + head * head_dim, 2 * width + (head + 1) * head_dim)
                keys = [ref[:, columns] for ref in halo_refs] + [own_ref[:, above]]
                values = [ref[:, above] for ref in halo_refs] + [own_ref[:, twice]]
                q = own_ref[:, columns]
                raw = [
                    lax.dot_general(q, k, contract_cols, preferred_element_type=jnp.float32) for k in keys
                ]
                bias = slanted(base_ref[head : head + 1, :], rows)[:, : count * rows]
                scores = jnp.concatenate(raw, axis=1) * score_scale + bias
                scores = jnp.where(same, scores, masked_score)
                top = jnp.max(scores, axis=1, keepdims=True)
                weights = jnp.exp(scores - top)
                total = jnp.sum(weights, axis=1, keepdims=True)
                weights = (weights / total).astype(jnp.bfloat16)
                out_ref[:, columns] = sum(
                    jnp.dot(
                        weights[:, i * rows : (i + 1) * rows], v, preferred_element_type=jnp.float32
                    )
                    for i, v in enumerate(values)
                )
                logs.append(top + jnp.log(total))
            log_ref[...] = lane_tile(logs, rows)

        return run

    arrays = [base, lengths, own, *halos]
    vmem = pl.BlockSpec(memory_space=pltpu.VMEM)
    specs = [vmem, pl.BlockSpec(memory_space=pltpu.SMEM)] + [vmem] * (1 + len(halos))
    out_shape = [
        jax.ShapeDtypeStruct((rows, width), jnp.float32),
        jax.ShapeDtypeStruct((rows, 128), jnp.float32),
    ]
    return arrays, specs, out_shape, [], begin


def local_queries(
    base, lengths, own, halos, d_mixed, local_out, local_log, share, heads, score_scale
):
    rows, width = d_mixed.shape
    head_dim = width // heads
    count = len(halos) + 1
    span = base.shape[1]

    def begin(ins, outs, scratch):
        base_ref, lengths_ref, own_ref, mix_ref, loc_ref, log_ref, share_ref, *halo_refs = ins
        dq_ref, diagonal_ref = outs

        def some_heads(some):
            first = lax.axis_index("mem") * rows
            same = same_book(lengths_ref, first, rows, first - (count - 1) * rows, count * rows)
            turned = (
                lax.broadcasted_iota(jnp.int32, (rows, rows), 0)
                + lax.broadcasted_iota(jnp.int32, (rows, rows), 1)
                == rows - 1
            ).astype(jnp.bfloat16)
            for head in some:
                columns = slice(head * head_dim, (head + 1) * head_dim)
                above = slice(width + head * head_dim, width + (head + 1) * head_dim)
                twice = slice(2 * width + head * head_dim, 2 * width + (head + 1) * head_dim)
                keys = [ref[:, columns] for ref in halo_refs] + [own_ref[:, above]]
                values = [ref[:, above] for ref in halo_refs] + [own_ref[:, twice]]
                q = own_ref[:, columns]
                d_out = ((1.0 - share_ref[head]) * mix_ref[:, columns]).astype(jnp.bfloat16)
                delta = jnp.sum(
                    d_out.astype(jnp.float32) * loc_ref[:, columns], axis=1, keepdims=True
                )
                raw = [
                    lax.dot_general(q, k, contract_cols, preferred_element_type=jnp.float32)
                    for k in keys
                ]
                bias = slanted(base_ref[head : head + 1, :], rows)[:, : count * rows]
                scores = jnp.concatenate(raw, axis=1) * score_scale + bias
                probs = jnp.exp(jnp.where(same, scores - log_ref[:, head : head + 1], masked_score))
                products = [
                    lax.dot_general(d_out, v, contract_cols, preferred_element_type=jnp.float32)
                    for v in values
                ]
                slopes = (probs * (jnp.concatenate(products, axis=1) - delta)).astype(jnp.bfloat16)
                slope_blocks = [slopes[:, i * rows : (i + 1) * rows] for i in range(count)]
                dq_ref[:, columns] = score_scale * sum(
                    jnp.dot(s, k, preferred_element_type=jnp.float32)
                    for s, k in zip(slope_blocks, keys)
                )
                mirrored = [
                    jnp.dot(s, turned, preferred_element_type=jnp.float32) for s in slope_blocks[::-1]
                ]
                mirrored.append(jnp.zeros((rows, span - count * rows), jnp.float32))
                leaned = pltpu.roll(jnp.concatenate(mirrored, axis=1), 0, 1, stride=1, stride_axis=0)
                diagonal_ref[head : head + 1, :] = jnp.sum(leaned, axis=0, keepdims=True)

        def run(part=0, parts=1):
            some_heads(range(part * heads // parts, (part + 1) * heads // parts))

        return run

    vmem = pl.BlockSpec(memory_space=pltpu.VMEM)
    smem = pl.BlockSpec(memory_space=pltpu.SMEM)
    arrays = [base, lengths, own, d_mixed, local_out, local_log, share, *halos]
    specs = [vmem, smem] + [vmem] * 4 + [smem] + [vmem] * len(halos)
    out_shape = [
        jax.ShapeDtypeStruct((rows, width), jnp.float32),
        jax.ShapeDtypeStruct((heads, span), jnp.float32),
    ]
    return arrays, specs, out_shape, [], begin


def local_keys(base, lengths, own, queries, sent, ratio, count, heads, score_scale):
    rows, width = own.shape[0], own.shape[1] // 3
    head_dim = width // heads
    groups = queries.shape[0] // rows

    def begin(ins, outs, scratch):
        base_ref, lengths_ref, own_ref, ratio_ref, queries_ref, sent_ref = ins
        (out_ref,) = outs
        queries_here, sent_here, sems = scratch
        copies = []
        for i in range(count):
            index = jnp.minimum(lax.axis_index("mem") + i, groups - 1)
            there = pl.ds(pl.multiple_of(index * rows, rows), rows)
            copies.append(
                pltpu.make_async_copy(queries_ref.at[there, :], queries_here.at[i], sems.at[0, i])
            )
            copies.append(pltpu.make_async_copy(sent_ref.at[there, :], sent_here.at[i], sems.at[1, i]))
        for copy in copies:
            copy.start()

        def run():
            for copy in copies:
                copy.wait()
            first = lax.axis_index("mem") * rows
            same = same_book(lengths_ref, first, rows, first, count * rows)
            stats = jnp.concatenate([joined_tile(sent_here[i, :, width:]).T for i in range(count)], axis=1)
            for head in range(heads):
                columns = slice(head * head_dim, (head + 1) * head_dim)
                above = slice(width + head * head_dim, width + (head + 1) * head_dim)
                twice = slice(2 * width + head * head_dim, 2 * width + (head + 1) * head_dim)
                k, v = own_ref[:, above], own_ref[:, twice]
                qs = [queries_here[i, :, columns] for i in range(count)]
                gs = [
                    (sent_here[i, :, columns].astype(jnp.float32) * ratio_ref[head]).astype(jnp.bfloat16)
                    for i in range(count)
                ]
                raw = [
                    lax.dot_general(k, q, contract_cols, preferred_element_type=jnp.float32) for q in qs
                ]
                bias = slanted(base_ref[head : head + 1, :], rows)[:, : count * rows]
                scores = jnp.concatenate(raw, axis=1) * score_scale + bias
                log = stats[2 * heads + head : 2 * heads + head + 1, :]
                delta = stats[3 * heads + head : 3 * heads + head + 1, :]
                probs = jnp.exp(jnp.where(same, scores - log, masked_score))
                products = [
                    lax.dot_general(v, g, contract_cols, preferred_element_type=jnp.float32) for g in gs
                ]
                slopes = (probs * (jnp.concatenate(products, axis=1) - delta)).astype(jnp.bfloat16)
                weights = probs.astype(jnp.bfloat16)
                blocks = [slice(i * rows, (i + 1) * rows) for i in range(count)]
                d_key = sum(
                    jnp.dot(slopes[:, b], q, preferred_element_type=jnp.float32) for b, q in zip(blocks, qs)
                )
                d_value = sum(
                    jnp.dot(weights[:, b], g, preferred_element_type=jnp.float32)
                    for b, g in zip(blocks, gs)
                )
                out_ref[:, above] = (d_key * score_scale).astype(jnp.bfloat16)
                out_ref[:, twice] = d_value.astype(jnp.bfloat16)

        return run

    vmem, anywhere = pl.BlockSpec(memory_space=pltpu.VMEM), pl.BlockSpec(memory_space=pl.ANY)
    smem = pl.BlockSpec(memory_space=pltpu.SMEM)
    arrays = [base, lengths, own, ratio, queries, sent]
    specs = [vmem, smem, vmem, smem, anywhere, anywhere]
    scratch = [
        pltpu.VMEM((count, rows, width), jnp.bfloat16),
        pltpu.VMEM((count, rows, width + 128), jnp.bfloat16),
        pltpu.SemaphoreType.DMA((2, count)),
    ]
    return arrays, specs, [jax.ShapeDtypeStruct((rows, 3 * width), jnp.bfloat16)], scratch, begin


def middle(
    tokens,
    memory_out,
    local_out,
    mem_log,
    local_log,
    share,
    out_weight,
    ffn_gain,
    up_weight,
    down_weight,
    cotangent,
    heads,
):
    rows, width = tokens.shape
    head_dim = width // heads
    hidden = up_weight.shape[1]
    block = math.gcd(hidden, 1024)
    steps = hidden // block

    def kernel(
        tokens_ref, mem_ref, loc_ref, mem_log_ref, log_ref, share_ref, out_w_ref, gain_ref, up_ref, down_ref, cot_ref, *refs
    ):
        mixed_ref, mid_ref, act_ref, d_up_ref, block_ref, d_res_ref, gain_part_ref, d_branch_ref, d_mix_ref = refs[:9]
        gate_ref, sent_ref, residual, branch_sum, d_mid_sum = refs[9:]
        i = pl.program_id(0)

        def scale_of(values):
            return lax.rsqrt(jnp.mean(values * values, axis=1, keepdims=True) + eps_norm)

        @pl.when(i == 0)
        def _():
            for head in range(heads):
                columns = slice(head * head_dim, (head + 1) * head_dim)
                part = share_ref[head]
                mixed_ref[:, columns] = (
                    part * mem_ref[:, columns] + (1.0 - part) * loc_ref[:, columns]
                ).astype(jnp.bfloat16)
            values = tokens_ref[...].astype(jnp.float32) + jnp.dot(
                mixed_ref[...], out_w_ref[...], preferred_element_type=jnp.float32
            )
            residual[...] = values
            mid_ref[...] = (values * scale_of(values) * gain_ref[...]).astype(jnp.bfloat16)
            branch_sum[...] = jnp.zeros_like(branch_sum)
            d_mid_sum[...] = jnp.zeros_like(d_mid_sum)

        up = jnp.dot(mid_ref[...], up_ref[...], preferred_element_type=jnp.float32)
        d_act = jnp.dot(cot_ref[...], down_ref[...], preferred_element_type=jnp.float32)
        below = 0.5 * (1.0 + lax.erf(up * math.sqrt(0.5)))
        density = jnp.exp(-0.5 * up * up) * (1.0 / math.sqrt(2.0 * math.pi))
        act = (up * below).astype(jnp.bfloat16)
        d_up = (d_act * (below + up * density)).astype(jnp.bfloat16)
        act_ref[...] = act
        d_up_ref[...] = d_up
        branch_sum[...] += lax.dot_general(
            act, down_ref[...], contract_cols, preferred_element_type=jnp.float32
        )
        d_mid_sum[...] += lax.dot_general(
            d_up, up_ref[...], contract_cols, preferred_element_type=jnp.float32
        )

        @pl.when(i == steps - 1)
        def _():
            values, d_mid = residual[...], d_mid_sum[...]
            block_ref[...] = (values + branch_sum[...]).astype(jnp.bfloat16)
            scale = scale_of(values)
            wanted = d_mid * gain_ref[...]
            slope = jnp.mean(values * wanted, axis=1, keepdims=True) * scale * scale * scale
            d_res = cot_ref[...].astype(jnp.float32) + scale * wanted - values * slope
            d_res_ref[...] = d_res
            gain_part_ref[...] = jnp.sum(d_mid * values * scale, axis=0, keepdims=True)
            d_branch_ref[...] = d_res.astype(jnp.bfloat16)
            d_mix_ref[...] = lax.dot_general(
                d_branch_ref[...], out_w_ref[...], contract_cols, preferred_element_type=jnp.float32
            )
            mem_deltas, deltas = [], []
            for head in range(heads):
                columns = slice(head * head_dim, (head + 1) * head_dim)
                part = share_ref[head]
                d_mix, mem_here, loc_here = d_mix_ref[:, columns], mem_ref[:, columns], loc_ref[:, columns]
                d_mem = (part * d_mix).astype(jnp.bfloat16)
                d_out = ((1.0 - part) * d_mix).astype(jnp.bfloat16)
                sent_ref[:, columns] = d_mem
                mem_deltas.append(
                    jnp.sum(d_mem.astype(jnp.float32) * mem_here, axis=1, keepdims=True)
                )
                deltas.append(jnp.sum(d_out.astype(jnp.float32) * loc_here, axis=1, keepdims=True))
                gate_ref[head : head + 1, :] = jnp.sum(
                    d_mix * (mem_here - loc_here), axis=0, keepdims=True
                )
            mem_logs = [mem_log_ref[:, head : head + 1] for head in range(heads)]
            logs = [log_ref[:, head : head + 1] for head in range(heads)]
            sent_ref[:, width:] = split_tile(lane_tile(mem_logs + mem_deltas + logs + deltas, rows))

    def whole(*shape):
        return pl.BlockSpec(shape, lambda i: (0, 0))

    weight = pl.BlockSpec((width, block), lambda i: (0, i))
    column = pl.BlockSpec((rows, block), lambda i: (0, i))
    full = whole(rows, width)
    low, high = jnp.bfloat16, jnp.float32
    outs = [
        (full, (rows, width), low),
        (full, (rows, width), low),
        (column, (rows, hidden), low),
        (column, (rows, hidden), low),
        (full, (rows, width), low),
        (full, (rows, width), high),
        (whole(1, width), (1, width), high),
        (full, (rows, width), low),
        (full, (rows, width), high),
        (whole(heads, head_dim), (heads, head_dim), high),
        (whole(rows, width + 128), (rows, width + 128), low),
    ]
    return pl.pallas_call(
        kernel,
        grid=(steps,),
        in_specs=[full, full, full, whole(rows, 128), whole(rows, 128)]
        + [pl.BlockSpec(memory_space=pltpu.SMEM)]
        + [whole(width, width), whole(1, width), weight, weight, full],
        out_specs=[spec for spec, _, _ in outs],
        out_shape=[jax.ShapeDtypeStruct(shape, dtype) for _, shape, dtype in outs],
        scratch_shapes=[pltpu.VMEM((rows, width), jnp.float32)] * 3,
        compiler_params=pltpu.CompilerParams(vmem_limit_bytes=VMEM_LIMIT),
        cost_estimate=lasting(18),
        name="middle",
    )(
        tokens,
        memory_out,
        local_out,
        mem_log,
        local_log,
        share,
        out_weight,
        ffn_gain[None, :],
        up_weight,
        down_weight,
        cotangent,
    )


def exchange_pairs(lefts, rights, other_lefts, other_right, send, recv):
    core = lax.axis_index("dp")
    copies, at = [], 0

    def push(source, target):
        i = len(copies)
        copy = pltpu.make_async_remote_copy(
            src_ref=source,
            dst_ref=target,
            send_sem=send.at[i],
            recv_sem=recv.at[i],
            device_id={"dp": 1 - core},
            device_id_type=pl.DeviceIdType.MESH,
        )
        copy.start()
        copies.append(copy)

    for i, (left, right) in enumerate(zip(lefts, rights)):
        half = right.shape[1] // 2
        push(left, other_lefts.at[i])
        there = pl.ds(pl.multiple_of((1 - core) * half, 128), half)
        push(right.at[:, there], other_right.at[:, pl.ds(at, half)])
        at += half
    return copies


def pair_products(lefts, rights, other_lefts, other_right, turned, store, copies):
    core = lax.axis_index("dp")
    rows = lefts[0].shape[0]
    at = 0
    for i, (left, right) in enumerate(zip(lefts, rights)):
        half = right.shape[1] // 2
        for copy in copies[2 * i : 2 * i + 2]:
            copy.wait_recv()
        turned[:, :rows] = left[...].T
        turned[:, rows:] = other_lefts[i].T
        block = math.gcd(half, 512)
        for column in range(0, half, block):
            kept = right[:, pl.ds(pl.multiple_of(core * half + column, 128), block)]
            both = jnp.concatenate([kept, other_right[:, at + column : at + column + block]], axis=0)
            store(
                at + column,
                jnp.dot(turned[...], both, preferred_element_type=jnp.float32).astype(jnp.bfloat16),
            )
        at += half


def pair_scratch(lefts, rights):
    rows, width = lefts[0].shape
    count = len(lefts)
    return [
        pltpu.VMEM((count, rows, width), jnp.bfloat16),
        pltpu.VMEM((rows, sum(right.shape[1] for right in rights) // 2), jnp.bfloat16),
        pltpu.VMEM((width, 2 * rows), jnp.bfloat16),
        pltpu.SemaphoreType.DMA((2 * count,)),
        pltpu.SemaphoreType.DMA((2 * count,)),
    ]


def pair_grads(lefts, rights, collective_id):
    count, width = len(lefts), lefts[0].shape[1]
    total = sum(right.shape[1] for right in rights) // 2
    block = math.gcd(*[right.shape[1] // 2 for right in rights], 512)

    def kernel(*refs):
        left_refs, right_refs, out_ref = refs[:count], refs[count : 2 * count], refs[2 * count]
        other_lefts, other_right, turned, send, recv, staged, out_sem = refs[2 * count + 1 :]
        barrier = pltpu.get_barrier_semaphore()
        partner = {"dp": 1 - lax.axis_index("dp")}
        pl.semaphore_signal(barrier, inc=1, device_id=partner, device_id_type=pl.DeviceIdType.MESH)
        pl.semaphore_wait(barrier, 1)
        copies = exchange_pairs(left_refs, right_refs, other_lefts, other_right, send, recv)
        written = []

        def store(column, value):
            slot = len(written) % 2
            if len(written) >= 2:
                written[-2].wait()
            staged[slot] = value
            copy = pltpu.make_async_copy(
                staged.at[slot], out_ref.at[:, pl.ds(column, block)], out_sem.at[slot]
            )
            copy.start()
            written.append(copy)

        pair_products(left_refs, right_refs, other_lefts, other_right, turned, store, copies)
        for copy in written[-2:]:
            copy.wait()
        for copy in copies:
            copy.wait_send()

    vmem = pl.BlockSpec(memory_space=pltpu.VMEM)
    return pl.pallas_call(
        kernel,
        in_specs=[vmem] * (2 * count),
        out_specs=pl.BlockSpec(memory_space=pl.ANY),
        out_shape=jax.ShapeDtypeStruct((width, total), jnp.bfloat16),
        scratch_shapes=pair_scratch(lefts, rights)
        + [pltpu.VMEM((2, width, block), jnp.bfloat16), pltpu.SemaphoreType.DMA((2,))],
        compiler_params=pltpu.CompilerParams(
            collective_id=collective_id, has_side_effects=True, vmem_limit_bytes=VMEM_LIMIT
        ),
        cost_estimate=lasting(10),
        name="pair_grads",
    )(*lefts, *rights)


def input_backward(tokens, attn_gain, d_projected, qkv_weight, d_residual):
    rows, width = tokens.shape

    def begin(ins, outs, scratch):
        tokens_ref, gain_ref, d_ref, weight_ref, residual_ref = ins
        grad_ref, part_ref = outs
        weight_here, sem = scratch
        copy = pltpu.make_async_copy(weight_ref, weight_here, sem)
        copy.start()

        def run():
            copy.wait()
            d_in = lax.dot_general(
                d_ref[...], weight_here[...], contract_cols, preferred_element_type=jnp.float32
            )
            x = tokens_ref[...].astype(jnp.float32)
            scale = lax.rsqrt(jnp.mean(x * x, axis=1, keepdims=True) + eps_norm)
            wanted = d_in * gain_ref[...]
            slope = jnp.mean(x * wanted, axis=1, keepdims=True) * scale * scale * scale
            grad_ref[...] = residual_ref[...] + scale * wanted - x * slope
            part_ref[...] = jnp.sum(d_in * x * scale, axis=0, keepdims=True)

        return run

    vmem = pl.BlockSpec(memory_space=pltpu.VMEM)
    arrays = [tokens, attn_gain[None, :], d_projected, qkv_weight, d_residual]
    specs = [vmem, vmem, vmem, pl.BlockSpec(memory_space=pl.ANY), vmem]
    out_shape = [
        jax.ShapeDtypeStruct((rows, width), jnp.float32),
        jax.ShapeDtypeStruct((1, width), jnp.float32),
    ]
    scratch = [pltpu.VMEM(qkv_weight.shape, qkv_weight.dtype), pltpu.SemaphoreType.DMA]
    return arrays, specs, out_shape, scratch, begin


def spread_halves(halves, outs):
    at = 0
    for out in outs:
        half = out.shape[1] // 2
        for c in (0, 1):
            out[:, c * half : (c + 1) * half] = halves[c, :, at : at + half].astype(jnp.float32)
        at += half


def join_halves(sums, collective_id):
    def kernel(sums_ref, both, send, recv):
        core = lax.axis_index("dp")
        partner = {"dp": 1 - core}
        barrier = pltpu.get_barrier_semaphore()
        pl.semaphore_signal(barrier, inc=1, device_id=partner, device_id_type=pl.DeviceIdType.MESH)
        pl.semaphore_wait(barrier, 1)
        copy = pltpu.make_async_remote_copy(
            src_ref=sums_ref,
            dst_ref=both.at[core],
            send_sem=send,
            recv_sem=recv,
            device_id=partner,
            device_id_type=pl.DeviceIdType.MESH,
        )
        copy.start()
        both[core] = sums_ref[...]
        copy.wait()

    vmem = pl.BlockSpec(memory_space=pltpu.VMEM)
    return pl.pallas_call(
        kernel,
        in_specs=[vmem],
        out_specs=vmem,
        out_shape=jax.ShapeDtypeStruct((2, *sums.shape), sums.dtype),
        scratch_shapes=[pltpu.SemaphoreType.DMA, pltpu.SemaphoreType.DMA],
        compiler_params=pltpu.CompilerParams(
            collective_id=collective_id, has_side_effects=True, vmem_limit_bytes=VMEM_LIMIT
        ),
        cost_estimate=lasting(4),
        name="join_halves",
    )(sums)


def write_results(late, late_widths, early, early_widths, small, input_grad, heads, buckets):
    rows, width = late.shape[1], late.shape[2] * 2 // 3
    lines = width // 128
    count = len(late_widths) + len(early_widths)

    def kernel(late_ref, early_ref, small_ref, input_ref, *outs):
        spread_halves(late_ref, outs[: len(late_widths)])
        spread_halves(early_ref, outs[len(late_widths) : count])
        attn_ref, ffn_ref, bias_ref, gate_ref, grad_ref = outs[count:]
        grad_ref[...] = input_ref[...]
        attn_ref[...] = small_ref[:lines, :]
        ffn_ref[...] = small_ref[lines : 2 * lines, :]
        for head in range(heads):
            line, lane = divmod(head * buckets, 128)
            here = small_ref[2 * lines + line : 2 * lines + line + 1, :]
            bias_ref[head : head + 1, :] = here[:, lane : lane + buckets]
        line = 2 * lines + heads * buckets // 128
        gate_ref[...] = small_ref[line : line + 1, :heads]

    shapes = [(rows, size) for size in [*late_widths, *early_widths]]
    shapes += [(lines, 128), (lines, 128), (heads, buckets), (1, heads), input_grad.shape]
    return pl.pallas_call(
        kernel,
        out_shape=[jax.ShapeDtypeStruct(shape, jnp.float32) for shape in shapes],
        compiler_params=pltpu.CompilerParams(vmem_limit_bytes=VMEM_LIMIT),
        cost_estimate=lasting(3),
        name="write_results",
    )(late, early, small, input_grad)


def finish_grads(lefts, rights, small, sources, collective_id, beside):
    width, total = lefts[0].shape[1], sum(right.shape[1] for right in rights) // 2
    rows = width // sources
    count = len(lefts)
    arrays, specs, more_out, more_scratch, begin = beside
    mesh_type = pl.DeviceIdType.MESH
    ref_shapes, sem_shapes = reduce_scratch(rows, total, jnp.bfloat16, sources)
    pair_shapes = pair_scratch(lefts, rights)
    sizes = [count, count, len(arrays), 1, 1, 1, len(more_out)]
    sizes += [len(ref_shapes), len(sem_shapes), len(pair_shapes), len(more_scratch), 8]

    def kernel(*refs):
        groups, at = [], 0
        for size in sizes:
            groups.append(refs[at : at + size])
            at += size
        left_refs, right_refs, ins, (small_ref,), (late,), (small_out,), more_refs = groups[:7]
        steps_refs, steps_sems, (other_lefts, other_right, turned, pair_send, pair_recv), scratch, own = groups[7:]
        parts, small_mine, smalls, core_small, small_send, small_recv, core_send, core_recv = own
        meanwhile = begin(ins, more_refs, scratch)
        me, core = lax.axis_index("mem"), lax.axis_index("dp")
        barrier = pltpu.get_barrier_semaphore()
        peers = [lax.rem(me + k, sources) for k in range(1, sources)]
        for peer in peers:
            pl.semaphore_signal(barrier, inc=1, device_id={"mem": peer}, device_id_type=mesh_type)
        pl.semaphore_signal(barrier, inc=1, device_id={"dp": 1 - core}, device_id_type=mesh_type)
        pl.semaphore_wait(barrier, sources)

        def merge(blocks):
            total = blocks[0][...].astype(jnp.float32)
            for block in blocks[1:]:
                total = total + block[...].astype(jnp.float32)
            return total

        def pack(target, total):
            target[...] = total.astype(jnp.bfloat16)

        def across_cores(source, target, i):
            copy = pltpu.make_async_remote_copy(
                src_ref=source,
                dst_ref=target,
                send_sem=core_send.at[i],
                recv_sem=core_recv.at[i],
                device_id={"dp": 1 - core},
                device_id_type=mesh_type,
            )
            copy.start()
            return copy

        pair_copies = exchange_pairs(
            left_refs, right_refs, other_lefts, other_right, pair_send, pair_recv
        )

        def store(column, value):
            parts[:, column : column + value.shape[1]] = value

        pair_products(
            left_refs, right_refs, other_lefts, other_right, turned, store, pair_copies
        )
        small_copies = [
            remote(small_mine, smalls.at[me], small_send.at[i], small_recv.at[me], peer)
            for i, peer in enumerate(peers)
        ]

        def between():
            meanwhile()
            small_mine[...] = small_ref[...]
            for i in range(width // 128):
                small_mine[i : i + 1, :] = more_refs[-1][:, i * 128 : (i + 1) * 128]
            smalls[me] = small_mine[...]
            for copy in small_copies:
                copy.start()

        final, still_open = reduce_steps(parts, sources, steps_refs, steps_sems, merge, pack, between)
        for here, blocks in final:
            late[core, here] = merge(blocks).astype(jnp.bfloat16)
        late_copy = across_cores(late.at[core], late.at[core], 0)
        for peer in peers:
            remote(
                smalls.at[peer], smalls.at[peer], small_send.at[0], small_recv.at[peer], peer
            ).wait_recv()
        group_small = smalls[0]
        for i in range(1, sources):
            group_small = group_small + smalls[i]
        core_small[0] = group_small
        small_copy = across_cores(core_small.at[0], core_small.at[1], 1)
        for copy in (late_copy, small_copy):
            copy.wait()
        small_out[...] = core_small[0] + core_small[1]
        for copy in still_open + small_copies + pair_copies:
            copy.wait_send()

    vmem = pl.BlockSpec(memory_space=pltpu.VMEM)
    return pl.pallas_call(
        kernel,
        in_specs=[vmem] * (2 * count) + specs + [vmem],
        out_specs=[vmem] * (2 + len(more_out)),
        out_shape=[jax.ShapeDtypeStruct((2, rows, total), jnp.bfloat16)]
        + [jax.ShapeDtypeStruct(small.shape, small.dtype)]
        + more_out,
        scratch_shapes=ref_shapes
        + sem_shapes
        + pair_shapes
        + more_scratch
        + [
            pltpu.VMEM((width, total), jnp.bfloat16),
            pltpu.VMEM(small.shape, small.dtype),
            pltpu.VMEM((sources, *small.shape), small.dtype),
            pltpu.VMEM((2, *small.shape), small.dtype),
        ]
        + [pltpu.SemaphoreType.DMA((sources,))] * 2
        + [pltpu.SemaphoreType.DMA((2,))] * 2,
        compiler_params=pltpu.CompilerParams(
            collective_id=collective_id, has_side_effects=True, vmem_limit_bytes=VMEM_LIMIT
        ),
        cost_estimate=lasting(45),
        name="finish_grads",
    )(*lefts, *rights, *arrays, small)


def on_device(
    tokens,
    attn_gain,
    qkv_weight,
    out_weight,
    bias_table,
    gate_logit,
    ffn_gain,
    up_weight,
    down_weight,
    memory_keys,
    memory_values,
    book_lengths,
    slot_shard,
    slot_index,
    slot_live,
    cotangent,
):
    rows, width = tokens.shape
    heads, buckets = bias_table.shape
    head_dim = width // heads
    top_count = slot_index.shape[2]
    hidden = up_weight.shape[1]
    groups = lax.axis_size("mem")
    capacity = -(-3 * rows * heads * top_count // (2 * groups) // 128) * 128
    score_scale = 1.0 / math.sqrt(head_dim)
    repeats = W // rows
    span = W + 2 * rows
    before = W - jnp.arange(span, dtype=jnp.int32)
    after = jnp.arange(span, dtype=jnp.int32)

    def bias_rows(offset):
        reached = (offset >= 0) & (offset < W)
        hot = (bucket_of(offset)[:, None] == jnp.arange(buckets, dtype=jnp.int32)) & reached[:, None]
        rows_of_bias = jnp.einsum(
            "rb,hb->hr", hot.astype(jnp.float32), bias_table, precision=lax.Precision.HIGHEST
        )
        return rows_of_bias + jnp.where(reached, 0.0, masked_score)

    before_bias, after_bias = bias_rows(before), bias_rows(after)
    bucket = bucket_of(jnp.arange(W, dtype=jnp.int32))
    one_hot = (bucket[:, None] == jnp.arange(buckets, dtype=jnp.int32)).astype(jnp.float32)
    tokens_f = tokens.astype(jnp.float32)
    normed_in = normed(tokens_f, attn_gain).astype(jnp.bfloat16)
    projected = jnp.dot(normed_in, qkv_weight, preferred_element_type=jnp.float32).astype(
        jnp.bfloat16
    )
    slots = memory_keys.shape[0]
    requests = place_requests(slot_shard, slot_index, slot_live, groups, capacity, slots)
    incoming = lax.all_to_all(requests, "mem", split_axis=0, concat_axis=0, tiled=True)
    keys_values, _ = lax.optimization_barrier((projected[:, width:], requests))
    distances = list(range(repeats, 0, -1))
    halos = [passed_along(keys_values, "mem", distance) for distance in distances[: repeats // 2]]
    index, row_ids, bounds = read_lists(incoming, heads, rows, slots)
    bounds = bounds.reshape(-1)
    index, before_bias, after_bias = lax.optimization_barrier((index, before_bias, after_bias))
    key_rows, value_rows = gather_rows(
        index.reshape(-1), bounds, memory_keys, memory_values, heads, groups, capacity
    )
    keys_values, key_rows = lax.optimization_barrier((keys_values, key_rows))
    halos += [passed_along(keys_values, "mem", distance) for distance in distances[repeats // 2 :]]
    all_queries = lax.all_gather(projected[:, :width], "mem", axis=0, tiled=True)
    local = local_forward(before_bias, book_lengths, projected, halos, heads, score_scale)
    partial = memory_forward(
        bounds,
        all_queries,
        key_rows,
        value_rows,
        row_ids,
        heads,
        groups,
        rows,
        score_scale,
    )
    if groups == 16:
        memory_out, mem_log, local_out, local_log = merge_partials(partial, groups, 1, heads, local)
    else:
        local_out, local_log = run_alone("local_forward", local)
        partial = lax.all_to_all(
            partial.reshape(groups, rows, width + 128),
            "mem",
            split_axis=0,
            concat_axis=0,
            tiled=True,
        ).reshape(groups * rows, width + 128)
        memory_out, mem_log = combine_partials(partial, heads, groups, rows)
    gate_share = jax.nn.sigmoid(gate_logit)
    (
        mixed_heads,
        normed_mid,
        activated,
        d_up,
        block_out,
        d_residual,
        ffn_gain_part,
        d_branch,
        d_mixed,
        gate_products,
        sent_grads,
    ) = middle(
        tokens,
        memory_out,
        local_out,
        mem_log,
        local_log,
        gate_share,
        out_weight,
        ffn_gain,
        up_weight,
        down_weight,
        cotangent,
        heads,
    )
    ffn_gain_part = ffn_gain_part.reshape(-1)
    early_halves = pair_grads(
        [mixed_heads, normed_mid, cotangent], [d_branch, d_up, activated], 5
    )
    early_sums = scattered(early_halves)
    sent_grads, _ = lax.optimization_barrier((sent_grads, early_halves))
    gate_part = jnp.sum(gate_products, axis=1) * gate_share * (1.0 - gate_share)
    local = local_queries(
        before_bias,
        book_lengths,
        projected,
        halos,
        d_mixed,
        local_out,
        local_log,
        gate_share,
        heads,
        score_scale,
    )
    if groups == 16:
        all_grads, d_queries, diagonals = gather_group(sent_grads, groups, 2, local)
    else:
        all_grads = lax.all_gather(sent_grads, "mem", axis=0, tiled=True)
        d_queries, diagonals = run_alone("local_queries", local)
    bias_part = jnp.dot(diagonals[:, rows - 1 : rows - 1 + W], one_hot, precision=lax.Precision.HIGHEST)
    d_partial = memory_backward(
        bounds,
        all_queries,
        all_grads,
        key_rows,
        value_rows,
        row_ids,
        heads,
        groups,
        rows,
        score_scale,
    )
    local = local_keys(
        after_bias,
        book_lengths,
        projected,
        all_queries,
        all_grads,
        (1.0 - gate_share) / gate_share,
        repeats + 1,
        heads,
        score_scale,
    )
    if groups == 16:
        d_projected = sum_queries(d_partial, d_queries, groups, 3, score_scale, local)
    else:
        (d_projected,) = run_alone("local_keys", local)
        d_partial, d_projected = lax.optimization_barrier((d_partial, d_projected))
        d_partial = jnp.sum(
            lax.all_to_all(
                d_partial.reshape(groups, rows, width), "mem", split_axis=0, concat_axis=0, tiled=True
            ).astype(jnp.float32),
            axis=0,
        )
        d_queries = (d_queries + d_partial * score_scale).astype(jnp.bfloat16)
        d_projected = jnp.concatenate([d_queries, d_projected[:, width:]], axis=1)
    beside = input_backward(tokens, attn_gain, d_projected, qkv_weight, d_residual)
    small = jnp.concatenate([ffn_gain_part, bias_part.reshape(-1), gate_part], axis=0)
    small = jnp.pad(small, (width, -small.shape[0] % 1024)).reshape(-1, 128)
    early_widths = [width, hidden, hidden]
    if groups == 16:
        late_both, small, tokens_grad, _ = finish_grads(
            [normed_in], [d_projected], small, groups, 4, beside
        )
        early_sums, small = lax.optimization_barrier((early_sums, small))
        early_both = join_halves(early_sums, 7)
    else:
        tokens_grad, attn_gain_part = run_alone("input_backward", beside)
        late_halves = pair_grads([normed_in], [d_projected], 6)
        late_halves, early_sums = lax.optimization_barrier((late_halves, early_sums))
        late_both = lax.all_gather(scattered(late_halves), "dp", axis=0)
        early_both = lax.all_gather(early_sums, "dp", axis=0)
        small = lax.psum(small.at[: width // 128].set(attn_gain_part.reshape(-1, 128)), ("dp", "mem"))
    qkv_grad, out_grad, up_grad, down_grad, attn_sum, ffn_sum, bias_sum, gate_sum, tokens_grad = (
        write_results(
            late_both, [3 * width], early_both, early_widths, small, tokens_grad, heads, buckets
        )
    )
    return (
        block_out,
        tokens_grad,
        qkv_grad,
        out_grad,
        up_grad,
        down_grad,
        attn_sum.reshape(-1),
        ffn_sum.reshape(-1),
        bias_sum,
        gate_sum.reshape(-1),
    )


def solution(mesh):
    in_specs = (
        P(("dp", "mem"), None),
        P(),
        P(),
        P(),
        P(),
        P(),
        P(),
        P(),
        P(),
        P("mem", None),
        P("mem", None),
        P("dp", None),
        P(("dp", "mem"), None, None, None),
        P(("dp", "mem"), None, None),
        P(("dp", "mem"), None, None),
        P(("dp", "mem"), None),
    )
    out_specs = (
        P(("dp", "mem"), None),
        P(("dp", "mem"), None),
        P("mem", None),
        P("mem", None),
        P("mem", None),
        P("mem", None),
        P(),
        P(),
        P(),
        P(),
    )
    return jax.shard_map(
        on_device, mesh=mesh, in_specs=in_specs, out_specs=out_specs, check_vma=False
    )
```

```python
import math

import jax
import jax.numpy as jnp
from jax import lax
from jax.experimental import pallas as pl
from jax.experimental.pallas import tpu as pltpu
from jax.sharding import PartitionSpec as P

W = 512
VMEM_LIMIT = 56 * 1024 * 1024


eps_norm = 1e-06
bucket_edges = tuple((math.ceil(16 * 8 ** (edge_step / 16)) for edge_step in range(1, 16)))
masked_score = -1e30
dead_score = -10000.0
contract_rows = (((0,), (0,)), ((), ()))
contract_cols = (((1,), (1,)), ((), ()))


def passed_along(value, axis, by):
    size = lax.axis_size(axis)
    pairs = [(i, i + by) for i in range(size) if 0 <= i + by < size]
    return lax.ppermute(value, axis, pairs)


def bucket_of(offset):
    past_edges = sum(((offset >= edge_pos).astype(jnp.int32) for edge_pos in bucket_edges))
    return jnp.where(offset < 16, offset, 16 + past_edges)


def normed(values, gain_vec):
    return (
        values * lax.rsqrt(jnp.mean(values * values, axis=-1, keepdims=True) + eps_norm) * gain_vec
    )


def place_requests(slot_shard, slot_index, slot_live, owners, capacity, slots):
    rows, heads, top_count = slot_index.shape
    entries, empty = rows * heads * top_count, heads * rows * slots
    if (owners + 1) * empty >= 2**31:
        raise ValueError("codes exceed int32")
    row_of = (
        jnp.arange(heads, dtype=jnp.int32)[None, :] * rows
        + jnp.arange(rows, dtype=jnp.int32)[:, None]
    )
    owner = jnp.where(slot_live > 0, slot_shard[..., 0], owners)
    codes = owner * empty + row_of[:, :, None] * slots + slot_index
    codes = lax.sort(codes.reshape(-1), is_stable=False)
    ends = jnp.sum(
        (codes[None, :] < (jnp.arange(owners, dtype=jnp.int32) + 1)[:, None] * empty).astype(jnp.int32),
        axis=1,
    )
    starts = jnp.concatenate([jnp.zeros((1,), jnp.int32), ends[:-1]])
    tall = -(-entries // 128)
    codes = jnp.pad(codes, (0, tall * 128 - entries)).reshape(tall, 128)
    long = capacity // 128

    def kernel(starts_ref, ends_ref, codes_ref, lists_ref, padded):
        padded[:tall, :] = codes_ref[...]
        padded[tall:, :] = jnp.zeros((long + 8, 128), jnp.int32)
        lane = lax.broadcasted_iota(jnp.int32, (long, 128), 1)
        place = lax.broadcasted_iota(jnp.int32, (long, 128), 0) * 128 + lane

        @pl.loop(0, owners)
        def _(i):
            start, end = starts_ref[i], ends_ref[i]
            shift = start % 128
            lines = padded[pl.ds(start // 128, long + 1), :]
            turned = pltpu.roll(lines, (128 - shift) % 128, 1)
            joined = jnp.where(lane < 128 - shift, turned[:long], turned[1:])
            lists_ref[i] = jnp.where(place < end - start, joined - i * empty, empty)

    return pl.pallas_call(
        kernel,
        in_specs=[pl.BlockSpec(memory_space=pltpu.SMEM)] * 2 + [pl.BlockSpec(memory_space=pltpu.VMEM)],
        out_shape=jax.ShapeDtypeStruct((owners, long, 128), jnp.int32),
        scratch_shapes=[pltpu.VMEM((tall + long + 8, 128), jnp.int32)],
        cost_estimate=lasting(3),
        name="make_lists",
    )(starts, ends, codes)


def read_lists(incoming, heads, rows, slots):
    sources, long, _ = incoming.shape

    def kernel(lists_ref, index_ref, ids_ref, bounds_ref):
        lane = lax.broadcasted_iota(jnp.int32, (1, 128), 1)

        def read(source):
            codes = lists_ref[source]
            ids = lax.div(codes, slots)
            index = lax.div(ids, rows) * slots + lax.rem(codes, slots)
            index_ref[source] = jnp.where(ids < heads * rows, index, 0)
            ids_ref[source, :long, :] = ids
            ids_ref[source, long:, :] = jnp.full((1, 128), heads * rows, jnp.int32)
            bounds = jnp.zeros((1, 128), jnp.int32)
            for head in range(1, heads + 1):
                below = jnp.sum(
                    jnp.where(codes < head * rows * slots, 1.0, 0.0), axis=0, keepdims=True
                )
                below = jnp.sum(below, axis=1, keepdims=True).astype(jnp.int32)
                bounds = jnp.where(lane == head, below, bounds)
            bounds_ref[pl.ds(source, 1), :] = bounds

        if sources > 16:
            pl.loop(0, sources)(read)
        else:
            for source in range(sources):
                read(source)

    return pl.pallas_call(
        kernel,
        out_shape=[
            jax.ShapeDtypeStruct((sources, long, 128), jnp.int32),
            jax.ShapeDtypeStruct((sources, long + 1, 128), jnp.int32),
            jax.ShapeDtypeStruct((sources, 128), jnp.int32),
        ],
        cost_estimate=lasting(3),
        name="read_lists",
    )(incoming)


def gather_rows(index, bounds, memory_keys, memory_values, heads, sources, capacity):
    slots, width = memory_keys.shape
    head_dim = width // heads
    step, part = 128, 16

    def kernel(index_ref, bounds_ref, keys, values, out_keys, out_values, key_table, value_table, key_rows, value_rows):
        i = pl.program_id(0)

        @pl.when(i < heads)
        def _():
            place = pl.ds(pl.multiple_of(i * slots, slots), slots)
            key_table[place, :] = keys[...].astype(jnp.float32)
            value_table[place, :] = values[...].astype(jnp.float32)

        @pl.when(i >= heads)
        def _():
            source = i - heads

            used = (bounds_ref[source * 128 + heads] + step - 1) // step

            def store(group):
                for at in range(0, step, part):
                    here = pl.ds(pl.multiple_of(group * step, step) + at, part)
                    out_keys[here, :] = key_rows[at : at + part, :].astype(jnp.bfloat16)
                    out_values[here, :] = value_rows[at : at + part, :].astype(jnp.bfloat16)

            @pl.loop(0, used)
            def _(group):
                store(jnp.maximum(group - 1, 0))
                first = source * capacity + group * step
                for u in range(step):
                    row = index_ref[first + u]
                    key_rows[u : u + 1, :] = key_table[pl.ds(row, 1), :]
                    value_rows[u : u + 1, :] = value_table[pl.ds(row, 1), :]

            pl.when(used > 0)(lambda: store(used - 1))

            @pl.loop(used, capacity // step)
            def _(group):
                here = pl.ds(pl.multiple_of(group * step, step), step)
                out_keys[here, :] = jnp.zeros((step, head_dim), jnp.bfloat16)
                out_values[here, :] = jnp.zeros((step, head_dim), jnp.bfloat16)

    table_spec = pl.BlockSpec((slots, head_dim), lambda i, *_: (0, jnp.minimum(i, heads - 1)))
    out_spec = pl.BlockSpec((capacity, head_dim), lambda i, *_: (jnp.maximum(i - heads, 0), 0))
    out_shape = jax.ShapeDtypeStruct((sources * capacity, head_dim), jnp.bfloat16)
    return pl.pallas_call(
        kernel,
        grid_spec=pltpu.PrefetchScalarGridSpec(
            num_scalar_prefetch=2,
            grid=(heads + sources,),
            in_specs=[table_spec, table_spec],
            out_specs=[out_spec, out_spec],
            scratch_shapes=[
                pltpu.VMEM((heads * slots, head_dim), jnp.float32),
                pltpu.VMEM((heads * slots, head_dim), jnp.float32),
                pltpu.VMEM((step, head_dim), jnp.float32),
                pltpu.VMEM((step, head_dim), jnp.float32),
            ],
        ),
        out_shape=[out_shape, out_shape],
        compiler_params=pltpu.CompilerParams(vmem_limit_bytes=VMEM_LIMIT),
        cost_estimate=lasting(42),
        name="gather_rows",
    )(index, bounds, memory_keys, memory_values)


def lasting(microseconds):
    return pl.CostEstimate(flops=0, bytes_accessed=3_000_000 * microseconds, transcendentals=0)


def triple(stat):
    part = lax.broadcasted_iota(jnp.int32, stat.shape, 1) // 16
    high = stat.astype(jnp.bfloat16).astype(jnp.float32)
    rest = stat - high
    middle = rest.astype(jnp.bfloat16).astype(jnp.float32)
    low = rest - middle
    chosen = jnp.where(part == 0, high, jnp.where(part == 1, middle, jnp.where(part == 2, low, 0.0)))
    return chosen.astype(jnp.bfloat16)


def window_of(bounds, source, head, heads, span, capacity):
    first, last = bounds[source * 128 + head], bounds[source * 128 + head + 1]
    start = jnp.minimum(first // 16 * 16, capacity - span)
    extra = jnp.maximum(last - start - 1, 0) // span
    return start, extra


def columns_of(head, head_dim):
    if isinstance(head, int):
        return slice(head * head_dim, (head + 1) * head_dim)
    return pl.ds(pl.multiple_of(head * head_dim, head_dim), head_dim)


def window_ids(id_ref, start, span):
    lines = id_ref[0, pl.ds(start // 128, span // 128 + 1), :]
    shift = start % 128
    turned = pltpu.roll(lines, (128 - shift) % 128, 1)
    lane = lax.broadcasted_iota(jnp.int32, (span // 128, 128), 1)
    return jnp.where(lane < 128 - shift, turned[:-1], turned[1:])


def owned(lines, first_row, count, start, least):
    row = lax.broadcasted_iota(jnp.int32, (count, 128), 0) + first_row
    masks = []
    for i in range(lines.shape[0]):
        mask = lines[i : i + 1, :] == row
        if least is not None:
            place = lax.broadcasted_iota(jnp.int32, (1, 128), 1) + start + i * 128
            mask = mask & (place >= least)
        masks.append(mask)
    return jnp.concatenate(masks, axis=1)


def memory_forward(bounds, queries, key_rows, value_rows, row_ids, heads, sources, rows, score_scale):
    capacity, head_dim = key_rows.shape[0] // sources, key_rows.shape[1]
    width = heads * head_dim
    span = min(384, capacity)
    chunk = math.gcd(rows, 32)

    def kernel(bounds_ref, q_ref, k_ref, v_ref, id_ref, out_ref, sums, tops, totals, raw, weights):
        source = pl.program_id(0)
        lane = lax.broadcasted_iota(jnp.int32, (chunk, 128), 1) % 16

        def window(heads_here, starts, least):
            here = [pl.ds(pl.multiple_of(start, 16), span) for start in starts]
            columns = [columns_of(head, head_dim) for head in heads_here]
            for slot in range(len(starts)):
                raw[slot] = lax.dot_general(
                    q_ref[:, columns[slot]],
                    k_ref[here[slot], :],
                    contract_cols,
                    preferred_element_type=jnp.float32,
                )
            for slot, (head, start) in enumerate(zip(heads_here, starts)):
                lines = window_ids(id_ref, start, span)
                for at in range(0, rows, chunk):
                    some = slice(at, at + chunk)
                    mine = owned(lines, head * rows + at, chunk, start, least)
                    scores = jnp.where(mine, raw[slot, some, :], masked_score)
                    top = jnp.maximum(jnp.max(scores, axis=1, keepdims=True), 0.1 * masked_score)
                    if least is not None:
                        old_top = jnp.max(
                            jnp.where(lane == head, tops[some, :], masked_score), axis=1, keepdims=True
                        )
                        top = jnp.maximum(top, old_top)
                    exps = jnp.exp((scores - top) * score_scale)
                    weights[slot, some, :] = exps.astype(jnp.bfloat16)
                    total = jnp.sum(exps, axis=1, keepdims=True)
                    if least is not None:
                        faded = jnp.exp((old_top - top) * score_scale)
                        sums[some, columns[slot]] = sums[some, columns[slot]] * faded
                        total = total + totals[some, :] * faded
                    tops[some, :] = jnp.where(lane == head, top, tops[some, :])
                    totals[some, :] = jnp.where(lane == heads + head, total, totals[some, :])
            for slot in range(len(starts)):
                found = jnp.dot(
                    weights[slot], v_ref[here[slot], :], preferred_element_type=jnp.float32
                )
                sums[:, columns[slot]] = found if least is None else sums[:, columns[slot]] + found

        tops[...] = jnp.zeros_like(tops)
        totals[...] = jnp.zeros_like(totals)

        windows = [window_of(bounds_ref, source, head, heads, span, capacity) for head in range(heads)]
        window(list(range(heads)), [start for start, _ in windows], None)

        @pl.when(sum(extra for _, extra in windows) > 0)
        def _():
            @pl.loop(0, heads)
            def _(head):
                start, extra = window_of(bounds_ref, source, head, heads, span, capacity)

                @pl.loop(0, extra)
                def _(turn):
                    least = start + (turn + 1) * span
                    window([head], [jnp.minimum(least, capacity - span)], least)

        out_ref[:, :width] = sums[...].astype(jnp.bfloat16)
        wide = lax.broadcasted_iota(jnp.int32, (rows, 128), 1) % 16
        out_ref[:, width:] = triple(jnp.where(wide < heads, tops[...] * score_scale, totals[...]))

    return pl.pallas_call(
        kernel,
        grid_spec=pltpu.PrefetchScalarGridSpec(
            num_scalar_prefetch=1,
            grid=(sources,),
            in_specs=[
                pl.BlockSpec((rows, width), lambda i, *_: (i, 0)),
                pl.BlockSpec((capacity, head_dim), lambda i, *_: (i, 0)),
                pl.BlockSpec((capacity, head_dim), lambda i, *_: (i, 0)),
                pl.BlockSpec((1, *row_ids.shape[1:]), lambda i, *_: (i, 0, 0)),
            ],
            out_specs=pl.BlockSpec((rows, width + 128), lambda i, *_: (i, 0)),
            scratch_shapes=[
                pltpu.VMEM((rows, width), jnp.float32),
                pltpu.VMEM((rows, 128), jnp.float32),
                pltpu.VMEM((rows, 128), jnp.float32),
                pltpu.VMEM((heads, rows, span), jnp.float32),
                pltpu.VMEM((heads, rows, span), jnp.bfloat16),
            ],
        ),
        out_shape=jax.ShapeDtypeStruct((sources * rows, width + 128), jnp.bfloat16),
        compiler_params=pltpu.CompilerParams(vmem_limit_bytes=VMEM_LIMIT),
        cost_estimate=lasting(25),
        name="memory_forward",
    )(bounds, queries, key_rows, value_rows, row_ids)


def combine_partials(partial, heads, sources, rows):
    width = partial.shape[1] - 128
    head_dim = width // heads

    def kernel(part_ref, out_ref, log_ref, sums, tops, totals):
        i = pl.program_id(0)

        @pl.when(i == 0)
        def _():
            sums[...] = jnp.zeros_like(sums)
            tops[...] = jnp.full_like(tops, masked_score)
            totals[...] = jnp.zeros_like(totals)

        stat = part_ref[:, width:].astype(jnp.float32)
        stat = stat + pltpu.roll(stat, 128 - 16, 1) + pltpu.roll(stat, 128 - 32, 1)
        new_total = pltpu.roll(stat, 128 - heads, 1)
        top = jnp.maximum(tops[...], stat)
        old_fade, new_fade = jnp.exp(tops[...] - top), jnp.exp(stat - top)
        tops[...] = top
        totals[...] = totals[...] * old_fade + new_total * new_fade
        for head in range(heads):
            columns = slice(head * head_dim, (head + 1) * head_dim)
            sums[:, columns] = (
                sums[:, columns] * old_fade[:, head : head + 1]
                + part_ref[:, columns].astype(jnp.float32) * new_fade[:, head : head + 1]
            )

        @pl.when(i == sources - 1)
        def _():
            live = totals[...] > 0
            total = jnp.where(live, totals[...], 1.0)
            log_ref[...] = jnp.where(live, tops[...] + jnp.log(total), 0.0)
            for head in range(heads):
                columns = slice(head * head_dim, (head + 1) * head_dim)
                out_ref[:, columns] = sums[:, columns] / total[:, head : head + 1]

    return pl.pallas_call(
        kernel,
        grid=(sources,),
        in_specs=[pl.BlockSpec((rows, width + 128), lambda i: (i, 0))],
        out_specs=[
            pl.BlockSpec((rows, width), lambda i: (0, 0)),
            pl.BlockSpec((rows, 128), lambda i: (0, 0)),
        ],
        scratch_shapes=[
            pltpu.VMEM((rows, width), jnp.float32),
            pltpu.VMEM((rows, 128), jnp.float32),
            pltpu.VMEM((rows, 128), jnp.float32),
        ],
        out_shape=[
            jax.ShapeDtypeStruct((rows, width), jnp.float32),
            jax.ShapeDtypeStruct((rows, 128), jnp.float32),
        ],
        compiler_params=pltpu.CompilerParams(vmem_limit_bytes=VMEM_LIMIT),
        cost_estimate=lasting(13),
        name="combine_partials",
    )(partial)


def memory_backward(bounds, queries, grads, key_rows, value_rows, row_ids, heads, sources, rows, score_scale):
    capacity, head_dim = key_rows.shape[0] // sources, key_rows.shape[1]
    width = heads * head_dim
    span = min(384, capacity)
    chunk = math.gcd(rows, 32)

    def kernel(bounds_ref, q_ref, g_ref, k_ref, v_ref, id_ref, out_ref, sums, stats, raw, products, slopes):
        source = pl.program_id(0)
        stats[...] = joined_tile(g_ref[:, width : width + 128])

        def window(heads_here, starts, least):
            here = [pl.ds(pl.multiple_of(start, 16), span) for start in starts]
            columns = [columns_of(head, head_dim) for head in heads_here]
            for slot in range(len(starts)):
                raw[slot] = lax.dot_general(
                    q_ref[:, columns[slot]],
                    k_ref[here[slot], :],
                    contract_cols,
                    preferred_element_type=jnp.float32,
                )
                products[slot] = lax.dot_general(
                    g_ref[:, columns[slot]],
                    v_ref[here[slot], :],
                    contract_cols,
                    preferred_element_type=jnp.float32,
                )
            for slot, (head, start) in enumerate(zip(heads_here, starts)):
                lines = window_ids(id_ref, start, span)
                turned = stats[...]
                if least is not None:
                    turned = pltpu.roll(turned, 128 - head, 1)
                elif head:
                    turned = turned[:, head:]
                for at in range(0, rows, chunk):
                    some = slice(at, at + chunk)
                    mine = owned(lines, head * rows + at, chunk, start, least)
                    log, delta = turned[some, :1], turned[some, heads : heads + 1]
                    probs = jnp.exp(jnp.where(mine, raw[slot, some, :] * score_scale - log, dead_score))
                    slopes[slot, some, :] = (probs * (products[slot, some, :] - delta)).astype(
                        jnp.bfloat16
                    )
            for slot in range(len(starts)):
                found = jnp.dot(
                    slopes[slot], k_ref[here[slot], :], preferred_element_type=jnp.float32
                )
                sums[:, columns[slot]] = found if least is None else sums[:, columns[slot]] + found

        windows = [window_of(bounds_ref, source, head, heads, span, capacity) for head in range(heads)]
        window(list(range(heads)), [start for start, _ in windows], None)

        @pl.when(sum(extra for _, extra in windows) > 0)
        def _():
            @pl.loop(0, heads)
            def _(head):
                start, extra = window_of(bounds_ref, source, head, heads, span, capacity)

                @pl.loop(0, extra)
                def _(turn):
                    least = start + (turn + 1) * span
                    window([head], [jnp.minimum(least, capacity - span)], least)

        out_ref[...] = sums[...].astype(jnp.bfloat16)

    return pl.pallas_call(
        kernel,
        grid_spec=pltpu.PrefetchScalarGridSpec(
            num_scalar_prefetch=1,
            grid=(sources,),
            in_specs=[
                pl.BlockSpec((rows, width), lambda i, *_: (i, 0)),
                pl.BlockSpec((rows, width + 128), lambda i, *_: (i, 0)),
                pl.BlockSpec((capacity, head_dim), lambda i, *_: (i, 0)),
                pl.BlockSpec((capacity, head_dim), lambda i, *_: (i, 0)),
                pl.BlockSpec((1, *row_ids.shape[1:]), lambda i, *_: (i, 0, 0)),
            ],
            out_specs=pl.BlockSpec((rows, width), lambda i, *_: (i, 0)),
            scratch_shapes=[
                pltpu.VMEM((rows, width), jnp.float32),
                pltpu.VMEM((rows, 128), jnp.float32),
                pltpu.VMEM((heads, rows, span), jnp.float32),
                pltpu.VMEM((heads, rows, span), jnp.float32),
                pltpu.VMEM((heads, rows, span), jnp.bfloat16),
            ],
        ),
        out_shape=jax.ShapeDtypeStruct((sources * rows, width), jnp.bfloat16),
        compiler_params=pltpu.CompilerParams(vmem_limit_bytes=VMEM_LIMIT),
        cost_estimate=lasting(25),
        name="memory_backward",
    )(bounds, queries, grads, key_rows, value_rows, row_ids)


def remote(source, target, send_sem, recv_sem, device):
    return pltpu.make_async_remote_copy(
        src_ref=source,
        dst_ref=target,
        send_sem=send_sem,
        recv_sem=recv_sem,
        device_id={"mem": device},
        device_id_type=pl.DeviceIdType.MESH,
    )


def grid_place(depth):
    me = lax.axis_index("mem")
    layer, column = me // 4, me % 4
    beside_x = column + 1 - 2 * (column % 2)
    beside_y = column + 2 - 4 * (column // 2)
    across = 3 - column

    def index_of(step, place):
        return (layer + step + depth) % depth * 4 + place

    return me, column, beside_x, beside_y, across, index_of


def greet(devices):
    barrier = pltpu.get_barrier_semaphore()
    for device in devices:
        pl.semaphore_signal(
            barrier, inc=1, device_id={"mem": device}, device_id_type=pl.DeviceIdType.MESH
        )
    pl.semaphore_wait(barrier, len(devices))


def gather_group(block, sources, collective_id, beside):
    rows, width = block.shape
    depth, half = sources // 4, rows // 2
    slots = 2 * depth - 1
    arrays, specs, more_out, more_scratch, begin = beside
    ins, outs = len(arrays), len(more_out)

    def kernel(x_ref, *refs):
        in_refs, (out_ref, *more_refs) = refs[:ins], refs[ins : ins + 1 + outs]
        (own_sem, send, recv), scratch = refs[ins + 1 + outs : ins + 4 + outs], refs[ins + 4 + outs :]
        meanwhile = begin(in_refs, more_refs, scratch)
        me = lax.axis_index("mem")
        layer, column = me // 4, me % 4
        to_x = me + 1 - 2 * (column % 2)
        to_y = me + 2 - 4 * (column // 2)
        across = layer * 4 + 3 - column
        has_above, has_below = layer + 1 < depth, layer > 0
        barrier = pltpu.get_barrier_semaphore()

        def signal(device):
            pl.semaphore_signal(
                barrier, inc=1, device_id={"mem": device}, device_id_type=pl.DeviceIdType.MESH
            )

        signal(to_x)
        signal(to_y)
        pl.when(has_above)(lambda: signal(me + 4))
        pl.when(has_below)(lambda: signal(me - 4))
        pl.semaphore_wait(barrier, 2 + has_above.astype(jnp.int32) + has_below.astype(jnp.int32))

        def part_of(index, part):
            start = pl.multiple_of(index * rows + part * half, half)
            return out_ref.at[pl.ds(start, half), :]

        own = pltpu.make_async_copy(x_ref, out_ref.at[pl.ds(pl.multiple_of(me * rows, rows), rows), :], own_sem)
        own.start()
        sent = []

        def push(condition, source, target, kind, slot, to_slot, part, device):
            copy = remote(source, target, send.at[kind, slot, part], recv.at[kind, to_slot, part], device)
            if condition is None:
                copy.start()
            else:
                pl.when(condition)(copy.start)
            sent.append((condition, copy))

        def arrived(index, kind, slot, part):
            target = part_of(index, part)
            remote(target, target, send.at[kind, slot, part], recv.at[kind, slot, part], to_x).wait_recv()

        def up_slot(distance):
            return distance

        def down_slot(distance):
            return depth - 1 + distance

        for part in (0, 1):
            mine = x_ref.at[pl.ds(part * half, half), :]
            push(has_above, mine, part_of(me, part), 0, 0, down_slot(1), part, me + 4)
            push(has_below, mine, part_of(me, part), 1, 0, up_slot(1), part, me - 4)
            mine_y = x_ref.at[pl.ds((1 - part) * half, half), :]
            push(None, mine, part_of(me, part), 2, 0, 0, part, to_x)
            push(None, mine_y, part_of(me, 1 - part), 3, 0, 0, 1 - part, to_y)

        def pass_on(condition, step, slot):
            def go():
                arrived(to_x + step, 2, slot, 0)
                copy_a.start()
                arrived(to_y + step, 3, slot, 1)
                copy_b.start()

            source_a, source_b = part_of(to_x + step, 0), part_of(to_y + step, 1)
            copy_a = remote(source_a, source_a, send.at[4, slot, 0], recv.at[4, slot, 0], to_y)
            copy_b = remote(source_b, source_b, send.at[5, slot, 1], recv.at[5, slot, 1], to_x)
            sent.append((condition, copy_a))
            sent.append((condition, copy_b))
            if condition is None:
                go()
            else:
                pl.when(condition)(go)

        def pass_all(distance):
            if distance == 0:
                pass_on(None, 0, 0)
            else:
                pass_on(layer + distance < depth, 4 * distance, up_slot(distance))
                pass_on(layer - distance >= 0, -4 * distance, down_slot(distance))

        for distance in range(1, depth):
            from_above, from_below = layer + distance < depth, layer - distance >= 0

            def take(kind, back_kind, step, slot, next_slot, onward, onward_device):
                for part in (0, 1):
                    arrived(me + step, kind, slot, part)
                    here = part_of(me + step, part)
                    if next_slot is not None:
                        pl.when(onward)(
                            remote(
                                here, here, send.at[kind, slot, part], recv.at[kind, next_slot, part], onward_device
                            ).start
                        )
                    remote(here, here, send.at[2, slot, part], recv.at[2, slot, part], to_x).start()
                    remote(here, here, send.at[3, slot, part], recv.at[3, slot, part], to_y).start()

            last = distance == depth - 1
            pl.when(from_above)(
                lambda: take(
                    1, 0, 4 * distance, up_slot(distance), None if last else up_slot(distance + 1), has_below, me - 4
                )
            )
            pl.when(from_below)(
                lambda: take(
                    0, 1, -4 * distance, down_slot(distance), None if last else down_slot(distance + 1), has_above, me + 4
                )
            )
            for condition, step, slot, kind, onward in (
                (from_above, 4 * distance, up_slot(distance), 1, has_below),
                (from_below, -4 * distance, down_slot(distance), 0, has_above),
            ):
                for part in (0, 1):
                    here = part_of(me + step, part)
                    if not last:
                        sent.append((condition & onward, remote(here, here, send.at[kind, slot, part], own_sem, me)))
                    sent.append((condition, remote(here, here, send.at[2, slot, part], own_sem, to_x)))
                    sent.append((condition, remote(here, here, send.at[3, slot, part], own_sem, to_y)))
            meanwhile(distance - 1, depth - 1)
            if distance > 1:
                pass_all(distance - 2)
        for distance in (depth - 2, depth - 1):
            pass_all(distance)

        def close(step, slot):
            arrived(to_x + step, 2, slot, 1)
            arrived(to_y + step, 3, slot, 0)
            arrived(across + step, 4, slot, 0)
            arrived(across + step, 5, slot, 1)

        close(0, 0)
        for distance in range(1, depth):
            pl.when(layer + distance < depth)(lambda: close(4 * distance, up_slot(distance)))
            pl.when(layer - distance >= 0)(lambda: close(-4 * distance, down_slot(distance)))
        for condition, copy in sent:
            if condition is None:
                copy.wait_send()
            else:
                pl.when(condition)(copy.wait_send)
        own.wait()

    return pl.pallas_call(
        kernel,
        in_specs=[pl.BlockSpec(memory_space=pl.ANY), *specs],
        out_specs=[pl.BlockSpec(memory_space=pl.ANY)] + [pl.BlockSpec(memory_space=pltpu.VMEM)] * outs,
        out_shape=[jax.ShapeDtypeStruct((sources * rows, width), block.dtype), *more_out],
        scratch_shapes=[
            pltpu.SemaphoreType.DMA,
            pltpu.SemaphoreType.DMA((6, slots, 2)),
            pltpu.SemaphoreType.DMA((6, slots, 2)),
            *more_scratch,
        ],
        compiler_params=pltpu.CompilerParams(
            collective_id=collective_id, has_side_effects=True, vmem_limit_bytes=VMEM_LIMIT
        ),
        cost_estimate=lasting(50),
        name="gather_group",
    )(block, *arrays)


def reduce_steps(parts_ref, sources, refs, sems, merge, pack, beside=None):
    half_a, half_b, from_x, from_y, from_z, out_x, out_y, out_z = refs
    send, recv_a, recv_b, recv_x, recv_y, recv_z = sems
    rows = parts_ref.shape[0] // sources
    depth, half = sources // 4, rows // 2
    me, column, beside_x, beside_y, across, index_of = grid_place(depth)
    to_x, to_y = index_of(0, beside_x), index_of(0, beside_y)
    order = [*range(1, depth), 0]
    queues = {"x": [], "y": [], "z": []}
    first_limit = 2 if beside is None else depth

    def piece(index, part):
        return parts_ref.at[pl.ds(pl.multiple_of(index * rows + part * half, half), half), :]

    def part_rows(part):
        return pl.ds(part * half, half)

    def push(link, source, target, kind, k, recv_sem, device, limit=2):
        queue = queues[link]
        while link != "z" and len(queue) >= limit:
            queue.pop(0).wait_send()
        copy = remote(source, target, send.at[kind, k], recv_sem, device)
        copy.start()
        queue.append(copy)

    def arrived(target, recv_sem):
        remote(target, target, send.at[0, 0], recv_sem, to_x).wait_recv()

    def plane_rest(k):
        push("x", piece(index_of(k, beside_x), 0), from_x.at[k, part_rows(0)], 2, k, recv_x.at[0, k], to_x)
        push("y", piece(index_of(k, beside_y), 1), from_y.at[k, part_rows(1)], 3, k, recv_y.at[1, k], to_y)

    def plane_merged(k):
        arrived(half_a.at[k], recv_a.at[k])
        pack(out_y.at[k], merge([piece(index_of(k, beside_y), 0), half_a.at[k]]))
        push("y", out_y.at[k], from_y.at[k, part_rows(0)], 4, k, recv_y.at[0, k], to_y)
        arrived(half_b.at[k], recv_b.at[k])
        pack(out_x.at[k], merge([piece(index_of(k, beside_x), 1), half_b.at[k]]))
        push("x", out_x.at[k], from_x.at[k, part_rows(1)], 5, k, recv_x.at[1, k], to_x)

    def column_step(k):
        for part in (0, 1):
            here = part_rows(part)
            arrived(from_x.at[k, here], recv_x.at[part, k])
            arrived(from_y.at[k, here], recv_y.at[part, k])
            if k:
                blocks = [piece(index_of(k, column), part), from_x.at[k, here], from_y.at[k, here]]
                pack(out_z.at[k, here], merge(blocks))
        if k:
            push("z", out_z.at[k], from_z.at[k], 6, k, recv_z.at[k], index_of(k, column))

    for k in order:
        far = index_of(k, across)
        push("x", piece(far, 0), half_a.at[k], 0, k, recv_a.at[k], to_x, first_limit)
        push("y", piece(far, 1), half_b.at[k], 1, k, recv_b.at[k], to_y, first_limit)
    if beside is not None:
        beside()
    for i, k in enumerate(order):
        plane_rest(k)
        plane_merged(k)
        if i:
            column_step(order[i - 1])
    column_step(order[-1])
    for k in range(1, depth):
        arrived(from_z.at[k], recv_z.at[k])
    final = []
    for part in (0, 1):
        here = part_rows(part)
        blocks = [piece(me, part), from_x.at[0, here], from_y.at[0, here]]
        final.append((here, blocks + [from_z.at[k, here] for k in range(1, depth)]))
    return final, [copy for queue in queues.values() for copy in queue]


def reduce_scratch(rows, width, dtype, sources):
    depth, half = sources // 4, rows // 2

    def slots(size):
        return pltpu.VMEM((depth, size, width), dtype)

    refs = [slots(half), slots(half), slots(rows), slots(rows), slots(rows)]
    refs += [slots(half), slots(half), slots(rows)]
    sems = [pltpu.SemaphoreType.DMA((7, depth))]
    sems += [pltpu.SemaphoreType.DMA((depth,))] * 2
    sems += [pltpu.SemaphoreType.DMA((2, depth))] * 2
    sems += [pltpu.SemaphoreType.DMA((depth,))]
    return refs, sems


def run_alone(name, beside):
    arrays, specs, out_shape, scratch, begin = beside
    ins, outs = len(arrays), len(out_shape)

    def kernel(*refs):
        begin(refs[:ins], refs[ins : ins + outs], refs[ins + outs :])()

    return pl.pallas_call(
        kernel,
        in_specs=specs,
        out_specs=[pl.BlockSpec(memory_space=pltpu.VMEM)] * outs,
        out_shape=out_shape,
        scratch_shapes=scratch,
        compiler_params=pltpu.CompilerParams(vmem_limit_bytes=VMEM_LIMIT),
        cost_estimate=lasting(8),
        name=name,
    )(*arrays)


def reduce_group(parts, sources, collective_id, merge, pack, finish, out_shape, beside):
    rows, width = parts.shape[0] // sources, parts.shape[1]
    depth = sources // 4
    arrays, specs, more_out, more_scratch, begin = beside
    ref_shapes, sem_shapes = reduce_scratch(rows, width, parts.dtype, sources)
    sizes = [len(arrays), len(out_shape), len(more_out), len(ref_shapes), len(sem_shapes), len(more_scratch)]

    def kernel(parts_ref, *refs):
        groups, at = [], 0
        for size in sizes:
            groups.append(refs[at : at + size])
            at += size
        ins, out_refs, more_refs, steps_refs, steps_sems, scratch = groups
        meanwhile = begin(ins, more_refs, scratch)
        last = finish
        if finish is None:
            meanwhile, last = meanwhile
        me, column, beside_x, beside_y, across, index_of = grid_place(depth)
        greet(
            [index_of(0, beside_x), index_of(0, beside_y)]
            + [index_of(-k, column) for k in range(1, depth)]
        )
        final, still_open = reduce_steps(
            parts_ref, sources, steps_refs, steps_sems, merge, pack, meanwhile
        )
        for here, blocks in final:
            if finish is None:
                last(here, merge(blocks))
            else:
                last([out.at[here] for out in out_refs], merge(blocks))
        for copy in still_open:
            copy.wait_send()

    vmem = pl.BlockSpec(memory_space=pltpu.VMEM)
    return pl.pallas_call(
        kernel,
        in_specs=[vmem, *specs],
        out_specs=[vmem] * (len(out_shape) + len(more_out)),
        out_shape=[*out_shape, *more_out],
        scratch_shapes=[*ref_shapes, *sem_shapes, *more_scratch],
        compiler_params=pltpu.CompilerParams(
            collective_id=collective_id, has_side_effects=True, vmem_limit_bytes=VMEM_LIMIT
        ),
        cost_estimate=lasting(50),
        name="reduce_group",
    )(parts, *arrays)


def sum_queries(parts, d_queries, sources, collective_id, score_scale, beside):
    rows, width = d_queries.shape
    arrays, specs, (whole,), more_scratch, begin = beside

    def merge(blocks):
        total = blocks[0][...].astype(jnp.float32)
        for block in blocks[1:]:
            total = total + block[...].astype(jnp.float32)
        return total

    def pack(target, total):
        target[...] = total.astype(parts.dtype)

    def begin_both(ins, outs, scratch):
        run = begin(ins[:-1], outs, scratch)

        def finish(here, total):
            outs[0][here, :width] = (ins[-1][here, :] + total * score_scale).astype(whole.dtype)

        return run, finish

    more = [*arrays, d_queries], [*specs, pl.BlockSpec(memory_space=pltpu.VMEM)], [whole], more_scratch, begin_both
    return reduce_group(parts, sources, collective_id, merge, pack, None, [], more)[0]


def merge_partials(parts, sources, collective_id, heads, beside):
    rows, width = parts.shape[0] // sources, parts.shape[1] - 128
    head_dim = width // heads

    def merge(blocks):
        stats = []
        for block in blocks:
            stat = block[:, width:].astype(jnp.float32)
            stats.append(stat + pltpu.roll(stat, 128 - 16, 1) + pltpu.roll(stat, 128 - 32, 1))
        top = stats[0]
        for stat in stats[1:]:
            top = jnp.maximum(top, stat)
        fades = [jnp.exp(stat - top) for stat in stats]
        total = sum(fade * pltpu.roll(stat, 128 - heads, 1) for fade, stat in zip(fades, stats))
        sums = []
        for head in range(heads):
            columns = slice(head * head_dim, (head + 1) * head_dim)
            sums.append(
                sum(
                    block[:, columns].astype(jnp.float32) * fade[:, head : head + 1]
                    for block, fade in zip(blocks, fades)
                )
            )
        return sums, top, total

    def pack(target, merged):
        sums, top, total = merged
        for head in range(heads):
            target[:, head * head_dim : (head + 1) * head_dim] = sums[head].astype(parts.dtype)
        lane = lax.broadcasted_iota(jnp.int32, top.shape, 1)
        stat = jnp.where(lane < heads, top, jnp.where(lane < 16, pltpu.roll(total, heads, 1), 0.0))
        target[:, width:] = triple(stat + pltpu.roll(stat, 16, 1) + pltpu.roll(stat, 32, 1))

    def finish(targets, merged):
        sums, top, total = merged
        live = total > 0
        total = jnp.where(live, total, 1.0)
        targets[1][...] = jnp.where(live, top + jnp.log(total), 0.0)
        for head in range(heads):
            targets[0][:, head * head_dim : (head + 1) * head_dim] = sums[head] / total[:, head : head + 1]

    out_shape = [
        jax.ShapeDtypeStruct((rows, width), jnp.float32),
        jax.ShapeDtypeStruct((rows, 128), jnp.float32),
    ]
    return reduce_group(parts, sources, collective_id, merge, pack, finish, out_shape, beside)


def scattered(halves):
    return lax.psum_scatter(halves, "mem", scatter_dimension=0, tiled=True)


def same_book(lengths_ref, first_row, rows, first_lane, lanes):
    row = lax.broadcasted_iota(jnp.int32, (rows, lanes), 0) + first_row
    lane = lax.broadcasted_iota(jnp.int32, (rows, lanes), 1) + first_lane
    end, same = 0, lane >= 0
    for i in range(lengths_ref.shape[1]):
        end = end + lengths_ref[0, i]
        same = same & ((row >= end) == (lane >= end))
    return same


def lane_tile(columns, rows):
    lane = lax.broadcasted_iota(jnp.int32, (rows, 128), 1)
    tile = jnp.zeros((rows, 128), jnp.float32)
    for i, column in enumerate(columns):
        tile = jnp.where(lane == i, column, tile)
    return tile


def split_tile(tile):
    lane = lax.broadcasted_iota(jnp.int32, tile.shape, 1)
    kept = jnp.where(lane < 32, tile, 0.0)
    kept = kept + pltpu.roll(kept, 32, 1) + pltpu.roll(kept, 64, 1)
    high = kept.astype(jnp.bfloat16).astype(jnp.float32)
    middle = (kept - high).astype(jnp.bfloat16).astype(jnp.float32)
    low = kept - high - middle
    part = lane // 32
    return jnp.where(part == 0, high, jnp.where(part == 1, middle, low)).astype(jnp.bfloat16)


def joined_tile(tile):
    tile = tile.astype(jnp.float32)
    return tile + pltpu.roll(tile, 128 - 32, 1) + pltpu.roll(tile, 128 - 64, 1)


def slanted(base, rows):
    return pltpu.roll(jnp.broadcast_to(base, (rows, base.shape[1])), 0, 1, stride=1, stride_axis=0)


def local_forward(base, lengths, own, halos, heads, score_scale):
    rows, width = own.shape[0], own.shape[1] // 3
    head_dim = width // heads
    count = len(halos) + 1

    def begin(ins, outs, scratch):
        base_ref, lengths_ref, own_ref, *halo_refs = ins
        out_ref, log_ref = outs

        def run():
            first = lax.axis_index("mem") * rows
            same = same_book(lengths_ref, first, rows, first - (count - 1) * rows, count * rows)
            logs = []
            for head in range(heads):
                columns = slice(head * head_dim, (head + 1) * head_dim)
                above = slice(width + head * head_dim, width + (head + 1) * head_dim)
                twice = slice(2 * width + head * head_dim, 2 * width + (head + 1) * head_dim)
                keys = [ref[:, columns] for ref in halo_refs] + [own_ref[:, above]]
                values = [ref[:, above] for ref in halo_refs] + [own_ref[:, twice]]
                q = own_ref[:, columns]
                raw = [
                    lax.dot_general(q, k, contract_cols, preferred_element_type=jnp.float32) for k in keys
                ]
                bias = slanted(base_ref[head : head + 1, :], rows)[:, : count * rows]
                scores = jnp.concatenate(raw, axis=1) * score_scale + bias
                scores = jnp.where(same, scores, masked_score)
                top = jnp.max(scores, axis=1, keepdims=True)
                weights = jnp.exp(scores - top)
                total = jnp.sum(weights, axis=1, keepdims=True)
                weights = (weights / total).astype(jnp.bfloat16)
                out_ref[:, columns] = sum(
                    jnp.dot(
                        weights[:, i * rows : (i + 1) * rows], v, preferred_element_type=jnp.float32
                    )
                    for i, v in enumerate(values)
                )
                logs.append(top + jnp.log(total))
            log_ref[...] = lane_tile(logs, rows)

        return run

    arrays = [base, lengths, own, *halos]
    vmem = pl.BlockSpec(memory_space=pltpu.VMEM)
    specs = [vmem, pl.BlockSpec(memory_space=pltpu.SMEM)] + [vmem] * (1 + len(halos))
    out_shape = [
        jax.ShapeDtypeStruct((rows, width), jnp.float32),
        jax.ShapeDtypeStruct((rows, 128), jnp.float32),
    ]
    return arrays, specs, out_shape, [], begin


def local_queries(
    base, lengths, own, halos, d_mixed, local_out, local_log, share, heads, score_scale
):
    rows, width = d_mixed.shape
    head_dim = width // heads
    count = len(halos) + 1
    span = base.shape[1]

    def begin(ins, outs, scratch):
        base_ref, lengths_ref, own_ref, mix_ref, loc_ref, log_ref, share_ref, *halo_refs = ins
        dq_ref, diagonal_ref = outs

        def some_heads(some):
            first = lax.axis_index("mem") * rows
            same = same_book(lengths_ref, first, rows, first - (count - 1) * rows, count * rows)
            turned = (
                lax.broadcasted_iota(jnp.int32, (rows, rows), 0)
                + lax.broadcasted_iota(jnp.int32, (rows, rows), 1)
                == rows - 1
            ).astype(jnp.bfloat16)
            for head in some:
                columns = slice(head * head_dim, (head + 1) * head_dim)
                above = slice(width + head * head_dim, width + (head + 1) * head_dim)
                twice = slice(2 * width + head * head_dim, 2 * width + (head + 1) * head_dim)
                keys = [ref[:, columns] for ref in halo_refs] + [own_ref[:, above]]
                values = [ref[:, above] for ref in halo_refs] + [own_ref[:, twice]]
                q = own_ref[:, columns]
                d_out = ((1.0 - share_ref[head]) * mix_ref[:, columns]).astype(jnp.bfloat16)
                delta = jnp.sum(
                    d_out.astype(jnp.float32) * loc_ref[:, columns], axis=1, keepdims=True
                )
                raw = [
                    lax.dot_general(q, k, contract_cols, preferred_element_type=jnp.float32)
                    for k in keys
                ]
                bias = slanted(base_ref[head : head + 1, :], rows)[:, : count * rows]
                scores = jnp.concatenate(raw, axis=1) * score_scale + bias
                probs = jnp.exp(jnp.where(same, scores - log_ref[:, head : head + 1], masked_score))
                products = [
                    lax.dot_general(d_out, v, contract_cols, preferred_element_type=jnp.float32)
                    for v in values
                ]
                slopes = (probs * (jnp.concatenate(products, axis=1) - delta)).astype(jnp.bfloat16)
                slope_blocks = [slopes[:, i * rows : (i + 1) * rows] for i in range(count)]
                dq_ref[:, columns] = score_scale * sum(
                    jnp.dot(s, k, preferred_element_type=jnp.float32)
                    for s, k in zip(slope_blocks, keys)
                )
                mirrored = [
                    jnp.dot(s, turned, preferred_element_type=jnp.float32) for s in slope_blocks[::-1]
                ]
                mirrored.append(jnp.zeros((rows, span - count * rows), jnp.float32))
                leaned = pltpu.roll(jnp.concatenate(mirrored, axis=1), 0, 1, stride=1, stride_axis=0)
                diagonal_ref[head : head + 1, :] = jnp.sum(leaned, axis=0, keepdims=True)

        def run(part=0, parts=1):
            some_heads(range(part * heads // parts, (part + 1) * heads // parts))

        return run

    vmem = pl.BlockSpec(memory_space=pltpu.VMEM)
    smem = pl.BlockSpec(memory_space=pltpu.SMEM)
    arrays = [base, lengths, own, d_mixed, local_out, local_log, share, *halos]
    specs = [vmem, smem] + [vmem] * 4 + [smem] + [vmem] * len(halos)
    out_shape = [
        jax.ShapeDtypeStruct((rows, width), jnp.float32),
        jax.ShapeDtypeStruct((heads, span), jnp.float32),
    ]
    return arrays, specs, out_shape, [], begin


def local_keys(base, lengths, own, queries, sent, ratio, count, heads, score_scale):
    rows, width = own.shape[0], own.shape[1] // 3
    head_dim = width // heads
    groups = queries.shape[0] // rows

    def begin(ins, outs, scratch):
        base_ref, lengths_ref, own_ref, ratio_ref, queries_ref, sent_ref = ins
        (out_ref,) = outs
        queries_here, sent_here, sems = scratch
        copies = []
        for i in range(count):
            index = jnp.minimum(lax.axis_index("mem") + i, groups - 1)
            there = pl.ds(pl.multiple_of(index * rows, rows), rows)
            copies.append(
                pltpu.make_async_copy(queries_ref.at[there, :], queries_here.at[i], sems.at[0, i])
            )
            copies.append(pltpu.make_async_copy(sent_ref.at[there, :], sent_here.at[i], sems.at[1, i]))
        for copy in copies:
            copy.start()

        def run():
            for copy in copies:
                copy.wait()
            first = lax.axis_index("mem") * rows
            same = same_book(lengths_ref, first, rows, first, count * rows)
            stats = jnp.concatenate([joined_tile(sent_here[i, :, width:]).T for i in range(count)], axis=1)
            for head in range(heads):
                columns = slice(head * head_dim, (head + 1) * head_dim)
                above = slice(width + head * head_dim, width + (head + 1) * head_dim)
                twice = slice(2 * width + head * head_dim, 2 * width + (head + 1) * head_dim)
                k, v = own_ref[:, above], own_ref[:, twice]
                qs = [queries_here[i, :, columns] for i in range(count)]
                gs = [
                    (sent_here[i, :, columns].astype(jnp.float32) * ratio_ref[head]).astype(jnp.bfloat16)
                    for i in range(count)
                ]
                raw = [
                    lax.dot_general(k, q, contract_cols, preferred_element_type=jnp.float32) for q in qs
                ]
                bias = slanted(base_ref[head : head + 1, :], rows)[:, : count * rows]
                scores = jnp.concatenate(raw, axis=1) * score_scale + bias
                log = stats[2 * heads + head : 2 * heads + head + 1, :]
                delta = stats[3 * heads + head : 3 * heads + head + 1, :]
                probs = jnp.exp(jnp.where(same, scores - log, masked_score))
                products = [
                    lax.dot_general(v, g, contract_cols, preferred_element_type=jnp.float32) for g in gs
                ]
                slopes = (probs * (jnp.concatenate(products, axis=1) - delta)).astype(jnp.bfloat16)
                weights = probs.astype(jnp.bfloat16)
                blocks = [slice(i * rows, (i + 1) * rows) for i in range(count)]
                d_key = sum(
                    jnp.dot(slopes[:, b], q, preferred_element_type=jnp.float32) for b, q in zip(blocks, qs)
                )
                d_value = sum(
                    jnp.dot(weights[:, b], g, preferred_element_type=jnp.float32)
                    for b, g in zip(blocks, gs)
                )
                out_ref[:, above] = (d_key * score_scale).astype(jnp.bfloat16)
                out_ref[:, twice] = d_value.astype(jnp.bfloat16)

        return run

    vmem, anywhere = pl.BlockSpec(memory_space=pltpu.VMEM), pl.BlockSpec(memory_space=pl.ANY)
    smem = pl.BlockSpec(memory_space=pltpu.SMEM)
    arrays = [base, lengths, own, ratio, queries, sent]
    specs = [vmem, smem, vmem, smem, anywhere, anywhere]
    scratch = [
        pltpu.VMEM((count, rows, width), jnp.bfloat16),
        pltpu.VMEM((count, rows, width + 128), jnp.bfloat16),
        pltpu.SemaphoreType.DMA((2, count)),
    ]
    return arrays, specs, [jax.ShapeDtypeStruct((rows, 3 * width), jnp.bfloat16)], scratch, begin


def middle(
    tokens,
    memory_out,
    local_out,
    mem_log,
    local_log,
    share,
    out_weight,
    ffn_gain,
    up_weight,
    down_weight,
    cotangent,
    heads,
):
    rows, width = tokens.shape
    head_dim = width // heads
    hidden = up_weight.shape[1]
    block = math.gcd(hidden, 1024)
    steps = hidden // block

    def kernel(
        tokens_ref, mem_ref, loc_ref, mem_log_ref, log_ref, share_ref, out_w_ref, gain_ref, up_ref, down_ref, cot_ref, *refs
    ):
        mixed_ref, mid_ref, act_ref, d_up_ref, block_ref, d_res_ref, gain_part_ref, d_branch_ref, d_mix_ref = refs[:9]
        gate_ref, sent_ref, residual, branch_sum, d_mid_sum = refs[9:]
        i = pl.program_id(0)

        def scale_of(values):
            return lax.rsqrt(jnp.mean(values * values, axis=1, keepdims=True) + eps_norm)

        @pl.when(i == 0)
        def _():
            for head in range(heads):
                columns = slice(head * head_dim, (head + 1) * head_dim)
                part = share_ref[head]
                mixed_ref[:, columns] = (
                    part * mem_ref[:, columns] + (1.0 - part) * loc_ref[:, columns]
                ).astype(jnp.bfloat16)
            values = tokens_ref[...].astype(jnp.float32) + jnp.dot(
                mixed_ref[...], out_w_ref[...], preferred_element_type=jnp.float32
            )
            residual[...] = values
            mid_ref[...] = (values * scale_of(values) * gain_ref[...]).astype(jnp.bfloat16)
            branch_sum[...] = jnp.zeros_like(branch_sum)
            d_mid_sum[...] = jnp.zeros_like(d_mid_sum)

        up = jnp.dot(mid_ref[...], up_ref[...], preferred_element_type=jnp.float32)
        d_act = jnp.dot(cot_ref[...], down_ref[...], preferred_element_type=jnp.float32)
        below = 0.5 * (1.0 + lax.erf(up * math.sqrt(0.5)))
        density = jnp.exp(-0.5 * up * up) * (1.0 / math.sqrt(2.0 * math.pi))
        act = (up * below).astype(jnp.bfloat16)
        d_up = (d_act * (below + up * density)).astype(jnp.bfloat16)
        act_ref[...] = act
        d_up_ref[...] = d_up
        branch_sum[...] += lax.dot_general(
            act, down_ref[...], contract_cols, preferred_element_type=jnp.float32
        )
        d_mid_sum[...] += lax.dot_general(
            d_up, up_ref[...], contract_cols, preferred_element_type=jnp.float32
        )

        @pl.when(i == steps - 1)
        def _():
            values, d_mid = residual[...], d_mid_sum[...]
            block_ref[...] = (values + branch_sum[...]).astype(jnp.bfloat16)
            scale = scale_of(values)
            wanted = d_mid * gain_ref[...]
            slope = jnp.mean(values * wanted, axis=1, keepdims=True) * scale * scale * scale
            d_res = cot_ref[...].astype(jnp.float32) + scale * wanted - values * slope
            d_res_ref[...] = d_res
            gain_part_ref[...] = jnp.sum(d_mid * values * scale, axis=0, keepdims=True)
            d_branch_ref[...] = d_res.astype(jnp.bfloat16)
            d_mix_ref[...] = lax.dot_general(
                d_branch_ref[...], out_w_ref[...], contract_cols, preferred_element_type=jnp.float32
            )
            mem_deltas, deltas = [], []
            for head in range(heads):
                columns = slice(head * head_dim, (head + 1) * head_dim)
                part = share_ref[head]
                d_mix, mem_here, loc_here = d_mix_ref[:, columns], mem_ref[:, columns], loc_ref[:, columns]
                d_mem = (part * d_mix).astype(jnp.bfloat16)
                d_out = ((1.0 - part) * d_mix).astype(jnp.bfloat16)
                sent_ref[:, columns] = d_mem
                mem_deltas.append(
                    jnp.sum(d_mem.astype(jnp.float32) * mem_here, axis=1, keepdims=True)
                )
                deltas.append(jnp.sum(d_out.astype(jnp.float32) * loc_here, axis=1, keepdims=True))
                gate_ref[head : head + 1, :] = jnp.sum(
                    d_mix * (mem_here - loc_here), axis=0, keepdims=True
                )
            mem_logs = [mem_log_ref[:, head : head + 1] for head in range(heads)]
            logs = [log_ref[:, head : head + 1] for head in range(heads)]
            sent_ref[:, width:] = split_tile(lane_tile(mem_logs + mem_deltas + logs + deltas, rows))

    def whole(*shape):
        return pl.BlockSpec(shape, lambda i: (0, 0))

    weight = pl.BlockSpec((width, block), lambda i: (0, i))
    column = pl.BlockSpec((rows, block), lambda i: (0, i))
    full = whole(rows, width)
    low, high = jnp.bfloat16, jnp.float32
    outs = [
        (full, (rows, width), low),
        (full, (rows, width), low),
        (column, (rows, hidden), low),
        (column, (rows, hidden), low),
        (full, (rows, width), low),
        (full, (rows, width), high),
        (whole(1, width), (1, width), high),
        (full, (rows, width), low),
        (full, (rows, width), high),
        (whole(heads, head_dim), (heads, head_dim), high),
        (whole(rows, width + 128), (rows, width + 128), low),
    ]
    return pl.pallas_call(
        kernel,
        grid=(steps,),
        in_specs=[full, full, full, whole(rows, 128), whole(rows, 128)]
        + [pl.BlockSpec(memory_space=pltpu.SMEM)]
        + [whole(width, width), whole(1, width), weight, weight, full],
        out_specs=[spec for spec, _, _ in outs],
        out_shape=[jax.ShapeDtypeStruct(shape, dtype) for _, shape, dtype in outs],
        scratch_shapes=[pltpu.VMEM((rows, width), jnp.float32)] * 3,
        compiler_params=pltpu.CompilerParams(vmem_limit_bytes=VMEM_LIMIT),
        cost_estimate=lasting(18),
        name="middle",
    )(
        tokens,
        memory_out,
        local_out,
        mem_log,
        local_log,
        share,
        out_weight,
        ffn_gain[None, :],
        up_weight,
        down_weight,
        cotangent,
    )


def exchange_pairs(lefts, rights, other_lefts, other_right, send, recv):
    core = lax.axis_index("dp")
    copies, at = [], 0

    def push(source, target):
        i = len(copies)
        copy = pltpu.make_async_remote_copy(
            src_ref=source,
            dst_ref=target,
            send_sem=send.at[i],
            recv_sem=recv.at[i],
            device_id={"dp": 1 - core},
            device_id_type=pl.DeviceIdType.MESH,
        )
        copy.start()
        copies.append(copy)

    for i, (left, right) in enumerate(zip(lefts, rights)):
        half = right.shape[1] // 2
        push(left, other_lefts.at[i])
        there = pl.ds(pl.multiple_of((1 - core) * half, 128), half)
        push(right.at[:, there], other_right.at[:, pl.ds(at, half)])
        at += half
    return copies


def pair_products(lefts, rights, other_lefts, other_right, turned, store, copies):
    core = lax.axis_index("dp")
    rows = lefts[0].shape[0]
    at = 0
    for i, (left, right) in enumerate(zip(lefts, rights)):
        half = right.shape[1] // 2
        for copy in copies[2 * i : 2 * i + 2]:
            copy.wait_recv()
        turned[:, :rows] = left[...].T
        turned[:, rows:] = other_lefts[i].T
        block = math.gcd(half, 512)
        for column in range(0, half, block):
            kept = right[:, pl.ds(pl.multiple_of(core * half + column, 128), block)]
            both = jnp.concatenate([kept, other_right[:, at + column : at + column + block]], axis=0)
            store(
                at + column,
                jnp.dot(turned[...], both, preferred_element_type=jnp.float32).astype(jnp.bfloat16),
            )
        at += half


def pair_scratch(lefts, rights):
    rows, width = lefts[0].shape
    count = len(lefts)
    return [
        pltpu.VMEM((count, rows, width), jnp.bfloat16),
        pltpu.VMEM((rows, sum(right.shape[1] for right in rights) // 2), jnp.bfloat16),
        pltpu.VMEM((width, 2 * rows), jnp.bfloat16),
        pltpu.SemaphoreType.DMA((2 * count,)),
        pltpu.SemaphoreType.DMA((2 * count,)),
    ]


def pair_grads(lefts, rights, collective_id):
    count, width = len(lefts), lefts[0].shape[1]
    total = sum(right.shape[1] for right in rights) // 2
    block = math.gcd(*[right.shape[1] // 2 for right in rights], 512)

    def kernel(*refs):
        left_refs, right_refs, out_ref = refs[:count], refs[count : 2 * count], refs[2 * count]
        other_lefts, other_right, turned, send, recv, staged, out_sem = refs[2 * count + 1 :]
        barrier = pltpu.get_barrier_semaphore()
        partner = {"dp": 1 - lax.axis_index("dp")}
        pl.semaphore_signal(barrier, inc=1, device_id=partner, device_id_type=pl.DeviceIdType.MESH)
        pl.semaphore_wait(barrier, 1)
        copies = exchange_pairs(left_refs, right_refs, other_lefts, other_right, send, recv)
        written = []

        def store(column, value):
            slot = len(written) % 2
            if len(written) >= 2:
                written[-2].wait()
            staged[slot] = value
            copy = pltpu.make_async_copy(
                staged.at[slot], out_ref.at[:, pl.ds(column, block)], out_sem.at[slot]
            )
            copy.start()
            written.append(copy)

        pair_products(left_refs, right_refs, other_lefts, other_right, turned, store, copies)
        for copy in written[-2:]:
            copy.wait()
        for copy in copies:
            copy.wait_send()

    vmem = pl.BlockSpec(memory_space=pltpu.VMEM)
    return pl.pallas_call(
        kernel,
        in_specs=[vmem] * (2 * count),
        out_specs=pl.BlockSpec(memory_space=pl.ANY),
        out_shape=jax.ShapeDtypeStruct((width, total), jnp.bfloat16),
        scratch_shapes=pair_scratch(lefts, rights)
        + [pltpu.VMEM((2, width, block), jnp.bfloat16), pltpu.SemaphoreType.DMA((2,))],
        compiler_params=pltpu.CompilerParams(
            collective_id=collective_id, has_side_effects=True, vmem_limit_bytes=VMEM_LIMIT
        ),
        cost_estimate=lasting(10),
        name="pair_grads",
    )(*lefts, *rights)


def input_backward(tokens, attn_gain, d_projected, qkv_weight, d_residual):
    rows, width = tokens.shape

    def begin(ins, outs, scratch):
        tokens_ref, gain_ref, d_ref, weight_ref, residual_ref = ins
        grad_ref, part_ref = outs
        weight_here, sem = scratch
        copy = pltpu.make_async_copy(weight_ref, weight_here, sem)
        copy.start()

        def run():
            copy.wait()
            d_in = lax.dot_general(
                d_ref[...], weight_here[...], contract_cols, preferred_element_type=jnp.float32
            )
            x = tokens_ref[...].astype(jnp.float32)
            scale = lax.rsqrt(jnp.mean(x * x, axis=1, keepdims=True) + eps_norm)
            wanted = d_in * gain_ref[...]
            slope = jnp.mean(x * wanted, axis=1, keepdims=True) * scale * scale * scale
            grad_ref[...] = residual_ref[...] + scale * wanted - x * slope
            part_ref[...] = jnp.sum(d_in * x * scale, axis=0, keepdims=True)

        return run

    vmem = pl.BlockSpec(memory_space=pltpu.VMEM)
    arrays = [tokens, attn_gain[None, :], d_projected, qkv_weight, d_residual]
    specs = [vmem, vmem, vmem, pl.BlockSpec(memory_space=pl.ANY), vmem]
    out_shape = [
        jax.ShapeDtypeStruct((rows, width), jnp.float32),
        jax.ShapeDtypeStruct((1, width), jnp.float32),
    ]
    scratch = [pltpu.VMEM(qkv_weight.shape, qkv_weight.dtype), pltpu.SemaphoreType.DMA]
    return arrays, specs, out_shape, scratch, begin


def spread_halves(halves, outs):
    at = 0
    for out in outs:
        half = out.shape[1] // 2
        for c in (0, 1):
            out[:, c * half : (c + 1) * half] = halves[c, :, at : at + half].astype(jnp.float32)
        at += half


def join_halves(sums, collective_id):
    def kernel(sums_ref, both, send, recv):
        core = lax.axis_index("dp")
        partner = {"dp": 1 - core}
        barrier = pltpu.get_barrier_semaphore()
        pl.semaphore_signal(barrier, inc=1, device_id=partner, device_id_type=pl.DeviceIdType.MESH)
        pl.semaphore_wait(barrier, 1)
        copy = pltpu.make_async_remote_copy(
            src_ref=sums_ref,
            dst_ref=both.at[core],
            send_sem=send,
            recv_sem=recv,
            device_id=partner,
            device_id_type=pl.DeviceIdType.MESH,
        )
        copy.start()
        both[core] = sums_ref[...]
        copy.wait()

    vmem = pl.BlockSpec(memory_space=pltpu.VMEM)
    return pl.pallas_call(
        kernel,
        in_specs=[vmem],
        out_specs=vmem,
        out_shape=jax.ShapeDtypeStruct((2, *sums.shape), sums.dtype),
        scratch_shapes=[pltpu.SemaphoreType.DMA, pltpu.SemaphoreType.DMA],
        compiler_params=pltpu.CompilerParams(
            collective_id=collective_id, has_side_effects=True, vmem_limit_bytes=VMEM_LIMIT
        ),
        cost_estimate=lasting(4),
        name="join_halves",
    )(sums)


def write_results(late, late_widths, early, early_widths, small, input_grad, heads, buckets):
    rows, width = late.shape[1], late.shape[2] * 2 // 3
    lines = width // 128
    count = len(late_widths) + len(early_widths)

    def kernel(late_ref, early_ref, small_ref, input_ref, *outs):
        spread_halves(late_ref, outs[: len(late_widths)])
        spread_halves(early_ref, outs[len(late_widths) : count])
        attn_ref, ffn_ref, bias_ref, gate_ref, grad_ref = outs[count:]
        grad_ref[...] = input_ref[...]
        attn_ref[...] = small_ref[:lines, :]
        ffn_ref[...] = small_ref[lines : 2 * lines, :]
        for head in range(heads):
            line, lane = divmod(head * buckets, 128)
            here = small_ref[2 * lines + line : 2 * lines + line + 1, :]
            bias_ref[head : head + 1, :] = here[:, lane : lane + buckets]
        line = 2 * lines + heads * buckets // 128
        gate_ref[...] = small_ref[line : line + 1, :heads]

    shapes = [(rows, size) for size in [*late_widths, *early_widths]]
    shapes += [(lines, 128), (lines, 128), (heads, buckets), (1, heads), input_grad.shape]
    return pl.pallas_call(
        kernel,
        out_shape=[jax.ShapeDtypeStruct(shape, jnp.float32) for shape in shapes],
        compiler_params=pltpu.CompilerParams(vmem_limit_bytes=VMEM_LIMIT),
        cost_estimate=lasting(3),
        name="write_results",
    )(late, early, small, input_grad)


def finish_grads(lefts, rights, small, sources, collective_id, beside):
    width, total = lefts[0].shape[1], sum(right.shape[1] for right in rights) // 2
    rows = width // sources
    count = len(lefts)
    arrays, specs, more_out, more_scratch, begin = beside
    mesh_type = pl.DeviceIdType.MESH
    ref_shapes, sem_shapes = reduce_scratch(rows, total, jnp.bfloat16, sources)
    pair_shapes = pair_scratch(lefts, rights)
    sizes = [count, count, len(arrays), 1, 1, 1, len(more_out)]
    sizes += [len(ref_shapes), len(sem_shapes), len(pair_shapes), len(more_scratch), 8]

    def kernel(*refs):
        groups, at = [], 0
        for size in sizes:
            groups.append(refs[at : at + size])
            at += size
        left_refs, right_refs, ins, (small_ref,), (late,), (small_out,), more_refs = groups[:7]
        steps_refs, steps_sems, (other_lefts, other_right, turned, pair_send, pair_recv), scratch, own = groups[7:]
        parts, small_mine, smalls, core_small, small_send, small_recv, core_send, core_recv = own
        meanwhile = begin(ins, more_refs, scratch)
        me, core = lax.axis_index("mem"), lax.axis_index("dp")
        barrier = pltpu.get_barrier_semaphore()
        peers = [lax.rem(me + k, sources) for k in range(1, sources)]
        for peer in peers:
            pl.semaphore_signal(barrier, inc=1, device_id={"mem": peer}, device_id_type=mesh_type)
        pl.semaphore_signal(barrier, inc=1, device_id={"dp": 1 - core}, device_id_type=mesh_type)
        pl.semaphore_wait(barrier, sources)

        def merge(blocks):
            total = blocks[0][...].astype(jnp.float32)
            for block in blocks[1:]:
                total = total + block[...].astype(jnp.float32)
            return total

        def pack(target, total):
            target[...] = total.astype(jnp.bfloat16)

        def across_cores(source, target, i):
            copy = pltpu.make_async_remote_copy(
                src_ref=source,
                dst_ref=target,
                send_sem=core_send.at[i],
                recv_sem=core_recv.at[i],
                device_id={"dp": 1 - core},
                device_id_type=mesh_type,
            )
            copy.start()
            return copy

        pair_copies = exchange_pairs(
            left_refs, right_refs, other_lefts, other_right, pair_send, pair_recv
        )

        def store(column, value):
            parts[:, column : column + value.shape[1]] = value

        pair_products(
            left_refs, right_refs, other_lefts, other_right, turned, store, pair_copies
        )
        small_copies = [
            remote(small_mine, smalls.at[me], small_send.at[i], small_recv.at[me], peer)
            for i, peer in enumerate(peers)
        ]

        def between():
            meanwhile()
            small_mine[...] = small_ref[...]
            for i in range(width // 128):
                small_mine[i : i + 1, :] = more_refs[-1][:, i * 128 : (i + 1) * 128]
            smalls[me] = small_mine[...]
            for copy in small_copies:
                copy.start()

        final, still_open = reduce_steps(parts, sources, steps_refs, steps_sems, merge, pack, between)
        for here, blocks in final:
            late[core, here] = merge(blocks).astype(jnp.bfloat16)
        late_copy = across_cores(late.at[core], late.at[core], 0)
        for peer in peers:
            remote(
                smalls.at[peer], smalls.at[peer], small_send.at[0], small_recv.at[peer], peer
            ).wait_recv()
        group_small = smalls[0]
        for i in range(1, sources):
            group_small = group_small + smalls[i]
        core_small[0] = group_small
        small_copy = across_cores(core_small.at[0], core_small.at[1], 1)
        for copy in (late_copy, small_copy):
            copy.wait()
        small_out[...] = core_small[0] + core_small[1]
        for copy in still_open + small_copies + pair_copies:
            copy.wait_send()

    vmem = pl.BlockSpec(memory_space=pltpu.VMEM)
    return pl.pallas_call(
        kernel,
        in_specs=[vmem] * (2 * count) + specs + [vmem],
        out_specs=[vmem] * (2 + len(more_out)),
        out_shape=[jax.ShapeDtypeStruct((2, rows, total), jnp.bfloat16)]
        + [jax.ShapeDtypeStruct(small.shape, small.dtype)]
        + more_out,
        scratch_shapes=ref_shapes
        + sem_shapes
        + pair_shapes
        + more_scratch
        + [
            pltpu.VMEM((width, total), jnp.bfloat16),
            pltpu.VMEM(small.shape, small.dtype),
            pltpu.VMEM((sources, *small.shape), small.dtype),
            pltpu.VMEM((2, *small.shape), small.dtype),
        ]
        + [pltpu.SemaphoreType.DMA((sources,))] * 2
        + [pltpu.SemaphoreType.DMA((2,))] * 2,
        compiler_params=pltpu.CompilerParams(
            collective_id=collective_id, has_side_effects=True, vmem_limit_bytes=VMEM_LIMIT
        ),
        cost_estimate=lasting(45),
        name="finish_grads",
    )(*lefts, *rights, *arrays, small)


def on_device(
    tokens,
    attn_gain,
    qkv_weight,
    out_weight,
    bias_table,
    gate_logit,
    ffn_gain,
    up_weight,
    down_weight,
    memory_keys,
    memory_values,
    book_lengths,
    slot_shard,
    slot_index,
    slot_live,
    cotangent,
):
    rows, width = tokens.shape
    heads, buckets = bias_table.shape
    head_dim = width // heads
    top_count = slot_index.shape[2]
    hidden = up_weight.shape[1]
    groups = lax.axis_size("mem")
    capacity = -(-3 * rows * heads * top_count // (2 * groups) // 128) * 128
    score_scale = 1.0 / math.sqrt(head_dim)
    repeats = W // rows
    span = W + 2 * rows
    before = W - jnp.arange(span, dtype=jnp.int32)
    after = jnp.arange(span, dtype=jnp.int32)

    def bias_rows(offset):
        reached = (offset >= 0) & (offset < W)
        hot = (bucket_of(offset)[:, None] == jnp.arange(buckets, dtype=jnp.int32)) & reached[:, None]
        rows_of_bias = jnp.einsum(
            "rb,hb->hr", hot.astype(jnp.float32), bias_table, precision=lax.Precision.HIGHEST
        )
        return rows_of_bias + jnp.where(reached, 0.0, masked_score)

    before_bias, after_bias = bias_rows(before), bias_rows(after)
    bucket = bucket_of(jnp.arange(W, dtype=jnp.int32))
    one_hot = (bucket[:, None] == jnp.arange(buckets, dtype=jnp.int32)).astype(jnp.float32)
    tokens_f = tokens.astype(jnp.float32)
    normed_in = normed(tokens_f, attn_gain).astype(jnp.bfloat16)
    projected = jnp.dot(normed_in, qkv_weight, preferred_element_type=jnp.float32).astype(
        jnp.bfloat16
    )
    slots = memory_keys.shape[0]
    requests = place_requests(slot_shard, slot_index, slot_live, groups, capacity, slots)
    incoming = lax.all_to_all(requests, "mem", split_axis=0, concat_axis=0, tiled=True)
    keys_values, _ = lax.optimization_barrier((projected[:, width:], requests))
    distances = list(range(repeats, 0, -1))
    halos = [passed_along(keys_values, "mem", distance) for distance in distances[: repeats // 2]]
    index, row_ids, bounds = read_lists(incoming, heads, rows, slots)
    bounds = bounds.reshape(-1)
    index, before_bias, after_bias = lax.optimization_barrier((index, before_bias, after_bias))
    key_rows, value_rows = gather_rows(
        index.reshape(-1), bounds, memory_keys, memory_values, heads, groups, capacity
    )
    keys_values, key_rows = lax.optimization_barrier((keys_values, key_rows))
    halos += [passed_along(keys_values, "mem", distance) for distance in distances[repeats // 2 :]]
    all_queries = lax.all_gather(projected[:, :width], "mem", axis=0, tiled=True)
    local = local_forward(before_bias, book_lengths, projected, halos, heads, score_scale)
    partial = memory_forward(
        bounds,
        all_queries,
        key_rows,
        value_rows,
        row_ids,
        heads,
        groups,
        rows,
        score_scale,
    )
    if groups == 16:
        memory_out, mem_log, local_out, local_log = merge_partials(partial, groups, 1, heads, local)
    else:
        local_out, local_log = run_alone("local_forward", local)
        partial = lax.all_to_all(
            partial.reshape(groups, rows, width + 128),
            "mem",
            split_axis=0,
            concat_axis=0,
            tiled=True,
        ).reshape(groups * rows, width + 128)
        memory_out, mem_log = combine_partials(partial, heads, groups, rows)
    gate_share = jax.nn.sigmoid(gate_logit)
    (
        mixed_heads,
        normed_mid,
        activated,
        d_up,
        block_out,
        d_residual,
        ffn_gain_part,
        d_branch,
        d_mixed,
        gate_products,
        sent_grads,
    ) = middle(
        tokens,
        memory_out,
        local_out,
        mem_log,
        local_log,
        gate_share,
        out_weight,
        ffn_gain,
        up_weight,
        down_weight,
        cotangent,
        heads,
    )
    ffn_gain_part = ffn_gain_part.reshape(-1)
    early_halves = pair_grads(
        [mixed_heads, normed_mid, cotangent], [d_branch, d_up, activated], 5
    )
    early_sums = scattered(early_halves)
    sent_grads, _ = lax.optimization_barrier((sent_grads, early_halves))
    gate_part = jnp.sum(gate_products, axis=1) * gate_share * (1.0 - gate_share)
    local = local_queries(
        before_bias,
        book_lengths,
        projected,
        halos,
        d_mixed,
        local_out,
        local_log,
        gate_share,
        heads,
        score_scale,
    )
    if groups == 16:
        all_grads, d_queries, diagonals = gather_group(sent_grads, groups, 2, local)
    else:
        all_grads = lax.all_gather(sent_grads, "mem", axis=0, tiled=True)
        d_queries, diagonals = run_alone("local_queries", local)
    bias_part = jnp.dot(diagonals[:, rows - 1 : rows - 1 + W], one_hot, precision=lax.Precision.HIGHEST)
    d_partial = memory_backward(
        bounds,
        all_queries,
        all_grads,
        key_rows,
        value_rows,
        row_ids,
        heads,
        groups,
        rows,
        score_scale,
    )
    local = local_keys(
        after_bias,
        book_lengths,
        projected,
        all_queries,
        all_grads,
        (1.0 - gate_share) / gate_share,
        repeats + 1,
        heads,
        score_scale,
    )
    if groups == 16:
        d_projected = sum_queries(d_partial, d_queries, groups, 3, score_scale, local)
    else:
        (d_projected,) = run_alone("local_keys", local)
        d_partial, d_projected = lax.optimization_barrier((d_partial, d_projected))
        d_partial = jnp.sum(
            lax.all_to_all(
                d_partial.reshape(groups, rows, width), "mem", split_axis=0, concat_axis=0, tiled=True
            ).astype(jnp.float32),
            axis=0,
        )
        d_queries = (d_queries + d_partial * score_scale).astype(jnp.bfloat16)
        d_projected = jnp.concatenate([d_queries, d_projected[:, width:]], axis=1)
    beside = input_backward(tokens, attn_gain, d_projected, qkv_weight, d_residual)
    small = jnp.concatenate([ffn_gain_part, bias_part.reshape(-1), gate_part], axis=0)
    small = jnp.pad(small, (width, -small.shape[0] % 1024)).reshape(-1, 128)
    early_widths = [width, hidden, hidden]
    if groups == 16:
        late_both, small, tokens_grad, _ = finish_grads(
            [normed_in], [d_projected], small, groups, 4, beside
        )
        early_sums, small = lax.optimization_barrier((early_sums, small))
        early_both = join_halves(early_sums, 7)
    else:
        tokens_grad, attn_gain_part = run_alone("input_backward", beside)
        late_halves = pair_grads([normed_in], [d_projected], 6)
        late_halves, early_sums = lax.optimization_barrier((late_halves, early_sums))
        late_both = lax.all_gather(scattered(late_halves), "dp", axis=0)
        early_both = lax.all_gather(early_sums, "dp", axis=0)
        small = lax.psum(small.at[: width // 128].set(attn_gain_part.reshape(-1, 128)), ("dp", "mem"))
    qkv_grad, out_grad, up_grad, down_grad, attn_sum, ffn_sum, bias_sum, gate_sum, tokens_grad = (
        write_results(
            late_both, [3 * width], early_both, early_widths, small, tokens_grad, heads, buckets
        )
    )
    return (
        block_out,
        tokens_grad,
        qkv_grad,
        out_grad,
        up_grad,
        down_grad,
        attn_sum.reshape(-1),
        ffn_sum.reshape(-1),
        bias_sum,
        gate_sum.reshape(-1),
    )


def solution(mesh):
    in_specs = (
        P(("dp", "mem"), None),
        P(),
        P(),
        P(),
        P(),
        P(),
        P(),
        P(),
        P(),
        P("mem", None),
        P("mem", None),
        P("dp", None),
        P(("dp", "mem"), None, None, None),
        P(("dp", "mem"), None, None),
        P(("dp", "mem"), None, None),
        P(("dp", "mem"), None),
    )
    out_specs = (
        P(("dp", "mem"), None),
        P(("dp", "mem"), None),
        P("mem", None),
        P("mem", None),
        P("mem", None),
        P("mem", None),
        P(),
        P(),
        P(),
        P(),
    )
    return jax.shard_map(
        on_device, mesh=mesh, in_specs=in_specs, out_specs=out_specs, check_vma=False
    )
```
